32 devices in a mesh: batch: 4 (over z), blk: 2 (over x), head: 4 (over y, core).
Axes of the slice: x: 2, y: 2, z: 4, core: 2. Of those that a mesh axis runs over, the one named last changes fastest.
Arguments:
- tokens: bfloat16 [8, 1024, 1280], P('batch', ('blk', 'head')), may hold values from -6 to 6
- segments: int32 [8, 1024], P('batch'), may hold values from 0 to 1023, as said below
- qkv_weight: bfloat16 [2, 1280, 3840], P(None, ('batch', 'blk', 'head')), may hold values from -0.15625 to 0.15625
- out_weight: bfloat16 [2, 1280, 1280], P(None, ('batch', 'blk', 'head')), may hold values from -1.25 to 1.25
- up_weight: bfloat16 [2, 1280, 1280], P(None, ('batch', 'blk', 'head')), may hold values from -0.15625 to 0.15625
- down_weight: bfloat16 [2, 1280, 1280], P(None, ('batch', 'blk', 'head')), may hold values from -0.15625 to 0.15625
- attn_gain: bfloat16 [2, 1280], P(None, ('batch', 'blk', 'head')), may hold values from 0.099609375 to 1.8984375
- mlp_gain: bfloat16 [2, 1280], P(None, ('batch', 'blk', 'head')), may hold values from 0.099609375 to 1.8984375
- scale_param: float32 [2, 80], replicated, may hold values from -1 to 1.5
- cotangent: bfloat16 [8, 1024, 1280], P('batch', ('blk', 'head')), may hold values from -6 to 6
Outputs:
- layer_out: bfloat16 [8, 1024, 1280], P('batch', ('blk', 'head'))
- input_grad: float32 [8, 1024, 1280], P('batch', ('blk', 'head'))
- qkv_grad: float32 [2, 1280, 3840], P(None, ('batch', 'blk', 'head'))
- out_grad: float32 [2, 1280, 1280], P(None, ('batch', 'blk', 'head'))
- up_grad: float32 [2, 1280, 1280], P(None, ('batch', 'blk', 'head'))
- down_grad: float32 [2, 1280, 1280], P(None, ('batch', 'blk', 'head'))
- attn_gain_grad: float32 [2, 1280], P(None, ('batch', 'blk', 'head'))
- mlp_gain_grad: float32 [2, 1280], P(None, ('batch', 'blk', 'head'))
- scale_grad: float32 [2, 80], replicated
The draws below stay inside these ranges and needn't reach their ends.
Inputs may be any that keep to these rules, and one draw needn't show every extreme that they name: `segments`: within each sequence the segment numbers start at 0 and never fall along the positions.
All inputs are finite; a program needn't handle non-finite values.
Results may differ from the reference program's by a relative error of at most 0.035.
Values may be sent and summed in bfloat16 or wider, within the bound.
No kernel may reach another device: no remote copies, remote signals or barrier semaphores. Data moves between devices by JAX's collectives and lax.ppermute only.
A program may use at most 256 MiB of HBM per device.

```python
import math
import jax
import jax.numpy as jnp
from jax import lax

D = 1280
HEADS = 16
HD = 80
FF = 1280
LAYERS = 2
WINDOW = 1024
BLOCK = 512
SEQUENCES = 8
LENGTH = 1024


def draw_segments(key, part):
    key = jax.random.fold_in(key, 7)
    split_keys = jax.random.split(key)
    boundary = jax.random.randint(split_keys[0], (SEQUENCES, LENGTH), 0, WINDOW + WINDOW // 2) == 0
    selected_option = jax.random.randint(split_keys[1], (), 0, SEQUENCES)
    places = jnp.arange(LENGTH, dtype=jnp.int32)
    seq_index = jnp.arange(SEQUENCES, dtype=jnp.int32)
    keep_open = (seq_index[:, None] == selected_option) & (places[None, :] >= BLOCK // 2) & (places[None, :] < LENGTH - BLOCK // 2 + 1)
    boundary = boundary & jnp.logical_not(keep_open) & (places[None, :] > 0)
    boundary = boundary | (places[None, :] == LENGTH - 1)
    starts = jnp.where(boundary, places[None, :], jnp.zeros((SEQUENCES, LENGTH), jnp.int32))
    return lax.cummax(starts, axis=1).astype(jnp.int32)


def shard_levels(rng, extent, cuts, low, top_value):
    level, own = 1.0, jax.random.fold_in(rng, 6)
    for dim, blocks in cuts:
        draws = jnp.exp(jax.random.uniform(jax.random.fold_in(own, dim), (blocks,), jnp.float32, low / len(cuts), top_value / len(cuts)))
        level = level * jnp.repeat(draws, extent[dim] // blocks).reshape([-1 if axis == dim else 1 for axis in range(len(extent))])
    return level


def normal_values(key, shape, scale, most, cuts=(), held_as=jnp.bfloat16):
    drawn = jax.random.normal(key, shape, jnp.float32) * scale
    if len(cuts) > 0:
        drawn = shard_levels(key, shape, cuts, -0.22, 0.18) * drawn
    return jnp.clip(drawn, min=-most, max=most).astype(held_as)


def setup_inputs(seed: int = 0) -> dict:
    streams_of = jax.random.split(jax.random.key(seed), 11)
    tokens = normal_values(streams_of[0], (SEQUENCES, LENGTH, D), 1.0, 6.0, ((0, 4), (1, 8)))
    segments = draw_segments(jax.random.fold_in(streams_of[10], 71), 0)
    qkv_weight = normal_values(streams_of[2], (LAYERS, D, 3 * D), D ** -0.5, 0.15625, ((1, 32),))
    out_weight = normal_values(streams_of[3], (LAYERS, D, D), (D // 64) ** -0.5, 1.25, ((1, 32),))
    up_weight = normal_values(streams_of[4], (LAYERS, D, FF), D ** -0.5, 0.15625, ((1, 32),))
    down_weight = normal_values(streams_of[5], (LAYERS, FF, D), FF ** -0.5, 0.15625, ((1, 32),))
    attn_gain = jnp.clip(1.0 + 0.18 * jax.random.normal(streams_of[6], (LAYERS, D), jnp.float32), 0.099609375, 1.8984375).astype(jnp.bfloat16)
    mlp_gain = jnp.clip(1.0 + 0.18 * jax.random.normal(streams_of[7], (LAYERS, D), jnp.float32), 0.099609375, 1.8984375).astype(jnp.bfloat16)
    scale_param = jnp.clip(jax.random.uniform(streams_of[8], (LAYERS, HD), jnp.float32, -1.0, 1.5), -1.0, 1.5)
    cotangent = normal_values(streams_of[9], (SEQUENCES, LENGTH, D), 1.0, 6.0, ((0, 4), (1, 8)))
    return dict(tokens=tokens, segments=segments, qkv_weight=qkv_weight, out_weight=out_weight, up_weight=up_weight, down_weight=down_weight, attn_gain=attn_gain, mlp_gain=mlp_gain, scale_param=scale_param, cotangent=cotangent)


@jax.custom_vjp
def low(v):
    return lax.optimization_barrier(v.astype(jnp.bfloat16)).astype(jnp.float32)

@jax.custom_vjp
def low_back(v):
    return v

def low_keep(v):
    return (low(v), None)

def low_pass(kept, grad):
    return (grad,)

def back_keep(v):
    return (v, None)

def back_low(kept, grad):
    return (low(grad),)
low.defvjp(low_keep, low_pass)
low_back.defvjp(back_keep, back_low)
EPSILON = 1e-06
SCALE_BASE = 1.4426950408889634
MASKED_SCORE = -1e+30
HIGHEST = lax.Precision.HIGHEST

def normalize(stream, gain):
    return stream * lax.rsqrt(lax.optimization_barrier(jnp.mean(stream * stream, axis=-1, keepdims=True)) + EPSILON) * gain

def block_attend(pieces):
    queries, keys, values, query_segs, key_segs, query_place, key_place = pieces
    scores = low_back(jnp.einsum('qhd,khd->hqk', queries, keys, precision=HIGHEST))
    near = (key_segs[None, :] == query_segs[:, None]) & (key_place[None, :] <= query_place[:, None]) & (query_place[:, None] - key_place[None, :] < WINDOW)
    scores = jnp.where(near[None], scores, MASKED_SCORE)
    top_score = lax.optimization_barrier(jnp.max(scores, axis=-1, keepdims=True))
    exp_terms = jnp.exp(scores - top_score)
    probs = exp_terms / lax.optimization_barrier(jnp.sum(exp_terms, axis=-1, keepdims=True))
    return jnp.einsum('hqk,khd->qhd', low(probs), values, precision=HIGHEST)

def forward_sequence(stream, seq_segments, params):
    qkv_all, out_all, up_all, down_all, attn_all, mlp_all, scale_all = params
    block_count = LENGTH // BLOCK
    places = jnp.arange(LENGTH, dtype=jnp.int32)
    query_place = places.reshape(block_count, BLOCK)
    window_index = (jnp.arange(block_count, dtype=jnp.int32)[:, None] * BLOCK + jnp.arange(BLOCK + WINDOW, dtype=jnp.int32)[None, :]).astype(jnp.int32)
    key_place = window_index - WINDOW
    padded_segs = jnp.concatenate([jnp.full((WINDOW,), -1, jnp.int32), seq_segments.astype(jnp.int32)])
    key_segs = padded_segs[window_index]
    query_segs = seq_segments.astype(jnp.int32).reshape(block_count, BLOCK)
    for layer_index in range(LAYERS):
        normed = low(normalize(stream, attn_all[layer_index]))
        projected = jnp.dot(normed, qkv_all[layer_index], precision=HIGHEST)
        scale_vec = SCALE_BASE / math.sqrt(HD) * jax.nn.softplus(scale_all[layer_index])
        query_pre = low_back(projected[:, :D])
        queries = low_back(low(query_pre.reshape(LENGTH, HEADS, HD) * scale_vec))
        keys = low_back(low(projected[:, D:2 * D])).reshape(LENGTH, HEADS, HD)
        values = low_back(low(projected[:, 2 * D:])).reshape(LENGTH, HEADS, HD)
        zero_pad = jnp.zeros((WINDOW, HEADS, HD), jnp.float32)
        keys_pad = jnp.concatenate([zero_pad, keys], axis=0)
        values_pad = jnp.concatenate([zero_pad, values], axis=0)
        attended = lax.map(jax.checkpoint(block_attend), (queries.reshape(block_count, BLOCK, HEADS, HD), keys_pad[window_index], values_pad[window_index], query_segs, key_segs, query_place, key_place))
        attended = low_back(low(attended.reshape(LENGTH, D)))
        stream = stream + low_back(jnp.dot(attended, out_all[layer_index], precision=HIGHEST))
        normed_two = low(normalize(stream, mlp_all[layer_index]))
        hidden = low_back(jnp.dot(normed_two, up_all[layer_index], precision=HIGHEST))
        active = low(hidden * jax.nn.sigmoid(hidden))
        stream = stream + low_back(jnp.dot(active, down_all[layer_index], precision=HIGHEST))
    return stream

def reference(tokens, segments, qkv_weight, out_weight, up_weight, down_weight, attn_gain, mlp_gain, scale_param, cotangent):
    params = (qkv_weight.astype(jnp.float32), out_weight.astype(jnp.float32), up_weight.astype(jnp.float32), down_weight.astype(jnp.float32), attn_gain.astype(jnp.float32), mlp_gain.astype(jnp.float32), scale_param.astype(jnp.float32))
    totals_init = jax.tree.map(jnp.zeros_like, params)

    def per_sequence(totals, item):
        seq_tokens, seq_segments, seq_cot = item

        def forward(stream, weights):
            return forward_sequence(stream, seq_segments, weights)
        value, pullback = jax.vjp(forward, seq_tokens.astype(jnp.float32), params)
        stream_grad, param_grads = pullback(seq_cot.astype(jnp.float32))
        totals = jax.tree.map(jnp.add, totals, param_grads)
        return (totals, (value.astype(jnp.bfloat16), stream_grad))
    totals, (layer_out, input_grad) = lax.scan(per_sequence, totals_init, (tokens, segments, cotangent))
    return (layer_out, input_grad, totals[0], totals[1], totals[2], totals[3], totals[4], totals[5], totals[6])
```

```python
import math

import jax
import jax.numpy as jnp
from jax import lax
from jax.sharding import PartitionSpec as P

WINDOW = 1024
EPSILON = 1e-06
SCALE_BASE = 1.4426950408889634
MASKED_SCORE = -1e30

ALL = ("batch", "blk", "head")
REST = ("batch", "blk")
F32 = jnp.float32
BF16 = jnp.bfloat16


def shifted(block, axis, distance):
    devices = range(lax.axis_size(axis))
    route = [(i - distance, i) for i in devices if i - distance in devices]
    return lax.ppermute(block, axis, route)


def dot(left, right):
    return jnp.dot(left, right, preferred_element_type=F32)


def dot_rows(left, right):
    return lax.dot_general(left, right, (((0,), (0,)), ((), ())), preferred_element_type=F32)


def dot_cols(left, right):
    return lax.dot_general(left, right, (((1,), (1,)), ((), ())), preferred_element_type=F32)


def normalize(stream, gain):
    factor = lax.rsqrt(jnp.mean(stream * stream, axis=-1, keepdims=True) + EPSILON)
    return stream * factor * gain, factor


def norm_back(upper, stream, factor, gain):
    inner = upper * gain
    gain_grad = jnp.sum(upper * stream * factor, axis=0)
    lower = factor * inner - stream * factor * factor * factor * jnp.mean(
        inner * stream, axis=-1, keepdims=True
    )
    return lower, gain_grad


class Plan:
    def __init__(self, tokens):
        self.seqs, self.rows, self.width = tokens.shape
        self.heads = lax.axis_size("head")
        self.blks = lax.axis_size("blk")
        self.block = self.rows * self.heads
        self.whole = self.seqs % self.blks == 0
        if self.whole:
            self.groups, self.own_seqs = self.blks, self.seqs // self.blks
            self.reach = 0
        else:
            self.groups, self.own_seqs = 1, self.seqs
            self.reach = min((WINDOW - 1) // self.block + 1, self.blks - 1)
        self.length = self.groups * self.block
        self.tokens = self.seqs * self.rows


def to_plan(plan, array):
    if plan.whole and plan.blks > 1:
        array = lax.all_to_all(array, "blk", split_axis=0, concat_axis=0, tiled=True)
    return array.reshape(plan.tokens, plan.width)


def from_plan(plan, flat):
    array = flat.reshape(plan.seqs, plan.rows, plan.width)
    if plan.whole and plan.blks > 1:
        array = lax.all_to_all(array, "blk", split_axis=0, concat_axis=0, tiled=True)
    return array


def in_sequence(plan, by_head, width):
    parts = by_head.reshape(plan.heads, plan.groups, plan.own_seqs, plan.rows, width)
    return parts.transpose(2, 1, 0, 3, 4).reshape(-1, width)


def by_owner(plan, rows, width):
    parts = rows.reshape(plan.own_seqs, plan.groups, plan.heads, plan.rows, width)
    return parts.transpose(2, 1, 0, 3, 4).reshape(plan.heads, plan.tokens, width)


def gather_tokens(plan, rows):
    moved = lax.all_gather(rows, "head", axis=0, tiled=False)
    return in_sequence(plan, moved, rows.shape[-1])


def scatter_tokens(plan, rows):
    width = rows.shape[-1]
    return lax.psum_scatter(
        by_owner(plan, rows.astype(BF16), width), "head", scatter_dimension=0, tiled=False
    ).astype(F32)


def heads_to_tokens(plan, rows):
    part = rows.shape[-1]
    moved = lax.all_to_all(
        by_owner(plan, rows, part), "head", split_axis=0, concat_axis=0, tiled=True
    )
    return moved.transpose(1, 0, 2).reshape(plan.tokens, plan.heads * part)


def tokens_to_heads(plan, rows):
    part = rows.shape[-1] // plan.heads
    sent = rows.reshape(plan.tokens, plan.heads, part).transpose(1, 0, 2)
    moved = lax.all_to_all(sent, "head", split_axis=0, concat_axis=0, tiled=True)
    return in_sequence(plan, moved, part)


def gather_qkv(rows):
    own, width = rows.shape
    heads = lax.axis_size("head")
    part = width // 3 // heads
    sent = rows.reshape(own, 3, heads, part).transpose(2, 0, 1, 3).reshape(heads, own, 3 * part)
    moved = lax.all_to_all(sent, "head", split_axis=0, concat_axis=0, tiled=True)
    full = lax.all_gather(moved, REST, axis=0, tiled=True)
    return full.reshape(-1, 3 * part)


def scatter_qkv(grad):
    heads = lax.axis_size("head")
    part = grad.shape[1] // 3
    summed = lax.psum_scatter(grad.astype(BF16), REST, scatter_dimension=0, tiled=True)
    own = summed.shape[0] // heads
    moved = lax.all_to_all(
        summed.reshape(heads, own, 3 * part), "head", split_axis=0, concat_axis=0, tiled=True
    )
    return (
        moved.reshape(heads, own, 3, part)
        .transpose(1, 2, 0, 3)
        .reshape(own, 3 * heads * part)
        .astype(F32)
    )


def window_mask(plan, segments, block_index):
    key_count = plan.length + plan.reach * plan.block
    if plan.whole:
        query_segs, key_segs = segments, segments
    else:
        leading = jnp.full((plan.own_seqs, plan.reach * plan.block), -1, jnp.int32)
        padded = jnp.concatenate([leading, segments], axis=1)
        start = block_index * plan.block
        query_segs = lax.dynamic_slice_in_dim(segments, start, plan.block, 1)
        key_segs = lax.dynamic_slice_in_dim(padded, start, key_count, 1)
    query_place = jnp.arange(plan.length, dtype=jnp.int32)[:, None] + plan.reach * plan.block
    key_place = jnp.arange(key_count, dtype=jnp.int32)[None, :]
    near = (key_place <= query_place) & (query_place - key_place < WINDOW)
    return (key_segs[:, None, :] == query_segs[:, :, None]) & near[None]


def with_earlier(plan, own):
    arrived = [own]
    for _ in range(plan.reach):
        arrived.append(shifted(arrived[-1], "blk", 1))
    return jnp.concatenate(arrived[::-1], axis=1) if plan.reach else own


def to_earlier(plan, grads):
    if not plan.reach:
        return grads
    block = plan.block
    total = grads[:, :block]
    for step in range(1, plan.reach + 1):
        total = (
            shifted(total.astype(BF16), "blk", -1).astype(F32)
            + grads[:, step * block : (step + 1) * block]
        )
    return total


def scores_of(queries, keys, allowed):
    scores = jnp.einsum("sqhd,skhd->shqk", queries, keys, preferred_element_type=F32)
    return jnp.where(allowed[:, None], scores, MASKED_SCORE)


def attend(queries, keys, values, allowed):
    scores = scores_of(queries, keys, allowed)
    top_score = jnp.max(scores, axis=-1, keepdims=True)
    exp_terms = jnp.exp(scores - top_score)
    totals = jnp.sum(exp_terms, axis=-1, keepdims=True)
    probs_low = (exp_terms / totals).astype(BF16)
    attended = jnp.einsum("shqk,skhd->sqhd", probs_low, values, preferred_element_type=F32)
    return attended, top_score + jnp.log(totals)


def attend_back(queries, keys, values, allowed, log_total, attended_grad):
    probs = jnp.exp(scores_of(queries, keys, allowed) - log_total)
    probs_low = probs.astype(BF16)
    values_grad = jnp.einsum(
        "shqk,sqhd->skhd", probs_low, attended_grad, preferred_element_type=F32
    )
    probs_grad = jnp.einsum("sqhd,skhd->shqk", attended_grad, values, preferred_element_type=F32)
    row_dot = jnp.sum(probs_grad * probs, axis=-1, keepdims=True)
    scores_low = (probs * (probs_grad - row_dot)).astype(BF16)
    queries_grad = jnp.einsum("shqk,skhd->sqhd", scores_low, keys, preferred_element_type=F32)
    keys_grad = jnp.einsum("shqk,sqhd->skhd", scores_low, queries, preferred_element_type=F32)
    return queries_grad, keys_grad, values_grad


def forward(plan, stream, qkv, dense, gains, scale_vec, allowed):
    width = plan.width
    head_dim = scale_vec.shape[0]
    part = qkv.shape[1] // 3
    local_heads = part // head_dim
    split = (plan.own_seqs, plan.length, local_heads, head_dim)
    out_w, up_w, down_w = dense[:, :width], dense[:, width:-width], dense[:, -width:]
    normed, factor_one = normalize(stream, gains[0])
    normed_all = gather_tokens(plan, normed.astype(BF16))
    projected = dot(normed_all, qkv)
    query_pre = projected[:, :part].reshape(split)
    queries = (query_pre * scale_vec).astype(BF16)
    keys = with_earlier(plan, projected[:, part : 2 * part].astype(BF16).reshape(split))
    values = with_earlier(plan, projected[:, 2 * part :].astype(BF16).reshape(split))
    attended_part, log_total = attend(queries, keys, values, allowed)
    attended = heads_to_tokens(plan, attended_part.astype(BF16).reshape(-1, part))
    middle = stream + dot(attended, out_w)
    normed_two, factor_two = normalize(middle, gains[1])
    normed_two = normed_two.astype(BF16)
    hidden = dot(normed_two, up_w)
    active = (hidden * jax.nn.sigmoid(hidden)).astype(BF16)
    result = middle + dot(active, down_w)
    kept = (
        stream, factor_one, normed_all, query_pre, queries, keys, values, log_total,
        attended, middle, factor_two, normed_two, hidden, active,
    )
    return result, kept


def backward(plan, upper, kept, qkv, dense, gains, scale_vec, allowed):
    (
        stream, factor_one, normed_all, query_pre, queries, keys, values, log_total,
        attended, middle, factor_two, normed_two, hidden, active,
    ) = kept
    width = plan.width
    head_dim = scale_vec.shape[0]
    part = qkv.shape[1] // 3
    out_w, up_w, down_w = dense[:, :width], dense[:, width:-width], dense[:, -width:]
    upper_low = upper.astype(BF16)
    down_grad = dot_rows(active, upper_low)
    active_grad = dot_cols(upper_low, down_w)
    gate = jax.nn.sigmoid(hidden)
    hidden_low = (active_grad * gate * (1.0 + hidden * (1.0 - gate))).astype(BF16)
    up_grad = dot_rows(normed_two, hidden_low)
    extra_two, mlp_gain_grad = norm_back(dot_cols(hidden_low, up_w), middle, factor_two, gains[1])
    middle_grad = upper + extra_two
    middle_low = middle_grad.astype(BF16)
    out_grad = dot_rows(attended, middle_low)
    dense_grad = jnp.concatenate([out_grad, up_grad, down_grad], axis=1).astype(BF16)
    dense_own = lax.psum_scatter(dense_grad, ALL, scatter_dimension=0, tiled=True)
    attended_grad = tokens_to_heads(plan, dot_cols(middle_low, out_w).astype(BF16))
    queries_grad, keys_grad, values_grad = attend_back(
        queries, keys, values, allowed, log_total, attended_grad.reshape(queries.shape)
    )
    query_bar = queries_grad.astype(BF16).astype(F32)
    scale_vec_grad = jnp.sum((query_bar * query_pre).reshape(-1, head_dim), axis=0)
    query_low = (query_bar * scale_vec).astype(BF16).reshape(-1, part)
    keys_low = to_earlier(plan, keys_grad).astype(BF16).reshape(-1, part)
    values_low = to_earlier(plan, values_grad).astype(BF16).reshape(-1, part)
    projected_low = jnp.concatenate([query_low, keys_low, values_low], axis=1)
    normed_grad = scatter_tokens(plan, dot_cols(projected_low, qkv))
    qkv_own = scatter_qkv(dot_rows(normed_all, projected_low))
    extra_one, attn_gain_grad = norm_back(normed_grad, stream, factor_one, gains[0])
    lower = middle_grad + extra_one
    return lower, qkv_own, dense_own, (attn_gain_grad, mlp_gain_grad), scale_vec_grad


def per_device(
    tokens,
    segments,
    qkv_weight,
    out_weight,
    up_weight,
    down_weight,
    attn_gain,
    mlp_gain,
    scale_param,
    cotangent,
):
    plan = Plan(tokens)
    layers, head_dim = scale_param.shape
    block_index = lax.axis_index("blk")
    scale_vecs = SCALE_BASE / math.sqrt(head_dim) * jax.nn.softplus(scale_param)
    own_gains = jnp.concatenate([attn_gain, mlp_gain], axis=0)
    gains = (
        lax.all_gather(own_gains.reshape(1, -1), ALL, axis=0, tiled=True)
        .reshape(-1, 2 * layers, attn_gain.shape[1])
        .transpose(1, 0, 2)
        .reshape(2 * layers, plan.width)
        .astype(F32)
    )
    if plan.whole:
        segments = lax.dynamic_slice_in_dim(
            segments, block_index * plan.own_seqs, plan.own_seqs, 0
        )
    allowed = window_mask(plan, segments, block_index)
    stream = to_plan(plan, tokens).astype(F32)
    qkvs, denses, kept = [], [], []
    for layer in range(layers):
        qkvs.append(gather_qkv(qkv_weight[layer]))
        own = jnp.concatenate([out_weight[layer], up_weight[layer], down_weight[layer]], axis=1)
        denses.append(lax.all_gather(own, ALL, axis=0, tiled=True))
        layer_gains = (gains[layer], gains[layers + layer])
        stream, saved = forward(
            plan, stream, qkvs[layer], denses[layer], layer_gains, scale_vecs[layer], allowed
        )
        kept.append(saved)
    layer_out = from_plan(plan, stream.astype(BF16))
    upper = to_plan(plan, cotangent).astype(F32)
    qkv_grads, dense_grads = [None] * layers, [None] * layers
    gain_grads, scale_grads = [None] * layers, [None] * layers
    for layer in reversed(range(layers)):
        layer_gains = (gains[layer], gains[layers + layer])
        upper, qkv_grads[layer], dense_grads[layer], gain_grads[layer], scale_grads[layer] = (
            backward(
                plan, upper, kept[layer], qkvs[layer], denses[layer], layer_gains,
                scale_vecs[layer], allowed,
            )
        )
    input_grad = from_plan(plan, upper.astype(BF16)).astype(F32)
    small = jnp.concatenate(
        [g[0] for g in gain_grads] + [g[1] for g in gain_grads] + scale_grads, axis=0
    )
    total = lax.psum(small, ALL)
    gain_total = total[: 2 * layers * plan.width].reshape(2 * layers, plan.width)
    owner = lax.axis_index(ALL)
    gain_rows = attn_gain.shape[1]
    own_total = lax.dynamic_slice_in_dim(gain_total, owner * gain_rows, gain_rows, 1)
    scale_total = total[2 * layers * plan.width :].reshape(layers, head_dim)
    scale_grad = scale_total * (SCALE_BASE / math.sqrt(head_dim)) * jax.nn.sigmoid(scale_param)
    dense_all = jnp.stack(dense_grads).astype(F32)
    width = plan.width
    return (
        layer_out,
        input_grad,
        jnp.stack(qkv_grads),
        dense_all[:, :, :width],
        dense_all[:, :, width:-width],
        dense_all[:, :, -width:],
        own_total[:layers],
        own_total[layers:],
        scale_grad,
    )


def solution(mesh):
    rows = P(None, ALL, None)
    by_token = P("batch", ("blk", "head"), None)
    return jax.shard_map(
        per_device,
        mesh=mesh,
        in_specs=(
            by_token, P("batch", None), rows, rows, rows, rows, P(None, ALL), P(None, ALL), P(),
            by_token,
        ),
        out_specs=(
            by_token, by_token, rows, rows, rows, rows, P(None, ALL), P(None, ALL), P(),
        ),
        check_vma=False,
    )
```

```python
import math

import jax
import jax.numpy as jnp
from jax import lax
from jax.sharding import PartitionSpec as P

WINDOW = 1024
EPSILON = 1e-06
SCALE_BASE = 1.4426950408889634
MASKED_SCORE = -1e30

ALL = ("batch", "blk", "head")
REST = ("batch", "blk")
F32 = jnp.float32
BF16 = jnp.bfloat16


def shifted(block, axis, distance):
    devices = range(lax.axis_size(axis))
    route = [(i - distance, i) for i in devices if i - distance in devices]
    return lax.ppermute(block, axis, route)


def dot(left, right):
    return jnp.dot(left, right, preferred_element_type=F32)


def dot_rows(left, right):
    return lax.dot_general(left, right, (((0,), (0,)), ((), ())), preferred_element_type=F32)


def dot_cols(left, right):
    return lax.dot_general(left, right, (((1,), (1,)), ((), ())), preferred_element_type=F32)


def swapped(array, axis, mask):
    size = lax.axis_size(axis)
    return lax.ppermute(array, axis, [(i, i ^ mask) for i in range(size)])


def pick(array, index, axis=0):
    return lax.dynamic_index_in_dim(array, index, axis, keepdims=False)


def small_slice():
    sizes = tuple(lax.axis_size(axis) for axis in ALL)
    return sizes == (4, 2, 4)


def normalize(stream, gain):
    factor = lax.rsqrt(jnp.mean(stream * stream, axis=-1, keepdims=True) + EPSILON)
    return stream * factor * gain, factor


def norm_back(upper, stream, factor, gain):
    inner = upper * gain
    return factor * inner - stream * factor * factor * factor * jnp.mean(
        inner * stream, axis=-1, keepdims=True
    )


def gain_grad(weight, weight_grad, gain):
    return jnp.sum(weight.astype(F32) * weight_grad, axis=-1) / gain.astype(F32)


class Plan:
    def __init__(self, tokens):
        self.seqs, self.rows, self.width = tokens.shape
        self.heads = lax.axis_size("head")
        self.blks = lax.axis_size("blk")
        self.block = self.rows * self.heads
        self.whole = self.seqs % self.blks == 0
        if self.whole:
            self.groups, self.own_seqs = self.blks, self.seqs // self.blks
            self.reach = 0
        else:
            self.groups, self.own_seqs = 1, self.seqs
            self.reach = min((WINDOW - 1) // self.block + 1, self.blks - 1)
        self.length = self.groups * self.block
        self.tokens = self.seqs * self.rows


def swap_blocks(plan, array):
    if not plan.whole or plan.blks == 1:
        return array
    if plan.blks > 2:
        return lax.all_to_all(array, "blk", split_axis=0, concat_axis=0, tiled=True)
    halves = array.reshape(2, plan.own_seqs, plan.rows, plan.width)
    me = lax.axis_index("blk")
    got = swapped(pick(halves, 1 - me), "blk", 1)
    kept = pick(halves, me)
    mine = me == 0
    swapped_halves = jnp.stack([jnp.where(mine, kept, got), jnp.where(mine, got, kept)])
    return swapped_halves.reshape(array.shape)


def to_plan(plan, array):
    return swap_blocks(plan, array).reshape(plan.tokens, plan.width)


def from_plan(plan, flat):
    return swap_blocks(plan, flat.reshape(plan.seqs, plan.rows, plan.width))


def in_sequence(plan, by_head, width):
    parts = by_head.reshape(plan.heads, plan.groups, plan.own_seqs, plan.rows, width)
    return parts.transpose(2, 1, 0, 3, 4).reshape(-1, width)


def by_owner(plan, rows, width):
    parts = rows.reshape(plan.own_seqs, plan.groups, plan.heads, plan.rows, width)
    return parts.transpose(2, 1, 0, 3, 4).reshape(plan.heads, plan.tokens, width)


def gather_tokens(plan, rows):
    width = rows.shape[-1]
    if not small_slice():
        moved = lax.all_gather(rows, "head", axis=0, tiled=False)
        return in_sequence(plan, moved, width)
    far = swapped(rows, "head", 2)
    near = swapped(rows, "head", 1)
    both = swapped(far, "head", 1)
    pieces = jnp.stack([rows, near, far, both])
    me = lax.axis_index("head")
    return in_sequence(plan, jnp.stack([pick(pieces, me ^ i) for i in range(4)]), width)


def scatter_tokens(plan, rows):
    width = rows.shape[-1]
    parts = by_owner(plan, rows, width)
    if not small_slice():
        return lax.psum_scatter(
            parts.astype(BF16), "head", scatter_dimension=0, tiled=False
        ).astype(F32)
    me = lax.axis_index("head")
    parts = parts.reshape(2, 2, plan.tokens, width)
    row, core = me // 2, me % 2
    halves = pick(parts, core, 1) + swapped(
        pick(parts, 1 - core, 1).astype(BF16), "head", 1
    ).astype(F32)
    return pick(halves, row) + swapped(pick(halves, 1 - row).astype(BF16), "head", 2).astype(F32)


def heads_to_tokens(plan, rows):
    part = rows.shape[-1]
    moved = lax.all_to_all(
        by_owner(plan, rows, part), "head", split_axis=0, concat_axis=0, tiled=True
    )
    return moved.transpose(1, 0, 2).reshape(plan.tokens, plan.heads * part)


def tokens_to_heads(plan, rows):
    part = rows.shape[-1] // plan.heads
    sent = rows.reshape(plan.tokens, plan.heads, part).transpose(1, 0, 2)
    moved = lax.all_to_all(sent, "head", split_axis=0, concat_axis=0, tiled=True)
    return in_sequence(plan, moved, part)


def gather_over(piece, axis):
    size = lax.axis_size(axis)
    pieces = jnp.stack([piece] + [swapped(piece, axis, mask) for mask in range(1, size)])
    me = lax.axis_index(axis)
    return jnp.stack([pick(pieces, me ^ i) for i in range(size)])


def gather_qkv(rows, extra):
    layers, own, width = rows.shape
    heads = lax.axis_size("head")
    part = width // 3 // heads
    sent = rows.reshape(layers, own, 3, heads, part).transpose(3, 0, 1, 2, 4)
    sent = sent.reshape(heads, layers, own, 3 * part)
    moved = lax.all_to_all(sent, "head", split_axis=0, concat_axis=0, tiled=True)
    full = []
    if not small_slice():
        for layer in range(layers):
            full.append(lax.all_gather(moved[:, layer], REST, axis=0, tiled=True))
            full[layer] = full[layer].reshape(-1, 3 * part)
        return full, lax.all_gather(extra, ALL, axis=0, tiled=True)
    with_extra = jnp.broadcast_to(extra[None], (heads, own, extra.shape[1]))
    extra_moved = lax.all_to_all(with_extra, "head", split_axis=0, concat_axis=0, tiled=True)
    extra_full = None
    for layer in range(layers):
        piece = moved[:, layer]
        if layer == 0:
            piece = jnp.concatenate([piece, extra_moved], axis=2)
        along = gather_over(piece, "batch")
        other = swapped(along, "blk", 1)
        mine = lax.axis_index("blk") == 0
        both = jnp.stack(
            [jnp.where(mine, along, other), jnp.where(mine, other, along)], axis=1
        ).reshape(-1, piece.shape[-1])
        full.append(both[:, : 3 * part])
        if layer == 0:
            extra_full = both[:, 3 * part :]
    return full, extra_full


def scatter_over(parts, axis):
    size = lax.axis_size(axis)
    me = lax.axis_index(axis)
    total = pick(parts, me).astype(F32)
    for mask in range(1, size):
        total = total + swapped(pick(parts, me ^ mask).astype(BF16), axis, mask).astype(F32)
    return total


def scatter_qkv(grad):
    heads = lax.axis_size("head")
    part = grad.shape[1] // 3
    if small_slice():
        parts = grad.reshape(4, 2, -1, 3 * part).transpose(1, 0, 2, 3)
        summed = scatter_over(scatter_over(parts, "blk"), "batch").astype(BF16)
    else:
        summed = lax.psum_scatter(grad.astype(BF16), REST, scatter_dimension=0, tiled=True)
    own = summed.shape[0] // heads
    moved = lax.all_to_all(
        summed.reshape(heads, own, 3 * part), "head", split_axis=0, concat_axis=0, tiled=True
    )
    return (
        moved.reshape(heads, own, 3, part)
        .transpose(1, 2, 0, 3)
        .reshape(own, 3 * heads * part)
        .astype(F32)
    )


def scatter_dense(grad, spread):
    if not (spread and small_slice()):
        return lax.psum_scatter(grad.astype(BF16), ALL, scatter_dimension=0, tiled=True).astype(F32)
    columns = grad.shape[1]
    core = lax.axis_index("head") % 2
    row = lax.axis_index("head") // 2
    parts = grad.reshape(4, 2, 2, 2, -1, columns)
    cored = (
        pick(parts, core, 3).astype(F32)
        + swapped(pick(parts, 1 - core, 3).astype(BF16), "head", 1).astype(F32)
    ).astype(BF16)
    half = columns // 2
    first, second = cored[..., :half], cored[..., half:]
    blk = lax.axis_index("blk")

    def over_blk(part, dim):
        got = swapped(pick(part, 1 - blk, dim).astype(BF16), "blk", 1).astype(F32)
        return pick(part, blk, dim).astype(F32) + got

    def over_row(part, dim):
        got = swapped(pick(part, 1 - row, dim).astype(BF16), "head", 2).astype(F32)
        return pick(part, row, dim).astype(F32) + got

    first = over_row(over_blk(first, 1), 1)
    second = over_blk(over_row(second, 2), 1)
    return scatter_over(jnp.concatenate([first, second], axis=-1), "batch")


def sum_all(array):
    if not small_slice():
        return lax.psum(array, ALL)
    for axis, mask in (("head", 1), ("head", 2), ("blk", 1), ("batch", 1), ("batch", 2)):
        array = array + swapped(array, axis, mask)
    return array


def window_mask(plan, segments, block_index):
    key_count = plan.length + plan.reach * plan.block
    if plan.whole:
        query_segs, key_segs = segments, segments
    else:
        leading = jnp.full((plan.own_seqs, plan.reach * plan.block), -1, jnp.int32)
        padded = jnp.concatenate([leading, segments], axis=1)
        start = block_index * plan.block
        query_segs = lax.dynamic_slice_in_dim(segments, start, plan.block, 1)
        key_segs = lax.dynamic_slice_in_dim(padded, start, key_count, 1)
    query_place = jnp.arange(plan.length, dtype=jnp.int32)[:, None] + plan.reach * plan.block
    key_place = jnp.arange(key_count, dtype=jnp.int32)[None, :]
    near = (key_place <= query_place) & (query_place - key_place < WINDOW)
    return (key_segs[:, None, :] == query_segs[:, :, None]) & near[None]


def with_earlier(plan, own):
    arrived = [own]
    for _ in range(plan.reach):
        arrived.append(shifted(arrived[-1], "blk", 1))
    return jnp.concatenate(arrived[::-1], axis=1) if plan.reach else own


def to_earlier(plan, grads):
    if not plan.reach:
        return grads
    block = plan.block
    total = grads[:, :block]
    for step in range(1, plan.reach + 1):
        total = (
            shifted(total.astype(BF16), "blk", -1).astype(F32)
            + grads[:, step * block : (step + 1) * block]
        )
    return total


def scores_of(queries, keys, allowed):
    scores = jnp.einsum("sqhd,skhd->shqk", queries, keys, preferred_element_type=F32)
    return jnp.where(allowed[:, None], scores, MASKED_SCORE)


def attend(queries, keys, values, allowed):
    scores = scores_of(queries, keys, allowed)
    top_score = jnp.max(scores, axis=-1, keepdims=True)
    exp_terms = jnp.exp(scores - top_score)
    totals = jnp.sum(exp_terms, axis=-1, keepdims=True)
    probs_low = (exp_terms / totals).astype(BF16)
    attended = jnp.einsum("shqk,skhd->sqhd", probs_low, values, preferred_element_type=F32)
    return attended, top_score + jnp.log(totals)


def attend_back(queries, keys, values, allowed, log_total, attended_grad):
    probs = jnp.exp(scores_of(queries, keys, allowed) - log_total)
    probs_low = probs.astype(BF16)
    values_grad = jnp.einsum(
        "shqk,sqhd->skhd", probs_low, attended_grad, preferred_element_type=F32
    )
    probs_grad = jnp.einsum("sqhd,skhd->shqk", attended_grad, values, preferred_element_type=F32)
    row_dot = jnp.sum(probs_grad * probs, axis=-1, keepdims=True)
    scores_low = (probs * (probs_grad - row_dot)).astype(BF16)
    queries_grad = jnp.einsum("shqk,skhd->sqhd", scores_low, keys, preferred_element_type=F32)
    keys_grad = jnp.einsum("shqk,sqhd->skhd", scores_low, queries, preferred_element_type=F32)
    return queries_grad, keys_grad, values_grad


def forward(plan, stream, qkv, dense, gains, scale_vec, allowed):
    width = plan.width
    head_dim = scale_vec.shape[0]
    part = qkv.shape[1] // 3
    local_heads = part // head_dim
    split = (plan.own_seqs, plan.length, local_heads, head_dim)
    out_w, up_w, down_w = dense[:, :width], dense[:, width:-width], dense[:, -width:]
    normed, factor_one = normalize(stream, gains[0])
    normed_all = gather_tokens(plan, normed.astype(BF16))
    projected = dot(normed_all, qkv)
    query_pre = projected[:, :part].reshape(split)
    queries = (query_pre * scale_vec).astype(BF16)
    keys = with_earlier(plan, projected[:, part : 2 * part].astype(BF16).reshape(split))
    values = with_earlier(plan, projected[:, 2 * part :].astype(BF16).reshape(split))
    attended_part, log_total = attend(queries, keys, values, allowed)
    attended = heads_to_tokens(plan, attended_part.astype(BF16).reshape(-1, part))
    middle = stream + dot(attended, out_w)
    normed_two, factor_two = normalize(middle, gains[1])
    normed_two = normed_two.astype(BF16)
    hidden = dot(normed_two, up_w)
    active = (hidden * jax.nn.sigmoid(hidden)).astype(BF16)
    result = middle + dot(active, down_w)
    kept = (
        stream, factor_one, normed_all, query_pre, queries, keys, values, log_total,
        attended, middle, factor_two, normed_two, hidden, active,
    )
    return result, kept


def backward(plan, upper, kept, qkv, dense, gains, scale_vec, allowed, spread):
    (
        stream, factor_one, normed_all, query_pre, queries, keys, values, log_total,
        attended, middle, factor_two, normed_two, hidden, active,
    ) = kept
    width = plan.width
    head_dim = scale_vec.shape[0]
    part = qkv.shape[1] // 3
    out_w, up_w, down_w = dense[:, :width], dense[:, width:-width], dense[:, -width:]
    upper_low = upper.astype(BF16)
    down_grad = dot_rows(active, upper_low)
    active_grad = dot_cols(upper_low, down_w)
    gate = jax.nn.sigmoid(hidden)
    hidden_low = (active_grad * gate * (1.0 + hidden * (1.0 - gate))).astype(BF16)
    up_grad = dot_rows(normed_two, hidden_low)
    extra_two = norm_back(dot_cols(hidden_low, up_w), middle, factor_two, gains[1])
    middle_grad = upper + extra_two
    middle_low = middle_grad.astype(BF16)
    out_grad = dot_rows(attended, middle_low)
    dense_grad = jnp.concatenate([out_grad, up_grad, down_grad], axis=1).astype(BF16)
    dense_own = scatter_dense(dense_grad, spread)
    attended_grad = tokens_to_heads(plan, dot_cols(middle_low, out_w).astype(BF16))
    queries_grad, keys_grad, values_grad = attend_back(
        queries, keys, values, allowed, log_total, attended_grad.reshape(queries.shape)
    )
    query_bar = queries_grad.astype(BF16).astype(F32)
    scale_vec_grad = jnp.sum((query_bar * query_pre).reshape(-1, head_dim), axis=0)
    query_low = (query_bar * scale_vec).astype(BF16).reshape(-1, part)
    keys_low = to_earlier(plan, keys_grad).astype(BF16).reshape(-1, part)
    values_low = to_earlier(plan, values_grad).astype(BF16).reshape(-1, part)
    projected_low = jnp.concatenate([query_low, keys_low, values_low], axis=1)
    normed_grad = scatter_tokens(plan, dot_cols(projected_low, qkv))
    qkv_own = scatter_qkv(dot_rows(normed_all, projected_low))
    lower = middle_grad + norm_back(normed_grad, stream, factor_one, gains[0])
    return lower, qkv_own, dense_own, scale_vec_grad


def per_device(
    tokens,
    segments,
    qkv_weight,
    out_weight,
    up_weight,
    down_weight,
    attn_gain,
    mlp_gain,
    scale_param,
    cotangent,
):
    plan = Plan(tokens)
    layers, head_dim = scale_param.shape
    block_index = lax.axis_index("blk")
    scale_vecs = SCALE_BASE / math.sqrt(head_dim) * jax.nn.softplus(scale_param)
    own_gains = jnp.concatenate([attn_gain, mlp_gain], axis=0)
    qkvs, gains = gather_qkv(qkv_weight, own_gains.T)
    gains = gains.T.astype(F32)
    if plan.whole:
        segments = lax.dynamic_slice_in_dim(
            segments, block_index * plan.own_seqs, plan.own_seqs, 0
        )
    allowed = window_mask(plan, segments, block_index)
    stream = to_plan(plan, tokens).astype(F32)
    denses, kept = [], []
    for layer in range(layers):
        own = jnp.concatenate([out_weight[layer], up_weight[layer], down_weight[layer]], axis=1)
        denses.append(lax.all_gather(own, ALL, axis=0, tiled=True))
        layer_gains = (gains[layer], gains[layers + layer])
        stream, saved = forward(
            plan, stream, qkvs[layer], denses[layer], layer_gains, scale_vecs[layer], allowed
        )
        kept.append(saved)
    layer_out = from_plan(plan, stream.astype(BF16))
    upper = to_plan(plan, cotangent).astype(F32)
    qkv_grads, dense_grads = [None] * layers, [None] * layers
    scale_grads = [None] * layers
    for layer in reversed(range(layers)):
        layer_gains = (gains[layer], gains[layers + layer])
        upper, qkv_grads[layer], dense_grads[layer], scale_grads[layer] = backward(
            plan, upper, kept[layer], qkvs[layer], denses[layer], layer_gains,
            scale_vecs[layer], allowed, layer == 0,
        )
    input_grad = from_plan(plan, upper.astype(BF16)).astype(F32)
    scale_total = sum_all(jnp.stack(scale_grads))
    scale_grad = scale_total * (SCALE_BASE / math.sqrt(head_dim)) * jax.nn.sigmoid(scale_param)
    dense_all = jnp.stack(dense_grads)
    qkv_all = jnp.stack(qkv_grads)
    width = plan.width
    up_all = dense_all[:, :, width:-width]
    return (
        layer_out,
        input_grad,
        qkv_all,
        dense_all[:, :, :width],
        up_all,
        dense_all[:, :, -width:],
        gain_grad(qkv_weight, qkv_all, attn_gain),
        gain_grad(up_weight, up_all, mlp_gain),
        scale_grad,
    )


def solution(mesh):
    rows = P(None, ALL, None)
    by_token = P("batch", ("blk", "head"), None)
    return jax.shard_map(
        per_device,
        mesh=mesh,
        in_specs=(
            by_token, P("batch", None), rows, rows, rows, rows, P(None, ALL), P(None, ALL), P(),
            by_token,
        ),
        out_specs=(
            by_token, by_token, rows, rows, rows, rows, P(None, ALL), P(None, ALL), P(),
        ),
        check_vma=False,
    )
```

```python
import functools
import math

import jax
import jax.numpy as jnp
from jax import lax
from jax.experimental import pallas as pl
from jax.experimental.pallas import tpu as pltpu
from jax.sharding import PartitionSpec as P

WINDOW = 1024
EPSILON = 1e-06
SCALE_BASE = 1.4426950408889634
MASKED_SCORE = -1e30

ALL = ("batch", "blk", "head")
REST = ("batch", "blk")
F32 = jnp.float32
BF16 = jnp.bfloat16


def shifted(block, axis, distance):
    devices = range(lax.axis_size(axis))
    route = [(i - distance, i) for i in devices if i - distance in devices]
    return lax.ppermute(block, axis, route)


NT = (((1,), (1,)), ((), ()))
TN = (((0,), (0,)), ((), ()))


def dot(left, right):
    return jnp.dot(left, right, preferred_element_type=F32)


def dot_rows(left, right):
    return lax.dot_general(left, right, (((0,), (0,)), ((), ())), preferred_element_type=F32)


def dot_cols(left, right):
    return lax.dot_general(left, right, (((1,), (1,)), ((), ())), preferred_element_type=F32)


def normalize(stream, gain):
    factor = lax.rsqrt(jnp.mean(stream * stream, axis=-1, keepdims=True) + EPSILON)
    return stream * factor * gain, factor


def norm_back(upper, stream, factor, gain):
    inner = upper * gain
    gain_grad = jnp.sum(upper * stream * factor, axis=0)
    lower = factor * inner - stream * factor * factor * factor * jnp.mean(
        inner * stream, axis=-1, keepdims=True
    )
    return lower, gain_grad


class Plan:
    def __init__(self, tokens):
        self.seqs, self.rows, self.width = tokens.shape
        self.heads = lax.axis_size("head")
        self.blks = lax.axis_size("blk")
        self.block = self.rows * self.heads
        self.whole = self.seqs % self.blks == 0
        if self.whole:
            self.groups, self.own_seqs = self.blks, self.seqs // self.blks
            self.reach = 0
        else:
            self.groups, self.own_seqs = 1, self.seqs
            self.reach = min((WINDOW - 1) // self.block + 1, self.blks - 1)
        self.length = self.groups * self.block
        self.tokens = self.seqs * self.rows


def to_plan(plan, array):
    if plan.whole and plan.blks > 1:
        array = lax.all_to_all(array, "blk", split_axis=0, concat_axis=0, tiled=True)
    return array.reshape(plan.tokens, plan.width)


def from_plan(plan, flat):
    array = flat.reshape(plan.seqs, plan.rows, plan.width)
    if plan.whole and plan.blks > 1:
        array = lax.all_to_all(array, "blk", split_axis=0, concat_axis=0, tiled=True)
    return array


def in_sequence(plan, by_head, width):
    parts = by_head.reshape(plan.heads, plan.groups, plan.own_seqs, plan.rows, width)
    return parts.transpose(2, 1, 0, 3, 4).reshape(-1, width)


def by_owner(plan, rows, width):
    parts = rows.reshape(plan.own_seqs, plan.groups, plan.heads, plan.rows, width)
    return parts.transpose(2, 1, 0, 3, 4).reshape(plan.heads, plan.tokens, width)


def gather_tokens(plan, rows):
    moved = lax.all_gather(rows, "head", axis=0, tiled=False)
    return in_sequence(plan, moved, rows.shape[-1])


def scatter_tokens(plan, rows):
    width = rows.shape[-1]
    return lax.psum_scatter(
        by_owner(plan, rows.astype(BF16), width), "head", scatter_dimension=0, tiled=False
    ).astype(F32)


def heads_to_tokens(plan, rows):
    part = rows.shape[-1]
    moved = lax.all_to_all(
        by_owner(plan, rows, part), "head", split_axis=0, concat_axis=0, tiled=True
    )
    return moved.transpose(1, 0, 2).reshape(plan.tokens, plan.heads * part)


def tokens_to_heads(plan, rows):
    part = rows.shape[-1] // plan.heads
    sent = rows.reshape(plan.tokens, plan.heads, part).transpose(1, 0, 2)
    moved = lax.all_to_all(sent, "head", split_axis=0, concat_axis=0, tiled=True)
    return in_sequence(plan, moved, part)


def gather_qkv(rows):
    own, width = rows.shape
    heads = lax.axis_size("head")
    part = width // 3 // heads
    sent = rows.reshape(own, 3, heads, part).transpose(2, 0, 1, 3).reshape(heads, own, 3 * part)
    moved = lax.all_to_all(sent, "head", split_axis=0, concat_axis=0, tiled=True)
    full = lax.all_gather(moved, REST, axis=0, tiled=True)
    return full.reshape(-1, 3 * part)


def scatter_qkv(grad):
    heads = lax.axis_size("head")
    part = grad.shape[1] // 3
    summed = lax.psum_scatter(grad.astype(BF16), REST, scatter_dimension=0, tiled=True)
    own = summed.shape[0] // heads
    moved = lax.all_to_all(
        summed.reshape(heads, own, 3 * part), "head", split_axis=0, concat_axis=0, tiled=True
    )
    return (
        moved.reshape(heads, own, 3, part)
        .transpose(1, 2, 0, 3)
        .reshape(own, 3 * heads * part)
        .astype(F32)
    )


def window_mask(plan, segments, block_index):
    key_count = plan.length + plan.reach * plan.block
    if plan.whole:
        query_segs, key_segs = segments, segments
    else:
        leading = jnp.full((plan.own_seqs, plan.reach * plan.block), -1, jnp.int32)
        padded = jnp.concatenate([leading, segments], axis=1)
        start = block_index * plan.block
        query_segs = lax.dynamic_slice_in_dim(segments, start, plan.block, 1)
        key_segs = lax.dynamic_slice_in_dim(padded, start, key_count, 1)
    query_place = jnp.arange(plan.length, dtype=jnp.int32)[:, None] + plan.reach * plan.block
    key_place = jnp.arange(key_count, dtype=jnp.int32)[None, :]
    near = (key_place <= query_place) & (query_place - key_place < WINDOW)
    return (key_segs[:, None, :] == query_segs[:, :, None]) & near[None]


def with_earlier(plan, own):
    arrived = [own]
    for _ in range(plan.reach):
        arrived.append(shifted(arrived[-1], "blk", 1))
    return jnp.concatenate(arrived[::-1], axis=1) if plan.reach else own


def to_earlier(plan, grads):
    if not plan.reach:
        return grads
    block = plan.block
    total = grads[:, :block]
    for step in range(1, plan.reach + 1):
        total = (
            shifted(total.astype(BF16), "blk", -1).astype(F32)
            + grads[:, step * block : (step + 1) * block]
        )
    return total


def scores_of(queries, keys, allowed):
    scores = jnp.einsum("sqhd,skhd->shqk", queries, keys, preferred_element_type=F32)
    return jnp.where(allowed[:, None], scores, MASKED_SCORE)


def attend(queries, keys, values, allowed):
    scores = scores_of(queries, keys, allowed)
    top_score = jnp.max(scores, axis=-1, keepdims=True)
    exp_terms = jnp.exp(scores - top_score)
    totals = jnp.sum(exp_terms, axis=-1, keepdims=True)
    probs_low = (exp_terms / totals).astype(BF16)
    attended = jnp.einsum("shqk,skhd->sqhd", probs_low, values, preferred_element_type=F32)
    return attended, top_score + jnp.log(totals)


def attend_back(queries, keys, values, allowed, log_total, attended_grad):
    probs = jnp.exp(scores_of(queries, keys, allowed) - log_total)
    probs_low = probs.astype(BF16)
    values_grad = jnp.einsum(
        "shqk,sqhd->skhd", probs_low, attended_grad, preferred_element_type=F32
    )
    probs_grad = jnp.einsum("sqhd,skhd->shqk", attended_grad, values, preferred_element_type=F32)
    row_dot = jnp.sum(probs_grad * probs, axis=-1, keepdims=True)
    scores_low = (probs * (probs_grad - row_dot)).astype(BF16)
    queries_grad = jnp.einsum("shqk,skhd->sqhd", scores_low, keys, preferred_element_type=F32)
    keys_grad = jnp.einsum("shqk,sqhd->skhd", scores_low, queries, preferred_element_type=F32)
    return queries_grad, keys_grad, values_grad


def forward(plan, stream, qkv, dense, gains, scale_vec, allowed):
    width = plan.width
    head_dim = scale_vec.shape[0]
    part = qkv.shape[1] // 3
    local_heads = part // head_dim
    split = (plan.own_seqs, plan.length, local_heads, head_dim)
    out_w, up_w, down_w = dense[:, :width], dense[:, width:-width], dense[:, -width:]
    normed, factor_one = normalize(stream, gains[0])
    normed_all = gather_tokens(plan, normed.astype(BF16))
    projected = dot(normed_all, qkv)
    query_pre = projected[:, :part].reshape(split)
    queries = (query_pre * scale_vec).astype(BF16)
    keys = with_earlier(plan, projected[:, part : 2 * part].astype(BF16).reshape(split))
    values = with_earlier(plan, projected[:, 2 * part :].astype(BF16).reshape(split))
    attended_part, log_total = attend(queries, keys, values, allowed)
    attended = heads_to_tokens(plan, attended_part.astype(BF16).reshape(-1, part))
    middle = stream + dot(attended, out_w)
    normed_two, factor_two = normalize(middle, gains[1])
    normed_two = normed_two.astype(BF16)
    hidden = dot(normed_two, up_w)
    active = (hidden * jax.nn.sigmoid(hidden)).astype(BF16)
    result = middle + dot(active, down_w)
    kept = (
        stream, factor_one, normed_all, query_pre, queries, keys, values, log_total,
        attended, middle, factor_two, normed_two, hidden, active,
    )
    return result, kept


def backward(plan, upper, kept, qkv, dense, gains, scale_vec, allowed):
    (
        stream, factor_one, normed_all, query_pre, queries, keys, values, log_total,
        attended, middle, factor_two, normed_two, hidden, active,
    ) = kept
    width = plan.width
    head_dim = scale_vec.shape[0]
    part = qkv.shape[1] // 3
    out_w, up_w, down_w = dense[:, :width], dense[:, width:-width], dense[:, -width:]
    upper_low = upper.astype(BF16)
    down_grad = dot_rows(active, upper_low)
    active_grad = dot_cols(upper_low, down_w)
    gate = jax.nn.sigmoid(hidden)
    hidden_low = (active_grad * gate * (1.0 + hidden * (1.0 - gate))).astype(BF16)
    up_grad = dot_rows(normed_two, hidden_low)
    extra_two, mlp_gain_grad = norm_back(dot_cols(hidden_low, up_w), middle, factor_two, gains[1])
    middle_grad = upper + extra_two
    middle_low = middle_grad.astype(BF16)
    out_grad = dot_rows(attended, middle_low)
    dense_grad = jnp.concatenate([out_grad, up_grad, down_grad], axis=1).astype(BF16)
    dense_own = lax.psum_scatter(dense_grad, ALL, scatter_dimension=0, tiled=True)
    attended_grad = tokens_to_heads(plan, dot_cols(middle_low, out_w).astype(BF16))
    queries_grad, keys_grad, values_grad = attend_back(
        queries, keys, values, allowed, log_total, attended_grad.reshape(queries.shape)
    )
    query_bar = queries_grad.astype(BF16).astype(F32)
    scale_vec_grad = jnp.sum((query_bar * query_pre).reshape(-1, head_dim), axis=0)
    query_low = (query_bar * scale_vec).astype(BF16).reshape(-1, part)
    keys_low = to_earlier(plan, keys_grad).astype(BF16).reshape(-1, part)
    values_low = to_earlier(plan, values_grad).astype(BF16).reshape(-1, part)
    projected_low = jnp.concatenate([query_low, keys_low, values_low], axis=1)
    normed_grad = scatter_tokens(plan, dot_cols(projected_low, qkv))
    qkv_own = scatter_qkv(dot_rows(normed_all, projected_low))
    extra_one, attn_gain_grad = norm_back(normed_grad, stream, factor_one, gains[0])
    lower = middle_grad + extra_one
    return lower, qkv_own, dense_own, (attn_gain_grad, mlp_gain_grad), scale_vec_grad


def general_device(
    tokens,
    segments,
    qkv_weight,
    out_weight,
    up_weight,
    down_weight,
    attn_gain,
    mlp_gain,
    scale_param,
    cotangent,
):
    plan = Plan(tokens)
    layers, head_dim = scale_param.shape
    block_index = lax.axis_index("blk")
    scale_vecs = SCALE_BASE / math.sqrt(head_dim) * jax.nn.softplus(scale_param)
    own_gains = jnp.concatenate([attn_gain, mlp_gain], axis=0)
    gains = (
        lax.all_gather(own_gains.reshape(1, -1), ALL, axis=0, tiled=True)
        .reshape(-1, 2 * layers, attn_gain.shape[1])
        .transpose(1, 0, 2)
        .reshape(2 * layers, plan.width)
        .astype(F32)
    )
    if plan.whole:
        segments = lax.dynamic_slice_in_dim(
            segments, block_index * plan.own_seqs, plan.own_seqs, 0
        )
    allowed = window_mask(plan, segments, block_index)
    stream = to_plan(plan, tokens).astype(F32)
    qkvs, denses, kept = [], [], []
    for layer in range(layers):
        qkvs.append(gather_qkv(qkv_weight[layer]))
        own = jnp.concatenate([out_weight[layer], up_weight[layer], down_weight[layer]], axis=1)
        denses.append(lax.all_gather(own, ALL, axis=0, tiled=True))
        layer_gains = (gains[layer], gains[layers + layer])
        stream, saved = forward(
            plan, stream, qkvs[layer], denses[layer], layer_gains, scale_vecs[layer], allowed
        )
        kept.append(saved)
    layer_out = from_plan(plan, stream.astype(BF16))
    upper = to_plan(plan, cotangent).astype(F32)
    qkv_grads, dense_grads = [None] * layers, [None] * layers
    gain_grads, scale_grads = [None] * layers, [None] * layers
    for layer in reversed(range(layers)):
        layer_gains = (gains[layer], gains[layers + layer])
        upper, qkv_grads[layer], dense_grads[layer], gain_grads[layer], scale_grads[layer] = (
            backward(
                plan, upper, kept[layer], qkvs[layer], denses[layer], layer_gains,
                scale_vecs[layer], allowed,
            )
        )
    input_grad = from_plan(plan, upper.astype(BF16)).astype(F32)
    small = jnp.concatenate(
        [g[0] for g in gain_grads] + [g[1] for g in gain_grads] + scale_grads, axis=0
    )
    total = lax.psum(small, ALL)
    gain_total = total[: 2 * layers * plan.width].reshape(2 * layers, plan.width)
    owner = lax.axis_index(ALL)
    gain_rows = attn_gain.shape[1]
    own_total = lax.dynamic_slice_in_dim(gain_total, owner * gain_rows, gain_rows, 1)
    scale_total = total[2 * layers * plan.width :].reshape(layers, head_dim)
    scale_grad = scale_total * (SCALE_BASE / math.sqrt(head_dim)) * jax.nn.sigmoid(scale_param)
    dense_all = jnp.stack(dense_grads).astype(F32)
    width = plan.width
    return (
        layer_out,
        input_grad,
        jnp.stack(qkv_grads),
        dense_all[:, :, :width],
        dense_all[:, :, width:-width],
        dense_all[:, :, -width:],
        own_total[:layers],
        own_total[layers:],
        scale_grad,
    )


Q_ROWS = 256
KERNEL = pltpu.CompilerParams(vmem_limit_bytes=50 * 1024 * 1024)


def allowed_keys(col, row, first):
    count = first + row.shape[1]
    key_place = lax.broadcasted_iota(jnp.int32, (count, row.shape[1]), 0)
    query_place = lax.broadcasted_iota(jnp.int32, (count, row.shape[1]), 1) + first
    return (col[:count] == row) & (key_place <= query_place)


def token_places(length, heads, token_rows):
    for first in range(0, length, Q_ROWS):
        parts = []
        for start in range(0, Q_ROWS, token_rows):
            place = (first + start) // token_rows
            parts.append((start, place % heads, place // heads * token_rows))
        yield first, parts


def attend_kernel(token_rows, proj_ref, scale_ref, col_ref, row_ref, out_ref, lse_ref):
    length = proj_ref.shape[-1]
    queries = (proj_ref[0, 0] * scale_ref[...]).astype(BF16)
    keys = proj_ref[1, 0].T.astype(BF16)
    values = proj_ref[2, 0].astype(BF16)
    for first, parts in token_places(length, out_ref.shape[0], token_rows):
        end = first + Q_ROWS
        scores = jnp.dot(keys[:end], queries[:, first:end], preferred_element_type=F32)
        allowed = allowed_keys(col_ref[...], row_ref[:, first:end], first)
        scores = jnp.where(allowed, scores, MASKED_SCORE)
        top = jnp.max(scores, axis=0, keepdims=True)
        terms = jnp.exp(scores - top)
        total = jnp.sum(terms, axis=0, keepdims=True)
        probs = (terms * (1.0 / total)).astype(BF16)
        attended = jnp.dot(values[:, :end], probs, preferred_element_type=F32).astype(BF16)
        lse_ref[0, :, first:end] = top + jnp.log(total)
        for start, owner, offset in parts:
            out_ref[owner, 0, :, offset : offset + token_rows] = attended[
                :, start : start + token_rows
            ]


def attend_rows(projected, scale_vec, segments, owners, token_rows):
    head_dim = scale_vec.shape[0]
    length = projected.shape[1]
    local_heads = projected.shape[0] // 3 // head_dim
    tokens = length // owners
    attended, log_total = pl.pallas_call(
        functools.partial(attend_kernel, token_rows),
        grid=(local_heads,),
        in_specs=[
            pl.BlockSpec((3, 1, head_dim, length), lambda h: (0, h, 0, 0)),
            pl.BlockSpec((head_dim, 1), lambda h: (0, 0)),
            pl.BlockSpec((length, 1), lambda h: (0, 0)),
            pl.BlockSpec((1, length), lambda h: (0, 0)),
        ],
        out_specs=[
            pl.BlockSpec((owners, 1, head_dim, tokens), lambda h: (0, h, 0, 0)),
            pl.BlockSpec((1, 1, length), lambda h: (h, 0, 0)),
        ],
        out_shape=[
            jax.ShapeDtypeStruct((owners, local_heads, head_dim, tokens), BF16),
            jax.ShapeDtypeStruct((local_heads, 1, length), F32),
        ],
        compiler_params=KERNEL,
        cost_estimate=pl.CostEstimate(
            flops=4 * local_heads * length * length * head_dim,
            bytes_accessed=projected.size * 4,
            transcendentals=local_heads * length * length // 2,
        ),
    )(
        projected.reshape(3, local_heads, head_dim, length),
        scale_vec.reshape(head_dim, 1),
        segments.reshape(length, 1),
        segments.reshape(1, length),
    )
    return attended.reshape(owners, local_heads * head_dim, tokens), log_total


def attend_back_kernel(
    token_rows,
    proj_ref,
    grad_ref,
    lse_ref,
    scale_ref,
    col_ref,
    row_ref,
    out_ref,
    scale_grad_ref,
    keys_acc,
    values_acc,
):
    length = proj_ref.shape[-1]
    scale = scale_ref[...]
    query_pre = proj_ref[0, 0]
    queries = (query_pre * scale).astype(BF16)
    keys_t = proj_ref[1, 0].astype(BF16)
    keys = proj_ref[1, 0].T.astype(BF16)
    values = proj_ref[2, 0].T.astype(BF16)
    keys_acc[...] = jnp.zeros_like(keys_acc)
    values_acc[...] = jnp.zeros_like(values_acc)
    scale_grad = jnp.zeros((scale.shape[0], 1), F32)
    for first, parts in token_places(length, grad_ref.shape[0], token_rows):
        end = first + Q_ROWS
        block = queries[:, first:end]
        grad = jnp.concatenate(
            [grad_ref[owner, 0, :, at : at + token_rows] for _, owner, at in parts], axis=1
        )
        scores = jnp.dot(keys[:end], block, preferred_element_type=F32)
        allowed = allowed_keys(col_ref[...], row_ref[:, first:end], first)
        scores = jnp.where(allowed, scores, MASKED_SCORE)
        probs = jnp.exp(scores - lse_ref[0, :, first:end])
        probs_grad = jnp.dot(values[:end], grad, preferred_element_type=F32)
        row_dot = jnp.sum(probs_grad * probs, axis=0, keepdims=True)
        scores_low = (probs * (probs_grad - row_dot)).astype(BF16)
        values_acc[:, :end] += lax.dot_general(
            grad, probs.astype(BF16), NT, preferred_element_type=F32
        )
        keys_acc[:, :end] += lax.dot_general(
            block, scores_low, NT, preferred_element_type=F32
        )
        query_bar = jnp.dot(keys_t[:, :end], scores_low, preferred_element_type=F32)
        query_bar = query_bar.astype(BF16).astype(F32)
        scale_grad += jnp.sum(query_bar * query_pre[:, first:end], axis=1, keepdims=True)
        out_ref[0, 0, :, first:end] = (query_bar * scale).astype(BF16)
    out_ref[1, 0] = keys_acc[...].astype(BF16)
    out_ref[2, 0] = values_acc[...].astype(BF16)
    spread = jnp.broadcast_to(scale_grad, scale_grad_ref.shape)

    @pl.when(pl.program_id(0) == 0)
    def _():
        scale_grad_ref[...] = spread

    @pl.when(pl.program_id(0) > 0)
    def _():
        scale_grad_ref[...] += spread


def attend_back_rows(projected, attended_grad, log_total, scale_vec, segments, token_rows):
    head_dim = scale_vec.shape[0]
    length = projected.shape[1]
    local_heads = projected.shape[0] // 3 // head_dim
    owners, _, tokens = attended_grad.shape
    lanes = 128
    grads, scale_grad = pl.pallas_call(
        functools.partial(attend_back_kernel, token_rows),
        grid=(local_heads,),
        in_specs=[
            pl.BlockSpec((3, 1, head_dim, length), lambda h: (0, h, 0, 0)),
            pl.BlockSpec((owners, 1, head_dim, tokens), lambda h: (0, h, 0, 0)),
            pl.BlockSpec((1, 1, length), lambda h: (h, 0, 0)),
            pl.BlockSpec((head_dim, 1), lambda h: (0, 0)),
            pl.BlockSpec((length, 1), lambda h: (0, 0)),
            pl.BlockSpec((1, length), lambda h: (0, 0)),
        ],
        out_specs=[
            pl.BlockSpec((3, 1, head_dim, length), lambda h: (0, h, 0, 0)),
            pl.BlockSpec((head_dim, lanes), lambda h: (0, 0)),
        ],
        out_shape=[
            jax.ShapeDtypeStruct((3, local_heads, head_dim, length), BF16),
            jax.ShapeDtypeStruct((head_dim, lanes), F32),
        ],
        scratch_shapes=[
            pltpu.VMEM((head_dim, length), F32),
            pltpu.VMEM((head_dim, length), F32),
        ],
        compiler_params=KERNEL,
        cost_estimate=pl.CostEstimate(
            flops=10 * local_heads * length * length * head_dim,
            bytes_accessed=projected.size * 6,
            transcendentals=local_heads * length * length // 2,
        ),
    )(
        projected.reshape(3, local_heads, head_dim, length),
        attended_grad.reshape(owners, local_heads, head_dim, tokens),
        log_total,
        scale_vec.reshape(head_dim, 1),
        segments.reshape(length, 1),
        segments.reshape(1, length),
    )
    return grads.reshape(3 * local_heads * head_dim, length), scale_grad[:, 0]


def dense_grad_kernel(attended_ref, normed_ref, active_ref, out_bar, up_bar, down_bar, grad_ref):
    width = out_bar.shape[1]
    grad_ref[:, :width] = jnp.dot(
        attended_ref[...], out_bar[...], preferred_element_type=F32
    ).astype(BF16)
    grad_ref[:, width : 2 * width] = lax.dot_general(
        normed_ref[...], up_bar[...], TN, preferred_element_type=F32
    ).astype(BF16)
    grad_ref[:, 2 * width :] = lax.dot_general(
        active_ref[...], down_bar[...], TN, preferred_element_type=F32
    ).astype(BF16)


def dense_grads(attended_t, normed, active, out_bar, up_bar, down_bar):
    width, tokens = attended_t.shape
    tile = 256
    whole = pl.BlockSpec((tokens, width), lambda i: (0, 0))
    columns = pl.BlockSpec((tokens, tile), lambda i: (0, i))
    return pl.pallas_call(
        dense_grad_kernel,
        grid=(width // tile,),
        in_specs=[
            pl.BlockSpec((tile, tokens), lambda i: (i, 0)), columns, columns, whole, whole, whole,
        ],
        out_specs=pl.BlockSpec((tile, 3 * width), lambda i: (i, 0)),
        out_shape=jax.ShapeDtypeStruct((width, 3 * width), BF16),
        compiler_params=KERNEL,
        cost_estimate=pl.CostEstimate(
            flops=6 * tokens * width * width, bytes_accessed=6 * width * width, transcendentals=0
        ),
    )(attended_t, normed, active, out_bar, up_bar, down_bar)


def tied(*arrays):
    return lax.optimization_barrier(arrays)


def swapped(array, axis, mask):
    size = lax.axis_size(axis)
    return lax.ppermute(array, axis, [(i, i ^ mask) for i in range(size)])


def pick(array, index, axis=0):
    return lax.dynamic_index_in_dim(array, index, axis, keepdims=False)


def swap_halves(array):
    me = lax.axis_index("blk")
    got = swapped(pick(array, 1 - me), "blk", 1)
    kept = pick(array, me)
    return jnp.stack([jnp.where(me == 0, kept, got), jnp.where(me == 0, got, kept)])


def gather_rows(rows):
    width = rows.shape[-1]
    far = swapped(rows, "head", 2)
    near = swapped(rows, "head", 1)
    both = swapped(far, "head", 1)
    pieces = jnp.stack([rows, near, far, both])
    me = lax.axis_index("head")
    ordered = jnp.stack([pick(pieces, me ^ i) for i in range(4)])
    return ordered.reshape(4, 2, -1, width).transpose(1, 0, 2, 3).reshape(-1, width)


def scatter_rows(rows):
    width = rows.shape[-1]
    me = lax.axis_index("head")
    row, core = me // 2, me % 2
    parts = rows.reshape(2, 2, 2, -1, width)
    halves = pick(parts, core, 2) + swapped(
        pick(parts, 1 - core, 2).astype(BF16), "head", 1
    ).astype(F32)
    got = swapped(pick(halves, 1 - row, 1).astype(BF16), "head", 2).astype(F32)
    return (pick(halves, row, 1) + got).reshape(-1, width)


def over_head(parts):
    return lax.all_to_all(parts, "head", split_axis=0, concat_axis=0, tiled=True)


def qkv_columns(rows, extra):
    own, width = rows.shape
    part = width // 3 // 4
    sent = rows.reshape(own, 3, 4, part).transpose(2, 0, 1, 3).reshape(4, own, 3 * part)
    if extra is not None:
        sent = jnp.concatenate([sent, jnp.broadcast_to(extra[None], (4,) + extra.shape)], axis=2)
    return over_head(sent)


def gather_columns(piece, early):
    along = [piece] + [swapped(piece, "batch", mask) for mask in (1, 2, 3)]
    if early:
        across = jnp.stack([swapped(part, "blk", 1) for part in along])
        along = jnp.stack(along)
    else:
        along = jnp.stack(along)
        across = swapped(along, "blk", 1)
    me, blk = lax.axis_index("batch"), lax.axis_index("blk")
    ordered = []
    for i in range(4):
        one, two = pick(along, me ^ i), pick(across, me ^ i)
        ordered += [jnp.where(blk == 0, one, two), jnp.where(blk == 0, two, one)]
    return jnp.stack(ordered).reshape(-1, piece.shape[-1])


def scatter_over_batch(parts):
    me = lax.axis_index("batch")
    total = pick(parts, me).astype(F32)
    for mask in (1, 2, 3):
        total = total + swapped(pick(parts, me ^ mask).astype(BF16), "batch", mask).astype(F32)
    return total


def scatter_columns(grad):
    blk = lax.axis_index("blk")
    columns = grad.shape[1]
    parts = grad.reshape(4, 2, -1, columns)
    summed = pick(parts, blk, 1) + swapped(
        pick(parts, 1 - blk, 1).astype(BF16), "blk", 1
    ).astype(F32)
    summed = scatter_over_batch(summed).astype(BF16)
    moved = over_head(summed.reshape(4, -1, columns))
    own = moved.shape[1]
    return moved.reshape(4, own, 3, -1).transpose(1, 2, 0, 3).reshape(own, -1).astype(F32)


def over_core(grad):
    core = lax.axis_index("head") % 2
    parts = grad.reshape(4, 2, 2, 2, -1, grad.shape[1])
    got = swapped(pick(parts, 1 - core, 3), "head", 1).astype(F32)
    return (pick(parts, core, 3).astype(F32) + got).astype(BF16)


def over_chips(cored):
    row, blk = lax.axis_index("head") // 2, lax.axis_index("blk")
    half = cored.shape[-1] // 2

    def over(part, axis, mask, mine, dim):
        got = swapped(pick(part, 1 - mine, dim), axis, mask).astype(F32)
        return (pick(part, mine, dim).astype(F32) + got).astype(BF16)

    first = over(cored[..., :half], "blk", 1, blk, 1)
    second = over(cored[..., half:], "head", 2, row, 2)
    first = over(first, "head", 2, row, 1)
    second = over(second, "blk", 1, blk, 1)
    return scatter_over_batch(jnp.concatenate([first, second], axis=-1))


def sum_all(array):
    for axis, mask in (("head", 1), ("head", 2), ("blk", 1), ("batch", 1), ("batch", 2)):
        array = array + swapped(array, axis, mask)
    return array


def gain_back(weight, weight_grad, gain):
    return jnp.sum(weight.astype(F32) * weight_grad, axis=-1) / gain.astype(F32)


def lower_of(upper, stream, factor, gain):
    return norm_back(upper, stream, factor, gain)[0]


def spread_device(
    tokens,
    segments,
    qkv_weight,
    out_weight,
    up_weight,
    down_weight,
    attn_gain,
    mlp_gain,
    scale_param,
    cotangent,
):
    layers, head_dim = scale_param.shape
    _, token_rows, width = tokens.shape
    scale_vecs = SCALE_BASE / math.sqrt(head_dim) * jax.nn.softplus(scale_param)
    segments = pick(segments, lax.axis_index("blk"))
    own_gains = jnp.concatenate([attn_gain, mlp_gain], axis=0)

    first = swap_halves(tokens).reshape(-1, width)
    columns = [qkv_columns(qkv_weight[0], own_gains.T)]
    columns[0], first = tied(columns[0], first)
    first_all = gather_rows(first)
    stream = first.astype(F32)
    with_gains = gather_columns(columns[0].reshape(-1, columns[0].shape[-1]), True)
    part3 = 3 * width // 4
    qkvs = [with_gains[:, :part3]]
    gains = with_gains[:, part3:].T.astype(F32)
    denses = []
    for layer in range(layers):
        own = jnp.concatenate([out_weight[layer], up_weight[layer], down_weight[layer]], axis=1)
        denses.append(lax.all_gather(own, ALL, axis=0, tiled=True))

    kept = []
    for layer in range(layers):
        if layer > 0:
            piece = qkv_columns(qkv_weight[layer], None)
            piece, _ = tied(piece.reshape(-1, part3), qkvs[layer - 1])
            qkvs.append(gather_columns(piece, False))
        qkv, dense = qkvs[layer], denses[layer]
        out_w, up_w, down_w = dense[:, :width], dense[:, width:-width], dense[:, -width:]
        normed, factor_one = normalize(stream, gains[layer])
        if layer == 0:
            normed_all = normalize(first_all.astype(F32), gains[0])[0].astype(BF16)
        else:
            normed_all = gather_rows(normed.astype(BF16))
        projected = lax.dot_general(
            qkv, normed_all, (((0,), (1,)), ((), ())), preferred_element_type=F32
        )
        attended, log_total = attend_rows(
            projected, scale_vecs[layer], segments, 4, token_rows
        )
        attended_t = over_head(attended).reshape(width, -1)
        middle = stream + dot_rows(attended_t, out_w)
        normed_two, factor_two = normalize(middle, gains[layers + layer])
        normed_two = normed_two.astype(BF16)
        hidden = dot(normed_two, up_w)
        active = (hidden * jax.nn.sigmoid(hidden)).astype(BF16)
        kept.append(
            (
                stream, factor_one, normed_all, projected, log_total, attended_t, middle,
                factor_two, normed_two, hidden, active,
            )
        )
        stream = middle + dot(active, down_w)
    layer_out = swap_halves(stream.astype(BF16).reshape(tokens.shape))
    upper = swap_halves(cotangent).reshape(-1, width).astype(F32)

    qkv_grads, dense_own, scale_grads = [None] * layers, [None] * layers, [None] * layers
    for layer in reversed(range(layers)):
        (
            stream, factor_one, normed_all, projected, log_total, attended_t, middle,
            factor_two, normed_two, hidden, active,
        ) = kept[layer]
        qkv, dense = qkvs[layer], denses[layer]
        out_w, up_w, down_w = dense[:, :width], dense[:, width:-width], dense[:, -width:]
        down_bar = upper.astype(BF16)
        gate = jax.nn.sigmoid(hidden)
        up_bar = (
            dot_cols(down_bar, down_w) * gate * (1.0 + hidden * (1.0 - gate))
        ).astype(BF16)
        middle_grad = upper + lower_of(
            dot_cols(up_bar, up_w), middle, factor_two, gains[layers + layer]
        )
        out_bar = middle_grad.astype(BF16)
        attended_grad = over_head(dot_cols(out_w, out_bar).astype(BF16).reshape(4, -1, out_bar.shape[0]))
        grads = dense_grads(attended_t, normed_two, active, out_bar, up_bar, down_bar)
        attended_grad, grads = tied(attended_grad, grads)
        cored = over_core(grads) if layer == 0 else None
        bars, scale_grads[layer] = attend_back_rows(
            projected, attended_grad, log_total, scale_vecs[layer], segments, token_rows
        )
        if layer == 0:
            bars, cored = tied(bars, cored)
            dense_own[layer] = over_chips(cored)
        else:
            dense_own[layer] = lax.psum_scatter(
                grads, ALL, scatter_dimension=0, tiled=True
            ).astype(F32)
        normed_grad = scatter_rows(
            lax.dot_general(bars, qkv, (((0,), (1,)), ((), ())), preferred_element_type=F32)
        )
        qkv_grads[layer] = scatter_columns(
            lax.dot_general(normed_all, bars, (((0,), (1,)), ((), ())), preferred_element_type=F32)
        )
        upper = middle_grad + lower_of(normed_grad, stream, factor_one, gains[layer])
    input_grad = swap_halves(upper.astype(BF16).reshape(tokens.shape)).astype(F32)
    scale_total = sum_all(jnp.stack(scale_grads))
    scale_grad = scale_total * (SCALE_BASE / math.sqrt(head_dim)) * jax.nn.sigmoid(scale_param)
    dense_all = jnp.stack(dense_own)
    qkv_all = jnp.stack(qkv_grads)
    up_all = dense_all[:, :, width:-width]
    return (
        layer_out,
        input_grad,
        qkv_all,
        dense_all[:, :, :width],
        up_all,
        dense_all[:, :, -width:],
        gain_back(qkv_weight, qkv_all, attn_gain),
        gain_back(up_weight, up_all, mlp_gain),
        scale_grad,
    )


def per_device(*args):
    tokens, segments = args[0], args[1]
    sizes = tuple(lax.axis_size(axis) for axis in ALL)
    heads = tokens.shape[2] // args[8].shape[1]
    spread = (
        sizes == (4, 2, 4)
        and tokens.shape[0] == 2
        and tokens.shape[1] % 128 == 0
        and Q_ROWS % tokens.shape[1] == 0
        and segments.shape[1] <= WINDOW
        and segments.shape[1] % Q_ROWS == 0
        and heads % 4 == 0
        and tokens.shape[2] % 256 == 0
    )
    return spread_device(*args) if spread else general_device(*args)


def solution(mesh):
    rows = P(None, ALL, None)
    by_token = P("batch", ("blk", "head"), None)
    return jax.shard_map(
        per_device,
        mesh=mesh,
        in_specs=(
            by_token, P("batch", None), rows, rows, rows, rows, P(None, ALL), P(None, ALL), P(),
            by_token,
        ),
        out_specs=(
            by_token, by_token, rows, rows, rows, rows, P(None, ALL), P(None, ALL), P(),
        ),
        check_vma=False,
    )
```

```python
import functools
import math

import jax
import jax.numpy as jnp
from jax import lax
from jax.experimental import pallas as pl
from jax.experimental.pallas import tpu as pltpu
from jax.sharding import PartitionSpec as P

WINDOW = 1024
EPSILON = 1e-06
SCALE_BASE = 1.4426950408889634
MASKED_SCORE = -1e30

ALL = ("batch", "blk", "head")
REST = ("batch", "blk")
F32 = jnp.float32
BF16 = jnp.bfloat16


def shifted(block, axis, distance):
    devices = range(lax.axis_size(axis))
    route = [(i - distance, i) for i in devices if i - distance in devices]
    return lax.ppermute(block, axis, route)


NT = (((1,), (1,)), ((), ()))
TN = (((0,), (0,)), ((), ()))


def dot(left, right):
    return jnp.dot(left, right, preferred_element_type=F32)


def dot_rows(left, right):
    return lax.dot_general(left, right, (((0,), (0,)), ((), ())), preferred_element_type=F32)


def dot_cols(left, right):
    return lax.dot_general(left, right, (((1,), (1,)), ((), ())), preferred_element_type=F32)


def normalize(stream, gain):
    factor = lax.rsqrt(jnp.mean(stream * stream, axis=-1, keepdims=True) + EPSILON)
    return stream * factor * gain, factor


def norm_back(upper, stream, factor, gain):
    inner = upper * gain
    gain_grad = jnp.sum(upper * stream * factor, axis=0)
    lower = factor * inner - stream * factor * factor * factor * jnp.mean(
        inner * stream, axis=-1, keepdims=True
    )
    return lower, gain_grad


class Plan:
    def __init__(self, tokens):
        self.seqs, self.rows, self.width = tokens.shape
        self.heads = lax.axis_size("head")
        self.blks = lax.axis_size("blk")
        self.block = self.rows * self.heads
        self.whole = self.seqs % self.blks == 0
        if self.whole:
            self.groups, self.own_seqs = self.blks, self.seqs // self.blks
            self.reach = 0
        else:
            self.groups, self.own_seqs = 1, self.seqs
            self.reach = min((WINDOW - 1) // self.block + 1, self.blks - 1)
        self.length = self.groups * self.block
        self.tokens = self.seqs * self.rows


def to_plan(plan, array):
    if plan.whole and plan.blks > 1:
        array = lax.all_to_all(array, "blk", split_axis=0, concat_axis=0, tiled=True)
    return array.reshape(plan.tokens, plan.width)


def from_plan(plan, flat):
    array = flat.reshape(plan.seqs, plan.rows, plan.width)
    if plan.whole and plan.blks > 1:
        array = lax.all_to_all(array, "blk", split_axis=0, concat_axis=0, tiled=True)
    return array


def in_sequence(plan, by_head, width):
    parts = by_head.reshape(plan.heads, plan.groups, plan.own_seqs, plan.rows, width)
    return parts.transpose(2, 1, 0, 3, 4).reshape(-1, width)


def by_owner(plan, rows, width):
    parts = rows.reshape(plan.own_seqs, plan.groups, plan.heads, plan.rows, width)
    return parts.transpose(2, 1, 0, 3, 4).reshape(plan.heads, plan.tokens, width)


def gather_tokens(plan, rows):
    moved = lax.all_gather(rows, "head", axis=0, tiled=False)
    return in_sequence(plan, moved, rows.shape[-1])


def scatter_tokens(plan, rows):
    width = rows.shape[-1]
    return lax.psum_scatter(
        by_owner(plan, rows.astype(BF16), width), "head", scatter_dimension=0, tiled=False
    ).astype(F32)


def heads_to_tokens(plan, rows):
    part = rows.shape[-1]
    moved = lax.all_to_all(
        by_owner(plan, rows, part), "head", split_axis=0, concat_axis=0, tiled=True
    )
    return moved.transpose(1, 0, 2).reshape(plan.tokens, plan.heads * part)


def tokens_to_heads(plan, rows):
    part = rows.shape[-1] // plan.heads
    sent = rows.reshape(plan.tokens, plan.heads, part).transpose(1, 0, 2)
    moved = lax.all_to_all(sent, "head", split_axis=0, concat_axis=0, tiled=True)
    return in_sequence(plan, moved, part)


def gather_qkv(rows):
    own, width = rows.shape
    heads = lax.axis_size("head")
    part = width // 3 // heads
    sent = rows.reshape(own, 3, heads, part).transpose(2, 0, 1, 3).reshape(heads, own, 3 * part)
    moved = lax.all_to_all(sent, "head", split_axis=0, concat_axis=0, tiled=True)
    full = lax.all_gather(moved, REST, axis=0, tiled=True)
    return full.reshape(-1, 3 * part)


def scatter_qkv(grad):
    heads = lax.axis_size("head")
    part = grad.shape[1] // 3
    summed = lax.psum_scatter(grad.astype(BF16), REST, scatter_dimension=0, tiled=True)
    own = summed.shape[0] // heads
    moved = lax.all_to_all(
        summed.reshape(heads, own, 3 * part), "head", split_axis=0, concat_axis=0, tiled=True
    )
    return (
        moved.reshape(heads, own, 3, part)
        .transpose(1, 2, 0, 3)
        .reshape(own, 3 * heads * part)
        .astype(F32)
    )


def window_mask(plan, segments, block_index):
    key_count = plan.length + plan.reach * plan.block
    if plan.whole:
        query_segs, key_segs = segments, segments
    else:
        leading = jnp.full((plan.own_seqs, plan.reach * plan.block), -1, jnp.int32)
        padded = jnp.concatenate([leading, segments], axis=1)
        start = block_index * plan.block
        query_segs = lax.dynamic_slice_in_dim(segments, start, plan.block, 1)
        key_segs = lax.dynamic_slice_in_dim(padded, start, key_count, 1)
    query_place = jnp.arange(plan.length, dtype=jnp.int32)[:, None] + plan.reach * plan.block
    key_place = jnp.arange(key_count, dtype=jnp.int32)[None, :]
    near = (key_place <= query_place) & (query_place - key_place < WINDOW)
    return (key_segs[:, None, :] == query_segs[:, :, None]) & near[None]


def with_earlier(plan, own):
    arrived = [own]
    for _ in range(plan.reach):
        arrived.append(shifted(arrived[-1], "blk", 1))
    return jnp.concatenate(arrived[::-1], axis=1) if plan.reach else own


def to_earlier(plan, grads):
    if not plan.reach:
        return grads
    block = plan.block
    total = grads[:, :block]
    for step in range(1, plan.reach + 1):
        total = (
            shifted(total.astype(BF16), "blk", -1).astype(F32)
            + grads[:, step * block : (step + 1) * block]
        )
    return total


def scores_of(queries, keys, allowed):
    scores = jnp.einsum("sqhd,skhd->shqk", queries, keys, preferred_element_type=F32)
    return jnp.where(allowed[:, None], scores, MASKED_SCORE)


def attend(queries, keys, values, allowed):
    scores = scores_of(queries, keys, allowed)
    top_score = jnp.max(scores, axis=-1, keepdims=True)
    exp_terms = jnp.exp(scores - top_score)
    totals = jnp.sum(exp_terms, axis=-1, keepdims=True)
    probs_low = (exp_terms / totals).astype(BF16)
    attended = jnp.einsum("shqk,skhd->sqhd", probs_low, values, preferred_element_type=F32)
    return attended, top_score + jnp.log(totals)


def attend_back(queries, keys, values, allowed, log_total, attended_grad):
    probs = jnp.exp(scores_of(queries, keys, allowed) - log_total)
    probs_low = probs.astype(BF16)
    values_grad = jnp.einsum(
        "shqk,sqhd->skhd", probs_low, attended_grad, preferred_element_type=F32
    )
    probs_grad = jnp.einsum("sqhd,skhd->shqk", attended_grad, values, preferred_element_type=F32)
    row_dot = jnp.sum(probs_grad * probs, axis=-1, keepdims=True)
    scores_low = (probs * (probs_grad - row_dot)).astype(BF16)
    queries_grad = jnp.einsum("shqk,skhd->sqhd", scores_low, keys, preferred_element_type=F32)
    keys_grad = jnp.einsum("shqk,sqhd->skhd", scores_low, queries, preferred_element_type=F32)
    return queries_grad, keys_grad, values_grad


def forward(plan, stream, qkv, dense, gains, scale_vec, allowed):
    width = plan.width
    head_dim = scale_vec.shape[0]
    part = qkv.shape[1] // 3
    local_heads = part // head_dim
    split = (plan.own_seqs, plan.length, local_heads, head_dim)
    out_w, up_w, down_w = dense[:, :width], dense[:, width:-width], dense[:, -width:]
    normed, factor_one = normalize(stream, gains[0])
    normed_all = gather_tokens(plan, normed.astype(BF16))
    projected = dot(normed_all, qkv)
    query_pre = projected[:, :part].reshape(split)
    queries = (query_pre * scale_vec).astype(BF16)
    keys = with_earlier(plan, projected[:, part : 2 * part].astype(BF16).reshape(split))
    values = with_earlier(plan, projected[:, 2 * part :].astype(BF16).reshape(split))
    attended_part, log_total = attend(queries, keys, values, allowed)
    attended = heads_to_tokens(plan, attended_part.astype(BF16).reshape(-1, part))
    middle = stream + dot(attended, out_w)
    normed_two, factor_two = normalize(middle, gains[1])
    normed_two = normed_two.astype(BF16)
    hidden = dot(normed_two, up_w)
    active = (hidden * jax.nn.sigmoid(hidden)).astype(BF16)
    result = middle + dot(active, down_w)
    kept = (
        stream, factor_one, normed_all, query_pre, queries, keys, values, log_total,
        attended, middle, factor_two, normed_two, hidden, active,
    )
    return result, kept


def backward(plan, upper, kept, qkv, dense, gains, scale_vec, allowed):
    (
        stream, factor_one, normed_all, query_pre, queries, keys, values, log_total,
        attended, middle, factor_two, normed_two, hidden, active,
    ) = kept
    width = plan.width
    head_dim = scale_vec.shape[0]
    part = qkv.shape[1] // 3
    out_w, up_w, down_w = dense[:, :width], dense[:, width:-width], dense[:, -width:]
    upper_low = upper.astype(BF16)
    down_grad = dot_rows(active, upper_low)
    active_grad = dot_cols(upper_low, down_w)
    gate = jax.nn.sigmoid(hidden)
    hidden_low = (active_grad * gate * (1.0 + hidden * (1.0 - gate))).astype(BF16)
    up_grad = dot_rows(normed_two, hidden_low)
    extra_two, mlp_gain_grad = norm_back(dot_cols(hidden_low, up_w), middle, factor_two, gains[1])
    middle_grad = upper + extra_two
    middle_low = middle_grad.astype(BF16)
    out_grad = dot_rows(attended, middle_low)
    dense_grad = jnp.concatenate([out_grad, up_grad, down_grad], axis=1).astype(BF16)
    dense_own = lax.psum_scatter(dense_grad, ALL, scatter_dimension=0, tiled=True)
    attended_grad = tokens_to_heads(plan, dot_cols(middle_low, out_w).astype(BF16))
    queries_grad, keys_grad, values_grad = attend_back(
        queries, keys, values, allowed, log_total, attended_grad.reshape(queries.shape)
    )
    query_bar = queries_grad.astype(BF16).astype(F32)
    scale_vec_grad = jnp.sum((query_bar * query_pre).reshape(-1, head_dim), axis=0)
    query_low = (query_bar * scale_vec).astype(BF16).reshape(-1, part)
    keys_low = to_earlier(plan, keys_grad).astype(BF16).reshape(-1, part)
    values_low = to_earlier(plan, values_grad).astype(BF16).reshape(-1, part)
    projected_low = jnp.concatenate([query_low, keys_low, values_low], axis=1)
    normed_grad = scatter_tokens(plan, dot_cols(projected_low, qkv))
    qkv_own = scatter_qkv(dot_rows(normed_all, projected_low))
    extra_one, attn_gain_grad = norm_back(normed_grad, stream, factor_one, gains[0])
    lower = middle_grad + extra_one
    return lower, qkv_own, dense_own, (attn_gain_grad, mlp_gain_grad), scale_vec_grad


def general_device(
    tokens,
    segments,
    qkv_weight,
    out_weight,
    up_weight,
    down_weight,
    attn_gain,
    mlp_gain,
    scale_param,
    cotangent,
):
    plan = Plan(tokens)
    layers, head_dim = scale_param.shape
    block_index = lax.axis_index("blk")
    scale_vecs = SCALE_BASE / math.sqrt(head_dim) * jax.nn.softplus(scale_param)
    own_gains = jnp.concatenate([attn_gain, mlp_gain], axis=0)
    gains = (
        lax.all_gather(own_gains.reshape(1, -1), ALL, axis=0, tiled=True)
        .reshape(-1, 2 * layers, attn_gain.shape[1])
        .transpose(1, 0, 2)
        .reshape(2 * layers, plan.width)
        .astype(F32)
    )
    if plan.whole:
        segments = lax.dynamic_slice_in_dim(
            segments, block_index * plan.own_seqs, plan.own_seqs, 0
        )
    allowed = window_mask(plan, segments, block_index)
    stream = to_plan(plan, tokens).astype(F32)
    qkvs, denses, kept = [], [], []
    for layer in range(layers):
        qkvs.append(gather_qkv(qkv_weight[layer]))
        own = jnp.concatenate([out_weight[layer], up_weight[layer], down_weight[layer]], axis=1)
        denses.append(lax.all_gather(own, ALL, axis=0, tiled=True))
        layer_gains = (gains[layer], gains[layers + layer])
        stream, saved = forward(
            plan, stream, qkvs[layer], denses[layer], layer_gains, scale_vecs[layer], allowed
        )
        kept.append(saved)
    layer_out = from_plan(plan, stream.astype(BF16))
    upper = to_plan(plan, cotangent).astype(F32)
    qkv_grads, dense_grads = [None] * layers, [None] * layers
    gain_grads, scale_grads = [None] * layers, [None] * layers
    for layer in reversed(range(layers)):
        layer_gains = (gains[layer], gains[layers + layer])
        upper, qkv_grads[layer], dense_grads[layer], gain_grads[layer], scale_grads[layer] = (
            backward(
                plan, upper, kept[layer], qkvs[layer], denses[layer], layer_gains,
                scale_vecs[layer], allowed,
            )
        )
    input_grad = from_plan(plan, upper.astype(BF16)).astype(F32)
    small = jnp.concatenate(
        [g[0] for g in gain_grads] + [g[1] for g in gain_grads] + scale_grads, axis=0
    )
    total = lax.psum(small, ALL)
    gain_total = total[: 2 * layers * plan.width].reshape(2 * layers, plan.width)
    owner = lax.axis_index(ALL)
    gain_rows = attn_gain.shape[1]
    own_total = lax.dynamic_slice_in_dim(gain_total, owner * gain_rows, gain_rows, 1)
    scale_total = total[2 * layers * plan.width :].reshape(layers, head_dim)
    scale_grad = scale_total * (SCALE_BASE / math.sqrt(head_dim)) * jax.nn.sigmoid(scale_param)
    dense_all = jnp.stack(dense_grads).astype(F32)
    width = plan.width
    return (
        layer_out,
        input_grad,
        jnp.stack(qkv_grads),
        dense_all[:, :, :width],
        dense_all[:, :, width:-width],
        dense_all[:, :, -width:],
        own_total[:layers],
        own_total[layers:],
        scale_grad,
    )


Q_ROWS = 256
KERNEL = pltpu.CompilerParams(vmem_limit_bytes=50 * 1024 * 1024)
LIGHT = pl.CostEstimate(flops=1 << 20, bytes_accessed=1 << 20, transcendentals=0)


def allowed_keys(col, row, first):
    count = first + row.shape[1]
    key_place = lax.broadcasted_iota(jnp.int32, (count, row.shape[1]), 0)
    query_place = lax.broadcasted_iota(jnp.int32, (count, row.shape[1]), 1) + first
    return (col[:count] == row) & (key_place <= query_place)


def token_places(length, heads, token_rows):
    for first in range(0, length, Q_ROWS):
        parts = []
        for start in range(0, Q_ROWS, token_rows):
            place = (first + start) // token_rows
            parts.append((start, place % heads, place // heads * token_rows))
        yield first, parts


def attend_kernel(token_rows, proj_ref, scale_ref, col_ref, row_ref, out_ref, lse_ref):
    length = proj_ref.shape[-1]
    queries = (proj_ref[0, 0] * scale_ref[...]).astype(BF16)
    keys = proj_ref[1, 0].T.astype(BF16)
    values = proj_ref[2, 0].astype(BF16)
    for first, parts in token_places(length, out_ref.shape[0], token_rows):
        end = first + Q_ROWS
        scores = jnp.dot(keys[:end], queries[:, first:end], preferred_element_type=F32)
        allowed = allowed_keys(col_ref[...], row_ref[:, first:end], first)
        scores = jnp.where(allowed, scores, MASKED_SCORE)
        top = jnp.max(scores, axis=0, keepdims=True)
        terms = jnp.exp(scores - top)
        total = jnp.sum(terms, axis=0, keepdims=True)
        probs = (terms * (1.0 / total)).astype(BF16)
        attended = jnp.dot(values[:, :end], probs, preferred_element_type=F32).astype(BF16)
        lse_ref[0, :, first:end] = top + jnp.log(total)
        for start, owner, offset in parts:
            out_ref[owner, 0, :, offset : offset + token_rows] = attended[
                :, start : start + token_rows
            ]


def attend_rows(projected, scale_vec, segments, owners, token_rows):
    head_dim = scale_vec.shape[0]
    length = projected.shape[1]
    local_heads = projected.shape[0] // 3 // head_dim
    tokens = length // owners
    attended, log_total = pl.pallas_call(
        functools.partial(attend_kernel, token_rows),
        grid=(local_heads,),
        in_specs=[
            pl.BlockSpec((3, 1, head_dim, length), lambda h: (0, h, 0, 0)),
            pl.BlockSpec((head_dim, 1), lambda h: (0, 0)),
            pl.BlockSpec((length, 1), lambda h: (0, 0)),
            pl.BlockSpec((1, length), lambda h: (0, 0)),
        ],
        out_specs=[
            pl.BlockSpec((owners, 1, head_dim, tokens), lambda h: (0, h, 0, 0)),
            pl.BlockSpec((1, 1, length), lambda h: (h, 0, 0)),
        ],
        out_shape=[
            jax.ShapeDtypeStruct((owners, local_heads, head_dim, tokens), BF16),
            jax.ShapeDtypeStruct((local_heads, 1, length), F32),
        ],
        compiler_params=KERNEL,
        cost_estimate=LIGHT,
    )(
        projected.reshape(3, local_heads, head_dim, length),
        scale_vec.reshape(head_dim, 1),
        segments.reshape(length, 1),
        segments.reshape(1, length),
    )
    return attended.reshape(owners, local_heads * head_dim, tokens), log_total


def attend_back_kernel(
    token_rows,
    proj_ref,
    grad_ref,
    lse_ref,
    scale_ref,
    col_ref,
    row_ref,
    out_ref,
    scale_grad_ref,
    keys_acc,
    values_acc,
):
    length = proj_ref.shape[-1]
    scale = scale_ref[...]
    query_pre = proj_ref[0, 0]
    queries = (query_pre * scale).astype(BF16)
    keys_t = proj_ref[1, 0].astype(BF16)
    keys = proj_ref[1, 0].T.astype(BF16)
    values = proj_ref[2, 0].T.astype(BF16)
    keys_acc[...] = jnp.zeros_like(keys_acc)
    values_acc[...] = jnp.zeros_like(values_acc)
    scale_grad = jnp.zeros((scale.shape[0], 1), F32)
    for first, parts in token_places(length, grad_ref.shape[0], token_rows):
        end = first + Q_ROWS
        block = queries[:, first:end]
        grad = jnp.concatenate(
            [grad_ref[owner, 0, :, at : at + token_rows] for _, owner, at in parts], axis=1
        )
        scores = jnp.dot(keys[:end], block, preferred_element_type=F32)
        allowed = allowed_keys(col_ref[...], row_ref[:, first:end], first)
        scores = jnp.where(allowed, scores, MASKED_SCORE)
        probs = jnp.exp(scores - lse_ref[0, :, first:end])
        probs_grad = jnp.dot(values[:end], grad, preferred_element_type=F32)
        row_dot = jnp.sum(probs_grad * probs, axis=0, keepdims=True)
        scores_low = (probs * (probs_grad - row_dot)).astype(BF16)
        values_acc[:, :end] += lax.dot_general(
            grad, probs.astype(BF16), NT, preferred_element_type=F32
        )
        keys_acc[:, :end] += lax.dot_general(
            block, scores_low, NT, preferred_element_type=F32
        )
        query_bar = jnp.dot(keys_t[:, :end], scores_low, preferred_element_type=F32)
        query_bar = query_bar.astype(BF16).astype(F32)
        scale_grad += jnp.sum(query_bar * query_pre[:, first:end], axis=1, keepdims=True)
        out_ref[0, 0, :, first:end] = (query_bar * scale).astype(BF16)
    out_ref[1, 0] = keys_acc[...].astype(BF16)
    out_ref[2, 0] = values_acc[...].astype(BF16)
    spread = jnp.broadcast_to(scale_grad, scale_grad_ref.shape)

    @pl.when(pl.program_id(0) == 0)
    def _():
        scale_grad_ref[...] = spread

    @pl.when(pl.program_id(0) > 0)
    def _():
        scale_grad_ref[...] += spread


def attend_back_rows(projected, attended_grad, log_total, scale_vec, segments, token_rows):
    head_dim = scale_vec.shape[0]
    length = projected.shape[1]
    local_heads = projected.shape[0] // 3 // head_dim
    owners, _, tokens = attended_grad.shape
    lanes = 128
    grads, scale_grad = pl.pallas_call(
        functools.partial(attend_back_kernel, token_rows),
        grid=(local_heads,),
        in_specs=[
            pl.BlockSpec((3, 1, head_dim, length), lambda h: (0, h, 0, 0)),
            pl.BlockSpec((owners, 1, head_dim, tokens), lambda h: (0, h, 0, 0)),
            pl.BlockSpec((1, 1, length), lambda h: (h, 0, 0)),
            pl.BlockSpec((head_dim, 1), lambda h: (0, 0)),
            pl.BlockSpec((length, 1), lambda h: (0, 0)),
            pl.BlockSpec((1, length), lambda h: (0, 0)),
        ],
        out_specs=[
            pl.BlockSpec((3, 1, head_dim, length), lambda h: (0, h, 0, 0)),
            pl.BlockSpec((head_dim, lanes), lambda h: (0, 0)),
        ],
        out_shape=[
            jax.ShapeDtypeStruct((3, local_heads, head_dim, length), BF16),
            jax.ShapeDtypeStruct((head_dim, lanes), F32),
        ],
        scratch_shapes=[
            pltpu.VMEM((head_dim, length), F32),
            pltpu.VMEM((head_dim, length), F32),
        ],
        compiler_params=KERNEL,
        cost_estimate=LIGHT,
    )(
        projected.reshape(3, local_heads, head_dim, length),
        attended_grad.reshape(owners, local_heads, head_dim, tokens),
        log_total,
        scale_vec.reshape(head_dim, 1),
        segments.reshape(length, 1),
        segments.reshape(1, length),
    )
    return grads.reshape(3 * local_heads * head_dim, length), scale_grad[:, 0]


def dense_grad_kernel(attended_ref, normed_ref, active_ref, out_bar, up_bar, down_bar, grad_ref):
    width = out_bar.shape[1]
    grad_ref[:, :width] = jnp.dot(
        attended_ref[...], out_bar[...], preferred_element_type=F32
    ).astype(BF16)
    grad_ref[:, width : 2 * width] = lax.dot_general(
        normed_ref[...], up_bar[...], TN, preferred_element_type=F32
    ).astype(BF16)
    grad_ref[:, 2 * width :] = lax.dot_general(
        active_ref[...], down_bar[...], TN, preferred_element_type=F32
    ).astype(BF16)


def dense_grads(attended_t, normed, active, out_bar, up_bar, down_bar):
    width, tokens = attended_t.shape
    tile = 256
    whole = pl.BlockSpec((tokens, width), lambda i: (0, 0))
    columns = pl.BlockSpec((tokens, tile), lambda i: (0, i))
    return pl.pallas_call(
        dense_grad_kernel,
        grid=(width // tile,),
        in_specs=[
            pl.BlockSpec((tile, tokens), lambda i: (i, 0)), columns, columns, whole, whole, whole,
        ],
        out_specs=pl.BlockSpec((tile, 3 * width), lambda i: (i, 0)),
        out_shape=jax.ShapeDtypeStruct((width, 3 * width), BF16),
        compiler_params=KERNEL,
        cost_estimate=LIGHT,
    )(attended_t, normed, active, out_bar, up_bar, down_bar)


def tied(*arrays):
    return lax.optimization_barrier(arrays)


def swapped(array, axis, mask):
    size = lax.axis_size(axis)
    return lax.ppermute(array, axis, [(i, i ^ mask) for i in range(size)])


def pick(array, index, axis=0):
    return lax.dynamic_index_in_dim(array, index, axis, keepdims=False)


def swap_halves(array):
    me = lax.axis_index("blk")
    got = swapped(pick(array, 1 - me), "blk", 1)
    kept = pick(array, me)
    return jnp.stack([jnp.where(me == 0, kept, got), jnp.where(me == 0, got, kept)])


def gather_rows(rows):
    width = rows.shape[-1]
    far = swapped(rows, "head", 2)
    near = swapped(rows, "head", 1)
    both = swapped(far, "head", 1)
    pieces = jnp.stack([rows, near, far, both])
    me = lax.axis_index("head")
    ordered = jnp.stack([pick(pieces, me ^ i) for i in range(4)])
    return ordered.reshape(4, 2, -1, width).transpose(1, 0, 2, 3).reshape(-1, width)


def scatter_rows(rows):
    width = rows.shape[-1]
    me = lax.axis_index("head")
    row, core = me // 2, me % 2
    parts = rows.reshape(2, 2, 2, -1, width)
    halves = pick(parts, core, 2) + swapped(
        pick(parts, 1 - core, 2).astype(BF16), "head", 1
    ).astype(F32)
    got = swapped(pick(halves, 1 - row, 1).astype(BF16), "head", 2).astype(F32)
    return (pick(halves, row, 1) + got).reshape(-1, width)


def over_head(parts):
    return lax.all_to_all(parts, "head", split_axis=0, concat_axis=0, tiled=True)


def qkv_columns(rows, extra):
    own, width = rows.shape
    part = width // 3 // 4
    sent = rows.reshape(own, 3, 4, part).transpose(2, 0, 1, 3).reshape(4, own, 3 * part)
    if extra is not None:
        sent = jnp.concatenate([sent, jnp.broadcast_to(extra[None], (4,) + extra.shape)], axis=2)
    return over_head(sent)


def along_batch(piece):
    return [piece] + [swapped(piece, "batch", mask) for mask in (1, 2, 3)]


def in_rows(along, across):
    me, blk = lax.axis_index("batch"), lax.axis_index("blk")
    ordered = []
    for i in range(4):
        one, two = pick(along, me ^ i), pick(across, me ^ i)
        ordered += [jnp.where(blk == 0, one, two), jnp.where(blk == 0, two, one)]
    return jnp.stack(ordered).reshape(-1, along.shape[-1])


def columns_over_blk(grad):
    blk = lax.axis_index("blk")
    parts = grad.reshape(4, 2, -1, grad.shape[1])
    return pick(parts, blk, 1), swapped(pick(parts, 1 - blk, 1).astype(BF16), "blk", 1)


def sent_over_batch(parts):
    me = lax.axis_index("batch")
    sent = [swapped(pick(parts, me ^ mask).astype(BF16), "batch", mask) for mask in (1, 2, 3)]
    return pick(parts, me).astype(F32), jnp.stack(sent)


def columns_to_rows(own, sent):
    summed = (own + jnp.sum(sent.astype(F32), axis=0)).astype(BF16)
    moved = over_head(summed.reshape(4, -1, summed.shape[-1]))
    rows = moved.shape[1]
    return moved.reshape(4, rows, 3, -1).transpose(1, 2, 0, 3).reshape(rows, -1).astype(F32)


def over_core(grad):
    core = lax.axis_index("head") % 2
    parts = grad.reshape(4, 2, 2, 2, -1, grad.shape[1])
    got = swapped(pick(parts, 1 - core, 3), "head", 1).astype(F32)
    return (pick(parts, core, 3).astype(F32) + got).astype(BF16)


def over_one(part, axis, mask, mine, dim):
    got = swapped(pick(part, 1 - mine, dim), axis, mask).astype(F32)
    return (pick(part, mine, dim).astype(F32) + got).astype(BF16)


def over_chips_first(cored):
    row, blk = lax.axis_index("head") // 2, lax.axis_index("blk")
    half = cored.shape[-1] // 2
    return (
        over_one(cored[..., :half], "blk", 1, blk, 1),
        over_one(cored[..., half:], "head", 2, row, 2),
    )


def over_chips_second(first, second):
    row, blk = lax.axis_index("head") // 2, lax.axis_index("blk")
    first = over_one(first, "head", 2, row, 1)
    second = over_one(second, "blk", 1, blk, 1)
    return jnp.concatenate([first, second], axis=-1)


def sum_all(array):
    for axis, mask in (("head", 1), ("head", 2), ("blk", 1), ("batch", 1), ("batch", 2)):
        array = array + swapped(array, axis, mask)
    return array


def gain_back(weight, weight_grad, gain):
    return jnp.sum(weight.astype(F32) * weight_grad, axis=-1) / gain.astype(F32)


def lower_of(upper, stream, factor, gain):
    return norm_back(upper, stream, factor, gain)[0]


def spread_device(
    tokens,
    segments,
    qkv_weight,
    out_weight,
    up_weight,
    down_weight,
    attn_gain,
    mlp_gain,
    scale_param,
    cotangent,
):
    layers, head_dim = scale_param.shape
    _, token_rows, width = tokens.shape
    scale_vecs = SCALE_BASE / math.sqrt(head_dim) * jax.nn.softplus(scale_param)
    segments = pick(segments, lax.axis_index("blk"))
    own_gains = jnp.concatenate([attn_gain, mlp_gain], axis=0)

    first = swap_halves(tokens).reshape(-1, width)
    columns = [qkv_columns(qkv_weight[0], own_gains.T)]
    columns[0], first = tied(columns[0], first)
    first_all = gather_rows(first)
    stream = first.astype(F32)
    along = along_batch(columns[0].reshape(-1, columns[0].shape[-1]))
    across = jnp.stack([swapped(part, "blk", 1) for part in along])
    along = jnp.stack(along)
    with_gains = in_rows(along, across)
    part3 = 3 * width // 4
    qkvs = [with_gains[:, :part3]]
    gains = with_gains[:, part3:].T.astype(F32)
    own = [w[layer] for layer in range(layers) for w in (out_weight, up_weight, down_weight)]
    dense_whole = lax.all_gather(jnp.concatenate(own, axis=1), ALL, axis=0, tiled=True)
    denses = [dense_whole[:, 3 * width * i : 3 * width * (i + 1)] for i in range(layers)]
    next_piece = qkv_columns(qkv_weight[1], None).reshape(-1, part3)
    next_piece, _ = tied(next_piece, along)
    next_along = jnp.stack(along_batch(next_piece))

    kept = []
    for layer in range(layers):
        qkv, dense = qkvs[layer], denses[layer]
        out_w, up_w, down_w = dense[:, :width], dense[:, width:-width], dense[:, -width:]
        normed, factor_one = normalize(stream, gains[layer])
        if layer == 0:
            normed_all = normalize(first_all.astype(F32), gains[0])[0].astype(BF16)
        else:
            normed_all = gather_rows(normed.astype(BF16))
        projected = lax.dot_general(
            qkv, normed_all, (((0,), (1,)), ((), ())), preferred_element_type=F32
        )
        attended, log_total = attend_rows(
            projected, scale_vecs[layer], segments, 4, token_rows
        )
        if layer == 0:
            attended, next_along = tied(attended, next_along)
            next_across = swapped(next_along, "blk", 1)
        attended_t = over_head(attended).reshape(width, -1)
        middle = stream + dot_rows(attended_t, out_w)
        if layer == 0:
            middle, next_across = tied(middle, next_across)
            qkvs.append(in_rows(next_along, next_across))
        normed_two, factor_two = normalize(middle, gains[layers + layer])
        normed_two = normed_two.astype(BF16)
        hidden = dot(normed_two, up_w)
        active = (hidden * jax.nn.sigmoid(hidden)).astype(BF16)
        kept.append(
            (
                stream, factor_one, normed_all, projected, log_total, attended_t, middle,
                factor_two, normed_two, hidden, active,
            )
        )
        stream = middle + dot(active, down_w)
    layer_out = swap_halves(stream.astype(BF16).reshape(tokens.shape))
    upper = swap_halves(cotangent).reshape(-1, width).astype(F32)

    qkv_grads, dense_own, scale_grads = [None] * layers, [None] * layers, [None] * layers
    for layer in reversed(range(layers)):
        (
            stream, factor_one, normed_all, projected, log_total, attended_t, middle,
            factor_two, normed_two, hidden, active,
        ) = kept[layer]
        qkv, dense = qkvs[layer], denses[layer]
        out_w, up_w, down_w = dense[:, :width], dense[:, width:-width], dense[:, -width:]
        down_bar = upper.astype(BF16)
        gate = jax.nn.sigmoid(hidden)
        up_bar = (
            dot_cols(down_bar, down_w) * gate * (1.0 + hidden * (1.0 - gate))
        ).astype(BF16)
        middle_grad = upper + lower_of(
            dot_cols(up_bar, up_w), middle, factor_two, gains[layers + layer]
        )
        out_bar = middle_grad.astype(BF16)
        attended_grad = over_head(dot_cols(out_w, out_bar).astype(BF16).reshape(4, -1, out_bar.shape[0]))
        grads = dense_grads(attended_t, normed_two, active, out_bar, up_bar, down_bar)
        if layer == 0:
            attended_grad, grads, later = tied(attended_grad, grads, later)
            own, sent = sent_over_batch(later[0] + later[1].astype(F32))
            cored = over_core(grads)
        else:
            attended_grad, grads = tied(attended_grad, grads)
        bars, scale_grads[layer] = attend_back_rows(
            projected, attended_grad, log_total, scale_vecs[layer], segments, token_rows
        )
        if layer == 0:
            bars, cored, sent = tied(bars, cored, sent)
            qkv_grads[1] = columns_to_rows(own, sent)
            halves = over_chips_first(cored)
        normed_grad = scatter_rows(
            lax.dot_general(bars, qkv, (((0,), (1,)), ((), ())), preferred_element_type=F32)
        )
        later = columns_over_blk(
            lax.dot_general(normed_all, bars, (((0,), (1,)), ((), ())), preferred_element_type=F32)
        )
        if layer == 0:
            normed_grad, halves, dense_own[1] = tied(normed_grad, halves, dense_own[1])
            own, sent = sent_over_batch(over_chips_second(*halves))
            dense_own[0] = own + jnp.sum(sent.astype(F32), axis=0)
            qkv_grads[0] = columns_to_rows(*sent_over_batch(later[0] + later[1].astype(F32)))
        else:
            dense_own[1] = lax.psum_scatter(grads, ALL, scatter_dimension=0, tiled=True)
        upper = middle_grad + lower_of(normed_grad, stream, factor_one, gains[layer])
    input_grad = swap_halves(upper.astype(BF16).reshape(tokens.shape)).astype(F32)
    scale_total = sum_all(jnp.stack(scale_grads))
    scale_grad = scale_total * (SCALE_BASE / math.sqrt(head_dim)) * jax.nn.sigmoid(scale_param)
    dense_all = jnp.stack([part.astype(F32) for part in dense_own])
    qkv_all = jnp.stack(qkv_grads)
    up_all = dense_all[:, :, width:-width]
    return (
        layer_out,
        input_grad,
        qkv_all,
        dense_all[:, :, :width],
        up_all,
        dense_all[:, :, -width:],
        gain_back(qkv_weight, qkv_all, attn_gain),
        gain_back(up_weight, up_all, mlp_gain),
        scale_grad,
    )


def per_device(*args):
    tokens, segments = args[0], args[1]
    sizes = tuple(lax.axis_size(axis) for axis in ALL)
    heads = tokens.shape[2] // args[8].shape[1]
    spread = (
        sizes == (4, 2, 4)
        and tokens.shape[0] == 2
        and args[2].shape[0] == 2
        and tokens.shape[1] % 128 == 0
        and Q_ROWS % tokens.shape[1] == 0
        and segments.shape[1] <= WINDOW
        and segments.shape[1] % Q_ROWS == 0
        and heads % 4 == 0
        and tokens.shape[2] % 256 == 0
    )
    return spread_device(*args) if spread else general_device(*args)


def solution(mesh):
    rows = P(None, ALL, None)
    by_token = P("batch", ("blk", "head"), None)
    return jax.shard_map(
        per_device,
        mesh=mesh,
        in_specs=(
            by_token, P("batch", None), rows, rows, rows, rows, P(None, ALL), P(None, ALL), P(),
            by_token,
        ),
        out_specs=(
            by_token, by_token, rows, rows, rows, rows, P(None, ALL), P(None, ALL), P(),
        ),
        check_vma=False,
    )
```

```python
import functools
import math

import jax
import jax.numpy as jnp
from jax import lax
from jax.experimental import pallas as pl
from jax.experimental.pallas import tpu as pltpu
from jax.sharding import PartitionSpec as P

WINDOW = 1024
EPSILON = 1e-06
SCALE_BASE = 1.4426950408889634
MASKED_SCORE = -1e30

ALL = ("batch", "blk", "head")
REST = ("batch", "blk")
F32 = jnp.float32
BF16 = jnp.bfloat16


def shifted(block, axis, distance):
    devices = range(lax.axis_size(axis))
    route = [(i - distance, i) for i in devices if i - distance in devices]
    return lax.ppermute(block, axis, route)


NT = (((1,), (1,)), ((), ()))
TN = (((0,), (0,)), ((), ()))


def dot(left, right):
    return jnp.dot(left, right, preferred_element_type=F32)


def dot_rows(left, right):
    return lax.dot_general(left, right, (((0,), (0,)), ((), ())), preferred_element_type=F32)


def dot_cols(left, right):
    return lax.dot_general(left, right, (((1,), (1,)), ((), ())), preferred_element_type=F32)


def normalize(stream, gain):
    factor = lax.rsqrt(jnp.mean(stream * stream, axis=-1, keepdims=True) + EPSILON)
    return stream * factor * gain, factor


def norm_back(upper, stream, factor, gain):
    inner = upper * gain
    gain_grad = jnp.sum(upper * stream * factor, axis=0)
    lower = factor * inner - stream * factor * factor * factor * jnp.mean(
        inner * stream, axis=-1, keepdims=True
    )
    return lower, gain_grad


class Plan:
    def __init__(self, tokens):
        self.seqs, self.rows, self.width = tokens.shape
        self.heads = lax.axis_size("head")
        self.blks = lax.axis_size("blk")
        self.block = self.rows * self.heads
        self.whole = self.seqs % self.blks == 0
        if self.whole:
            self.groups, self.own_seqs = self.blks, self.seqs // self.blks
            self.reach = 0
        else:
            self.groups, self.own_seqs = 1, self.seqs
            self.reach = min((WINDOW - 1) // self.block + 1, self.blks - 1)
        self.length = self.groups * self.block
        self.tokens = self.seqs * self.rows


def to_plan(plan, array):
    if plan.whole and plan.blks > 1:
        array = lax.all_to_all(array, "blk", split_axis=0, concat_axis=0, tiled=True)
    return array.reshape(plan.tokens, plan.width)


def from_plan(plan, flat):
    array = flat.reshape(plan.seqs, plan.rows, plan.width)
    if plan.whole and plan.blks > 1:
        array = lax.all_to_all(array, "blk", split_axis=0, concat_axis=0, tiled=True)
    return array


def in_sequence(plan, by_head, width):
    parts = by_head.reshape(plan.heads, plan.groups, plan.own_seqs, plan.rows, width)
    return parts.transpose(2, 1, 0, 3, 4).reshape(-1, width)


def by_owner(plan, rows, width):
    parts = rows.reshape(plan.own_seqs, plan.groups, plan.heads, plan.rows, width)
    return parts.transpose(2, 1, 0, 3, 4).reshape(plan.heads, plan.tokens, width)


def gather_tokens(plan, rows):
    moved = lax.all_gather(rows, "head", axis=0, tiled=False)
    return in_sequence(plan, moved, rows.shape[-1])


def scatter_tokens(plan, rows):
    width = rows.shape[-1]
    return lax.psum_scatter(
        by_owner(plan, rows.astype(BF16), width), "head", scatter_dimension=0, tiled=False
    ).astype(F32)


def heads_to_tokens(plan, rows):
    part = rows.shape[-1]
    moved = lax.all_to_all(
        by_owner(plan, rows, part), "head", split_axis=0, concat_axis=0, tiled=True
    )
    return moved.transpose(1, 0, 2).reshape(plan.tokens, plan.heads * part)


def tokens_to_heads(plan, rows):
    part = rows.shape[-1] // plan.heads
    sent = rows.reshape(plan.tokens, plan.heads, part).transpose(1, 0, 2)
    moved = lax.all_to_all(sent, "head", split_axis=0, concat_axis=0, tiled=True)
    return in_sequence(plan, moved, part)


def gather_qkv(rows):
    own, width = rows.shape
    heads = lax.axis_size("head")
    part = width // 3 // heads
    sent = rows.reshape(own, 3, heads, part).transpose(2, 0, 1, 3).reshape(heads, own, 3 * part)
    moved = lax.all_to_all(sent, "head", split_axis=0, concat_axis=0, tiled=True)
    full = lax.all_gather(moved, REST, axis=0, tiled=True)
    return full.reshape(-1, 3 * part)


def scatter_qkv(grad):
    heads = lax.axis_size("head")
    part = grad.shape[1] // 3
    summed = lax.psum_scatter(grad.astype(BF16), REST, scatter_dimension=0, tiled=True)
    own = summed.shape[0] // heads
    moved = lax.all_to_all(
        summed.reshape(heads, own, 3 * part), "head", split_axis=0, concat_axis=0, tiled=True
    )
    return (
        moved.reshape(heads, own, 3, part)
        .transpose(1, 2, 0, 3)
        .reshape(own, 3 * heads * part)
        .astype(F32)
    )


def window_mask(plan, segments, block_index):
    key_count = plan.length + plan.reach * plan.block
    if plan.whole:
        query_segs, key_segs = segments, segments
    else:
        leading = jnp.full((plan.own_seqs, plan.reach * plan.block), -1, jnp.int32)
        padded = jnp.concatenate([leading, segments], axis=1)
        start = block_index * plan.block
        query_segs = lax.dynamic_slice_in_dim(segments, start, plan.block, 1)
        key_segs = lax.dynamic_slice_in_dim(padded, start, key_count, 1)
    query_place = jnp.arange(plan.length, dtype=jnp.int32)[:, None] + plan.reach * plan.block
    key_place = jnp.arange(key_count, dtype=jnp.int32)[None, :]
    near = (key_place <= query_place) & (query_place - key_place < WINDOW)
    return (key_segs[:, None, :] == query_segs[:, :, None]) & near[None]


def with_earlier(plan, own):
    arrived = [own]
    for _ in range(plan.reach):
        arrived.append(shifted(arrived[-1], "blk", 1))
    return jnp.concatenate(arrived[::-1], axis=1) if plan.reach else own


def to_earlier(plan, grads):
    if not plan.reach:
        return grads
    block = plan.block
    total = grads[:, :block]
    for step in range(1, plan.reach + 1):
        total = (
            shifted(total.astype(BF16), "blk", -1).astype(F32)
            + grads[:, step * block : (step + 1) * block]
        )
    return total


def scores_of(queries, keys, allowed):
    scores = jnp.einsum("sqhd,skhd->shqk", queries, keys, preferred_element_type=F32)
    return jnp.where(allowed[:, None], scores, MASKED_SCORE)


def attend(queries, keys, values, allowed):
    scores = scores_of(queries, keys, allowed)
    top_score = jnp.max(scores, axis=-1, keepdims=True)
    exp_terms = jnp.exp(scores - top_score)
    totals = jnp.sum(exp_terms, axis=-1, keepdims=True)
    probs_low = (exp_terms / totals).astype(BF16)
    attended = jnp.einsum("shqk,skhd->sqhd", probs_low, values, preferred_element_type=F32)
    return attended, top_score + jnp.log(totals)


def attend_back(queries, keys, values, allowed, log_total, attended_grad):
    probs = jnp.exp(scores_of(queries, keys, allowed) - log_total)
    probs_low = probs.astype(BF16)
    values_grad = jnp.einsum(
        "shqk,sqhd->skhd", probs_low, attended_grad, preferred_element_type=F32
    )
    probs_grad = jnp.einsum("sqhd,skhd->shqk", attended_grad, values, preferred_element_type=F32)
    row_dot = jnp.sum(probs_grad * probs, axis=-1, keepdims=True)
    scores_low = (probs * (probs_grad - row_dot)).astype(BF16)
    queries_grad = jnp.einsum("shqk,skhd->sqhd", scores_low, keys, preferred_element_type=F32)
    keys_grad = jnp.einsum("shqk,sqhd->skhd", scores_low, queries, preferred_element_type=F32)
    return queries_grad, keys_grad, values_grad


def forward(plan, stream, qkv, dense, gains, scale_vec, allowed):
    width = plan.width
    head_dim = scale_vec.shape[0]
    part = qkv.shape[1] // 3
    local_heads = part // head_dim
    split = (plan.own_seqs, plan.length, local_heads, head_dim)
    out_w, up_w, down_w = dense[:, :width], dense[:, width:-width], dense[:, -width:]
    normed, factor_one = normalize(stream, gains[0])
    normed_all = gather_tokens(plan, normed.astype(BF16))
    projected = dot(normed_all, qkv)
    query_pre = projected[:, :part].reshape(split)
    queries = (query_pre * scale_vec).astype(BF16)
    keys = with_earlier(plan, projected[:, part : 2 * part].astype(BF16).reshape(split))
    values = with_earlier(plan, projected[:, 2 * part :].astype(BF16).reshape(split))
    attended_part, log_total = attend(queries, keys, values, allowed)
    attended = heads_to_tokens(plan, attended_part.astype(BF16).reshape(-1, part))
    middle = stream + dot(attended, out_w)
    normed_two, factor_two = normalize(middle, gains[1])
    normed_two = normed_two.astype(BF16)
    hidden = dot(normed_two, up_w)
    active = (hidden * jax.nn.sigmoid(hidden)).astype(BF16)
    result = middle + dot(active, down_w)
    kept = (
        stream, factor_one, normed_all, query_pre, queries, keys, values, log_total,
        attended, middle, factor_two, normed_two, hidden, active,
    )
    return result, kept


def backward(plan, upper, kept, qkv, dense, gains, scale_vec, allowed):
    (
        stream, factor_one, normed_all, query_pre, queries, keys, values, log_total,
        attended, middle, factor_two, normed_two, hidden, active,
    ) = kept
    width = plan.width
    head_dim = scale_vec.shape[0]
    part = qkv.shape[1] // 3
    out_w, up_w, down_w = dense[:, :width], dense[:, width:-width], dense[:, -width:]
    upper_low = upper.astype(BF16)
    down_grad = dot_rows(active, upper_low)
    active_grad = dot_cols(upper_low, down_w)
    gate = jax.nn.sigmoid(hidden)
    hidden_low = (active_grad * gate * (1.0 + hidden * (1.0 - gate))).astype(BF16)
    up_grad = dot_rows(normed_two, hidden_low)
    extra_two, mlp_gain_grad = norm_back(dot_cols(hidden_low, up_w), middle, factor_two, gains[1])
    middle_grad = upper + extra_two
    middle_low = middle_grad.astype(BF16)
    out_grad = dot_rows(attended, middle_low)
    dense_grad = jnp.concatenate([out_grad, up_grad, down_grad], axis=1).astype(BF16)
    dense_own = lax.psum_scatter(dense_grad, ALL, scatter_dimension=0, tiled=True)
    attended_grad = tokens_to_heads(plan, dot_cols(middle_low, out_w).astype(BF16))
    queries_grad, keys_grad, values_grad = attend_back(
        queries, keys, values, allowed, log_total, attended_grad.reshape(queries.shape)
    )
    query_bar = queries_grad.astype(BF16).astype(F32)
    scale_vec_grad = jnp.sum((query_bar * query_pre).reshape(-1, head_dim), axis=0)
    query_low = (query_bar * scale_vec).astype(BF16).reshape(-1, part)
    keys_low = to_earlier(plan, keys_grad).astype(BF16).reshape(-1, part)
    values_low = to_earlier(plan, values_grad).astype(BF16).reshape(-1, part)
    projected_low = jnp.concatenate([query_low, keys_low, values_low], axis=1)
    normed_grad = scatter_tokens(plan, dot_cols(projected_low, qkv))
    qkv_own = scatter_qkv(dot_rows(normed_all, projected_low))
    extra_one, attn_gain_grad = norm_back(normed_grad, stream, factor_one, gains[0])
    lower = middle_grad + extra_one
    return lower, qkv_own, dense_own, (attn_gain_grad, mlp_gain_grad), scale_vec_grad


def general_device(
    tokens,
    segments,
    qkv_weight,
    out_weight,
    up_weight,
    down_weight,
    attn_gain,
    mlp_gain,
    scale_param,
    cotangent,
):
    plan = Plan(tokens)
    layers, head_dim = scale_param.shape
    block_index = lax.axis_index("blk")
    scale_vecs = SCALE_BASE / math.sqrt(head_dim) * jax.nn.softplus(scale_param)
    own_gains = jnp.concatenate([attn_gain, mlp_gain], axis=0)
    gains = (
        lax.all_gather(own_gains.reshape(1, -1), ALL, axis=0, tiled=True)
        .reshape(-1, 2 * layers, attn_gain.shape[1])
        .transpose(1, 0, 2)
        .reshape(2 * layers, plan.width)
        .astype(F32)
    )
    if plan.whole:
        segments = lax.dynamic_slice_in_dim(
            segments, block_index * plan.own_seqs, plan.own_seqs, 0
        )
    allowed = window_mask(plan, segments, block_index)
    stream = to_plan(plan, tokens).astype(F32)
    qkvs, denses, kept = [], [], []
    for layer in range(layers):
        qkvs.append(gather_qkv(qkv_weight[layer]))
        own = jnp.concatenate([out_weight[layer], up_weight[layer], down_weight[layer]], axis=1)
        denses.append(lax.all_gather(own, ALL, axis=0, tiled=True))
        layer_gains = (gains[layer], gains[layers + layer])
        stream, saved = forward(
            plan, stream, qkvs[layer], denses[layer], layer_gains, scale_vecs[layer], allowed
        )
        kept.append(saved)
    layer_out = from_plan(plan, stream.astype(BF16))
    upper = to_plan(plan, cotangent).astype(F32)
    qkv_grads, dense_grads = [None] * layers, [None] * layers
    gain_grads, scale_grads = [None] * layers, [None] * layers
    for layer in reversed(range(layers)):
        layer_gains = (gains[layer], gains[layers + layer])
        upper, qkv_grads[layer], dense_grads[layer], gain_grads[layer], scale_grads[layer] = (
            backward(
                plan, upper, kept[layer], qkvs[layer], denses[layer], layer_gains,
                scale_vecs[layer], allowed,
            )
        )
    input_grad = from_plan(plan, upper.astype(BF16)).astype(F32)
    small = jnp.concatenate(
        [g[0] for g in gain_grads] + [g[1] for g in gain_grads] + scale_grads, axis=0
    )
    total = lax.psum(small, ALL)
    gain_total = total[: 2 * layers * plan.width].reshape(2 * layers, plan.width)
    owner = lax.axis_index(ALL)
    gain_rows = attn_gain.shape[1]
    own_total = lax.dynamic_slice_in_dim(gain_total, owner * gain_rows, gain_rows, 1)
    scale_total = total[2 * layers * plan.width :].reshape(layers, head_dim)
    scale_grad = scale_total * (SCALE_BASE / math.sqrt(head_dim)) * jax.nn.sigmoid(scale_param)
    dense_all = jnp.stack(dense_grads).astype(F32)
    width = plan.width
    return (
        layer_out,
        input_grad,
        jnp.stack(qkv_grads),
        dense_all[:, :, :width],
        dense_all[:, :, width:-width],
        dense_all[:, :, -width:],
        own_total[:layers],
        own_total[layers:],
        scale_grad,
    )


Q_ROWS = 256
KERNEL = pltpu.CompilerParams(vmem_limit_bytes=50 * 1024 * 1024)
LIGHT = pl.CostEstimate(flops=1 << 20, bytes_accessed=1 << 20, transcendentals=0)


def allowed_keys(col, row, first):
    count = first + row.shape[1]
    key_place = lax.broadcasted_iota(jnp.int32, (count, row.shape[1]), 0)
    query_place = lax.broadcasted_iota(jnp.int32, (count, row.shape[1]), 1) + first
    return (col[:count] == row) & (key_place <= query_place)


def token_places(length, heads, token_rows):
    for first in range(0, length, Q_ROWS):
        parts = []
        for start in range(0, Q_ROWS, token_rows):
            place = (first + start) // token_rows
            parts.append((start, place % heads, place // heads * token_rows))
        yield first, parts


def attend_kernel(token_rows, proj_ref, scale_ref, col_ref, row_ref, out_ref, lse_ref):
    length = proj_ref.shape[-1]
    queries = (proj_ref[0, 0] * scale_ref[...]).astype(BF16)
    keys = proj_ref[1, 0].T.astype(BF16)
    values = proj_ref[2, 0].astype(BF16)
    for first, parts in token_places(length, out_ref.shape[0], token_rows):
        end = first + Q_ROWS
        scores = jnp.dot(keys[:end], queries[:, first:end], preferred_element_type=F32)
        allowed = allowed_keys(col_ref[...], row_ref[:, first:end], first)
        scores = jnp.where(allowed, scores, MASKED_SCORE)
        top = jnp.max(scores, axis=0, keepdims=True)
        terms = jnp.exp(scores - top)
        total = jnp.sum(terms, axis=0, keepdims=True)
        probs = (terms * (1.0 / total)).astype(BF16)
        attended = jnp.dot(values[:, :end], probs, preferred_element_type=F32).astype(BF16)
        lse_ref[0, :, first:end] = top + jnp.log(total)
        for start, owner, offset in parts:
            out_ref[owner, 0, :, offset : offset + token_rows] = attended[
                :, start : start + token_rows
            ]


def attend_rows(projected, scale_vec, segments, owners, token_rows):
    head_dim = scale_vec.shape[0]
    length = projected.shape[1]
    local_heads = projected.shape[0] // 3 // head_dim
    tokens = length // owners
    attended, log_total = pl.pallas_call(
        functools.partial(attend_kernel, token_rows),
        grid=(local_heads,),
        in_specs=[
            pl.BlockSpec((3, 1, head_dim, length), lambda h: (0, h, 0, 0)),
            pl.BlockSpec((head_dim, 1), lambda h: (0, 0)),
            pl.BlockSpec((length, 1), lambda h: (0, 0)),
            pl.BlockSpec((1, length), lambda h: (0, 0)),
        ],
        out_specs=[
            pl.BlockSpec((owners, 1, head_dim, tokens), lambda h: (0, h, 0, 0)),
            pl.BlockSpec((1, 1, length), lambda h: (h, 0, 0)),
        ],
        out_shape=[
            jax.ShapeDtypeStruct((owners, local_heads, head_dim, tokens), BF16),
            jax.ShapeDtypeStruct((local_heads, 1, length), F32),
        ],
        compiler_params=KERNEL,
        cost_estimate=LIGHT,
    )(
        projected.reshape(3, local_heads, head_dim, length),
        scale_vec.reshape(head_dim, 1),
        segments.reshape(length, 1),
        segments.reshape(1, length),
    )
    return attended.reshape(owners, local_heads * head_dim, tokens), log_total


def attend_back_kernel(
    token_rows,
    proj_ref,
    grad_ref,
    lse_ref,
    scale_ref,
    col_ref,
    row_ref,
    out_ref,
    scale_grad_ref,
    keys_acc,
    values_acc,
):
    length = proj_ref.shape[-1]
    scale = scale_ref[...]
    query_pre = proj_ref[0, 0]
    queries = (query_pre * scale).astype(BF16)
    keys_t = proj_ref[1, 0].astype(BF16)
    keys = proj_ref[1, 0].T.astype(BF16)
    values = proj_ref[2, 0].T.astype(BF16)
    keys_acc[...] = jnp.zeros_like(keys_acc)
    values_acc[...] = jnp.zeros_like(values_acc)
    scale_grad = jnp.zeros((scale.shape[0], 1), F32)
    for first, parts in token_places(length, grad_ref.shape[0], token_rows):
        end = first + Q_ROWS
        block = queries[:, first:end]
        grad = jnp.concatenate(
            [grad_ref[owner, 0, :, at : at + token_rows] for _, owner, at in parts], axis=1
        )
        scores = jnp.dot(keys[:end], block, preferred_element_type=F32)
        allowed = allowed_keys(col_ref[...], row_ref[:, first:end], first)
        scores = jnp.where(allowed, scores, MASKED_SCORE)
        probs = jnp.exp(scores - lse_ref[0, :, first:end])
        probs_grad = jnp.dot(values[:end], grad, preferred_element_type=F32)
        row_dot = jnp.sum(probs_grad * probs, axis=0, keepdims=True)
        scores_low = (probs * (probs_grad - row_dot)).astype(BF16)
        values_acc[:, :end] += lax.dot_general(
            grad, probs.astype(BF16), NT, preferred_element_type=F32
        )
        keys_acc[:, :end] += lax.dot_general(
            block, scores_low, NT, preferred_element_type=F32
        )
        query_bar = jnp.dot(keys_t[:, :end], scores_low, preferred_element_type=F32)
        query_bar = query_bar.astype(BF16).astype(F32)
        scale_grad += jnp.sum(query_bar * query_pre[:, first:end], axis=1, keepdims=True)
        out_ref[0, 0, :, first:end] = (query_bar * scale).astype(BF16)
    out_ref[1, 0] = keys_acc[...].astype(BF16)
    out_ref[2, 0] = values_acc[...].astype(BF16)
    spread = jnp.broadcast_to(scale_grad, scale_grad_ref.shape)

    @pl.when(pl.program_id(0) == 0)
    def _():
        scale_grad_ref[...] = spread

    @pl.when(pl.program_id(0) > 0)
    def _():
        scale_grad_ref[...] += spread


def attend_back_rows(projected, attended_grad, log_total, scale_vec, segments, token_rows):
    head_dim = scale_vec.shape[0]
    length = projected.shape[1]
    local_heads = projected.shape[0] // 3 // head_dim
    owners, _, tokens = attended_grad.shape
    lanes = 128
    grads, scale_grad = pl.pallas_call(
        functools.partial(attend_back_kernel, token_rows),
        grid=(local_heads,),
        in_specs=[
            pl.BlockSpec((3, 1, head_dim, length), lambda h: (0, h, 0, 0)),
            pl.BlockSpec((owners, 1, head_dim, tokens), lambda h: (0, h, 0, 0)),
            pl.BlockSpec((1, 1, length), lambda h: (h, 0, 0)),
            pl.BlockSpec((head_dim, 1), lambda h: (0, 0)),
            pl.BlockSpec((length, 1), lambda h: (0, 0)),
            pl.BlockSpec((1, length), lambda h: (0, 0)),
        ],
        out_specs=[
            pl.BlockSpec((3, 1, head_dim, length), lambda h: (0, h, 0, 0)),
            pl.BlockSpec((head_dim, lanes), lambda h: (0, 0)),
        ],
        out_shape=[
            jax.ShapeDtypeStruct((3, local_heads, head_dim, length), BF16),
            jax.ShapeDtypeStruct((head_dim, lanes), F32),
        ],
        scratch_shapes=[
            pltpu.VMEM((head_dim, length), F32),
            pltpu.VMEM((head_dim, length), F32),
        ],
        compiler_params=KERNEL,
        cost_estimate=LIGHT,
    )(
        projected.reshape(3, local_heads, head_dim, length),
        attended_grad.reshape(owners, local_heads, head_dim, tokens),
        log_total,
        scale_vec.reshape(head_dim, 1),
        segments.reshape(length, 1),
        segments.reshape(1, length),
    )
    return grads.reshape(3 * local_heads * head_dim, length), scale_grad[:, 0]


def dense_grad_kernel(
    core_ref, attended_ref, normed_ref, active_ref, out_bar, up_bar, down_bar,
    own_ref, other_ref, normed_t, active_t,
):
    tile = pl.program_id(0)
    rows, width = own_ref.shape[2] * own_ref.shape[3] * 2, out_bar.shape[1]

    @pl.when(tile == 0)
    def _():
        normed_t[...] = normed_ref[...].astype(F32).T.astype(BF16)
        active_t[...] = active_ref[...].astype(F32).T.astype(BF16)

    start = pl.multiple_of(tile * rows, rows)
    first_core = core_ref[0] == 0
    lefts = (attended_ref, normed_t, active_t)
    for i, (left, right) in enumerate(zip(lefts, (out_bar, up_bar, down_bar))):
        grad = jnp.dot(left[pl.ds(start, rows), :], right[...], preferred_element_type=F32)
        grad = grad.reshape(2, 2, rows // 4, width)
        one, two = grad[:, 0], grad[:, 1]
        own_ref[0, 0, :, :, i * width : (i + 1) * width] = jnp.where(
            first_core, one, two
        ).astype(BF16)
        other_ref[0, 0, :, :, i * width : (i + 1) * width] = jnp.where(
            first_core, two, one
        ).astype(BF16)


def dense_grads(attended_t, normed, active, out_bar, up_bar, down_bar):
    width, tokens = attended_t.shape
    own = width // 32
    whole = pl.BlockSpec((tokens, width), lambda i, core: (0, 0))
    rows = pl.BlockSpec((1, 1, 2, own, 3 * width), lambda i, core: (i // 2, i % 2, 0, 0, 0))
    shape = jax.ShapeDtypeStruct((4, 2, 2, own, 3 * width), BF16)
    return pl.pallas_call(
        dense_grad_kernel,
        grid_spec=pltpu.PrefetchScalarGridSpec(
            num_scalar_prefetch=1,
            grid=(8,),
            in_specs=[pl.BlockSpec((width, tokens), lambda i, core: (0, 0))] + [whole] * 5,
            out_specs=[rows, rows],
            scratch_shapes=[pltpu.VMEM((width, tokens), BF16)] * 2,
        ),
        out_shape=[shape, shape],
        compiler_params=KERNEL,
        cost_estimate=LIGHT,
    )(place()[2:], attended_t, normed, active, out_bar, up_bar, down_bar)


def place():
    head = lax.axis_index("head")
    return jnp.stack([lax.axis_index("blk"), head // 2, head % 2]).astype(jnp.int32)


def assemble_kernel(place_ref, *refs):
    pieces, whole_ref, sems = refs[:10], refs[10], refs[11]
    half = whole_ref.shape[-1] // 2
    blk, row, core = place_ref[0], place_ref[1], place_ref[2]
    copies = []
    for i in range(2):
        at_core = core if i == 0 else 1 - core
        own, across, beside, one, two = pieces[5 * i : 5 * i + 5]
        for piece, at_blk, at_row, columns in (
            (own, blk, row, None),
            (across, 1 - blk, row, None),
            (beside, blk, 1 - row, None),
            (one, 1 - blk, 1 - row, pl.ds(0, half)),
            (two, 1 - blk, 1 - row, pl.ds(half, half)),
        ):
            target = whole_ref.at[:, at_blk, at_row, at_core]
            if columns is not None:
                target = whole_ref.at[:, at_blk, at_row, at_core, :, columns]
            copies.append(pltpu.make_async_copy(piece, target, sems.at[len(copies)]))
    for copy in copies:
        copy.start()
    for copy in copies:
        copy.wait()


def assemble(pieces):
    batch, own, columns = pieces[0].shape
    whole = pl.pallas_call(
        assemble_kernel,
        grid_spec=pltpu.PrefetchScalarGridSpec(
            num_scalar_prefetch=1,
            grid=(1,),
            in_specs=[pl.BlockSpec(memory_space=pl.ANY)] * 10,
            out_specs=pl.BlockSpec(memory_space=pl.ANY),
            scratch_shapes=[pltpu.SemaphoreType.DMA((10,))],
        ),
        out_shape=jax.ShapeDtypeStruct((batch, 2, 2, 2, own, columns), BF16),
        compiler_params=KERNEL,
        cost_estimate=LIGHT,
    )(place(), *pieces)
    return whole.reshape(-1, columns)


def tied(*arrays):
    return lax.optimization_barrier(arrays)


def swapped(array, axis, mask):
    size = lax.axis_size(axis)
    return lax.ppermute(array, axis, [(i, i ^ mask) for i in range(size)])


def pick(array, index, axis=0):
    return lax.dynamic_index_in_dim(array, index, axis, keepdims=False)


def swap_halves(array):
    me = lax.axis_index("blk")
    got = swapped(pick(array, 1 - me), "blk", 1)
    kept = pick(array, me)
    return jnp.stack([jnp.where(me == 0, kept, got), jnp.where(me == 0, got, kept)])


def gather_rows(rows):
    width = rows.shape[-1]
    far = swapped(rows, "head", 2)
    near = swapped(rows, "head", 1)
    both = swapped(far, "head", 1)
    pieces = jnp.stack([rows, near, far, both])
    me = lax.axis_index("head")
    ordered = jnp.stack([pick(pieces, me ^ i) for i in range(4)])
    return ordered.reshape(4, 2, -1, width).transpose(1, 0, 2, 3).reshape(-1, width)


def scatter_rows(rows):
    width = rows.shape[-1]
    me = lax.axis_index("head")
    row, core = me // 2, me % 2
    parts = rows.reshape(2, 2, 2, -1, width)
    halves = pick(parts, core, 2) + swapped(
        pick(parts, 1 - core, 2).astype(BF16), "head", 1
    ).astype(F32)
    got = swapped(pick(halves, 1 - row, 1).astype(BF16), "head", 2).astype(F32)
    return (pick(halves, row, 1) + got).reshape(-1, width)


def over_head(parts):
    return lax.all_to_all(parts, "head", split_axis=0, concat_axis=0, tiled=True)


def qkv_columns(rows, extra):
    own, width = rows.shape
    part = width // 3 // 4
    sent = rows.reshape(own, 3, 4, part).transpose(2, 0, 1, 3).reshape(4, own, 3 * part)
    if extra is not None:
        sent = jnp.concatenate([sent, jnp.broadcast_to(extra[None], (4,) + extra.shape)], axis=2)
    return over_head(sent)


def along_batch(piece):
    return lax.all_gather(piece, "batch", axis=0, tiled=False)


def along_blk(along):
    other = swapped(along, "blk", 1)
    first = lax.axis_index("blk") == 0
    both = jnp.stack([jnp.where(first, along, other), jnp.where(first, other, along)], axis=1)
    return both.reshape(-1, along.shape[-1])


def other_core(array):
    return swapped(array, "head", 1)


def to_neighbours(along):
    return swapped(along, "blk", 1), swapped(along, "head", 2)


def to_diagonal(across, beside):
    half = across.shape[-1] // 2
    return swapped(across[..., :half], "head", 2), swapped(beside[..., half:], "blk", 1)


def columns_over_blk(grad):
    blk = lax.axis_index("blk")
    parts = grad.reshape(4, 2, -1, grad.shape[1])
    return pick(parts, blk, 1), swapped(pick(parts, 1 - blk, 1).astype(BF16), "blk", 1)


def over_batch(parts):
    return lax.psum_scatter(parts.astype(BF16), "batch", scatter_dimension=0, tiled=False)


def columns_to_rows(summed):
    moved = over_head(summed.reshape(4, -1, summed.shape[-1]))
    rows = moved.shape[1]
    return moved.reshape(4, rows, 3, -1).transpose(1, 2, 0, 3).reshape(rows, -1).astype(F32)


def diagonal_sent(cored):
    blk, row, _ = place()
    rows = pick(pick(cored, 1 - blk, 1), 1 - row, 1)
    half = rows.shape[-1] // 2
    return swapped(rows[..., :half], "blk", 1), swapped(rows[..., half:], "head", 2)


def neighbours_sent(cored, one, two):
    blk, row, _ = place()
    half = one.shape[-1]
    across = pick(pick(cored, 1 - blk, 1), row, 1)
    beside = pick(pick(cored, blk, 1), 1 - row, 1)
    across = jnp.concatenate(
        [across[..., :half], across[..., half:].astype(F32) + two.astype(F32)], axis=-1
    ).astype(BF16)
    beside = jnp.concatenate(
        [beside[..., :half].astype(F32) + one.astype(F32), beside[..., half:]], axis=-1
    ).astype(BF16)
    return swapped(across, "blk", 1), swapped(beside, "head", 2)


def own_sum(cored, across, beside):
    blk, row, _ = place()
    own = pick(pick(cored, blk, 1), row, 1)
    return own.astype(F32) + across.astype(F32) + beside.astype(F32)


def sum_all(array):
    for axis, mask in (("head", 1), ("head", 2), ("blk", 1), ("batch", 1), ("batch", 2)):
        array = array + swapped(array, axis, mask)
    return array


def gain_back(weight, weight_grad, gain):
    return jnp.sum(weight.astype(F32) * weight_grad, axis=-1) / gain.astype(F32)


def lower_of(upper, stream, factor, gain):
    return norm_back(upper, stream, factor, gain)[0]


def spread_device(
    tokens,
    segments,
    qkv_weight,
    out_weight,
    up_weight,
    down_weight,
    attn_gain,
    mlp_gain,
    scale_param,
    cotangent,
):
    layers, head_dim = scale_param.shape
    _, token_rows, width = tokens.shape
    scale_vecs = SCALE_BASE / math.sqrt(head_dim) * jax.nn.softplus(scale_param)
    segments = pick(segments, lax.axis_index("blk"))
    own_gains = jnp.concatenate([attn_gain, mlp_gain], axis=0)

    first = swap_halves(tokens).reshape(-1, width)
    columns = [qkv_columns(qkv_weight[0], own_gains.T)]
    columns[0], first = tied(columns[0], first)
    first_all = gather_rows(first)
    stream = first.astype(F32)
    first_columns = columns[0].reshape(-1, columns[0].shape[-1])
    part3 = 3 * width // 4
    dense_own = [
        jnp.concatenate([out_weight[i], up_weight[i], down_weight[i]], axis=1) for i in (0, 1)
    ]
    along = along_batch(first_columns)
    dense_along = [along_batch(dense_own[0]), None]
    with_gains = along_blk(along)
    qkvs = [with_gains[:, :part3], None]
    gains = with_gains[:, part3:].T.astype(F32)
    near = [to_neighbours(dense_along[0]), None]
    next_along = along_batch(qkv_columns(qkv_weight[1], None).reshape(-1, part3))
    dense_along[1] = along_batch(dense_own[1])

    def dense_of(layer):
        pieces = (dense_along[layer],) + near[layer] + to_diagonal(*near[layer])
        return assemble(pieces + tuple(other_core(piece) for piece in pieces))

    kept, denses = [], []
    for layer in range(layers):
        qkv = qkvs[layer]
        normed, factor_one = normalize(stream, gains[layer])
        if layer == 0:
            normed_all = normalize(first_all.astype(F32), gains[0])[0].astype(BF16)
        else:
            normed_all = gather_rows(normed.astype(BF16))
        projected = lax.dot_general(
            qkv, normed_all, (((0,), (1,)), ((), ())), preferred_element_type=F32
        )
        attended, log_total = attend_rows(
            projected, scale_vecs[layer], segments, 4, token_rows
        )
        if layer == 0:
            attended, near[0] = tied(attended, near[0])
        else:
            attended, near[1] = tied(attended, near[1])
        denses.append(dense_of(layer))
        dense = denses[layer]
        out_w, up_w, down_w = dense[:, :width], dense[:, width:-width], dense[:, -width:]
        attended_t = over_head(attended).reshape(width, -1)
        middle = stream + dot_rows(attended_t, out_w)
        if layer == 0:
            middle, next_along, dense_along[1] = tied(middle, next_along, dense_along[1])
            qkvs[1] = along_blk(next_along)
            near[1] = to_neighbours(dense_along[1])
        normed_two, factor_two = normalize(middle, gains[layers + layer])
        normed_two = normed_two.astype(BF16)
        hidden = dot(normed_two, up_w)
        active = (hidden * jax.nn.sigmoid(hidden)).astype(BF16)
        kept.append(
            (
                stream, factor_one, normed_all, projected, log_total, attended_t, middle,
                factor_two, normed_two, hidden, active,
            )
        )
        stream = middle + dot(active, down_w)
    layer_out = swap_halves(stream.astype(BF16).reshape(tokens.shape))
    upper = swap_halves(cotangent).reshape(-1, width).astype(F32)

    qkv_grads, dense_grad, scale_grads = [None] * layers, [None] * layers, [None] * layers
    for layer in reversed(range(layers)):
        (
            stream, factor_one, normed_all, projected, log_total, attended_t, middle,
            factor_two, normed_two, hidden, active,
        ) = kept[layer]
        qkv, dense = qkvs[layer], denses[layer]
        out_w, up_w, down_w = dense[:, :width], dense[:, width:-width], dense[:, -width:]
        down_bar = upper.astype(BF16)
        gate = jax.nn.sigmoid(hidden)
        up_bar = (
            dot_cols(down_bar, down_w) * gate * (1.0 + hidden * (1.0 - gate))
        ).astype(BF16)
        middle_grad = upper + lower_of(
            dot_cols(up_bar, up_w), middle, factor_two, gains[layers + layer]
        )
        out_bar = middle_grad.astype(BF16)
        attended_grad = over_head(dot_cols(out_w, out_bar).astype(BF16).reshape(4, -1, out_bar.shape[0]))
        grads, others = dense_grads(attended_t, normed_two, active, out_bar, up_bar, down_bar)
        if layer == 0:
            attended_grad, others, sent, later = tied(attended_grad, others, sent, later)
            dense_grad[1] = over_batch(own_sum(cored, *sent))
            qkv_sum = over_batch(later[0] + later[1].astype(F32))
        else:
            attended_grad, others = tied(attended_grad, others)
        others = other_core(others)
        bars, scale_grads[layer] = attend_back_rows(
            projected, attended_grad, log_total, scale_vecs[layer], segments, token_rows
        )
        bars, others = tied(bars, others)
        cored = (grads.astype(F32) + others.astype(F32)).astype(BF16)
        diagonal = diagonal_sent(cored)
        normed_grad = scatter_rows(
            lax.dot_general(bars, qkv, (((0,), (1,)), ((), ())), preferred_element_type=F32)
        )
        later = columns_over_blk(
            lax.dot_general(normed_all, bars, (((0,), (1,)), ((), ())), preferred_element_type=F32)
        )
        normed_grad, diagonal = tied(normed_grad, diagonal)
        sent = neighbours_sent(cored, *diagonal)
        if layer == 0:
            dense_grad[0] = over_batch(own_sum(cored, *sent))
            qkv_grads[1] = columns_to_rows(qkv_sum)
            qkv_grads[0] = columns_to_rows(over_batch(later[0] + later[1].astype(F32)))
        upper = middle_grad + lower_of(normed_grad, stream, factor_one, gains[layer])
    input_grad = swap_halves(upper.astype(BF16).reshape(tokens.shape)).astype(F32)
    scale_total = sum_all(jnp.stack(scale_grads))
    scale_grad = scale_total * (SCALE_BASE / math.sqrt(head_dim)) * jax.nn.sigmoid(scale_param)
    dense_all = jnp.stack([part.astype(F32) for part in dense_grad])
    qkv_all = jnp.stack(qkv_grads)
    up_all = dense_all[:, :, width:-width]
    return (
        layer_out,
        input_grad,
        qkv_all,
        dense_all[:, :, :width],
        up_all,
        dense_all[:, :, -width:],
        gain_back(qkv_weight, qkv_all, attn_gain),
        gain_back(up_weight, up_all, mlp_gain),
        scale_grad,
    )


def per_device(*args):
    tokens, segments = args[0], args[1]
    sizes = tuple(lax.axis_size(axis) for axis in ALL)
    heads = tokens.shape[2] // args[8].shape[1]
    spread = (
        sizes == (4, 2, 4)
        and tokens.shape[0] == 2
        and args[2].shape[0] == 2
        and tokens.shape[1] % 128 == 0
        and Q_ROWS % tokens.shape[1] == 0
        and segments.shape[1] <= WINDOW
        and segments.shape[1] % Q_ROWS == 0
        and heads % 4 == 0
        and tokens.shape[2] % 256 == 0
    )
    return spread_device(*args) if spread else general_device(*args)


def solution(mesh):
    rows = P(None, ALL, None)
    by_token = P("batch", ("blk", "head"), None)
    return jax.shard_map(
        per_device,
        mesh=mesh,
        in_specs=(
            by_token, P("batch", None), rows, rows, rows, rows, P(None, ALL), P(None, ALL), P(),
            by_token,
        ),
        out_specs=(
            by_token, by_token, rows, rows, rows, rows, P(None, ALL), P(None, ALL), P(),
        ),
        check_vma=False,
    )
```

```python
import functools
import math

import jax
import jax.numpy as jnp
from jax import lax
from jax.experimental import pallas as pl
from jax.experimental.pallas import tpu as pltpu
from jax.sharding import PartitionSpec as P

WINDOW = 1024
EPSILON = 1e-06
SCALE_BASE = 1.4426950408889634
MASKED_SCORE = -1e30

ALL = ("batch", "blk", "head")
REST = ("batch", "blk")
F32 = jnp.float32
BF16 = jnp.bfloat16


def shifted(block, axis, distance):
    devices = range(lax.axis_size(axis))
    route = [(i - distance, i) for i in devices if i - distance in devices]
    return lax.ppermute(block, axis, route)


NT = (((1,), (1,)), ((), ()))
TN = (((0,), (0,)), ((), ()))


def dot(left, right):
    return jnp.dot(left, right, preferred_element_type=F32)


def dot_rows(left, right):
    return lax.dot_general(left, right, (((0,), (0,)), ((), ())), preferred_element_type=F32)


def dot_cols(left, right):
    return lax.dot_general(left, right, (((1,), (1,)), ((), ())), preferred_element_type=F32)


def normalize(stream, gain):
    factor = lax.rsqrt(jnp.mean(stream * stream, axis=-1, keepdims=True) + EPSILON)
    return stream * factor * gain, factor


def norm_back(upper, stream, factor, gain):
    inner = upper * gain
    gain_grad = jnp.sum(upper * stream * factor, axis=0)
    lower = factor * inner - stream * factor * factor * factor * jnp.mean(
        inner * stream, axis=-1, keepdims=True
    )
    return lower, gain_grad


class Plan:
    def __init__(self, tokens):
        self.seqs, self.rows, self.width = tokens.shape
        self.heads = lax.axis_size("head")
        self.blks = lax.axis_size("blk")
        self.block = self.rows * self.heads
        self.whole = self.seqs % self.blks == 0
        if self.whole:
            self.groups, self.own_seqs = self.blks, self.seqs // self.blks
            self.reach = 0
        else:
            self.groups, self.own_seqs = 1, self.seqs
            self.reach = min((WINDOW - 1) // self.block + 1, self.blks - 1)
        self.length = self.groups * self.block
        self.tokens = self.seqs * self.rows


def to_plan(plan, array):
    if plan.whole and plan.blks > 1:
        array = lax.all_to_all(array, "blk", split_axis=0, concat_axis=0, tiled=True)
    return array.reshape(plan.tokens, plan.width)


def from_plan(plan, flat):
    array = flat.reshape(plan.seqs, plan.rows, plan.width)
    if plan.whole and plan.blks > 1:
        array = lax.all_to_all(array, "blk", split_axis=0, concat_axis=0, tiled=True)
    return array


def in_sequence(plan, by_head, width):
    parts = by_head.reshape(plan.heads, plan.groups, plan.own_seqs, plan.rows, width)
    return parts.transpose(2, 1, 0, 3, 4).reshape(-1, width)


def by_owner(plan, rows, width):
    parts = rows.reshape(plan.own_seqs, plan.groups, plan.heads, plan.rows, width)
    return parts.transpose(2, 1, 0, 3, 4).reshape(plan.heads, plan.tokens, width)


def gather_tokens(plan, rows):
    moved = lax.all_gather(rows, "head", axis=0, tiled=False)
    return in_sequence(plan, moved, rows.shape[-1])


def scatter_tokens(plan, rows):
    width = rows.shape[-1]
    return lax.psum_scatter(
        by_owner(plan, rows.astype(BF16), width), "head", scatter_dimension=0, tiled=False
    ).astype(F32)


def heads_to_tokens(plan, rows):
    part = rows.shape[-1]
    moved = lax.all_to_all(
        by_owner(plan, rows, part), "head", split_axis=0, concat_axis=0, tiled=True
    )
    return moved.transpose(1, 0, 2).reshape(plan.tokens, plan.heads * part)


def tokens_to_heads(plan, rows):
    part = rows.shape[-1] // plan.heads
    sent = rows.reshape(plan.tokens, plan.heads, part).transpose(1, 0, 2)
    moved = lax.all_to_all(sent, "head", split_axis=0, concat_axis=0, tiled=True)
    return in_sequence(plan, moved, part)


def gather_qkv(rows):
    own, width = rows.shape
    heads = lax.axis_size("head")
    part = width // 3 // heads
    sent = rows.reshape(own, 3, heads, part).transpose(2, 0, 1, 3).reshape(heads, own, 3 * part)
    moved = lax.all_to_all(sent, "head", split_axis=0, concat_axis=0, tiled=True)
    full = lax.all_gather(moved, REST, axis=0, tiled=True)
    return full.reshape(-1, 3 * part)


def scatter_qkv(grad):
    heads = lax.axis_size("head")
    part = grad.shape[1] // 3
    summed = lax.psum_scatter(grad.astype(BF16), REST, scatter_dimension=0, tiled=True)
    own = summed.shape[0] // heads
    moved = lax.all_to_all(
        summed.reshape(heads, own, 3 * part), "head", split_axis=0, concat_axis=0, tiled=True
    )
    return (
        moved.reshape(heads, own, 3, part)
        .transpose(1, 2, 0, 3)
        .reshape(own, 3 * heads * part)
        .astype(F32)
    )


def window_mask(plan, segments, block_index):
    key_count = plan.length + plan.reach * plan.block
    if plan.whole:
        query_segs, key_segs = segments, segments
    else:
        leading = jnp.full((plan.own_seqs, plan.reach * plan.block), -1, jnp.int32)
        padded = jnp.concatenate([leading, segments], axis=1)
        start = block_index * plan.block
        query_segs = lax.dynamic_slice_in_dim(segments, start, plan.block, 1)
        key_segs = lax.dynamic_slice_in_dim(padded, start, key_count, 1)
    query_place = jnp.arange(plan.length, dtype=jnp.int32)[:, None] + plan.reach * plan.block
    key_place = jnp.arange(key_count, dtype=jnp.int32)[None, :]
    near = (key_place <= query_place) & (query_place - key_place < WINDOW)
    return (key_segs[:, None, :] == query_segs[:, :, None]) & near[None]


def with_earlier(plan, own):
    arrived = [own]
    for _ in range(plan.reach):
        arrived.append(shifted(arrived[-1], "blk", 1))
    return jnp.concatenate(arrived[::-1], axis=1) if plan.reach else own


def to_earlier(plan, grads):
    if not plan.reach:
        return grads
    block = plan.block
    total = grads[:, :block]
    for step in range(1, plan.reach + 1):
        total = (
            shifted(total.astype(BF16), "blk", -1).astype(F32)
            + grads[:, step * block : (step + 1) * block]
        )
    return total


def scores_of(queries, keys, allowed):
    scores = jnp.einsum("sqhd,skhd->shqk", queries, keys, preferred_element_type=F32)
    return jnp.where(allowed[:, None], scores, MASKED_SCORE)


def attend(queries, keys, values, allowed):
    scores = scores_of(queries, keys, allowed)
    top_score = jnp.max(scores, axis=-1, keepdims=True)
    exp_terms = jnp.exp(scores - top_score)
    totals = jnp.sum(exp_terms, axis=-1, keepdims=True)
    probs_low = (exp_terms / totals).astype(BF16)
    attended = jnp.einsum("shqk,skhd->sqhd", probs_low, values, preferred_element_type=F32)
    return attended, top_score + jnp.log(totals)


def attend_back(queries, keys, values, allowed, log_total, attended_grad):
    probs = jnp.exp(scores_of(queries, keys, allowed) - log_total)
    probs_low = probs.astype(BF16)
    values_grad = jnp.einsum(
        "shqk,sqhd->skhd", probs_low, attended_grad, preferred_element_type=F32
    )
    probs_grad = jnp.einsum("sqhd,skhd->shqk", attended_grad, values, preferred_element_type=F32)
    row_dot = jnp.sum(probs_grad * probs, axis=-1, keepdims=True)
    scores_low = (probs * (probs_grad - row_dot)).astype(BF16)
    queries_grad = jnp.einsum("shqk,skhd->sqhd", scores_low, keys, preferred_element_type=F32)
    keys_grad = jnp.einsum("shqk,sqhd->skhd", scores_low, queries, preferred_element_type=F32)
    return queries_grad, keys_grad, values_grad


def forward(plan, stream, qkv, dense, gains, scale_vec, allowed):
    width = plan.width
    head_dim = scale_vec.shape[0]
    part = qkv.shape[1] // 3
    local_heads = part // head_dim
    split = (plan.own_seqs, plan.length, local_heads, head_dim)
    out_w, up_w, down_w = dense[:, :width], dense[:, width:-width], dense[:, -width:]
    normed, factor_one = normalize(stream, gains[0])
    normed_all = gather_tokens(plan, normed.astype(BF16))
    projected = dot(normed_all, qkv)
    query_pre = projected[:, :part].reshape(split)
    queries = (query_pre * scale_vec).astype(BF16)
    keys = with_earlier(plan, projected[:, part : 2 * part].astype(BF16).reshape(split))
    values = with_earlier(plan, projected[:, 2 * part :].astype(BF16).reshape(split))
    attended_part, log_total = attend(queries, keys, values, allowed)
    attended = heads_to_tokens(plan, attended_part.astype(BF16).reshape(-1, part))
    middle = stream + dot(attended, out_w)
    normed_two, factor_two = normalize(middle, gains[1])
    normed_two = normed_two.astype(BF16)
    hidden = dot(normed_two, up_w)
    active = (hidden * jax.nn.sigmoid(hidden)).astype(BF16)
    result = middle + dot(active, down_w)
    kept = (
        stream, factor_one, normed_all, query_pre, queries, keys, values, log_total,
        attended, middle, factor_two, normed_two, hidden, active,
    )
    return result, kept


def backward(plan, upper, kept, qkv, dense, gains, scale_vec, allowed):
    (
        stream, factor_one, normed_all, query_pre, queries, keys, values, log_total,
        attended, middle, factor_two, normed_two, hidden, active,
    ) = kept
    width = plan.width
    head_dim = scale_vec.shape[0]
    part = qkv.shape[1] // 3
    out_w, up_w, down_w = dense[:, :width], dense[:, width:-width], dense[:, -width:]
    upper_low = upper.astype(BF16)
    down_grad = dot_rows(active, upper_low)
    active_grad = dot_cols(upper_low, down_w)
    gate = jax.nn.sigmoid(hidden)
    hidden_low = (active_grad * gate * (1.0 + hidden * (1.0 - gate))).astype(BF16)
    up_grad = dot_rows(normed_two, hidden_low)
    extra_two, mlp_gain_grad = norm_back(dot_cols(hidden_low, up_w), middle, factor_two, gains[1])
    middle_grad = upper + extra_two
    middle_low = middle_grad.astype(BF16)
    out_grad = dot_rows(attended, middle_low)
    dense_grad = jnp.concatenate([out_grad, up_grad, down_grad], axis=1).astype(BF16)
    dense_own = lax.psum_scatter(dense_grad, ALL, scatter_dimension=0, tiled=True)
    attended_grad = tokens_to_heads(plan, dot_cols(middle_low, out_w).astype(BF16))
    queries_grad, keys_grad, values_grad = attend_back(
        queries, keys, values, allowed, log_total, attended_grad.reshape(queries.shape)
    )
    query_bar = queries_grad.astype(BF16).astype(F32)
    scale_vec_grad = jnp.sum((query_bar * query_pre).reshape(-1, head_dim), axis=0)
    query_low = (query_bar * scale_vec).astype(BF16).reshape(-1, part)
    keys_low = to_earlier(plan, keys_grad).astype(BF16).reshape(-1, part)
    values_low = to_earlier(plan, values_grad).astype(BF16).reshape(-1, part)
    projected_low = jnp.concatenate([query_low, keys_low, values_low], axis=1)
    normed_grad = scatter_tokens(plan, dot_cols(projected_low, qkv))
    qkv_own = scatter_qkv(dot_rows(normed_all, projected_low))
    extra_one, attn_gain_grad = norm_back(normed_grad, stream, factor_one, gains[0])
    lower = middle_grad + extra_one
    return lower, qkv_own, dense_own, (attn_gain_grad, mlp_gain_grad), scale_vec_grad


def general_device(
    tokens,
    segments,
    qkv_weight,
    out_weight,
    up_weight,
    down_weight,
    attn_gain,
    mlp_gain,
    scale_param,
    cotangent,
):
    plan = Plan(tokens)
    layers, head_dim = scale_param.shape
    block_index = lax.axis_index("blk")
    scale_vecs = SCALE_BASE / math.sqrt(head_dim) * jax.nn.softplus(scale_param)
    own_gains = jnp.concatenate([attn_gain, mlp_gain], axis=0)
    gains = (
        lax.all_gather(own_gains.reshape(1, -1), ALL, axis=0, tiled=True)
        .reshape(-1, 2 * layers, attn_gain.shape[1])
        .transpose(1, 0, 2)
        .reshape(2 * layers, plan.width)
        .astype(F32)
    )
    if plan.whole:
        segments = lax.dynamic_slice_in_dim(
            segments, block_index * plan.own_seqs, plan.own_seqs, 0
        )
    allowed = window_mask(plan, segments, block_index)
    stream = to_plan(plan, tokens).astype(F32)
    qkvs, denses, kept = [], [], []
    for layer in range(layers):
        qkvs.append(gather_qkv(qkv_weight[layer]))
        own = jnp.concatenate([out_weight[layer], up_weight[layer], down_weight[layer]], axis=1)
        denses.append(lax.all_gather(own, ALL, axis=0, tiled=True))
        layer_gains = (gains[layer], gains[layers + layer])
        stream, saved = forward(
            plan, stream, qkvs[layer], denses[layer], layer_gains, scale_vecs[layer], allowed
        )
        kept.append(saved)
    layer_out = from_plan(plan, stream.astype(BF16))
    upper = to_plan(plan, cotangent).astype(F32)
    qkv_grads, dense_grads = [None] * layers, [None] * layers
    gain_grads, scale_grads = [None] * layers, [None] * layers
    for layer in reversed(range(layers)):
        layer_gains = (gains[layer], gains[layers + layer])
        upper, qkv_grads[layer], dense_grads[layer], gain_grads[layer], scale_grads[layer] = (
            backward(
                plan, upper, kept[layer], qkvs[layer], denses[layer], layer_gains,
                scale_vecs[layer], allowed,
            )
        )
    input_grad = from_plan(plan, upper.astype(BF16)).astype(F32)
    small = jnp.concatenate(
        [g[0] for g in gain_grads] + [g[1] for g in gain_grads] + scale_grads, axis=0
    )
    total = lax.psum(small, ALL)
    gain_total = total[: 2 * layers * plan.width].reshape(2 * layers, plan.width)
    owner = lax.axis_index(ALL)
    gain_rows = attn_gain.shape[1]
    own_total = lax.dynamic_slice_in_dim(gain_total, owner * gain_rows, gain_rows, 1)
    scale_total = total[2 * layers * plan.width :].reshape(layers, head_dim)
    scale_grad = scale_total * (SCALE_BASE / math.sqrt(head_dim)) * jax.nn.sigmoid(scale_param)
    dense_all = jnp.stack(dense_grads).astype(F32)
    width = plan.width
    return (
        layer_out,
        input_grad,
        jnp.stack(qkv_grads),
        dense_all[:, :, :width],
        dense_all[:, :, width:-width],
        dense_all[:, :, -width:],
        own_total[:layers],
        own_total[layers:],
        scale_grad,
    )


Q_ROWS = 256
KERNEL = pltpu.CompilerParams(vmem_limit_bytes=50 * 1024 * 1024)
LIGHT = pl.CostEstimate(flops=1 << 20, bytes_accessed=1 << 20, transcendentals=0)


def allowed_keys(col, row, first):
    count = first + row.shape[1]
    key_place = lax.broadcasted_iota(jnp.int32, (count, row.shape[1]), 0)
    query_place = lax.broadcasted_iota(jnp.int32, (count, row.shape[1]), 1) + first
    return (col[:count] == row) & (key_place <= query_place)


def token_places(length, heads, token_rows):
    for first in range(0, length, Q_ROWS):
        parts = []
        for start in range(0, Q_ROWS, token_rows):
            place = (first + start) // token_rows
            parts.append((start, place % heads, place // heads * token_rows))
        yield first, parts


def attend_kernel(token_rows, proj_ref, scale_ref, col_ref, row_ref, out_ref, lse_ref):
    length = proj_ref.shape[-1]
    queries = (proj_ref[0, 0] * scale_ref[...]).astype(BF16)
    keys = proj_ref[1, 0].T.astype(BF16)
    values = proj_ref[2, 0].astype(BF16)
    for first, parts in token_places(length, out_ref.shape[0], token_rows):
        end = first + Q_ROWS
        scores = jnp.dot(keys[:end], queries[:, first:end], preferred_element_type=F32)
        allowed = allowed_keys(col_ref[...], row_ref[:, first:end], first)
        scores = jnp.where(allowed, scores, MASKED_SCORE)
        top = jnp.max(scores, axis=0, keepdims=True)
        terms = jnp.exp(scores - top)
        total = jnp.sum(terms, axis=0, keepdims=True)
        probs = (terms * (1.0 / total)).astype(BF16)
        attended = jnp.dot(values[:, :end], probs, preferred_element_type=F32).astype(BF16)
        lse_ref[0, :, first:end] = top + jnp.log(total)
        for start, owner, offset in parts:
            out_ref[owner, 0, :, offset : offset + token_rows] = attended[
                :, start : start + token_rows
            ]


def attend_rows(projected, scale_vec, segments, owners, token_rows):
    head_dim = scale_vec.shape[0]
    length = projected.shape[1]
    local_heads = projected.shape[0] // 3 // head_dim
    tokens = length // owners
    attended, log_total = pl.pallas_call(
        functools.partial(attend_kernel, token_rows),
        grid=(local_heads,),
        in_specs=[
            pl.BlockSpec((3, 1, head_dim, length), lambda h: (0, h, 0, 0)),
            pl.BlockSpec((head_dim, 1), lambda h: (0, 0)),
            pl.BlockSpec((length, 1), lambda h: (0, 0)),
            pl.BlockSpec((1, length), lambda h: (0, 0)),
        ],
        out_specs=[
            pl.BlockSpec((owners, 1, head_dim, tokens), lambda h: (0, h, 0, 0)),
            pl.BlockSpec((1, 1, length), lambda h: (h, 0, 0)),
        ],
        out_shape=[
            jax.ShapeDtypeStruct((owners, local_heads, head_dim, tokens), BF16),
            jax.ShapeDtypeStruct((local_heads, 1, length), F32),
        ],
        compiler_params=KERNEL,
        cost_estimate=LIGHT,
    )(
        projected.reshape(3, local_heads, head_dim, length),
        scale_vec.reshape(head_dim, 1),
        segments.reshape(length, 1),
        segments.reshape(1, length),
    )
    return attended.reshape(owners, local_heads * head_dim, tokens), log_total


def attend_back_kernel(
    token_rows,
    proj_ref,
    grad_ref,
    lse_ref,
    scale_ref,
    col_ref,
    row_ref,
    out_ref,
    scale_grad_ref,
    keys_acc,
    values_acc,
):
    length = proj_ref.shape[-1]
    scale = scale_ref[...]
    query_pre = proj_ref[0, 0]
    queries = (query_pre * scale).astype(BF16)
    keys_t = proj_ref[1, 0].astype(BF16)
    keys = proj_ref[1, 0].T.astype(BF16)
    values = proj_ref[2, 0].T.astype(BF16)
    keys_acc[...] = jnp.zeros_like(keys_acc)
    values_acc[...] = jnp.zeros_like(values_acc)
    scale_grad = jnp.zeros((scale.shape[0], 1), F32)
    for first, parts in token_places(length, grad_ref.shape[0], token_rows):
        end = first + Q_ROWS
        block = queries[:, first:end]
        grad = jnp.concatenate(
            [grad_ref[owner, 0, :, at : at + token_rows] for _, owner, at in parts], axis=1
        )
        scores = jnp.dot(keys[:end], block, preferred_element_type=F32)
        allowed = allowed_keys(col_ref[...], row_ref[:, first:end], first)
        scores = jnp.where(allowed, scores, MASKED_SCORE)
        probs = jnp.exp(scores - lse_ref[0, :, first:end])
        probs_grad = jnp.dot(values[:end], grad, preferred_element_type=F32)
        row_dot = jnp.sum(probs_grad * probs, axis=0, keepdims=True)
        scores_low = (probs * (probs_grad - row_dot)).astype(BF16)
        values_acc[:, :end] += lax.dot_general(
            grad, probs.astype(BF16), NT, preferred_element_type=F32
        )
        keys_acc[:, :end] += lax.dot_general(
            block, scores_low, NT, preferred_element_type=F32
        )
        query_bar = jnp.dot(keys_t[:, :end], scores_low, preferred_element_type=F32)
        query_bar = query_bar.astype(BF16).astype(F32)
        scale_grad += jnp.sum(query_bar * query_pre[:, first:end], axis=1, keepdims=True)
        out_ref[0, 0, :, first:end] = (query_bar * scale).astype(BF16)
    out_ref[1, 0] = keys_acc[...].astype(BF16)
    out_ref[2, 0] = values_acc[...].astype(BF16)
    spread = jnp.broadcast_to(scale_grad, scale_grad_ref.shape)

    @pl.when(pl.program_id(0) == 0)
    def _():
        scale_grad_ref[...] = spread

    @pl.when(pl.program_id(0) > 0)
    def _():
        scale_grad_ref[...] += spread


def attend_back_rows(projected, attended_grad, log_total, scale_vec, segments, token_rows):
    head_dim = scale_vec.shape[0]
    length = projected.shape[1]
    local_heads = projected.shape[0] // 3 // head_dim
    owners, _, tokens = attended_grad.shape
    lanes = 128
    grads, scale_grad = pl.pallas_call(
        functools.partial(attend_back_kernel, token_rows),
        grid=(local_heads,),
        in_specs=[
            pl.BlockSpec((3, 1, head_dim, length), lambda h: (0, h, 0, 0)),
            pl.BlockSpec((owners, 1, head_dim, tokens), lambda h: (0, h, 0, 0)),
            pl.BlockSpec((1, 1, length), lambda h: (h, 0, 0)),
            pl.BlockSpec((head_dim, 1), lambda h: (0, 0)),
            pl.BlockSpec((length, 1), lambda h: (0, 0)),
            pl.BlockSpec((1, length), lambda h: (0, 0)),
        ],
        out_specs=[
            pl.BlockSpec((3, 1, head_dim, length), lambda h: (0, h, 0, 0)),
            pl.BlockSpec((head_dim, lanes), lambda h: (0, 0)),
        ],
        out_shape=[
            jax.ShapeDtypeStruct((3, local_heads, head_dim, length), BF16),
            jax.ShapeDtypeStruct((head_dim, lanes), F32),
        ],
        scratch_shapes=[
            pltpu.VMEM((head_dim, length), F32),
            pltpu.VMEM((head_dim, length), F32),
        ],
        compiler_params=KERNEL,
        cost_estimate=LIGHT,
    )(
        projected.reshape(3, local_heads, head_dim, length),
        attended_grad.reshape(owners, local_heads, head_dim, tokens),
        log_total,
        scale_vec.reshape(head_dim, 1),
        segments.reshape(length, 1),
        segments.reshape(1, length),
    )
    return grads.reshape(3 * local_heads * head_dim, length), scale_grad[:, 0]


def dense_grad_kernel(
    core_ref, attended_ref, normed_ref, active_ref, out_bar, up_bar, down_bar,
    own_ref, other_ref, normed_t, active_t,
):
    tile = pl.program_id(0)
    rows, width = own_ref.shape[2] * own_ref.shape[3] * 2, out_bar.shape[1]

    @pl.when(tile == 0)
    def _():
        normed_t[...] = normed_ref[...].astype(F32).T.astype(BF16)
        active_t[...] = active_ref[...].astype(F32).T.astype(BF16)

    start = pl.multiple_of(tile * rows, rows)
    first_core = core_ref[0] == 0
    lefts = (attended_ref, normed_t, active_t)
    for i, (left, right) in enumerate(zip(lefts, (out_bar, up_bar, down_bar))):
        grad = jnp.dot(left[pl.ds(start, rows), :], right[...], preferred_element_type=F32)
        grad = grad.reshape(2, 2, rows // 4, width)
        one, two = grad[:, 0], grad[:, 1]
        own_ref[0, 0, :, :, i * width : (i + 1) * width] = jnp.where(
            first_core, one, two
        ).astype(BF16)
        other_ref[0, 0, :, :, i * width : (i + 1) * width] = jnp.where(
            first_core, two, one
        ).astype(BF16)


def dense_grads(attended_t, normed, active, out_bar, up_bar, down_bar):
    width, tokens = attended_t.shape
    own = width // 32
    whole = pl.BlockSpec((tokens, width), lambda i, core: (0, 0))
    rows = pl.BlockSpec((1, 1, 2, own, 3 * width), lambda i, core: (i // 2, i % 2, 0, 0, 0))
    shape = jax.ShapeDtypeStruct((4, 2, 2, own, 3 * width), BF16)
    return pl.pallas_call(
        dense_grad_kernel,
        grid_spec=pltpu.PrefetchScalarGridSpec(
            num_scalar_prefetch=1,
            grid=(8,),
            in_specs=[pl.BlockSpec((width, tokens), lambda i, core: (0, 0))] + [whole] * 5,
            out_specs=[rows, rows],
            scratch_shapes=[pltpu.VMEM((width, tokens), BF16)] * 2,
        ),
        out_shape=[shape, shape],
        compiler_params=KERNEL,
        cost_estimate=LIGHT,
    )(place()[2:], attended_t, normed, active, out_bar, up_bar, down_bar)


def place():
    head = lax.axis_index("head")
    return jnp.stack([lax.axis_index("blk"), head // 2, head % 2]).astype(jnp.int32)


def assemble_kernel(place_ref, *refs):
    pieces, whole_ref = refs[:10], refs[10]
    half = whole_ref.shape[-1] // 2
    blk, row, core = place_ref[0], place_ref[1], place_ref[2]
    for i in range(2):
        at_core = core if i == 0 else 1 - core
        own, across, beside, one, two = pieces[5 * i : 5 * i + 5]
        whole_ref[0, blk, row, at_core] = own[0]
        whole_ref[0, 1 - blk, row, at_core] = across[0]
        whole_ref[0, blk, 1 - row, at_core] = beside[0]
        whole_ref[0, 1 - blk, 1 - row, at_core, :, :half] = one[0]
        whole_ref[0, 1 - blk, 1 - row, at_core, :, half:] = two[0]


def assemble(pieces):
    batch, own, columns = pieces[0].shape
    specs = [
        pl.BlockSpec((1, own, piece.shape[-1]), lambda i, at: (i, 0, 0)) for piece in pieces
    ]
    whole = pl.pallas_call(
        assemble_kernel,
        grid_spec=pltpu.PrefetchScalarGridSpec(
            num_scalar_prefetch=1,
            grid=(batch,),
            in_specs=specs,
            out_specs=pl.BlockSpec((1, 2, 2, 2, own, columns), lambda i, at: (i, 0, 0, 0, 0, 0)),
        ),
        out_shape=jax.ShapeDtypeStruct((batch, 2, 2, 2, own, columns), BF16),
        compiler_params=KERNEL,
        cost_estimate=LIGHT,
    )(place(), *pieces)
    return whole.reshape(-1, columns)


def tied(*arrays):
    return lax.optimization_barrier(arrays)


def swapped(array, axis, mask):
    size = lax.axis_size(axis)
    return lax.ppermute(array, axis, [(i, i ^ mask) for i in range(size)])


def pick(array, index, axis=0):
    return lax.dynamic_index_in_dim(array, index, axis, keepdims=False)


def swap_halves(array):
    me = lax.axis_index("blk")
    got = swapped(pick(array, 1 - me), "blk", 1)
    kept = pick(array, me)
    return jnp.stack([jnp.where(me == 0, kept, got), jnp.where(me == 0, got, kept)])


def gather_rows(rows):
    width = rows.shape[-1]
    far = swapped(rows, "head", 2)
    near = swapped(rows, "head", 1)
    both = swapped(far, "head", 1)
    pieces = jnp.stack([rows, near, far, both])
    me = lax.axis_index("head")
    ordered = jnp.stack([pick(pieces, me ^ i) for i in range(4)])
    return ordered.reshape(4, 2, -1, width).transpose(1, 0, 2, 3).reshape(-1, width)


def scatter_rows(rows):
    width = rows.shape[-1]
    me = lax.axis_index("head")
    row, core = me // 2, me % 2
    parts = rows.reshape(2, 2, 2, -1, width)
    halves = pick(parts, core, 2) + swapped(
        pick(parts, 1 - core, 2).astype(BF16), "head", 1
    ).astype(F32)
    got = swapped(pick(halves, 1 - row, 1).astype(BF16), "head", 2).astype(F32)
    return (pick(halves, row, 1) + got).reshape(-1, width)


def over_head(parts):
    return lax.all_to_all(parts, "head", split_axis=0, concat_axis=0, tiled=True)


def qkv_columns(rows, extra):
    own, width = rows.shape
    part = width // 3 // 4
    sent = rows.reshape(own, 3, 4, part).transpose(2, 0, 1, 3).reshape(4, own, 3 * part)
    if extra is not None:
        sent = jnp.concatenate([sent, jnp.broadcast_to(extra[None], (4,) + extra.shape)], axis=2)
    return over_head(sent)


def along_batch(piece):
    return lax.all_gather(piece, "batch", axis=0, tiled=False)


def along_blk(along):
    other = swapped(along, "blk", 1)
    first = lax.axis_index("blk") == 0
    both = jnp.stack([jnp.where(first, along, other), jnp.where(first, other, along)], axis=1)
    return both.reshape(-1, along.shape[-1])


def other_core(array):
    return swapped(array, "head", 1)


def to_neighbours(along):
    return swapped(along, "blk", 1), swapped(along, "head", 2)


def to_diagonal(across, beside):
    half = across.shape[-1] // 2
    return swapped(across[..., :half], "head", 2), swapped(beside[..., half:], "blk", 1)


def columns_over_blk(grad):
    blk = lax.axis_index("blk")
    parts = grad.reshape(4, 2, -1, grad.shape[1])
    return pick(parts, blk, 1), swapped(pick(parts, 1 - blk, 1).astype(BF16), "blk", 1)


def over_batch(parts):
    return lax.psum_scatter(parts.astype(BF16), "batch", scatter_dimension=0, tiled=False)


def columns_to_rows(summed):
    moved = over_head(summed.reshape(4, -1, summed.shape[-1]))
    rows = moved.shape[1]
    return moved.reshape(4, rows, 3, -1).transpose(1, 2, 0, 3).reshape(rows, -1).astype(F32)


def diagonal_sent(cored):
    blk, row, _ = place()
    rows = pick(pick(cored, 1 - blk, 1), 1 - row, 1)
    half = rows.shape[-1] // 2
    return swapped(rows[..., :half], "blk", 1), swapped(rows[..., half:], "head", 2)


def neighbours_sent(cored, one, two):
    blk, row, _ = place()
    half = one.shape[-1]
    across = pick(pick(cored, 1 - blk, 1), row, 1)
    beside = pick(pick(cored, blk, 1), 1 - row, 1)
    across = jnp.concatenate(
        [across[..., :half], across[..., half:].astype(F32) + two.astype(F32)], axis=-1
    ).astype(BF16)
    beside = jnp.concatenate(
        [beside[..., :half].astype(F32) + one.astype(F32), beside[..., half:]], axis=-1
    ).astype(BF16)
    return swapped(across, "blk", 1), swapped(beside, "head", 2)


def own_sum(cored, across, beside):
    blk, row, _ = place()
    own = pick(pick(cored, blk, 1), row, 1)
    return own.astype(F32) + across.astype(F32) + beside.astype(F32)


def sum_all(array):
    for axis, mask in (("head", 1), ("head", 2), ("blk", 1), ("batch", 1), ("batch", 2)):
        array = array + swapped(array, axis, mask)
    return array


def gain_back(weight, weight_grad, gain):
    return jnp.sum(weight.astype(F32) * weight_grad, axis=-1) / gain.astype(F32)


def lower_of(upper, stream, factor, gain):
    return norm_back(upper, stream, factor, gain)[0]


def spread_device(
    tokens,
    segments,
    qkv_weight,
    out_weight,
    up_weight,
    down_weight,
    attn_gain,
    mlp_gain,
    scale_param,
    cotangent,
):
    layers, head_dim = scale_param.shape
    _, token_rows, width = tokens.shape
    scale_vecs = SCALE_BASE / math.sqrt(head_dim) * jax.nn.softplus(scale_param)
    segments = pick(segments, lax.axis_index("blk"))
    own_gains = jnp.concatenate([attn_gain, mlp_gain], axis=0)

    first = swap_halves(tokens).reshape(-1, width)
    columns = [qkv_columns(qkv_weight[0], own_gains.T)]
    columns[0], first = tied(columns[0], first)
    first_all = gather_rows(first)
    stream = first.astype(F32)
    first_columns = columns[0].reshape(-1, columns[0].shape[-1])
    part3 = 3 * width // 4
    dense_own = [
        jnp.concatenate([out_weight[i], up_weight[i], down_weight[i]], axis=1) for i in (0, 1)
    ]
    along = along_batch(first_columns)
    dense_along = [along_batch(dense_own[0]), None]
    with_gains = along_blk(along)
    qkvs = [with_gains[:, :part3], None]
    gains = with_gains[:, part3:].T.astype(F32)
    near = [to_neighbours(dense_along[0]), None]
    next_along = along_batch(qkv_columns(qkv_weight[1], None).reshape(-1, part3))
    dense_along[1] = along_batch(dense_own[1])

    def dense_of(layer):
        pieces = (dense_along[layer],) + near[layer] + to_diagonal(*near[layer])
        return assemble(pieces + tuple(other_core(piece) for piece in pieces))

    kept, denses = [], []
    for layer in range(layers):
        qkv = qkvs[layer]
        normed, factor_one = normalize(stream, gains[layer])
        if layer == 0:
            normed_all = normalize(first_all.astype(F32), gains[0])[0].astype(BF16)
        else:
            normed_all = gather_rows(normed.astype(BF16))
        projected = lax.dot_general(
            qkv, normed_all, (((0,), (1,)), ((), ())), preferred_element_type=F32
        )
        attended, log_total = attend_rows(
            projected, scale_vecs[layer], segments, 4, token_rows
        )
        if layer == 0:
            attended, near[0] = tied(attended, near[0])
        else:
            attended, near[1] = tied(attended, near[1])
        denses.append(dense_of(layer))
        dense = denses[layer]
        out_w, up_w, down_w = dense[:, :width], dense[:, width:-width], dense[:, -width:]
        attended_t = over_head(attended).reshape(width, -1)
        middle = stream + dot_rows(attended_t, out_w)
        if layer == 0:
            middle, next_along, dense_along[1] = tied(middle, next_along, dense_along[1])
            qkvs[1] = along_blk(next_along)
            near[1] = to_neighbours(dense_along[1])
        normed_two, factor_two = normalize(middle, gains[layers + layer])
        normed_two = normed_two.astype(BF16)
        hidden = dot(normed_two, up_w)
        active = (hidden * jax.nn.sigmoid(hidden)).astype(BF16)
        kept.append(
            (
                stream, factor_one, normed_all, projected, log_total, attended_t, middle,
                factor_two, normed_two, hidden, active,
            )
        )
        stream = middle + dot(active, down_w)
    layer_out = swap_halves(stream.astype(BF16).reshape(tokens.shape))
    upper = swap_halves(cotangent).reshape(-1, width).astype(F32)

    qkv_grads, dense_grad, scale_grads = [None] * layers, [None] * layers, [None] * layers
    for layer in reversed(range(layers)):
        (
            stream, factor_one, normed_all, projected, log_total, attended_t, middle,
            factor_two, normed_two, hidden, active,
        ) = kept[layer]
        qkv, dense = qkvs[layer], denses[layer]
        out_w, up_w, down_w = dense[:, :width], dense[:, width:-width], dense[:, -width:]
        down_bar = upper.astype(BF16)
        gate = jax.nn.sigmoid(hidden)
        up_bar = (
            dot_cols(down_bar, down_w) * gate * (1.0 + hidden * (1.0 - gate))
        ).astype(BF16)
        middle_grad = upper + lower_of(
            dot_cols(up_bar, up_w), middle, factor_two, gains[layers + layer]
        )
        out_bar = middle_grad.astype(BF16)
        attended_grad = over_head(dot_cols(out_w, out_bar).astype(BF16).reshape(4, -1, out_bar.shape[0]))
        grads, others = dense_grads(attended_t, normed_two, active, out_bar, up_bar, down_bar)
        if layer == 0:
            attended_grad, others, sent, later = tied(attended_grad, others, sent, later)
            dense_grad[1] = over_batch(own_sum(cored, *sent))
            qkv_sum = over_batch(later[0] + later[1].astype(F32))
        else:
            attended_grad, others = tied(attended_grad, others)
        others = other_core(others)
        bars, scale_grads[layer] = attend_back_rows(
            projected, attended_grad, log_total, scale_vecs[layer], segments, token_rows
        )
        bars, others = tied(bars, others)
        cored = (grads.astype(F32) + others.astype(F32)).astype(BF16)
        diagonal = diagonal_sent(cored)
        normed_grad = scatter_rows(
            lax.dot_general(bars, qkv, (((0,), (1,)), ((), ())), preferred_element_type=F32)
        )
        later = columns_over_blk(
            lax.dot_general(normed_all, bars, (((0,), (1,)), ((), ())), preferred_element_type=F32)
        )
        if layer == 0:
            normed_grad, diagonal, later = tied(normed_grad, diagonal, later)
        else:
            normed_grad, diagonal = tied(normed_grad, diagonal)
        sent = neighbours_sent(cored, *diagonal)
        if layer == 0:
            dense_grad[0] = over_batch(own_sum(cored, *sent))
            qkv_grads[1] = columns_to_rows(qkv_sum)
            qkv_grads[0] = columns_to_rows(over_batch(later[0] + later[1].astype(F32)))
        upper = middle_grad + lower_of(normed_grad, stream, factor_one, gains[layer])
    input_grad = swap_halves(upper.astype(BF16).reshape(tokens.shape)).astype(F32)
    scale_total = sum_all(jnp.stack(scale_grads))
    scale_grad = scale_total * (SCALE_BASE / math.sqrt(head_dim)) * jax.nn.sigmoid(scale_param)
    dense_all = jnp.stack([part.astype(F32) for part in dense_grad])
    qkv_all = jnp.stack(qkv_grads)
    up_all = dense_all[:, :, width:-width]
    return (
        layer_out,
        input_grad,
        qkv_all,
        dense_all[:, :, :width],
        up_all,
        dense_all[:, :, -width:],
        gain_back(qkv_weight, qkv_all, attn_gain),
        gain_back(up_weight, up_all, mlp_gain),
        scale_grad,
    )


def per_device(*args):
    tokens, segments = args[0], args[1]
    sizes = tuple(lax.axis_size(axis) for axis in ALL)
    heads = tokens.shape[2] // args[8].shape[1]
    spread = (
        sizes == (4, 2, 4)
        and tokens.shape[0] == 2
        and args[2].shape[0] == 2
        and tokens.shape[1] % 128 == 0
        and Q_ROWS % tokens.shape[1] == 0
        and segments.shape[1] <= WINDOW
        and segments.shape[1] % Q_ROWS == 0
        and heads % 4 == 0
        and tokens.shape[2] % 256 == 0
    )
    return spread_device(*args) if spread else general_device(*args)


def solution(mesh):
    rows = P(None, ALL, None)
    by_token = P("batch", ("blk", "head"), None)
    return jax.shard_map(
        per_device,
        mesh=mesh,
        in_specs=(
            by_token, P("batch", None), rows, rows, rows, rows, P(None, ALL), P(None, ALL), P(),
            by_token,
        ),
        out_specs=(
            by_token, by_token, rows, rows, rows, rows, P(None, ALL), P(None, ALL), P(),
        ),
        check_vma=False,
    )
```

```python
import functools
import math

import jax
import jax.numpy as jnp
from jax import lax
from jax.experimental import pallas as pl
from jax.experimental.pallas import tpu as pltpu
from jax.sharding import PartitionSpec as P

WINDOW = 1024
EPSILON = 1e-06
SCALE_BASE = 1.4426950408889634
MASKED_SCORE = -1e30

ALL = ("batch", "blk", "head")
REST = ("batch", "blk")
F32 = jnp.float32
BF16 = jnp.bfloat16


def shifted(block, axis, distance):
    devices = range(lax.axis_size(axis))
    route = [(i - distance, i) for i in devices if i - distance in devices]
    return lax.ppermute(block, axis, route)


NT = (((1,), (1,)), ((), ()))
TN = (((0,), (0,)), ((), ()))


def dot(left, right):
    return jnp.dot(left, right, preferred_element_type=F32)


def dot_rows(left, right):
    return lax.dot_general(left, right, (((0,), (0,)), ((), ())), preferred_element_type=F32)


def dot_cols(left, right):
    return lax.dot_general(left, right, (((1,), (1,)), ((), ())), preferred_element_type=F32)


def normalize(stream, gain):
    factor = lax.rsqrt(jnp.mean(stream * stream, axis=-1, keepdims=True) + EPSILON)
    return stream * factor * gain, factor


def norm_back(upper, stream, factor, gain):
    inner = upper * gain
    gain_grad = jnp.sum(upper * stream * factor, axis=0)
    lower = factor * inner - stream * factor * factor * factor * jnp.mean(
        inner * stream, axis=-1, keepdims=True
    )
    return lower, gain_grad


class Plan:
    def __init__(self, tokens):
        self.seqs, self.rows, self.width = tokens.shape
        self.heads = lax.axis_size("head")
        self.blks = lax.axis_size("blk")
        self.block = self.rows * self.heads
        self.whole = self.seqs % self.blks == 0
        if self.whole:
            self.groups, self.own_seqs = self.blks, self.seqs // self.blks
            self.reach = 0
        else:
            self.groups, self.own_seqs = 1, self.seqs
            self.reach = min((WINDOW - 1) // self.block + 1, self.blks - 1)
        self.length = self.groups * self.block
        self.tokens = self.seqs * self.rows


def to_plan(plan, array):
    if plan.whole and plan.blks > 1:
        array = lax.all_to_all(array, "blk", split_axis=0, concat_axis=0, tiled=True)
    return array.reshape(plan.tokens, plan.width)


def from_plan(plan, flat):
    array = flat.reshape(plan.seqs, plan.rows, plan.width)
    if plan.whole and plan.blks > 1:
        array = lax.all_to_all(array, "blk", split_axis=0, concat_axis=0, tiled=True)
    return array


def in_sequence(plan, by_head, width):
    parts = by_head.reshape(plan.heads, plan.groups, plan.own_seqs, plan.rows, width)
    return parts.transpose(2, 1, 0, 3, 4).reshape(-1, width)


def by_owner(plan, rows, width):
    parts = rows.reshape(plan.own_seqs, plan.groups, plan.heads, plan.rows, width)
    return parts.transpose(2, 1, 0, 3, 4).reshape(plan.heads, plan.tokens, width)


def gather_tokens(plan, rows):
    moved = lax.all_gather(rows, "head", axis=0, tiled=False)
    return in_sequence(plan, moved, rows.shape[-1])


def scatter_tokens(plan, rows):
    width = rows.shape[-1]
    return lax.psum_scatter(
        by_owner(plan, rows.astype(BF16), width), "head", scatter_dimension=0, tiled=False
    ).astype(F32)


def heads_to_tokens(plan, rows):
    part = rows.shape[-1]
    moved = lax.all_to_all(
        by_owner(plan, rows, part), "head", split_axis=0, concat_axis=0, tiled=True
    )
    return moved.transpose(1, 0, 2).reshape(plan.tokens, plan.heads * part)


def tokens_to_heads(plan, rows):
    part = rows.shape[-1] // plan.heads
    sent = rows.reshape(plan.tokens, plan.heads, part).transpose(1, 0, 2)
    moved = lax.all_to_all(sent, "head", split_axis=0, concat_axis=0, tiled=True)
    return in_sequence(plan, moved, part)


def gather_qkv(rows):
    own, width = rows.shape
    heads = lax.axis_size("head")
    part = width // 3 // heads
    sent = rows.reshape(own, 3, heads, part).transpose(2, 0, 1, 3).reshape(heads, own, 3 * part)
    moved = lax.all_to_all(sent, "head", split_axis=0, concat_axis=0, tiled=True)
    full = lax.all_gather(moved, REST, axis=0, tiled=True)
    return full.reshape(-1, 3 * part)


def scatter_qkv(grad):
    heads = lax.axis_size("head")
    part = grad.shape[1] // 3
    summed = lax.psum_scatter(grad.astype(BF16), REST, scatter_dimension=0, tiled=True)
    own = summed.shape[0] // heads
    moved = lax.all_to_all(
        summed.reshape(heads, own, 3 * part), "head", split_axis=0, concat_axis=0, tiled=True
    )
    return (
        moved.reshape(heads, own, 3, part)
        .transpose(1, 2, 0, 3)
        .reshape(own, 3 * heads * part)
        .astype(F32)
    )


def window_mask(plan, segments, block_index):
    key_count = plan.length + plan.reach * plan.block
    if plan.whole:
        query_segs, key_segs = segments, segments
    else:
        leading = jnp.full((plan.own_seqs, plan.reach * plan.block), -1, jnp.int32)
        padded = jnp.concatenate([leading, segments], axis=1)
        start = block_index * plan.block
        query_segs = lax.dynamic_slice_in_dim(segments, start, plan.block, 1)
        key_segs = lax.dynamic_slice_in_dim(padded, start, key_count, 1)
    query_place = jnp.arange(plan.length, dtype=jnp.int32)[:, None] + plan.reach * plan.block
    key_place = jnp.arange(key_count, dtype=jnp.int32)[None, :]
    near = (key_place <= query_place) & (query_place - key_place < WINDOW)
    return (key_segs[:, None, :] == query_segs[:, :, None]) & near[None]


def with_earlier(plan, own):
    arrived = [own]
    for _ in range(plan.reach):
        arrived.append(shifted(arrived[-1], "blk", 1))
    return jnp.concatenate(arrived[::-1], axis=1) if plan.reach else own


def to_earlier(plan, grads):
    if not plan.reach:
        return grads
    block = plan.block
    total = grads[:, :block]
    for step in range(1, plan.reach + 1):
        total = (
            shifted(total.astype(BF16), "blk", -1).astype(F32)
            + grads[:, step * block : (step + 1) * block]
        )
    return total


def scores_of(queries, keys, allowed):
    scores = jnp.einsum("sqhd,skhd->shqk", queries, keys, preferred_element_type=F32)
    return jnp.where(allowed[:, None], scores, MASKED_SCORE)


def attend(queries, keys, values, allowed):
    scores = scores_of(queries, keys, allowed)
    top_score = jnp.max(scores, axis=-1, keepdims=True)
    exp_terms = jnp.exp(scores - top_score)
    totals = jnp.sum(exp_terms, axis=-1, keepdims=True)
    probs_low = (exp_terms / totals).astype(BF16)
    attended = jnp.einsum("shqk,skhd->sqhd", probs_low, values, preferred_element_type=F32)
    return attended, top_score + jnp.log(totals)


def attend_back(queries, keys, values, allowed, log_total, attended_grad):
    probs = jnp.exp(scores_of(queries, keys, allowed) - log_total)
    probs_low = probs.astype(BF16)
    values_grad = jnp.einsum(
        "shqk,sqhd->skhd", probs_low, attended_grad, preferred_element_type=F32
    )
    probs_grad = jnp.einsum("sqhd,skhd->shqk", attended_grad, values, preferred_element_type=F32)
    row_dot = jnp.sum(probs_grad * probs, axis=-1, keepdims=True)
    scores_low = (probs * (probs_grad - row_dot)).astype(BF16)
    queries_grad = jnp.einsum("shqk,skhd->sqhd", scores_low, keys, preferred_element_type=F32)
    keys_grad = jnp.einsum("shqk,sqhd->skhd", scores_low, queries, preferred_element_type=F32)
    return queries_grad, keys_grad, values_grad


def forward(plan, stream, qkv, dense, gains, scale_vec, allowed):
    width = plan.width
    head_dim = scale_vec.shape[0]
    part = qkv.shape[1] // 3
    local_heads = part // head_dim
    split = (plan.own_seqs, plan.length, local_heads, head_dim)
    out_w, up_w, down_w = dense[:, :width], dense[:, width:-width], dense[:, -width:]
    normed, factor_one = normalize(stream, gains[0])
    normed_all = gather_tokens(plan, normed.astype(BF16))
    projected = dot(normed_all, qkv)
    query_pre = projected[:, :part].reshape(split)
    queries = (query_pre * scale_vec).astype(BF16)
    keys = with_earlier(plan, projected[:, part : 2 * part].astype(BF16).reshape(split))
    values = with_earlier(plan, projected[:, 2 * part :].astype(BF16).reshape(split))
    attended_part, log_total = attend(queries, keys, values, allowed)
    attended = heads_to_tokens(plan, attended_part.astype(BF16).reshape(-1, part))
    middle = stream + dot(attended, out_w)
    normed_two, factor_two = normalize(middle, gains[1])
    normed_two = normed_two.astype(BF16)
    hidden = dot(normed_two, up_w)
    active = (hidden * jax.nn.sigmoid(hidden)).astype(BF16)
    result = middle + dot(active, down_w)
    kept = (
        stream, factor_one, normed_all, query_pre, queries, keys, values, log_total,
        attended, middle, factor_two, normed_two, hidden, active,
    )
    return result, kept


def backward(plan, upper, kept, qkv, dense, gains, scale_vec, allowed):
    (
        stream, factor_one, normed_all, query_pre, queries, keys, values, log_total,
        attended, middle, factor_two, normed_two, hidden, active,
    ) = kept
    width = plan.width
    head_dim = scale_vec.shape[0]
    part = qkv.shape[1] // 3
    out_w, up_w, down_w = dense[:, :width], dense[:, width:-width], dense[:, -width:]
    upper_low = upper.astype(BF16)
    down_grad = dot_rows(active, upper_low)
    active_grad = dot_cols(upper_low, down_w)
    gate = jax.nn.sigmoid(hidden)
    hidden_low = (active_grad * gate * (1.0 + hidden * (1.0 - gate))).astype(BF16)
    up_grad = dot_rows(normed_two, hidden_low)
    extra_two, mlp_gain_grad = norm_back(dot_cols(hidden_low, up_w), middle, factor_two, gains[1])
    middle_grad = upper + extra_two
    middle_low = middle_grad.astype(BF16)
    out_grad = dot_rows(attended, middle_low)
    dense_grad = jnp.concatenate([out_grad, up_grad, down_grad], axis=1).astype(BF16)
    dense_own = lax.psum_scatter(dense_grad, ALL, scatter_dimension=0, tiled=True)
    attended_grad = tokens_to_heads(plan, dot_cols(middle_low, out_w).astype(BF16))
    queries_grad, keys_grad, values_grad = attend_back(
        queries, keys, values, allowed, log_total, attended_grad.reshape(queries.shape)
    )
    query_bar = queries_grad.astype(BF16).astype(F32)
    scale_vec_grad = jnp.sum((query_bar * query_pre).reshape(-1, head_dim), axis=0)
    query_low = (query_bar * scale_vec).astype(BF16).reshape(-1, part)
    keys_low = to_earlier(plan, keys_grad).astype(BF16).reshape(-1, part)
    values_low = to_earlier(plan, values_grad).astype(BF16).reshape(-1, part)
    projected_low = jnp.concatenate([query_low, keys_low, values_low], axis=1)
    normed_grad = scatter_tokens(plan, dot_cols(projected_low, qkv))
    qkv_own = scatter_qkv(dot_rows(normed_all, projected_low))
    extra_one, attn_gain_grad = norm_back(normed_grad, stream, factor_one, gains[0])
    lower = middle_grad + extra_one
    return lower, qkv_own, dense_own, (attn_gain_grad, mlp_gain_grad), scale_vec_grad


def general_device(
    tokens,
    segments,
    qkv_weight,
    out_weight,
    up_weight,
    down_weight,
    attn_gain,
    mlp_gain,
    scale_param,
    cotangent,
):
    plan = Plan(tokens)
    layers, head_dim = scale_param.shape
    block_index = lax.axis_index("blk")
    scale_vecs = SCALE_BASE / math.sqrt(head_dim) * jax.nn.softplus(scale_param)
    own_gains = jnp.concatenate([attn_gain, mlp_gain], axis=0)
    gains = (
        lax.all_gather(own_gains.reshape(1, -1), ALL, axis=0, tiled=True)
        .reshape(-1, 2 * layers, attn_gain.shape[1])
        .transpose(1, 0, 2)
        .reshape(2 * layers, plan.width)
        .astype(F32)
    )
    if plan.whole:
        segments = lax.dynamic_slice_in_dim(
            segments, block_index * plan.own_seqs, plan.own_seqs, 0
        )
    allowed = window_mask(plan, segments, block_index)
    stream = to_plan(plan, tokens).astype(F32)
    qkvs, denses, kept = [], [], []
    for layer in range(layers):
        qkvs.append(gather_qkv(qkv_weight[layer]))
        own = jnp.concatenate([out_weight[layer], up_weight[layer], down_weight[layer]], axis=1)
        denses.append(lax.all_gather(own, ALL, axis=0, tiled=True))
        layer_gains = (gains[layer], gains[layers + layer])
        stream, saved = forward(
            plan, stream, qkvs[layer], denses[layer], layer_gains, scale_vecs[layer], allowed
        )
        kept.append(saved)
    layer_out = from_plan(plan, stream.astype(BF16))
    upper = to_plan(plan, cotangent).astype(F32)
    qkv_grads, dense_grads = [None] * layers, [None] * layers
    gain_grads, scale_grads = [None] * layers, [None] * layers
    for layer in reversed(range(layers)):
        layer_gains = (gains[layer], gains[layers + layer])
        upper, qkv_grads[layer], dense_grads[layer], gain_grads[layer], scale_grads[layer] = (
            backward(
                plan, upper, kept[layer], qkvs[layer], denses[layer], layer_gains,
                scale_vecs[layer], allowed,
            )
        )
    input_grad = from_plan(plan, upper.astype(BF16)).astype(F32)
    small = jnp.concatenate(
        [g[0] for g in gain_grads] + [g[1] for g in gain_grads] + scale_grads, axis=0
    )
    total = lax.psum(small, ALL)
    gain_total = total[: 2 * layers * plan.width].reshape(2 * layers, plan.width)
    owner = lax.axis_index(ALL)
    gain_rows = attn_gain.shape[1]
    own_total = lax.dynamic_slice_in_dim(gain_total, owner * gain_rows, gain_rows, 1)
    scale_total = total[2 * layers * plan.width :].reshape(layers, head_dim)
    scale_grad = scale_total * (SCALE_BASE / math.sqrt(head_dim)) * jax.nn.sigmoid(scale_param)
    dense_all = jnp.stack(dense_grads).astype(F32)
    width = plan.width
    return (
        layer_out,
        input_grad,
        jnp.stack(qkv_grads),
        dense_all[:, :, :width],
        dense_all[:, :, width:-width],
        dense_all[:, :, -width:],
        own_total[:layers],
        own_total[layers:],
        scale_grad,
    )


Q_ROWS = 256
KERNEL = pltpu.CompilerParams(vmem_limit_bytes=50 * 1024 * 1024)
LIGHT = pl.CostEstimate(flops=1 << 20, bytes_accessed=1 << 20, transcendentals=0)


def allowed_keys(col, row, first):
    count = first + row.shape[1]
    key_place = lax.broadcasted_iota(jnp.int32, (count, row.shape[1]), 0)
    query_place = lax.broadcasted_iota(jnp.int32, (count, row.shape[1]), 1) + first
    return (col[:count] == row) & (key_place <= query_place)


def token_places(length, heads, token_rows):
    for first in range(0, length, Q_ROWS):
        parts = []
        for start in range(0, Q_ROWS, token_rows):
            place = (first + start) // token_rows
            parts.append((start, place % heads, place // heads * token_rows))
        yield first, parts


def attend_kernel(token_rows, proj_ref, scale_ref, col_ref, row_ref, out_ref, lse_ref):
    length = proj_ref.shape[-1]
    queries = (proj_ref[0, 0] * scale_ref[...]).astype(BF16)
    keys = proj_ref[1, 0].T.astype(BF16)
    values = proj_ref[2, 0].astype(BF16)
    for first, parts in token_places(length, out_ref.shape[0], token_rows):
        end = first + Q_ROWS
        scores = jnp.dot(keys[:end], queries[:, first:end], preferred_element_type=F32)
        allowed = allowed_keys(col_ref[...], row_ref[:, first:end], first)
        scores = jnp.where(allowed, scores, MASKED_SCORE)
        top = jnp.max(scores, axis=0, keepdims=True)
        terms = jnp.exp(scores - top)
        total = jnp.sum(terms, axis=0, keepdims=True)
        probs = (terms * (1.0 / total)).astype(BF16)
        attended = jnp.dot(values[:, :end], probs, preferred_element_type=F32).astype(BF16)
        lse_ref[0, :, first:end] = top + jnp.log(total)
        for start, owner, offset in parts:
            out_ref[owner, 0, :, offset : offset + token_rows] = attended[
                :, start : start + token_rows
            ]


def attend_rows(projected, scale_vec, segments, owners, token_rows):
    head_dim = scale_vec.shape[0]
    length = projected.shape[1]
    local_heads = projected.shape[0] // 3 // head_dim
    tokens = length // owners
    attended, log_total = pl.pallas_call(
        functools.partial(attend_kernel, token_rows),
        grid=(local_heads,),
        in_specs=[
            pl.BlockSpec((3, 1, head_dim, length), lambda h: (0, h, 0, 0)),
            pl.BlockSpec((head_dim, 1), lambda h: (0, 0)),
            pl.BlockSpec((length, 1), lambda h: (0, 0)),
            pl.BlockSpec((1, length), lambda h: (0, 0)),
        ],
        out_specs=[
            pl.BlockSpec((owners, 1, head_dim, tokens), lambda h: (0, h, 0, 0)),
            pl.BlockSpec((1, 1, length), lambda h: (h, 0, 0)),
        ],
        out_shape=[
            jax.ShapeDtypeStruct((owners, local_heads, head_dim, tokens), BF16),
            jax.ShapeDtypeStruct((local_heads, 1, length), F32),
        ],
        compiler_params=KERNEL,
        cost_estimate=LIGHT,
    )(
        projected.reshape(3, local_heads, head_dim, length),
        scale_vec.reshape(head_dim, 1),
        segments.reshape(length, 1),
        segments.reshape(1, length),
    )
    return attended.reshape(owners, local_heads * head_dim, tokens), log_total


def attend_back_kernel(
    token_rows,
    proj_ref,
    grad_ref,
    lse_ref,
    scale_ref,
    col_ref,
    row_ref,
    out_ref,
    scale_grad_ref,
    keys_acc,
    values_acc,
):
    length = proj_ref.shape[-1]
    scale = scale_ref[...]
    query_pre = proj_ref[0, 0]
    queries = (query_pre * scale).astype(BF16)
    keys_t = proj_ref[1, 0].astype(BF16)
    keys = proj_ref[1, 0].T.astype(BF16)
    values = proj_ref[2, 0].T.astype(BF16)
    keys_acc[...] = jnp.zeros_like(keys_acc)
    values_acc[...] = jnp.zeros_like(values_acc)
    scale_grad = jnp.zeros((scale.shape[0], 1), F32)
    for first, parts in token_places(length, grad_ref.shape[0], token_rows):
        end = first + Q_ROWS
        block = queries[:, first:end]
        grad = jnp.concatenate(
            [grad_ref[owner, 0, :, at : at + token_rows] for _, owner, at in parts], axis=1
        )
        scores = jnp.dot(keys[:end], block, preferred_element_type=F32)
        allowed = allowed_keys(col_ref[...], row_ref[:, first:end], first)
        scores = jnp.where(allowed, scores, MASKED_SCORE)
        probs = jnp.exp(scores - lse_ref[0, :, first:end])
        probs_grad = jnp.dot(values[:end], grad, preferred_element_type=F32)
        row_dot = jnp.sum(probs_grad * probs, axis=0, keepdims=True)
        scores_low = (probs * (probs_grad - row_dot)).astype(BF16)
        values_acc[:, :end] += lax.dot_general(
            grad, probs.astype(BF16), NT, preferred_element_type=F32
        )
        keys_acc[:, :end] += lax.dot_general(
            block, scores_low, NT, preferred_element_type=F32
        )
        query_bar = jnp.dot(keys_t[:, :end], scores_low, preferred_element_type=F32)
        query_bar = query_bar.astype(BF16).astype(F32)
        scale_grad += jnp.sum(query_bar * query_pre[:, first:end], axis=1, keepdims=True)
        out_ref[0, 0, :, first:end] = (query_bar * scale).astype(BF16)
    out_ref[1, 0] = keys_acc[...].astype(BF16)
    out_ref[2, 0] = values_acc[...].astype(BF16)
    spread = jnp.broadcast_to(scale_grad, scale_grad_ref.shape)

    @pl.when(pl.program_id(0) == 0)
    def _():
        scale_grad_ref[...] = spread

    @pl.when(pl.program_id(0) > 0)
    def _():
        scale_grad_ref[...] += spread


def attend_back_rows(projected, attended_grad, log_total, scale_vec, segments, token_rows):
    head_dim = scale_vec.shape[0]
    length = projected.shape[1]
    local_heads = projected.shape[0] // 3 // head_dim
    owners, _, tokens = attended_grad.shape
    lanes = 128
    grads, scale_grad = pl.pallas_call(
        functools.partial(attend_back_kernel, token_rows),
        grid=(local_heads,),
        in_specs=[
            pl.BlockSpec((3, 1, head_dim, length), lambda h: (0, h, 0, 0)),
            pl.BlockSpec((owners, 1, head_dim, tokens), lambda h: (0, h, 0, 0)),
            pl.BlockSpec((1, 1, length), lambda h: (h, 0, 0)),
            pl.BlockSpec((head_dim, 1), lambda h: (0, 0)),
            pl.BlockSpec((length, 1), lambda h: (0, 0)),
            pl.BlockSpec((1, length), lambda h: (0, 0)),
        ],
        out_specs=[
            pl.BlockSpec((3, 1, head_dim, length), lambda h: (0, h, 0, 0)),
            pl.BlockSpec((head_dim, lanes), lambda h: (0, 0)),
        ],
        out_shape=[
            jax.ShapeDtypeStruct((3, local_heads, head_dim, length), BF16),
            jax.ShapeDtypeStruct((head_dim, lanes), F32),
        ],
        scratch_shapes=[
            pltpu.VMEM((head_dim, length), F32),
            pltpu.VMEM((head_dim, length), F32),
        ],
        compiler_params=KERNEL,
        cost_estimate=LIGHT,
    )(
        projected.reshape(3, local_heads, head_dim, length),
        attended_grad.reshape(owners, local_heads, head_dim, tokens),
        log_total,
        scale_vec.reshape(head_dim, 1),
        segments.reshape(length, 1),
        segments.reshape(1, length),
    )
    return grads.reshape(3 * local_heads * head_dim, length), scale_grad[:, 0]


def dense_grad_kernel(
    core_ref, attended_ref, normed_ref, active_ref, out_bar, up_bar, down_bar,
    own_ref, other_ref, normed_t, active_t,
):
    tile = pl.program_id(0)
    rows, width = own_ref.shape[2] * own_ref.shape[3] * 2, out_bar.shape[1]

    @pl.when(tile == 0)
    def _():
        normed_t[...] = normed_ref[...].astype(F32).T.astype(BF16)
        active_t[...] = active_ref[...].astype(F32).T.astype(BF16)

    start = pl.multiple_of(tile * rows, rows)
    first_core = core_ref[0] == 0
    lefts = (attended_ref, normed_t, active_t)
    for i, (left, right) in enumerate(zip(lefts, (out_bar, up_bar, down_bar))):
        grad = jnp.dot(left[pl.ds(start, rows), :], right[...], preferred_element_type=F32)
        grad = grad.reshape(2, 2, rows // 4, width)
        one, two = grad[:, 0], grad[:, 1]
        own_ref[0, 0, :, :, i * width : (i + 1) * width] = jnp.where(
            first_core, one, two
        ).astype(BF16)
        other_ref[0, 0, :, :, i * width : (i + 1) * width] = jnp.where(
            first_core, two, one
        ).astype(BF16)


def dense_grads(attended_t, normed, active, out_bar, up_bar, down_bar):
    width, tokens = attended_t.shape
    own = width // 32
    whole = pl.BlockSpec((tokens, width), lambda i, core: (0, 0))
    rows = pl.BlockSpec((1, 1, 2, own, 3 * width), lambda i, core: (i // 2, i % 2, 0, 0, 0))
    shape = jax.ShapeDtypeStruct((4, 2, 2, own, 3 * width), BF16)
    return pl.pallas_call(
        dense_grad_kernel,
        grid_spec=pltpu.PrefetchScalarGridSpec(
            num_scalar_prefetch=1,
            grid=(8,),
            in_specs=[pl.BlockSpec((width, tokens), lambda i, core: (0, 0))] + [whole] * 5,
            out_specs=[rows, rows],
            scratch_shapes=[pltpu.VMEM((width, tokens), BF16)] * 2,
        ),
        out_shape=[shape, shape],
        compiler_params=KERNEL,
        cost_estimate=LIGHT,
    )(place()[2:], attended_t, normed, active, out_bar, up_bar, down_bar)


def place():
    head = lax.axis_index("head")
    return jnp.stack([lax.axis_index("blk"), head // 2, head % 2]).astype(jnp.int32)


def assemble_kernel(place_ref, *refs):
    pieces, whole_ref = refs[:10], refs[10]
    half = whole_ref.shape[-1] // 2
    blk, row, core = place_ref[0], place_ref[1], place_ref[2]
    for i in range(2):
        at_core = core if i == 0 else 1 - core
        own, across, beside, one, two = pieces[5 * i : 5 * i + 5]
        whole_ref[0, blk, row, at_core] = own[0]
        whole_ref[0, 1 - blk, row, at_core] = across[0]
        whole_ref[0, blk, 1 - row, at_core] = beside[0]
        whole_ref[0, 1 - blk, 1 - row, at_core, :, :half] = one[0]
        whole_ref[0, 1 - blk, 1 - row, at_core, :, half:] = two[0]


def assemble(pieces):
    batch, own, columns = pieces[0].shape
    specs = [
        pl.BlockSpec((1, own, piece.shape[-1]), lambda i, at: (i, 0, 0)) for piece in pieces
    ]
    whole = pl.pallas_call(
        assemble_kernel,
        grid_spec=pltpu.PrefetchScalarGridSpec(
            num_scalar_prefetch=1,
            grid=(batch,),
            in_specs=specs,
            out_specs=pl.BlockSpec((1, 2, 2, 2, own, columns), lambda i, at: (i, 0, 0, 0, 0, 0)),
        ),
        out_shape=jax.ShapeDtypeStruct((batch, 2, 2, 2, own, columns), BF16),
        compiler_params=KERNEL,
        cost_estimate=LIGHT,
    )(place(), *pieces)
    return whole.reshape(-1, columns)


def tied(*arrays):
    return lax.optimization_barrier(arrays)


def swapped(array, axis, mask):
    size = lax.axis_size(axis)
    return lax.ppermute(array, axis, [(i, i ^ mask) for i in range(size)])


def pick(array, index, axis=0):
    return lax.dynamic_index_in_dim(array, index, axis, keepdims=False)


def swap_halves(array):
    me = lax.axis_index("blk")
    got = swapped(pick(array, 1 - me), "blk", 1)
    kept = pick(array, me)
    return jnp.stack([jnp.where(me == 0, kept, got), jnp.where(me == 0, got, kept)])


def gather_rows(rows):
    width = rows.shape[-1]
    far = swapped(rows, "head", 2)
    near = swapped(rows, "head", 1)
    both = swapped(far, "head", 1)
    pieces = jnp.stack([rows, near, far, both])
    me = lax.axis_index("head")
    ordered = jnp.stack([pick(pieces, me ^ i) for i in range(4)])
    return ordered.reshape(4, 2, -1, width).transpose(1, 0, 2, 3).reshape(-1, width)


def scatter_core(rows):
    core = lax.axis_index("head") % 2
    parts = rows.reshape(2, 2, 2, -1, rows.shape[-1])
    got = swapped(pick(parts, 1 - core, 2).astype(BF16), "head", 1).astype(F32)
    return pick(parts, core, 2) + got


def scatter_row(halves):
    row = lax.axis_index("head") // 2
    got = swapped(pick(halves, 1 - row, 1).astype(BF16), "head", 2).astype(F32)
    return (pick(halves, row, 1) + got).reshape(-1, halves.shape[-1])


def over_head(parts):
    return lax.all_to_all(parts, "head", split_axis=0, concat_axis=0, tiled=True)


def qkv_columns(rows, extra):
    own, width = rows.shape
    part = width // 3 // 4
    sent = rows.reshape(own, 3, 4, part).transpose(2, 0, 1, 3).reshape(4, own, 3 * part)
    if extra is not None:
        sent = jnp.concatenate([sent, jnp.broadcast_to(extra[None], (4,) + extra.shape)], axis=2)
    return over_head(sent)


def along_batch(piece):
    return lax.all_gather(piece, "batch", axis=0, tiled=False)


def in_rows(along, across):
    first = lax.axis_index("blk") == 0
    both = jnp.stack([jnp.where(first, along, across), jnp.where(first, across, along)], axis=1)
    return both.reshape(-1, along.shape[-1])


def other_core(array):
    return swapped(array, "head", 1)


def to_neighbours(along):
    return swapped(along, "blk", 1), swapped(along, "head", 2)


def to_beside(across):
    return swapped(across[..., : across.shape[-1] // 2], "head", 2)


def to_across(beside):
    return swapped(beside[..., beside.shape[-1] // 2 :], "blk", 1)


def over_batch(parts):
    return lax.psum_scatter(parts.astype(BF16), "batch", scatter_dimension=0, tiled=False)


def columns_to_rows(halves):
    blk = lax.axis_index("blk")
    got = swapped(pick(halves, 1 - blk), "blk", 1).astype(F32)
    summed = (pick(halves, blk).astype(F32) + got).astype(BF16)
    moved = over_head(summed.reshape(4, -1, summed.shape[-1]))
    rows = moved.shape[1]
    return moved.reshape(4, rows, 3, -1).transpose(1, 2, 0, 3).reshape(rows, -1).astype(F32)


def diagonal_sent(cored):
    blk, row, _ = place()
    rows = pick(pick(cored, 1 - blk, 1), 1 - row, 1)
    half = rows.shape[-1] // 2
    return swapped(rows[..., :half], "blk", 1), swapped(rows[..., half:], "head", 2)


def neighbours_sent(cored, one, two):
    blk, row, _ = place()
    half = one.shape[-1]
    across = pick(pick(cored, 1 - blk, 1), row, 1)
    beside = pick(pick(cored, blk, 1), 1 - row, 1)
    across = jnp.concatenate(
        [across[..., :half], across[..., half:].astype(F32) + two.astype(F32)], axis=-1
    ).astype(BF16)
    beside = jnp.concatenate(
        [beside[..., :half].astype(F32) + one.astype(F32), beside[..., half:]], axis=-1
    ).astype(BF16)
    return swapped(across, "blk", 1), swapped(beside, "head", 2)


def own_sum(cored, across, beside):
    blk, row, _ = place()
    own = pick(pick(cored, blk, 1), row, 1)
    return own.astype(F32) + across.astype(F32) + beside.astype(F32)


def sum_all(array):
    for axis, mask in (("head", 1), ("head", 2), ("blk", 1), ("batch", 1), ("batch", 2)):
        array = array + swapped(array, axis, mask)
    return array


def gain_back(weight, weight_grad, gain):
    return jnp.sum(weight.astype(F32) * weight_grad, axis=-1) / gain.astype(F32)


def lower_of(upper, stream, factor, gain):
    return norm_back(upper, stream, factor, gain)[0]


def spread_device(
    tokens,
    segments,
    qkv_weight,
    out_weight,
    up_weight,
    down_weight,
    attn_gain,
    mlp_gain,
    scale_param,
    cotangent,
):
    layers, head_dim = scale_param.shape
    _, token_rows, width = tokens.shape
    scale_vecs = SCALE_BASE / math.sqrt(head_dim) * jax.nn.softplus(scale_param)
    segments = pick(segments, lax.axis_index("blk"))
    own_gains = jnp.concatenate([attn_gain, mlp_gain], axis=0)

    first = swap_halves(tokens).reshape(-1, width)
    columns = [qkv_columns(qkv_weight[0], own_gains.T)]
    columns[0], first = tied(columns[0], first)
    first_all = gather_rows(first)
    stream = first.astype(F32)
    first_columns = columns[0].reshape(-1, columns[0].shape[-1])
    part3 = 3 * width // 4
    dense_own = [
        jnp.concatenate([out_weight[i], up_weight[i], down_weight[i]], axis=1) for i in (0, 1)
    ]
    dense_along = along_batch(dense_own[0])
    first_columns, dense_along = tied(first_columns, dense_along)
    across, beside = to_neighbours(dense_along)
    along = along_batch(first_columns)
    along, dense_next = tied(along, dense_own[1])
    dense_next = along_batch(dense_next)
    qkv_across = swapped(along, "blk", 1)
    one = to_beside(across)
    qkv_across, beside_after = tied(qkv_across, beside)
    with_gains = in_rows(along, qkv_across)
    two = to_across(beside_after)
    qkvs = [with_gains[:, :part3], None]
    gains = with_gains[:, part3:].T.astype(F32)
    pieces = [(dense_along, across, beside, one, two)]
    next_columns = qkv_columns(qkv_weight[1], None).reshape(-1, part3)
    next_columns, dense_next = tied(next_columns, dense_next)
    next_along = along_batch(next_columns)
    beside = swapped(dense_next, "head", 2)
    two, dense_after = tied(two, dense_next)
    across = swapped(dense_after, "blk", 1)
    across, next_along = tied(across, next_along)
    next_across = swapped(next_along, "blk", 1)
    one = to_beside(across)
    next_across, beside_after = tied(next_across, beside)
    two = to_across(beside_after)
    pieces.append((dense_next, across, beside, one, two))

    def dense_of(layer):
        return assemble(pieces[layer] + tuple(other_core(piece) for piece in pieces[layer]))

    kept, denses = [], []
    for layer in range(layers):
        normed, factor_one = normalize(stream, gains[layer])
        if layer == 0:
            normed_all = normalize(first_all.astype(F32), gains[0])[0].astype(BF16)
        else:
            normed, next_across = tied(normed.astype(BF16), next_across)
            normed_all = gather_rows(normed)
            qkvs[1] = in_rows(next_along, next_across)
        qkv = qkvs[layer]
        projected = lax.dot_general(
            qkv, normed_all, (((0,), (1,)), ((), ())), preferred_element_type=F32
        )
        attended, log_total = attend_rows(
            projected, scale_vecs[layer], segments, 4, token_rows
        )
        attended, late = tied(attended, pieces[layer][3:])
        pieces[layer] = pieces[layer][:3] + late
        denses.append(dense_of(layer))
        dense = denses[layer]
        out_w, up_w, down_w = dense[:, :width], dense[:, width:-width], dense[:, -width:]
        attended_t = over_head(attended).reshape(width, -1)
        middle = stream + dot_rows(attended_t, out_w)
        normed_two, factor_two = normalize(middle, gains[layers + layer])
        normed_two = normed_two.astype(BF16)
        hidden = dot(normed_two, up_w)
        active = (hidden * jax.nn.sigmoid(hidden)).astype(BF16)
        kept.append(
            (
                stream, factor_one, normed_all, projected, log_total, attended_t, middle,
                factor_two, normed_two, hidden, active,
            )
        )
        stream = middle + dot(active, down_w)
    layer_out = swap_halves(stream.astype(BF16).reshape(tokens.shape))
    upper = swap_halves(cotangent).reshape(-1, width).astype(F32)

    qkv_sums, dense_grad, scale_grads = [None] * layers, [None] * layers, [None] * layers
    for layer in reversed(range(layers)):
        (
            stream, factor_one, normed_all, projected, log_total, attended_t, middle,
            factor_two, normed_two, hidden, active,
        ) = kept[layer]
        qkv, dense = qkvs[layer], denses[layer]
        out_w, up_w, down_w = dense[:, :width], dense[:, width:-width], dense[:, -width:]
        down_bar = upper.astype(BF16)
        gate = jax.nn.sigmoid(hidden)
        up_bar = (
            dot_cols(down_bar, down_w) * gate * (1.0 + hidden * (1.0 - gate))
        ).astype(BF16)
        middle_grad = upper + lower_of(
            dot_cols(up_bar, up_w), middle, factor_two, gains[layers + layer]
        )
        out_bar = middle_grad.astype(BF16)
        attended_grad = over_head(dot_cols(out_w, out_bar).astype(BF16).reshape(4, -1, out_bar.shape[0]))
        grads, others = dense_grads(attended_t, normed_two, active, out_bar, up_bar, down_bar)
        if layer == 0:
            attended_grad, others, diagonal = tied(attended_grad, others, diagonal)
            sent = neighbours_sent(cored, *diagonal)
            last = cored
        else:
            attended_grad, others = tied(attended_grad, others)
        others = other_core(others)
        bars, scale_grads[layer] = attend_back_rows(
            projected, attended_grad, log_total, scale_vecs[layer], segments, token_rows
        )
        bars, others = tied(bars, others)
        cored = (grads.astype(F32) + others.astype(F32)).astype(BF16)
        halves = scatter_core(
            lax.dot_general(bars, qkv, (((0,), (1,)), ((), ())), preferred_element_type=F32)
        )
        qkv_grad = lax.dot_general(
            normed_all, bars, (((0,), (1,)), ((), ())), preferred_element_type=F32
        )
        qkv_sums[layer] = over_batch(qkv_grad.reshape(4, 2, -1, qkv_grad.shape[-1]))
        if layer == 0:
            diagonal = diagonal_sent(cored)
            halves, diagonal = tied(halves, diagonal)
            normed_grad = scatter_row(halves)
            normed_grad, sent = tied(normed_grad, sent)
            dense_grad[1] = over_batch(own_sum(last, *sent))
            sent = neighbours_sent(cored, *diagonal)
            dense_grad[0] = over_batch(own_sum(cored, *sent))
            qkv_grads = [columns_to_rows(part) for part in qkv_sums]
        else:
            normed_grad = scatter_row(halves)
            normed_grad, cored = tied(normed_grad, cored)
            diagonal = diagonal_sent(cored)
        upper = middle_grad + lower_of(normed_grad, stream, factor_one, gains[layer])
    input_grad = swap_halves(upper.astype(BF16).reshape(tokens.shape)).astype(F32)
    scale_total = sum_all(jnp.stack(scale_grads))
    scale_grad = scale_total * (SCALE_BASE / math.sqrt(head_dim)) * jax.nn.sigmoid(scale_param)
    dense_all = jnp.stack([part.astype(F32) for part in dense_grad])
    qkv_all = jnp.stack(qkv_grads)
    up_all = dense_all[:, :, width:-width]
    return (
        layer_out,
        input_grad,
        qkv_all,
        dense_all[:, :, :width],
        up_all,
        dense_all[:, :, -width:],
        gain_back(qkv_weight, qkv_all, attn_gain),
        gain_back(up_weight, up_all, mlp_gain),
        scale_grad,
    )


def per_device(*args):
    tokens, segments = args[0], args[1]
    sizes = tuple(lax.axis_size(axis) for axis in ALL)
    heads = tokens.shape[2] // args[8].shape[1]
    spread = (
        sizes == (4, 2, 4)
        and tokens.shape[0] == 2
        and args[2].shape[0] == 2
        and tokens.shape[1] % 128 == 0
        and Q_ROWS % tokens.shape[1] == 0
        and segments.shape[1] <= WINDOW
        and segments.shape[1] % Q_ROWS == 0
        and heads % 4 == 0
        and tokens.shape[2] % 256 == 0
    )
    return spread_device(*args) if spread else general_device(*args)


def solution(mesh):
    rows = P(None, ALL, None)
    by_token = P("batch", ("blk", "head"), None)
    return jax.shard_map(
        per_device,
        mesh=mesh,
        in_specs=(
            by_token, P("batch", None), rows, rows, rows, rows, P(None, ALL), P(None, ALL), P(),
            by_token,
        ),
        out_specs=(
            by_token, by_token, rows, rows, rows, rows, P(None, ALL), P(None, ALL), P(),
        ),
        check_vma=False,
    )
```

```python
import functools
import math

import jax
import jax.numpy as jnp
from jax import lax
from jax.experimental import pallas as pl
from jax.experimental.pallas import tpu as pltpu
from jax.sharding import PartitionSpec as P

WINDOW = 1024
EPSILON = 1e-06
SCALE_BASE = 1.4426950408889634
MASKED_SCORE = -1e30

ALL = ("batch", "blk", "head")
REST = ("batch", "blk")
F32 = jnp.float32
BF16 = jnp.bfloat16


def shifted(block, axis, distance):
    devices = range(lax.axis_size(axis))
    route = [(i - distance, i) for i in devices if i - distance in devices]
    return lax.ppermute(block, axis, route)


NT = (((1,), (1,)), ((), ()))
TN = (((0,), (0,)), ((), ()))


def dot(left, right):
    return jnp.dot(left, right, preferred_element_type=F32)


def dot_rows(left, right):
    return lax.dot_general(left, right, (((0,), (0,)), ((), ())), preferred_element_type=F32)


def dot_cols(left, right):
    return lax.dot_general(left, right, (((1,), (1,)), ((), ())), preferred_element_type=F32)


def normalize(stream, gain):
    factor = lax.rsqrt(jnp.mean(stream * stream, axis=-1, keepdims=True) + EPSILON)
    return stream * factor * gain, factor


def norm_back(upper, stream, factor, gain):
    inner = upper * gain
    gain_grad = jnp.sum(upper * stream * factor, axis=0)
    lower = factor * inner - stream * factor * factor * factor * jnp.mean(
        inner * stream, axis=-1, keepdims=True
    )
    return lower, gain_grad


class Plan:
    def __init__(self, tokens):
        self.seqs, self.rows, self.width = tokens.shape
        self.heads = lax.axis_size("head")
        self.blks = lax.axis_size("blk")
        self.block = self.rows * self.heads
        self.whole = self.seqs % self.blks == 0
        if self.whole:
            self.groups, self.own_seqs = self.blks, self.seqs // self.blks
            self.reach = 0
        else:
            self.groups, self.own_seqs = 1, self.seqs
            self.reach = min((WINDOW - 1) // self.block + 1, self.blks - 1)
        self.length = self.groups * self.block
        self.tokens = self.seqs * self.rows


def to_plan(plan, array):
    if plan.whole and plan.blks > 1:
        array = lax.all_to_all(array, "blk", split_axis=0, concat_axis=0, tiled=True)
    return array.reshape(plan.tokens, plan.width)


def from_plan(plan, flat):
    array = flat.reshape(plan.seqs, plan.rows, plan.width)
    if plan.whole and plan.blks > 1:
        array = lax.all_to_all(array, "blk", split_axis=0, concat_axis=0, tiled=True)
    return array


def in_sequence(plan, by_head, width):
    parts = by_head.reshape(plan.heads, plan.groups, plan.own_seqs, plan.rows, width)
    return parts.transpose(2, 1, 0, 3, 4).reshape(-1, width)


def by_owner(plan, rows, width):
    parts = rows.reshape(plan.own_seqs, plan.groups, plan.heads, plan.rows, width)
    return parts.transpose(2, 1, 0, 3, 4).reshape(plan.heads, plan.tokens, width)


def gather_tokens(plan, rows):
    moved = lax.all_gather(rows, "head", axis=0, tiled=False)
    return in_sequence(plan, moved, rows.shape[-1])


def scatter_tokens(plan, rows):
    width = rows.shape[-1]
    return lax.psum_scatter(
        by_owner(plan, rows.astype(BF16), width), "head", scatter_dimension=0, tiled=False
    ).astype(F32)


def heads_to_tokens(plan, rows):
    part = rows.shape[-1]
    moved = lax.all_to_all(
        by_owner(plan, rows, part), "head", split_axis=0, concat_axis=0, tiled=True
    )
    return moved.transpose(1, 0, 2).reshape(plan.tokens, plan.heads * part)


def tokens_to_heads(plan, rows):
    part = rows.shape[-1] // plan.heads
    sent = rows.reshape(plan.tokens, plan.heads, part).transpose(1, 0, 2)
    moved = lax.all_to_all(sent, "head", split_axis=0, concat_axis=0, tiled=True)
    return in_sequence(plan, moved, part)


def gather_qkv(rows):
    own, width = rows.shape
    heads = lax.axis_size("head")
    part = width // 3 // heads
    sent = rows.reshape(own, 3, heads, part).transpose(2, 0, 1, 3).reshape(heads, own, 3 * part)
    moved = lax.all_to_all(sent, "head", split_axis=0, concat_axis=0, tiled=True)
    full = lax.all_gather(moved, REST, axis=0, tiled=True)
    return full.reshape(-1, 3 * part)


def scatter_qkv(grad):
    heads = lax.axis_size("head")
    part = grad.shape[1] // 3
    summed = lax.psum_scatter(grad.astype(BF16), REST, scatter_dimension=0, tiled=True)
    own = summed.shape[0] // heads
    moved = lax.all_to_all(
        summed.reshape(heads, own, 3 * part), "head", split_axis=0, concat_axis=0, tiled=True
    )
    return (
        moved.reshape(heads, own, 3, part)
        .transpose(1, 2, 0, 3)
        .reshape(own, 3 * heads * part)
        .astype(F32)
    )


def window_mask(plan, segments, block_index):
    key_count = plan.length + plan.reach * plan.block
    if plan.whole:
        query_segs, key_segs = segments, segments
    else:
        leading = jnp.full((plan.own_seqs, plan.reach * plan.block), -1, jnp.int32)
        padded = jnp.concatenate([leading, segments], axis=1)
        start = block_index * plan.block
        query_segs = lax.dynamic_slice_in_dim(segments, start, plan.block, 1)
        key_segs = lax.dynamic_slice_in_dim(padded, start, key_count, 1)
    query_place = jnp.arange(plan.length, dtype=jnp.int32)[:, None] + plan.reach * plan.block
    key_place = jnp.arange(key_count, dtype=jnp.int32)[None, :]
    near = (key_place <= query_place) & (query_place - key_place < WINDOW)
    return (key_segs[:, None, :] == query_segs[:, :, None]) & near[None]


def with_earlier(plan, own):
    arrived = [own]
    for _ in range(plan.reach):
        arrived.append(shifted(arrived[-1], "blk", 1))
    return jnp.concatenate(arrived[::-1], axis=1) if plan.reach else own


def to_earlier(plan, grads):
    if not plan.reach:
        return grads
    block = plan.block
    total = grads[:, :block]
    for step in range(1, plan.reach + 1):
        total = (
            shifted(total.astype(BF16), "blk", -1).astype(F32)
            + grads[:, step * block : (step + 1) * block]
        )
    return total


def scores_of(queries, keys, allowed):
    scores = jnp.einsum("sqhd,skhd->shqk", queries, keys, preferred_element_type=F32)
    return jnp.where(allowed[:, None], scores, MASKED_SCORE)


def attend(queries, keys, values, allowed):
    scores = scores_of(queries, keys, allowed)
    top_score = jnp.max(scores, axis=-1, keepdims=True)
    exp_terms = jnp.exp(scores - top_score)
    totals = jnp.sum(exp_terms, axis=-1, keepdims=True)
    probs_low = (exp_terms / totals).astype(BF16)
    attended = jnp.einsum("shqk,skhd->sqhd", probs_low, values, preferred_element_type=F32)
    return attended, top_score + jnp.log(totals)


def attend_back(queries, keys, values, allowed, log_total, attended_grad):
    probs = jnp.exp(scores_of(queries, keys, allowed) - log_total)
    probs_low = probs.astype(BF16)
    values_grad = jnp.einsum(
        "shqk,sqhd->skhd", probs_low, attended_grad, preferred_element_type=F32
    )
    probs_grad = jnp.einsum("sqhd,skhd->shqk", attended_grad, values, preferred_element_type=F32)
    row_dot = jnp.sum(probs_grad * probs, axis=-1, keepdims=True)
    scores_low = (probs * (probs_grad - row_dot)).astype(BF16)
    queries_grad = jnp.einsum("shqk,skhd->sqhd", scores_low, keys, preferred_element_type=F32)
    keys_grad = jnp.einsum("shqk,sqhd->skhd", scores_low, queries, preferred_element_type=F32)
    return queries_grad, keys_grad, values_grad


def forward(plan, stream, qkv, dense, gains, scale_vec, allowed):
    width = plan.width
    head_dim = scale_vec.shape[0]
    part = qkv.shape[1] // 3
    local_heads = part // head_dim
    split = (plan.own_seqs, plan.length, local_heads, head_dim)
    out_w, up_w, down_w = dense[:, :width], dense[:, width:-width], dense[:, -width:]
    normed, factor_one = normalize(stream, gains[0])
    normed_all = gather_tokens(plan, normed.astype(BF16))
    projected = dot(normed_all, qkv)
    query_pre = projected[:, :part].reshape(split)
    queries = (query_pre * scale_vec).astype(BF16)
    keys = with_earlier(plan, projected[:, part : 2 * part].astype(BF16).reshape(split))
    values = with_earlier(plan, projected[:, 2 * part :].astype(BF16).reshape(split))
    attended_part, log_total = attend(queries, keys, values, allowed)
    attended = heads_to_tokens(plan, attended_part.astype(BF16).reshape(-1, part))
    middle = stream + dot(attended, out_w)
    normed_two, factor_two = normalize(middle, gains[1])
    normed_two = normed_two.astype(BF16)
    hidden = dot(normed_two, up_w)
    active = (hidden * jax.nn.sigmoid(hidden)).astype(BF16)
    result = middle + dot(active, down_w)
    kept = (
        stream, factor_one, normed_all, query_pre, queries, keys, values, log_total,
        attended, middle, factor_two, normed_two, hidden, active,
    )
    return result, kept


def backward(plan, upper, kept, qkv, dense, gains, scale_vec, allowed):
    (
        stream, factor_one, normed_all, query_pre, queries, keys, values, log_total,
        attended, middle, factor_two, normed_two, hidden, active,
    ) = kept
    width = plan.width
    head_dim = scale_vec.shape[0]
    part = qkv.shape[1] // 3
    out_w, up_w, down_w = dense[:, :width], dense[:, width:-width], dense[:, -width:]
    upper_low = upper.astype(BF16)
    down_grad = dot_rows(active, upper_low)
    active_grad = dot_cols(upper_low, down_w)
    gate = jax.nn.sigmoid(hidden)
    hidden_low = (active_grad * gate * (1.0 + hidden * (1.0 - gate))).astype(BF16)
    up_grad = dot_rows(normed_two, hidden_low)
    extra_two, mlp_gain_grad = norm_back(dot_cols(hidden_low, up_w), middle, factor_two, gains[1])
    middle_grad = upper + extra_two
    middle_low = middle_grad.astype(BF16)
    out_grad = dot_rows(attended, middle_low)
    dense_grad = jnp.concatenate([out_grad, up_grad, down_grad], axis=1).astype(BF16)
    dense_own = lax.psum_scatter(dense_grad, ALL, scatter_dimension=0, tiled=True)
    attended_grad = tokens_to_heads(plan, dot_cols(middle_low, out_w).astype(BF16))
    queries_grad, keys_grad, values_grad = attend_back(
        queries, keys, values, allowed, log_total, attended_grad.reshape(queries.shape)
    )
    query_bar = queries_grad.astype(BF16).astype(F32)
    scale_vec_grad = jnp.sum((query_bar * query_pre).reshape(-1, head_dim), axis=0)
    query_low = (query_bar * scale_vec).astype(BF16).reshape(-1, part)
    keys_low = to_earlier(plan, keys_grad).astype(BF16).reshape(-1, part)
    values_low = to_earlier(plan, values_grad).astype(BF16).reshape(-1, part)
    projected_low = jnp.concatenate([query_low, keys_low, values_low], axis=1)
    normed_grad = scatter_tokens(plan, dot_cols(projected_low, qkv))
    qkv_own = scatter_qkv(dot_rows(normed_all, projected_low))
    extra_one, attn_gain_grad = norm_back(normed_grad, stream, factor_one, gains[0])
    lower = middle_grad + extra_one
    return lower, qkv_own, dense_own, (attn_gain_grad, mlp_gain_grad), scale_vec_grad


def general_device(
    tokens,
    segments,
    qkv_weight,
    out_weight,
    up_weight,
    down_weight,
    attn_gain,
    mlp_gain,
    scale_param,
    cotangent,
):
    plan = Plan(tokens)
    layers, head_dim = scale_param.shape
    block_index = lax.axis_index("blk")
    scale_vecs = SCALE_BASE / math.sqrt(head_dim) * jax.nn.softplus(scale_param)
    own_gains = jnp.concatenate([attn_gain, mlp_gain], axis=0)
    gains = (
        lax.all_gather(own_gains.reshape(1, -1), ALL, axis=0, tiled=True)
        .reshape(-1, 2 * layers, attn_gain.shape[1])
        .transpose(1, 0, 2)
        .reshape(2 * layers, plan.width)
        .astype(F32)
    )
    if plan.whole:
        segments = lax.dynamic_slice_in_dim(
            segments, block_index * plan.own_seqs, plan.own_seqs, 0
        )
    allowed = window_mask(plan, segments, block_index)
    stream = to_plan(plan, tokens).astype(F32)
    qkvs, denses, kept = [], [], []
    for layer in range(layers):
        qkvs.append(gather_qkv(qkv_weight[layer]))
        own = jnp.concatenate([out_weight[layer], up_weight[layer], down_weight[layer]], axis=1)
        denses.append(lax.all_gather(own, ALL, axis=0, tiled=True))
        layer_gains = (gains[layer], gains[layers + layer])
        stream, saved = forward(
            plan, stream, qkvs[layer], denses[layer], layer_gains, scale_vecs[layer], allowed
        )
        kept.append(saved)
    layer_out = from_plan(plan, stream.astype(BF16))
    upper = to_plan(plan, cotangent).astype(F32)
    qkv_grads, dense_grads = [None] * layers, [None] * layers
    gain_grads, scale_grads = [None] * layers, [None] * layers
    for layer in reversed(range(layers)):
        layer_gains = (gains[layer], gains[layers + layer])
        upper, qkv_grads[layer], dense_grads[layer], gain_grads[layer], scale_grads[layer] = (
            backward(
                plan, upper, kept[layer], qkvs[layer], denses[layer], layer_gains,
                scale_vecs[layer], allowed,
            )
        )
    input_grad = from_plan(plan, upper.astype(BF16)).astype(F32)
    small = jnp.concatenate(
        [g[0] for g in gain_grads] + [g[1] for g in gain_grads] + scale_grads, axis=0
    )
    total = lax.psum(small, ALL)
    gain_total = total[: 2 * layers * plan.width].reshape(2 * layers, plan.width)
    owner = lax.axis_index(ALL)
    gain_rows = attn_gain.shape[1]
    own_total = lax.dynamic_slice_in_dim(gain_total, owner * gain_rows, gain_rows, 1)
    scale_total = total[2 * layers * plan.width :].reshape(layers, head_dim)
    scale_grad = scale_total * (SCALE_BASE / math.sqrt(head_dim)) * jax.nn.sigmoid(scale_param)
    dense_all = jnp.stack(dense_grads).astype(F32)
    width = plan.width
    return (
        layer_out,
        input_grad,
        jnp.stack(qkv_grads),
        dense_all[:, :, :width],
        dense_all[:, :, width:-width],
        dense_all[:, :, -width:],
        own_total[:layers],
        own_total[layers:],
        scale_grad,
    )


Q_ROWS = 256
KERNEL = pltpu.CompilerParams(vmem_limit_bytes=50 * 1024 * 1024)
LIGHT = pl.CostEstimate(flops=1 << 20, bytes_accessed=1 << 20, transcendentals=0)


def allowed_keys(col, row, first):
    count = first + row.shape[1]
    key_place = lax.broadcasted_iota(jnp.int32, (count, row.shape[1]), 0)
    query_place = lax.broadcasted_iota(jnp.int32, (count, row.shape[1]), 1) + first
    return (col[:count] == row) & (key_place <= query_place)


def token_places(length, heads, token_rows):
    for first in range(0, length, Q_ROWS):
        parts = []
        for start in range(0, Q_ROWS, token_rows):
            place = (first + start) // token_rows
            parts.append((start, place % heads, place // heads * token_rows))
        yield first, parts


def attend_kernel(token_rows, proj_ref, scale_ref, col_ref, row_ref, out_ref, lse_ref):
    length = proj_ref.shape[-1]
    queries = (proj_ref[0, 0] * scale_ref[...]).astype(BF16)
    keys = proj_ref[1, 0].T.astype(BF16)
    values = proj_ref[2, 0].astype(BF16)
    for first, parts in token_places(length, out_ref.shape[0], token_rows):
        end = first + Q_ROWS
        scores = jnp.dot(keys[:end], queries[:, first:end], preferred_element_type=F32)
        allowed = allowed_keys(col_ref[...], row_ref[:, first:end], first)
        scores = jnp.where(allowed, scores, MASKED_SCORE)
        top = jnp.max(scores, axis=0, keepdims=True)
        terms = jnp.exp(scores - top)
        total = jnp.sum(terms, axis=0, keepdims=True)
        probs = (terms * (1.0 / total)).astype(BF16)
        attended = jnp.dot(values[:, :end], probs, preferred_element_type=F32).astype(BF16)
        lse_ref[0, :, first:end] = top + jnp.log(total)
        for start, owner, offset in parts:
            out_ref[owner, 0, :, offset : offset + token_rows] = attended[
                :, start : start + token_rows
            ]


def attend_rows(projected, scale_vec, segments, owners, token_rows):
    head_dim = scale_vec.shape[0]
    length = projected.shape[1]
    local_heads = projected.shape[0] // 3 // head_dim
    tokens = length // owners
    attended, log_total = pl.pallas_call(
        functools.partial(attend_kernel, token_rows),
        grid=(local_heads,),
        in_specs=[
            pl.BlockSpec((3, 1, head_dim, length), lambda h: (0, h, 0, 0)),
            pl.BlockSpec((head_dim, 1), lambda h: (0, 0)),
            pl.BlockSpec((length, 1), lambda h: (0, 0)),
            pl.BlockSpec((1, length), lambda h: (0, 0)),
        ],
        out_specs=[
            pl.BlockSpec((owners, 1, head_dim, tokens), lambda h: (0, h, 0, 0)),
            pl.BlockSpec((1, 1, length), lambda h: (h, 0, 0)),
        ],
        out_shape=[
            jax.ShapeDtypeStruct((owners, local_heads, head_dim, tokens), BF16),
            jax.ShapeDtypeStruct((local_heads, 1, length), F32),
        ],
        compiler_params=KERNEL,
        cost_estimate=LIGHT,
    )(
        projected.reshape(3, local_heads, head_dim, length),
        scale_vec.reshape(head_dim, 1),
        segments.reshape(length, 1),
        segments.reshape(1, length),
    )
    return attended.reshape(owners, local_heads * head_dim, tokens), log_total


def attend_back_kernel(
    token_rows,
    proj_ref,
    grad_ref,
    lse_ref,
    scale_ref,
    col_ref,
    row_ref,
    out_ref,
    scale_grad_ref,
    keys_acc,
    values_acc,
):
    length = proj_ref.shape[-1]
    scale = scale_ref[...]
    query_pre = proj_ref[0, 0]
    queries = (query_pre * scale).astype(BF16)
    keys_t = proj_ref[1, 0].astype(BF16)
    keys = proj_ref[1, 0].T.astype(BF16)
    values = proj_ref[2, 0].T.astype(BF16)
    keys_acc[...] = jnp.zeros_like(keys_acc)
    values_acc[...] = jnp.zeros_like(values_acc)
    scale_grad = jnp.zeros((scale.shape[0], 1), F32)
    for first, parts in token_places(length, grad_ref.shape[0], token_rows):
        end = first + Q_ROWS
        block = queries[:, first:end]
        grad = jnp.concatenate(
            [grad_ref[owner, 0, :, at : at + token_rows] for _, owner, at in parts], axis=1
        )
        scores = jnp.dot(keys[:end], block, preferred_element_type=F32)
        allowed = allowed_keys(col_ref[...], row_ref[:, first:end], first)
        scores = jnp.where(allowed, scores, MASKED_SCORE)
        probs = jnp.exp(scores - lse_ref[0, :, first:end])
        probs_grad = jnp.dot(values[:end], grad, preferred_element_type=F32)
        row_dot = jnp.sum(probs_grad * probs, axis=0, keepdims=True)
        scores_low = (probs * (probs_grad - row_dot)).astype(BF16)
        values_acc[:, :end] += lax.dot_general(
            grad, probs.astype(BF16), NT, preferred_element_type=F32
        )
        keys_acc[:, :end] += lax.dot_general(
            block, scores_low, NT, preferred_element_type=F32
        )
        query_bar = jnp.dot(keys_t[:, :end], scores_low, preferred_element_type=F32)
        query_bar = query_bar.astype(BF16).astype(F32)
        scale_grad += jnp.sum(query_bar * query_pre[:, first:end], axis=1, keepdims=True)
        out_ref[0, 0, :, first:end] = (query_bar * scale).astype(BF16)
    out_ref[1, 0] = keys_acc[...].astype(BF16)
    out_ref[2, 0] = values_acc[...].astype(BF16)
    spread = jnp.broadcast_to(scale_grad, scale_grad_ref.shape)

    @pl.when(pl.program_id(0) == 0)
    def _():
        scale_grad_ref[...] = spread

    @pl.when(pl.program_id(0) > 0)
    def _():
        scale_grad_ref[...] += spread


def attend_back_rows(projected, attended_grad, log_total, scale_vec, segments, token_rows):
    head_dim = scale_vec.shape[0]
    length = projected.shape[1]
    local_heads = projected.shape[0] // 3 // head_dim
    owners, _, tokens = attended_grad.shape
    lanes = 128
    grads, scale_grad = pl.pallas_call(
        functools.partial(attend_back_kernel, token_rows),
        grid=(local_heads,),
        in_specs=[
            pl.BlockSpec((3, 1, head_dim, length), lambda h: (0, h, 0, 0)),
            pl.BlockSpec((owners, 1, head_dim, tokens), lambda h: (0, h, 0, 0)),
            pl.BlockSpec((1, 1, length), lambda h: (h, 0, 0)),
            pl.BlockSpec((head_dim, 1), lambda h: (0, 0)),
            pl.BlockSpec((length, 1), lambda h: (0, 0)),
            pl.BlockSpec((1, length), lambda h: (0, 0)),
        ],
        out_specs=[
            pl.BlockSpec((3, 1, head_dim, length), lambda h: (0, h, 0, 0)),
            pl.BlockSpec((head_dim, lanes), lambda h: (0, 0)),
        ],
        out_shape=[
            jax.ShapeDtypeStruct((3, local_heads, head_dim, length), BF16),
            jax.ShapeDtypeStruct((head_dim, lanes), F32),
        ],
        scratch_shapes=[
            pltpu.VMEM((head_dim, length), F32),
            pltpu.VMEM((head_dim, length), F32),
        ],
        compiler_params=KERNEL,
        cost_estimate=LIGHT,
    )(
        projected.reshape(3, local_heads, head_dim, length),
        attended_grad.reshape(owners, local_heads, head_dim, tokens),
        log_total,
        scale_vec.reshape(head_dim, 1),
        segments.reshape(length, 1),
        segments.reshape(1, length),
    )
    return grads.reshape(3 * local_heads * head_dim, length), scale_grad[:, 0]


def dense_grad_kernel(
    core_ref, attended_ref, normed_ref, active_ref, out_bar, up_bar, down_bar,
    own_ref, other_ref, normed_t, active_t,
):
    tile = pl.program_id(0)
    rows, width = own_ref.shape[2] * own_ref.shape[3] * 2, out_bar.shape[1]

    @pl.when(tile == 0)
    def _():
        normed_t[...] = normed_ref[...].astype(F32).T.astype(BF16)
        active_t[...] = active_ref[...].astype(F32).T.astype(BF16)

    start = pl.multiple_of(tile * rows, rows)
    first_core = core_ref[2] == 0
    lefts = (attended_ref, normed_t, active_t)
    for i, (left, right) in enumerate(zip(lefts, (out_bar, up_bar, down_bar))):
        grad = jnp.dot(left[pl.ds(start, rows), :], right[...], preferred_element_type=F32)
        grad = grad.reshape(2, 2, rows // 4, width)
        one, two = grad[:, 0], grad[:, 1]
        own_ref[0, 0, :, :, i * width : (i + 1) * width] = jnp.where(
            first_core, one, two
        ).astype(BF16)
        other_ref[0, 0, :, :, i * width : (i + 1) * width] = jnp.where(
            first_core, two, one
        ).astype(BF16)


def dense_grads(attended_t, normed, active, out_bar, up_bar, down_bar):
    width, tokens = attended_t.shape
    own = width // 32
    whole = pl.BlockSpec((tokens, width), lambda i, core: (0, 0))
    rows = pl.BlockSpec((1, 1, 2, own, 3 * width), lambda i, core: (i // 2, i % 2, 0, 0, 0))
    shape = jax.ShapeDtypeStruct((4, 2, 2, own, 3 * width), BF16)
    return pl.pallas_call(
        dense_grad_kernel,
        grid_spec=pltpu.PrefetchScalarGridSpec(
            num_scalar_prefetch=1,
            grid=(8,),
            in_specs=[pl.BlockSpec((width, tokens), lambda i, core: (0, 0))] + [whole] * 5,
            out_specs=[rows, rows],
            scratch_shapes=[pltpu.VMEM((width, tokens), BF16)] * 2,
        ),
        out_shape=[shape, shape],
        compiler_params=KERNEL,
        cost_estimate=LIGHT,
    )(place(), attended_t, normed, active, out_bar, up_bar, down_bar)


def place():
    head = lax.axis_index("head")
    index = [lax.axis_index("blk"), head // 2, head % 2, lax.axis_index("batch")]
    return jnp.stack(index).astype(jnp.int32)


def assemble_kernel(place_ref, *refs):
    pieces, whole_ref = refs[:10], refs[10]
    half = whole_ref.shape[-1] // 2
    blk, row, core = place_ref[0], place_ref[1], place_ref[2]
    for i in range(2):
        at_core = core if i == 0 else 1 - core
        own, across, beside, one, two = pieces[5 * i : 5 * i + 5]
        whole_ref[0, blk, row, at_core] = own[0]
        whole_ref[0, 1 - blk, row, at_core] = across[0]
        whole_ref[0, blk, 1 - row, at_core] = beside[0]
        whole_ref[0, 1 - blk, 1 - row, at_core, :, :half] = one[0]
        whole_ref[0, 1 - blk, 1 - row, at_core, :, half:] = two[0]


def assemble(pieces):
    batch, own, columns = pieces[0].shape
    specs = [
        pl.BlockSpec((1, own, piece.shape[-1]), lambda i, at: (i ^ at[3], 0, 0))
        for piece in pieces
    ]
    whole = pl.pallas_call(
        assemble_kernel,
        grid_spec=pltpu.PrefetchScalarGridSpec(
            num_scalar_prefetch=1,
            grid=(batch,),
            in_specs=specs,
            out_specs=pl.BlockSpec((1, 2, 2, 2, own, columns), lambda i, at: (i, 0, 0, 0, 0, 0)),
        ),
        out_shape=jax.ShapeDtypeStruct((batch, 2, 2, 2, own, columns), BF16),
        compiler_params=KERNEL,
        cost_estimate=LIGHT,
    )(place(), *pieces)
    return whole.reshape(-1, columns)


def assemble_columns_kernel(place_ref, along_ref, across_ref, whole_ref, *extra_ref):
    blk = place_ref[0]
    columns = whole_ref.shape[-1]
    whole_ref[0, blk] = along_ref[0, :, :columns]
    whole_ref[0, 1 - blk] = across_ref[0, :, :columns]
    for extra in extra_ref:
        extra[0, blk] = along_ref[0, :, columns:]
        extra[0, 1 - blk] = across_ref[0, :, columns:]


def assemble_columns(along, across, columns):
    batch, own, both = along.shape
    rows = pl.BlockSpec((1, own, both), lambda i, at: (i ^ at[3], 0, 0))
    shapes = [(batch, 2, own, columns)]
    if both > columns:
        shapes.append((batch, 2, own, both - columns))
    parts = pl.pallas_call(
        assemble_columns_kernel,
        grid_spec=pltpu.PrefetchScalarGridSpec(
            num_scalar_prefetch=1,
            grid=(batch,),
            in_specs=[rows, rows],
            out_specs=[pl.BlockSpec((1,) + s[1:], lambda i, at: (i, 0, 0, 0)) for s in shapes],
        ),
        out_shape=[jax.ShapeDtypeStruct(s, BF16) for s in shapes],
        compiler_params=KERNEL,
        cost_estimate=LIGHT,
    )(place(), along, across)
    return [part.reshape(-1, part.shape[-1]) for part in parts]


def project_kernel(with_norm, place_ref, *refs):
    pieces, (gain_ref, weight_ref, normed_ref, projected_ref) = refs[:4], refs[4:]
    head = place_ref[1] * 2 + place_ref[2]
    rows = pieces[0].shape[0]
    for i, piece in enumerate(pieces):
        value = piece[...]
        if with_norm:
            stream = value.astype(F32)
            factor = lax.rsqrt(jnp.mean(stream * stream, axis=-1, keepdims=True) + EPSILON)
            value = (stream * factor * gain_ref[...]).astype(BF16)
        normed_ref[pl.ds(pl.multiple_of((head ^ i) * rows, rows), rows), :] = value
    projected = jnp.dot(normed_ref[...], weight_ref[...], preferred_element_type=F32)
    projected_ref[...] = projected.T


def project(pieces, gain, weight, with_norm, token_rows):
    tokens, width = pieces[0].shape
    length, columns = 4 * tokens, weight.shape[1]
    groups = tokens // token_rows
    piece = pl.BlockSpec((token_rows, width), lambda g, at: (g, 0))
    return pl.pallas_call(
        functools.partial(project_kernel, with_norm),
        grid_spec=pltpu.PrefetchScalarGridSpec(
            num_scalar_prefetch=1,
            grid=(groups,),
            in_specs=[piece] * 4
            + [
                pl.BlockSpec((1, width), lambda g, at: (0, 0)),
                pl.BlockSpec((width, columns), lambda g, at: (0, 0)),
            ],
            out_specs=[
                pl.BlockSpec((4 * token_rows, width), lambda g, at: (g, 0)),
                pl.BlockSpec((columns, 4 * token_rows), lambda g, at: (0, g)),
            ],
        ),
        out_shape=[
            jax.ShapeDtypeStruct((length, width), BF16),
            jax.ShapeDtypeStruct((columns, length), F32),
        ],
        compiler_params=KERNEL,
        cost_estimate=LIGHT,
    )(place(), *pieces, gain.reshape(1, width), weight)


def project_back_kernel(
    place_ref, bars_ref, weight_ref, normed_ref, own_ref, other_ref, mine_ref, sent_ref, total
):
    step = pl.program_id(0)
    bars = bars_ref[...].astype(F32).T.astype(BF16)
    upper = lax.dot_general(bars, weight_ref[...], NT, preferred_element_type=F32)
    rows = upper.shape[0] // 2
    first_core = place_ref[2] == 0
    one, two = upper[:rows], upper[rows:]
    own_ref[0, 0] = jnp.where(first_core, one, two)
    other_ref[0, 0] = jnp.where(first_core, two, one).astype(BF16)
    grad = lax.dot_general(normed_ref[...], bars, TN, preferred_element_type=F32)

    @pl.when(step == 0)
    def _():
        total[...] = grad

    @pl.when(step > 0)
    def _():
        total[...] += grad

    @pl.when(step == pl.num_programs(0) - 1)
    def _():
        batch, own, columns = mine_ref.shape
        first_blk = place_ref[0] == 0
        for i in range(batch):
            one = total[2 * i * own : (2 * i + 1) * own, :]
            two = total[(2 * i + 1) * own : (2 * i + 2) * own, :]
            mine_ref[i] = jnp.where(first_blk, one, two)
            sent_ref[i] = jnp.where(first_blk, two, one).astype(BF16)


def project_back(bars, weight, normed, token_rows):
    columns, length = bars.shape
    width = weight.shape[0]
    pair = 2 * token_rows
    quarter = pl.BlockSpec((1, 1, token_rows, width), lambda s, at: (s // 2, s % 2, 0, 0))
    rows = (4, width // 8, columns)
    whole = pl.BlockSpec(rows, lambda s, at: (0, 0, 0))
    return pl.pallas_call(
        project_back_kernel,
        grid_spec=pltpu.PrefetchScalarGridSpec(
            num_scalar_prefetch=1,
            grid=(length // pair,),
            in_specs=[
                pl.BlockSpec((columns, pair), lambda s, at: (0, s)),
                pl.BlockSpec((width, columns), lambda s, at: (0, 0)),
                pl.BlockSpec((pair, width), lambda s, at: (s, 0)),
            ],
            out_specs=[quarter, quarter, whole, whole],
            scratch_shapes=[pltpu.VMEM((width, columns), F32)],
        ),
        out_shape=[
            jax.ShapeDtypeStruct((2, 2, token_rows, width), F32),
            jax.ShapeDtypeStruct((2, 2, token_rows, width), BF16),
            jax.ShapeDtypeStruct(rows, F32),
            jax.ShapeDtypeStruct(rows, BF16),
        ],
        compiler_params=KERNEL,
        cost_estimate=LIGHT,
    )(place(), bars, weight, normed)


def tied(*arrays):
    return lax.optimization_barrier(arrays)


def swapped(array, axis, mask):
    size = lax.axis_size(axis)
    return lax.ppermute(array, axis, [(i, i ^ mask) for i in range(size)])


def pick(array, index, axis=0):
    return lax.dynamic_index_in_dim(array, index, axis, keepdims=False)


def swap_halves(array):
    me = lax.axis_index("blk")
    got = swapped(pick(array, 1 - me), "blk", 1)
    kept = pick(array, me)
    return jnp.stack([jnp.where(me == 0, kept, got), jnp.where(me == 0, got, kept)])


def scatter_row(halves):
    row = lax.axis_index("head") // 2
    got = swapped(pick(halves, 1 - row, 1).astype(BF16), "head", 2).astype(F32)
    return (pick(halves, row, 1) + got).reshape(-1, halves.shape[-1])


def over_head(parts):
    return lax.all_to_all(parts, "head", split_axis=0, concat_axis=0, tiled=True)


def qkv_columns(rows, extra):
    own, width = rows.shape
    part = width // 3 // 4
    sent = rows.reshape(own, 3, 4, part).transpose(2, 0, 1, 3).reshape(4, own, 3 * part)
    if extra is not None:
        sent = jnp.concatenate([sent, jnp.broadcast_to(extra[None], (4,) + extra.shape)], axis=2)
    return over_head(sent)


def along_batch(piece):
    return jnp.stack([piece] + [swapped(piece, "batch", mask) for mask in (1, 2, 3)])


def other_core(array):
    return swapped(array, "head", 1)


def to_neighbours(along):
    return swapped(along, "blk", 1), swapped(along, "head", 2)


def to_beside(across):
    return swapped(across[..., : across.shape[-1] // 2], "head", 2)


def to_across(beside):
    return swapped(beside[..., beside.shape[-1] // 2 :], "blk", 1)


def over_batch(parts):
    me = lax.axis_index("batch")
    total = pick(parts, me).astype(F32)
    for mask in (1, 2, 3):
        total = total + swapped(pick(parts, me ^ mask).astype(BF16), "batch", mask).astype(F32)
    return total


def columns_to_rows(summed):
    moved = over_head(summed.astype(BF16).reshape(4, -1, summed.shape[-1]))
    rows = moved.shape[1]
    return moved.reshape(4, rows, 3, -1).transpose(1, 2, 0, 3).reshape(rows, -1).astype(F32)


def diagonal_sent(cored):
    blk, row = place()[:2]
    rows = pick(pick(cored, 1 - blk, 1), 1 - row, 1)
    half = rows.shape[-1] // 2
    return swapped(rows[..., :half], "blk", 1), swapped(rows[..., half:], "head", 2)


def neighbours_sent(cored, one, two):
    blk, row = place()[:2]
    half = one.shape[-1]
    across = pick(pick(cored, 1 - blk, 1), row, 1)
    beside = pick(pick(cored, blk, 1), 1 - row, 1)
    across = jnp.concatenate(
        [across[..., :half], across[..., half:].astype(F32) + two.astype(F32)], axis=-1
    ).astype(BF16)
    beside = jnp.concatenate(
        [beside[..., :half].astype(F32) + one.astype(F32), beside[..., half:]], axis=-1
    ).astype(BF16)
    return swapped(across, "blk", 1), swapped(beside, "head", 2)


def own_sum(cored, across, beside):
    blk, row = place()[:2]
    own = pick(pick(cored, blk, 1), row, 1)
    return own.astype(F32) + across.astype(F32) + beside.astype(F32)


def sum_all(array):
    for axis, mask in (("head", 1), ("head", 2), ("blk", 1), ("batch", 1), ("batch", 2)):
        array = array + swapped(array, axis, mask)
    return array


def gain_back(weight, weight_grad, gain):
    return jnp.sum(weight.astype(F32) * weight_grad, axis=-1) / gain.astype(F32)


def lower_of(upper, stream, factor, gain):
    return norm_back(upper, stream, factor, gain)[0]


def spread_device(
    tokens,
    segments,
    qkv_weight,
    out_weight,
    up_weight,
    down_weight,
    attn_gain,
    mlp_gain,
    scale_param,
    cotangent,
):
    layers, head_dim = scale_param.shape
    _, token_rows, width = tokens.shape
    scale_vecs = SCALE_BASE / math.sqrt(head_dim) * jax.nn.softplus(scale_param)
    segments = pick(segments, lax.axis_index("blk"))
    own_gains = jnp.concatenate([attn_gain, mlp_gain], axis=0)

    part3 = 3 * width // 4
    dense_own = [
        jnp.concatenate([out_weight[i], up_weight[i], down_weight[i]], axis=1) for i in (0, 1)
    ]

    first = swap_halves(tokens).reshape(-1, width)
    stream = first.astype(F32)
    dense_near = along_batch(dense_own[0])
    columns = qkv_columns(qkv_weight[0], own_gains.T)
    columns, first = tied(columns.reshape(-1, columns.shape[-1]), first)
    along = along_batch(columns)
    far = swapped(first, "head", 2)
    near = other_core(first)
    dense_near, far = tied(dense_near, far)
    token_pieces = (first, near, far, other_core(far))
    across, beside = swapped(dense_near, "blk", 1), swapped(dense_near, "head", 2)
    along, across, beside, dense_next = tied(along, across, beside, dense_own[1])
    qkv_across = swapped(along, "blk", 1)
    one = to_beside(across)
    dense_next = along_batch(dense_next)
    next_columns = qkv_columns(qkv_weight[1], None).reshape(-1, part3)
    qkv_across, one, beside, dense_next, next_columns = tied(
        qkv_across, one, beside, dense_next, next_columns
    )
    two = to_across(beside)
    pieces = [(dense_near, across, beside, one, two)]
    beside = swapped(dense_next, "head", 2)
    next_along = along_batch(next_columns)
    weight, gains = assemble_columns(along, qkv_across, part3)
    qkvs = [weight]
    gains = gains.T.astype(F32)

    kept, denses = [], []
    for layer in range(layers):
        normed, factor_one = normalize(stream, gains[layer])
        if layer == 1:
            normed, across = tied(normed.astype(BF16), across)
            far = swapped(normed, "head", 2)
            next_across = swapped(next_along, "blk", 1)
            far, after = tied(far, across)
            one = to_beside(after)
            token_pieces = (normed, other_core(normed), far, other_core(far))
            next_across, after = tied(next_across, beside)
            two = to_across(after)
            pieces.append((dense_next, across, beside, one, two))
            qkvs.append(assemble_columns(next_along, next_across, part3)[0])
        normed_all, projected = project(
            token_pieces, gains[layer], qkvs[layer], layer == 0, token_rows
        )
        attended, log_total = attend_rows(
            projected, scale_vecs[layer], segments, 4, token_rows
        )
        if layer == 0:
            attended, two, next_along = tied(attended, pieces[0][4], next_along)
            pieces[0] = pieces[0][:4] + (two,)
            across = swapped(dense_next, "blk", 1)
        else:
            attended, one, two = tied(attended, *pieces[1][3:])
            pieces[1] = pieces[1][:3] + (one, two)
        swaps = tuple(other_core(piece) for piece in pieces[layer])
        attended_t = over_head(attended)
        if layer == 0:
            attended_t, beside, swaps = tied(attended_t, beside, swaps)
        else:
            attended_t, swaps = tied(attended_t, swaps)
        attended_t = attended_t.reshape(width, -1)
        denses.append(assemble(pieces[layer] + swaps))
        dense = denses[layer]
        out_w, up_w, down_w = dense[:, :width], dense[:, width:-width], dense[:, -width:]
        middle = stream + dot_rows(attended_t, out_w)
        normed_two, factor_two = normalize(middle, gains[layers + layer])
        normed_two = normed_two.astype(BF16)
        hidden = dot(normed_two, up_w)
        active = (hidden * jax.nn.sigmoid(hidden)).astype(BF16)
        kept.append(
            (
                stream, factor_one, normed_all, projected, log_total, attended_t, middle,
                factor_two, normed_two, hidden, active,
            )
        )
        stream = middle + dot(active, down_w)
    layer_out = swap_halves(stream.astype(BF16).reshape(tokens.shape))
    upper = swap_halves(cotangent).reshape(-1, width).astype(F32)

    dense_grad, scale_grads = [None] * layers, [None] * layers
    for layer in reversed(range(layers)):
        (
            stream, factor_one, normed_all, projected, log_total, attended_t, middle,
            factor_two, normed_two, hidden, active,
        ) = kept[layer]
        qkv, dense = qkvs[layer], denses[layer]
        out_w, up_w, down_w = dense[:, :width], dense[:, width:-width], dense[:, -width:]
        down_bar = upper.astype(BF16)
        gate = jax.nn.sigmoid(hidden)
        up_bar = (
            dot_cols(down_bar, down_w) * gate * (1.0 + hidden * (1.0 - gate))
        ).astype(BF16)
        middle_grad = upper + lower_of(
            dot_cols(up_bar, up_w), middle, factor_two, gains[layers + layer]
        )
        out_bar = middle_grad.astype(BF16)
        attended_grad = over_head(dot_cols(out_w, out_bar).astype(BF16).reshape(4, -1, out_bar.shape[0]))
        grads, others = dense_grads(attended_t, normed_two, active, out_bar, up_bar, down_bar)
        if layer == 0:
            attended_grad, others, diagonal = tied(attended_grad, others, diagonal)
            sent = neighbours_sent(cored, *diagonal)
            last = cored
        else:
            attended_grad, others = tied(attended_grad, others)
        others = other_core(others)
        bars, scale_grads[layer] = attend_back_rows(
            projected, attended_grad, log_total, scale_vecs[layer], segments, token_rows
        )
        if layer == 0:
            bars, others, got = tied(bars, others, got)
            qkv_sums = [None, over_batch(mine + got.astype(F32))]
        else:
            bars, others = tied(bars, others)
        cored = (grads.astype(F32) + others.astype(F32)).astype(BF16)
        halves, to_core, mine, got = project_back(bars, qkv, normed_all, token_rows)
        halves = halves + other_core(to_core).astype(F32)
        if layer == 0:
            got = swapped(got, "blk", 1)
            diagonal = diagonal_sent(cored)
            halves, diagonal, sent = tied(halves, diagonal, sent)
            dense_grad[1] = over_batch(own_sum(last, *sent))
            sent = neighbours_sent(cored, *diagonal)
            normed_grad = scatter_row(halves)
            normed_grad, got, sent = tied(normed_grad, got, sent)
            qkv_sums[0] = over_batch(mine + got.astype(F32))
            dense_grad[0] = over_batch(own_sum(cored, *sent))
            qkv_grads = [columns_to_rows(part) for part in qkv_sums]
        else:
            normed_grad = scatter_row(halves)
            normed_grad, cored, got = tied(normed_grad, cored, got)
            diagonal = diagonal_sent(cored)
            got = swapped(got, "blk", 1)
        upper = middle_grad + lower_of(normed_grad, stream, factor_one, gains[layer])
    input_grad = swap_halves(upper.astype(BF16).reshape(tokens.shape)).astype(F32)
    scale_total = sum_all(jnp.stack(scale_grads))
    scale_grad = scale_total * (SCALE_BASE / math.sqrt(head_dim)) * jax.nn.sigmoid(scale_param)
    dense_all = jnp.stack([part.astype(F32) for part in dense_grad])
    qkv_all = jnp.stack(qkv_grads)
    up_all = dense_all[:, :, width:-width]
    return (
        layer_out,
        input_grad,
        qkv_all,
        dense_all[:, :, :width],
        up_all,
        dense_all[:, :, -width:],
        gain_back(qkv_weight, qkv_all, attn_gain),
        gain_back(up_weight, up_all, mlp_gain),
        scale_grad,
    )


def per_device(*args):
    tokens, segments = args[0], args[1]
    sizes = tuple(lax.axis_size(axis) for axis in ALL)
    heads = tokens.shape[2] // args[8].shape[1]
    spread = (
        sizes == (4, 2, 4)
        and tokens.shape[0] == 2
        and args[2].shape[0] == 2
        and tokens.shape[1] % 128 == 0
        and Q_ROWS % tokens.shape[1] == 0
        and segments.shape[1] <= WINDOW
        and segments.shape[1] % Q_ROWS == 0
        and heads % 4 == 0
        and tokens.shape[2] % 256 == 0
    )
    return spread_device(*args) if spread else general_device(*args)


def solution(mesh):
    rows = P(None, ALL, None)
    by_token = P("batch", ("blk", "head"), None)
    return jax.shard_map(
        per_device,
        mesh=mesh,
        in_specs=(
            by_token, P("batch", None), rows, rows, rows, rows, P(None, ALL), P(None, ALL), P(),
            by_token,
        ),
        out_specs=(
            by_token, by_token, rows, rows, rows, rows, P(None, ALL), P(None, ALL), P(),
        ),
        check_vma=False,
    )
```

```python
import functools
import math

import jax
import jax.numpy as jnp
from jax import lax
from jax.experimental import pallas as pl
from jax.experimental.pallas import tpu as pltpu
from jax.sharding import PartitionSpec as P

WINDOW = 1024
EPSILON = 1e-06
SCALE_BASE = 1.4426950408889634
MASKED_SCORE = -1e30

ALL = ("batch", "blk", "head")
REST = ("batch", "blk")
F32 = jnp.float32
BF16 = jnp.bfloat16


def shifted(block, axis, distance):
    devices = range(lax.axis_size(axis))
    route = [(i - distance, i) for i in devices if i - distance in devices]
    return lax.ppermute(block, axis, route)


NT = (((1,), (1,)), ((), ()))
TN = (((0,), (0,)), ((), ()))


def dot(left, right):
    return jnp.dot(left, right, preferred_element_type=F32)


def dot_rows(left, right):
    return lax.dot_general(left, right, (((0,), (0,)), ((), ())), preferred_element_type=F32)


def dot_cols(left, right):
    return lax.dot_general(left, right, (((1,), (1,)), ((), ())), preferred_element_type=F32)


def normalize(stream, gain):
    factor = lax.rsqrt(jnp.mean(stream * stream, axis=-1, keepdims=True) + EPSILON)
    return stream * factor * gain, factor


def norm_back(upper, stream, factor, gain):
    inner = upper * gain
    gain_grad = jnp.sum(upper * stream * factor, axis=0)
    lower = factor * inner - stream * factor * factor * factor * jnp.mean(
        inner * stream, axis=-1, keepdims=True
    )
    return lower, gain_grad


class Plan:
    def __init__(self, tokens):
        self.seqs, self.rows, self.width = tokens.shape
        self.heads = lax.axis_size("head")
        self.blks = lax.axis_size("blk")
        self.block = self.rows * self.heads
        self.whole = self.seqs % self.blks == 0
        if self.whole:
            self.groups, self.own_seqs = self.blks, self.seqs // self.blks
            self.reach = 0
        else:
            self.groups, self.own_seqs = 1, self.seqs
            self.reach = min((WINDOW - 1) // self.block + 1, self.blks - 1)
        self.length = self.groups * self.block
        self.tokens = self.seqs * self.rows


def to_plan(plan, array):
    if plan.whole and plan.blks > 1:
        array = lax.all_to_all(array, "blk", split_axis=0, concat_axis=0, tiled=True)
    return array.reshape(plan.tokens, plan.width)


def from_plan(plan, flat):
    array = flat.reshape(plan.seqs, plan.rows, plan.width)
    if plan.whole and plan.blks > 1:
        array = lax.all_to_all(array, "blk", split_axis=0, concat_axis=0, tiled=True)
    return array


def in_sequence(plan, by_head, width):
    parts = by_head.reshape(plan.heads, plan.groups, plan.own_seqs, plan.rows, width)
    return parts.transpose(2, 1, 0, 3, 4).reshape(-1, width)


def by_owner(plan, rows, width):
    parts = rows.reshape(plan.own_seqs, plan.groups, plan.heads, plan.rows, width)
    return parts.transpose(2, 1, 0, 3, 4).reshape(plan.heads, plan.tokens, width)


def gather_tokens(plan, rows):
    moved = lax.all_gather(rows, "head", axis=0, tiled=False)
    return in_sequence(plan, moved, rows.shape[-1])


def scatter_tokens(plan, rows):
    width = rows.shape[-1]
    return lax.psum_scatter(
        by_owner(plan, rows.astype(BF16), width), "head", scatter_dimension=0, tiled=False
    ).astype(F32)


def heads_to_tokens(plan, rows):
    part = rows.shape[-1]
    moved = lax.all_to_all(
        by_owner(plan, rows, part), "head", split_axis=0, concat_axis=0, tiled=True
    )
    return moved.transpose(1, 0, 2).reshape(plan.tokens, plan.heads * part)


def tokens_to_heads(plan, rows):
    part = rows.shape[-1] // plan.heads
    sent = rows.reshape(plan.tokens, plan.heads, part).transpose(1, 0, 2)
    moved = lax.all_to_all(sent, "head", split_axis=0, concat_axis=0, tiled=True)
    return in_sequence(plan, moved, part)


def gather_qkv(rows):
    own, width = rows.shape
    heads = lax.axis_size("head")
    part = width // 3 // heads
    sent = rows.reshape(own, 3, heads, part).transpose(2, 0, 1, 3).reshape(heads, own, 3 * part)
    moved = lax.all_to_all(sent, "head", split_axis=0, concat_axis=0, tiled=True)
    full = lax.all_gather(moved, REST, axis=0, tiled=True)
    return full.reshape(-1, 3 * part)


def scatter_qkv(grad):
    heads = lax.axis_size("head")
    part = grad.shape[1] // 3
    summed = lax.psum_scatter(grad.astype(BF16), REST, scatter_dimension=0, tiled=True)
    own = summed.shape[0] // heads
    moved = lax.all_to_all(
        summed.reshape(heads, own, 3 * part), "head", split_axis=0, concat_axis=0, tiled=True
    )
    return (
        moved.reshape(heads, own, 3, part)
        .transpose(1, 2, 0, 3)
        .reshape(own, 3 * heads * part)
        .astype(F32)
    )


def window_mask(plan, segments, block_index):
    key_count = plan.length + plan.reach * plan.block
    if plan.whole:
        query_segs, key_segs = segments, segments
    else:
        leading = jnp.full((plan.own_seqs, plan.reach * plan.block), -1, jnp.int32)
        padded = jnp.concatenate([leading, segments], axis=1)
        start = block_index * plan.block
        query_segs = lax.dynamic_slice_in_dim(segments, start, plan.block, 1)
        key_segs = lax.dynamic_slice_in_dim(padded, start, key_count, 1)
    query_place = jnp.arange(plan.length, dtype=jnp.int32)[:, None] + plan.reach * plan.block
    key_place = jnp.arange(key_count, dtype=jnp.int32)[None, :]
    near = (key_place <= query_place) & (query_place - key_place < WINDOW)
    return (key_segs[:, None, :] == query_segs[:, :, None]) & near[None]


def with_earlier(plan, own):
    arrived = [own]
    for _ in range(plan.reach):
        arrived.append(shifted(arrived[-1], "blk", 1))
    return jnp.concatenate(arrived[::-1], axis=1) if plan.reach else own


def to_earlier(plan, grads):
    if not plan.reach:
        return grads
    block = plan.block
    total = grads[:, :block]
    for step in range(1, plan.reach + 1):
        total = (
            shifted(total.astype(BF16), "blk", -1).astype(F32)
            + grads[:, step * block : (step + 1) * block]
        )
    return total


def scores_of(queries, keys, allowed):
    scores = jnp.einsum("sqhd,skhd->shqk", queries, keys, preferred_element_type=F32)
    return jnp.where(allowed[:, None], scores, MASKED_SCORE)


def attend(queries, keys, values, allowed):
    scores = scores_of(queries, keys, allowed)
    top_score = jnp.max(scores, axis=-1, keepdims=True)
    exp_terms = jnp.exp(scores - top_score)
    totals = jnp.sum(exp_terms, axis=-1, keepdims=True)
    probs_low = (exp_terms / totals).astype(BF16)
    attended = jnp.einsum("shqk,skhd->sqhd", probs_low, values, preferred_element_type=F32)
    return attended, top_score + jnp.log(totals)


def attend_back(queries, keys, values, allowed, log_total, attended_grad):
    probs = jnp.exp(scores_of(queries, keys, allowed) - log_total)
    probs_low = probs.astype(BF16)
    values_grad = jnp.einsum(
        "shqk,sqhd->skhd", probs_low, attended_grad, preferred_element_type=F32
    )
    probs_grad = jnp.einsum("sqhd,skhd->shqk", attended_grad, values, preferred_element_type=F32)
    row_dot = jnp.sum(probs_grad * probs, axis=-1, keepdims=True)
    scores_low = (probs * (probs_grad - row_dot)).astype(BF16)
    queries_grad = jnp.einsum("shqk,skhd->sqhd", scores_low, keys, preferred_element_type=F32)
    keys_grad = jnp.einsum("shqk,sqhd->skhd", scores_low, queries, preferred_element_type=F32)
    return queries_grad, keys_grad, values_grad


def forward(plan, stream, qkv, dense, gains, scale_vec, allowed):
    width = plan.width
    head_dim = scale_vec.shape[0]
    part = qkv.shape[1] // 3
    local_heads = part // head_dim
    split = (plan.own_seqs, plan.length, local_heads, head_dim)
    out_w, up_w, down_w = dense[:, :width], dense[:, width:-width], dense[:, -width:]
    normed, factor_one = normalize(stream, gains[0])
    normed_all = gather_tokens(plan, normed.astype(BF16))
    projected = dot(normed_all, qkv)
    query_pre = projected[:, :part].reshape(split)
    queries = (query_pre * scale_vec).astype(BF16)
    keys = with_earlier(plan, projected[:, part : 2 * part].astype(BF16).reshape(split))
    values = with_earlier(plan, projected[:, 2 * part :].astype(BF16).reshape(split))
    attended_part, log_total = attend(queries, keys, values, allowed)
    attended = heads_to_tokens(plan, attended_part.astype(BF16).reshape(-1, part))
    middle = stream + dot(attended, out_w)
    normed_two, factor_two = normalize(middle, gains[1])
    normed_two = normed_two.astype(BF16)
    hidden = dot(normed_two, up_w)
    active = (hidden * jax.nn.sigmoid(hidden)).astype(BF16)
    result = middle + dot(active, down_w)
    kept = (
        stream, factor_one, normed_all, query_pre, queries, keys, values, log_total,
        attended, middle, factor_two, normed_two, hidden, active,
    )
    return result, kept


def backward(plan, upper, kept, qkv, dense, gains, scale_vec, allowed):
    (
        stream, factor_one, normed_all, query_pre, queries, keys, values, log_total,
        attended, middle, factor_two, normed_two, hidden, active,
    ) = kept
    width = plan.width
    head_dim = scale_vec.shape[0]
    part = qkv.shape[1] // 3
    out_w, up_w, down_w = dense[:, :width], dense[:, width:-width], dense[:, -width:]
    upper_low = upper.astype(BF16)
    down_grad = dot_rows(active, upper_low)
    active_grad = dot_cols(upper_low, down_w)
    gate = jax.nn.sigmoid(hidden)
    hidden_low = (active_grad * gate * (1.0 + hidden * (1.0 - gate))).astype(BF16)
    up_grad = dot_rows(normed_two, hidden_low)
    extra_two, mlp_gain_grad = norm_back(dot_cols(hidden_low, up_w), middle, factor_two, gains[1])
    middle_grad = upper + extra_two
    middle_low = middle_grad.astype(BF16)
    out_grad = dot_rows(attended, middle_low)
    dense_grad = jnp.concatenate([out_grad, up_grad, down_grad], axis=1).astype(BF16)
    dense_own = lax.psum_scatter(dense_grad, ALL, scatter_dimension=0, tiled=True)
    attended_grad = tokens_to_heads(plan, dot_cols(middle_low, out_w).astype(BF16))
    queries_grad, keys_grad, values_grad = attend_back(
        queries, keys, values, allowed, log_total, attended_grad.reshape(queries.shape)
    )
    query_bar = queries_grad.astype(BF16).astype(F32)
    scale_vec_grad = jnp.sum((query_bar * query_pre).reshape(-1, head_dim), axis=0)
    query_low = (query_bar * scale_vec).astype(BF16).reshape(-1, part)
    keys_low = to_earlier(plan, keys_grad).astype(BF16).reshape(-1, part)
    values_low = to_earlier(plan, values_grad).astype(BF16).reshape(-1, part)
    projected_low = jnp.concatenate([query_low, keys_low, values_low], axis=1)
    normed_grad = scatter_tokens(plan, dot_cols(projected_low, qkv))
    qkv_own = scatter_qkv(dot_rows(normed_all, projected_low))
    extra_one, attn_gain_grad = norm_back(normed_grad, stream, factor_one, gains[0])
    lower = middle_grad + extra_one
    return lower, qkv_own, dense_own, (attn_gain_grad, mlp_gain_grad), scale_vec_grad


def general_device(
    tokens,
    segments,
    qkv_weight,
    out_weight,
    up_weight,
    down_weight,
    attn_gain,
    mlp_gain,
    scale_param,
    cotangent,
):
    plan = Plan(tokens)
    layers, head_dim = scale_param.shape
    block_index = lax.axis_index("blk")
    scale_vecs = SCALE_BASE / math.sqrt(head_dim) * jax.nn.softplus(scale_param)
    own_gains = jnp.concatenate([attn_gain, mlp_gain], axis=0)
    gains = (
        lax.all_gather(own_gains.reshape(1, -1), ALL, axis=0, tiled=True)
        .reshape(-1, 2 * layers, attn_gain.shape[1])
        .transpose(1, 0, 2)
        .reshape(2 * layers, plan.width)
        .astype(F32)
    )
    if plan.whole:
        segments = lax.dynamic_slice_in_dim(
            segments, block_index * plan.own_seqs, plan.own_seqs, 0
        )
    allowed = window_mask(plan, segments, block_index)
    stream = to_plan(plan, tokens).astype(F32)
    qkvs, denses, kept = [], [], []
    for layer in range(layers):
        qkvs.append(gather_qkv(qkv_weight[layer]))
        own = jnp.concatenate([out_weight[layer], up_weight[layer], down_weight[layer]], axis=1)
        denses.append(lax.all_gather(own, ALL, axis=0, tiled=True))
        layer_gains = (gains[layer], gains[layers + layer])
        stream, saved = forward(
            plan, stream, qkvs[layer], denses[layer], layer_gains, scale_vecs[layer], allowed
        )
        kept.append(saved)
    layer_out = from_plan(plan, stream.astype(BF16))
    upper = to_plan(plan, cotangent).astype(F32)
    qkv_grads, dense_grads = [None] * layers, [None] * layers
    gain_grads, scale_grads = [None] * layers, [None] * layers
    for layer in reversed(range(layers)):
        layer_gains = (gains[layer], gains[layers + layer])
        upper, qkv_grads[layer], dense_grads[layer], gain_grads[layer], scale_grads[layer] = (
            backward(
                plan, upper, kept[layer], qkvs[layer], denses[layer], layer_gains,
                scale_vecs[layer], allowed,
            )
        )
    input_grad = from_plan(plan, upper.astype(BF16)).astype(F32)
    small = jnp.concatenate(
        [g[0] for g in gain_grads] + [g[1] for g in gain_grads] + scale_grads, axis=0
    )
    total = lax.psum(small, ALL)
    gain_total = total[: 2 * layers * plan.width].reshape(2 * layers, plan.width)
    owner = lax.axis_index(ALL)
    gain_rows = attn_gain.shape[1]
    own_total = lax.dynamic_slice_in_dim(gain_total, owner * gain_rows, gain_rows, 1)
    scale_total = total[2 * layers * plan.width :].reshape(layers, head_dim)
    scale_grad = scale_total * (SCALE_BASE / math.sqrt(head_dim)) * jax.nn.sigmoid(scale_param)
    dense_all = jnp.stack(dense_grads).astype(F32)
    width = plan.width
    return (
        layer_out,
        input_grad,
        jnp.stack(qkv_grads),
        dense_all[:, :, :width],
        dense_all[:, :, width:-width],
        dense_all[:, :, -width:],
        own_total[:layers],
        own_total[layers:],
        scale_grad,
    )


Q_ROWS = 256
KERNEL = pltpu.CompilerParams(vmem_limit_bytes=32 * 1024 * 1024)
LIGHT = pl.CostEstimate(flops=1 << 20, bytes_accessed=1 << 20, transcendentals=0)


def allowed_keys(col, row, first):
    count = first + row.shape[1]
    key_place = lax.broadcasted_iota(jnp.int32, (count, row.shape[1]), 0)
    query_place = lax.broadcasted_iota(jnp.int32, (count, row.shape[1]), 1) + first
    return (col[:count] == row) & (key_place <= query_place)


def token_places(length, heads, token_rows):
    for first in range(0, length, Q_ROWS):
        parts = []
        for start in range(0, Q_ROWS, token_rows):
            place = (first + start) // token_rows
            parts.append((start, place % heads, place // heads * token_rows))
        yield first, parts


def attend_kernel(token_rows, proj_ref, scale_ref, col_ref, row_ref, out_ref, lse_ref):
    length = proj_ref.shape[-1]
    queries = (proj_ref[0, 0] * scale_ref[...]).astype(BF16)
    keys = proj_ref[1, 0].T.astype(BF16)
    values = proj_ref[2, 0].astype(BF16)
    for first, parts in token_places(length, out_ref.shape[0], token_rows):
        end = first + Q_ROWS
        scores = jnp.dot(keys[:end], queries[:, first:end], preferred_element_type=F32)
        allowed = allowed_keys(col_ref[...], row_ref[:, first:end], first)
        scores = jnp.where(allowed, scores, MASKED_SCORE)
        top = jnp.max(scores, axis=0, keepdims=True)
        terms = jnp.exp(scores - top)
        total = jnp.sum(terms, axis=0, keepdims=True)
        probs = (terms * (1.0 / total)).astype(BF16)
        attended = jnp.dot(values[:, :end], probs, preferred_element_type=F32).astype(BF16)
        lse_ref[0, :, first:end] = top + jnp.log(total)
        for start, owner, offset in parts:
            out_ref[owner, 0, :, offset : offset + token_rows] = attended[
                :, start : start + token_rows
            ]


def attend_rows(projected, scale_vec, segments, owners, token_rows):
    head_dim = scale_vec.shape[0]
    length = projected.shape[1]
    local_heads = projected.shape[0] // 3 // head_dim
    tokens = length // owners
    attended, log_total = pl.pallas_call(
        functools.partial(attend_kernel, token_rows),
        grid=(local_heads,),
        in_specs=[
            pl.BlockSpec((3, 1, head_dim, length), lambda h: (0, h, 0, 0)),
            pl.BlockSpec((head_dim, 1), lambda h: (0, 0)),
            pl.BlockSpec((length, 1), lambda h: (0, 0)),
            pl.BlockSpec((1, length), lambda h: (0, 0)),
        ],
        out_specs=[
            pl.BlockSpec((owners, 1, head_dim, tokens), lambda h: (0, h, 0, 0)),
            pl.BlockSpec((1, 1, length), lambda h: (h, 0, 0)),
        ],
        out_shape=[
            jax.ShapeDtypeStruct((owners, local_heads, head_dim, tokens), BF16),
            jax.ShapeDtypeStruct((local_heads, 1, length), F32),
        ],
        compiler_params=KERNEL,
        cost_estimate=LIGHT,
    )(
        projected.reshape(3, local_heads, head_dim, length),
        scale_vec.reshape(head_dim, 1),
        segments.reshape(length, 1),
        segments.reshape(1, length),
    )
    return attended.reshape(owners, local_heads * head_dim, tokens), log_total


def attend_back_kernel(
    token_rows,
    proj_ref,
    grad_ref,
    lse_ref,
    scale_ref,
    col_ref,
    row_ref,
    out_ref,
    scale_grad_ref,
    keys_acc,
    values_acc,
):
    length = proj_ref.shape[-1]
    scale = scale_ref[...]
    query_pre = proj_ref[0, 0]
    queries = (query_pre * scale).astype(BF16)
    keys_t = proj_ref[1, 0].astype(BF16)
    keys = proj_ref[1, 0].T.astype(BF16)
    values = proj_ref[2, 0].T.astype(BF16)
    keys_acc[...] = jnp.zeros_like(keys_acc)
    values_acc[...] = jnp.zeros_like(values_acc)
    scale_grad = jnp.zeros((scale.shape[0], 1), F32)
    for first, parts in token_places(length, grad_ref.shape[0], token_rows):
        end = first + Q_ROWS
        block = queries[:, first:end]
        grad = jnp.concatenate(
            [grad_ref[owner, 0, :, at : at + token_rows] for _, owner, at in parts], axis=1
        )
        scores = jnp.dot(keys[:end], block, preferred_element_type=F32)
        allowed = allowed_keys(col_ref[...], row_ref[:, first:end], first)
        scores = jnp.where(allowed, scores, MASKED_SCORE)
        probs = jnp.exp(scores - lse_ref[0, :, first:end])
        probs_grad = jnp.dot(values[:end], grad, preferred_element_type=F32)
        row_dot = jnp.sum(probs_grad * probs, axis=0, keepdims=True)
        scores_low = (probs * (probs_grad - row_dot)).astype(BF16)
        values_acc[:, :end] += lax.dot_general(
            grad, probs.astype(BF16), NT, preferred_element_type=F32
        )
        keys_acc[:, :end] += lax.dot_general(
            block, scores_low, NT, preferred_element_type=F32
        )
        query_bar = jnp.dot(keys_t[:, :end], scores_low, preferred_element_type=F32)
        query_bar = query_bar.astype(BF16).astype(F32)
        scale_grad += jnp.sum(query_bar * query_pre[:, first:end], axis=1, keepdims=True)
        out_ref[0, 0, :, first:end] = (query_bar * scale).astype(BF16)
    out_ref[1, 0] = keys_acc[...].astype(BF16)
    out_ref[2, 0] = values_acc[...].astype(BF16)
    spread = jnp.broadcast_to(scale_grad, scale_grad_ref.shape)

    @pl.when(pl.program_id(0) == 0)
    def _():
        scale_grad_ref[...] = spread

    @pl.when(pl.program_id(0) > 0)
    def _():
        scale_grad_ref[...] += spread


def attend_back_rows(projected, attended_grad, log_total, scale_vec, segments, token_rows):
    head_dim = scale_vec.shape[0]
    length = projected.shape[1]
    local_heads = projected.shape[0] // 3 // head_dim
    owners, _, tokens = attended_grad.shape
    lanes = 128
    grads, scale_grad = pl.pallas_call(
        functools.partial(attend_back_kernel, token_rows),
        grid=(local_heads,),
        in_specs=[
            pl.BlockSpec((3, 1, head_dim, length), lambda h: (0, h, 0, 0)),
            pl.BlockSpec((owners, 1, head_dim, tokens), lambda h: (0, h, 0, 0)),
            pl.BlockSpec((1, 1, length), lambda h: (h, 0, 0)),
            pl.BlockSpec((head_dim, 1), lambda h: (0, 0)),
            pl.BlockSpec((length, 1), lambda h: (0, 0)),
            pl.BlockSpec((1, length), lambda h: (0, 0)),
        ],
        out_specs=[
            pl.BlockSpec((3, 1, head_dim, length), lambda h: (0, h, 0, 0)),
            pl.BlockSpec((head_dim, lanes), lambda h: (0, 0)),
        ],
        out_shape=[
            jax.ShapeDtypeStruct((3, local_heads, head_dim, length), BF16),
            jax.ShapeDtypeStruct((head_dim, lanes), F32),
        ],
        scratch_shapes=[
            pltpu.VMEM((head_dim, length), F32),
            pltpu.VMEM((head_dim, length), F32),
        ],
        compiler_params=KERNEL,
        cost_estimate=LIGHT,
    )(
        projected.reshape(3, local_heads, head_dim, length),
        attended_grad.reshape(owners, local_heads, head_dim, tokens),
        log_total,
        scale_vec.reshape(head_dim, 1),
        segments.reshape(length, 1),
        segments.reshape(1, length),
    )
    return grads.reshape(3 * local_heads * head_dim, length), scale_grad[:, 0]


def dense_grad_kernel(
    core_ref, attended_ref, normed_ref, active_ref, out_bar, up_bar, down_bar,
    own_ref, other_ref, normed_t, active_t,
):
    tile = pl.program_id(0)
    rows, width = own_ref.shape[1] * own_ref.shape[3] * 2, out_bar.shape[1]

    @pl.when(tile == 0)
    def _():
        normed_t[...] = normed_ref[...].astype(F32).T.astype(BF16)
        active_t[...] = active_ref[...].astype(F32).T.astype(BF16)

    start = pl.multiple_of(tile * rows, rows)
    first_core = core_ref[2] == 0
    lefts = (attended_ref, normed_t, active_t)
    for i, (left, right) in enumerate(zip(lefts, (out_bar, up_bar, down_bar))):
        grad = jnp.dot(left[pl.ds(start, rows), :], right[...], preferred_element_type=F32)
        grad = grad.reshape(2, 2, rows // 4, width)
        one, two = grad[:, 0], grad[:, 1]
        own_ref[0, :, 0, :, i * width : (i + 1) * width] = jnp.where(
            first_core, one, two
        ).astype(BF16)
        other_ref[0, :, 0, :, i * width : (i + 1) * width] = jnp.where(
            first_core, two, one
        ).astype(BF16)


def dense_grads(attended_t, normed, active, out_bar, up_bar, down_bar):
    width, tokens = attended_t.shape
    own = width // 32
    whole = pl.BlockSpec((tokens, width), lambda i, core: (0, 0))
    rows = pl.BlockSpec((1, 2, 1, own, 3 * width), lambda i, core: (i % 2, 0, i // 2, 0, 0))
    shape = jax.ShapeDtypeStruct((2, 2, 4, own, 3 * width), BF16)
    return pl.pallas_call(
        dense_grad_kernel,
        grid_spec=pltpu.PrefetchScalarGridSpec(
            num_scalar_prefetch=1,
            grid=(8,),
            in_specs=[pl.BlockSpec((width, tokens), lambda i, core: (0, 0))] + [whole] * 5,
            out_specs=[rows, rows],
            scratch_shapes=[pltpu.VMEM((width, tokens), BF16)] * 2,
        ),
        out_shape=[shape, shape],
        compiler_params=KERNEL,
        cost_estimate=LIGHT,
    )(place(), attended_t, normed, active, out_bar, up_bar, down_bar)


def place():
    head = lax.axis_index("head")
    return jnp.stack([lax.axis_index("blk"), head // 2, head % 2]).astype(jnp.int32)


def assemble_kernel(place_ref, *refs):
    pieces, whole_ref = refs[:10], refs[10]
    half = whole_ref.shape[-1] // 2
    blk, row, core = place_ref[0], place_ref[1], place_ref[2]
    for i in range(2):
        at_core = core if i == 0 else 1 - core
        own, across, beside, one, two = pieces[5 * i : 5 * i + 5]
        whole_ref[0, blk, row, at_core] = own[0]
        whole_ref[0, 1 - blk, row, at_core] = across[0]
        whole_ref[0, blk, 1 - row, at_core] = beside[0]
        whole_ref[0, 1 - blk, 1 - row, at_core, :, :half] = one[0]
        whole_ref[0, 1 - blk, 1 - row, at_core, :, half:] = two[0]


def assemble(pieces):
    batch, own, columns = pieces[0].shape
    specs = [
        pl.BlockSpec((1, own, piece.shape[-1]), lambda i, at: (i, 0, 0))
        for piece in pieces
    ]
    whole = pl.pallas_call(
        assemble_kernel,
        grid_spec=pltpu.PrefetchScalarGridSpec(
            num_scalar_prefetch=1,
            grid=(batch,),
            in_specs=specs,
            out_specs=pl.BlockSpec((1, 2, 2, 2, own, columns), lambda i, at: (i, 0, 0, 0, 0, 0)),
        ),
        out_shape=jax.ShapeDtypeStruct((batch, 2, 2, 2, own, columns), BF16),
        compiler_params=KERNEL,
        cost_estimate=LIGHT,
    )(place(), *pieces)
    return whole.reshape(-1, columns)


def assemble_columns_kernel(place_ref, along_ref, across_ref, whole_ref, *extra_ref):
    blk = place_ref[0]
    columns = whole_ref.shape[-1]
    whole_ref[0, blk] = along_ref[0, :, :columns]
    whole_ref[0, 1 - blk] = across_ref[0, :, :columns]
    for extra in extra_ref:
        extra[0, blk] = along_ref[0, :, columns:]
        extra[0, 1 - blk] = across_ref[0, :, columns:]


def assemble_columns(along, across, columns):
    batch, own, both = along.shape
    rows = pl.BlockSpec((1, own, both), lambda i, at: (i, 0, 0))
    shapes = [(batch, 2, own, columns)]
    if both > columns:
        shapes.append((batch, 2, own, both - columns))
    parts = pl.pallas_call(
        assemble_columns_kernel,
        grid_spec=pltpu.PrefetchScalarGridSpec(
            num_scalar_prefetch=1,
            grid=(batch,),
            in_specs=[rows, rows],
            out_specs=[pl.BlockSpec((1,) + s[1:], lambda i, at: (i, 0, 0, 0)) for s in shapes],
        ),
        out_shape=[jax.ShapeDtypeStruct(s, BF16) for s in shapes],
        compiler_params=KERNEL,
        cost_estimate=LIGHT,
    )(place(), along, across)
    return [part.reshape(-1, part.shape[-1]) for part in parts]


def project_kernel(with_norm, place_ref, *refs):
    pieces, (gain_ref, weight_ref, normed_ref, projected_ref) = refs[:4], refs[4:]
    head = place_ref[1] * 2 + place_ref[2]
    rows = pieces[0].shape[0]
    for i, piece in enumerate(pieces):
        value = piece[...]
        if with_norm:
            stream = value.astype(F32)
            factor = lax.rsqrt(jnp.mean(stream * stream, axis=-1, keepdims=True) + EPSILON)
            value = (stream * factor * gain_ref[...]).astype(BF16)
        normed_ref[pl.ds(pl.multiple_of((head ^ i) * rows, rows), rows), :] = value
    projected = jnp.dot(normed_ref[...], weight_ref[...], preferred_element_type=F32)
    projected_ref[...] = projected.T


def project(pieces, gain, weight, with_norm, token_rows):
    tokens, width = pieces[0].shape
    length, columns = 4 * tokens, weight.shape[1]
    groups = tokens // token_rows
    piece = pl.BlockSpec((token_rows, width), lambda g, at: (g, 0))
    return pl.pallas_call(
        functools.partial(project_kernel, with_norm),
        grid_spec=pltpu.PrefetchScalarGridSpec(
            num_scalar_prefetch=1,
            grid=(groups,),
            in_specs=[piece] * 4
            + [
                pl.BlockSpec((1, width), lambda g, at: (0, 0)),
                pl.BlockSpec((width, columns), lambda g, at: (0, 0)),
            ],
            out_specs=[
                pl.BlockSpec((4 * token_rows, width), lambda g, at: (g, 0)),
                pl.BlockSpec((columns, 4 * token_rows), lambda g, at: (0, g)),
            ],
        ),
        out_shape=[
            jax.ShapeDtypeStruct((length, width), BF16),
            jax.ShapeDtypeStruct((columns, length), F32),
        ],
        compiler_params=KERNEL,
        cost_estimate=LIGHT,
    )(place(), *pieces, gain.reshape(1, width), weight)


def project_back_kernel(
    place_ref, bars_ref, weight_ref, normed_ref, own_ref, other_ref, mine_ref, sent_ref, bars_t
):
    @pl.when(pl.program_id(0) == 0)
    def _():
        bars_t[...] = bars_ref[...].astype(F32).T.astype(BF16)

    upper = lax.dot_general(bars_t[...], weight_ref[...], NT, preferred_element_type=F32)
    upper = upper.reshape(2, 2, 2, -1, upper.shape[-1])
    first_core = place_ref[2] == 0
    one, two = upper[:, :, 0], upper[:, :, 1]
    own_ref[...] = jnp.where(first_core, one, two)
    other_ref[...] = jnp.where(first_core, two, one).astype(BF16)
    grad = lax.dot_general(normed_ref[...], bars_t[...], TN, preferred_element_type=F32)
    batch, own, columns = mine_ref.shape
    grad = grad.reshape(batch, 2, own, columns)
    first_blk = place_ref[0] == 0
    one, two = grad[:, 0], grad[:, 1]
    mine_ref[...] = jnp.where(first_blk, one, two)
    sent_ref[...] = jnp.where(first_blk, two, one).astype(BF16)


def project_back(bars, weight, normed, token_rows):
    columns, length = bars.shape
    width = weight.shape[0]
    tile = width // 2
    quarter = pl.BlockSpec((2, 2, token_rows, tile), lambda i, at: (0, 0, 0, i))
    rows = (4, width // 8, columns)
    half = pl.BlockSpec((2,) + rows[1:], lambda i, at: (i, 0, 0))
    return pl.pallas_call(
        project_back_kernel,
        grid_spec=pltpu.PrefetchScalarGridSpec(
            num_scalar_prefetch=1,
            grid=(2,),
            in_specs=[
                pl.BlockSpec((columns, length), lambda i, at: (0, 0)),
                pl.BlockSpec((tile, columns), lambda i, at: (i, 0)),
                pl.BlockSpec((length, tile), lambda i, at: (0, i)),
            ],
            out_specs=[quarter, quarter, half, half],
            scratch_shapes=[pltpu.VMEM((length, columns), BF16)],
        ),
        out_shape=[
            jax.ShapeDtypeStruct((2, 2, token_rows, width), F32),
            jax.ShapeDtypeStruct((2, 2, token_rows, width), BF16),
            jax.ShapeDtypeStruct(rows, F32),
            jax.ShapeDtypeStruct(rows, BF16),
        ],
        compiler_params=KERNEL,
        cost_estimate=LIGHT,
    )(place(), bars, weight, normed)


def tied(*arrays):
    return lax.optimization_barrier(arrays)


def swapped(array, axis, mask):
    size = lax.axis_size(axis)
    return lax.ppermute(array, axis, [(i, i ^ mask) for i in range(size)])


def pick(array, index, axis=0):
    return lax.dynamic_index_in_dim(array, index, axis, keepdims=False)


def swap_halves(array):
    me = lax.axis_index("blk")
    got = swapped(pick(array, 1 - me), "blk", 1)
    kept = pick(array, me)
    return jnp.stack([jnp.where(me == 0, kept, got), jnp.where(me == 0, got, kept)])


def scatter_row(halves):
    row = lax.axis_index("head") // 2
    got = swapped(pick(halves, 1 - row, 1).astype(BF16), "head", 2).astype(F32)
    return (pick(halves, row, 1) + got).reshape(-1, halves.shape[-1])


def over_head(parts):
    return lax.all_to_all(parts, "head", split_axis=0, concat_axis=0, tiled=True)


def qkv_columns(rows, extra):
    own, width = rows.shape
    part = width // 3 // 4
    sent = rows.reshape(own, 3, 4, part).transpose(2, 0, 1, 3).reshape(4, own, 3 * part)
    if extra is not None:
        sent = jnp.concatenate([sent, jnp.broadcast_to(extra[None], (4,) + extra.shape)], axis=2)
    return over_head(sent)


def along_batch(piece):
    return lax.all_gather(piece, "batch", axis=0, tiled=False)


def other_core(array):
    return swapped(array, "head", 1)


def to_beside(across):
    return swapped(across[..., : across.shape[-1] // 2], "head", 2)


def to_across(beside):
    return swapped(beside[..., beside.shape[-1] // 2 :], "blk", 1)


def over_batch(parts):
    return lax.psum_scatter(parts.astype(BF16), "batch", scatter_dimension=0, tiled=False)


def columns_to_rows(summed):
    moved = over_head(summed.astype(BF16).reshape(4, -1, summed.shape[-1]))
    rows = moved.shape[1]
    return moved.reshape(4, rows, 3, -1).transpose(1, 2, 0, 3).reshape(rows, -1).astype(F32)


def diagonal_sent(cored):
    blk, row = place()[:2]
    rows = pick(pick(cored, 1 - blk), 1 - row)
    half = rows.shape[-1] // 2
    return swapped(rows[..., :half], "blk", 1), swapped(rows[..., half:], "head", 2)


def neighbours_sent(cored, one, two):
    blk, row = place()[:2]
    half = one.shape[-1]
    across = pick(pick(cored, 1 - blk), row)
    beside = pick(pick(cored, blk), 1 - row)
    across = jnp.concatenate(
        [across[..., :half], across[..., half:].astype(F32) + two.astype(F32)], axis=-1
    ).astype(BF16)
    beside = jnp.concatenate(
        [beside[..., :half].astype(F32) + one.astype(F32), beside[..., half:]], axis=-1
    ).astype(BF16)
    return swapped(across, "blk", 1), swapped(beside, "head", 2)


def own_sum(cored, across, beside):
    blk, row = place()[:2]
    own = pick(pick(cored, blk), row)
    return own.astype(F32) + across.astype(F32) + beside.astype(F32)


def sum_all(array):
    for axis, mask in (("head", 1), ("head", 2), ("blk", 1), ("batch", 1), ("batch", 2)):
        array = array + swapped(array, axis, mask)
    return array


def gain_back(weight, weight_grad, gain):
    return jnp.sum(weight.astype(F32) * weight_grad, axis=-1) / gain.astype(F32)


def lower_of(upper, stream, factor, gain):
    return norm_back(upper, stream, factor, gain)[0]


def spread_device(
    tokens,
    segments,
    qkv_weight,
    out_weight,
    up_weight,
    down_weight,
    attn_gain,
    mlp_gain,
    scale_param,
    cotangent,
):
    layers, head_dim = scale_param.shape
    _, token_rows, width = tokens.shape
    scale_vecs = SCALE_BASE / math.sqrt(head_dim) * jax.nn.softplus(scale_param)
    segments = pick(segments, lax.axis_index("blk"))
    own_gains = jnp.concatenate([attn_gain, mlp_gain], axis=0)

    part3 = 3 * width // 4
    dense_own = [
        jnp.concatenate([out_weight[i], up_weight[i], down_weight[i]], axis=1) for i in (0, 1)
    ]

    first = swap_halves(tokens).reshape(-1, width)
    upper = swap_halves(cotangent).reshape(-1, width)
    dense_near = along_batch(dense_own[0])
    columns = qkv_columns(qkv_weight[0], own_gains.T)
    columns, first, upper = tied(columns.reshape(-1, columns.shape[-1]), first, upper)
    stream, upper = first.astype(F32), upper.astype(F32)
    far, near = swapped(first, "head", 2), other_core(first)
    both = other_core(far)
    next_columns = qkv_columns(qkv_weight[1], None).reshape(-1, part3)
    columns, dense_near, near, far, both, next_columns = tied(
        columns, dense_near, near, far, both, next_columns
    )
    token_pieces = (first, near, far, both)
    across, beside = swapped(dense_near, "blk", 1), swapped(dense_near, "head", 2)
    along = along_batch(columns)
    along, across, beside, next_columns = tied(along, across, beside, next_columns)
    qkv_across = swapped(along, "blk", 1)
    one = to_beside(across)
    next_along = along_batch(next_columns)
    qkv_across, one, beside, next_along, dense_next = tied(
        qkv_across, one, beside, next_along, dense_own[1]
    )
    two = to_across(beside)
    pieces = [(dense_near, across, beside, one, two)]
    dense_next = along_batch(dense_next)
    weight, gains = assemble_columns(along, qkv_across, part3)
    qkvs = [weight]
    gains = gains.T.astype(F32)

    kept, denses = [], []
    for layer in range(layers):
        normed, factor_one = normalize(stream, gains[layer])
        if layer == 1:
            normed, next_across, dense_after = tied(normed.astype(BF16), next_across, dense_next)
            far, near = swapped(normed, "head", 2), other_core(normed)
            across = swapped(dense_after, "blk", 1)
            far, near, across, beside = tied(far, near, across, beside)
            token_pieces = (normed, near, far, other_core(far))
            one, two = to_beside(across), to_across(beside)
            pieces.append((dense_next, across, beside, one, two))
            qkvs.append(assemble_columns(next_along, next_across, part3)[0])
        normed_all, projected = project(
            token_pieces, gains[layer], qkvs[layer], layer == 0, token_rows
        )
        attended, log_total = attend_rows(
            projected, scale_vecs[layer], segments, 4, token_rows
        )
        attended, one, two = tied(attended, *pieces[layer][3:])
        pieces[layer] = pieces[layer][:3] + (one, two)
        swaps = tuple(other_core(piece) for piece in pieces[layer])
        attended_t = over_head(attended)
        if layer == 0:
            attended_t, swaps, dense_next = tied(attended_t, swaps, dense_next)
            next_across = swapped(next_along, "blk", 1)
            beside = swapped(dense_next, "head", 2)
        else:
            attended_t, swaps = tied(attended_t, swaps)
        attended_t = attended_t.reshape(width, -1)
        denses.append(assemble(pieces[layer] + swaps))
        dense = denses[layer]
        out_w, up_w, down_w = dense[:, :width], dense[:, width:-width], dense[:, -width:]
        middle = stream + dot_rows(attended_t, out_w)
        normed_two, factor_two = normalize(middle, gains[layers + layer])
        normed_two = normed_two.astype(BF16)
        hidden = dot(normed_two, up_w)
        active = (hidden * jax.nn.sigmoid(hidden)).astype(BF16)
        kept.append(
            (
                stream, factor_one, normed_all, projected, log_total, attended_t, middle,
                factor_two, normed_two, hidden, active,
            )
        )
        stream = middle + dot(active, down_w)
    layer_out = swap_halves(stream.astype(BF16).reshape(tokens.shape))

    dense_grad, scale_grads = [None] * layers, [None] * layers
    for layer in reversed(range(layers)):
        (
            stream, factor_one, normed_all, projected, log_total, attended_t, middle,
            factor_two, normed_two, hidden, active,
        ) = kept[layer]
        qkv, dense = qkvs[layer], denses[layer]
        out_w, up_w, down_w = dense[:, :width], dense[:, width:-width], dense[:, -width:]
        down_bar = upper.astype(BF16)
        gate = jax.nn.sigmoid(hidden)
        up_bar = (
            dot_cols(down_bar, down_w) * gate * (1.0 + hidden * (1.0 - gate))
        ).astype(BF16)
        middle_grad = upper + lower_of(
            dot_cols(up_bar, up_w), middle, factor_two, gains[layers + layer]
        )
        out_bar = middle_grad.astype(BF16)
        attended_grad = over_head(dot_cols(out_w, out_bar).astype(BF16).reshape(4, -1, out_bar.shape[0]))
        grads, others = dense_grads(attended_t, normed_two, active, out_bar, up_bar, down_bar)
        if layer == 0:
            attended_grad, others, diagonal, got = tied(attended_grad, others, diagonal, got)
            sent = neighbours_sent(cored, *diagonal)
            last = cored
            qkv_sums = [None, over_batch(mine + got.astype(F32))]
        else:
            attended_grad, others, layer_out = tied(attended_grad, others, layer_out)
        others = other_core(others)
        bars, scale_grads[layer] = attend_back_rows(
            projected, attended_grad, log_total, scale_vecs[layer], segments, token_rows
        )
        bars, others = tied(bars, others)
        cored = (grads.astype(F32) + others.astype(F32)).astype(BF16)
        if layer == 0:
            bars, cored = tied(bars, cored)
            diagonal = diagonal_sent(cored)
        halves, to_core, mine, got = project_back(bars, qkv, normed_all, token_rows)
        halves = halves + other_core(to_core).astype(F32)
        if layer == 0:
            got = swapped(got, "blk", 1)
            halves, diagonal, sent = tied(halves, diagonal, sent)
            dense_grad[1] = over_batch(own_sum(last, *sent))
            sent = neighbours_sent(cored, *diagonal)
            normed_grad = scatter_row(halves)
            normed_grad, got, sent = tied(normed_grad, got, sent)
            qkv_sums[0] = over_batch(mine + got.astype(F32))
            dense_grad[0] = over_batch(own_sum(cored, *sent))
            qkv_grads = [columns_to_rows(part) for part in qkv_sums]
        else:
            normed_grad = scatter_row(halves)
            normed_grad, cored, got = tied(normed_grad, cored, got)
            diagonal = diagonal_sent(cored)
            got = swapped(got, "blk", 1)
        upper = middle_grad + lower_of(normed_grad, stream, factor_one, gains[layer])
    input_grad = swap_halves(upper.astype(BF16).reshape(tokens.shape)).astype(F32)
    scale_total = sum_all(jnp.stack(scale_grads))
    scale_grad = scale_total * (SCALE_BASE / math.sqrt(head_dim)) * jax.nn.sigmoid(scale_param)
    dense_all = jnp.stack([part.astype(F32) for part in dense_grad])
    qkv_all = jnp.stack(qkv_grads)
    up_all = dense_all[:, :, width:-width]
    return (
        layer_out,
        input_grad,
        qkv_all,
        dense_all[:, :, :width],
        up_all,
        dense_all[:, :, -width:],
        gain_back(qkv_weight, qkv_all, attn_gain),
        gain_back(up_weight, up_all, mlp_gain),
        scale_grad,
    )


def per_device(*args):
    tokens, segments = args[0], args[1]
    sizes = tuple(lax.axis_size(axis) for axis in ALL)
    heads = tokens.shape[2] // args[8].shape[1]
    spread = (
        sizes == (4, 2, 4)
        and tokens.shape[0] == 2
        and args[2].shape[0] == 2
        and tokens.shape[1] % 128 == 0
        and Q_ROWS % tokens.shape[1] == 0
        and segments.shape[1] <= WINDOW
        and segments.shape[1] % Q_ROWS == 0
        and heads % 4 == 0
        and tokens.shape[2] % 256 == 0
    )
    return spread_device(*args) if spread else general_device(*args)


def solution(mesh):
    rows = P(None, ALL, None)
    by_token = P("batch", ("blk", "head"), None)
    return jax.shard_map(
        per_device,
        mesh=mesh,
        in_specs=(
            by_token, P("batch", None), rows, rows, rows, rows, P(None, ALL), P(None, ALL), P(),
            by_token,
        ),
        out_specs=(
            by_token, by_token, rows, rows, rows, rows, P(None, ALL), P(None, ALL), P(),
        ),
        check_vma=False,
    )
```

```python
import functools
import math

import jax
import jax.numpy as jnp
from jax import lax
from jax.experimental import pallas as pl
from jax.experimental.pallas import tpu as pltpu
from jax.sharding import PartitionSpec as P

WINDOW = 1024
EPSILON = 1e-06
SCALE_BASE = 1.4426950408889634
MASKED_SCORE = -1e30

ALL = ("batch", "blk", "head")
REST = ("batch", "blk")
F32 = jnp.float32
BF16 = jnp.bfloat16


def shifted(block, axis, distance):
    devices = range(lax.axis_size(axis))
    route = [(i - distance, i) for i in devices if i - distance in devices]
    return lax.ppermute(block, axis, route)


NT = (((1,), (1,)), ((), ()))
TN = (((0,), (0,)), ((), ()))


def dot(left, right):
    return jnp.dot(left, right, preferred_element_type=F32)


def dot_rows(left, right):
    return lax.dot_general(left, right, (((0,), (0,)), ((), ())), preferred_element_type=F32)


def dot_cols(left, right):
    return lax.dot_general(left, right, (((1,), (1,)), ((), ())), preferred_element_type=F32)


def normalize(stream, gain):
    factor = lax.rsqrt(jnp.mean(stream * stream, axis=-1, keepdims=True) + EPSILON)
    return stream * factor * gain, factor


def norm_back(upper, stream, factor, gain):
    inner = upper * gain
    gain_grad = jnp.sum(upper * stream * factor, axis=0)
    lower = factor * inner - stream * factor * factor * factor * jnp.mean(
        inner * stream, axis=-1, keepdims=True
    )
    return lower, gain_grad


class Plan:
    def __init__(self, tokens):
        self.seqs, self.rows, self.width = tokens.shape
        self.heads = lax.axis_size("head")
        self.blks = lax.axis_size("blk")
        self.block = self.rows * self.heads
        self.whole = self.seqs % self.blks == 0
        if self.whole:
            self.groups, self.own_seqs = self.blks, self.seqs // self.blks
            self.reach = 0
        else:
            self.groups, self.own_seqs = 1, self.seqs
            self.reach = min((WINDOW - 1) // self.block + 1, self.blks - 1)
        self.length = self.groups * self.block
        self.tokens = self.seqs * self.rows


def to_plan(plan, array):
    if plan.whole and plan.blks > 1:
        array = lax.all_to_all(array, "blk", split_axis=0, concat_axis=0, tiled=True)
    return array.reshape(plan.tokens, plan.width)


def from_plan(plan, flat):
    array = flat.reshape(plan.seqs, plan.rows, plan.width)
    if plan.whole and plan.blks > 1:
        array = lax.all_to_all(array, "blk", split_axis=0, concat_axis=0, tiled=True)
    return array


def in_sequence(plan, by_head, width):
    parts = by_head.reshape(plan.heads, plan.groups, plan.own_seqs, plan.rows, width)
    return parts.transpose(2, 1, 0, 3, 4).reshape(-1, width)


def by_owner(plan, rows, width):
    parts = rows.reshape(plan.own_seqs, plan.groups, plan.heads, plan.rows, width)
    return parts.transpose(2, 1, 0, 3, 4).reshape(plan.heads, plan.tokens, width)


def gather_tokens(plan, rows):
    moved = lax.all_gather(rows, "head", axis=0, tiled=False)
    return in_sequence(plan, moved, rows.shape[-1])


def scatter_tokens(plan, rows):
    width = rows.shape[-1]
    return lax.psum_scatter(
        by_owner(plan, rows.astype(BF16), width), "head", scatter_dimension=0, tiled=False
    ).astype(F32)


def heads_to_tokens(plan, rows):
    part = rows.shape[-1]
    moved = lax.all_to_all(
        by_owner(plan, rows, part), "head", split_axis=0, concat_axis=0, tiled=True
    )
    return moved.transpose(1, 0, 2).reshape(plan.tokens, plan.heads * part)


def tokens_to_heads(plan, rows):
    part = rows.shape[-1] // plan.heads
    sent = rows.reshape(plan.tokens, plan.heads, part).transpose(1, 0, 2)
    moved = lax.all_to_all(sent, "head", split_axis=0, concat_axis=0, tiled=True)
    return in_sequence(plan, moved, part)


def gather_qkv(rows):
    own, width = rows.shape
    heads = lax.axis_size("head")
    part = width // 3 // heads
    sent = rows.reshape(own, 3, heads, part).transpose(2, 0, 1, 3).reshape(heads, own, 3 * part)
    moved = lax.all_to_all(sent, "head", split_axis=0, concat_axis=0, tiled=True)
    full = lax.all_gather(moved, REST, axis=0, tiled=True)
    return full.reshape(-1, 3 * part)


def scatter_qkv(grad):
    heads = lax.axis_size("head")
    part = grad.shape[1] // 3
    summed = lax.psum_scatter(grad.astype(BF16), REST, scatter_dimension=0, tiled=True)
    own = summed.shape[0] // heads
    moved = lax.all_to_all(
        summed.reshape(heads, own, 3 * part), "head", split_axis=0, concat_axis=0, tiled=True
    )
    return (
        moved.reshape(heads, own, 3, part)
        .transpose(1, 2, 0, 3)
        .reshape(own, 3 * heads * part)
        .astype(F32)
    )


def window_mask(plan, segments, block_index):
    key_count = plan.length + plan.reach * plan.block
    if plan.whole:
        query_segs, key_segs = segments, segments
    else:
        leading = jnp.full((plan.own_seqs, plan.reach * plan.block), -1, jnp.int32)
        padded = jnp.concatenate([leading, segments], axis=1)
        start = block_index * plan.block
        query_segs = lax.dynamic_slice_in_dim(segments, start, plan.block, 1)
        key_segs = lax.dynamic_slice_in_dim(padded, start, key_count, 1)
    query_place = jnp.arange(plan.length, dtype=jnp.int32)[:, None] + plan.reach * plan.block
    key_place = jnp.arange(key_count, dtype=jnp.int32)[None, :]
    near = (key_place <= query_place) & (query_place - key_place < WINDOW)
    return (key_segs[:, None, :] == query_segs[:, :, None]) & near[None]


def with_earlier(plan, own):
    arrived = [own]
    for _ in range(plan.reach):
        arrived.append(shifted(arrived[-1], "blk", 1))
    return jnp.concatenate(arrived[::-1], axis=1) if plan.reach else own


def to_earlier(plan, grads):
    if not plan.reach:
        return grads
    block = plan.block
    total = grads[:, :block]
    for step in range(1, plan.reach + 1):
        total = (
            shifted(total.astype(BF16), "blk", -1).astype(F32)
            + grads[:, step * block : (step + 1) * block]
        )
    return total


def scores_of(queries, keys, allowed):
    scores = jnp.einsum("sqhd,skhd->shqk", queries, keys, preferred_element_type=F32)
    return jnp.where(allowed[:, None], scores, MASKED_SCORE)


def attend(queries, keys, values, allowed):
    scores = scores_of(queries, keys, allowed)
    top_score = jnp.max(scores, axis=-1, keepdims=True)
    exp_terms = jnp.exp(scores - top_score)
    totals = jnp.sum(exp_terms, axis=-1, keepdims=True)
    probs_low = (exp_terms / totals).astype(BF16)
    attended = jnp.einsum("shqk,skhd->sqhd", probs_low, values, preferred_element_type=F32)
    return attended, top_score + jnp.log(totals)


def attend_back(queries, keys, values, allowed, log_total, attended_grad):
    probs = jnp.exp(scores_of(queries, keys, allowed) - log_total)
    probs_low = probs.astype(BF16)
    values_grad = jnp.einsum(
        "shqk,sqhd->skhd", probs_low, attended_grad, preferred_element_type=F32
    )
    probs_grad = jnp.einsum("sqhd,skhd->shqk", attended_grad, values, preferred_element_type=F32)
    row_dot = jnp.sum(probs_grad * probs, axis=-1, keepdims=True)
    scores_low = (probs * (probs_grad - row_dot)).astype(BF16)
    queries_grad = jnp.einsum("shqk,skhd->sqhd", scores_low, keys, preferred_element_type=F32)
    keys_grad = jnp.einsum("shqk,sqhd->skhd", scores_low, queries, preferred_element_type=F32)
    return queries_grad, keys_grad, values_grad


def forward(plan, stream, qkv, dense, gains, scale_vec, allowed):
    width = plan.width
    head_dim = scale_vec.shape[0]
    part = qkv.shape[1] // 3
    local_heads = part // head_dim
    split = (plan.own_seqs, plan.length, local_heads, head_dim)
    out_w, up_w, down_w = dense[:, :width], dense[:, width:-width], dense[:, -width:]
    normed, factor_one = normalize(stream, gains[0])
    normed_all = gather_tokens(plan, normed.astype(BF16))
    projected = dot(normed_all, qkv)
    query_pre = projected[:, :part].reshape(split)
    queries = (query_pre * scale_vec).astype(BF16)
    keys = with_earlier(plan, projected[:, part : 2 * part].astype(BF16).reshape(split))
    values = with_earlier(plan, projected[:, 2 * part :].astype(BF16).reshape(split))
    attended_part, log_total = attend(queries, keys, values, allowed)
    attended = heads_to_tokens(plan, attended_part.astype(BF16).reshape(-1, part))
    middle = stream + dot(attended, out_w)
    normed_two, factor_two = normalize(middle, gains[1])
    normed_two = normed_two.astype(BF16)
    hidden = dot(normed_two, up_w)
    active = (hidden * jax.nn.sigmoid(hidden)).astype(BF16)
    result = middle + dot(active, down_w)
    kept = (
        stream, factor_one, normed_all, query_pre, queries, keys, values, log_total,
        attended, middle, factor_two, normed_two, hidden, active,
    )
    return result, kept


def backward(plan, upper, kept, qkv, dense, gains, scale_vec, allowed):
    (
        stream, factor_one, normed_all, query_pre, queries, keys, values, log_total,
        attended, middle, factor_two, normed_two, hidden, active,
    ) = kept
    width = plan.width
    head_dim = scale_vec.shape[0]
    part = qkv.shape[1] // 3
    out_w, up_w, down_w = dense[:, :width], dense[:, width:-width], dense[:, -width:]
    upper_low = upper.astype(BF16)
    down_grad = dot_rows(active, upper_low)
    active_grad = dot_cols(upper_low, down_w)
    gate = jax.nn.sigmoid(hidden)
    hidden_low = (active_grad * gate * (1.0 + hidden * (1.0 - gate))).astype(BF16)
    up_grad = dot_rows(normed_two, hidden_low)
    extra_two, mlp_gain_grad = norm_back(dot_cols(hidden_low, up_w), middle, factor_two, gains[1])
    middle_grad = upper + extra_two
    middle_low = middle_grad.astype(BF16)
    out_grad = dot_rows(attended, middle_low)
    dense_grad = jnp.concatenate([out_grad, up_grad, down_grad], axis=1).astype(BF16)
    dense_own = lax.psum_scatter(dense_grad, ALL, scatter_dimension=0, tiled=True)
    attended_grad = tokens_to_heads(plan, dot_cols(middle_low, out_w).astype(BF16))
    queries_grad, keys_grad, values_grad = attend_back(
        queries, keys, values, allowed, log_total, attended_grad.reshape(queries.shape)
    )
    query_bar = queries_grad.astype(BF16).astype(F32)
    scale_vec_grad = jnp.sum((query_bar * query_pre).reshape(-1, head_dim), axis=0)
    query_low = (query_bar * scale_vec).astype(BF16).reshape(-1, part)
    keys_low = to_earlier(plan, keys_grad).astype(BF16).reshape(-1, part)
    values_low = to_earlier(plan, values_grad).astype(BF16).reshape(-1, part)
    projected_low = jnp.concatenate([query_low, keys_low, values_low], axis=1)
    normed_grad = scatter_tokens(plan, dot_cols(projected_low, qkv))
    qkv_own = scatter_qkv(dot_rows(normed_all, projected_low))
    extra_one, attn_gain_grad = norm_back(normed_grad, stream, factor_one, gains[0])
    lower = middle_grad + extra_one
    return lower, qkv_own, dense_own, (attn_gain_grad, mlp_gain_grad), scale_vec_grad


def general_device(
    tokens,
    segments,
    qkv_weight,
    out_weight,
    up_weight,
    down_weight,
    attn_gain,
    mlp_gain,
    scale_param,
    cotangent,
):
    plan = Plan(tokens)
    layers, head_dim = scale_param.shape
    block_index = lax.axis_index("blk")
    scale_vecs = SCALE_BASE / math.sqrt(head_dim) * jax.nn.softplus(scale_param)
    own_gains = jnp.concatenate([attn_gain, mlp_gain], axis=0)
    gains = (
        lax.all_gather(own_gains.reshape(1, -1), ALL, axis=0, tiled=True)
        .reshape(-1, 2 * layers, attn_gain.shape[1])
        .transpose(1, 0, 2)
        .reshape(2 * layers, plan.width)
        .astype(F32)
    )
    if plan.whole:
        segments = lax.dynamic_slice_in_dim(
            segments, block_index * plan.own_seqs, plan.own_seqs, 0
        )
    allowed = window_mask(plan, segments, block_index)
    stream = to_plan(plan, tokens).astype(F32)
    qkvs, denses, kept = [], [], []
    for layer in range(layers):
        qkvs.append(gather_qkv(qkv_weight[layer]))
        own = jnp.concatenate([out_weight[layer], up_weight[layer], down_weight[layer]], axis=1)
        denses.append(lax.all_gather(own, ALL, axis=0, tiled=True))
        layer_gains = (gains[layer], gains[layers + layer])
        stream, saved = forward(
            plan, stream, qkvs[layer], denses[layer], layer_gains, scale_vecs[layer], allowed
        )
        kept.append(saved)
    layer_out = from_plan(plan, stream.astype(BF16))
    upper = to_plan(plan, cotangent).astype(F32)
    qkv_grads, dense_grads = [None] * layers, [None] * layers
    gain_grads, scale_grads = [None] * layers, [None] * layers
    for layer in reversed(range(layers)):
        layer_gains = (gains[layer], gains[layers + layer])
        upper, qkv_grads[layer], dense_grads[layer], gain_grads[layer], scale_grads[layer] = (
            backward(
                plan, upper, kept[layer], qkvs[layer], denses[layer], layer_gains,
                scale_vecs[layer], allowed,
            )
        )
    input_grad = from_plan(plan, upper.astype(BF16)).astype(F32)
    small = jnp.concatenate(
        [g[0] for g in gain_grads] + [g[1] for g in gain_grads] + scale_grads, axis=0
    )
    total = lax.psum(small, ALL)
    gain_total = total[: 2 * layers * plan.width].reshape(2 * layers, plan.width)
    owner = lax.axis_index(ALL)
    gain_rows = attn_gain.shape[1]
    own_total = lax.dynamic_slice_in_dim(gain_total, owner * gain_rows, gain_rows, 1)
    scale_total = total[2 * layers * plan.width :].reshape(layers, head_dim)
    scale_grad = scale_total * (SCALE_BASE / math.sqrt(head_dim)) * jax.nn.sigmoid(scale_param)
    dense_all = jnp.stack(dense_grads).astype(F32)
    width = plan.width
    return (
        layer_out,
        input_grad,
        jnp.stack(qkv_grads),
        dense_all[:, :, :width],
        dense_all[:, :, width:-width],
        dense_all[:, :, -width:],
        own_total[:layers],
        own_total[layers:],
        scale_grad,
    )


Q_ROWS = 256
KERNEL = pltpu.CompilerParams(vmem_limit_bytes=32 * 1024 * 1024)
LIGHT = pl.CostEstimate(flops=1 << 20, bytes_accessed=1 << 20, transcendentals=0)


def allowed_keys(col, row, first):
    count = first + row.shape[1]
    key_place = lax.broadcasted_iota(jnp.int32, (count, row.shape[1]), 0)
    query_place = lax.broadcasted_iota(jnp.int32, (count, row.shape[1]), 1) + first
    return (col[:count] == row) & (key_place <= query_place)


def token_places(length, heads, token_rows):
    for first in range(0, length, Q_ROWS):
        parts = []
        for start in range(0, Q_ROWS, token_rows):
            place = (first + start) // token_rows
            parts.append((start, place % heads, place // heads * token_rows))
        yield first, parts


def attend_kernel(token_rows, proj_ref, scale_ref, col_ref, row_ref, out_ref, lse_ref):
    length = proj_ref.shape[-1]
    queries = (proj_ref[0, 0] * scale_ref[...]).astype(BF16)
    keys = proj_ref[1, 0].T.astype(BF16)
    values = proj_ref[2, 0].astype(BF16)
    for first, parts in token_places(length, out_ref.shape[0], token_rows):
        end = first + Q_ROWS
        scores = jnp.dot(keys[:end], queries[:, first:end], preferred_element_type=F32)
        allowed = allowed_keys(col_ref[...], row_ref[:, first:end], first)
        scores = jnp.where(allowed, scores, MASKED_SCORE)
        top = jnp.max(scores, axis=0, keepdims=True)
        terms = jnp.exp(scores - top)
        total = jnp.sum(terms, axis=0, keepdims=True)
        probs = (terms * (1.0 / total)).astype(BF16)
        attended = jnp.dot(values[:, :end], probs, preferred_element_type=F32).astype(BF16)
        lse_ref[0, :, first:end] = top + jnp.log(total)
        for start, owner, offset in parts:
            out_ref[owner, 0, :, offset : offset + token_rows] = attended[
                :, start : start + token_rows
            ]


def attend_rows(projected, scale_vec, segments, owners, token_rows):
    head_dim = scale_vec.shape[0]
    length = projected.shape[1]
    local_heads = projected.shape[0] // 3 // head_dim
    tokens = length // owners
    attended, log_total = pl.pallas_call(
        functools.partial(attend_kernel, token_rows),
        grid=(local_heads,),
        in_specs=[
            pl.BlockSpec((3, 1, head_dim, length), lambda h: (0, h, 0, 0)),
            pl.BlockSpec((head_dim, 1), lambda h: (0, 0)),
            pl.BlockSpec((length, 1), lambda h: (0, 0)),
            pl.BlockSpec((1, length), lambda h: (0, 0)),
        ],
        out_specs=[
            pl.BlockSpec((owners, 1, head_dim, tokens), lambda h: (0, h, 0, 0)),
            pl.BlockSpec((1, 1, length), lambda h: (h, 0, 0)),
        ],
        out_shape=[
            jax.ShapeDtypeStruct((owners, local_heads, head_dim, tokens), BF16),
            jax.ShapeDtypeStruct((local_heads, 1, length), F32),
        ],
        compiler_params=KERNEL,
        cost_estimate=LIGHT,
    )(
        projected.reshape(3, local_heads, head_dim, length),
        scale_vec.reshape(head_dim, 1),
        segments.reshape(length, 1),
        segments.reshape(1, length),
    )
    return attended.reshape(owners, local_heads * head_dim, tokens), log_total


def attend_back_kernel(
    token_rows,
    proj_ref,
    grad_ref,
    lse_ref,
    scale_ref,
    col_ref,
    row_ref,
    out_ref,
    scale_grad_ref,
    keys_acc,
    values_acc,
):
    length = proj_ref.shape[-1]
    scale = scale_ref[...]
    query_pre = proj_ref[0, 0]
    queries = (query_pre * scale).astype(BF16)
    keys_t = proj_ref[1, 0].astype(BF16)
    keys = proj_ref[1, 0].T.astype(BF16)
    values = proj_ref[2, 0].T.astype(BF16)
    keys_acc[...] = jnp.zeros_like(keys_acc)
    values_acc[...] = jnp.zeros_like(values_acc)
    scale_grad = jnp.zeros((scale.shape[0], 1), F32)
    for first, parts in token_places(length, grad_ref.shape[0], token_rows):
        end = first + Q_ROWS
        block = queries[:, first:end]
        grad = jnp.concatenate(
            [grad_ref[owner, 0, :, at : at + token_rows] for _, owner, at in parts], axis=1
        )
        scores = jnp.dot(keys[:end], block, preferred_element_type=F32)
        allowed = allowed_keys(col_ref[...], row_ref[:, first:end], first)
        scores = jnp.where(allowed, scores, MASKED_SCORE)
        probs = jnp.exp(scores - lse_ref[0, :, first:end])
        probs_grad = jnp.dot(values[:end], grad, preferred_element_type=F32)
        row_dot = jnp.sum(probs_grad * probs, axis=0, keepdims=True)
        scores_low = (probs * (probs_grad - row_dot)).astype(BF16)
        values_acc[:, :end] += lax.dot_general(
            grad, probs.astype(BF16), NT, preferred_element_type=F32
        )
        keys_acc[:, :end] += lax.dot_general(
            block, scores_low, NT, preferred_element_type=F32
        )
        query_bar = jnp.dot(keys_t[:, :end], scores_low, preferred_element_type=F32)
        query_bar = query_bar.astype(BF16).astype(F32)
        scale_grad += jnp.sum(query_bar * query_pre[:, first:end], axis=1, keepdims=True)
        out_ref[0, 0, :, first:end] = (query_bar * scale).astype(BF16)
    out_ref[1, 0] = keys_acc[...].astype(BF16)
    out_ref[2, 0] = values_acc[...].astype(BF16)
    spread = jnp.broadcast_to(scale_grad, scale_grad_ref.shape)

    @pl.when(pl.program_id(0) == 0)
    def _():
        scale_grad_ref[...] = spread

    @pl.when(pl.program_id(0) > 0)
    def _():
        scale_grad_ref[...] += spread


def attend_back_rows(projected, attended_grad, log_total, scale_vec, segments, token_rows):
    head_dim = scale_vec.shape[0]
    length = projected.shape[1]
    local_heads = projected.shape[0] // 3 // head_dim
    owners, _, tokens = attended_grad.shape
    lanes = 128
    grads, scale_grad = pl.pallas_call(
        functools.partial(attend_back_kernel, token_rows),
        grid=(local_heads,),
        in_specs=[
            pl.BlockSpec((3, 1, head_dim, length), lambda h: (0, h, 0, 0)),
            pl.BlockSpec((owners, 1, head_dim, tokens), lambda h: (0, h, 0, 0)),
            pl.BlockSpec((1, 1, length), lambda h: (h, 0, 0)),
            pl.BlockSpec((head_dim, 1), lambda h: (0, 0)),
            pl.BlockSpec((length, 1), lambda h: (0, 0)),
            pl.BlockSpec((1, length), lambda h: (0, 0)),
        ],
        out_specs=[
            pl.BlockSpec((3, 1, head_dim, length), lambda h: (0, h, 0, 0)),
            pl.BlockSpec((head_dim, lanes), lambda h: (0, 0)),
        ],
        out_shape=[
            jax.ShapeDtypeStruct((3, local_heads, head_dim, length), BF16),
            jax.ShapeDtypeStruct((head_dim, lanes), F32),
        ],
        scratch_shapes=[
            pltpu.VMEM((head_dim, length), F32),
            pltpu.VMEM((head_dim, length), F32),
        ],
        compiler_params=KERNEL,
        cost_estimate=LIGHT,
    )(
        projected.reshape(3, local_heads, head_dim, length),
        attended_grad.reshape(owners, local_heads, head_dim, tokens),
        log_total,
        scale_vec.reshape(head_dim, 1),
        segments.reshape(length, 1),
        segments.reshape(1, length),
    )
    return grads.reshape(3 * local_heads * head_dim, length), scale_grad[:, 0]


def dense_grad_kernel(
    core_ref, attended_ref, normed_ref, active_ref, out_bar, up_bar, down_bar,
    own_ref, other_ref, normed_t, active_t,
):
    tile = pl.program_id(0)
    rows, width = own_ref.shape[1] * own_ref.shape[3] * 2, out_bar.shape[1]

    @pl.when(tile == 0)
    def _():
        normed_t[...] = normed_ref[...].astype(F32).T.astype(BF16)
        active_t[...] = active_ref[...].astype(F32).T.astype(BF16)

    start = pl.multiple_of(tile * rows, rows)
    first_core = core_ref[2] == 0
    lefts = (attended_ref, normed_t, active_t)
    for i, (left, right) in enumerate(zip(lefts, (out_bar, up_bar, down_bar))):
        grad = jnp.dot(left[pl.ds(start, rows), :], right[...], preferred_element_type=F32)
        grad = grad.reshape(2, 2, rows // 4, width)
        one, two = grad[:, 0], grad[:, 1]
        own_ref[0, :, 0, :, i * width : (i + 1) * width] = jnp.where(
            first_core, one, two
        ).astype(BF16)
        other_ref[0, :, 0, :, i * width : (i + 1) * width] = jnp.where(
            first_core, two, one
        ).astype(BF16)


def dense_grads(attended_t, normed, active, out_bar, up_bar, down_bar):
    width, tokens = attended_t.shape
    own = width // 32
    whole = pl.BlockSpec((tokens, width), lambda i, core: (0, 0))
    rows = pl.BlockSpec((1, 2, 1, own, 3 * width), lambda i, core: (i % 2, 0, i // 2, 0, 0))
    shape = jax.ShapeDtypeStruct((2, 2, 4, own, 3 * width), BF16)
    return pl.pallas_call(
        dense_grad_kernel,
        grid_spec=pltpu.PrefetchScalarGridSpec(
            num_scalar_prefetch=1,
            grid=(8,),
            in_specs=[pl.BlockSpec((width, tokens), lambda i, core: (0, 0))] + [whole] * 5,
            out_specs=[rows, rows],
            scratch_shapes=[pltpu.VMEM((width, tokens), BF16)] * 2,
        ),
        out_shape=[shape, shape],
        compiler_params=KERNEL,
        cost_estimate=LIGHT,
    )(place(), attended_t, normed, active, out_bar, up_bar, down_bar)


def place():
    head = lax.axis_index("head")
    return jnp.stack([lax.axis_index("blk"), head // 2, head % 2]).astype(jnp.int32)


def assemble_kernel(place_ref, *refs):
    pieces, whole_ref = refs[:10], refs[10]
    half = whole_ref.shape[-1] // 2
    blk, row, core = place_ref[0], place_ref[1], place_ref[2]
    for i in range(2):
        at_core = core if i == 0 else 1 - core
        own, across, beside, one, two = pieces[5 * i : 5 * i + 5]
        whole_ref[0, blk, row, at_core] = own[0]
        whole_ref[0, 1 - blk, row, at_core] = across[0]
        whole_ref[0, blk, 1 - row, at_core] = beside[0]
        whole_ref[0, 1 - blk, 1 - row, at_core, :, :half] = one[0]
        whole_ref[0, 1 - blk, 1 - row, at_core, :, half:] = two[0]


def assemble(pieces):
    batch, own, columns = pieces[0].shape
    specs = [
        pl.BlockSpec((1, own, piece.shape[-1]), lambda i, at: (i, 0, 0))
        for piece in pieces
    ]
    whole = pl.pallas_call(
        assemble_kernel,
        grid_spec=pltpu.PrefetchScalarGridSpec(
            num_scalar_prefetch=1,
            grid=(batch,),
            in_specs=specs,
            out_specs=pl.BlockSpec((1, 2, 2, 2, own, columns), lambda i, at: (i, 0, 0, 0, 0, 0)),
        ),
        out_shape=jax.ShapeDtypeStruct((batch, 2, 2, 2, own, columns), BF16),
        compiler_params=KERNEL,
        cost_estimate=LIGHT,
    )(place(), *pieces)
    return whole.reshape(-1, columns)


def assemble_columns_kernel(place_ref, along_ref, across_ref, whole_ref, *extra_ref):
    blk = place_ref[0]
    columns = whole_ref.shape[-1]
    whole_ref[0, blk] = along_ref[0, :, :columns]
    whole_ref[0, 1 - blk] = across_ref[0, :, :columns]
    for extra in extra_ref:
        extra[0, blk] = along_ref[0, :, columns:]
        extra[0, 1 - blk] = across_ref[0, :, columns:]


def assemble_columns(along, across, columns):
    batch, own, both = along.shape
    rows = pl.BlockSpec((1, own, both), lambda i, at: (i, 0, 0))
    shapes = [(batch, 2, own, columns)]
    if both > columns:
        shapes.append((batch, 2, own, both - columns))
    parts = pl.pallas_call(
        assemble_columns_kernel,
        grid_spec=pltpu.PrefetchScalarGridSpec(
            num_scalar_prefetch=1,
            grid=(batch,),
            in_specs=[rows, rows],
            out_specs=[pl.BlockSpec((1,) + s[1:], lambda i, at: (i, 0, 0, 0)) for s in shapes],
        ),
        out_shape=[jax.ShapeDtypeStruct(s, BF16) for s in shapes],
        compiler_params=KERNEL,
        cost_estimate=LIGHT,
    )(place(), along, across)
    return [part.reshape(-1, part.shape[-1]) for part in parts]


def project_kernel(with_norm, place_ref, *refs):
    pieces, (gain_ref, weight_ref, normed_ref, projected_ref) = refs[:4], refs[4:]
    head = place_ref[1] * 2 + place_ref[2]
    rows = pieces[0].shape[0]
    for i, piece in enumerate(pieces):
        value = piece[...]
        if with_norm:
            stream = value.astype(F32)
            factor = lax.rsqrt(jnp.mean(stream * stream, axis=-1, keepdims=True) + EPSILON)
            value = (stream * factor * gain_ref[...]).astype(BF16)
        normed_ref[pl.ds(pl.multiple_of((head ^ i) * rows, rows), rows), :] = value
    projected = jnp.dot(normed_ref[...], weight_ref[...], preferred_element_type=F32)
    projected_ref[...] = projected.T


def project(pieces, gain, weight, with_norm, token_rows):
    tokens, width = pieces[0].shape
    length, columns = 4 * tokens, weight.shape[1]
    groups = tokens // token_rows
    piece = pl.BlockSpec((token_rows, width), lambda g, at: (g, 0))
    return pl.pallas_call(
        functools.partial(project_kernel, with_norm),
        grid_spec=pltpu.PrefetchScalarGridSpec(
            num_scalar_prefetch=1,
            grid=(groups,),
            in_specs=[piece] * 4
            + [
                pl.BlockSpec((1, width), lambda g, at: (0, 0)),
                pl.BlockSpec((width, columns), lambda g, at: (0, 0)),
            ],
            out_specs=[
                pl.BlockSpec((4 * token_rows, width), lambda g, at: (g, 0)),
                pl.BlockSpec((columns, 4 * token_rows), lambda g, at: (0, g)),
            ],
        ),
        out_shape=[
            jax.ShapeDtypeStruct((length, width), BF16),
            jax.ShapeDtypeStruct((columns, length), F32),
        ],
        compiler_params=KERNEL,
        cost_estimate=LIGHT,
    )(place(), *pieces, gain.reshape(1, width), weight)


def project_back_kernel(
    place_ref, bars_ref, weight_ref, normed_ref, own_ref, other_ref, grad_ref, bars_t
):
    @pl.when(pl.program_id(0) == 0)
    def _():
        bars_t[...] = bars_ref[...].astype(F32).T.astype(BF16)

    upper = lax.dot_general(bars_t[...], weight_ref[...], NT, preferred_element_type=F32)
    upper = upper.reshape(2, 2, 2, -1, upper.shape[-1])
    first_core = place_ref[2] == 0
    one, two = upper[:, :, 0], upper[:, :, 1]
    own_ref[...] = jnp.where(first_core, one, two)
    other_ref[...] = jnp.where(first_core, two, one).astype(BF16)
    grad = lax.dot_general(normed_ref[...], bars_t[...], TN, preferred_element_type=F32)
    grad_ref[...] = grad.astype(BF16)


def project_back(bars, weight, normed, token_rows):
    columns, length = bars.shape
    width = weight.shape[0]
    tile = width // 2
    quarter = pl.BlockSpec((2, 2, token_rows, tile), lambda i, at: (0, 0, 0, i))
    return pl.pallas_call(
        project_back_kernel,
        grid_spec=pltpu.PrefetchScalarGridSpec(
            num_scalar_prefetch=1,
            grid=(2,),
            in_specs=[
                pl.BlockSpec((columns, length), lambda i, at: (0, 0)),
                pl.BlockSpec((tile, columns), lambda i, at: (i, 0)),
                pl.BlockSpec((length, tile), lambda i, at: (0, i)),
            ],
            out_specs=[quarter, quarter, pl.BlockSpec((tile, columns), lambda i, at: (i, 0))],
            scratch_shapes=[pltpu.VMEM((length, columns), BF16)],
        ),
        out_shape=[
            jax.ShapeDtypeStruct((2, 2, token_rows, width), F32),
            jax.ShapeDtypeStruct((2, 2, token_rows, width), BF16),
            jax.ShapeDtypeStruct((width, columns), BF16),
        ],
        compiler_params=KERNEL,
        cost_estimate=LIGHT,
    )(place(), bars, weight, normed)


def tied(*arrays):
    return lax.optimization_barrier(arrays)


def swapped(array, axis, mask):
    size = lax.axis_size(axis)
    return lax.ppermute(array, axis, [(i, i ^ mask) for i in range(size)])


def pick(array, index, axis=0):
    return lax.dynamic_index_in_dim(array, index, axis, keepdims=False)


def swap_halves(array):
    me = lax.axis_index("blk")
    got = swapped(pick(array, 1 - me), "blk", 1)
    kept = pick(array, me)
    return jnp.stack([jnp.where(me == 0, kept, got), jnp.where(me == 0, got, kept)])


def scatter_row(halves):
    row = lax.axis_index("head") // 2
    got = swapped(pick(halves, 1 - row, 1).astype(BF16), "head", 2).astype(F32)
    return (pick(halves, row, 1) + got).reshape(-1, halves.shape[-1])


def over_head(parts):
    return lax.all_to_all(parts, "head", split_axis=0, concat_axis=0, tiled=True)


def qkv_columns(rows, extra):
    own, width = rows.shape
    part = width // 3 // 4
    sent = rows.reshape(own, 3, 4, part).transpose(2, 0, 1, 3).reshape(4, own, 3 * part)
    if extra is not None:
        sent = jnp.concatenate([sent, jnp.broadcast_to(extra[None], (4,) + extra.shape)], axis=2)
    return over_head(sent)


def along_batch(piece):
    return lax.all_gather(piece, "batch", axis=0, tiled=False)


def other_core(array):
    return swapped(array, "head", 1)


def to_beside(across):
    return swapped(across[..., : across.shape[-1] // 2], "head", 2)


def to_across(beside):
    return swapped(beside[..., beside.shape[-1] // 2 :], "blk", 1)


def over_batch(parts):
    return lax.psum_scatter(parts.astype(BF16), "batch", scatter_dimension=0, tiled=False)


def across_sum(halves):
    blk = lax.axis_index("blk")
    got = swapped(pick(halves, 1 - blk), "blk", 1).astype(F32)
    return (pick(halves, blk).astype(F32) + got).astype(BF16)


def columns_to_rows(summed):
    moved = over_head(summed.reshape(4, -1, summed.shape[-1]))
    rows = moved.shape[1]
    return moved.reshape(4, rows, 3, -1).transpose(1, 2, 0, 3).reshape(rows, -1).astype(F32)


def diagonal_sent(cored):
    blk, row = place()[:2]
    rows = pick(pick(cored, 1 - blk), 1 - row)
    half = rows.shape[-1] // 2
    return swapped(rows[..., :half], "blk", 1), swapped(rows[..., half:], "head", 2)


def neighbours_sent(cored, one, two):
    blk, row = place()[:2]
    half = one.shape[-1]
    across = pick(pick(cored, 1 - blk), row)
    beside = pick(pick(cored, blk), 1 - row)
    across = jnp.concatenate(
        [across[..., :half], across[..., half:].astype(F32) + two.astype(F32)], axis=-1
    ).astype(BF16)
    beside = jnp.concatenate(
        [beside[..., :half].astype(F32) + one.astype(F32), beside[..., half:]], axis=-1
    ).astype(BF16)
    return swapped(across, "blk", 1), swapped(beside, "head", 2)


def own_sum(cored, across, beside):
    blk, row = place()[:2]
    own = pick(pick(cored, blk), row)
    return own.astype(F32) + across.astype(F32) + beside.astype(F32)


def sum_all(array):
    for axis, mask in (("head", 1), ("head", 2), ("blk", 1), ("batch", 1), ("batch", 2)):
        array = array + swapped(array, axis, mask)
    return array


def gain_back(weight, weight_grad, gain):
    return jnp.sum(weight.astype(F32) * weight_grad, axis=-1) / gain.astype(F32)


def lower_of(upper, stream, factor, gain):
    return norm_back(upper, stream, factor, gain)[0]


def spread_device(
    tokens,
    segments,
    qkv_weight,
    out_weight,
    up_weight,
    down_weight,
    attn_gain,
    mlp_gain,
    scale_param,
    cotangent,
):
    layers, head_dim = scale_param.shape
    _, token_rows, width = tokens.shape
    scale_vecs = SCALE_BASE / math.sqrt(head_dim) * jax.nn.softplus(scale_param)
    segments = pick(segments, lax.axis_index("blk"))
    own_gains = jnp.concatenate([attn_gain, mlp_gain], axis=0)

    part3 = 3 * width // 4
    dense_own = [
        jnp.concatenate([out_weight[i], up_weight[i], down_weight[i]], axis=1) for i in (0, 1)
    ]

    first = swap_halves(tokens).reshape(-1, width)
    upper = swap_halves(cotangent).reshape(-1, width)
    dense_near = along_batch(dense_own[0])
    columns = qkv_columns(qkv_weight[0], own_gains.T)
    columns, first, upper = tied(columns.reshape(-1, columns.shape[-1]), first, upper)
    stream, upper = first.astype(F32), upper.astype(F32)
    far, near = swapped(first, "head", 2), other_core(first)
    both = other_core(far)
    columns, dense_near, near, far, both = tied(columns, dense_near, near, far, both)
    token_pieces = (first, near, far, both)
    across, beside = swapped(dense_near, "blk", 1), swapped(dense_near, "head", 2)
    along = along_batch(columns)
    next_columns = qkv_columns(qkv_weight[1], None).reshape(-1, part3)
    along, across, beside, next_columns = tied(along, across, beside, next_columns)
    qkv_across = swapped(along, "blk", 1)
    one = to_beside(across)
    next_along = along_batch(next_columns)
    qkv_across, one, beside, next_along, dense_next = tied(
        qkv_across, one, beside, next_along, dense_own[1]
    )
    two = to_across(beside)
    next_across = swapped(next_along, "blk", 1)
    pieces = [(dense_near, across, beside, one, two)]
    dense_next = along_batch(dense_next)
    weight, gains = assemble_columns(along, qkv_across, part3)
    qkvs = [weight]
    gains = gains.T.astype(F32)

    kept, denses = [], []
    for layer in range(layers):
        normed, factor_one = normalize(stream, gains[layer])
        if layer == 1:
            normed, across, beside = tied(normed.astype(BF16), across, beside)
            far, near = swapped(normed, "head", 2), other_core(normed)
            far, near, across, beside = tied(far, near, across, beside)
            token_pieces = (normed, near, far, other_core(far))
            one, two = to_beside(across), to_across(beside)
            pieces.append((dense_next, across, beside, one, two))
            qkvs.append(assemble_columns(next_along, next_across, part3)[0])
        normed_all, projected = project(
            token_pieces, gains[layer], qkvs[layer], layer == 0, token_rows
        )
        attended, log_total = attend_rows(
            projected, scale_vecs[layer], segments, 4, token_rows
        )
        attended, one, two = tied(attended, *pieces[layer][3:])
        pieces[layer] = pieces[layer][:3] + (one, two)
        swaps = tuple(other_core(piece) for piece in pieces[layer])
        if layer == 0:
            attended, next_across, dense_next = tied(attended, next_across, dense_next)
            across, beside = swapped(dense_next, "blk", 1), swapped(dense_next, "head", 2)
        attended_t, swaps = tied(over_head(attended), swaps)
        attended_t = attended_t.reshape(width, -1)
        denses.append(assemble(pieces[layer] + swaps))
        dense = denses[layer]
        out_w, up_w, down_w = dense[:, :width], dense[:, width:-width], dense[:, -width:]
        middle = stream + dot_rows(attended_t, out_w)
        normed_two, factor_two = normalize(middle, gains[layers + layer])
        normed_two = normed_two.astype(BF16)
        hidden = dot(normed_two, up_w)
        active = (hidden * jax.nn.sigmoid(hidden)).astype(BF16)
        kept.append(
            (
                stream, factor_one, normed_all, projected, log_total, attended_t, middle,
                factor_two, normed_two, hidden, active,
            )
        )
        stream = middle + dot(active, down_w)
    layer_out = swap_halves(stream.astype(BF16).reshape(tokens.shape))

    scale_grads = [None] * layers
    for layer in reversed(range(layers)):
        (
            stream, factor_one, normed_all, projected, log_total, attended_t, middle,
            factor_two, normed_two, hidden, active,
        ) = kept[layer]
        qkv, dense = qkvs[layer], denses[layer]
        out_w, up_w, down_w = dense[:, :width], dense[:, width:-width], dense[:, -width:]
        down_bar = upper.astype(BF16)
        gate = jax.nn.sigmoid(hidden)
        up_bar = (
            dot_cols(down_bar, down_w) * gate * (1.0 + hidden * (1.0 - gate))
        ).astype(BF16)
        middle_grad = upper + lower_of(
            dot_cols(up_bar, up_w), middle, factor_two, gains[layers + layer]
        )
        out_bar = middle_grad.astype(BF16)
        if layer == 0:
            out_bar, diagonal = tied(out_bar, diagonal)
            sent = neighbours_sent(cored, *diagonal)
        attended_grad = over_head(dot_cols(out_w, out_bar).astype(BF16).reshape(4, -1, out_bar.shape[0]))
        grads, others = dense_grads(attended_t, normed_two, active, out_bar, up_bar, down_bar)
        if layer == 0:
            attended_grad, others, z_sum = tied(attended_grad, others, z_sum)
            z_across = across_sum(z_sum)
        else:
            attended_grad, others, layer_out = tied(attended_grad, others, layer_out)
        others = other_core(others)
        bars, scale_grads[layer] = attend_back_rows(
            projected, attended_grad, log_total, scale_vecs[layer], segments, token_rows
        )
        if layer == 0:
            bars, others, sent, z_across = tied(bars, others, sent, z_across)
            summed = own_sum(cored, *sent)
        else:
            bars, others = tied(bars, others)
        cored = (grads.astype(F32) + others.astype(F32)).astype(BF16)
        if layer == 0:
            bars, cored, summed = tied(bars, cored, summed)
            diagonal = diagonal_sent(cored)
            summed = over_batch(summed)
        halves, to_core, qkv_grad = project_back(bars, qkv, normed_all, token_rows)
        halves = halves + other_core(to_core).astype(F32)
        z_sum = over_batch(qkv_grad.reshape(4, 2, -1, qkv_grad.shape[-1]))
        if layer == 0:
            halves, diagonal = tied(halves, diagonal)
            sent = neighbours_sent(cored, *diagonal)
            normed_grad = scatter_row(halves)
            normed_grad, sent, summed = tied(normed_grad, sent, summed)
            dense_grad = [over_batch(own_sum(cored, *sent)), summed]
            qkv_grads = [columns_to_rows(across_sum(z_sum)), columns_to_rows(z_across)]
        else:
            normed_grad = scatter_row(halves)
            normed_grad, cored = tied(normed_grad, cored)
            diagonal = diagonal_sent(cored)
        upper = middle_grad + lower_of(normed_grad, stream, factor_one, gains[layer])
    input_grad = swap_halves(upper.astype(BF16).reshape(tokens.shape)).astype(F32)
    scale_total = sum_all(jnp.stack(scale_grads))
    scale_grad = scale_total * (SCALE_BASE / math.sqrt(head_dim)) * jax.nn.sigmoid(scale_param)
    dense_all = jnp.stack([part.astype(F32) for part in dense_grad])
    qkv_all = jnp.stack(qkv_grads)
    up_all = dense_all[:, :, width:-width]
    return (
        layer_out,
        input_grad,
        qkv_all,
        dense_all[:, :, :width],
        up_all,
        dense_all[:, :, -width:],
        gain_back(qkv_weight, qkv_all, attn_gain),
        gain_back(up_weight, up_all, mlp_gain),
        scale_grad,
    )


def per_device(*args):
    tokens, segments = args[0], args[1]
    sizes = tuple(lax.axis_size(axis) for axis in ALL)
    heads = tokens.shape[2] // args[8].shape[1]
    spread = (
        sizes == (4, 2, 4)
        and tokens.shape[0] == 2
        and args[2].shape[0] == 2
        and tokens.shape[1] % 128 == 0
        and Q_ROWS % tokens.shape[1] == 0
        and segments.shape[1] <= WINDOW
        and segments.shape[1] % Q_ROWS == 0
        and heads % 4 == 0
        and tokens.shape[2] % 256 == 0
    )
    return spread_device(*args) if spread else general_device(*args)


def solution(mesh):
    rows = P(None, ALL, None)
    by_token = P("batch", ("blk", "head"), None)
    return jax.shard_map(
        per_device,
        mesh=mesh,
        in_specs=(
            by_token, P("batch", None), rows, rows, rows, rows, P(None, ALL), P(None, ALL), P(),
            by_token,
        ),
        out_specs=(
            by_token, by_token, rows, rows, rows, rows, P(None, ALL), P(None, ALL), P(),
        ),
        check_vma=False,
    )
```

```python
import functools
import math

import jax
import jax.numpy as jnp
from jax import lax
from jax.experimental import pallas as pl
from jax.experimental.pallas import tpu as pltpu
from jax.sharding import PartitionSpec as P

WINDOW = 1024
EPSILON = 1e-06
SCALE_BASE = 1.4426950408889634
MASKED_SCORE = -1e30

ALL = ("batch", "blk", "head")
REST = ("batch", "blk")
F32 = jnp.float32
BF16 = jnp.bfloat16


def shifted(block, axis, distance):
    devices = range(lax.axis_size(axis))
    route = [(i - distance, i) for i in devices if i - distance in devices]
    return lax.ppermute(block, axis, route)


NT = (((1,), (1,)), ((), ()))
TN = (((0,), (0,)), ((), ()))


def dot(left, right):
    return jnp.dot(left, right, preferred_element_type=F32)


def dot_rows(left, right):
    return lax.dot_general(left, right, (((0,), (0,)), ((), ())), preferred_element_type=F32)


def dot_cols(left, right):
    return lax.dot_general(left, right, (((1,), (1,)), ((), ())), preferred_element_type=F32)


def normalize(stream, gain):
    factor = lax.rsqrt(jnp.mean(stream * stream, axis=-1, keepdims=True) + EPSILON)
    return stream * factor * gain, factor


def norm_back(upper, stream, factor, gain):
    inner = upper * gain
    gain_grad = jnp.sum(upper * stream * factor, axis=0)
    lower = factor * inner - stream * factor * factor * factor * jnp.mean(
        inner * stream, axis=-1, keepdims=True
    )
    return lower, gain_grad


class Plan:
    def __init__(self, tokens):
        self.seqs, self.rows, self.width = tokens.shape
        self.heads = lax.axis_size("head")
        self.blks = lax.axis_size("blk")
        self.block = self.rows * self.heads
        self.whole = self.seqs % self.blks == 0
        if self.whole:
            self.groups, self.own_seqs = self.blks, self.seqs // self.blks
            self.reach = 0
        else:
            self.groups, self.own_seqs = 1, self.seqs
            self.reach = min((WINDOW - 1) // self.block + 1, self.blks - 1)
        self.length = self.groups * self.block
        self.tokens = self.seqs * self.rows


def to_plan(plan, array):
    if plan.whole and plan.blks > 1:
        array = lax.all_to_all(array, "blk", split_axis=0, concat_axis=0, tiled=True)
    return array.reshape(plan.tokens, plan.width)


def from_plan(plan, flat):
    array = flat.reshape(plan.seqs, plan.rows, plan.width)
    if plan.whole and plan.blks > 1:
        array = lax.all_to_all(array, "blk", split_axis=0, concat_axis=0, tiled=True)
    return array


def in_sequence(plan, by_head, width):
    parts = by_head.reshape(plan.heads, plan.groups, plan.own_seqs, plan.rows, width)
    return parts.transpose(2, 1, 0, 3, 4).reshape(-1, width)


def by_owner(plan, rows, width):
    parts = rows.reshape(plan.own_seqs, plan.groups, plan.heads, plan.rows, width)
    return parts.transpose(2, 1, 0, 3, 4).reshape(plan.heads, plan.tokens, width)


def gather_tokens(plan, rows):
    moved = lax.all_gather(rows, "head", axis=0, tiled=False)
    return in_sequence(plan, moved, rows.shape[-1])


def scatter_tokens(plan, rows):
    width = rows.shape[-1]
    return lax.psum_scatter(
        by_owner(plan, rows.astype(BF16), width), "head", scatter_dimension=0, tiled=False
    ).astype(F32)


def heads_to_tokens(plan, rows):
    part = rows.shape[-1]
    moved = lax.all_to_all(
        by_owner(plan, rows, part), "head", split_axis=0, concat_axis=0, tiled=True
    )
    return moved.transpose(1, 0, 2).reshape(plan.tokens, plan.heads * part)


def tokens_to_heads(plan, rows):
    part = rows.shape[-1] // plan.heads
    sent = rows.reshape(plan.tokens, plan.heads, part).transpose(1, 0, 2)
    moved = lax.all_to_all(sent, "head", split_axis=0, concat_axis=0, tiled=True)
    return in_sequence(plan, moved, part)


def gather_qkv(rows):
    own, width = rows.shape
    heads = lax.axis_size("head")
    part = width // 3 // heads
    sent = rows.reshape(own, 3, heads, part).transpose(2, 0, 1, 3).reshape(heads, own, 3 * part)
    moved = lax.all_to_all(sent, "head", split_axis=0, concat_axis=0, tiled=True)
    full = lax.all_gather(moved, REST, axis=0, tiled=True)
    return full.reshape(-1, 3 * part)


def scatter_qkv(grad):
    heads = lax.axis_size("head")
    part = grad.shape[1] // 3
    summed = lax.psum_scatter(grad.astype(BF16), REST, scatter_dimension=0, tiled=True)
    own = summed.shape[0] // heads
    moved = lax.all_to_all(
        summed.reshape(heads, own, 3 * part), "head", split_axis=0, concat_axis=0, tiled=True
    )
    return (
        moved.reshape(heads, own, 3, part)
        .transpose(1, 2, 0, 3)
        .reshape(own, 3 * heads * part)
        .astype(F32)
    )


def window_mask(plan, segments, block_index):
    key_count = plan.length + plan.reach * plan.block
    if plan.whole:
        query_segs, key_segs = segments, segments
    else:
        leading = jnp.full((plan.own_seqs, plan.reach * plan.block), -1, jnp.int32)
        padded = jnp.concatenate([leading, segments], axis=1)
        start = block_index * plan.block
        query_segs = lax.dynamic_slice_in_dim(segments, start, plan.block, 1)
        key_segs = lax.dynamic_slice_in_dim(padded, start, key_count, 1)
    query_place = jnp.arange(plan.length, dtype=jnp.int32)[:, None] + plan.reach * plan.block
    key_place = jnp.arange(key_count, dtype=jnp.int32)[None, :]
    near = (key_place <= query_place) & (query_place - key_place < WINDOW)
    return (key_segs[:, None, :] == query_segs[:, :, None]) & near[None]


def with_earlier(plan, own):
    arrived = [own]
    for _ in range(plan.reach):
        arrived.append(shifted(arrived[-1], "blk", 1))
    return jnp.concatenate(arrived[::-1], axis=1) if plan.reach else own


def to_earlier(plan, grads):
    if not plan.reach:
        return grads
    block = plan.block
    total = grads[:, :block]
    for step in range(1, plan.reach + 1):
        total = (
            shifted(total.astype(BF16), "blk", -1).astype(F32)
            + grads[:, step * block : (step + 1) * block]
        )
    return total


def scores_of(queries, keys, allowed):
    scores = jnp.einsum("sqhd,skhd->shqk", queries, keys, preferred_element_type=F32)
    return jnp.where(allowed[:, None], scores, MASKED_SCORE)


def attend(queries, keys, values, allowed):
    scores = scores_of(queries, keys, allowed)
    top_score = jnp.max(scores, axis=-1, keepdims=True)
    exp_terms = jnp.exp(scores - top_score)
    totals = jnp.sum(exp_terms, axis=-1, keepdims=True)
    probs_low = (exp_terms / totals).astype(BF16)
    attended = jnp.einsum("shqk,skhd->sqhd", probs_low, values, preferred_element_type=F32)
    return attended, top_score + jnp.log(totals)


def attend_back(queries, keys, values, allowed, log_total, attended_grad):
    probs = jnp.exp(scores_of(queries, keys, allowed) - log_total)
    probs_low = probs.astype(BF16)
    values_grad = jnp.einsum(
        "shqk,sqhd->skhd", probs_low, attended_grad, preferred_element_type=F32
    )
    probs_grad = jnp.einsum("sqhd,skhd->shqk", attended_grad, values, preferred_element_type=F32)
    row_dot = jnp.sum(probs_grad * probs, axis=-1, keepdims=True)
    scores_low = (probs * (probs_grad - row_dot)).astype(BF16)
    queries_grad = jnp.einsum("shqk,skhd->sqhd", scores_low, keys, preferred_element_type=F32)
    keys_grad = jnp.einsum("shqk,sqhd->skhd", scores_low, queries, preferred_element_type=F32)
    return queries_grad, keys_grad, values_grad


def forward(plan, stream, qkv, dense, gains, scale_vec, allowed):
    width = plan.width
    head_dim = scale_vec.shape[0]
    part = qkv.shape[1] // 3
    local_heads = part // head_dim
    split = (plan.own_seqs, plan.length, local_heads, head_dim)
    out_w, up_w, down_w = dense[:, :width], dense[:, width:-width], dense[:, -width:]
    normed, factor_one = normalize(stream, gains[0])
    normed_all = gather_tokens(plan, normed.astype(BF16))
    projected = dot(normed_all, qkv)
    query_pre = projected[:, :part].reshape(split)
    queries = (query_pre * scale_vec).astype(BF16)
    keys = with_earlier(plan, projected[:, part : 2 * part].astype(BF16).reshape(split))
    values = with_earlier(plan, projected[:, 2 * part :].astype(BF16).reshape(split))
    attended_part, log_total = attend(queries, keys, values, allowed)
    attended = heads_to_tokens(plan, attended_part.astype(BF16).reshape(-1, part))
    middle = stream + dot(attended, out_w)
    normed_two, factor_two = normalize(middle, gains[1])
    normed_two = normed_two.astype(BF16)
    hidden = dot(normed_two, up_w)
    active = (hidden * jax.nn.sigmoid(hidden)).astype(BF16)
    result = middle + dot(active, down_w)
    kept = (
        stream, factor_one, normed_all, query_pre, queries, keys, values, log_total,
        attended, middle, factor_two, normed_two, hidden, active,
    )
    return result, kept


def backward(plan, upper, kept, qkv, dense, gains, scale_vec, allowed):
    (
        stream, factor_one, normed_all, query_pre, queries, keys, values, log_total,
        attended, middle, factor_two, normed_two, hidden, active,
    ) = kept
    width = plan.width
    head_dim = scale_vec.shape[0]
    part = qkv.shape[1] // 3
    out_w, up_w, down_w = dense[:, :width], dense[:, width:-width], dense[:, -width:]
    upper_low = upper.astype(BF16)
    down_grad = dot_rows(active, upper_low)
    active_grad = dot_cols(upper_low, down_w)
    gate = jax.nn.sigmoid(hidden)
    hidden_low = (active_grad * gate * (1.0 + hidden * (1.0 - gate))).astype(BF16)
    up_grad = dot_rows(normed_two, hidden_low)
    extra_two, mlp_gain_grad = norm_back(dot_cols(hidden_low, up_w), middle, factor_two, gains[1])
    middle_grad = upper + extra_two
    middle_low = middle_grad.astype(BF16)
    out_grad = dot_rows(attended, middle_low)
    dense_grad = jnp.concatenate([out_grad, up_grad, down_grad], axis=1).astype(BF16)
    dense_own = lax.psum_scatter(dense_grad, ALL, scatter_dimension=0, tiled=True)
    attended_grad = tokens_to_heads(plan, dot_cols(middle_low, out_w).astype(BF16))
    queries_grad, keys_grad, values_grad = attend_back(
        queries, keys, values, allowed, log_total, attended_grad.reshape(queries.shape)
    )
    query_bar = queries_grad.astype(BF16).astype(F32)
    scale_vec_grad = jnp.sum((query_bar * query_pre).reshape(-1, head_dim), axis=0)
    query_low = (query_bar * scale_vec).astype(BF16).reshape(-1, part)
    keys_low = to_earlier(plan, keys_grad).astype(BF16).reshape(-1, part)
    values_low = to_earlier(plan, values_grad).astype(BF16).reshape(-1, part)
    projected_low = jnp.concatenate([query_low, keys_low, values_low], axis=1)
    normed_grad = scatter_tokens(plan, dot_cols(projected_low, qkv))
    qkv_own = scatter_qkv(dot_rows(normed_all, projected_low))
    extra_one, attn_gain_grad = norm_back(normed_grad, stream, factor_one, gains[0])
    lower = middle_grad + extra_one
    return lower, qkv_own, dense_own, (attn_gain_grad, mlp_gain_grad), scale_vec_grad


def general_device(
    tokens,
    segments,
    qkv_weight,
    out_weight,
    up_weight,
    down_weight,
    attn_gain,
    mlp_gain,
    scale_param,
    cotangent,
):
    plan = Plan(tokens)
    layers, head_dim = scale_param.shape
    block_index = lax.axis_index("blk")
    scale_vecs = SCALE_BASE / math.sqrt(head_dim) * jax.nn.softplus(scale_param)
    own_gains = jnp.concatenate([attn_gain, mlp_gain], axis=0)
    gains = (
        lax.all_gather(own_gains.reshape(1, -1), ALL, axis=0, tiled=True)
        .reshape(-1, 2 * layers, attn_gain.shape[1])
        .transpose(1, 0, 2)
        .reshape(2 * layers, plan.width)
        .astype(F32)
    )
    if plan.whole:
        segments = lax.dynamic_slice_in_dim(
            segments, block_index * plan.own_seqs, plan.own_seqs, 0
        )
    allowed = window_mask(plan, segments, block_index)
    stream = to_plan(plan, tokens).astype(F32)
    qkvs, denses, kept = [], [], []
    for layer in range(layers):
        qkvs.append(gather_qkv(qkv_weight[layer]))
        own = jnp.concatenate([out_weight[layer], up_weight[layer], down_weight[layer]], axis=1)
        denses.append(lax.all_gather(own, ALL, axis=0, tiled=True))
        layer_gains = (gains[layer], gains[layers + layer])
        stream, saved = forward(
            plan, stream, qkvs[layer], denses[layer], layer_gains, scale_vecs[layer], allowed
        )
        kept.append(saved)
    layer_out = from_plan(plan, stream.astype(BF16))
    upper = to_plan(plan, cotangent).astype(F32)
    qkv_grads, dense_grads = [None] * layers, [None] * layers
    gain_grads, scale_grads = [None] * layers, [None] * layers
    for layer in reversed(range(layers)):
        layer_gains = (gains[layer], gains[layers + layer])
        upper, qkv_grads[layer], dense_grads[layer], gain_grads[layer], scale_grads[layer] = (
            backward(
                plan, upper, kept[layer], qkvs[layer], denses[layer], layer_gains,
                scale_vecs[layer], allowed,
            )
        )
    input_grad = from_plan(plan, upper.astype(BF16)).astype(F32)
    small = jnp.concatenate(
        [g[0] for g in gain_grads] + [g[1] for g in gain_grads] + scale_grads, axis=0
    )
    total = lax.psum(small, ALL)
    gain_total = total[: 2 * layers * plan.width].reshape(2 * layers, plan.width)
    owner = lax.axis_index(ALL)
    gain_rows = attn_gain.shape[1]
    own_total = lax.dynamic_slice_in_dim(gain_total, owner * gain_rows, gain_rows, 1)
    scale_total = total[2 * layers * plan.width :].reshape(layers, head_dim)
    scale_grad = scale_total * (SCALE_BASE / math.sqrt(head_dim)) * jax.nn.sigmoid(scale_param)
    dense_all = jnp.stack(dense_grads).astype(F32)
    width = plan.width
    return (
        layer_out,
        input_grad,
        jnp.stack(qkv_grads),
        dense_all[:, :, :width],
        dense_all[:, :, width:-width],
        dense_all[:, :, -width:],
        own_total[:layers],
        own_total[layers:],
        scale_grad,
    )


Q_ROWS = 256
KERNEL = pltpu.CompilerParams(vmem_limit_bytes=32 * 1024 * 1024)
LIGHT = pl.CostEstimate(flops=1 << 20, bytes_accessed=1 << 20, transcendentals=0)


def in_hbm(*arrays):
    return [pltpu.with_memory_space_constraint(array, pltpu.HBM) for array in arrays]


def allowed_keys(col, row, first):
    count = first + row.shape[1]
    key_place = lax.broadcasted_iota(jnp.int32, (count, row.shape[1]), 0)
    query_place = lax.broadcasted_iota(jnp.int32, (count, row.shape[1]), 1) + first
    return (col[:count] == row) & (key_place <= query_place)


def token_places(length, heads, token_rows):
    for first in range(0, length, Q_ROWS):
        parts = []
        for start in range(0, Q_ROWS, token_rows):
            place = (first + start) // token_rows
            parts.append((start, place % heads, place // heads * token_rows))
        yield first, parts


def attend_kernel(token_rows, proj_ref, scale_ref, col_ref, row_ref, out_ref, lse_ref):
    length = proj_ref.shape[-1]
    queries = (proj_ref[0, 0] * scale_ref[...]).astype(BF16)
    keys = proj_ref[1, 0].T.astype(BF16)
    values = proj_ref[2, 0].astype(BF16)
    for first, parts in token_places(length, out_ref.shape[0], token_rows):
        end = first + Q_ROWS
        scores = jnp.dot(keys[:end], queries[:, first:end], preferred_element_type=F32)
        allowed = allowed_keys(col_ref[...], row_ref[:, first:end], first)
        scores = jnp.where(allowed, scores, MASKED_SCORE)
        top = jnp.max(scores, axis=0, keepdims=True)
        terms = jnp.exp(scores - top)
        total = jnp.sum(terms, axis=0, keepdims=True)
        probs = (terms * (1.0 / total)).astype(BF16)
        attended = jnp.dot(values[:, :end], probs, preferred_element_type=F32).astype(BF16)
        lse_ref[0, :, first:end] = top + jnp.log(total)
        for start, owner, offset in parts:
            out_ref[owner, 0, :, offset : offset + token_rows] = attended[
                :, start : start + token_rows
            ]


def attend_rows(projected, scale_vec, segments, owners, token_rows):
    head_dim = scale_vec.shape[0]
    length = projected.shape[1]
    local_heads = projected.shape[0] // 3 // head_dim
    tokens = length // owners
    attended, log_total = pl.pallas_call(
        functools.partial(attend_kernel, token_rows),
        grid=(local_heads,),
        in_specs=[
            pl.BlockSpec((3, 1, head_dim, length), lambda h: (0, h, 0, 0)),
            pl.BlockSpec((head_dim, 1), lambda h: (0, 0)),
            pl.BlockSpec((length, 1), lambda h: (0, 0)),
            pl.BlockSpec((1, length), lambda h: (0, 0)),
        ],
        out_specs=[
            pl.BlockSpec((owners, 1, head_dim, tokens), lambda h: (0, h, 0, 0)),
            pl.BlockSpec((1, 1, length), lambda h: (h, 0, 0)),
        ],
        out_shape=[
            pltpu.HBM((owners, local_heads, head_dim, tokens), BF16),
            pltpu.HBM((local_heads, 1, length), F32),
        ],
        compiler_params=KERNEL,
        cost_estimate=LIGHT,
    )(
        *in_hbm(projected.reshape(3, local_heads, head_dim, length)),
        scale_vec.reshape(head_dim, 1),
        segments.reshape(length, 1),
        segments.reshape(1, length),
    )
    return attended.reshape(owners, local_heads * head_dim, tokens), log_total


def attend_back_kernel(
    token_rows,
    proj_ref,
    grad_ref,
    lse_ref,
    scale_ref,
    col_ref,
    row_ref,
    out_ref,
    scale_grad_ref,
    keys_acc,
    values_acc,
):
    length = proj_ref.shape[-1]
    scale = scale_ref[...]
    query_pre = proj_ref[0, 0]
    queries = (query_pre * scale).astype(BF16)
    keys_t = proj_ref[1, 0].astype(BF16)
    keys = proj_ref[1, 0].T.astype(BF16)
    values = proj_ref[2, 0].T.astype(BF16)
    keys_acc[...] = jnp.zeros_like(keys_acc)
    values_acc[...] = jnp.zeros_like(values_acc)
    scale_grad = jnp.zeros((scale.shape[0], 1), F32)
    for first, parts in token_places(length, grad_ref.shape[0], token_rows):
        end = first + Q_ROWS
        block = queries[:, first:end]
        grad = jnp.concatenate(
            [grad_ref[owner, 0, :, at : at + token_rows] for _, owner, at in parts], axis=1
        )
        scores = jnp.dot(keys[:end], block, preferred_element_type=F32)
        allowed = allowed_keys(col_ref[...], row_ref[:, first:end], first)
        scores = jnp.where(allowed, scores, MASKED_SCORE)
        probs = jnp.exp(scores - lse_ref[0, :, first:end])
        probs_grad = jnp.dot(values[:end], grad, preferred_element_type=F32)
        row_dot = jnp.sum(probs_grad * probs, axis=0, keepdims=True)
        scores_low = (probs * (probs_grad - row_dot)).astype(BF16)
        values_acc[:, :end] += lax.dot_general(
            grad, probs.astype(BF16), NT, preferred_element_type=F32
        )
        keys_acc[:, :end] += lax.dot_general(
            block, scores_low, NT, preferred_element_type=F32
        )
        query_bar = jnp.dot(keys_t[:, :end], scores_low, preferred_element_type=F32)
        query_bar = query_bar.astype(BF16).astype(F32)
        scale_grad += jnp.sum(query_bar * query_pre[:, first:end], axis=1, keepdims=True)
        out_ref[0, 0, :, first:end] = (query_bar * scale).astype(BF16)
    out_ref[1, 0] = keys_acc[...].astype(BF16)
    out_ref[2, 0] = values_acc[...].astype(BF16)
    spread = jnp.broadcast_to(scale_grad, scale_grad_ref.shape)

    @pl.when(pl.program_id(0) == 0)
    def _():
        scale_grad_ref[...] = spread

    @pl.when(pl.program_id(0) > 0)
    def _():
        scale_grad_ref[...] += spread


def attend_back_rows(projected, attended_grad, log_total, scale_vec, segments, token_rows):
    head_dim = scale_vec.shape[0]
    length = projected.shape[1]
    local_heads = projected.shape[0] // 3 // head_dim
    owners, _, tokens = attended_grad.shape
    lanes = 128
    grads, scale_grad = pl.pallas_call(
        functools.partial(attend_back_kernel, token_rows),
        grid=(local_heads,),
        in_specs=[
            pl.BlockSpec((3, 1, head_dim, length), lambda h: (0, h, 0, 0)),
            pl.BlockSpec((owners, 1, head_dim, tokens), lambda h: (0, h, 0, 0)),
            pl.BlockSpec((1, 1, length), lambda h: (h, 0, 0)),
            pl.BlockSpec((head_dim, 1), lambda h: (0, 0)),
            pl.BlockSpec((length, 1), lambda h: (0, 0)),
            pl.BlockSpec((1, length), lambda h: (0, 0)),
        ],
        out_specs=[
            pl.BlockSpec((3, 1, head_dim, length), lambda h: (0, h, 0, 0)),
            pl.BlockSpec((head_dim, lanes), lambda h: (0, 0)),
        ],
        out_shape=[
            pltpu.HBM((3, local_heads, head_dim, length), BF16),
            pltpu.HBM((head_dim, lanes), F32),
        ],
        scratch_shapes=[
            pltpu.VMEM((head_dim, length), F32),
            pltpu.VMEM((head_dim, length), F32),
        ],
        compiler_params=KERNEL,
        cost_estimate=LIGHT,
    )(
        *in_hbm(
            projected.reshape(3, local_heads, head_dim, length),
            attended_grad.reshape(owners, local_heads, head_dim, tokens),
        ),
        log_total,
        scale_vec.reshape(head_dim, 1),
        segments.reshape(length, 1),
        segments.reshape(1, length),
    )
    return grads.reshape(3 * local_heads * head_dim, length), scale_grad[:, 0]


def dense_grad_kernel(
    core_ref, attended_ref, normed_ref, active_ref, out_bar, up_bar, down_bar,
    own_ref, other_ref, normed_t, active_t,
):
    tile = pl.program_id(0)
    rows, width = own_ref.shape[1] * own_ref.shape[3] * 2, out_bar.shape[1]

    @pl.when(tile == 0)
    def _():
        normed_t[...] = normed_ref[...].astype(F32).T.astype(BF16)
        active_t[...] = active_ref[...].astype(F32).T.astype(BF16)

    start = pl.multiple_of(tile * rows, rows)
    first_core = core_ref[2] == 0
    lefts = (attended_ref, normed_t, active_t)
    for i, (left, right) in enumerate(zip(lefts, (out_bar, up_bar, down_bar))):
        grad = jnp.dot(left[pl.ds(start, rows), :], right[...], preferred_element_type=F32)
        grad = grad.reshape(2, 2, rows // 4, width)
        one, two = grad[:, 0], grad[:, 1]
        own_ref[0, :, 0, :, i * width : (i + 1) * width] = jnp.where(
            first_core, one, two
        ).astype(BF16)
        other_ref[0, :, 0, :, i * width : (i + 1) * width] = jnp.where(
            first_core, two, one
        ).astype(BF16)


def dense_grads(attended_t, normed, active, out_bar, up_bar, down_bar):
    width, tokens = attended_t.shape
    own = width // 32
    whole = pl.BlockSpec((tokens, width), lambda i, core: (0, 0))
    rows = pl.BlockSpec((1, 2, 1, own, 3 * width), lambda i, core: (i % 2, 0, i // 2, 0, 0))
    shape = pltpu.HBM((2, 2, 4, own, 3 * width), BF16)
    return pl.pallas_call(
        dense_grad_kernel,
        grid_spec=pltpu.PrefetchScalarGridSpec(
            num_scalar_prefetch=1,
            grid=(8,),
            in_specs=[pl.BlockSpec((width, tokens), lambda i, core: (0, 0))] + [whole] * 5,
            out_specs=[rows, rows],
            scratch_shapes=[pltpu.VMEM((width, tokens), BF16)] * 2,
        ),
        out_shape=[shape, shape],
        compiler_params=KERNEL,
        cost_estimate=LIGHT,
    )(place(), *in_hbm(attended_t, normed, active, out_bar, up_bar, down_bar))


def place():
    head = lax.axis_index("head")
    return jnp.stack([lax.axis_index("blk"), head // 2, head % 2]).astype(jnp.int32)


def assemble_kernel(place_ref, *refs):
    pieces, whole_ref = refs[:10], refs[10]
    half = whole_ref.shape[-1] // 2
    blk, row, core = place_ref[0], place_ref[1], place_ref[2]
    for i in range(2):
        at_core = core if i == 0 else 1 - core
        own, across, beside, one, two = pieces[5 * i : 5 * i + 5]
        whole_ref[0, blk, row, at_core] = own[0]
        whole_ref[0, 1 - blk, row, at_core] = across[0]
        whole_ref[0, blk, 1 - row, at_core] = beside[0]
        whole_ref[0, 1 - blk, 1 - row, at_core, :, :half] = one[0]
        whole_ref[0, 1 - blk, 1 - row, at_core, :, half:] = two[0]


def assemble(pieces):
    batch, own, columns = pieces[0].shape
    specs = [
        pl.BlockSpec((1, own, piece.shape[-1]), lambda i, at: (i, 0, 0))
        for piece in pieces
    ]
    whole = pl.pallas_call(
        assemble_kernel,
        grid_spec=pltpu.PrefetchScalarGridSpec(
            num_scalar_prefetch=1,
            grid=(batch,),
            in_specs=specs,
            out_specs=pl.BlockSpec((1, 2, 2, 2, own, columns), lambda i, at: (i, 0, 0, 0, 0, 0)),
        ),
        out_shape=pltpu.HBM((batch, 2, 2, 2, own, columns), BF16),
        compiler_params=KERNEL,
        cost_estimate=LIGHT,
    )(place(), *in_hbm(*pieces))
    return whole.reshape(-1, columns)


def assemble_columns_kernel(place_ref, along_ref, across_ref, whole_ref, *extra_ref):
    blk = place_ref[0]
    columns = whole_ref.shape[-1]
    whole_ref[0, blk] = along_ref[0, :, :columns]
    whole_ref[0, 1 - blk] = across_ref[0, :, :columns]
    for extra in extra_ref:
        extra[0, blk] = along_ref[0, :, columns:]
        extra[0, 1 - blk] = across_ref[0, :, columns:]


def assemble_columns(along, across, columns):
    batch, own, both = along.shape
    rows = pl.BlockSpec((1, own, both), lambda i, at: (i, 0, 0))
    shapes = [(batch, 2, own, columns)]
    if both > columns:
        shapes.append((batch, 2, own, both - columns))
    parts = pl.pallas_call(
        assemble_columns_kernel,
        grid_spec=pltpu.PrefetchScalarGridSpec(
            num_scalar_prefetch=1,
            grid=(batch,),
            in_specs=[rows, rows],
            out_specs=[pl.BlockSpec((1,) + s[1:], lambda i, at: (i, 0, 0, 0)) for s in shapes],
        ),
        out_shape=[pltpu.HBM(s, BF16) for s in shapes],
        compiler_params=KERNEL,
        cost_estimate=LIGHT,
    )(place(), *in_hbm(along, across))
    return [part.reshape(-1, part.shape[-1]) for part in parts]


def project_kernel(with_norm, place_ref, *refs):
    pieces, (gain_ref, weight_ref, normed_ref, projected_ref) = refs[:4], refs[4:]
    head = place_ref[1] * 2 + place_ref[2]
    rows = pieces[0].shape[0]
    for i, piece in enumerate(pieces):
        value = piece[...]
        if with_norm:
            stream = value.astype(F32)
            factor = lax.rsqrt(jnp.mean(stream * stream, axis=-1, keepdims=True) + EPSILON)
            value = (stream * factor * gain_ref[...]).astype(BF16)
        normed_ref[pl.ds(pl.multiple_of((head ^ i) * rows, rows), rows), :] = value
    projected = jnp.dot(normed_ref[...], weight_ref[...], preferred_element_type=F32)
    projected_ref[...] = projected.T


def project(pieces, gain, weight, with_norm, token_rows):
    tokens, width = pieces[0].shape
    length, columns = 4 * tokens, weight.shape[1]
    groups = tokens // token_rows
    piece = pl.BlockSpec((token_rows, width), lambda g, at: (g, 0))
    return pl.pallas_call(
        functools.partial(project_kernel, with_norm),
        grid_spec=pltpu.PrefetchScalarGridSpec(
            num_scalar_prefetch=1,
            grid=(groups,),
            in_specs=[piece] * 4
            + [
                pl.BlockSpec((1, width), lambda g, at: (0, 0)),
                pl.BlockSpec((width, columns), lambda g, at: (0, 0)),
            ],
            out_specs=[
                pl.BlockSpec((4 * token_rows, width), lambda g, at: (g, 0)),
                pl.BlockSpec((columns, 4 * token_rows), lambda g, at: (0, g)),
            ],
        ),
        out_shape=[
            pltpu.HBM((length, width), BF16),
            pltpu.HBM((columns, length), F32),
        ],
        compiler_params=KERNEL,
        cost_estimate=LIGHT,
    )(place(), *in_hbm(*pieces), gain.reshape(1, width), *in_hbm(weight))


def project_back_kernel(
    place_ref, bars_ref, weight_ref, normed_ref, own_ref, other_ref, grad_ref, bars_t
):
    @pl.when(pl.program_id(0) == 0)
    def _():
        bars_t[...] = bars_ref[...].astype(F32).T.astype(BF16)

    upper = lax.dot_general(bars_t[...], weight_ref[...], NT, preferred_element_type=F32)
    upper = upper.reshape(2, 2, 2, -1, upper.shape[-1])
    first_core = place_ref[2] == 0
    one, two = upper[:, :, 0], upper[:, :, 1]
    own_ref[...] = jnp.where(first_core, one, two)
    other_ref[...] = jnp.where(first_core, two, one).astype(BF16)
    grad = lax.dot_general(normed_ref[...], bars_t[...], TN, preferred_element_type=F32)
    grad_ref[...] = grad.astype(BF16)


def project_back(bars, weight, normed, token_rows):
    columns, length = bars.shape
    width = weight.shape[0]
    tile = width // 2
    quarter = pl.BlockSpec((2, 2, token_rows, tile), lambda i, at: (0, 0, 0, i))
    return pl.pallas_call(
        project_back_kernel,
        grid_spec=pltpu.PrefetchScalarGridSpec(
            num_scalar_prefetch=1,
            grid=(2,),
            in_specs=[
                pl.BlockSpec((columns, length), lambda i, at: (0, 0)),
                pl.BlockSpec((tile, columns), lambda i, at: (i, 0)),
                pl.BlockSpec((length, tile), lambda i, at: (0, i)),
            ],
            out_specs=[quarter, quarter, pl.BlockSpec((tile, columns), lambda i, at: (i, 0))],
            scratch_shapes=[pltpu.VMEM((length, columns), BF16)],
        ),
        out_shape=[
            pltpu.HBM((2, 2, token_rows, width), F32),
            pltpu.HBM((2, 2, token_rows, width), BF16),
            pltpu.HBM((width, columns), BF16),
        ],
        compiler_params=KERNEL,
        cost_estimate=LIGHT,
    )(place(), *in_hbm(bars, weight, normed))


def tied(*arrays):
    return lax.optimization_barrier(arrays)


def swapped(array, axis, mask):
    size = lax.axis_size(axis)
    return lax.ppermute(array, axis, [(i, i ^ mask) for i in range(size)])


def pick(array, index, axis=0):
    return lax.dynamic_index_in_dim(array, index, axis, keepdims=False)


def swap_halves(array):
    me = lax.axis_index("blk")
    got = swapped(pick(array, 1 - me), "blk", 1)
    kept = pick(array, me)
    return jnp.stack([jnp.where(me == 0, kept, got), jnp.where(me == 0, got, kept)])


def scatter_row(halves):
    row = lax.axis_index("head") // 2
    got = swapped(pick(halves, 1 - row, 1).astype(BF16), "head", 2).astype(F32)
    return (pick(halves, row, 1) + got).reshape(-1, halves.shape[-1])


def over_head(parts):
    return lax.all_to_all(parts, "head", split_axis=0, concat_axis=0, tiled=True)


def qkv_columns(rows, extra):
    own, width = rows.shape
    part = width // 3 // 4
    sent = rows.reshape(own, 3, 4, part).transpose(2, 0, 1, 3).reshape(4, own, 3 * part)
    if extra is not None:
        sent = jnp.concatenate([sent, jnp.broadcast_to(extra[None], (4,) + extra.shape)], axis=2)
    return over_head(sent)


def along_batch(piece):
    return lax.all_gather(piece, "batch", axis=0, tiled=False)


def other_core(array):
    return swapped(array, "head", 1)


def to_beside(across):
    return swapped(across[..., : across.shape[-1] // 2], "head", 2)


def to_across(beside):
    return swapped(beside[..., beside.shape[-1] // 2 :], "blk", 1)


def over_batch(parts):
    return lax.psum_scatter(parts.astype(BF16), "batch", scatter_dimension=0, tiled=False)


def across_sum(halves):
    blk = lax.axis_index("blk")
    got = swapped(pick(halves, 1 - blk), "blk", 1).astype(F32)
    return (pick(halves, blk).astype(F32) + got).astype(BF16)


def columns_to_rows(summed):
    moved = over_head(summed.reshape(4, -1, summed.shape[-1]))
    rows = moved.shape[1]
    return moved.reshape(4, rows, 3, -1).transpose(1, 2, 0, 3).reshape(rows, -1).astype(F32)


def diagonal_rows(cored):
    blk, row = place()[:2]
    rows = pick(pick(cored, 1 - blk), 1 - row)
    half = rows.shape[-1] // 2
    return rows[..., :half], rows[..., half:]


def neighbour_rows(cored, one, two):
    blk, row = place()[:2]
    half = one.shape[-1]
    across = pick(pick(cored, 1 - blk), row)
    beside = pick(pick(cored, blk), 1 - row)
    across = jnp.concatenate(
        [across[..., :half], across[..., half:].astype(F32) + two.astype(F32)], axis=-1
    ).astype(BF16)
    beside = jnp.concatenate(
        [beside[..., :half].astype(F32) + one.astype(F32), beside[..., half:]], axis=-1
    ).astype(BF16)
    return across, beside


def sent_beside_and_across(across, beside):
    return swapped(across, "blk", 1), swapped(beside, "head", 2)


def own_sum(cored, across, beside):
    blk, row = place()[:2]
    own = pick(pick(cored, blk), row)
    return own.astype(F32) + across.astype(F32) + beside.astype(F32)


def sum_all(array):
    for axis, mask in (("head", 1), ("head", 2), ("blk", 1), ("batch", 1), ("batch", 2)):
        array = array + swapped(array, axis, mask)
    return array


def gain_back(weight, weight_grad, gain):
    return jnp.sum(weight.astype(F32) * weight_grad, axis=-1) / gain.astype(F32)


def lower_of(upper, stream, factor, gain):
    return norm_back(upper, stream, factor, gain)[0]


def spread_device(
    tokens,
    segments,
    qkv_weight,
    out_weight,
    up_weight,
    down_weight,
    attn_gain,
    mlp_gain,
    scale_param,
    cotangent,
):
    layers, head_dim = scale_param.shape
    _, token_rows, width = tokens.shape
    scale_vecs = SCALE_BASE / math.sqrt(head_dim) * jax.nn.softplus(scale_param)
    segments = pick(segments, lax.axis_index("blk"))
    own_gains = jnp.concatenate([attn_gain, mlp_gain], axis=0)

    part3 = 3 * width // 4
    dense_own = [
        jnp.concatenate([out_weight[i], up_weight[i], down_weight[i]], axis=1) for i in (0, 1)
    ]

    first = swap_halves(tokens).reshape(-1, width)
    upper = swap_halves(cotangent).reshape(-1, width)
    dense_near = along_batch(dense_own[0])
    columns = qkv_columns(qkv_weight[0], own_gains.T)
    columns, first, upper = tied(columns.reshape(-1, columns.shape[-1]), first, upper)
    stream, upper = first.astype(F32), upper.astype(F32)
    far, near = swapped(first, "head", 2), other_core(first)
    both = other_core(far)
    columns, dense_near, near, far, both = tied(columns, dense_near, near, far, both)
    token_pieces = (first, near, far, both)
    across, beside = swapped(dense_near, "blk", 1), swapped(dense_near, "head", 2)
    along = along_batch(columns)
    next_columns = qkv_columns(qkv_weight[1], None).reshape(-1, part3)
    along, across, beside, next_columns = tied(along, across, beside, next_columns)
    qkv_across = swapped(along, "blk", 1)
    one = to_beside(across)
    next_along = along_batch(next_columns)
    qkv_across, one, beside, next_along, dense_next = tied(
        qkv_across, one, beside, next_along, dense_own[1]
    )
    two, next_along = tied(to_across(beside), next_along)
    next_across = swapped(next_along, "blk", 1)
    pieces = [(dense_near, across, beside, one, two)]
    dense_next = along_batch(dense_next)
    weight, gains = assemble_columns(along, qkv_across, part3)
    qkvs = [weight]
    gains = gains.T.astype(F32)

    kept, denses = [], []
    for layer in range(layers):
        normed, factor_one = normalize(stream, gains[layer])
        if layer == 1:
            normed, beside = tied(normed.astype(BF16), beside)
            far, near = swapped(normed, "head", 2), other_core(normed)
            far, near, across, beside = tied(far, near, across, beside)
            token_pieces = (normed, near, far, other_core(far))
            one, two = to_beside(across), to_across(beside)
            pieces.append((dense_next, across, beside, one, two))
            qkvs.append(assemble_columns(next_along, next_across, part3)[0])
        normed_all, projected = project(
            token_pieces, gains[layer], qkvs[layer], layer == 0, token_rows
        )
        attended, log_total = attend_rows(
            projected, scale_vecs[layer], segments, 4, token_rows
        )
        attended, one, two = tied(attended, *pieces[layer][3:])
        pieces[layer] = pieces[layer][:3] + (one, two)
        swaps = tuple(other_core(piece) for piece in pieces[layer])
        if layer == 0:
            attended, dense_next = tied(attended, dense_next)
            beside = swapped(dense_next, "head", 2)
            attended_t, swaps, next_across, dense_next = tied(
                over_head(attended), swaps, next_across, dense_next
            )
            across = swapped(dense_next, "blk", 1)
        else:
            attended_t, swaps = tied(over_head(attended), swaps)
        attended_t = attended_t.reshape(width, -1)
        denses.append(assemble(pieces[layer] + swaps))
        dense = denses[layer]
        out_w, up_w, down_w = dense[:, :width], dense[:, width:-width], dense[:, -width:]
        middle = stream + dot_rows(attended_t, out_w)
        normed_two, factor_two = normalize(middle, gains[layers + layer])
        normed_two = normed_two.astype(BF16)
        hidden = dot(normed_two, up_w)
        active = (hidden * jax.nn.sigmoid(hidden)).astype(BF16)
        kept.append(
            (
                stream, factor_one, normed_all, projected, log_total, attended_t, middle,
                factor_two, normed_two, hidden, active,
            )
        )
        stream = middle + dot(active, down_w)
    layer_out = swap_halves(stream.astype(BF16).reshape(tokens.shape))

    scale_grads = [None] * layers
    for layer in reversed(range(layers)):
        (
            stream, factor_one, normed_all, projected, log_total, attended_t, middle,
            factor_two, normed_two, hidden, active,
        ) = kept[layer]
        qkv, dense = qkvs[layer], denses[layer]
        out_w, up_w, down_w = dense[:, :width], dense[:, width:-width], dense[:, -width:]
        down_bar = upper.astype(BF16)
        gate = jax.nn.sigmoid(hidden)
        up_bar = (
            dot_cols(down_bar, down_w) * gate * (1.0 + hidden * (1.0 - gate))
        ).astype(BF16)
        middle_grad = upper + lower_of(
            dot_cols(up_bar, up_w), middle, factor_two, gains[layers + layer]
        )
        out_bar = middle_grad.astype(BF16)
        if layer == 0:
            out_bar, diagonal = tied(out_bar, diagonal)
            out_bar, rows = tied(out_bar, neighbour_rows(cored, *diagonal))
            sent = sent_beside_and_across(*rows)
        attended_grad = over_head(dot_cols(out_w, out_bar).astype(BF16).reshape(4, -1, out_bar.shape[0]))
        grads, others = dense_grads(attended_t, normed_two, active, out_bar, up_bar, down_bar)
        if layer == 0:
            attended_grad, others, z_sum = tied(attended_grad, others, z_sum)
            z_across = across_sum(z_sum)
        else:
            attended_grad, others, layer_out = tied(attended_grad, others, layer_out)
        others = other_core(others)
        bars, scale_grads[layer] = attend_back_rows(
            projected, attended_grad, log_total, scale_vecs[layer], segments, token_rows
        )
        if layer == 0:
            bars, others, sent = tied(bars, others, sent)
            summed = own_sum(cored, *sent)
        else:
            bars, others = tied(bars, others)
        cored = (grads.astype(F32) + others.astype(F32)).astype(BF16)
        if layer == 0:
            bars, summed, rows = tied(bars, summed, diagonal_rows(cored))
            diagonal = sent_beside_and_across(*rows)
            summed = over_batch(summed)
        halves, to_core, qkv_grad = project_back(bars, qkv, normed_all, token_rows)
        halves = halves + other_core(to_core).astype(F32)
        z_sum = over_batch(qkv_grad.reshape(4, 2, -1, qkv_grad.shape[-1]))
        if layer == 0:
            halves, diagonal = tied(halves, diagonal)
            halves, rows = tied(halves, neighbour_rows(cored, *diagonal))
            sent = sent_beside_and_across(*rows)
            normed_grad = scatter_row(halves)
            normed_grad, sent, summed, z_across = tied(normed_grad, sent, summed, z_across)
            dense_grad = [over_batch(own_sum(cored, *sent)), summed]
            qkv_grads = [columns_to_rows(across_sum(z_sum)), columns_to_rows(z_across)]
        else:
            normed_grad = scatter_row(halves)
            normed_grad, cored = tied(normed_grad, cored)
            diagonal = sent_beside_and_across(*diagonal_rows(cored))
        upper = middle_grad + lower_of(normed_grad, stream, factor_one, gains[layer])
    input_grad = swap_halves(upper.astype(BF16).reshape(tokens.shape)).astype(F32)
    scale_total = sum_all(jnp.stack(scale_grads))
    scale_grad = scale_total * (SCALE_BASE / math.sqrt(head_dim)) * jax.nn.sigmoid(scale_param)
    dense_all = jnp.stack([part.astype(F32) for part in dense_grad])
    qkv_all = jnp.stack(qkv_grads)
    up_all = dense_all[:, :, width:-width]
    return (
        layer_out,
        input_grad,
        qkv_all,
        dense_all[:, :, :width],
        up_all,
        dense_all[:, :, -width:],
        gain_back(qkv_weight, qkv_all, attn_gain),
        gain_back(up_weight, up_all, mlp_gain),
        scale_grad,
    )


def per_device(*args):
    tokens, segments = args[0], args[1]
    sizes = tuple(lax.axis_size(axis) for axis in ALL)
    heads = tokens.shape[2] // args[8].shape[1]
    spread = (
        sizes == (4, 2, 4)
        and tokens.shape[0] == 2
        and args[2].shape[0] == 2
        and tokens.shape[1] % 128 == 0
        and Q_ROWS % tokens.shape[1] == 0
        and segments.shape[1] <= WINDOW
        and segments.shape[1] % Q_ROWS == 0
        and heads % 4 == 0
        and tokens.shape[2] % 256 == 0
    )
    return spread_device(*args) if spread else general_device(*args)


def solution(mesh):
    rows = P(None, ALL, None)
    by_token = P("batch", ("blk", "head"), None)
    return jax.shard_map(
        per_device,
        mesh=mesh,
        in_specs=(
            by_token, P("batch", None), rows, rows, rows, rows, P(None, ALL), P(None, ALL), P(),
            by_token,
        ),
        out_specs=(
            by_token, by_token, rows, rows, rows, rows, P(None, ALL), P(None, ALL), P(),
        ),
        check_vma=False,
    )
```

```python
import functools
import math

import jax
import jax.numpy as jnp
from jax import lax
from jax.experimental import pallas as pl
from jax.experimental.pallas import tpu as pltpu
from jax.sharding import PartitionSpec as P

WINDOW = 1024
EPSILON = 1e-06
SCALE_BASE = 1.4426950408889634
MASKED_SCORE = -1e30

ALL = ("batch", "blk", "head")
REST = ("batch", "blk")
F32 = jnp.float32
BF16 = jnp.bfloat16


def shifted(block, axis, distance):
    devices = range(lax.axis_size(axis))
    route = [(i - distance, i) for i in devices if i - distance in devices]
    return lax.ppermute(block, axis, route)


NT = (((1,), (1,)), ((), ()))
TN = (((0,), (0,)), ((), ()))


def dot(left, right):
    return jnp.dot(left, right, preferred_element_type=F32)


def dot_rows(left, right):
    return lax.dot_general(left, right, (((0,), (0,)), ((), ())), preferred_element_type=F32)


def dot_cols(left, right):
    return lax.dot_general(left, right, (((1,), (1,)), ((), ())), preferred_element_type=F32)


def normalize(stream, gain):
    factor = lax.rsqrt(jnp.mean(stream * stream, axis=-1, keepdims=True) + EPSILON)
    return stream * factor * gain, factor


def norm_back(upper, stream, factor, gain):
    inner = upper * gain
    gain_grad = jnp.sum(upper * stream * factor, axis=0)
    lower = factor * inner - stream * factor * factor * factor * jnp.mean(
        inner * stream, axis=-1, keepdims=True
    )
    return lower, gain_grad


class Plan:
    def __init__(self, tokens):
        self.seqs, self.rows, self.width = tokens.shape
        self.heads = lax.axis_size("head")
        self.blks = lax.axis_size("blk")
        self.block = self.rows * self.heads
        self.whole = self.seqs % self.blks == 0
        if self.whole:
            self.groups, self.own_seqs = self.blks, self.seqs // self.blks
            self.reach = 0
        else:
            self.groups, self.own_seqs = 1, self.seqs
            self.reach = min((WINDOW - 1) // self.block + 1, self.blks - 1)
        self.length = self.groups * self.block
        self.tokens = self.seqs * self.rows


def to_plan(plan, array):
    if plan.whole and plan.blks > 1:
        array = lax.all_to_all(array, "blk", split_axis=0, concat_axis=0, tiled=True)
    return array.reshape(plan.tokens, plan.width)


def from_plan(plan, flat):
    array = flat.reshape(plan.seqs, plan.rows, plan.width)
    if plan.whole and plan.blks > 1:
        array = lax.all_to_all(array, "blk", split_axis=0, concat_axis=0, tiled=True)
    return array


def in_sequence(plan, by_head, width):
    parts = by_head.reshape(plan.heads, plan.groups, plan.own_seqs, plan.rows, width)
    return parts.transpose(2, 1, 0, 3, 4).reshape(-1, width)


def by_owner(plan, rows, width):
    parts = rows.reshape(plan.own_seqs, plan.groups, plan.heads, plan.rows, width)
    return parts.transpose(2, 1, 0, 3, 4).reshape(plan.heads, plan.tokens, width)


def gather_tokens(plan, rows):
    moved = lax.all_gather(rows, "head", axis=0, tiled=False)
    return in_sequence(plan, moved, rows.shape[-1])


def scatter_tokens(plan, rows):
    width = rows.shape[-1]
    return lax.psum_scatter(
        by_owner(plan, rows.astype(BF16), width), "head", scatter_dimension=0, tiled=False
    ).astype(F32)


def heads_to_tokens(plan, rows):
    part = rows.shape[-1]
    moved = lax.all_to_all(
        by_owner(plan, rows, part), "head", split_axis=0, concat_axis=0, tiled=True
    )
    return moved.transpose(1, 0, 2).reshape(plan.tokens, plan.heads * part)


def tokens_to_heads(plan, rows):
    part = rows.shape[-1] // plan.heads
    sent = rows.reshape(plan.tokens, plan.heads, part).transpose(1, 0, 2)
    moved = lax.all_to_all(sent, "head", split_axis=0, concat_axis=0, tiled=True)
    return in_sequence(plan, moved, part)


def gather_qkv(rows):
    own, width = rows.shape
    heads = lax.axis_size("head")
    part = width // 3 // heads
    sent = rows.reshape(own, 3, heads, part).transpose(2, 0, 1, 3).reshape(heads, own, 3 * part)
    moved = lax.all_to_all(sent, "head", split_axis=0, concat_axis=0, tiled=True)
    full = lax.all_gather(moved, REST, axis=0, tiled=True)
    return full.reshape(-1, 3 * part)


def scatter_qkv(grad):
    heads = lax.axis_size("head")
    part = grad.shape[1] // 3
    summed = lax.psum_scatter(grad.astype(BF16), REST, scatter_dimension=0, tiled=True)
    own = summed.shape[0] // heads
    moved = lax.all_to_all(
        summed.reshape(heads, own, 3 * part), "head", split_axis=0, concat_axis=0, tiled=True
    )
    return (
        moved.reshape(heads, own, 3, part)
        .transpose(1, 2, 0, 3)
        .reshape(own, 3 * heads * part)
        .astype(F32)
    )


def window_mask(plan, segments, block_index):
    key_count = plan.length + plan.reach * plan.block
    if plan.whole:
        query_segs, key_segs = segments, segments
    else:
        leading = jnp.full((plan.own_seqs, plan.reach * plan.block), -1, jnp.int32)
        padded = jnp.concatenate([leading, segments], axis=1)
        start = block_index * plan.block
        query_segs = lax.dynamic_slice_in_dim(segments, start, plan.block, 1)
        key_segs = lax.dynamic_slice_in_dim(padded, start, key_count, 1)
    query_place = jnp.arange(plan.length, dtype=jnp.int32)[:, None] + plan.reach * plan.block
    key_place = jnp.arange(key_count, dtype=jnp.int32)[None, :]
    near = (key_place <= query_place) & (query_place - key_place < WINDOW)
    return (key_segs[:, None, :] == query_segs[:, :, None]) & near[None]


def with_earlier(plan, own):
    arrived = [own]
    for _ in range(plan.reach):
        arrived.append(shifted(arrived[-1], "blk", 1))
    return jnp.concatenate(arrived[::-1], axis=1) if plan.reach else own


def to_earlier(plan, grads):
    if not plan.reach:
        return grads
    block = plan.block
    total = grads[:, :block]
    for step in range(1, plan.reach + 1):
        total = (
            shifted(total.astype(BF16), "blk", -1).astype(F32)
            + grads[:, step * block : (step + 1) * block]
        )
    return total


def scores_of(queries, keys, allowed):
    scores = jnp.einsum("sqhd,skhd->shqk", queries, keys, preferred_element_type=F32)
    return jnp.where(allowed[:, None], scores, MASKED_SCORE)


def attend(queries, keys, values, allowed):
    scores = scores_of(queries, keys, allowed)
    top_score = jnp.max(scores, axis=-1, keepdims=True)
    exp_terms = jnp.exp(scores - top_score)
    totals = jnp.sum(exp_terms, axis=-1, keepdims=True)
    probs_low = (exp_terms / totals).astype(BF16)
    attended = jnp.einsum("shqk,skhd->sqhd", probs_low, values, preferred_element_type=F32)
    return attended, top_score + jnp.log(totals)


def attend_back(queries, keys, values, allowed, log_total, attended_grad):
    probs = jnp.exp(scores_of(queries, keys, allowed) - log_total)
    probs_low = probs.astype(BF16)
    values_grad = jnp.einsum(
        "shqk,sqhd->skhd", probs_low, attended_grad, preferred_element_type=F32
    )
    probs_grad = jnp.einsum("sqhd,skhd->shqk", attended_grad, values, preferred_element_type=F32)
    row_dot = jnp.sum(probs_grad * probs, axis=-1, keepdims=True)
    scores_low = (probs * (probs_grad - row_dot)).astype(BF16)
    queries_grad = jnp.einsum("shqk,skhd->sqhd", scores_low, keys, preferred_element_type=F32)
    keys_grad = jnp.einsum("shqk,sqhd->skhd", scores_low, queries, preferred_element_type=F32)
    return queries_grad, keys_grad, values_grad


def forward(plan, stream, qkv, dense, gains, scale_vec, allowed):
    width = plan.width
    head_dim = scale_vec.shape[0]
    part = qkv.shape[1] // 3
    local_heads = part // head_dim
    split = (plan.own_seqs, plan.length, local_heads, head_dim)
    out_w, up_w, down_w = dense[:, :width], dense[:, width:-width], dense[:, -width:]
    normed, factor_one = normalize(stream, gains[0])
    normed_all = gather_tokens(plan, normed.astype(BF16))
    projected = dot(normed_all, qkv)
    query_pre = projected[:, :part].reshape(split)
    queries = (query_pre * scale_vec).astype(BF16)
    keys = with_earlier(plan, projected[:, part : 2 * part].astype(BF16).reshape(split))
    values = with_earlier(plan, projected[:, 2 * part :].astype(BF16).reshape(split))
    attended_part, log_total = attend(queries, keys, values, allowed)
    attended = heads_to_tokens(plan, attended_part.astype(BF16).reshape(-1, part))
    middle = stream + dot(attended, out_w)
    normed_two, factor_two = normalize(middle, gains[1])
    normed_two = normed_two.astype(BF16)
    hidden = dot(normed_two, up_w)
    active = (hidden * jax.nn.sigmoid(hidden)).astype(BF16)
    result = middle + dot(active, down_w)
    kept = (
        stream, factor_one, normed_all, query_pre, queries, keys, values, log_total,
        attended, middle, factor_two, normed_two, hidden, active,
    )
    return result, kept


def backward(plan, upper, kept, qkv, dense, gains, scale_vec, allowed):
    (
        stream, factor_one, normed_all, query_pre, queries, keys, values, log_total,
        attended, middle, factor_two, normed_two, hidden, active,
    ) = kept
    width = plan.width
    head_dim = scale_vec.shape[0]
    part = qkv.shape[1] // 3
    out_w, up_w, down_w = dense[:, :width], dense[:, width:-width], dense[:, -width:]
    upper_low = upper.astype(BF16)
    down_grad = dot_rows(active, upper_low)
    active_grad = dot_cols(upper_low, down_w)
    gate = jax.nn.sigmoid(hidden)
    hidden_low = (active_grad * gate * (1.0 + hidden * (1.0 - gate))).astype(BF16)
    up_grad = dot_rows(normed_two, hidden_low)
    extra_two, mlp_gain_grad = norm_back(dot_cols(hidden_low, up_w), middle, factor_two, gains[1])
    middle_grad = upper + extra_two
    middle_low = middle_grad.astype(BF16)
    out_grad = dot_rows(attended, middle_low)
    dense_grad = jnp.concatenate([out_grad, up_grad, down_grad], axis=1).astype(BF16)
    dense_own = lax.psum_scatter(dense_grad, ALL, scatter_dimension=0, tiled=True)
    attended_grad = tokens_to_heads(plan, dot_cols(middle_low, out_w).astype(BF16))
    queries_grad, keys_grad, values_grad = attend_back(
        queries, keys, values, allowed, log_total, attended_grad.reshape(queries.shape)
    )
    query_bar = queries_grad.astype(BF16).astype(F32)
    scale_vec_grad = jnp.sum((query_bar * query_pre).reshape(-1, head_dim), axis=0)
    query_low = (query_bar * scale_vec).astype(BF16).reshape(-1, part)
    keys_low = to_earlier(plan, keys_grad).astype(BF16).reshape(-1, part)
    values_low = to_earlier(plan, values_grad).astype(BF16).reshape(-1, part)
    projected_low = jnp.concatenate([query_low, keys_low, values_low], axis=1)
    normed_grad = scatter_tokens(plan, dot_cols(projected_low, qkv))
    qkv_own = scatter_qkv(dot_rows(normed_all, projected_low))
    extra_one, attn_gain_grad = norm_back(normed_grad, stream, factor_one, gains[0])
    lower = middle_grad + extra_one
    return lower, qkv_own, dense_own, (attn_gain_grad, mlp_gain_grad), scale_vec_grad


def general_device(
    tokens,
    segments,
    qkv_weight,
    out_weight,
    up_weight,
    down_weight,
    attn_gain,
    mlp_gain,
    scale_param,
    cotangent,
):
    plan = Plan(tokens)
    layers, head_dim = scale_param.shape
    block_index = lax.axis_index("blk")
    scale_vecs = SCALE_BASE / math.sqrt(head_dim) * jax.nn.softplus(scale_param)
    own_gains = jnp.concatenate([attn_gain, mlp_gain], axis=0)
    gains = (
        lax.all_gather(own_gains.reshape(1, -1), ALL, axis=0, tiled=True)
        .reshape(-1, 2 * layers, attn_gain.shape[1])
        .transpose(1, 0, 2)
        .reshape(2 * layers, plan.width)
        .astype(F32)
    )
    if plan.whole:
        segments = lax.dynamic_slice_in_dim(
            segments, block_index * plan.own_seqs, plan.own_seqs, 0
        )
    allowed = window_mask(plan, segments, block_index)
    stream = to_plan(plan, tokens).astype(F32)
    qkvs, denses, kept = [], [], []
    for layer in range(layers):
        qkvs.append(gather_qkv(qkv_weight[layer]))
        own = jnp.concatenate([out_weight[layer], up_weight[layer], down_weight[layer]], axis=1)
        denses.append(lax.all_gather(own, ALL, axis=0, tiled=True))
        layer_gains = (gains[layer], gains[layers + layer])
        stream, saved = forward(
            plan, stream, qkvs[layer], denses[layer], layer_gains, scale_vecs[layer], allowed
        )
        kept.append(saved)
    layer_out = from_plan(plan, stream.astype(BF16))
    upper = to_plan(plan, cotangent).astype(F32)
    qkv_grads, dense_grads = [None] * layers, [None] * layers
    gain_grads, scale_grads = [None] * layers, [None] * layers
    for layer in reversed(range(layers)):
        layer_gains = (gains[layer], gains[layers + layer])
        upper, qkv_grads[layer], dense_grads[layer], gain_grads[layer], scale_grads[layer] = (
            backward(
                plan, upper, kept[layer], qkvs[layer], denses[layer], layer_gains,
                scale_vecs[layer], allowed,
            )
        )
    input_grad = from_plan(plan, upper.astype(BF16)).astype(F32)
    small = jnp.concatenate(
        [g[0] for g in gain_grads] + [g[1] for g in gain_grads] + scale_grads, axis=0
    )
    total = lax.psum(small, ALL)
    gain_total = total[: 2 * layers * plan.width].reshape(2 * layers, plan.width)
    owner = lax.axis_index(ALL)
    gain_rows = attn_gain.shape[1]
    own_total = lax.dynamic_slice_in_dim(gain_total, owner * gain_rows, gain_rows, 1)
    scale_total = total[2 * layers * plan.width :].reshape(layers, head_dim)
    scale_grad = scale_total * (SCALE_BASE / math.sqrt(head_dim)) * jax.nn.sigmoid(scale_param)
    dense_all = jnp.stack(dense_grads).astype(F32)
    width = plan.width
    return (
        layer_out,
        input_grad,
        jnp.stack(qkv_grads),
        dense_all[:, :, :width],
        dense_all[:, :, width:-width],
        dense_all[:, :, -width:],
        own_total[:layers],
        own_total[layers:],
        scale_grad,
    )


Q_ROWS = 256
KERNEL = pltpu.CompilerParams(vmem_limit_bytes=32 * 1024 * 1024)


def lasting(microseconds):
    weight = 10 * microseconds
    return pl.CostEstimate(
        flops=weight * 10**9, bytes_accessed=weight * 3 * 10**6, transcendentals=0
    )


def in_hbm(*arrays):
    return [pltpu.with_memory_space_constraint(array, pltpu.HBM) for array in arrays]


def allowed_keys(col, row, first):
    count = first + row.shape[1]
    key_place = lax.broadcasted_iota(jnp.int32, (count, row.shape[1]), 0)
    query_place = lax.broadcasted_iota(jnp.int32, (count, row.shape[1]), 1) + first
    return (col[:count] == row) & (key_place <= query_place)


def token_places(length, heads, token_rows):
    for first in range(0, length, Q_ROWS):
        parts = []
        for start in range(0, Q_ROWS, token_rows):
            place = (first + start) // token_rows
            parts.append((start, place % heads, place // heads * token_rows))
        yield first, parts


def attend_kernel(token_rows, proj_ref, scale_ref, col_ref, row_ref, out_ref, lse_ref):
    length = proj_ref.shape[-1]
    queries = (proj_ref[0, 0] * scale_ref[...]).astype(BF16)
    keys = proj_ref[1, 0].T.astype(BF16)
    values = proj_ref[2, 0].astype(BF16)
    for first, parts in token_places(length, out_ref.shape[0], token_rows):
        end = first + Q_ROWS
        scores = jnp.dot(keys[:end], queries[:, first:end], preferred_element_type=F32)
        allowed = allowed_keys(col_ref[...], row_ref[:, first:end], first)
        scores = jnp.where(allowed, scores, MASKED_SCORE)
        top = jnp.max(scores, axis=0, keepdims=True)
        terms = jnp.exp(scores - top)
        total = jnp.sum(terms, axis=0, keepdims=True)
        probs = (terms * (1.0 / total)).astype(BF16)
        attended = jnp.dot(values[:, :end], probs, preferred_element_type=F32).astype(BF16)
        lse_ref[0, :, first:end] = top + jnp.log(total)
        for start, owner, offset in parts:
            out_ref[owner, 0, :, offset : offset + token_rows] = attended[
                :, start : start + token_rows
            ]


def attend_rows(projected, scale_vec, segments, owners, token_rows):
    head_dim = scale_vec.shape[0]
    length = projected.shape[1]
    local_heads = projected.shape[0] // 3 // head_dim
    tokens = length // owners
    attended, log_total = pl.pallas_call(
        functools.partial(attend_kernel, token_rows),
        grid=(local_heads,),
        in_specs=[
            pl.BlockSpec((3, 1, head_dim, length), lambda h: (0, h, 0, 0)),
            pl.BlockSpec((head_dim, 1), lambda h: (0, 0)),
            pl.BlockSpec((length, 1), lambda h: (0, 0)),
            pl.BlockSpec((1, length), lambda h: (0, 0)),
        ],
        out_specs=[
            pl.BlockSpec((owners, 1, head_dim, tokens), lambda h: (0, h, 0, 0)),
            pl.BlockSpec((1, 1, length), lambda h: (h, 0, 0)),
        ],
        out_shape=[
            jax.ShapeDtypeStruct((owners, local_heads, head_dim, tokens), BF16),
            jax.ShapeDtypeStruct((local_heads, 1, length), F32),
        ],
        compiler_params=KERNEL,
        cost_estimate=lasting(10),
    )(
        projected.reshape(3, local_heads, head_dim, length),
        scale_vec.reshape(head_dim, 1),
        segments.reshape(length, 1),
        segments.reshape(1, length),
    )
    return attended.reshape(owners, local_heads * head_dim, tokens), log_total


def attend_back_kernel(
    token_rows,
    proj_ref,
    grad_ref,
    lse_ref,
    scale_ref,
    col_ref,
    row_ref,
    out_ref,
    scale_grad_ref,
    keys_acc,
    values_acc,
):
    length = proj_ref.shape[-1]
    scale = scale_ref[...]
    query_pre = proj_ref[0, 0]
    queries = (query_pre * scale).astype(BF16)
    keys_t = proj_ref[1, 0].astype(BF16)
    keys = proj_ref[1, 0].T.astype(BF16)
    values = proj_ref[2, 0].T.astype(BF16)
    keys_acc[...] = jnp.zeros_like(keys_acc)
    values_acc[...] = jnp.zeros_like(values_acc)
    scale_grad = jnp.zeros((scale.shape[0], 1), F32)
    for first, parts in token_places(length, grad_ref.shape[0], token_rows):
        end = first + Q_ROWS
        block = queries[:, first:end]
        grad = jnp.concatenate(
            [grad_ref[owner, 0, :, at : at + token_rows] for _, owner, at in parts], axis=1
        )
        scores = jnp.dot(keys[:end], block, preferred_element_type=F32)
        allowed = allowed_keys(col_ref[...], row_ref[:, first:end], first)
        scores = jnp.where(allowed, scores, MASKED_SCORE)
        probs = jnp.exp(scores - lse_ref[0, :, first:end])
        probs_grad = jnp.dot(values[:end], grad, preferred_element_type=F32)
        row_dot = jnp.sum(probs_grad * probs, axis=0, keepdims=True)
        scores_low = (probs * (probs_grad - row_dot)).astype(BF16)
        values_acc[:, :end] += lax.dot_general(
            grad, probs.astype(BF16), NT, preferred_element_type=F32
        )
        keys_acc[:, :end] += lax.dot_general(
            block, scores_low, NT, preferred_element_type=F32
        )
        query_bar = jnp.dot(keys_t[:, :end], scores_low, preferred_element_type=F32)
        query_bar = query_bar.astype(BF16).astype(F32)
        scale_grad += jnp.sum(query_bar * query_pre[:, first:end], axis=1, keepdims=True)
        out_ref[0, 0, :, first:end] = (query_bar * scale).astype(BF16)
    out_ref[1, 0] = keys_acc[...].astype(BF16)
    out_ref[2, 0] = values_acc[...].astype(BF16)
    spread = jnp.broadcast_to(scale_grad, scale_grad_ref.shape)

    @pl.when(pl.program_id(0) == 0)
    def _():
        scale_grad_ref[...] = spread

    @pl.when(pl.program_id(0) > 0)
    def _():
        scale_grad_ref[...] += spread


def attend_back_rows(projected, attended_grad, log_total, scale_vec, segments, token_rows):
    head_dim = scale_vec.shape[0]
    length = projected.shape[1]
    local_heads = projected.shape[0] // 3 // head_dim
    owners, _, tokens = attended_grad.shape
    lanes = 128
    grads, scale_grad = pl.pallas_call(
        functools.partial(attend_back_kernel, token_rows),
        grid=(local_heads,),
        in_specs=[
            pl.BlockSpec((3, 1, head_dim, length), lambda h: (0, h, 0, 0)),
            pl.BlockSpec((owners, 1, head_dim, tokens), lambda h: (0, h, 0, 0)),
            pl.BlockSpec((1, 1, length), lambda h: (h, 0, 0)),
            pl.BlockSpec((head_dim, 1), lambda h: (0, 0)),
            pl.BlockSpec((length, 1), lambda h: (0, 0)),
            pl.BlockSpec((1, length), lambda h: (0, 0)),
        ],
        out_specs=[
            pl.BlockSpec((3, 1, head_dim, length), lambda h: (0, h, 0, 0)),
            pl.BlockSpec((head_dim, lanes), lambda h: (0, 0)),
        ],
        out_shape=[
            pltpu.HBM((3, local_heads, head_dim, length), BF16),
            pltpu.HBM((head_dim, lanes), F32),
        ],
        scratch_shapes=[
            pltpu.VMEM((head_dim, length), F32),
            pltpu.VMEM((head_dim, length), F32),
        ],
        compiler_params=KERNEL,
        cost_estimate=lasting(12),
    )(
        *in_hbm(
            projected.reshape(3, local_heads, head_dim, length),
            attended_grad.reshape(owners, local_heads, head_dim, tokens),
        ),
        log_total,
        scale_vec.reshape(head_dim, 1),
        segments.reshape(length, 1),
        segments.reshape(1, length),
    )
    return grads.reshape(3 * local_heads * head_dim, length), scale_grad[:, 0]


def dense_grad_kernel(
    core_ref, attended_ref, normed_ref, active_ref, out_bar, up_bar, down_bar,
    own_ref, other_ref, normed_t, active_t,
):
    tile = pl.program_id(0)
    rows, width = own_ref.shape[1] * own_ref.shape[3] * 2, out_bar.shape[1]

    @pl.when(tile == 0)
    def _():
        normed_t[...] = normed_ref[...].astype(F32).T.astype(BF16)
        active_t[...] = active_ref[...].astype(F32).T.astype(BF16)

    start = pl.multiple_of(tile * rows, rows)
    first_core = core_ref[2] == 0
    lefts = (attended_ref, normed_t, active_t)
    for i, (left, right) in enumerate(zip(lefts, (out_bar, up_bar, down_bar))):
        grad = jnp.dot(left[pl.ds(start, rows), :], right[...], preferred_element_type=F32)
        grad = grad.reshape(2, 2, rows // 4, width)
        one, two = grad[:, 0], grad[:, 1]
        own_ref[0, :, 0, :, i * width : (i + 1) * width] = jnp.where(
            first_core, one, two
        ).astype(BF16)
        other_ref[0, :, 0, :, i * width : (i + 1) * width] = jnp.where(
            first_core, two, one
        ).astype(BF16)


def dense_grads(attended_t, normed, active, out_bar, up_bar, down_bar):
    width, tokens = attended_t.shape
    own = width // 32
    whole = pl.BlockSpec((tokens, width), lambda i, core: (0, 0))
    rows = pl.BlockSpec((1, 2, 1, own, 3 * width), lambda i, core: (i % 2, 0, i // 2, 0, 0))
    shape = pltpu.HBM((2, 2, 4, own, 3 * width), BF16)
    return pl.pallas_call(
        dense_grad_kernel,
        grid_spec=pltpu.PrefetchScalarGridSpec(
            num_scalar_prefetch=1,
            grid=(8,),
            in_specs=[pl.BlockSpec((width, tokens), lambda i, core: (0, 0))] + [whole] * 5,
            out_specs=[rows, rows],
            scratch_shapes=[pltpu.VMEM((width, tokens), BF16)] * 2,
        ),
        out_shape=[shape, shape],
        compiler_params=KERNEL,
        cost_estimate=lasting(8),
    )(place(), *in_hbm(attended_t, normed, active, out_bar, up_bar, down_bar))


def place():
    head = lax.axis_index("head")
    index = [lax.axis_index("blk"), head // 2, head % 2, lax.axis_index("batch")]
    return jnp.stack(index).astype(jnp.int32)


def assemble_kernel(place_ref, *refs):
    pieces, whole_ref = refs[:10], refs[10]
    half = whole_ref.shape[-1] // 2
    blk, row, core = place_ref[0], place_ref[1], place_ref[2]
    for i in range(2):
        at_core = core if i == 0 else 1 - core
        own, across, beside, one, two = pieces[5 * i : 5 * i + 5]
        whole_ref[0, blk, row, at_core] = own[0]
        whole_ref[0, 1 - blk, row, at_core] = across[0]
        whole_ref[0, blk, 1 - row, at_core] = beside[0]
        whole_ref[0, 1 - blk, 1 - row, at_core, :, :half] = one[0]
        whole_ref[0, 1 - blk, 1 - row, at_core, :, half:] = two[0]


def assemble(pieces):
    batch, own, columns = pieces[0].shape
    specs = [
        pl.BlockSpec((1, own, piece.shape[-1]), lambda i, at: (i, 0, 0))
        for piece in pieces
    ]
    whole = pl.pallas_call(
        assemble_kernel,
        grid_spec=pltpu.PrefetchScalarGridSpec(
            num_scalar_prefetch=1,
            grid=(batch,),
            in_specs=specs,
            out_specs=pl.BlockSpec((1, 2, 2, 2, own, columns), lambda i, at: (i, 0, 0, 0, 0, 0)),
        ),
        out_shape=jax.ShapeDtypeStruct((batch, 2, 2, 2, own, columns), BF16),
        compiler_params=KERNEL,
        cost_estimate=lasting(6),
    )(place(), *pieces)
    return whole.reshape(-1, columns)


def assemble_columns_kernel(place_ref, along_ref, across_ref, whole_ref, *extra_ref):
    blk = place_ref[0]
    columns = whole_ref.shape[-1]
    whole_ref[0, blk] = along_ref[0, :, :columns]
    whole_ref[0, 1 - blk] = across_ref[0, :, :columns]
    for extra in extra_ref:
        extra[0, blk] = along_ref[0, :, columns:]
        extra[0, 1 - blk] = across_ref[0, :, columns:]


def assemble_columns(along, across, columns, by_distance):
    batch, own, both = along.shape
    rows = pl.BlockSpec(
        (1, own, both), lambda i, at: (i ^ at[3] if by_distance else i, 0, 0)
    )
    shapes = [(batch, 2, own, columns)]
    if both > columns:
        shapes.append((batch, 2, own, both - columns))
    parts = pl.pallas_call(
        assemble_columns_kernel,
        grid_spec=pltpu.PrefetchScalarGridSpec(
            num_scalar_prefetch=1,
            grid=(batch,),
            in_specs=[rows, rows],
            out_specs=[pl.BlockSpec((1,) + s[1:], lambda i, at: (i, 0, 0, 0)) for s in shapes],
        ),
        out_shape=[pltpu.HBM(s, BF16) for s in shapes],
        compiler_params=KERNEL,
        cost_estimate=lasting(3),
    )(place(), *in_hbm(along, across))
    return [part.reshape(-1, part.shape[-1]) for part in parts]


def project_kernel(with_norm, place_ref, *refs):
    pieces, (gain_ref, weight_ref, normed_ref, projected_ref) = refs[:4], refs[4:]
    head = place_ref[1] * 2 + place_ref[2]
    rows = pieces[0].shape[0]
    for i, piece in enumerate(pieces):
        value = piece[...]
        if with_norm:
            stream = value.astype(F32)
            factor = lax.rsqrt(jnp.mean(stream * stream, axis=-1, keepdims=True) + EPSILON)
            value = (stream * factor * gain_ref[...]).astype(BF16)
        normed_ref[pl.ds(pl.multiple_of((head ^ i) * rows, rows), rows), :] = value
    projected = jnp.dot(normed_ref[...], weight_ref[...], preferred_element_type=F32)
    projected_ref[...] = projected.T


def project(pieces, gain, weight, with_norm, token_rows):
    tokens, width = pieces[0].shape
    length, columns = 4 * tokens, weight.shape[1]
    groups = tokens // token_rows
    piece = pl.BlockSpec((token_rows, width), lambda g, at: (g, 0))
    return pl.pallas_call(
        functools.partial(project_kernel, with_norm),
        grid_spec=pltpu.PrefetchScalarGridSpec(
            num_scalar_prefetch=1,
            grid=(groups,),
            in_specs=[piece] * 4
            + [
                pl.BlockSpec((1, width), lambda g, at: (0, 0)),
                pl.BlockSpec((width, columns), lambda g, at: (0, 0)),
            ],
            out_specs=[
                pl.BlockSpec((4 * token_rows, width), lambda g, at: (g, 0)),
                pl.BlockSpec((columns, 4 * token_rows), lambda g, at: (0, g)),
            ],
        ),
        out_shape=[
            pltpu.HBM((length, width), BF16),
            pltpu.HBM((columns, length), F32),
        ],
        compiler_params=KERNEL,
        cost_estimate=lasting(7),
    )(place(), *in_hbm(*pieces), gain.reshape(1, width), *in_hbm(weight))


def project_back_kernel(
    place_ref, bars_ref, weight_ref, normed_ref, own_ref, other_ref, grad_ref, bars_t
):
    @pl.when(pl.program_id(0) == 0)
    def _():
        bars_t[...] = bars_ref[...].astype(F32).T.astype(BF16)

    upper = lax.dot_general(bars_t[...], weight_ref[...], NT, preferred_element_type=F32)
    upper = upper.reshape(2, 2, 2, -1, upper.shape[-1])
    first_core = place_ref[2] == 0
    one, two = upper[:, :, 0], upper[:, :, 1]
    own_ref[...] = jnp.where(first_core, one, two)
    other_ref[...] = jnp.where(first_core, two, one).astype(BF16)
    grad = lax.dot_general(normed_ref[...], bars_t[...], TN, preferred_element_type=F32)
    grad_ref[...] = grad.astype(BF16)


def project_back(bars, weight, normed, token_rows):
    columns, length = bars.shape
    width = weight.shape[0]
    tile = width // 2
    quarter = pl.BlockSpec((2, 2, token_rows, tile), lambda i, at: (0, 0, 0, i))
    return pl.pallas_call(
        project_back_kernel,
        grid_spec=pltpu.PrefetchScalarGridSpec(
            num_scalar_prefetch=1,
            grid=(2,),
            in_specs=[
                pl.BlockSpec((columns, length), lambda i, at: (0, 0)),
                pl.BlockSpec((tile, columns), lambda i, at: (i, 0)),
                pl.BlockSpec((length, tile), lambda i, at: (0, i)),
            ],
            out_specs=[quarter, quarter, pl.BlockSpec((tile, columns), lambda i, at: (i, 0))],
            scratch_shapes=[pltpu.VMEM((length, columns), BF16)],
        ),
        out_shape=[
            pltpu.HBM((2, 2, token_rows, width), F32),
            pltpu.HBM((2, 2, token_rows, width), BF16),
            pltpu.HBM((width, columns), BF16),
        ],
        compiler_params=KERNEL,
        cost_estimate=lasting(11),
    )(place(), *in_hbm(bars, weight, normed))


def tied(*arrays):
    return lax.optimization_barrier(arrays)


def swapped(array, axis, mask):
    size = lax.axis_size(axis)
    return lax.ppermute(array, axis, [(i, i ^ mask) for i in range(size)])


def pick(array, index, axis=0):
    return lax.dynamic_index_in_dim(array, index, axis, keepdims=False)


def swap_halves(array):
    me = lax.axis_index("blk")
    got = swapped(pick(array, 1 - me), "blk", 1)
    kept = pick(array, me)
    return jnp.stack([jnp.where(me == 0, kept, got), jnp.where(me == 0, got, kept)])


def scatter_row(halves):
    row = lax.axis_index("head") // 2
    got = swapped(pick(halves, 1 - row, 1).astype(BF16), "head", 2).astype(F32)
    return (pick(halves, row, 1) + got).reshape(-1, halves.shape[-1])


def over_head(parts):
    return lax.all_to_all(parts, "head", split_axis=0, concat_axis=0, tiled=True)


def qkv_columns(rows, extra):
    own, width = rows.shape
    part = width // 3 // 4
    sent = rows.reshape(own, 3, 4, part).transpose(2, 0, 1, 3).reshape(4, own, 3 * part)
    if extra is not None:
        sent = jnp.concatenate([sent, jnp.broadcast_to(extra[None], (4,) + extra.shape)], axis=2)
    return over_head(sent)


def along_batch(piece):
    return lax.all_gather(piece, "batch", axis=0, tiled=False)


def other_core(array):
    return swapped(array, "head", 1)


def to_beside(across):
    return swapped(across[..., : across.shape[-1] // 2], "head", 2)


def to_across(beside):
    return swapped(beside[..., beside.shape[-1] // 2 :], "blk", 1)


def over_batch(parts):
    return lax.psum_scatter(parts.astype(BF16), "batch", scatter_dimension=0, tiled=False)


def across_sum(halves):
    blk = lax.axis_index("blk")
    got = swapped(pick(halves, 1 - blk), "blk", 1).astype(F32)
    return (pick(halves, blk).astype(F32) + got).astype(BF16)


def columns_to_rows(summed):
    moved = over_head(summed.reshape(4, -1, summed.shape[-1]))
    rows = moved.shape[1]
    return moved.reshape(4, rows, 3, -1).transpose(1, 2, 0, 3).reshape(rows, -1).astype(F32)


def diagonal_rows(cored):
    blk, row = place()[:2]
    rows = pick(pick(cored, 1 - blk), 1 - row)
    half = rows.shape[-1] // 2
    return rows[..., :half], rows[..., half:]


def neighbour_rows(cored, one, two):
    blk, row = place()[:2]
    half = one.shape[-1]
    across = pick(pick(cored, 1 - blk), row)
    beside = pick(pick(cored, blk), 1 - row)
    across = jnp.concatenate(
        [across[..., :half], across[..., half:].astype(F32) + two.astype(F32)], axis=-1
    ).astype(BF16)
    beside = jnp.concatenate(
        [beside[..., :half].astype(F32) + one.astype(F32), beside[..., half:]], axis=-1
    ).astype(BF16)
    return across, beside


def sent_beside_and_across(across, beside):
    return swapped(across, "blk", 1), swapped(beside, "head", 2)


def own_sum(cored, across, beside):
    blk, row = place()[:2]
    own = pick(pick(cored, blk), row)
    return own.astype(F32) + across.astype(F32) + beside.astype(F32)


def sum_all(array):
    for axis, mask in (("head", 1), ("head", 2), ("blk", 1), ("batch", 1), ("batch", 2)):
        array = array + swapped(array, axis, mask)
    return array


def gain_back(weight, weight_grad, gain):
    return jnp.sum(weight.astype(F32) * weight_grad, axis=-1) / gain.astype(F32)


def lower_of(upper, stream, factor, gain):
    return norm_back(upper, stream, factor, gain)[0]


def spread_device(
    tokens,
    segments,
    qkv_weight,
    out_weight,
    up_weight,
    down_weight,
    attn_gain,
    mlp_gain,
    scale_param,
    cotangent,
):
    layers, head_dim = scale_param.shape
    _, token_rows, width = tokens.shape
    scale_vecs = SCALE_BASE / math.sqrt(head_dim) * jax.nn.softplus(scale_param)
    segments = pick(segments, lax.axis_index("blk"))
    own_gains = jnp.concatenate([attn_gain, mlp_gain], axis=0)

    part3 = 3 * width // 4
    dense_own = [
        jnp.concatenate([out_weight[i], up_weight[i], down_weight[i]], axis=1) for i in (0, 1)
    ]

    first = swap_halves(tokens).reshape(-1, width)
    dense_near = along_batch(dense_own[0])
    columns = qkv_columns(qkv_weight[0], own_gains.T)
    columns, first = tied(columns.reshape(-1, columns.shape[-1]), first)
    stream = first.astype(F32)
    along = [columns] + [swapped(columns, "batch", mask) for mask in (1, 2, 3)]
    far, near = swapped(first, "head", 2), other_core(first)
    far, along = tied(far, along)
    both = other_core(far)
    next_columns = qkv_columns(qkv_weight[1], None).reshape(-1, part3)
    along, dense_near, near, both, next_columns = tied(
        along, dense_near, near, both, next_columns
    )
    token_pieces = (first, near, far, both)
    along = jnp.stack(along)
    qkv_across = swapped(along, "blk", 1)
    beside = swapped(dense_near, "head", 2)
    next_along = along_batch(next_columns)
    qkv_across, dense_near, beside = tied(qkv_across, dense_near, beside)
    across = swapped(dense_near, "blk", 1)
    weight, gains = assemble_columns(along, qkv_across, part3, True)
    qkvs = [weight]
    gains = gains.T.astype(F32)

    kept, denses = [], []
    for layer in range(layers):
        normed, factor_one = normalize(stream, gains[layer])
        if layer == 1:
            normed, beside, next_across, dense_after = tied(
                normed.astype(BF16), beside, next_across, dense_next
            )
            far, near = swapped(normed, "head", 2), other_core(normed)
            across = swapped(dense_after, "blk", 1)
            token_pieces = (normed, near, far, other_core(far))
            qkvs.append(assemble_columns(next_along, next_across, part3, False)[0])
        normed_all, projected = project(
            token_pieces, gains[layer], qkvs[layer], layer == 0, token_rows
        )
        if layer == 0:
            projected, next_along, dense_next = tied(projected, next_along, dense_own[1])
            dense_next = along_batch(dense_next)
        else:
            projected, across, beside = tied(projected, across, beside)
            one, two = to_beside(across), to_across(beside)
        attended, log_total = attend_rows(
            projected, scale_vecs[layer], segments, 4, token_rows
        )
        if layer == 0:
            attended, across = tied(attended, across)
            one, two = to_beside(across), to_across(beside)
            pieces = (dense_near, across, beside, one, two)
            swaps = tuple(other_core(piece) for piece in pieces)
            attended_t, swaps, one, two, next_along, dense_next = tied(
                over_head(attended), swaps, one, two, next_along, dense_next
            )
            pieces = pieces[:3] + (one, two) + swaps
            next_across = swapped(next_along, "blk", 1)
            beside = swapped(dense_next, "head", 2)
        else:
            attended, one, two = tied(attended, one, two)
            pieces = (dense_next, across, beside, one, two)
            swaps = tuple(other_core(piece) for piece in pieces)
            attended_t, swaps, cotangent = tied(over_head(attended), swaps, cotangent)
            pieces += swaps
            upper = swap_halves(cotangent)
        attended_t = attended_t.reshape(width, -1)
        denses.append(assemble(pieces))
        dense = denses[layer]
        out_w, up_w, down_w = dense[:, :width], dense[:, width:-width], dense[:, -width:]
        middle = stream + dot_rows(attended_t, out_w)
        normed_two, factor_two = normalize(middle, gains[layers + layer])
        normed_two = normed_two.astype(BF16)
        hidden = dot(normed_two, up_w)
        active = (hidden * jax.nn.sigmoid(hidden)).astype(BF16)
        kept.append(
            (
                stream, factor_one, normed_all, projected, log_total, attended_t, middle,
                factor_two, normed_two, hidden, active,
            )
        )
        stream = middle + dot(active, down_w)
    layer_out = swap_halves(stream.astype(BF16).reshape(tokens.shape))
    upper = upper.reshape(-1, width).astype(F32)

    scale_grads = [None] * layers
    for layer in reversed(range(layers)):
        (
            stream, factor_one, normed_all, projected, log_total, attended_t, middle,
            factor_two, normed_two, hidden, active,
        ) = kept[layer]
        qkv, dense = qkvs[layer], denses[layer]
        out_w, up_w, down_w = dense[:, :width], dense[:, width:-width], dense[:, -width:]
        down_bar = upper.astype(BF16)
        gate = jax.nn.sigmoid(hidden)
        up_bar = (
            dot_cols(down_bar, down_w) * gate * (1.0 + hidden * (1.0 - gate))
        ).astype(BF16)
        middle_grad = upper + lower_of(
            dot_cols(up_bar, up_w), middle, factor_two, gains[layers + layer]
        )
        out_bar = middle_grad.astype(BF16)
        if layer == 0:
            out_bar, diagonal = tied(out_bar, diagonal)
            out_bar, rows = tied(out_bar, neighbour_rows(cored, *diagonal))
            sent = sent_beside_and_across(*rows)
        attended_grad = over_head(dot_cols(out_w, out_bar).astype(BF16).reshape(4, -1, out_bar.shape[0]))
        grads, others = dense_grads(attended_t, normed_two, active, out_bar, up_bar, down_bar)
        if layer == 0:
            attended_grad, others, z_sum = tied(attended_grad, others, z_sum)
            z_across = across_sum(z_sum)
        else:
            attended_grad, others, layer_out = tied(attended_grad, others, layer_out)
        others = other_core(others)
        bars, scale_grads[layer] = attend_back_rows(
            projected, attended_grad, log_total, scale_vecs[layer], segments, token_rows
        )
        if layer == 0:
            bars, others, sent = tied(bars, others, sent)
            summed = own_sum(cored, *sent)
        else:
            bars, others = tied(bars, others)
        cored = (grads.astype(F32) + others.astype(F32)).astype(BF16)
        if layer == 0:
            bars, summed, rows = tied(bars, summed, diagonal_rows(cored))
            diagonal = sent_beside_and_across(*rows)
            summed = over_batch(summed)
        halves, to_core, qkv_grad = project_back(bars, qkv, normed_all, token_rows)
        halves = halves + other_core(to_core).astype(F32)
        z_sum = over_batch(qkv_grad.reshape(4, 2, -1, qkv_grad.shape[-1]))
        if layer == 0:
            halves, diagonal = tied(halves, diagonal)
            halves, rows = tied(halves, neighbour_rows(cored, *diagonal))
            sent = sent_beside_and_across(*rows)
            normed_grad = scatter_row(halves)
            normed_grad, sent, summed, z_across = tied(normed_grad, sent, summed, z_across)
            dense_grad = [over_batch(own_sum(cored, *sent)), summed]
            qkv_grads = [columns_to_rows(across_sum(z_sum)), columns_to_rows(z_across)]
        else:
            normed_grad = scatter_row(halves)
            normed_grad, cored = tied(normed_grad, cored)
            diagonal = sent_beside_and_across(*diagonal_rows(cored))
        upper = middle_grad + lower_of(normed_grad, stream, factor_one, gains[layer])
    input_grad = swap_halves(upper.astype(BF16).reshape(tokens.shape)).astype(F32)
    scale_total = sum_all(jnp.stack(scale_grads))
    scale_grad = scale_total * (SCALE_BASE / math.sqrt(head_dim)) * jax.nn.sigmoid(scale_param)
    dense_all = jnp.stack([part.astype(F32) for part in dense_grad])
    qkv_all = jnp.stack(qkv_grads)
    up_all = dense_all[:, :, width:-width]
    return (
        layer_out,
        input_grad,
        qkv_all,
        dense_all[:, :, :width],
        up_all,
        dense_all[:, :, -width:],
        gain_back(qkv_weight, qkv_all, attn_gain),
        gain_back(up_weight, up_all, mlp_gain),
        scale_grad,
    )


def per_device(*args):
    tokens, segments = args[0], args[1]
    sizes = tuple(lax.axis_size(axis) for axis in ALL)
    heads = tokens.shape[2] // args[8].shape[1]
    spread = (
        sizes == (4, 2, 4)
        and tokens.shape[0] == 2
        and args[2].shape[0] == 2
        and tokens.shape[1] % 128 == 0
        and Q_ROWS % tokens.shape[1] == 0
        and segments.shape[1] <= WINDOW
        and segments.shape[1] % Q_ROWS == 0
        and heads % 4 == 0
        and tokens.shape[2] % 256 == 0
    )
    return spread_device(*args) if spread else general_device(*args)


def solution(mesh):
    rows = P(None, ALL, None)
    by_token = P("batch", ("blk", "head"), None)
    return jax.shard_map(
        per_device,
        mesh=mesh,
        in_specs=(
            by_token, P("batch", None), rows, rows, rows, rows, P(None, ALL), P(None, ALL), P(),
            by_token,
        ),
        out_specs=(
            by_token, by_token, rows, rows, rows, rows, P(None, ALL), P(None, ALL), P(),
        ),
        check_vma=False,
    )
```

```python
import functools
import math

import jax
import jax.numpy as jnp
from jax import lax
from jax.experimental import pallas as pl
from jax.experimental.pallas import tpu as pltpu
from jax.sharding import PartitionSpec as P

WINDOW = 1024
EPSILON = 1e-06
SCALE_BASE = 1.4426950408889634
MASKED_SCORE = -1e30

ALL = ("batch", "blk", "head")
REST = ("batch", "blk")
F32 = jnp.float32
BF16 = jnp.bfloat16


def shifted(block, axis, distance):
    devices = range(lax.axis_size(axis))
    route = [(i - distance, i) for i in devices if i - distance in devices]
    return lax.ppermute(block, axis, route)


NT = (((1,), (1,)), ((), ()))
TN = (((0,), (0,)), ((), ()))


def dot(left, right):
    return jnp.dot(left, right, preferred_element_type=F32)


def dot_rows(left, right):
    return lax.dot_general(left, right, (((0,), (0,)), ((), ())), preferred_element_type=F32)


def dot_cols(left, right):
    return lax.dot_general(left, right, (((1,), (1,)), ((), ())), preferred_element_type=F32)


def normalize(stream, gain):
    factor = lax.rsqrt(jnp.mean(stream * stream, axis=-1, keepdims=True) + EPSILON)
    return stream * factor * gain, factor


def norm_back(upper, stream, factor, gain):
    inner = upper * gain
    gain_grad = jnp.sum(upper * stream * factor, axis=0)
    lower = factor * inner - stream * factor * factor * factor * jnp.mean(
        inner * stream, axis=-1, keepdims=True
    )
    return lower, gain_grad


class Plan:
    def __init__(self, tokens):
        self.seqs, self.rows, self.width = tokens.shape
        self.heads = lax.axis_size("head")
        self.blks = lax.axis_size("blk")
        self.block = self.rows * self.heads
        self.whole = self.seqs % self.blks == 0
        if self.whole:
            self.groups, self.own_seqs = self.blks, self.seqs // self.blks
            self.reach = 0
        else:
            self.groups, self.own_seqs = 1, self.seqs
            self.reach = min((WINDOW - 1) // self.block + 1, self.blks - 1)
        self.length = self.groups * self.block
        self.tokens = self.seqs * self.rows


def to_plan(plan, array):
    if plan.whole and plan.blks > 1:
        array = lax.all_to_all(array, "blk", split_axis=0, concat_axis=0, tiled=True)
    return array.reshape(plan.tokens, plan.width)


def from_plan(plan, flat):
    array = flat.reshape(plan.seqs, plan.rows, plan.width)
    if plan.whole and plan.blks > 1:
        array = lax.all_to_all(array, "blk", split_axis=0, concat_axis=0, tiled=True)
    return array


def in_sequence(plan, by_head, width):
    parts = by_head.reshape(plan.heads, plan.groups, plan.own_seqs, plan.rows, width)
    return parts.transpose(2, 1, 0, 3, 4).reshape(-1, width)


def by_owner(plan, rows, width):
    parts = rows.reshape(plan.own_seqs, plan.groups, plan.heads, plan.rows, width)
    return parts.transpose(2, 1, 0, 3, 4).reshape(plan.heads, plan.tokens, width)


def gather_tokens(plan, rows):
    moved = lax.all_gather(rows, "head", axis=0, tiled=False)
    return in_sequence(plan, moved, rows.shape[-1])


def scatter_tokens(plan, rows):
    width = rows.shape[-1]
    return lax.psum_scatter(
        by_owner(plan, rows.astype(BF16), width), "head", scatter_dimension=0, tiled=False
    ).astype(F32)


def heads_to_tokens(plan, rows):
    part = rows.shape[-1]
    moved = lax.all_to_all(
        by_owner(plan, rows, part), "head", split_axis=0, concat_axis=0, tiled=True
    )
    return moved.transpose(1, 0, 2).reshape(plan.tokens, plan.heads * part)


def tokens_to_heads(plan, rows):
    part = rows.shape[-1] // plan.heads
    sent = rows.reshape(plan.tokens, plan.heads, part).transpose(1, 0, 2)
    moved = lax.all_to_all(sent, "head", split_axis=0, concat_axis=0, tiled=True)
    return in_sequence(plan, moved, part)


def gather_qkv(rows):
    own, width = rows.shape
    heads = lax.axis_size("head")
    part = width // 3 // heads
    sent = rows.reshape(own, 3, heads, part).transpose(2, 0, 1, 3).reshape(heads, own, 3 * part)
    moved = lax.all_to_all(sent, "head", split_axis=0, concat_axis=0, tiled=True)
    full = lax.all_gather(moved, REST, axis=0, tiled=True)
    return full.reshape(-1, 3 * part)


def scatter_qkv(grad):
    heads = lax.axis_size("head")
    part = grad.shape[1] // 3
    summed = lax.psum_scatter(grad.astype(BF16), REST, scatter_dimension=0, tiled=True)
    own = summed.shape[0] // heads
    moved = lax.all_to_all(
        summed.reshape(heads, own, 3 * part), "head", split_axis=0, concat_axis=0, tiled=True
    )
    return (
        moved.reshape(heads, own, 3, part)
        .transpose(1, 2, 0, 3)
        .reshape(own, 3 * heads * part)
        .astype(F32)
    )


def window_mask(plan, segments, block_index):
    key_count = plan.length + plan.reach * plan.block
    if plan.whole:
        query_segs, key_segs = segments, segments
    else:
        leading = jnp.full((plan.own_seqs, plan.reach * plan.block), -1, jnp.int32)
        padded = jnp.concatenate([leading, segments], axis=1)
        start = block_index * plan.block
        query_segs = lax.dynamic_slice_in_dim(segments, start, plan.block, 1)
        key_segs = lax.dynamic_slice_in_dim(padded, start, key_count, 1)
    query_place = jnp.arange(plan.length, dtype=jnp.int32)[:, None] + plan.reach * plan.block
    key_place = jnp.arange(key_count, dtype=jnp.int32)[None, :]
    near = (key_place <= query_place) & (query_place - key_place < WINDOW)
    return (key_segs[:, None, :] == query_segs[:, :, None]) & near[None]


def with_earlier(plan, own):
    arrived = [own]
    for _ in range(plan.reach):
        arrived.append(shifted(arrived[-1], "blk", 1))
    return jnp.concatenate(arrived[::-1], axis=1) if plan.reach else own


def to_earlier(plan, grads):
    if not plan.reach:
        return grads
    block = plan.block
    total = grads[:, :block]
    for step in range(1, plan.reach + 1):
        total = (
            shifted(total.astype(BF16), "blk", -1).astype(F32)
            + grads[:, step * block : (step + 1) * block]
        )
    return total


def scores_of(queries, keys, allowed):
    scores = jnp.einsum("sqhd,skhd->shqk", queries, keys, preferred_element_type=F32)
    return jnp.where(allowed[:, None], scores, MASKED_SCORE)


def attend(queries, keys, values, allowed):
    scores = scores_of(queries, keys, allowed)
    top_score = jnp.max(scores, axis=-1, keepdims=True)
    exp_terms = jnp.exp(scores - top_score)
    totals = jnp.sum(exp_terms, axis=-1, keepdims=True)
    probs_low = (exp_terms / totals).astype(BF16)
    attended = jnp.einsum("shqk,skhd->sqhd", probs_low, values, preferred_element_type=F32)
    return attended, top_score + jnp.log(totals)


def attend_back(queries, keys, values, allowed, log_total, attended_grad):
    probs = jnp.exp(scores_of(queries, keys, allowed) - log_total)
    probs_low = probs.astype(BF16)
    values_grad = jnp.einsum(
        "shqk,sqhd->skhd", probs_low, attended_grad, preferred_element_type=F32
    )
    probs_grad = jnp.einsum("sqhd,skhd->shqk", attended_grad, values, preferred_element_type=F32)
    row_dot = jnp.sum(probs_grad * probs, axis=-1, keepdims=True)
    scores_low = (probs * (probs_grad - row_dot)).astype(BF16)
    queries_grad = jnp.einsum("shqk,skhd->sqhd", scores_low, keys, preferred_element_type=F32)
    keys_grad = jnp.einsum("shqk,sqhd->skhd", scores_low, queries, preferred_element_type=F32)
    return queries_grad, keys_grad, values_grad


def forward(plan, stream, qkv, dense, gains, scale_vec, allowed):
    width = plan.width
    head_dim = scale_vec.shape[0]
    part = qkv.shape[1] // 3
    local_heads = part // head_dim
    split = (plan.own_seqs, plan.length, local_heads, head_dim)
    out_w, up_w, down_w = dense[:, :width], dense[:, width:-width], dense[:, -width:]
    normed, factor_one = normalize(stream, gains[0])
    normed_all = gather_tokens(plan, normed.astype(BF16))
    projected = dot(normed_all, qkv)
    query_pre = projected[:, :part].reshape(split)
    queries = (query_pre * scale_vec).astype(BF16)
    keys = with_earlier(plan, projected[:, part : 2 * part].astype(BF16).reshape(split))
    values = with_earlier(plan, projected[:, 2 * part :].astype(BF16).reshape(split))
    attended_part, log_total = attend(queries, keys, values, allowed)
    attended = heads_to_tokens(plan, attended_part.astype(BF16).reshape(-1, part))
    middle = stream + dot(attended, out_w)
    normed_two, factor_two = normalize(middle, gains[1])
    normed_two = normed_two.astype(BF16)
    hidden = dot(normed_two, up_w)
    active = (hidden * jax.nn.sigmoid(hidden)).astype(BF16)
    result = middle + dot(active, down_w)
    kept = (
        stream, factor_one, normed_all, query_pre, queries, keys, values, log_total,
        attended, middle, factor_two, normed_two, hidden, active,
    )
    return result, kept


def backward(plan, upper, kept, qkv, dense, gains, scale_vec, allowed):
    (
        stream, factor_one, normed_all, query_pre, queries, keys, values, log_total,
        attended, middle, factor_two, normed_two, hidden, active,
    ) = kept
    width = plan.width
    head_dim = scale_vec.shape[0]
    part = qkv.shape[1] // 3
    out_w, up_w, down_w = dense[:, :width], dense[:, width:-width], dense[:, -width:]
    upper_low = upper.astype(BF16)
    down_grad = dot_rows(active, upper_low)
    active_grad = dot_cols(upper_low, down_w)
    gate = jax.nn.sigmoid(hidden)
    hidden_low = (active_grad * gate * (1.0 + hidden * (1.0 - gate))).astype(BF16)
    up_grad = dot_rows(normed_two, hidden_low)
    extra_two, mlp_gain_grad = norm_back(dot_cols(hidden_low, up_w), middle, factor_two, gains[1])
    middle_grad = upper + extra_two
    middle_low = middle_grad.astype(BF16)
    out_grad = dot_rows(attended, middle_low)
    dense_grad = jnp.concatenate([out_grad, up_grad, down_grad], axis=1).astype(BF16)
    dense_own = lax.psum_scatter(dense_grad, ALL, scatter_dimension=0, tiled=True)
    attended_grad = tokens_to_heads(plan, dot_cols(middle_low, out_w).astype(BF16))
    queries_grad, keys_grad, values_grad = attend_back(
        queries, keys, values, allowed, log_total, attended_grad.reshape(queries.shape)
    )
    query_bar = queries_grad.astype(BF16).astype(F32)
    scale_vec_grad = jnp.sum((query_bar * query_pre).reshape(-1, head_dim), axis=0)
    query_low = (query_bar * scale_vec).astype(BF16).reshape(-1, part)
    keys_low = to_earlier(plan, keys_grad).astype(BF16).reshape(-1, part)
    values_low = to_earlier(plan, values_grad).astype(BF16).reshape(-1, part)
    projected_low = jnp.concatenate([query_low, keys_low, values_low], axis=1)
    normed_grad = scatter_tokens(plan, dot_cols(projected_low, qkv))
    qkv_own = scatter_qkv(dot_rows(normed_all, projected_low))
    extra_one, attn_gain_grad = norm_back(normed_grad, stream, factor_one, gains[0])
    lower = middle_grad + extra_one
    return lower, qkv_own, dense_own, (attn_gain_grad, mlp_gain_grad), scale_vec_grad


def general_device(
    tokens,
    segments,
    qkv_weight,
    out_weight,
    up_weight,
    down_weight,
    attn_gain,
    mlp_gain,
    scale_param,
    cotangent,
):
    plan = Plan(tokens)
    layers, head_dim = scale_param.shape
    block_index = lax.axis_index("blk")
    scale_vecs = SCALE_BASE / math.sqrt(head_dim) * jax.nn.softplus(scale_param)
    own_gains = jnp.concatenate([attn_gain, mlp_gain], axis=0)
    gains = (
        lax.all_gather(own_gains.reshape(1, -1), ALL, axis=0, tiled=True)
        .reshape(-1, 2 * layers, attn_gain.shape[1])
        .transpose(1, 0, 2)
        .reshape(2 * layers, plan.width)
        .astype(F32)
    )
    if plan.whole:
        segments = lax.dynamic_slice_in_dim(
            segments, block_index * plan.own_seqs, plan.own_seqs, 0
        )
    allowed = window_mask(plan, segments, block_index)
    stream = to_plan(plan, tokens).astype(F32)
    qkvs, denses, kept = [], [], []
    for layer in range(layers):
        qkvs.append(gather_qkv(qkv_weight[layer]))
        own = jnp.concatenate([out_weight[layer], up_weight[layer], down_weight[layer]], axis=1)
        denses.append(lax.all_gather(own, ALL, axis=0, tiled=True))
        layer_gains = (gains[layer], gains[layers + layer])
        stream, saved = forward(
            plan, stream, qkvs[layer], denses[layer], layer_gains, scale_vecs[layer], allowed
        )
        kept.append(saved)
    layer_out = from_plan(plan, stream.astype(BF16))
    upper = to_plan(plan, cotangent).astype(F32)
    qkv_grads, dense_grads = [None] * layers, [None] * layers
    gain_grads, scale_grads = [None] * layers, [None] * layers
    for layer in reversed(range(layers)):
        layer_gains = (gains[layer], gains[layers + layer])
        upper, qkv_grads[layer], dense_grads[layer], gain_grads[layer], scale_grads[layer] = (
            backward(
                plan, upper, kept[layer], qkvs[layer], denses[layer], layer_gains,
                scale_vecs[layer], allowed,
            )
        )
    input_grad = from_plan(plan, upper.astype(BF16)).astype(F32)
    small = jnp.concatenate(
        [g[0] for g in gain_grads] + [g[1] for g in gain_grads] + scale_grads, axis=0
    )
    total = lax.psum(small, ALL)
    gain_total = total[: 2 * layers * plan.width].reshape(2 * layers, plan.width)
    owner = lax.axis_index(ALL)
    gain_rows = attn_gain.shape[1]
    own_total = lax.dynamic_slice_in_dim(gain_total, owner * gain_rows, gain_rows, 1)
    scale_total = total[2 * layers * plan.width :].reshape(layers, head_dim)
    scale_grad = scale_total * (SCALE_BASE / math.sqrt(head_dim)) * jax.nn.sigmoid(scale_param)
    dense_all = jnp.stack(dense_grads).astype(F32)
    width = plan.width
    return (
        layer_out,
        input_grad,
        jnp.stack(qkv_grads),
        dense_all[:, :, :width],
        dense_all[:, :, width:-width],
        dense_all[:, :, -width:],
        own_total[:layers],
        own_total[layers:],
        scale_grad,
    )


Q_ROWS = 256
KERNEL = pltpu.CompilerParams(vmem_limit_bytes=32 * 1024 * 1024)
LIGHT = pl.CostEstimate(flops=1 << 20, bytes_accessed=1 << 20, transcendentals=0)


def in_hbm(*arrays):
    return [pltpu.with_memory_space_constraint(array, pltpu.HBM) for array in arrays]


def allowed_keys(col, row, first):
    count = first + row.shape[1]
    key_place = lax.broadcasted_iota(jnp.int32, (count, row.shape[1]), 0)
    query_place = lax.broadcasted_iota(jnp.int32, (count, row.shape[1]), 1) + first
    return (col[:count] == row) & (key_place <= query_place)


def token_places(length, heads, token_rows):
    for first in range(0, length, Q_ROWS):
        parts = []
        for start in range(0, Q_ROWS, token_rows):
            place = (first + start) // token_rows
            parts.append((start, place % heads, place // heads * token_rows))
        yield first, parts


def attend_kernel(token_rows, proj_ref, scale_ref, col_ref, row_ref, out_ref, lse_ref):
    length = proj_ref.shape[-1]
    queries = (proj_ref[0, 0] * scale_ref[...]).astype(BF16)
    keys = proj_ref[1, 0].T.astype(BF16)
    values = proj_ref[2, 0].astype(BF16)
    for first, parts in token_places(length, out_ref.shape[0], token_rows):
        end = first + Q_ROWS
        scores = jnp.dot(keys[:end], queries[:, first:end], preferred_element_type=F32)
        allowed = allowed_keys(col_ref[...], row_ref[:, first:end], first)
        scores = jnp.where(allowed, scores, MASKED_SCORE)
        top = jnp.max(scores, axis=0, keepdims=True)
        terms = jnp.exp(scores - top)
        total = jnp.sum(terms, axis=0, keepdims=True)
        probs = (terms * (1.0 / total)).astype(BF16)
        attended = jnp.dot(values[:, :end], probs, preferred_element_type=F32).astype(BF16)
        lse_ref[0, :, first:end] = top + jnp.log(total)
        for start, owner, offset in parts:
            out_ref[owner, 0, :, offset : offset + token_rows] = attended[
                :, start : start + token_rows
            ]


def attend_rows(projected, scale_vec, segments, owners, token_rows):
    head_dim = scale_vec.shape[0]
    length = projected.shape[1]
    local_heads = projected.shape[0] // 3 // head_dim
    tokens = length // owners
    attended, log_total = pl.pallas_call(
        functools.partial(attend_kernel, token_rows),
        grid=(local_heads,),
        in_specs=[
            pl.BlockSpec((3, 1, head_dim, length), lambda h: (0, h, 0, 0)),
            pl.BlockSpec((head_dim, 1), lambda h: (0, 0)),
            pl.BlockSpec((length, 1), lambda h: (0, 0)),
            pl.BlockSpec((1, length), lambda h: (0, 0)),
        ],
        out_specs=[
            pl.BlockSpec((owners, 1, head_dim, tokens), lambda h: (0, h, 0, 0)),
            pl.BlockSpec((1, 1, length), lambda h: (h, 0, 0)),
        ],
        out_shape=[
            jax.ShapeDtypeStruct((owners, local_heads, head_dim, tokens), BF16),
            jax.ShapeDtypeStruct((local_heads, 1, length), F32),
        ],
        compiler_params=KERNEL,
        cost_estimate=LIGHT,
    )(
        projected.reshape(3, local_heads, head_dim, length),
        scale_vec.reshape(head_dim, 1),
        segments.reshape(length, 1),
        segments.reshape(1, length),
    )
    return attended.reshape(owners, local_heads * head_dim, tokens), log_total


def attend_back_kernel(
    token_rows,
    proj_ref,
    grad_ref,
    lse_ref,
    scale_ref,
    col_ref,
    row_ref,
    out_ref,
    scale_grad_ref,
    keys_acc,
    values_acc,
):
    length = proj_ref.shape[-1]
    scale = scale_ref[...]
    query_pre = proj_ref[0, 0]
    queries = (query_pre * scale).astype(BF16)
    keys_t = proj_ref[1, 0].astype(BF16)
    keys = proj_ref[1, 0].T.astype(BF16)
    values = proj_ref[2, 0].T.astype(BF16)
    keys_acc[...] = jnp.zeros_like(keys_acc)
    values_acc[...] = jnp.zeros_like(values_acc)
    scale_grad = jnp.zeros((scale.shape[0], 1), F32)
    for first, parts in token_places(length, grad_ref.shape[0], token_rows):
        end = first + Q_ROWS
        block = queries[:, first:end]
        grad = jnp.concatenate(
            [grad_ref[owner, 0, :, at : at + token_rows] for _, owner, at in parts], axis=1
        )
        scores = jnp.dot(keys[:end], block, preferred_element_type=F32)
        allowed = allowed_keys(col_ref[...], row_ref[:, first:end], first)
        scores = jnp.where(allowed, scores, MASKED_SCORE)
        probs = jnp.exp(scores - lse_ref[0, :, first:end])
        probs_grad = jnp.dot(values[:end], grad, preferred_element_type=F32)
        row_dot = jnp.sum(probs_grad * probs, axis=0, keepdims=True)
        scores_low = (probs * (probs_grad - row_dot)).astype(BF16)
        values_acc[:, :end] += lax.dot_general(
            grad, probs.astype(BF16), NT, preferred_element_type=F32
        )
        keys_acc[:, :end] += lax.dot_general(
            block, scores_low, NT, preferred_element_type=F32
        )
        query_bar = jnp.dot(keys_t[:, :end], scores_low, preferred_element_type=F32)
        query_bar = query_bar.astype(BF16).astype(F32)
        scale_grad += jnp.sum(query_bar * query_pre[:, first:end], axis=1, keepdims=True)
        out_ref[0, 0, :, first:end] = (query_bar * scale).astype(BF16)
    out_ref[1, 0] = keys_acc[...].astype(BF16)
    out_ref[2, 0] = values_acc[...].astype(BF16)
    spread = jnp.broadcast_to(scale_grad, scale_grad_ref.shape)

    @pl.when(pl.program_id(0) == 0)
    def _():
        scale_grad_ref[...] = spread

    @pl.when(pl.program_id(0) > 0)
    def _():
        scale_grad_ref[...] += spread


def attend_back_rows(projected, attended_grad, log_total, scale_vec, segments, token_rows):
    head_dim = scale_vec.shape[0]
    length = projected.shape[1]
    local_heads = projected.shape[0] // 3 // head_dim
    owners, _, tokens = attended_grad.shape
    lanes = 128
    grads, scale_grad = pl.pallas_call(
        functools.partial(attend_back_kernel, token_rows),
        grid=(local_heads,),
        in_specs=[
            pl.BlockSpec((3, 1, head_dim, length), lambda h: (0, h, 0, 0)),
            pl.BlockSpec((owners, 1, head_dim, tokens), lambda h: (0, h, 0, 0)),
            pl.BlockSpec((1, 1, length), lambda h: (h, 0, 0)),
            pl.BlockSpec((head_dim, 1), lambda h: (0, 0)),
            pl.BlockSpec((length, 1), lambda h: (0, 0)),
            pl.BlockSpec((1, length), lambda h: (0, 0)),
        ],
        out_specs=[
            pl.BlockSpec((3, 1, head_dim, length), lambda h: (0, h, 0, 0)),
            pl.BlockSpec((head_dim, lanes), lambda h: (0, 0)),
        ],
        out_shape=[
            pltpu.HBM((3, local_heads, head_dim, length), BF16),
            pltpu.HBM((head_dim, lanes), F32),
        ],
        scratch_shapes=[
            pltpu.VMEM((head_dim, length), F32),
            pltpu.VMEM((head_dim, length), F32),
        ],
        compiler_params=KERNEL,
        cost_estimate=LIGHT,
    )(
        *in_hbm(
            projected.reshape(3, local_heads, head_dim, length),
            attended_grad.reshape(owners, local_heads, head_dim, tokens),
        ),
        log_total,
        scale_vec.reshape(head_dim, 1),
        segments.reshape(length, 1),
        segments.reshape(1, length),
    )
    return grads.reshape(3 * local_heads * head_dim, length), scale_grad[:, 0]


def dense_grad_kernel(
    core_ref, attended_ref, normed_ref, active_ref, out_bar, up_bar, down_bar,
    own_ref, other_ref, normed_t, active_t,
):
    tile = pl.program_id(0)
    rows, width = own_ref.shape[1] * own_ref.shape[3] * 2, out_bar.shape[1]

    @pl.when(tile == 0)
    def _():
        normed_t[...] = normed_ref[...].astype(F32).T.astype(BF16)
        active_t[...] = active_ref[...].astype(F32).T.astype(BF16)

    start = pl.multiple_of(tile * rows, rows)
    first_core = core_ref[2] == 0
    lefts = (attended_ref, normed_t, active_t)
    for i, (left, right) in enumerate(zip(lefts, (out_bar, up_bar, down_bar))):
        grad = jnp.dot(left[pl.ds(start, rows), :], right[...], preferred_element_type=F32)
        grad = grad.reshape(2, 2, rows // 4, width)
        one, two = grad[:, 0], grad[:, 1]
        own_ref[0, :, 0, :, i * width : (i + 1) * width] = jnp.where(
            first_core, one, two
        ).astype(BF16)
        other_ref[0, :, 0, :, i * width : (i + 1) * width] = jnp.where(
            first_core, two, one
        ).astype(BF16)


def dense_grads(attended_t, normed, active, out_bar, up_bar, down_bar):
    width, tokens = attended_t.shape
    own = width // 32
    whole = pl.BlockSpec((tokens, width), lambda i, core: (0, 0))
    rows = pl.BlockSpec((1, 2, 1, own, 3 * width), lambda i, core: (i % 2, 0, i // 2, 0, 0))
    shape = pltpu.HBM((2, 2, 4, own, 3 * width), BF16)
    return pl.pallas_call(
        dense_grad_kernel,
        grid_spec=pltpu.PrefetchScalarGridSpec(
            num_scalar_prefetch=1,
            grid=(8,),
            in_specs=[pl.BlockSpec((width, tokens), lambda i, core: (0, 0))] + [whole] * 5,
            out_specs=[rows, rows],
            scratch_shapes=[pltpu.VMEM((width, tokens), BF16)] * 2,
        ),
        out_shape=[shape, shape],
        compiler_params=KERNEL,
        cost_estimate=LIGHT,
    )(place(), *in_hbm(attended_t, normed, active, out_bar, up_bar, down_bar))


def place():
    head = lax.axis_index("head")
    return jnp.stack([lax.axis_index("blk"), head // 2, head % 2]).astype(jnp.int32)


def assemble_kernel(place_ref, *refs):
    pieces, whole_ref = refs[:10], refs[10]
    half = whole_ref.shape[-1] // 2
    blk, row, core = place_ref[0], place_ref[1], place_ref[2]
    for i in range(2):
        at_core = core if i == 0 else 1 - core
        own, across, beside, one, two = pieces[5 * i : 5 * i + 5]
        whole_ref[0, blk, row, at_core] = own[0]
        whole_ref[0, 1 - blk, row, at_core] = across[0]
        whole_ref[0, blk, 1 - row, at_core] = beside[0]
        whole_ref[0, 1 - blk, 1 - row, at_core, :, :half] = one[0]
        whole_ref[0, 1 - blk, 1 - row, at_core, :, half:] = two[0]


def assemble(pieces):
    batch, own, columns = pieces[0].shape
    specs = [
        pl.BlockSpec((1, own, piece.shape[-1]), lambda i, at: (i, 0, 0))
        for piece in pieces
    ]
    whole = pl.pallas_call(
        assemble_kernel,
        grid_spec=pltpu.PrefetchScalarGridSpec(
            num_scalar_prefetch=1,
            grid=(batch,),
            in_specs=specs,
            out_specs=pl.BlockSpec((1, 2, 2, 2, own, columns), lambda i, at: (i, 0, 0, 0, 0, 0)),
        ),
        out_shape=jax.ShapeDtypeStruct((batch, 2, 2, 2, own, columns), BF16),
        compiler_params=KERNEL,
        cost_estimate=LIGHT,
    )(place(), *pieces)
    return whole.reshape(-1, columns)


def assemble_columns_kernel(place_ref, along_ref, across_ref, whole_ref, *extra_ref):
    blk = place_ref[0]
    columns = whole_ref.shape[-1]
    whole_ref[0, blk] = along_ref[0, :, :columns]
    whole_ref[0, 1 - blk] = across_ref[0, :, :columns]
    for extra in extra_ref:
        extra[0, blk] = along_ref[0, :, columns:]
        extra[0, 1 - blk] = across_ref[0, :, columns:]


def assemble_columns(along, across, columns):
    batch, own, both = along.shape
    rows = pl.BlockSpec((1, own, both), lambda i, at: (i, 0, 0))
    shapes = [(batch, 2, own, columns)]
    if both > columns:
        shapes.append((batch, 2, own, both - columns))
    parts = pl.pallas_call(
        assemble_columns_kernel,
        grid_spec=pltpu.PrefetchScalarGridSpec(
            num_scalar_prefetch=1,
            grid=(batch,),
            in_specs=[rows, rows],
            out_specs=[pl.BlockSpec((1,) + s[1:], lambda i, at: (i, 0, 0, 0)) for s in shapes],
        ),
        out_shape=[pltpu.HBM(s, BF16) for s in shapes],
        compiler_params=KERNEL,
        cost_estimate=LIGHT,
    )(place(), *in_hbm(along, across))
    return [part.reshape(-1, part.shape[-1]) for part in parts]


def project_kernel(with_norm, place_ref, *refs):
    pieces, (gain_ref, weight_ref, normed_ref, projected_ref) = refs[:4], refs[4:]
    head = place_ref[1] * 2 + place_ref[2]
    rows = pieces[0].shape[0]
    for i, piece in enumerate(pieces):
        value = piece[...]
        if with_norm:
            stream = value.astype(F32)
            factor = lax.rsqrt(jnp.mean(stream * stream, axis=-1, keepdims=True) + EPSILON)
            value = (stream * factor * gain_ref[...]).astype(BF16)
        normed_ref[pl.ds(pl.multiple_of((head ^ i) * rows, rows), rows), :] = value
    projected = jnp.dot(normed_ref[...], weight_ref[...], preferred_element_type=F32)
    projected_ref[...] = projected.T


def project(pieces, gain, weight, with_norm, token_rows):
    tokens, width = pieces[0].shape
    length, columns = 4 * tokens, weight.shape[1]
    groups = tokens // token_rows
    piece = pl.BlockSpec((token_rows, width), lambda g, at: (g, 0))
    return pl.pallas_call(
        functools.partial(project_kernel, with_norm),
        grid_spec=pltpu.PrefetchScalarGridSpec(
            num_scalar_prefetch=1,
            grid=(groups,),
            in_specs=[piece] * 4
            + [
                pl.BlockSpec((1, width), lambda g, at: (0, 0)),
                pl.BlockSpec((width, columns), lambda g, at: (0, 0)),
            ],
            out_specs=[
                pl.BlockSpec((4 * token_rows, width), lambda g, at: (g, 0)),
                pl.BlockSpec((columns, 4 * token_rows), lambda g, at: (0, g)),
            ],
        ),
        out_shape=[
            pltpu.HBM((length, width), BF16),
            pltpu.HBM((columns, length), F32),
        ],
        compiler_params=KERNEL,
        cost_estimate=LIGHT,
    )(place(), *in_hbm(*pieces), gain.reshape(1, width), *in_hbm(weight))


def project_back_kernel(
    place_ref, bars_ref, weight_ref, normed_ref, own_ref, other_ref, grad_ref, bars_t
):
    @pl.when(pl.program_id(0) == 0)
    def _():
        bars_t[...] = bars_ref[...].astype(F32).T.astype(BF16)

    upper = lax.dot_general(bars_t[...], weight_ref[...], NT, preferred_element_type=F32)
    upper = upper.reshape(2, 2, 2, -1, upper.shape[-1])
    first_core = place_ref[2] == 0
    one, two = upper[:, :, 0], upper[:, :, 1]
    own_ref[...] = jnp.where(first_core, one, two)
    other_ref[...] = jnp.where(first_core, two, one).astype(BF16)
    grad = lax.dot_general(normed_ref[...], bars_t[...], TN, preferred_element_type=F32)
    grad_ref[...] = grad.astype(BF16)


def project_back(bars, weight, normed, token_rows):
    columns, length = bars.shape
    width = weight.shape[0]
    tile = width // 2
    quarter = pl.BlockSpec((2, 2, token_rows, tile), lambda i, at: (0, 0, 0, i))
    return pl.pallas_call(
        project_back_kernel,
        grid_spec=pltpu.PrefetchScalarGridSpec(
            num_scalar_prefetch=1,
            grid=(2,),
            in_specs=[
                pl.BlockSpec((columns, length), lambda i, at: (0, 0)),
                pl.BlockSpec((tile, columns), lambda i, at: (i, 0)),
                pl.BlockSpec((length, tile), lambda i, at: (0, i)),
            ],
            out_specs=[quarter, quarter, pl.BlockSpec((tile, columns), lambda i, at: (i, 0))],
            scratch_shapes=[pltpu.VMEM((length, columns), BF16)],
        ),
        out_shape=[
            pltpu.HBM((2, 2, token_rows, width), F32),
            pltpu.HBM((2, 2, token_rows, width), BF16),
            pltpu.HBM((width, columns), BF16),
        ],
        compiler_params=KERNEL,
        cost_estimate=LIGHT,
    )(place(), *in_hbm(bars, weight, normed))


def rows_back_kernel(place_ref, bars_ref, weight_ref, own_ref, other_ref, bars_t):
    @pl.when(pl.program_id(0) == 0)
    def _():
        bars_t[...] = bars_ref[...].astype(F32).T.astype(BF16)

    upper = lax.dot_general(bars_t[...], weight_ref[...], NT, preferred_element_type=F32)
    upper = upper.reshape(2, 2, 2, -1, upper.shape[-1])
    first_core = place_ref[2] == 0
    one, two = upper[:, :, 0], upper[:, :, 1]
    own_ref[...] = jnp.where(first_core, one, two)
    other_ref[...] = jnp.where(first_core, two, one).astype(BF16)


def rows_back(bars, weight, token_rows):
    columns, length = bars.shape
    width = weight.shape[0]
    tile = width // 2
    quarter = pl.BlockSpec((2, 2, token_rows, tile), lambda i, at: (0, 0, 0, i))
    return pl.pallas_call(
        rows_back_kernel,
        grid_spec=pltpu.PrefetchScalarGridSpec(
            num_scalar_prefetch=1,
            grid=(2,),
            in_specs=[
                pl.BlockSpec((columns, length), lambda i, at: (0, 0)),
                pl.BlockSpec((tile, columns), lambda i, at: (i, 0)),
            ],
            out_specs=[quarter, quarter],
            scratch_shapes=[pltpu.VMEM((length, columns), BF16)],
        ),
        out_shape=[
            pltpu.HBM((2, 2, token_rows, width), F32),
            pltpu.HBM((2, 2, token_rows, width), BF16),
        ],
        compiler_params=KERNEL,
        cost_estimate=LIGHT,
    )(place(), *in_hbm(bars, weight))


def weight_back_kernel(bars_ref, normed_ref, grad_ref):
    grad = jnp.dot(bars_ref[...], normed_ref[...], preferred_element_type=F32)
    grad_ref[...] = grad.T.astype(BF16)


def weight_back(bars, normed):
    columns, length = bars.shape
    width = normed.shape[1]
    tile = width // 5
    return pl.pallas_call(
        weight_back_kernel,
        grid=(5,),
        in_specs=[
            pl.BlockSpec((columns, length), lambda i: (0, 0)),
            pl.BlockSpec((length, tile), lambda i: (0, i)),
        ],
        out_specs=pl.BlockSpec((tile, columns), lambda i: (i, 0)),
        out_shape=pltpu.HBM((width, columns), BF16),
        compiler_params=KERNEL,
        cost_estimate=LIGHT,
    )(*in_hbm(bars, normed))


def tied(*arrays):
    return lax.optimization_barrier(arrays)


def swapped(array, axis, mask):
    size = lax.axis_size(axis)
    return lax.ppermute(array, axis, [(i, i ^ mask) for i in range(size)])


def pick(array, index, axis=0):
    return lax.dynamic_index_in_dim(array, index, axis, keepdims=False)


def swap_halves(array):
    me = lax.axis_index("blk")
    got = swapped(pick(array, 1 - me), "blk", 1)
    kept = pick(array, me)
    return jnp.stack([jnp.where(me == 0, kept, got), jnp.where(me == 0, got, kept)])


def scatter_row(halves):
    row = lax.axis_index("head") // 2
    got = swapped(pick(halves, 1 - row, 1).astype(BF16), "head", 2).astype(F32)
    return (pick(halves, row, 1) + got).reshape(-1, halves.shape[-1])


def over_head(parts):
    return lax.all_to_all(parts, "head", split_axis=0, concat_axis=0, tiled=True)


def qkv_columns(rows, extra):
    own, width = rows.shape
    part = width // 3 // 4
    sent = rows.reshape(own, 3, 4, part).transpose(2, 0, 1, 3).reshape(4, own, 3 * part)
    if extra is not None:
        sent = jnp.concatenate([sent, jnp.broadcast_to(extra[None], (4,) + extra.shape)], axis=2)
    return over_head(sent)


def along_batch(piece):
    return lax.all_gather(piece, "batch", axis=0, tiled=False)


def other_core(array):
    return swapped(array, "head", 1)


def to_beside(across):
    return swapped(across[..., : across.shape[-1] // 2], "head", 2)


def to_across(beside):
    return swapped(beside[..., beside.shape[-1] // 2 :], "blk", 1)


def over_batch(parts):
    return lax.psum_scatter(parts.astype(BF16), "batch", scatter_dimension=0, tiled=False)


def across_sum(halves):
    blk = lax.axis_index("blk")
    got = swapped(pick(halves, 1 - blk), "blk", 1).astype(F32)
    return (pick(halves, blk).astype(F32) + got).astype(BF16)


def columns_to_rows(summed):
    moved = over_head(summed.reshape(4, -1, summed.shape[-1]))
    rows = moved.shape[1]
    return moved.reshape(4, rows, 3, -1).transpose(1, 2, 0, 3).reshape(rows, -1).astype(F32)


def diagonal_rows(cored):
    blk, row = place()[:2]
    rows = pick(pick(cored, 1 - blk), 1 - row)
    half = rows.shape[-1] // 2
    return rows[..., :half], rows[..., half:]


def neighbour_rows(cored, one, two):
    blk, row = place()[:2]
    half = one.shape[-1]
    across = pick(pick(cored, 1 - blk), row)
    beside = pick(pick(cored, blk), 1 - row)
    across = jnp.concatenate(
        [across[..., :half], across[..., half:].astype(F32) + two.astype(F32)], axis=-1
    ).astype(BF16)
    beside = jnp.concatenate(
        [beside[..., :half].astype(F32) + one.astype(F32), beside[..., half:]], axis=-1
    ).astype(BF16)
    return across, beside


def sent_beside_and_across(across, beside):
    return swapped(across, "blk", 1), swapped(beside, "head", 2)


def heads_grad(weight, out_bar):
    return dot_cols(weight, out_bar).astype(BF16).reshape(4, -1, out_bar.shape[0])


def own_sum(cored, across, beside):
    blk, row = place()[:2]
    own = pick(pick(cored, blk), row)
    return own.astype(F32) + across.astype(F32) + beside.astype(F32)


def sum_all(array):
    for axis, mask in (("head", 1), ("head", 2), ("blk", 1), ("batch", 1), ("batch", 2)):
        array = array + swapped(array, axis, mask)
    return array


def gain_back(weight, weight_grad, gain):
    return jnp.sum(weight.astype(F32) * weight_grad, axis=-1) / gain.astype(F32)


def lower_of(upper, stream, factor, gain):
    return norm_back(upper, stream, factor, gain)[0]


def spread_device(
    tokens,
    segments,
    qkv_weight,
    out_weight,
    up_weight,
    down_weight,
    attn_gain,
    mlp_gain,
    scale_param,
    cotangent,
):
    layers, head_dim = scale_param.shape
    _, token_rows, width = tokens.shape
    scale_vecs = SCALE_BASE / math.sqrt(head_dim) * jax.nn.softplus(scale_param)
    segments = pick(segments, lax.axis_index("blk"))
    own_gains = jnp.concatenate([attn_gain, mlp_gain], axis=0)

    part3 = 3 * width // 4
    dense_own = [
        jnp.concatenate([out_weight[i], up_weight[i], down_weight[i]], axis=1) for i in (0, 1)
    ]

    first = swap_halves(tokens).reshape(-1, width)
    columns = qkv_columns(qkv_weight[0], own_gains.T)
    columns, first = tied(columns.reshape(-1, columns.shape[-1]), first)
    stream = first.astype(F32)
    along = along_batch(columns)
    far, near = swapped(first, "head", 2), other_core(first)
    both = other_core(far)
    along, near, far, both, dense_near = tied(along, near, far, both, dense_own[0])
    token_pieces = (first, near, far, both)
    dense_near = along_batch(dense_near)
    qkv_across = swapped(along, "blk", 1)
    next_columns = qkv_columns(qkv_weight[1], None).reshape(-1, part3)
    qkv_across, dense_near, next_columns = tied(qkv_across, dense_near, next_columns)
    across, beside = swapped(dense_near, "blk", 1), swapped(dense_near, "head", 2)
    next_along = along_batch(next_columns)
    weight, gains = assemble_columns(along, qkv_across, part3)
    qkvs = [weight]
    gains = gains.T.astype(F32)

    kept, denses = [], []
    for layer in range(layers):
        normed, factor_one = normalize(stream, gains[layer])
        if layer == 1:
            normed, next_across, dense_next = tied(normed.astype(BF16), next_across, dense_next)
            far, near = swapped(normed, "head", 2), other_core(normed)
            across = swapped(dense_next, "blk", 1)
            far, dense_after = tied(far, dense_next)
            beside = swapped(dense_after, "head", 2)
            token_pieces = (normed, near, far, other_core(far))
            qkvs.append(assemble_columns(next_along, next_across, part3)[0])
        normed_all, projected = project(
            token_pieces, gains[layer], qkvs[layer], layer == 0, token_rows
        )
        attended, log_total = attend_rows(
            projected, scale_vecs[layer], segments, 4, token_rows
        )
        attended, across, beside = tied(attended, across, beside)
        one, two = to_beside(across), to_across(beside)
        if layer == 0:
            next_along, dense_next = tied(next_along, dense_own[1])
            dense_next = along_batch(dense_next)
            attended_t, one, two, next_along = tied(over_head(attended), one, two, next_along)
            next_across = swapped(next_along, "blk", 1)
        else:
            dense_near = dense_next
            attended_t, one, two, cotangent = tied(over_head(attended), one, two, cotangent)
            upper = swap_halves(cotangent)
        pieces = (dense_near, across, beside, one, two)
        pieces += tuple(other_core(piece) for piece in pieces)
        attended_t = attended_t.reshape(width, -1)
        denses.append(assemble(pieces))
        dense = denses[layer]
        out_w, up_w, down_w = dense[:, :width], dense[:, width:-width], dense[:, -width:]
        middle = stream + dot_rows(attended_t, out_w)
        normed_two, factor_two = normalize(middle, gains[layers + layer])
        normed_two = normed_two.astype(BF16)
        hidden = dot(normed_two, up_w)
        active = (hidden * jax.nn.sigmoid(hidden)).astype(BF16)
        kept.append(
            (
                stream, factor_one, normed_all, projected, log_total, attended_t, middle,
                factor_two, normed_two, hidden, active,
            )
        )
        stream = middle + dot(active, down_w)
    layer_out = swap_halves(stream.astype(BF16).reshape(tokens.shape))
    upper = upper.reshape(-1, width).astype(F32)

    scale_grads = [None] * layers
    for layer in reversed(range(layers)):
        (
            stream, factor_one, normed_all, projected, log_total, attended_t, middle,
            factor_two, normed_two, hidden, active,
        ) = kept[layer]
        qkv, dense = qkvs[layer], denses[layer]
        out_w, up_w, down_w = dense[:, :width], dense[:, width:-width], dense[:, -width:]
        down_bar = upper.astype(BF16)
        gate = jax.nn.sigmoid(hidden)
        up_bar = (
            dot_cols(down_bar, down_w) * gate * (1.0 + hidden * (1.0 - gate))
        ).astype(BF16)
        middle_grad = upper + lower_of(
            dot_cols(up_bar, up_w), middle, factor_two, gains[layers + layer]
        )
        out_bar = middle_grad.astype(BF16)
        if layer == 0:
            attended_grad = over_head(heads_grad(out_w, out_bar))
            grads, others = dense_grads(attended_t, normed_two, active, out_bar, up_bar, down_bar)
            attended_grad, others, z_sum, across, beside = tied(
                attended_grad, others, z_sum, across, beside
            )
            others = other_core(others)
            attended_grad, summed = tied(attended_grad, own_sum(cored, across, beside))
            summed = over_batch(summed)
            z_across = across_sum(z_sum)
        else:
            attended_grad = over_head(heads_grad(out_w, out_bar))
            grads, others = dense_grads(attended_t, normed_two, active, out_bar, up_bar, down_bar)
            attended_grad, others, layer_out = tied(attended_grad, others, layer_out)
            others = other_core(others)
        bars, scale_grads[layer] = attend_back_rows(
            projected, attended_grad, log_total, scale_vecs[layer], segments, token_rows
        )
        if layer == 0:
            bars, others = tied(bars, others)
            qkv_grad = weight_back(bars, normed_all)
            bars, qkv_grad = tied(bars, qkv_grad)
            z_sum = over_batch(qkv_grad.reshape(4, 2, -1, qkv_grad.shape[-1]))
            cored = (grads.astype(F32) + others.astype(F32)).astype(BF16)
            bars, rows = tied(bars, diagonal_rows(cored))
            diagonal = sent_beside_and_across(*rows)
            halves, to_core = rows_back(bars, qkv, token_rows)
            halves, to_core, diagonal, summed = tied(halves, to_core, diagonal, summed)
            halves, to_core, rows = tied(halves, to_core, neighbour_rows(cored, *diagonal))
            sent = sent_beside_and_across(*rows)
            halves = halves + other_core(to_core).astype(F32)
            halves, sent = tied(halves, sent)
            dense_first = over_batch(own_sum(cored, *sent))
            normed_grad = scatter_row(halves)
            normed_grad, z_sum, z_across = tied(normed_grad, z_sum, z_across)
            dense_grad = [dense_first, summed]
            qkv_grads = [columns_to_rows(across_sum(z_sum)), columns_to_rows(z_across)]
        else:
            bars, others = tied(bars, others)
            cored = (grads.astype(F32) + others.astype(F32)).astype(BF16)
            bars, rows = tied(bars, diagonal_rows(cored))
            diagonal = sent_beside_and_across(*rows)
            halves, to_core, qkv_grad = project_back(bars, qkv, normed_all, token_rows)
            z_sum = over_batch(qkv_grad.reshape(4, 2, -1, qkv_grad.shape[-1]))
            to_core, halves, diagonal = tied(to_core, halves, diagonal)
            to_core, rows = tied(to_core, neighbour_rows(cored, *diagonal))
            across = swapped(rows[0], "blk", 1)
            halves = halves + other_core(to_core).astype(F32)
            normed_grad = scatter_row(halves)
            normed_grad, beside = tied(normed_grad, rows[1])
            beside = swapped(beside, "head", 2)
        upper = middle_grad + lower_of(normed_grad, stream, factor_one, gains[layer])
    input_grad = swap_halves(upper.astype(BF16).reshape(tokens.shape)).astype(F32)
    scale_total = sum_all(jnp.stack(scale_grads))
    scale_grad = scale_total * (SCALE_BASE / math.sqrt(head_dim)) * jax.nn.sigmoid(scale_param)
    dense_all = jnp.stack([part.astype(F32) for part in dense_grad])
    qkv_all = jnp.stack(qkv_grads)
    up_all = dense_all[:, :, width:-width]
    return (
        layer_out,
        input_grad,
        qkv_all,
        dense_all[:, :, :width],
        up_all,
        dense_all[:, :, -width:],
        gain_back(qkv_weight, qkv_all, attn_gain),
        gain_back(up_weight, up_all, mlp_gain),
        scale_grad,
    )


def per_device(*args):
    tokens, segments = args[0], args[1]
    sizes = tuple(lax.axis_size(axis) for axis in ALL)
    heads = tokens.shape[2] // args[8].shape[1]
    spread = (
        sizes == (4, 2, 4)
        and tokens.shape[0] == 2
        and args[2].shape[0] == 2
        and tokens.shape[1] % 128 == 0
        and Q_ROWS % tokens.shape[1] == 0
        and segments.shape[1] <= WINDOW
        and segments.shape[1] % Q_ROWS == 0
        and heads % 4 == 0
        and tokens.shape[2] % 256 == 0
    )
    return spread_device(*args) if spread else general_device(*args)


def solution(mesh):
    rows = P(None, ALL, None)
    by_token = P("batch", ("blk", "head"), None)
    return jax.shard_map(
        per_device,
        mesh=mesh,
        in_specs=(
            by_token, P("batch", None), rows, rows, rows, rows, P(None, ALL), P(None, ALL), P(),
            by_token,
        ),
        out_specs=(
            by_token, by_token, rows, rows, rows, rows, P(None, ALL), P(None, ALL), P(),
        ),
        check_vma=False,
    )
```

```python
import functools
import math

import jax
import jax.numpy as jnp
from jax import lax
from jax.experimental import pallas as pl
from jax.experimental.pallas import tpu as pltpu
from jax.sharding import PartitionSpec as P

WINDOW = 1024
EPSILON = 1e-06
SCALE_BASE = 1.4426950408889634
MASKED_SCORE = -1e30

ALL = ("batch", "blk", "head")
REST = ("batch", "blk")
F32 = jnp.float32
BF16 = jnp.bfloat16


def shifted(block, axis, distance):
    devices = range(lax.axis_size(axis))
    route = [(i - distance, i) for i in devices if i - distance in devices]
    return lax.ppermute(block, axis, route)


NT = (((1,), (1,)), ((), ()))
TN = (((0,), (0,)), ((), ()))


def dot(left, right):
    return jnp.dot(left, right, preferred_element_type=F32)


def dot_rows(left, right):
    return lax.dot_general(left, right, (((0,), (0,)), ((), ())), preferred_element_type=F32)


def dot_cols(left, right):
    return lax.dot_general(left, right, (((1,), (1,)), ((), ())), preferred_element_type=F32)


def normalize(stream, gain):
    factor = lax.rsqrt(jnp.mean(stream * stream, axis=-1, keepdims=True) + EPSILON)
    return stream * factor * gain, factor


def norm_back(upper, stream, factor, gain):
    inner = upper * gain
    gain_grad = jnp.sum(upper * stream * factor, axis=0)
    lower = factor * inner - stream * factor * factor * factor * jnp.mean(
        inner * stream, axis=-1, keepdims=True
    )
    return lower, gain_grad


class Plan:
    def __init__(self, tokens):
        self.seqs, self.rows, self.width = tokens.shape
        self.heads = lax.axis_size("head")
        self.blks = lax.axis_size("blk")
        self.block = self.rows * self.heads
        self.whole = self.seqs % self.blks == 0
        if self.whole:
            self.groups, self.own_seqs = self.blks, self.seqs // self.blks
            self.reach = 0
        else:
            self.groups, self.own_seqs = 1, self.seqs
            self.reach = min((WINDOW - 1) // self.block + 1, self.blks - 1)
        self.length = self.groups * self.block
        self.tokens = self.seqs * self.rows


def to_plan(plan, array):
    if plan.whole and plan.blks > 1:
        array = lax.all_to_all(array, "blk", split_axis=0, concat_axis=0, tiled=True)
    return array.reshape(plan.tokens, plan.width)


def from_plan(plan, flat):
    array = flat.reshape(plan.seqs, plan.rows, plan.width)
    if plan.whole and plan.blks > 1:
        array = lax.all_to_all(array, "blk", split_axis=0, concat_axis=0, tiled=True)
    return array


def in_sequence(plan, by_head, width):
    parts = by_head.reshape(plan.heads, plan.groups, plan.own_seqs, plan.rows, width)
    return parts.transpose(2, 1, 0, 3, 4).reshape(-1, width)


def by_owner(plan, rows, width):
    parts = rows.reshape(plan.own_seqs, plan.groups, plan.heads, plan.rows, width)
    return parts.transpose(2, 1, 0, 3, 4).reshape(plan.heads, plan.tokens, width)


def gather_tokens(plan, rows):
    moved = lax.all_gather(rows, "head", axis=0, tiled=False)
    return in_sequence(plan, moved, rows.shape[-1])


def scatter_tokens(plan, rows):
    width = rows.shape[-1]
    return lax.psum_scatter(
        by_owner(plan, rows.astype(BF16), width), "head", scatter_dimension=0, tiled=False
    ).astype(F32)


def heads_to_tokens(plan, rows):
    part = rows.shape[-1]
    moved = lax.all_to_all(
        by_owner(plan, rows, part), "head", split_axis=0, concat_axis=0, tiled=True
    )
    return moved.transpose(1, 0, 2).reshape(plan.tokens, plan.heads * part)


def tokens_to_heads(plan, rows):
    part = rows.shape[-1] // plan.heads
    sent = rows.reshape(plan.tokens, plan.heads, part).transpose(1, 0, 2)
    moved = lax.all_to_all(sent, "head", split_axis=0, concat_axis=0, tiled=True)
    return in_sequence(plan, moved, part)


def gather_qkv(rows):
    own, width = rows.shape
    heads = lax.axis_size("head")
    part = width // 3 // heads
    sent = rows.reshape(own, 3, heads, part).transpose(2, 0, 1, 3).reshape(heads, own, 3 * part)
    moved = lax.all_to_all(sent, "head", split_axis=0, concat_axis=0, tiled=True)
    full = lax.all_gather(moved, REST, axis=0, tiled=True)
    return full.reshape(-1, 3 * part)


def scatter_qkv(grad):
    heads = lax.axis_size("head")
    part = grad.shape[1] // 3
    summed = lax.psum_scatter(grad.astype(BF16), REST, scatter_dimension=0, tiled=True)
    own = summed.shape[0] // heads
    moved = lax.all_to_all(
        summed.reshape(heads, own, 3 * part), "head", split_axis=0, concat_axis=0, tiled=True
    )
    return (
        moved.reshape(heads, own, 3, part)
        .transpose(1, 2, 0, 3)
        .reshape(own, 3 * heads * part)
        .astype(F32)
    )


def window_mask(plan, segments, block_index):
    key_count = plan.length + plan.reach * plan.block
    if plan.whole:
        query_segs, key_segs = segments, segments
    else:
        leading = jnp.full((plan.own_seqs, plan.reach * plan.block), -1, jnp.int32)
        padded = jnp.concatenate([leading, segments], axis=1)
        start = block_index * plan.block
        query_segs = lax.dynamic_slice_in_dim(segments, start, plan.block, 1)
        key_segs = lax.dynamic_slice_in_dim(padded, start, key_count, 1)
    query_place = jnp.arange(plan.length, dtype=jnp.int32)[:, None] + plan.reach * plan.block
    key_place = jnp.arange(key_count, dtype=jnp.int32)[None, :]
    near = (key_place <= query_place) & (query_place - key_place < WINDOW)
    return (key_segs[:, None, :] == query_segs[:, :, None]) & near[None]


def with_earlier(plan, own):
    arrived = [own]
    for _ in range(plan.reach):
        arrived.append(shifted(arrived[-1], "blk", 1))
    return jnp.concatenate(arrived[::-1], axis=1) if plan.reach else own


def to_earlier(plan, grads):
    if not plan.reach:
        return grads
    block = plan.block
    total = grads[:, :block]
    for step in range(1, plan.reach + 1):
        total = (
            shifted(total.astype(BF16), "blk", -1).astype(F32)
            + grads[:, step * block : (step + 1) * block]
        )
    return total


def scores_of(queries, keys, allowed):
    scores = jnp.einsum("sqhd,skhd->shqk", queries, keys, preferred_element_type=F32)
    return jnp.where(allowed[:, None], scores, MASKED_SCORE)


def attend(queries, keys, values, allowed):
    scores = scores_of(queries, keys, allowed)
    top_score = jnp.max(scores, axis=-1, keepdims=True)
    exp_terms = jnp.exp(scores - top_score)
    totals = jnp.sum(exp_terms, axis=-1, keepdims=True)
    probs_low = (exp_terms / totals).astype(BF16)
    attended = jnp.einsum("shqk,skhd->sqhd", probs_low, values, preferred_element_type=F32)
    return attended, top_score + jnp.log(totals)


def attend_back(queries, keys, values, allowed, log_total, attended_grad):
    probs = jnp.exp(scores_of(queries, keys, allowed) - log_total)
    probs_low = probs.astype(BF16)
    values_grad = jnp.einsum(
        "shqk,sqhd->skhd", probs_low, attended_grad, preferred_element_type=F32
    )
    probs_grad = jnp.einsum("sqhd,skhd->shqk", attended_grad, values, preferred_element_type=F32)
    row_dot = jnp.sum(probs_grad * probs, axis=-1, keepdims=True)
    scores_low = (probs * (probs_grad - row_dot)).astype(BF16)
    queries_grad = jnp.einsum("shqk,skhd->sqhd", scores_low, keys, preferred_element_type=F32)
    keys_grad = jnp.einsum("shqk,sqhd->skhd", scores_low, queries, preferred_element_type=F32)
    return queries_grad, keys_grad, values_grad


def forward(plan, stream, qkv, dense, gains, scale_vec, allowed):
    width = plan.width
    head_dim = scale_vec.shape[0]
    part = qkv.shape[1] // 3
    local_heads = part // head_dim
    split = (plan.own_seqs, plan.length, local_heads, head_dim)
    out_w, up_w, down_w = dense[:, :width], dense[:, width:-width], dense[:, -width:]
    normed, factor_one = normalize(stream, gains[0])
    normed_all = gather_tokens(plan, normed.astype(BF16))
    projected = dot(normed_all, qkv)
    query_pre = projected[:, :part].reshape(split)
    queries = (query_pre * scale_vec).astype(BF16)
    keys = with_earlier(plan, projected[:, part : 2 * part].astype(BF16).reshape(split))
    values = with_earlier(plan, projected[:, 2 * part :].astype(BF16).reshape(split))
    attended_part, log_total = attend(queries, keys, values, allowed)
    attended = heads_to_tokens(plan, attended_part.astype(BF16).reshape(-1, part))
    middle = stream + dot(attended, out_w)
    normed_two, factor_two = normalize(middle, gains[1])
    normed_two = normed_two.astype(BF16)
    hidden = dot(normed_two, up_w)
    active = (hidden * jax.nn.sigmoid(hidden)).astype(BF16)
    result = middle + dot(active, down_w)
    kept = (
        stream, factor_one, normed_all, query_pre, queries, keys, values, log_total,
        attended, middle, factor_two, normed_two, hidden, active,
    )
    return result, kept


def backward(plan, upper, kept, qkv, dense, gains, scale_vec, allowed):
    (
        stream, factor_one, normed_all, query_pre, queries, keys, values, log_total,
        attended, middle, factor_two, normed_two, hidden, active,
    ) = kept
    width = plan.width
    head_dim = scale_vec.shape[0]
    part = qkv.shape[1] // 3
    out_w, up_w, down_w = dense[:, :width], dense[:, width:-width], dense[:, -width:]
    upper_low = upper.astype(BF16)
    down_grad = dot_rows(active, upper_low)
    active_grad = dot_cols(upper_low, down_w)
    gate = jax.nn.sigmoid(hidden)
    hidden_low = (active_grad * gate * (1.0 + hidden * (1.0 - gate))).astype(BF16)
    up_grad = dot_rows(normed_two, hidden_low)
    extra_two, mlp_gain_grad = norm_back(dot_cols(hidden_low, up_w), middle, factor_two, gains[1])
    middle_grad = upper + extra_two
    middle_low = middle_grad.astype(BF16)
    out_grad = dot_rows(attended, middle_low)
    dense_grad = jnp.concatenate([out_grad, up_grad, down_grad], axis=1).astype(BF16)
    dense_own = lax.psum_scatter(dense_grad, ALL, scatter_dimension=0, tiled=True)
    attended_grad = tokens_to_heads(plan, dot_cols(middle_low, out_w).astype(BF16))
    queries_grad, keys_grad, values_grad = attend_back(
        queries, keys, values, allowed, log_total, attended_grad.reshape(queries.shape)
    )
    query_bar = queries_grad.astype(BF16).astype(F32)
    scale_vec_grad = jnp.sum((query_bar * query_pre).reshape(-1, head_dim), axis=0)
    query_low = (query_bar * scale_vec).astype(BF16).reshape(-1, part)
    keys_low = to_earlier(plan, keys_grad).astype(BF16).reshape(-1, part)
    values_low = to_earlier(plan, values_grad).astype(BF16).reshape(-1, part)
    projected_low = jnp.concatenate([query_low, keys_low, values_low], axis=1)
    normed_grad = scatter_tokens(plan, dot_cols(projected_low, qkv))
    qkv_own = scatter_qkv(dot_rows(normed_all, projected_low))
    extra_one, attn_gain_grad = norm_back(normed_grad, stream, factor_one, gains[0])
    lower = middle_grad + extra_one
    return lower, qkv_own, dense_own, (attn_gain_grad, mlp_gain_grad), scale_vec_grad


def general_device(
    tokens,
    segments,
    qkv_weight,
    out_weight,
    up_weight,
    down_weight,
    attn_gain,
    mlp_gain,
    scale_param,
    cotangent,
):
    plan = Plan(tokens)
    layers, head_dim = scale_param.shape
    block_index = lax.axis_index("blk")
    scale_vecs = SCALE_BASE / math.sqrt(head_dim) * jax.nn.softplus(scale_param)
    own_gains = jnp.concatenate([attn_gain, mlp_gain], axis=0)
    gains = (
        lax.all_gather(own_gains.reshape(1, -1), ALL, axis=0, tiled=True)
        .reshape(-1, 2 * layers, attn_gain.shape[1])
        .transpose(1, 0, 2)
        .reshape(2 * layers, plan.width)
        .astype(F32)
    )
    if plan.whole:
        segments = lax.dynamic_slice_in_dim(
            segments, block_index * plan.own_seqs, plan.own_seqs, 0
        )
    allowed = window_mask(plan, segments, block_index)
    stream = to_plan(plan, tokens).astype(F32)
    qkvs, denses, kept = [], [], []
    for layer in range(layers):
        qkvs.append(gather_qkv(qkv_weight[layer]))
        own = jnp.concatenate([out_weight[layer], up_weight[layer], down_weight[layer]], axis=1)
        denses.append(lax.all_gather(own, ALL, axis=0, tiled=True))
        layer_gains = (gains[layer], gains[layers + layer])
        stream, saved = forward(
            plan, stream, qkvs[layer], denses[layer], layer_gains, scale_vecs[layer], allowed
        )
        kept.append(saved)
    layer_out = from_plan(plan, stream.astype(BF16))
    upper = to_plan(plan, cotangent).astype(F32)
    qkv_grads, dense_grads = [None] * layers, [None] * layers
    gain_grads, scale_grads = [None] * layers, [None] * layers
    for layer in reversed(range(layers)):
        layer_gains = (gains[layer], gains[layers + layer])
        upper, qkv_grads[layer], dense_grads[layer], gain_grads[layer], scale_grads[layer] = (
            backward(
                plan, upper, kept[layer], qkvs[layer], denses[layer], layer_gains,
                scale_vecs[layer], allowed,
            )
        )
    input_grad = from_plan(plan, upper.astype(BF16)).astype(F32)
    small = jnp.concatenate(
        [g[0] for g in gain_grads] + [g[1] for g in gain_grads] + scale_grads, axis=0
    )
    total = lax.psum(small, ALL)
    gain_total = total[: 2 * layers * plan.width].reshape(2 * layers, plan.width)
    owner = lax.axis_index(ALL)
    gain_rows = attn_gain.shape[1]
    own_total = lax.dynamic_slice_in_dim(gain_total, owner * gain_rows, gain_rows, 1)
    scale_total = total[2 * layers * plan.width :].reshape(layers, head_dim)
    scale_grad = scale_total * (SCALE_BASE / math.sqrt(head_dim)) * jax.nn.sigmoid(scale_param)
    dense_all = jnp.stack(dense_grads).astype(F32)
    width = plan.width
    return (
        layer_out,
        input_grad,
        jnp.stack(qkv_grads),
        dense_all[:, :, :width],
        dense_all[:, :, width:-width],
        dense_all[:, :, -width:],
        own_total[:layers],
        own_total[layers:],
        scale_grad,
    )


Q_ROWS = 256
KERNEL = pltpu.CompilerParams(vmem_limit_bytes=32 * 1024 * 1024)
LIGHT = pl.CostEstimate(flops=1 << 20, bytes_accessed=1 << 20, transcendentals=0)


def in_hbm(*arrays):
    return [pltpu.with_memory_space_constraint(array, pltpu.HBM) for array in arrays]


def allowed_keys(col, row, first):
    count = first + row.shape[1]
    key_place = lax.broadcasted_iota(jnp.int32, (count, row.shape[1]), 0)
    query_place = lax.broadcasted_iota(jnp.int32, (count, row.shape[1]), 1) + first
    return (col[:count] == row) & (key_place <= query_place)


def token_places(length, heads, token_rows):
    for first in range(0, length, Q_ROWS):
        parts = []
        for start in range(0, Q_ROWS, token_rows):
            place = (first + start) // token_rows
            parts.append((start, place % heads, place // heads * token_rows))
        yield first, parts


def attend_kernel(token_rows, proj_ref, scale_ref, col_ref, row_ref, out_ref, lse_ref):
    length = proj_ref.shape[-1]
    queries = (proj_ref[0, 0] * scale_ref[...]).astype(BF16)
    keys = proj_ref[1, 0].T.astype(BF16)
    values = proj_ref[2, 0].astype(BF16)
    for first, parts in token_places(length, out_ref.shape[0], token_rows):
        end = first + Q_ROWS
        scores = jnp.dot(keys[:end], queries[:, first:end], preferred_element_type=F32)
        allowed = allowed_keys(col_ref[...], row_ref[:, first:end], first)
        scores = jnp.where(allowed, scores, MASKED_SCORE)
        top = jnp.max(scores, axis=0, keepdims=True)
        terms = jnp.exp(scores - top)
        total = jnp.sum(terms, axis=0, keepdims=True)
        probs = (terms * (1.0 / total)).astype(BF16)
        attended = jnp.dot(values[:, :end], probs, preferred_element_type=F32).astype(BF16)
        lse_ref[0, :, first:end] = top + jnp.log(total)
        for start, owner, offset in parts:
            out_ref[owner, 0, :, offset : offset + token_rows] = attended[
                :, start : start + token_rows
            ]


def attend_rows(projected, scale_vec, segments, owners, token_rows):
    head_dim = scale_vec.shape[0]
    length = projected.shape[1]
    local_heads = projected.shape[0] // 3 // head_dim
    tokens = length // owners
    attended, log_total = pl.pallas_call(
        functools.partial(attend_kernel, token_rows),
        grid=(local_heads,),
        in_specs=[
            pl.BlockSpec((3, 1, head_dim, length), lambda h: (0, h, 0, 0)),
            pl.BlockSpec((head_dim, 1), lambda h: (0, 0)),
            pl.BlockSpec((length, 1), lambda h: (0, 0)),
            pl.BlockSpec((1, length), lambda h: (0, 0)),
        ],
        out_specs=[
            pl.BlockSpec((owners, 1, head_dim, tokens), lambda h: (0, h, 0, 0)),
            pl.BlockSpec((1, 1, length), lambda h: (h, 0, 0)),
        ],
        out_shape=[
            jax.ShapeDtypeStruct((owners, local_heads, head_dim, tokens), BF16),
            jax.ShapeDtypeStruct((local_heads, 1, length), F32),
        ],
        compiler_params=KERNEL,
        cost_estimate=LIGHT,
    )(
        projected.reshape(3, local_heads, head_dim, length),
        scale_vec.reshape(head_dim, 1),
        segments.reshape(length, 1),
        segments.reshape(1, length),
    )
    return attended.reshape(owners, local_heads * head_dim, tokens), log_total


def attend_back_kernel(
    token_rows,
    proj_ref,
    grad_ref,
    lse_ref,
    scale_ref,
    col_ref,
    row_ref,
    out_ref,
    scale_grad_ref,
    keys_acc,
    values_acc,
):
    length = proj_ref.shape[-1]
    scale = scale_ref[...]
    query_pre = proj_ref[0, 0]
    queries = (query_pre * scale).astype(BF16)
    keys_t = proj_ref[1, 0].astype(BF16)
    keys = proj_ref[1, 0].T.astype(BF16)
    values = proj_ref[2, 0].T.astype(BF16)
    keys_acc[...] = jnp.zeros_like(keys_acc)
    values_acc[...] = jnp.zeros_like(values_acc)
    scale_grad = jnp.zeros((scale.shape[0], 1), F32)
    for first, parts in token_places(length, grad_ref.shape[0], token_rows):
        end = first + Q_ROWS
        block = queries[:, first:end]
        grad = jnp.concatenate(
            [grad_ref[owner, 0, :, at : at + token_rows] for _, owner, at in parts], axis=1
        )
        scores = jnp.dot(keys[:end], block, preferred_element_type=F32)
        allowed = allowed_keys(col_ref[...], row_ref[:, first:end], first)
        scores = jnp.where(allowed, scores, MASKED_SCORE)
        probs = jnp.exp(scores - lse_ref[0, :, first:end])
        probs_grad = jnp.dot(values[:end], grad, preferred_element_type=F32)
        row_dot = jnp.sum(probs_grad * probs, axis=0, keepdims=True)
        scores_low = (probs * (probs_grad - row_dot)).astype(BF16)
        values_acc[:, :end] += lax.dot_general(
            grad, probs.astype(BF16), NT, preferred_element_type=F32
        )
        keys_acc[:, :end] += lax.dot_general(
            block, scores_low, NT, preferred_element_type=F32
        )
        query_bar = jnp.dot(keys_t[:, :end], scores_low, preferred_element_type=F32)
        query_bar = query_bar.astype(BF16).astype(F32)
        scale_grad += jnp.sum(query_bar * query_pre[:, first:end], axis=1, keepdims=True)
        out_ref[0, 0, :, first:end] = (query_bar * scale).astype(BF16)
    out_ref[1, 0] = keys_acc[...].astype(BF16)
    out_ref[2, 0] = values_acc[...].astype(BF16)
    spread = jnp.broadcast_to(scale_grad, scale_grad_ref.shape)

    @pl.when(pl.program_id(0) == 0)
    def _():
        scale_grad_ref[...] = spread

    @pl.when(pl.program_id(0) > 0)
    def _():
        scale_grad_ref[...] += spread


def attend_back_rows(projected, attended_grad, log_total, scale_vec, segments, token_rows):
    head_dim = scale_vec.shape[0]
    length = projected.shape[1]
    local_heads = projected.shape[0] // 3 // head_dim
    owners, _, tokens = attended_grad.shape
    lanes = 128
    grads, scale_grad = pl.pallas_call(
        functools.partial(attend_back_kernel, token_rows),
        grid=(local_heads,),
        in_specs=[
            pl.BlockSpec((3, 1, head_dim, length), lambda h: (0, h, 0, 0)),
            pl.BlockSpec((owners, 1, head_dim, tokens), lambda h: (0, h, 0, 0)),
            pl.BlockSpec((1, 1, length), lambda h: (h, 0, 0)),
            pl.BlockSpec((head_dim, 1), lambda h: (0, 0)),
            pl.BlockSpec((length, 1), lambda h: (0, 0)),
            pl.BlockSpec((1, length), lambda h: (0, 0)),
        ],
        out_specs=[
            pl.BlockSpec((3, 1, head_dim, length), lambda h: (0, h, 0, 0)),
            pl.BlockSpec((head_dim, lanes), lambda h: (0, 0)),
        ],
        out_shape=[
            pltpu.HBM((3, local_heads, head_dim, length), BF16),
            pltpu.HBM((head_dim, lanes), F32),
        ],
        scratch_shapes=[
            pltpu.VMEM((head_dim, length), F32),
            pltpu.VMEM((head_dim, length), F32),
        ],
        compiler_params=KERNEL,
        cost_estimate=LIGHT,
    )(
        *in_hbm(
            projected.reshape(3, local_heads, head_dim, length),
            attended_grad.reshape(owners, local_heads, head_dim, tokens),
        ),
        log_total,
        scale_vec.reshape(head_dim, 1),
        segments.reshape(length, 1),
        segments.reshape(1, length),
    )
    return grads.reshape(3 * local_heads * head_dim, length), scale_grad[:, 0]


def dense_grad_kernel(
    core_ref, attended_ref, normed_ref, active_ref, out_bar, up_bar, down_bar,
    own_ref, other_ref, normed_t, active_t,
):
    tile = pl.program_id(0)
    rows, width = own_ref.shape[1] * own_ref.shape[3] * 2, out_bar.shape[1]

    @pl.when(tile == 0)
    def _():
        normed_t[...] = normed_ref[...].astype(F32).T.astype(BF16)
        active_t[...] = active_ref[...].astype(F32).T.astype(BF16)

    start = pl.multiple_of(tile * rows, rows)
    first_core = core_ref[2] == 0
    lefts = (attended_ref, normed_t, active_t)
    for i, (left, right) in enumerate(zip(lefts, (out_bar, up_bar, down_bar))):
        grad = jnp.dot(left[pl.ds(start, rows), :], right[...], preferred_element_type=F32)
        grad = grad.reshape(2, 2, rows // 4, width)
        one, two = grad[:, 0], grad[:, 1]
        own_ref[0, :, 0, :, i * width : (i + 1) * width] = jnp.where(
            first_core, one, two
        ).astype(BF16)
        other_ref[0, :, 0, :, i * width : (i + 1) * width] = jnp.where(
            first_core, two, one
        ).astype(BF16)


def dense_grads(attended_t, normed, active, out_bar, up_bar, down_bar):
    width, tokens = attended_t.shape
    own = width // 32
    whole = pl.BlockSpec((tokens, width), lambda i, core: (0, 0))
    rows = pl.BlockSpec((1, 2, 1, own, 3 * width), lambda i, core: (i % 2, 0, i // 2, 0, 0))
    shape = pltpu.HBM((2, 2, 4, own, 3 * width), BF16)
    return pl.pallas_call(
        dense_grad_kernel,
        grid_spec=pltpu.PrefetchScalarGridSpec(
            num_scalar_prefetch=1,
            grid=(8,),
            in_specs=[pl.BlockSpec((width, tokens), lambda i, core: (0, 0))] + [whole] * 5,
            out_specs=[rows, rows],
            scratch_shapes=[pltpu.VMEM((width, tokens), BF16)] * 2,
        ),
        out_shape=[shape, shape],
        compiler_params=KERNEL,
        cost_estimate=LIGHT,
    )(place(), *in_hbm(attended_t, normed, active, out_bar, up_bar, down_bar))


def place():
    head = lax.axis_index("head")
    return jnp.stack([lax.axis_index("blk"), head // 2, head % 2]).astype(jnp.int32)


def assemble_kernel(place_ref, *refs):
    pieces, whole_ref = refs[:10], refs[10]
    half = whole_ref.shape[-1] // 2
    blk, row, core = place_ref[0], place_ref[1], place_ref[2]
    for i in range(2):
        at_core = core if i == 0 else 1 - core
        own, across, beside, one, two = pieces[5 * i : 5 * i + 5]
        whole_ref[0, blk, row, at_core] = own[0]
        whole_ref[0, 1 - blk, row, at_core] = across[0]
        whole_ref[0, blk, 1 - row, at_core] = beside[0]
        whole_ref[0, 1 - blk, 1 - row, at_core, :, :half] = one[0]
        whole_ref[0, 1 - blk, 1 - row, at_core, :, half:] = two[0]


def assemble(pieces):
    batch, own, columns = pieces[0].shape
    specs = [
        pl.BlockSpec((1, own, piece.shape[-1]), lambda i, at: (i, 0, 0))
        for piece in pieces
    ]
    whole = pl.pallas_call(
        assemble_kernel,
        grid_spec=pltpu.PrefetchScalarGridSpec(
            num_scalar_prefetch=1,
            grid=(batch,),
            in_specs=specs,
            out_specs=pl.BlockSpec((1, 2, 2, 2, own, columns), lambda i, at: (i, 0, 0, 0, 0, 0)),
        ),
        out_shape=jax.ShapeDtypeStruct((batch, 2, 2, 2, own, columns), BF16),
        compiler_params=KERNEL,
        cost_estimate=LIGHT,
    )(place(), *pieces)
    return whole.reshape(-1, columns)


def assemble_columns_kernel(place_ref, along_ref, across_ref, whole_ref, *extra_ref):
    blk = place_ref[0]
    columns = whole_ref.shape[-1]
    whole_ref[0, blk] = along_ref[0, :, :columns]
    whole_ref[0, 1 - blk] = across_ref[0, :, :columns]
    for extra in extra_ref:
        extra[0, blk] = along_ref[0, :, columns:]
        extra[0, 1 - blk] = across_ref[0, :, columns:]


def assemble_columns(along, across, columns):
    batch, own, both = along.shape
    rows = pl.BlockSpec((1, own, both), lambda i, at: (i, 0, 0))
    shapes = [(batch, 2, own, columns)]
    if both > columns:
        shapes.append((batch, 2, own, both - columns))
    parts = pl.pallas_call(
        assemble_columns_kernel,
        grid_spec=pltpu.PrefetchScalarGridSpec(
            num_scalar_prefetch=1,
            grid=(batch,),
            in_specs=[rows, rows],
            out_specs=[pl.BlockSpec((1,) + s[1:], lambda i, at: (i, 0, 0, 0)) for s in shapes],
        ),
        out_shape=[pltpu.HBM(s, BF16) for s in shapes],
        compiler_params=KERNEL,
        cost_estimate=LIGHT,
    )(place(), *in_hbm(along, across))
    return [part.reshape(-1, part.shape[-1]) for part in parts]


def project_kernel(with_norm, place_ref, *refs):
    pieces, (gain_ref, weight_ref, normed_ref, projected_ref) = refs[:4], refs[4:]
    head = place_ref[1] * 2 + place_ref[2]
    rows = pieces[0].shape[0]
    for i, piece in enumerate(pieces):
        value = piece[...]
        if with_norm:
            stream = value.astype(F32)
            factor = lax.rsqrt(jnp.mean(stream * stream, axis=-1, keepdims=True) + EPSILON)
            value = (stream * factor * gain_ref[...]).astype(BF16)
        normed_ref[pl.ds(pl.multiple_of((head ^ i) * rows, rows), rows), :] = value
    projected = jnp.dot(normed_ref[...], weight_ref[...], preferred_element_type=F32)
    projected_ref[...] = projected.T


def project(pieces, gain, weight, with_norm, token_rows):
    tokens, width = pieces[0].shape
    length, columns = 4 * tokens, weight.shape[1]
    groups = tokens // token_rows
    piece = pl.BlockSpec((token_rows, width), lambda g, at: (g, 0))
    return pl.pallas_call(
        functools.partial(project_kernel, with_norm),
        grid_spec=pltpu.PrefetchScalarGridSpec(
            num_scalar_prefetch=1,
            grid=(groups,),
            in_specs=[piece] * 4
            + [
                pl.BlockSpec((1, width), lambda g, at: (0, 0)),
                pl.BlockSpec((width, columns), lambda g, at: (0, 0)),
            ],
            out_specs=[
                pl.BlockSpec((4 * token_rows, width), lambda g, at: (g, 0)),
                pl.BlockSpec((columns, 4 * token_rows), lambda g, at: (0, g)),
            ],
        ),
        out_shape=[
            pltpu.HBM((length, width), BF16),
            pltpu.HBM((columns, length), F32),
        ],
        compiler_params=KERNEL,
        cost_estimate=LIGHT,
    )(place(), *in_hbm(*pieces), gain.reshape(1, width), *in_hbm(weight))


def project_back_kernel(
    place_ref, bars_ref, weight_ref, normed_ref, own_ref, other_ref, grad_ref, bars_t
):
    @pl.when(pl.program_id(0) == 0)
    def _():
        bars_t[...] = bars_ref[...].astype(F32).T.astype(BF16)

    upper = lax.dot_general(bars_t[...], weight_ref[...], NT, preferred_element_type=F32)
    upper = upper.reshape(2, 2, 2, -1, upper.shape[-1])
    first_core = place_ref[2] == 0
    one, two = upper[:, :, 0], upper[:, :, 1]
    own_ref[...] = jnp.where(first_core, one, two)
    other_ref[...] = jnp.where(first_core, two, one).astype(BF16)
    grad = lax.dot_general(normed_ref[...], bars_t[...], TN, preferred_element_type=F32)
    grad_ref[...] = grad.astype(BF16)


def project_back(bars, weight, normed, token_rows):
    columns, length = bars.shape
    width = weight.shape[0]
    tile = width // 2
    quarter = pl.BlockSpec((2, 2, token_rows, tile), lambda i, at: (0, 0, 0, i))
    return pl.pallas_call(
        project_back_kernel,
        grid_spec=pltpu.PrefetchScalarGridSpec(
            num_scalar_prefetch=1,
            grid=(2,),
            in_specs=[
                pl.BlockSpec((columns, length), lambda i, at: (0, 0)),
                pl.BlockSpec((tile, columns), lambda i, at: (i, 0)),
                pl.BlockSpec((length, tile), lambda i, at: (0, i)),
            ],
            out_specs=[quarter, quarter, pl.BlockSpec((tile, columns), lambda i, at: (i, 0))],
            scratch_shapes=[pltpu.VMEM((length, columns), BF16)],
        ),
        out_shape=[
            pltpu.HBM((2, 2, token_rows, width), F32),
            pltpu.HBM((2, 2, token_rows, width), BF16),
            pltpu.HBM((width, columns), BF16),
        ],
        compiler_params=KERNEL,
        cost_estimate=LIGHT,
    )(place(), *in_hbm(bars, weight, normed))


def rows_back_kernel(place_ref, bars_ref, weight_ref, own_ref, other_ref, bars_t):
    @pl.when(pl.program_id(0) == 0)
    def _():
        bars_t[...] = bars_ref[...].astype(F32).T.astype(BF16)

    upper = lax.dot_general(bars_t[...], weight_ref[...], NT, preferred_element_type=F32)
    upper = upper.reshape(2, 2, 2, -1, upper.shape[-1])
    first_core = place_ref[2] == 0
    one, two = upper[:, :, 0], upper[:, :, 1]
    own_ref[...] = jnp.where(first_core, one, two)
    other_ref[...] = jnp.where(first_core, two, one).astype(BF16)


def rows_back(bars, weight, token_rows):
    columns, length = bars.shape
    width = weight.shape[0]
    tile = width // 2
    quarter = pl.BlockSpec((2, 2, token_rows, tile), lambda i, at: (0, 0, 0, i))
    return pl.pallas_call(
        rows_back_kernel,
        grid_spec=pltpu.PrefetchScalarGridSpec(
            num_scalar_prefetch=1,
            grid=(2,),
            in_specs=[
                pl.BlockSpec((columns, length), lambda i, at: (0, 0)),
                pl.BlockSpec((tile, columns), lambda i, at: (i, 0)),
            ],
            out_specs=[quarter, quarter],
            scratch_shapes=[pltpu.VMEM((length, columns), BF16)],
        ),
        out_shape=[
            pltpu.HBM((2, 2, token_rows, width), F32),
            pltpu.HBM((2, 2, token_rows, width), BF16),
        ],
        compiler_params=KERNEL,
        cost_estimate=LIGHT,
    )(place(), *in_hbm(bars, weight))


def weight_back_kernel(bars_ref, normed_ref, grad_ref):
    grad = jnp.dot(bars_ref[...], normed_ref[...], preferred_element_type=F32)
    grad_ref[...] = grad.T.astype(BF16)


def weight_back(bars, normed):
    columns, length = bars.shape
    width = normed.shape[1]
    tile = width // 5
    return pl.pallas_call(
        weight_back_kernel,
        grid=(5,),
        in_specs=[
            pl.BlockSpec((columns, length), lambda i: (0, 0)),
            pl.BlockSpec((length, tile), lambda i: (0, i)),
        ],
        out_specs=pl.BlockSpec((tile, columns), lambda i: (i, 0)),
        out_shape=pltpu.HBM((width, columns), BF16),
        compiler_params=KERNEL,
        cost_estimate=LIGHT,
    )(*in_hbm(bars, normed))


def tied(*arrays):
    return lax.optimization_barrier(arrays)


def swapped(array, axis, mask):
    size = lax.axis_size(axis)
    return lax.ppermute(array, axis, [(i, i ^ mask) for i in range(size)])


def pick(array, index, axis=0):
    return lax.dynamic_index_in_dim(array, index, axis, keepdims=False)


def swap_halves(array):
    me = lax.axis_index("blk")
    got = swapped(pick(array, 1 - me), "blk", 1)
    kept = pick(array, me)
    return jnp.stack([jnp.where(me == 0, kept, got), jnp.where(me == 0, got, kept)])


def scatter_row(halves):
    row = lax.axis_index("head") // 2
    got = swapped(pick(halves, 1 - row, 1).astype(BF16), "head", 2).astype(F32)
    return (pick(halves, row, 1) + got).reshape(-1, halves.shape[-1])


def over_head(parts):
    return lax.all_to_all(parts, "head", split_axis=0, concat_axis=0, tiled=True)


def qkv_columns(rows, extra):
    own, width = rows.shape
    part = width // 3 // 4
    sent = rows.reshape(own, 3, 4, part).transpose(2, 0, 1, 3).reshape(4, own, 3 * part)
    if extra is not None:
        sent = jnp.concatenate([sent, jnp.broadcast_to(extra[None], (4,) + extra.shape)], axis=2)
    return over_head(sent)


def along_batch(piece):
    return lax.all_gather(piece, "batch", axis=0, tiled=False)


def other_core(array):
    return swapped(array, "head", 1)


def to_beside(across):
    return swapped(across[..., : across.shape[-1] // 2], "head", 2)


def to_across(beside):
    return swapped(beside[..., beside.shape[-1] // 2 :], "blk", 1)


def over_batch(parts):
    return lax.psum_scatter(parts.astype(BF16), "batch", scatter_dimension=0, tiled=False)


def across_sum(halves):
    blk = lax.axis_index("blk")
    got = swapped(pick(halves, 1 - blk), "blk", 1).astype(F32)
    return (pick(halves, blk).astype(F32) + got).astype(BF16)


def columns_to_rows(summed):
    moved = over_head(summed.reshape(4, -1, summed.shape[-1]))
    rows = moved.shape[1]
    return moved.reshape(4, rows, 3, -1).transpose(1, 2, 0, 3).reshape(rows, -1).astype(F32)


def diagonal_rows(cored):
    blk, row = place()[:2]
    rows = pick(pick(cored, 1 - blk), 1 - row)
    half = rows.shape[-1] // 2
    return rows[..., :half], rows[..., half:]


def neighbour_rows(cored, one, two):
    blk, row = place()[:2]
    half = one.shape[-1]
    across = pick(pick(cored, 1 - blk), row)
    beside = pick(pick(cored, blk), 1 - row)
    across = jnp.concatenate(
        [across[..., :half], across[..., half:].astype(F32) + two.astype(F32)], axis=-1
    ).astype(BF16)
    beside = jnp.concatenate(
        [beside[..., :half].astype(F32) + one.astype(F32), beside[..., half:]], axis=-1
    ).astype(BF16)
    return across, beside


def sent_beside_and_across(across, beside):
    return swapped(across, "blk", 1), swapped(beside, "head", 2)


def heads_grad(weight, out_bar):
    return dot_cols(weight, out_bar).astype(BF16).reshape(4, -1, out_bar.shape[0])


def own_sum(cored, across, beside):
    blk, row = place()[:2]
    own = pick(pick(cored, blk), row)
    return own.astype(F32) + across.astype(F32) + beside.astype(F32)


def sum_all(array):
    for axis, mask in (("head", 1), ("head", 2), ("blk", 1), ("batch", 1), ("batch", 2)):
        array = array + swapped(array, axis, mask)
    return array


def gain_back(weight, weight_grad, gain):
    return jnp.sum(weight.astype(F32) * weight_grad, axis=-1) / gain.astype(F32)


def lower_of(upper, stream, factor, gain):
    return norm_back(upper, stream, factor, gain)[0]


def spread_device(
    tokens,
    segments,
    qkv_weight,
    out_weight,
    up_weight,
    down_weight,
    attn_gain,
    mlp_gain,
    scale_param,
    cotangent,
):
    layers, head_dim = scale_param.shape
    _, token_rows, width = tokens.shape
    scale_vecs = SCALE_BASE / math.sqrt(head_dim) * jax.nn.softplus(scale_param)
    segments = pick(segments, lax.axis_index("blk"))
    own_gains = jnp.concatenate([attn_gain, mlp_gain], axis=0)

    part3 = 3 * width // 4
    dense_own = [
        jnp.concatenate([out_weight[i], up_weight[i], down_weight[i]], axis=1) for i in (0, 1)
    ]

    first = swap_halves(tokens).reshape(-1, width)
    columns = qkv_columns(qkv_weight[0], own_gains.T)
    columns, first = tied(columns.reshape(-1, columns.shape[-1]), first)
    stream = first.astype(F32)
    along = along_batch(columns)
    far, near = swapped(first, "head", 2), other_core(first)
    both = other_core(far)
    along, near, far, both, dense_near = tied(along, near, far, both, dense_own[0])
    token_pieces = (first, near, far, both)
    dense_near = along_batch(dense_near)
    qkv_across = swapped(along, "blk", 1)
    next_columns = qkv_columns(qkv_weight[1], None).reshape(-1, part3)
    qkv_across, dense_near, next_columns, dense_next = tied(
        qkv_across, dense_near, next_columns, dense_own[1]
    )
    across, beside = swapped(dense_near, "blk", 1), swapped(dense_near, "head", 2)
    next_along, dense_next = along_batch(next_columns), along_batch(dense_next)
    weight, gains = assemble_columns(along, qkv_across, part3)
    qkvs = [weight]
    gains = gains.T.astype(F32)

    kept, denses = [], []
    for layer in range(layers):
        normed, factor_one = normalize(stream, gains[layer])
        if layer == 1:
            normed, next_across = tied(normed.astype(BF16), next_across)
            far, near = swapped(normed, "head", 2), other_core(normed)
            far, dense_next = tied(far, dense_next)
            across, beside = swapped(dense_next, "blk", 1), swapped(dense_next, "head", 2)
            token_pieces = (normed, near, far, other_core(far))
            qkvs.append(assemble_columns(next_along, next_across, part3)[0])
        normed_all, projected = project(
            token_pieces, gains[layer], qkvs[layer], layer == 0, token_rows
        )
        if layer == 1:
            projected, cotangent = tied(projected, cotangent)
            upper = swap_halves(cotangent)
        attended, log_total = attend_rows(
            projected, scale_vecs[layer], segments, 4, token_rows
        )
        if layer == 1:
            attended, upper = tied(attended, upper)
        attended, across, beside = tied(attended, across, beside)
        one, two = to_beside(across), to_across(beside)
        if layer == 0:
            two, next_along = tied(two, next_along)
            next_across = swapped(next_along, "blk", 1)
        else:
            dense_near = dense_next
        attended_t, one, two = tied(over_head(attended), one, two)
        pieces = (dense_near, across, beside, one, two)
        pieces += tuple(other_core(piece) for piece in pieces)
        attended_t = attended_t.reshape(width, -1)
        denses.append(assemble(pieces))
        dense = denses[layer]
        out_w, up_w, down_w = dense[:, :width], dense[:, width:-width], dense[:, -width:]
        middle = stream + dot_rows(attended_t, out_w)
        normed_two, factor_two = normalize(middle, gains[layers + layer])
        normed_two = normed_two.astype(BF16)
        hidden = dot(normed_two, up_w)
        active = (hidden * jax.nn.sigmoid(hidden)).astype(BF16)
        kept.append(
            (
                stream, factor_one, normed_all, projected, log_total, attended_t, middle,
                factor_two, normed_two, hidden, active,
            )
        )
        stream = middle + dot(active, down_w)
    layer_out = swap_halves(stream.astype(BF16).reshape(tokens.shape))
    upper = upper.reshape(-1, width).astype(F32)

    scale_grads = [None] * layers
    for layer in reversed(range(layers)):
        (
            stream, factor_one, normed_all, projected, log_total, attended_t, middle,
            factor_two, normed_two, hidden, active,
        ) = kept[layer]
        qkv, dense = qkvs[layer], denses[layer]
        out_w, up_w, down_w = dense[:, :width], dense[:, width:-width], dense[:, -width:]
        down_bar = upper.astype(BF16)
        gate = jax.nn.sigmoid(hidden)
        up_bar = (
            dot_cols(down_bar, down_w) * gate * (1.0 + hidden * (1.0 - gate))
        ).astype(BF16)
        middle_grad = upper + lower_of(
            dot_cols(up_bar, up_w), middle, factor_two, gains[layers + layer]
        )
        out_bar = middle_grad.astype(BF16)
        if layer == 0:
            attended_grad = over_head(heads_grad(out_w, out_bar))
            grads, others = dense_grads(attended_t, normed_two, active, out_bar, up_bar, down_bar)
            attended_grad, others, z_sum, across, beside = tied(
                attended_grad, others, z_sum, across, beside
            )
            others = other_core(others)
            attended_grad, summed = tied(attended_grad, own_sum(cored, across, beside))
            summed = over_batch(summed)
            z_across = across_sum(z_sum)
        else:
            attended_grad = over_head(heads_grad(out_w, out_bar))
            grads, others = dense_grads(attended_t, normed_two, active, out_bar, up_bar, down_bar)
            attended_grad, others, layer_out = tied(attended_grad, others, layer_out)
            others = other_core(others)
        bars, scale_grads[layer] = attend_back_rows(
            projected, attended_grad, log_total, scale_vecs[layer], segments, token_rows
        )
        if layer == 0:
            bars, others = tied(bars, others)
            qkv_grad = weight_back(bars, normed_all)
            bars, qkv_grad = tied(bars, qkv_grad)
            z_sum = over_batch(qkv_grad.reshape(4, 2, -1, qkv_grad.shape[-1]))
            cored = (grads.astype(F32) + others.astype(F32)).astype(BF16)
            bars, rows = tied(bars, diagonal_rows(cored))
            diagonal = sent_beside_and_across(*rows)
            halves, to_core = rows_back(bars, qkv, token_rows)
            halves, to_core, diagonal, summed = tied(halves, to_core, diagonal, summed)
            halves, to_core, rows = tied(halves, to_core, neighbour_rows(cored, *diagonal))
            sent = sent_beside_and_across(*rows)
            halves = halves + other_core(to_core).astype(F32)
            halves, sent, z_sum = tied(halves, sent, z_sum)
            dense_first = over_batch(own_sum(cored, *sent))
            normed_grad = scatter_row(halves)
            normed_grad, z_across = tied(normed_grad, z_across)
            dense_grad = [dense_first, summed]
            qkv_grads = [columns_to_rows(across_sum(z_sum)), columns_to_rows(z_across)]
        else:
            bars, others = tied(bars, others)
            cored = (grads.astype(F32) + others.astype(F32)).astype(BF16)
            bars, rows = tied(bars, diagonal_rows(cored))
            diagonal = sent_beside_and_across(*rows)
            halves, to_core, qkv_grad = project_back(bars, qkv, normed_all, token_rows)
            z_sum = over_batch(qkv_grad.reshape(4, 2, -1, qkv_grad.shape[-1]))
            to_core, halves, diagonal = tied(to_core, halves, diagonal)
            to_core, rows = tied(to_core, neighbour_rows(cored, *diagonal))
            across = swapped(rows[0], "blk", 1)
            halves = halves + other_core(to_core).astype(F32)
            normed_grad = scatter_row(halves)
            normed_grad, beside = tied(normed_grad, rows[1])
            beside = swapped(beside, "head", 2)
        upper = middle_grad + lower_of(normed_grad, stream, factor_one, gains[layer])
    input_grad = swap_halves(upper.astype(BF16).reshape(tokens.shape)).astype(F32)
    scale_total = sum_all(jnp.stack(scale_grads))
    scale_grad = scale_total * (SCALE_BASE / math.sqrt(head_dim)) * jax.nn.sigmoid(scale_param)
    dense_all = jnp.stack([part.astype(F32) for part in dense_grad])
    qkv_all = jnp.stack(qkv_grads)
    up_all = dense_all[:, :, width:-width]
    return (
        layer_out,
        input_grad,
        qkv_all,
        dense_all[:, :, :width],
        up_all,
        dense_all[:, :, -width:],
        gain_back(qkv_weight, qkv_all, attn_gain),
        gain_back(up_weight, up_all, mlp_gain),
        scale_grad,
    )


def per_device(*args):
    tokens, segments = args[0], args[1]
    sizes = tuple(lax.axis_size(axis) for axis in ALL)
    heads = tokens.shape[2] // args[8].shape[1]
    spread = (
        sizes == (4, 2, 4)
        and tokens.shape[0] == 2
        and args[2].shape[0] == 2
        and tokens.shape[1] % 128 == 0
        and Q_ROWS % tokens.shape[1] == 0
        and segments.shape[1] <= WINDOW
        and segments.shape[1] % Q_ROWS == 0
        and heads % 4 == 0
        and tokens.shape[2] % 256 == 0
    )
    return spread_device(*args) if spread else general_device(*args)


def solution(mesh):
    rows = P(None, ALL, None)
    by_token = P("batch", ("blk", "head"), None)
    return jax.shard_map(
        per_device,
        mesh=mesh,
        in_specs=(
            by_token, P("batch", None), rows, rows, rows, rows, P(None, ALL), P(None, ALL), P(),
            by_token,
        ),
        out_specs=(
            by_token, by_token, rows, rows, rows, rows, P(None, ALL), P(None, ALL), P(),
        ),
        check_vma=False,
    )
```

```python
import functools
import math

import jax
import jax.numpy as jnp
from jax import lax
from jax.experimental import pallas as pl
from jax.experimental.pallas import tpu as pltpu
from jax.sharding import PartitionSpec as P

WINDOW = 1024
EPSILON = 1e-06
SCALE_BASE = 1.4426950408889634
MASKED_SCORE = -1e30

ALL = ("batch", "blk", "head")
REST = ("batch", "blk")
F32 = jnp.float32
BF16 = jnp.bfloat16


def shifted(block, axis, distance):
    devices = range(lax.axis_size(axis))
    route = [(i - distance, i) for i in devices if i - distance in devices]
    return lax.ppermute(block, axis, route)


NT = (((1,), (1,)), ((), ()))
TN = (((0,), (0,)), ((), ()))


def dot(left, right):
    return jnp.dot(left, right, preferred_element_type=F32)


def dot_rows(left, right):
    return lax.dot_general(left, right, (((0,), (0,)), ((), ())), preferred_element_type=F32)


def dot_cols(left, right):
    return lax.dot_general(left, right, (((1,), (1,)), ((), ())), preferred_element_type=F32)


def normalize(stream, gain):
    factor = lax.rsqrt(jnp.mean(stream * stream, axis=-1, keepdims=True) + EPSILON)
    return stream * factor * gain, factor


def norm_back(upper, stream, factor, gain):
    inner = upper * gain
    gain_grad = jnp.sum(upper * stream * factor, axis=0)
    lower = factor * inner - stream * factor * factor * factor * jnp.mean(
        inner * stream, axis=-1, keepdims=True
    )
    return lower, gain_grad


class Plan:
    def __init__(self, tokens):
        self.seqs, self.rows, self.width = tokens.shape
        self.heads = lax.axis_size("head")
        self.blks = lax.axis_size("blk")
        self.block = self.rows * self.heads
        self.whole = self.seqs % self.blks == 0
        if self.whole:
            self.groups, self.own_seqs = self.blks, self.seqs // self.blks
            self.reach = 0
        else:
            self.groups, self.own_seqs = 1, self.seqs
            self.reach = min((WINDOW - 1) // self.block + 1, self.blks - 1)
        self.length = self.groups * self.block
        self.tokens = self.seqs * self.rows


def to_plan(plan, array):
    if plan.whole and plan.blks > 1:
        array = lax.all_to_all(array, "blk", split_axis=0, concat_axis=0, tiled=True)
    return array.reshape(plan.tokens, plan.width)


def from_plan(plan, flat):
    array = flat.reshape(plan.seqs, plan.rows, plan.width)
    if plan.whole and plan.blks > 1:
        array = lax.all_to_all(array, "blk", split_axis=0, concat_axis=0, tiled=True)
    return array


def in_sequence(plan, by_head, width):
    parts = by_head.reshape(plan.heads, plan.groups, plan.own_seqs, plan.rows, width)
    return parts.transpose(2, 1, 0, 3, 4).reshape(-1, width)


def by_owner(plan, rows, width):
    parts = rows.reshape(plan.own_seqs, plan.groups, plan.heads, plan.rows, width)
    return parts.transpose(2, 1, 0, 3, 4).reshape(plan.heads, plan.tokens, width)


def gather_tokens(plan, rows):
    moved = lax.all_gather(rows, "head", axis=0, tiled=False)
    return in_sequence(plan, moved, rows.shape[-1])


def scatter_tokens(plan, rows):
    width = rows.shape[-1]
    return lax.psum_scatter(
        by_owner(plan, rows.astype(BF16), width), "head", scatter_dimension=0, tiled=False
    ).astype(F32)


def heads_to_tokens(plan, rows):
    part = rows.shape[-1]
    moved = lax.all_to_all(
        by_owner(plan, rows, part), "head", split_axis=0, concat_axis=0, tiled=True
    )
    return moved.transpose(1, 0, 2).reshape(plan.tokens, plan.heads * part)


def tokens_to_heads(plan, rows):
    part = rows.shape[-1] // plan.heads
    sent = rows.reshape(plan.tokens, plan.heads, part).transpose(1, 0, 2)
    moved = lax.all_to_all(sent, "head", split_axis=0, concat_axis=0, tiled=True)
    return in_sequence(plan, moved, part)


def gather_qkv(rows):
    own, width = rows.shape
    heads = lax.axis_size("head")
    part = width // 3 // heads
    sent = rows.reshape(own, 3, heads, part).transpose(2, 0, 1, 3).reshape(heads, own, 3 * part)
    moved = lax.all_to_all(sent, "head", split_axis=0, concat_axis=0, tiled=True)
    full = lax.all_gather(moved, REST, axis=0, tiled=True)
    return full.reshape(-1, 3 * part)


def scatter_qkv(grad):
    heads = lax.axis_size("head")
    part = grad.shape[1] // 3
    summed = lax.psum_scatter(grad.astype(BF16), REST, scatter_dimension=0, tiled=True)
    own = summed.shape[0] // heads
    moved = lax.all_to_all(
        summed.reshape(heads, own, 3 * part), "head", split_axis=0, concat_axis=0, tiled=True
    )
    return (
        moved.reshape(heads, own, 3, part)
        .transpose(1, 2, 0, 3)
        .reshape(own, 3 * heads * part)
        .astype(F32)
    )


def window_mask(plan, segments, block_index):
    key_count = plan.length + plan.reach * plan.block
    if plan.whole:
        query_segs, key_segs = segments, segments
    else:
        leading = jnp.full((plan.own_seqs, plan.reach * plan.block), -1, jnp.int32)
        padded = jnp.concatenate([leading, segments], axis=1)
        start = block_index * plan.block
        query_segs = lax.dynamic_slice_in_dim(segments, start, plan.block, 1)
        key_segs = lax.dynamic_slice_in_dim(padded, start, key_count, 1)
    query_place = jnp.arange(plan.length, dtype=jnp.int32)[:, None] + plan.reach * plan.block
    key_place = jnp.arange(key_count, dtype=jnp.int32)[None, :]
    near = (key_place <= query_place) & (query_place - key_place < WINDOW)
    return (key_segs[:, None, :] == query_segs[:, :, None]) & near[None]


def with_earlier(plan, own):
    arrived = [own]
    for _ in range(plan.reach):
        arrived.append(shifted(arrived[-1], "blk", 1))
    return jnp.concatenate(arrived[::-1], axis=1) if plan.reach else own


def to_earlier(plan, grads):
    if not plan.reach:
        return grads
    block = plan.block
    total = grads[:, :block]
    for step in range(1, plan.reach + 1):
        total = (
            shifted(total.astype(BF16), "blk", -1).astype(F32)
            + grads[:, step * block : (step + 1) * block]
        )
    return total


def scores_of(queries, keys, allowed):
    scores = jnp.einsum("sqhd,skhd->shqk", queries, keys, preferred_element_type=F32)
    return jnp.where(allowed[:, None], scores, MASKED_SCORE)


def attend(queries, keys, values, allowed):
    scores = scores_of(queries, keys, allowed)
    top_score = jnp.max(scores, axis=-1, keepdims=True)
    exp_terms = jnp.exp(scores - top_score)
    totals = jnp.sum(exp_terms, axis=-1, keepdims=True)
    probs_low = (exp_terms / totals).astype(BF16)
    attended = jnp.einsum("shqk,skhd->sqhd", probs_low, values, preferred_element_type=F32)
    return attended, top_score + jnp.log(totals)


def attend_back(queries, keys, values, allowed, log_total, attended_grad):
    probs = jnp.exp(scores_of(queries, keys, allowed) - log_total)
    probs_low = probs.astype(BF16)
    values_grad = jnp.einsum(
        "shqk,sqhd->skhd", probs_low, attended_grad, preferred_element_type=F32
    )
    probs_grad = jnp.einsum("sqhd,skhd->shqk", attended_grad, values, preferred_element_type=F32)
    row_dot = jnp.sum(probs_grad * probs, axis=-1, keepdims=True)
    scores_low = (probs * (probs_grad - row_dot)).astype(BF16)
    queries_grad = jnp.einsum("shqk,skhd->sqhd", scores_low, keys, preferred_element_type=F32)
    keys_grad = jnp.einsum("shqk,sqhd->skhd", scores_low, queries, preferred_element_type=F32)
    return queries_grad, keys_grad, values_grad


def forward(plan, stream, qkv, dense, gains, scale_vec, allowed):
    width = plan.width
    head_dim = scale_vec.shape[0]
    part = qkv.shape[1] // 3
    local_heads = part // head_dim
    split = (plan.own_seqs, plan.length, local_heads, head_dim)
    out_w, up_w, down_w = dense[:, :width], dense[:, width:-width], dense[:, -width:]
    normed, factor_one = normalize(stream, gains[0])
    normed_all = gather_tokens(plan, normed.astype(BF16))
    projected = dot(normed_all, qkv)
    query_pre = projected[:, :part].reshape(split)
    queries = (query_pre * scale_vec).astype(BF16)
    keys = with_earlier(plan, projected[:, part : 2 * part].astype(BF16).reshape(split))
    values = with_earlier(plan, projected[:, 2 * part :].astype(BF16).reshape(split))
    attended_part, log_total = attend(queries, keys, values, allowed)
    attended = heads_to_tokens(plan, attended_part.astype(BF16).reshape(-1, part))
    middle = stream + dot(attended, out_w)
    normed_two, factor_two = normalize(middle, gains[1])
    normed_two = normed_two.astype(BF16)
    hidden = dot(normed_two, up_w)
    active = (hidden * jax.nn.sigmoid(hidden)).astype(BF16)
    result = middle + dot(active, down_w)
    kept = (
        stream, factor_one, normed_all, query_pre, queries, keys, values, log_total,
        attended, middle, factor_two, normed_two, hidden, active,
    )
    return result, kept


def backward(plan, upper, kept, qkv, dense, gains, scale_vec, allowed):
    (
        stream, factor_one, normed_all, query_pre, queries, keys, values, log_total,
        attended, middle, factor_two, normed_two, hidden, active,
    ) = kept
    width = plan.width
    head_dim = scale_vec.shape[0]
    part = qkv.shape[1] // 3
    out_w, up_w, down_w = dense[:, :width], dense[:, width:-width], dense[:, -width:]
    upper_low = upper.astype(BF16)
    down_grad = dot_rows(active, upper_low)
    active_grad = dot_cols(upper_low, down_w)
    gate = jax.nn.sigmoid(hidden)
    hidden_low = (active_grad * gate * (1.0 + hidden * (1.0 - gate))).astype(BF16)
    up_grad = dot_rows(normed_two, hidden_low)
    extra_two, mlp_gain_grad = norm_back(dot_cols(hidden_low, up_w), middle, factor_two, gains[1])
    middle_grad = upper + extra_two
    middle_low = middle_grad.astype(BF16)
    out_grad = dot_rows(attended, middle_low)
    dense_grad = jnp.concatenate([out_grad, up_grad, down_grad], axis=1).astype(BF16)
    dense_own = lax.psum_scatter(dense_grad, ALL, scatter_dimension=0, tiled=True)
    attended_grad = tokens_to_heads(plan, dot_cols(middle_low, out_w).astype(BF16))
    queries_grad, keys_grad, values_grad = attend_back(
        queries, keys, values, allowed, log_total, attended_grad.reshape(queries.shape)
    )
    query_bar = queries_grad.astype(BF16).astype(F32)
    scale_vec_grad = jnp.sum((query_bar * query_pre).reshape(-1, head_dim), axis=0)
    query_low = (query_bar * scale_vec).astype(BF16).reshape(-1, part)
    keys_low = to_earlier(plan, keys_grad).astype(BF16).reshape(-1, part)
    values_low = to_earlier(plan, values_grad).astype(BF16).reshape(-1, part)
    projected_low = jnp.concatenate([query_low, keys_low, values_low], axis=1)
    normed_grad = scatter_tokens(plan, dot_cols(projected_low, qkv))
    qkv_own = scatter_qkv(dot_rows(normed_all, projected_low))
    extra_one, attn_gain_grad = norm_back(normed_grad, stream, factor_one, gains[0])
    lower = middle_grad + extra_one
    return lower, qkv_own, dense_own, (attn_gain_grad, mlp_gain_grad), scale_vec_grad


def general_device(
    tokens,
    segments,
    qkv_weight,
    out_weight,
    up_weight,
    down_weight,
    attn_gain,
    mlp_gain,
    scale_param,
    cotangent,
):
    plan = Plan(tokens)
    layers, head_dim = scale_param.shape
    block_index = lax.axis_index("blk")
    scale_vecs = SCALE_BASE / math.sqrt(head_dim) * jax.nn.softplus(scale_param)
    own_gains = jnp.concatenate([attn_gain, mlp_gain], axis=0)
    gains = (
        lax.all_gather(own_gains.reshape(1, -1), ALL, axis=0, tiled=True)
        .reshape(-1, 2 * layers, attn_gain.shape[1])
        .transpose(1, 0, 2)
        .reshape(2 * layers, plan.width)
        .astype(F32)
    )
    if plan.whole:
        segments = lax.dynamic_slice_in_dim(
            segments, block_index * plan.own_seqs, plan.own_seqs, 0
        )
    allowed = window_mask(plan, segments, block_index)
    stream = to_plan(plan, tokens).astype(F32)
    qkvs, denses, kept = [], [], []
    for layer in range(layers):
        qkvs.append(gather_qkv(qkv_weight[layer]))
        own = jnp.concatenate([out_weight[layer], up_weight[layer], down_weight[layer]], axis=1)
        denses.append(lax.all_gather(own, ALL, axis=0, tiled=True))
        layer_gains = (gains[layer], gains[layers + layer])
        stream, saved = forward(
            plan, stream, qkvs[layer], denses[layer], layer_gains, scale_vecs[layer], allowed
        )
        kept.append(saved)
    layer_out = from_plan(plan, stream.astype(BF16))
    upper = to_plan(plan, cotangent).astype(F32)
    qkv_grads, dense_grads = [None] * layers, [None] * layers
    gain_grads, scale_grads = [None] * layers, [None] * layers
    for layer in reversed(range(layers)):
        layer_gains = (gains[layer], gains[layers + layer])
        upper, qkv_grads[layer], dense_grads[layer], gain_grads[layer], scale_grads[layer] = (
            backward(
                plan, upper, kept[layer], qkvs[layer], denses[layer], layer_gains,
                scale_vecs[layer], allowed,
            )
        )
    input_grad = from_plan(plan, upper.astype(BF16)).astype(F32)
    small = jnp.concatenate(
        [g[0] for g in gain_grads] + [g[1] for g in gain_grads] + scale_grads, axis=0
    )
    total = lax.psum(small, ALL)
    gain_total = total[: 2 * layers * plan.width].reshape(2 * layers, plan.width)
    owner = lax.axis_index(ALL)
    gain_rows = attn_gain.shape[1]
    own_total = lax.dynamic_slice_in_dim(gain_total, owner * gain_rows, gain_rows, 1)
    scale_total = total[2 * layers * plan.width :].reshape(layers, head_dim)
    scale_grad = scale_total * (SCALE_BASE / math.sqrt(head_dim)) * jax.nn.sigmoid(scale_param)
    dense_all = jnp.stack(dense_grads).astype(F32)
    width = plan.width
    return (
        layer_out,
        input_grad,
        jnp.stack(qkv_grads),
        dense_all[:, :, :width],
        dense_all[:, :, width:-width],
        dense_all[:, :, -width:],
        own_total[:layers],
        own_total[layers:],
        scale_grad,
    )


Q_ROWS = 256
KERNEL = pltpu.CompilerParams(vmem_limit_bytes=32 * 1024 * 1024)
LIGHT = pl.CostEstimate(flops=1 << 20, bytes_accessed=1 << 20, transcendentals=0)


def in_hbm(*arrays):
    return [pltpu.with_memory_space_constraint(array, pltpu.HBM) for array in arrays]


def allowed_keys(col, row, first):
    count = first + row.shape[1]
    key_place = lax.broadcasted_iota(jnp.int32, (count, row.shape[1]), 0)
    query_place = lax.broadcasted_iota(jnp.int32, (count, row.shape[1]), 1) + first
    return (col[:count] == row) & (key_place <= query_place)


def token_places(length, heads, token_rows):
    for first in range(0, length, Q_ROWS):
        parts = []
        for start in range(0, Q_ROWS, token_rows):
            place = (first + start) // token_rows
            parts.append((start, place % heads, place // heads * token_rows))
        yield first, parts


def attend_kernel(token_rows, proj_ref, scale_ref, col_ref, row_ref, out_ref, lse_ref):
    length = proj_ref.shape[-1]
    queries = (proj_ref[0, 0] * scale_ref[...]).astype(BF16)
    keys = proj_ref[1, 0].T.astype(BF16)
    values = proj_ref[2, 0].astype(BF16)
    for first, parts in token_places(length, out_ref.shape[0], token_rows):
        end = first + Q_ROWS
        scores = jnp.dot(keys[:end], queries[:, first:end], preferred_element_type=F32)
        allowed = allowed_keys(col_ref[...], row_ref[:, first:end], first)
        scores = jnp.where(allowed, scores, MASKED_SCORE)
        top = jnp.max(scores, axis=0, keepdims=True)
        terms = jnp.exp(scores - top)
        total = jnp.sum(terms, axis=0, keepdims=True)
        probs = (terms * (1.0 / total)).astype(BF16)
        attended = jnp.dot(values[:, :end], probs, preferred_element_type=F32).astype(BF16)
        lse_ref[0, :, first:end] = top + jnp.log(total)
        for start, owner, offset in parts:
            out_ref[owner, 0, :, offset : offset + token_rows] = attended[
                :, start : start + token_rows
            ]


def attend_rows(projected, scale_vec, segments, owners, token_rows):
    head_dim = scale_vec.shape[0]
    length = projected.shape[1]
    local_heads = projected.shape[0] // 3 // head_dim
    tokens = length // owners
    attended, log_total = pl.pallas_call(
        functools.partial(attend_kernel, token_rows),
        grid=(local_heads,),
        in_specs=[
            pl.BlockSpec((3, 1, head_dim, length), lambda h: (0, h, 0, 0)),
            pl.BlockSpec((head_dim, 1), lambda h: (0, 0)),
            pl.BlockSpec((length, 1), lambda h: (0, 0)),
            pl.BlockSpec((1, length), lambda h: (0, 0)),
        ],
        out_specs=[
            pl.BlockSpec((owners, 1, head_dim, tokens), lambda h: (0, h, 0, 0)),
            pl.BlockSpec((1, 1, length), lambda h: (h, 0, 0)),
        ],
        out_shape=[
            jax.ShapeDtypeStruct((owners, local_heads, head_dim, tokens), BF16),
            jax.ShapeDtypeStruct((local_heads, 1, length), F32),
        ],
        compiler_params=KERNEL,
        cost_estimate=LIGHT,
    )(
        projected.reshape(3, local_heads, head_dim, length),
        scale_vec.reshape(head_dim, 1),
        segments.reshape(length, 1),
        segments.reshape(1, length),
    )
    return attended.reshape(owners, local_heads * head_dim, tokens), log_total


def attend_back_kernel(
    token_rows,
    proj_ref,
    grad_ref,
    lse_ref,
    scale_ref,
    col_ref,
    row_ref,
    out_ref,
    scale_grad_ref,
    keys_acc,
    values_acc,
):
    length = proj_ref.shape[-1]
    scale = scale_ref[...]
    query_pre = proj_ref[0, 0]
    queries = (query_pre * scale).astype(BF16)
    keys_t = proj_ref[1, 0].astype(BF16)
    keys = proj_ref[1, 0].T.astype(BF16)
    values = proj_ref[2, 0].T.astype(BF16)
    keys_acc[...] = jnp.zeros_like(keys_acc)
    values_acc[...] = jnp.zeros_like(values_acc)
    scale_grad = jnp.zeros((scale.shape[0], 1), F32)
    for first, parts in token_places(length, grad_ref.shape[0], token_rows):
        end = first + Q_ROWS
        block = queries[:, first:end]
        grad = jnp.concatenate(
            [grad_ref[owner, 0, :, at : at + token_rows] for _, owner, at in parts], axis=1
        )
        scores = jnp.dot(keys[:end], block, preferred_element_type=F32)
        allowed = allowed_keys(col_ref[...], row_ref[:, first:end], first)
        scores = jnp.where(allowed, scores, MASKED_SCORE)
        probs = jnp.exp(scores - lse_ref[0, :, first:end])
        probs_grad = jnp.dot(values[:end], grad, preferred_element_type=F32)
        row_dot = jnp.sum(probs_grad * probs, axis=0, keepdims=True)
        scores_low = (probs * (probs_grad - row_dot)).astype(BF16)
        values_acc[:, :end] += lax.dot_general(
            grad, probs.astype(BF16), NT, preferred_element_type=F32
        )
        keys_acc[:, :end] += lax.dot_general(
            block, scores_low, NT, preferred_element_type=F32
        )
        query_bar = jnp.dot(keys_t[:, :end], scores_low, preferred_element_type=F32)
        query_bar = query_bar.astype(BF16).astype(F32)
        scale_grad += jnp.sum(query_bar * query_pre[:, first:end], axis=1, keepdims=True)
        out_ref[0, 0, :, first:end] = (query_bar * scale).astype(BF16)
    out_ref[1, 0] = keys_acc[...].astype(BF16)
    out_ref[2, 0] = values_acc[...].astype(BF16)
    spread = jnp.broadcast_to(scale_grad, scale_grad_ref.shape)

    @pl.when(pl.program_id(0) == 0)
    def _():
        scale_grad_ref[...] = spread

    @pl.when(pl.program_id(0) > 0)
    def _():
        scale_grad_ref[...] += spread


def attend_back_rows(projected, attended_grad, log_total, scale_vec, segments, token_rows):
    head_dim = scale_vec.shape[0]
    length = projected.shape[1]
    local_heads = projected.shape[0] // 3 // head_dim
    owners, _, tokens = attended_grad.shape
    lanes = 128
    grads, scale_grad = pl.pallas_call(
        functools.partial(attend_back_kernel, token_rows),
        grid=(local_heads,),
        in_specs=[
            pl.BlockSpec((3, 1, head_dim, length), lambda h: (0, h, 0, 0)),
            pl.BlockSpec((owners, 1, head_dim, tokens), lambda h: (0, h, 0, 0)),
            pl.BlockSpec((1, 1, length), lambda h: (h, 0, 0)),
            pl.BlockSpec((head_dim, 1), lambda h: (0, 0)),
            pl.BlockSpec((length, 1), lambda h: (0, 0)),
            pl.BlockSpec((1, length), lambda h: (0, 0)),
        ],
        out_specs=[
            pl.BlockSpec((3, 1, head_dim, length), lambda h: (0, h, 0, 0)),
            pl.BlockSpec((head_dim, lanes), lambda h: (0, 0)),
        ],
        out_shape=[
            pltpu.HBM((3, local_heads, head_dim, length), BF16),
            pltpu.HBM((head_dim, lanes), F32),
        ],
        scratch_shapes=[
            pltpu.VMEM((head_dim, length), F32),
            pltpu.VMEM((head_dim, length), F32),
        ],
        compiler_params=KERNEL,
        cost_estimate=LIGHT,
    )(
        *in_hbm(
            projected.reshape(3, local_heads, head_dim, length),
            attended_grad.reshape(owners, local_heads, head_dim, tokens),
        ),
        log_total,
        scale_vec.reshape(head_dim, 1),
        segments.reshape(length, 1),
        segments.reshape(1, length),
    )
    return grads.reshape(3 * local_heads * head_dim, length), scale_grad[:, 0]


def dense_grad_kernel(
    core_ref, attended_ref, normed_ref, active_ref, out_bar, up_bar, down_bar,
    own_ref, other_ref, normed_t, active_t,
):
    tile = pl.program_id(0)
    rows, width = own_ref.shape[1] * own_ref.shape[3] * 2, out_bar.shape[1]

    @pl.when(tile == 0)
    def _():
        normed_t[...] = normed_ref[...].astype(F32).T.astype(BF16)
        active_t[...] = active_ref[...].astype(F32).T.astype(BF16)

    start = pl.multiple_of(tile * rows, rows)
    first_core = core_ref[2] == 0
    lefts = (attended_ref, normed_t, active_t)
    for i, (left, right) in enumerate(zip(lefts, (out_bar, up_bar, down_bar))):
        grad = jnp.dot(left[pl.ds(start, rows), :], right[...], preferred_element_type=F32)
        grad = grad.reshape(2, 2, rows // 4, width)
        one, two = grad[:, 0], grad[:, 1]
        own_ref[0, :, 0, :, i * width : (i + 1) * width] = jnp.where(
            first_core, one, two
        ).astype(BF16)
        other_ref[0, :, 0, :, i * width : (i + 1) * width] = jnp.where(
            first_core, two, one
        ).astype(BF16)


def dense_grads(attended_t, normed, active, out_bar, up_bar, down_bar):
    width, tokens = attended_t.shape
    own = width // 32
    whole = pl.BlockSpec((tokens, width), lambda i, core: (0, 0))
    rows = pl.BlockSpec((1, 2, 1, own, 3 * width), lambda i, core: (i % 2, 0, i // 2, 0, 0))
    shape = pltpu.HBM((2, 2, 4, own, 3 * width), BF16)
    return pl.pallas_call(
        dense_grad_kernel,
        grid_spec=pltpu.PrefetchScalarGridSpec(
            num_scalar_prefetch=1,
            grid=(8,),
            in_specs=[pl.BlockSpec((width, tokens), lambda i, core: (0, 0))] + [whole] * 5,
            out_specs=[rows, rows],
            scratch_shapes=[pltpu.VMEM((width, tokens), BF16)] * 2,
        ),
        out_shape=[shape, shape],
        compiler_params=KERNEL,
        cost_estimate=LIGHT,
    )(place(), *in_hbm(attended_t, normed, active, out_bar, up_bar, down_bar))


def place():
    head = lax.axis_index("head")
    return jnp.stack([lax.axis_index("blk"), head // 2, head % 2]).astype(jnp.int32)


def assemble_kernel(place_ref, *refs):
    pieces, whole_ref = refs[:10], refs[10]
    half = whole_ref.shape[-1] // 2
    blk, row, core = place_ref[0], place_ref[1], place_ref[2]
    for i in range(2):
        at_core = core if i == 0 else 1 - core
        own, across, beside, one, two = pieces[5 * i : 5 * i + 5]
        whole_ref[0, blk, row, at_core] = own[0]
        whole_ref[0, 1 - blk, row, at_core] = across[0]
        whole_ref[0, blk, 1 - row, at_core] = beside[0]
        whole_ref[0, 1 - blk, 1 - row, at_core, :, :half] = one[0]
        whole_ref[0, 1 - blk, 1 - row, at_core, :, half:] = two[0]


def assemble(pieces):
    batch, own, columns = pieces[0].shape
    specs = [
        pl.BlockSpec((1, own, piece.shape[-1]), lambda i, at: (i, 0, 0))
        for piece in pieces
    ]
    whole = pl.pallas_call(
        assemble_kernel,
        grid_spec=pltpu.PrefetchScalarGridSpec(
            num_scalar_prefetch=1,
            grid=(batch,),
            in_specs=specs,
            out_specs=pl.BlockSpec((1, 2, 2, 2, own, columns), lambda i, at: (i, 0, 0, 0, 0, 0)),
        ),
        out_shape=jax.ShapeDtypeStruct((batch, 2, 2, 2, own, columns), BF16),
        compiler_params=KERNEL,
        cost_estimate=LIGHT,
    )(place(), *pieces)
    return whole.reshape(-1, columns)


def assemble_columns_kernel(place_ref, along_ref, across_ref, whole_ref, *extra_ref):
    blk = place_ref[0]
    columns = whole_ref.shape[-1]
    whole_ref[0, blk] = along_ref[0, :, :columns]
    whole_ref[0, 1 - blk] = across_ref[0, :, :columns]
    for extra in extra_ref:
        extra[0, blk] = along_ref[0, :, columns:]
        extra[0, 1 - blk] = across_ref[0, :, columns:]


def assemble_columns(along, across, columns):
    batch, own, both = along.shape
    rows = pl.BlockSpec((1, own, both), lambda i, at: (i, 0, 0))
    shapes = [(batch, 2, own, columns)]
    if both > columns:
        shapes.append((batch, 2, own, both - columns))
    parts = pl.pallas_call(
        assemble_columns_kernel,
        grid_spec=pltpu.PrefetchScalarGridSpec(
            num_scalar_prefetch=1,
            grid=(batch,),
            in_specs=[rows, rows],
            out_specs=[pl.BlockSpec((1,) + s[1:], lambda i, at: (i, 0, 0, 0)) for s in shapes],
        ),
        out_shape=[pltpu.HBM(s, BF16) for s in shapes],
        compiler_params=KERNEL,
        cost_estimate=LIGHT,
    )(place(), *in_hbm(along, across))
    return [part.reshape(-1, part.shape[-1]) for part in parts]


def assemble_wide_kernel(place_ref, along_ref, across_ref, whole_ref):
    blk = place_ref[0]
    own, columns = along_ref.shape[1], whole_ref.shape[-1]
    for i in range(along_ref.shape[-1] // columns):
        place, part = slice(i * own, (i + 1) * own), slice(i * columns, (i + 1) * columns)
        whole_ref[0, blk, place, :] = along_ref[0, :, part]
        whole_ref[0, 1 - blk, place, :] = across_ref[0, :, part]


def assemble_wide(along, across, columns):
    batch, own, wide = along.shape
    rows = own * (wide // columns)
    piece = pl.BlockSpec((1, own, wide), lambda i, at: (i, 0, 0))
    whole = pl.pallas_call(
        assemble_wide_kernel,
        grid_spec=pltpu.PrefetchScalarGridSpec(
            num_scalar_prefetch=1,
            grid=(batch,),
            in_specs=[piece, piece],
            out_specs=pl.BlockSpec((1, 2, rows, columns), lambda i, at: (i, 0, 0, 0)),
        ),
        out_shape=pltpu.HBM((batch, 2, rows, columns), BF16),
        compiler_params=KERNEL,
        cost_estimate=LIGHT,
    )(place(), *in_hbm(along, across))
    return whole.reshape(-1, columns)


def project_kernel(with_norm, place_ref, *refs):
    pieces, (gain_ref, weight_ref, normed_ref, projected_ref) = refs[:4], refs[4:]
    head = place_ref[1] * 2 + place_ref[2]
    rows = pieces[0].shape[0]
    for i, piece in enumerate(pieces):
        value = piece[...]
        if with_norm:
            stream = value.astype(F32)
            factor = lax.rsqrt(jnp.mean(stream * stream, axis=-1, keepdims=True) + EPSILON)
            value = (stream * factor * gain_ref[...]).astype(BF16)
        normed_ref[pl.ds(pl.multiple_of((head ^ i) * rows, rows), rows), :] = value
    projected = jnp.dot(normed_ref[...], weight_ref[...], preferred_element_type=F32)
    projected_ref[...] = projected.T


def project(pieces, gain, weight, with_norm, token_rows):
    tokens, width = pieces[0].shape
    length, columns = 4 * tokens, weight.shape[1]
    groups = tokens // token_rows
    piece = pl.BlockSpec((token_rows, width), lambda g, at: (g, 0))
    return pl.pallas_call(
        functools.partial(project_kernel, with_norm),
        grid_spec=pltpu.PrefetchScalarGridSpec(
            num_scalar_prefetch=1,
            grid=(groups,),
            in_specs=[piece] * 4
            + [
                pl.BlockSpec((1, width), lambda g, at: (0, 0)),
                pl.BlockSpec((width, columns), lambda g, at: (0, 0)),
            ],
            out_specs=[
                pl.BlockSpec((4 * token_rows, width), lambda g, at: (g, 0)),
                pl.BlockSpec((columns, 4 * token_rows), lambda g, at: (0, g)),
            ],
        ),
        out_shape=[
            pltpu.HBM((length, width), BF16),
            pltpu.HBM((columns, length), F32),
        ],
        compiler_params=KERNEL,
        cost_estimate=LIGHT,
    )(place(), *in_hbm(*pieces), gain.reshape(1, width), *in_hbm(weight))


def project_back_kernel(
    place_ref, bars_ref, weight_ref, normed_ref, own_ref, other_ref, grad_ref, bars_t
):
    @pl.when(pl.program_id(0) == 0)
    def _():
        bars_t[...] = bars_ref[...].astype(F32).T.astype(BF16)

    upper = lax.dot_general(bars_t[...], weight_ref[...], NT, preferred_element_type=F32)
    upper = upper.reshape(2, 2, 2, -1, upper.shape[-1])
    first_core = place_ref[2] == 0
    one, two = upper[:, :, 0], upper[:, :, 1]
    own_ref[...] = jnp.where(first_core, one, two)
    other_ref[...] = jnp.where(first_core, two, one).astype(BF16)
    grad = lax.dot_general(normed_ref[...], bars_t[...], TN, preferred_element_type=F32)
    grad_ref[...] = grad.astype(BF16)


def project_back(bars, weight, normed, token_rows):
    columns, length = bars.shape
    width = weight.shape[0]
    tile = width // 2
    quarter = pl.BlockSpec((2, 2, token_rows, tile), lambda i, at: (0, 0, 0, i))
    return pl.pallas_call(
        project_back_kernel,
        grid_spec=pltpu.PrefetchScalarGridSpec(
            num_scalar_prefetch=1,
            grid=(2,),
            in_specs=[
                pl.BlockSpec((columns, length), lambda i, at: (0, 0)),
                pl.BlockSpec((tile, columns), lambda i, at: (i, 0)),
                pl.BlockSpec((length, tile), lambda i, at: (0, i)),
            ],
            out_specs=[quarter, quarter, pl.BlockSpec((tile, columns), lambda i, at: (i, 0))],
            scratch_shapes=[pltpu.VMEM((length, columns), BF16)],
        ),
        out_shape=[
            pltpu.HBM((2, 2, token_rows, width), F32),
            pltpu.HBM((2, 2, token_rows, width), BF16),
            pltpu.HBM((width, columns), BF16),
        ],
        compiler_params=KERNEL,
        cost_estimate=LIGHT,
    )(place(), *in_hbm(bars, weight, normed))


def rows_back_kernel(place_ref, bars_ref, weight_ref, own_ref, other_ref, bars_t):
    @pl.when(pl.program_id(0) == 0)
    def _():
        bars_t[...] = bars_ref[...].astype(F32).T.astype(BF16)

    upper = lax.dot_general(bars_t[...], weight_ref[...], NT, preferred_element_type=F32)
    upper = upper.reshape(2, 2, 2, -1, upper.shape[-1])
    first_core = place_ref[2] == 0
    one, two = upper[:, :, 0], upper[:, :, 1]
    own_ref[...] = jnp.where(first_core, one, two)
    other_ref[...] = jnp.where(first_core, two, one).astype(BF16)


def rows_back(bars, weight, token_rows):
    columns, length = bars.shape
    width = weight.shape[0]
    tile = width // 2
    quarter = pl.BlockSpec((2, 2, token_rows, tile), lambda i, at: (0, 0, 0, i))
    return pl.pallas_call(
        rows_back_kernel,
        grid_spec=pltpu.PrefetchScalarGridSpec(
            num_scalar_prefetch=1,
            grid=(2,),
            in_specs=[
                pl.BlockSpec((columns, length), lambda i, at: (0, 0)),
                pl.BlockSpec((tile, columns), lambda i, at: (i, 0)),
            ],
            out_specs=[quarter, quarter],
            scratch_shapes=[pltpu.VMEM((length, columns), BF16)],
        ),
        out_shape=[
            pltpu.HBM((2, 2, token_rows, width), F32),
            pltpu.HBM((2, 2, token_rows, width), BF16),
        ],
        compiler_params=KERNEL,
        cost_estimate=LIGHT,
    )(place(), *in_hbm(bars, weight))


def weight_back_kernel(bars_ref, normed_ref, grad_ref):
    grad = jnp.dot(bars_ref[...], normed_ref[...], preferred_element_type=F32)
    grad_ref[...] = grad.T.astype(BF16)


def weight_back(bars, normed):
    columns, length = bars.shape
    width = normed.shape[1]
    tile = width // 5
    return pl.pallas_call(
        weight_back_kernel,
        grid=(5,),
        in_specs=[
            pl.BlockSpec((columns, length), lambda i: (0, 0)),
            pl.BlockSpec((length, tile), lambda i: (0, i)),
        ],
        out_specs=pl.BlockSpec((tile, columns), lambda i: (i, 0)),
        out_shape=pltpu.HBM((width, columns), BF16),
        compiler_params=KERNEL,
        cost_estimate=LIGHT,
    )(*in_hbm(bars, normed))


def tied(*arrays):
    return lax.optimization_barrier(arrays)


def swapped(array, axis, mask):
    size = lax.axis_size(axis)
    return lax.ppermute(array, axis, [(i, i ^ mask) for i in range(size)])


def pick(array, index, axis=0):
    return lax.dynamic_index_in_dim(array, index, axis, keepdims=False)


def swap_halves(array):
    me = lax.axis_index("blk")
    got = swapped(pick(array, 1 - me), "blk", 1)
    kept = pick(array, me)
    return jnp.stack([jnp.where(me == 0, kept, got), jnp.where(me == 0, got, kept)])


def scatter_row(halves):
    row = lax.axis_index("head") // 2
    got = swapped(pick(halves, 1 - row, 1).astype(BF16), "head", 2).astype(F32)
    return (pick(halves, row, 1) + got).reshape(-1, halves.shape[-1])


def over_head(parts):
    return lax.all_to_all(parts, "head", split_axis=0, concat_axis=0, tiled=True)


def qkv_columns(rows, extra):
    own, width = rows.shape
    part = width // 3 // 4
    sent = rows.reshape(own, 3, 4, part).transpose(2, 0, 1, 3).reshape(4, own, 3 * part)
    if extra is not None:
        sent = jnp.concatenate([sent, jnp.broadcast_to(extra[None], (4,) + extra.shape)], axis=2)
    return over_head(sent)


def along_batch(piece):
    return lax.all_gather(piece, "batch", axis=0, tiled=False)


def other_core(array):
    return swapped(array, "head", 1)


def to_beside(across):
    return swapped(across[..., : across.shape[-1] // 2], "head", 2)


def to_across(beside):
    return swapped(beside[..., beside.shape[-1] // 2 :], "blk", 1)


def over_batch(parts):
    return lax.psum_scatter(parts.astype(BF16), "batch", scatter_dimension=0, tiled=False)


def across_sum(halves):
    blk = lax.axis_index("blk")
    got = swapped(pick(halves, 1 - blk), "blk", 1).astype(F32)
    return (pick(halves, blk).astype(F32) + got).astype(BF16)


def columns_to_rows(summed):
    moved = over_head(summed.reshape(4, -1, summed.shape[-1]))
    rows = moved.shape[1]
    return moved.reshape(4, rows, 3, -1).transpose(1, 2, 0, 3).reshape(rows, -1).astype(F32)


def diagonal_rows(cored):
    blk, row = place()[:2]
    rows = pick(pick(cored, 1 - blk), 1 - row)
    half = rows.shape[-1] // 2
    return rows[..., :half], rows[..., half:]


def neighbour_rows(cored, one, two):
    blk, row = place()[:2]
    half = one.shape[-1]
    across = pick(pick(cored, 1 - blk), row)
    beside = pick(pick(cored, blk), 1 - row)
    across = jnp.concatenate(
        [across[..., :half], across[..., half:].astype(F32) + two.astype(F32)], axis=-1
    ).astype(BF16)
    beside = jnp.concatenate(
        [beside[..., :half].astype(F32) + one.astype(F32), beside[..., half:]], axis=-1
    ).astype(BF16)
    return across, beside


def sent_beside_and_across(across, beside):
    return swapped(across, "blk", 1), swapped(beside, "head", 2)


def heads_grad(weight, out_bar):
    return dot_cols(weight, out_bar).astype(BF16).reshape(4, -1, out_bar.shape[0])


def own_sum(cored, across, beside):
    blk, row = place()[:2]
    own = pick(pick(cored, blk), row)
    return own.astype(F32) + across.astype(F32) + beside.astype(F32)


def sum_all(array):
    for axis, mask in (("head", 1), ("head", 2), ("blk", 1), ("batch", 1), ("batch", 2)):
        array = array + swapped(array, axis, mask)
    return array


def gain_back(weight, weight_grad, gain):
    return jnp.sum(weight.astype(F32) * weight_grad, axis=-1) / gain.astype(F32)


def lower_of(upper, stream, factor, gain):
    return norm_back(upper, stream, factor, gain)[0]


def spread_device(
    tokens,
    segments,
    qkv_weight,
    out_weight,
    up_weight,
    down_weight,
    attn_gain,
    mlp_gain,
    scale_param,
    cotangent,
):
    layers, head_dim = scale_param.shape
    _, token_rows, width = tokens.shape
    scale_vecs = SCALE_BASE / math.sqrt(head_dim) * jax.nn.softplus(scale_param)
    segments = pick(segments, lax.axis_index("blk"))
    own_gains = jnp.concatenate([attn_gain, mlp_gain], axis=0)

    part3 = 3 * width // 4
    dense_own = [
        jnp.concatenate([out_weight[i], up_weight[i], down_weight[i]], axis=1) for i in (0, 1)
    ]

    first = swap_halves(tokens).reshape(-1, width)
    columns = qkv_columns(qkv_weight[0], own_gains.T)
    columns, first = tied(columns.reshape(-1, columns.shape[-1]), first)
    stream = first.astype(F32)
    along = along_batch(columns)
    far, near = swapped(first, "head", 2), other_core(first)
    both = other_core(far)
    along, near, far, both, dense_near = tied(along, near, far, both, dense_own[0])
    token_pieces = (first, near, far, both)
    dense_near = along_batch(dense_near)
    qkv_across = swapped(along, "blk", 1)
    next_columns = jnp.concatenate(list(qkv_columns(qkv_weight[1], None)), axis=1)
    qkv_across, dense_near, next_columns = tied(qkv_across, dense_near, next_columns)
    across, beside = swapped(dense_near, "blk", 1), swapped(dense_near, "head", 2)
    next_both = along_batch(jnp.stack([next_columns, dense_own[1]]))
    weight, gains = assemble_columns(along, qkv_across, part3)
    qkvs = [weight]
    gains = gains.T.astype(F32)

    kept, denses = [], []
    for layer in range(layers):
        normed, factor_one = normalize(stream, gains[layer])
        if layer == 1:
            normed, next_across, beside, dense_next = tied(
                normed.astype(BF16), next_across, beside, dense_next
            )
            far, near = swapped(normed, "head", 2), other_core(normed)
            across = swapped(dense_next, "blk", 1)
            token_pieces = (normed, near, far, other_core(far))
            qkvs.append(assemble_wide(next_along, next_across, part3))
        normed_all, projected = project(
            token_pieces, gains[layer], qkvs[layer], layer == 0, token_rows
        )
        if layer == 1:
            projected, across = tied(projected, across)
            one, two = to_beside(across), to_across(beside)
        attended, log_total = attend_rows(
            projected, scale_vecs[layer], segments, 4, token_rows
        )
        if layer == 0:
            attended, across, beside = tied(attended, across, beside)
            one, two = to_beside(across), to_across(beside)
        if layer == 0:
            attended_t, one, two, next_both = tied(over_head(attended), one, two, next_both)
            next_along, dense_next = next_both[:, 0], next_both[:, 1]
            next_across = swapped(next_along, "blk", 1)
        else:
            dense_near = dense_next
            attended, one, two, cotangent = tied(attended, one, two, cotangent)
            upper = swap_halves(cotangent)
            attended_t, upper = tied(over_head(attended), upper)
        pieces = (dense_near, across, beside, one, two)
        pieces += tuple(other_core(piece) for piece in pieces)
        if layer == 0:
            beside = swapped(dense_next, "head", 2)
        attended_t = attended_t.reshape(width, -1)
        denses.append(assemble(pieces))
        dense = denses[layer]
        out_w, up_w, down_w = dense[:, :width], dense[:, width:-width], dense[:, -width:]
        middle = stream + dot_rows(attended_t, out_w)
        normed_two, factor_two = normalize(middle, gains[layers + layer])
        normed_two = normed_two.astype(BF16)
        hidden = dot(normed_two, up_w)
        active = (hidden * jax.nn.sigmoid(hidden)).astype(BF16)
        kept.append(
            (
                stream, factor_one, normed_all, projected, log_total, attended_t, middle,
                factor_two, normed_two, hidden, active,
            )
        )
        stream = middle + dot(active, down_w)
    layer_out = swap_halves(stream.astype(BF16).reshape(tokens.shape))
    upper = upper.reshape(-1, width).astype(F32)

    scale_grads = [None] * layers
    for layer in reversed(range(layers)):
        (
            stream, factor_one, normed_all, projected, log_total, attended_t, middle,
            factor_two, normed_two, hidden, active,
        ) = kept[layer]
        qkv, dense = qkvs[layer], denses[layer]
        out_w, up_w, down_w = dense[:, :width], dense[:, width:-width], dense[:, -width:]
        down_bar = upper.astype(BF16)
        gate = jax.nn.sigmoid(hidden)
        up_bar = (
            dot_cols(down_bar, down_w) * gate * (1.0 + hidden * (1.0 - gate))
        ).astype(BF16)
        middle_grad = upper + lower_of(
            dot_cols(up_bar, up_w), middle, factor_two, gains[layers + layer]
        )
        out_bar = middle_grad.astype(BF16)
        if layer == 0:
            attended_grad = over_head(heads_grad(out_w, out_bar))
            grads, others = dense_grads(attended_t, normed_two, active, out_bar, up_bar, down_bar)
            attended_grad, others, z_sum, across, beside = tied(
                attended_grad, others, z_sum, across, beside
            )
            others = other_core(others)
            attended_grad, summed = tied(attended_grad, own_sum(cored, across, beside))
            summed = over_batch(summed)
            z_across = across_sum(z_sum)
        else:
            attended_grad = over_head(heads_grad(out_w, out_bar))
            grads, others = dense_grads(attended_t, normed_two, active, out_bar, up_bar, down_bar)
            attended_grad, others, layer_out = tied(attended_grad, others, layer_out)
            others = other_core(others)
        bars, scale_grads[layer] = attend_back_rows(
            projected, attended_grad, log_total, scale_vecs[layer], segments, token_rows
        )
        if layer == 0:
            bars, others = tied(bars, others)
            qkv_grad = weight_back(bars, normed_all)
            bars, qkv_grad = tied(bars, qkv_grad)
            z_sum = over_batch(qkv_grad.reshape(4, 2, -1, qkv_grad.shape[-1]))
            cored = (grads.astype(F32) + others.astype(F32)).astype(BF16)
            bars, rows = tied(bars, diagonal_rows(cored))
            diagonal = sent_beside_and_across(*rows)
            halves, to_core = rows_back(bars, qkv, token_rows)
            halves, to_core, diagonal, summed = tied(halves, to_core, diagonal, summed)
            halves, to_core, rows = tied(halves, to_core, neighbour_rows(cored, *diagonal))
            sent = sent_beside_and_across(*rows)
            halves = halves + other_core(to_core).astype(F32)
            halves, sent, z_sum = tied(halves, sent, z_sum)
            halves, own = tied(halves, own_sum(cored, *sent))
            dense_first = over_batch(own)
            normed_grad = scatter_row(halves)
            normed_grad, z_across, scale_grads[0] = tied(normed_grad, z_across, scale_grads[0])
            dense_grad = [dense_first, summed]
            qkv_grads = [columns_to_rows(across_sum(z_sum)), columns_to_rows(z_across)]
        else:
            bars, others = tied(bars, others)
            cored = (grads.astype(F32) + others.astype(F32)).astype(BF16)
            bars, rows = tied(bars, diagonal_rows(cored))
            diagonal = sent_beside_and_across(*rows)
            halves, to_core, qkv_grad = project_back(bars, qkv, normed_all, token_rows)
            z_sum = over_batch(qkv_grad.reshape(4, 2, -1, qkv_grad.shape[-1]))
            to_core, halves, diagonal = tied(to_core, halves, diagonal)
            to_core, rows = tied(to_core, neighbour_rows(cored, *diagonal))
            across = swapped(rows[0], "blk", 1)
            halves = halves + other_core(to_core).astype(F32)
            normed_grad = scatter_row(halves)
            normed_grad, beside = tied(normed_grad, rows[1])
            beside = swapped(beside, "head", 2)
        upper = middle_grad + lower_of(normed_grad, stream, factor_one, gains[layer])
    input_grad = swap_halves(upper.astype(BF16).reshape(tokens.shape)).astype(F32)
    scale_total = sum_all(jnp.stack(scale_grads))
    scale_grad = scale_total * (SCALE_BASE / math.sqrt(head_dim)) * jax.nn.sigmoid(scale_param)
    dense_all = jnp.stack([part.astype(F32) for part in dense_grad])
    qkv_all = jnp.stack(qkv_grads)
    up_all = dense_all[:, :, width:-width]
    return (
        layer_out,
        input_grad,
        qkv_all,
        dense_all[:, :, :width],
        up_all,
        dense_all[:, :, -width:],
        gain_back(qkv_weight, qkv_all, attn_gain),
        gain_back(up_weight, up_all, mlp_gain),
        scale_grad,
    )


def per_device(*args):
    tokens, segments = args[0], args[1]
    sizes = tuple(lax.axis_size(axis) for axis in ALL)
    heads = tokens.shape[2] // args[8].shape[1]
    spread = (
        sizes == (4, 2, 4)
        and tokens.shape[0] == 2
        and args[2].shape[0] == 2
        and tokens.shape[1] % 128 == 0
        and Q_ROWS % tokens.shape[1] == 0
        and segments.shape[1] <= WINDOW
        and segments.shape[1] % Q_ROWS == 0
        and heads % 4 == 0
        and tokens.shape[2] % 256 == 0
    )
    return spread_device(*args) if spread else general_device(*args)


def solution(mesh):
    rows = P(None, ALL, None)
    by_token = P("batch", ("blk", "head"), None)
    return jax.shard_map(
        per_device,
        mesh=mesh,
        in_specs=(
            by_token, P("batch", None), rows, rows, rows, rows, P(None, ALL), P(None, ALL), P(),
            by_token,
        ),
        out_specs=(
            by_token, by_token, rows, rows, rows, rows, P(None, ALL), P(None, ALL), P(),
        ),
        check_vma=False,
    )
```

```python
import functools
import math

import jax
import jax.numpy as jnp
from jax import lax
from jax.experimental import pallas as pl
from jax.experimental.pallas import tpu as pltpu
from jax.sharding import PartitionSpec as P

WINDOW = 1024
EPSILON = 1e-06
SCALE_BASE = 1.4426950408889634
MASKED_SCORE = -1e30

ALL = ("batch", "blk", "head")
REST = ("batch", "blk")
F32 = jnp.float32
BF16 = jnp.bfloat16


def shifted(block, axis, distance):
    devices = range(lax.axis_size(axis))
    route = [(i - distance, i) for i in devices if i - distance in devices]
    return lax.ppermute(block, axis, route)


NT = (((1,), (1,)), ((), ()))
TN = (((0,), (0,)), ((), ()))


def dot(left, right):
    return jnp.dot(left, right, preferred_element_type=F32)


def dot_rows(left, right):
    return lax.dot_general(left, right, (((0,), (0,)), ((), ())), preferred_element_type=F32)


def dot_cols(left, right):
    return lax.dot_general(left, right, (((1,), (1,)), ((), ())), preferred_element_type=F32)


def normalize(stream, gain):
    factor = lax.rsqrt(jnp.mean(stream * stream, axis=-1, keepdims=True) + EPSILON)
    return stream * factor * gain, factor


def norm_back(upper, stream, factor, gain):
    inner = upper * gain
    gain_grad = jnp.sum(upper * stream * factor, axis=0)
    lower = factor * inner - stream * factor * factor * factor * jnp.mean(
        inner * stream, axis=-1, keepdims=True
    )
    return lower, gain_grad


class Plan:
    def __init__(self, tokens):
        self.seqs, self.rows, self.width = tokens.shape
        self.heads = lax.axis_size("head")
        self.blks = lax.axis_size("blk")
        self.block = self.rows * self.heads
        self.whole = self.seqs % self.blks == 0
        if self.whole:
            self.groups, self.own_seqs = self.blks, self.seqs // self.blks
            self.reach = 0
        else:
            self.groups, self.own_seqs = 1, self.seqs
            self.reach = min((WINDOW - 1) // self.block + 1, self.blks - 1)
        self.length = self.groups * self.block
        self.tokens = self.seqs * self.rows


def to_plan(plan, array):
    if plan.whole and plan.blks > 1:
        array = lax.all_to_all(array, "blk", split_axis=0, concat_axis=0, tiled=True)
    return array.reshape(plan.tokens, plan.width)


def from_plan(plan, flat):
    array = flat.reshape(plan.seqs, plan.rows, plan.width)
    if plan.whole and plan.blks > 1:
        array = lax.all_to_all(array, "blk", split_axis=0, concat_axis=0, tiled=True)
    return array


def in_sequence(plan, by_head, width):
    parts = by_head.reshape(plan.heads, plan.groups, plan.own_seqs, plan.rows, width)
    return parts.transpose(2, 1, 0, 3, 4).reshape(-1, width)


def by_owner(plan, rows, width):
    parts = rows.reshape(plan.own_seqs, plan.groups, plan.heads, plan.rows, width)
    return parts.transpose(2, 1, 0, 3, 4).reshape(plan.heads, plan.tokens, width)


def gather_tokens(plan, rows):
    moved = lax.all_gather(rows, "head", axis=0, tiled=False)
    return in_sequence(plan, moved, rows.shape[-1])


def scatter_tokens(plan, rows):
    width = rows.shape[-1]
    return lax.psum_scatter(
        by_owner(plan, rows.astype(BF16), width), "head", scatter_dimension=0, tiled=False
    ).astype(F32)


def heads_to_tokens(plan, rows):
    part = rows.shape[-1]
    moved = lax.all_to_all(
        by_owner(plan, rows, part), "head", split_axis=0, concat_axis=0, tiled=True
    )
    return moved.transpose(1, 0, 2).reshape(plan.tokens, plan.heads * part)


def tokens_to_heads(plan, rows):
    part = rows.shape[-1] // plan.heads
    sent = rows.reshape(plan.tokens, plan.heads, part).transpose(1, 0, 2)
    moved = lax.all_to_all(sent, "head", split_axis=0, concat_axis=0, tiled=True)
    return in_sequence(plan, moved, part)


def gather_qkv(rows):
    own, width = rows.shape
    heads = lax.axis_size("head")
    part = width // 3 // heads
    sent = rows.reshape(own, 3, heads, part).transpose(2, 0, 1, 3).reshape(heads, own, 3 * part)
    moved = lax.all_to_all(sent, "head", split_axis=0, concat_axis=0, tiled=True)
    full = lax.all_gather(moved, REST, axis=0, tiled=True)
    return full.reshape(-1, 3 * part)


def scatter_qkv(grad):
    heads = lax.axis_size("head")
    part = grad.shape[1] // 3
    summed = lax.psum_scatter(grad.astype(BF16), REST, scatter_dimension=0, tiled=True)
    own = summed.shape[0] // heads
    moved = lax.all_to_all(
        summed.reshape(heads, own, 3 * part), "head", split_axis=0, concat_axis=0, tiled=True
    )
    return (
        moved.reshape(heads, own, 3, part)
        .transpose(1, 2, 0, 3)
        .reshape(own, 3 * heads * part)
        .astype(F32)
    )


def window_mask(plan, segments, block_index):
    key_count = plan.length + plan.reach * plan.block
    if plan.whole:
        query_segs, key_segs = segments, segments
    else:
        leading = jnp.full((plan.own_seqs, plan.reach * plan.block), -1, jnp.int32)
        padded = jnp.concatenate([leading, segments], axis=1)
        start = block_index * plan.block
        query_segs = lax.dynamic_slice_in_dim(segments, start, plan.block, 1)
        key_segs = lax.dynamic_slice_in_dim(padded, start, key_count, 1)
    query_place = jnp.arange(plan.length, dtype=jnp.int32)[:, None] + plan.reach * plan.block
    key_place = jnp.arange(key_count, dtype=jnp.int32)[None, :]
    near = (key_place <= query_place) & (query_place - key_place < WINDOW)
    return (key_segs[:, None, :] == query_segs[:, :, None]) & near[None]


def with_earlier(plan, own):
    arrived = [own]
    for _ in range(plan.reach):
        arrived.append(shifted(arrived[-1], "blk", 1))
    return jnp.concatenate(arrived[::-1], axis=1) if plan.reach else own


def to_earlier(plan, grads):
    if not plan.reach:
        return grads
    block = plan.block
    total = grads[:, :block]
    for step in range(1, plan.reach + 1):
        total = (
            shifted(total.astype(BF16), "blk", -1).astype(F32)
            + grads[:, step * block : (step + 1) * block]
        )
    return total


def scores_of(queries, keys, allowed):
    scores = jnp.einsum("sqhd,skhd->shqk", queries, keys, preferred_element_type=F32)
    return jnp.where(allowed[:, None], scores, MASKED_SCORE)


def attend(queries, keys, values, allowed):
    scores = scores_of(queries, keys, allowed)
    top_score = jnp.max(scores, axis=-1, keepdims=True)
    exp_terms = jnp.exp(scores - top_score)
    totals = jnp.sum(exp_terms, axis=-1, keepdims=True)
    probs_low = (exp_terms / totals).astype(BF16)
    attended = jnp.einsum("shqk,skhd->sqhd", probs_low, values, preferred_element_type=F32)
    return attended, top_score + jnp.log(totals)


def attend_back(queries, keys, values, allowed, log_total, attended_grad):
    probs = jnp.exp(scores_of(queries, keys, allowed) - log_total)
    probs_low = probs.astype(BF16)
    values_grad = jnp.einsum(
        "shqk,sqhd->skhd", probs_low, attended_grad, preferred_element_type=F32
    )
    probs_grad = jnp.einsum("sqhd,skhd->shqk", attended_grad, values, preferred_element_type=F32)
    row_dot = jnp.sum(probs_grad * probs, axis=-1, keepdims=True)
    scores_low = (probs * (probs_grad - row_dot)).astype(BF16)
    queries_grad = jnp.einsum("shqk,skhd->sqhd", scores_low, keys, preferred_element_type=F32)
    keys_grad = jnp.einsum("shqk,sqhd->skhd", scores_low, queries, preferred_element_type=F32)
    return queries_grad, keys_grad, values_grad


def forward(plan, stream, qkv, dense, gains, scale_vec, allowed):
    width = plan.width
    head_dim = scale_vec.shape[0]
    part = qkv.shape[1] // 3
    local_heads = part // head_dim
    split = (plan.own_seqs, plan.length, local_heads, head_dim)
    out_w, up_w, down_w = dense[:, :width], dense[:, width:-width], dense[:, -width:]
    normed, factor_one = normalize(stream, gains[0])
    normed_all = gather_tokens(plan, normed.astype(BF16))
    projected = dot(normed_all, qkv)
    query_pre = projected[:, :part].reshape(split)
    queries = (query_pre * scale_vec).astype(BF16)
    keys = with_earlier(plan, projected[:, part : 2 * part].astype(BF16).reshape(split))
    values = with_earlier(plan, projected[:, 2 * part :].astype(BF16).reshape(split))
    attended_part, log_total = attend(queries, keys, values, allowed)
    attended = heads_to_tokens(plan, attended_part.astype(BF16).reshape(-1, part))
    middle = stream + dot(attended, out_w)
    normed_two, factor_two = normalize(middle, gains[1])
    normed_two = normed_two.astype(BF16)
    hidden = dot(normed_two, up_w)
    active = (hidden * jax.nn.sigmoid(hidden)).astype(BF16)
    result = middle + dot(active, down_w)
    kept = (
        stream, factor_one, normed_all, query_pre, queries, keys, values, log_total,
        attended, middle, factor_two, normed_two, hidden, active,
    )
    return result, kept


def backward(plan, upper, kept, qkv, dense, gains, scale_vec, allowed):
    (
        stream, factor_one, normed_all, query_pre, queries, keys, values, log_total,
        attended, middle, factor_two, normed_two, hidden, active,
    ) = kept
    width = plan.width
    head_dim = scale_vec.shape[0]
    part = qkv.shape[1] // 3
    out_w, up_w, down_w = dense[:, :width], dense[:, width:-width], dense[:, -width:]
    upper_low = upper.astype(BF16)
    down_grad = dot_rows(active, upper_low)
    active_grad = dot_cols(upper_low, down_w)
    gate = jax.nn.sigmoid(hidden)
    hidden_low = (active_grad * gate * (1.0 + hidden * (1.0 - gate))).astype(BF16)
    up_grad = dot_rows(normed_two, hidden_low)
    extra_two, mlp_gain_grad = norm_back(dot_cols(hidden_low, up_w), middle, factor_two, gains[1])
    middle_grad = upper + extra_two
    middle_low = middle_grad.astype(BF16)
    out_grad = dot_rows(attended, middle_low)
    dense_grad = jnp.concatenate([out_grad, up_grad, down_grad], axis=1).astype(BF16)
    dense_own = lax.psum_scatter(dense_grad, ALL, scatter_dimension=0, tiled=True)
    attended_grad = tokens_to_heads(plan, dot_cols(middle_low, out_w).astype(BF16))
    queries_grad, keys_grad, values_grad = attend_back(
        queries, keys, values, allowed, log_total, attended_grad.reshape(queries.shape)
    )
    query_bar = queries_grad.astype(BF16).astype(F32)
    scale_vec_grad = jnp.sum((query_bar * query_pre).reshape(-1, head_dim), axis=0)
    query_low = (query_bar * scale_vec).astype(BF16).reshape(-1, part)
    keys_low = to_earlier(plan, keys_grad).astype(BF16).reshape(-1, part)
    values_low = to_earlier(plan, values_grad).astype(BF16).reshape(-1, part)
    projected_low = jnp.concatenate([query_low, keys_low, values_low], axis=1)
    normed_grad = scatter_tokens(plan, dot_cols(projected_low, qkv))
    qkv_own = scatter_qkv(dot_rows(normed_all, projected_low))
    extra_one, attn_gain_grad = norm_back(normed_grad, stream, factor_one, gains[0])
    lower = middle_grad + extra_one
    return lower, qkv_own, dense_own, (attn_gain_grad, mlp_gain_grad), scale_vec_grad


def general_device(
    tokens,
    segments,
    qkv_weight,
    out_weight,
    up_weight,
    down_weight,
    attn_gain,
    mlp_gain,
    scale_param,
    cotangent,
):
    plan = Plan(tokens)
    layers, head_dim = scale_param.shape
    block_index = lax.axis_index("blk")
    scale_vecs = SCALE_BASE / math.sqrt(head_dim) * jax.nn.softplus(scale_param)
    own_gains = jnp.concatenate([attn_gain, mlp_gain], axis=0)
    gains = (
        lax.all_gather(own_gains.reshape(1, -1), ALL, axis=0, tiled=True)
        .reshape(-1, 2 * layers, attn_gain.shape[1])
        .transpose(1, 0, 2)
        .reshape(2 * layers, plan.width)
        .astype(F32)
    )
    if plan.whole:
        segments = lax.dynamic_slice_in_dim(
            segments, block_index * plan.own_seqs, plan.own_seqs, 0
        )
    allowed = window_mask(plan, segments, block_index)
    stream = to_plan(plan, tokens).astype(F32)
    qkvs, denses, kept = [], [], []
    for layer in range(layers):
        qkvs.append(gather_qkv(qkv_weight[layer]))
        own = jnp.concatenate([out_weight[layer], up_weight[layer], down_weight[layer]], axis=1)
        denses.append(lax.all_gather(own, ALL, axis=0, tiled=True))
        layer_gains = (gains[layer], gains[layers + layer])
        stream, saved = forward(
            plan, stream, qkvs[layer], denses[layer], layer_gains, scale_vecs[layer], allowed
        )
        kept.append(saved)
    layer_out = from_plan(plan, stream.astype(BF16))
    upper = to_plan(plan, cotangent).astype(F32)
    qkv_grads, dense_grads = [None] * layers, [None] * layers
    gain_grads, scale_grads = [None] * layers, [None] * layers
    for layer in reversed(range(layers)):
        layer_gains = (gains[layer], gains[layers + layer])
        upper, qkv_grads[layer], dense_grads[layer], gain_grads[layer], scale_grads[layer] = (
            backward(
                plan, upper, kept[layer], qkvs[layer], denses[layer], layer_gains,
                scale_vecs[layer], allowed,
            )
        )
    input_grad = from_plan(plan, upper.astype(BF16)).astype(F32)
    small = jnp.concatenate(
        [g[0] for g in gain_grads] + [g[1] for g in gain_grads] + scale_grads, axis=0
    )
    total = lax.psum(small, ALL)
    gain_total = total[: 2 * layers * plan.width].reshape(2 * layers, plan.width)
    owner = lax.axis_index(ALL)
    gain_rows = attn_gain.shape[1]
    own_total = lax.dynamic_slice_in_dim(gain_total, owner * gain_rows, gain_rows, 1)
    scale_total = total[2 * layers * plan.width :].reshape(layers, head_dim)
    scale_grad = scale_total * (SCALE_BASE / math.sqrt(head_dim)) * jax.nn.sigmoid(scale_param)
    dense_all = jnp.stack(dense_grads).astype(F32)
    width = plan.width
    return (
        layer_out,
        input_grad,
        jnp.stack(qkv_grads),
        dense_all[:, :, :width],
        dense_all[:, :, width:-width],
        dense_all[:, :, -width:],
        own_total[:layers],
        own_total[layers:],
        scale_grad,
    )


Q_ROWS = 256
KERNEL = pltpu.CompilerParams(vmem_limit_bytes=32 * 1024 * 1024)
LIGHT = pl.CostEstimate(flops=1 << 20, bytes_accessed=1 << 20, transcendentals=0)


def in_hbm(*arrays):
    return [pltpu.with_memory_space_constraint(array, pltpu.HBM) for array in arrays]


def allowed_keys(col, row, first):
    count = first + row.shape[1]
    key_place = lax.broadcasted_iota(jnp.int32, (count, row.shape[1]), 0)
    query_place = lax.broadcasted_iota(jnp.int32, (count, row.shape[1]), 1) + first
    return (col[:count] == row) & (key_place <= query_place)


def token_places(length, heads, token_rows):
    for first in range(0, length, Q_ROWS):
        parts = []
        for start in range(0, Q_ROWS, token_rows):
            place = (first + start) // token_rows
            parts.append((start, place % heads, place // heads * token_rows))
        yield first, parts


def attend_kernel(token_rows, proj_ref, scale_ref, col_ref, row_ref, out_ref, lse_ref):
    length = proj_ref.shape[-1]
    queries = (proj_ref[0, 0] * scale_ref[...]).astype(BF16)
    keys = proj_ref[1, 0].T.astype(BF16)
    values = proj_ref[2, 0].astype(BF16)
    for first, parts in token_places(length, out_ref.shape[0], token_rows):
        end = first + Q_ROWS
        scores = jnp.dot(keys[:end], queries[:, first:end], preferred_element_type=F32)
        allowed = allowed_keys(col_ref[...], row_ref[:, first:end], first)
        scores = jnp.where(allowed, scores, MASKED_SCORE)
        top = jnp.max(scores, axis=0, keepdims=True)
        terms = jnp.exp(scores - top)
        total = jnp.sum(terms, axis=0, keepdims=True)
        probs = (terms * (1.0 / total)).astype(BF16)
        attended = jnp.dot(values[:, :end], probs, preferred_element_type=F32).astype(BF16)
        lse_ref[0, :, first:end] = top + jnp.log(total)
        for start, owner, offset in parts:
            out_ref[owner, 0, :, offset : offset + token_rows] = attended[
                :, start : start + token_rows
            ]


def attend_rows(projected, scale_vec, segments, owners, token_rows):
    head_dim = scale_vec.shape[0]
    length = projected.shape[1]
    local_heads = projected.shape[0] // 3 // head_dim
    tokens = length // owners
    attended, log_total = pl.pallas_call(
        functools.partial(attend_kernel, token_rows),
        grid=(local_heads,),
        in_specs=[
            pl.BlockSpec((3, 1, head_dim, length), lambda h: (0, h, 0, 0)),
            pl.BlockSpec((head_dim, 1), lambda h: (0, 0)),
            pl.BlockSpec((length, 1), lambda h: (0, 0)),
            pl.BlockSpec((1, length), lambda h: (0, 0)),
        ],
        out_specs=[
            pl.BlockSpec((owners, 1, head_dim, tokens), lambda h: (0, h, 0, 0)),
            pl.BlockSpec((1, 1, length), lambda h: (h, 0, 0)),
        ],
        out_shape=[
            jax.ShapeDtypeStruct((owners, local_heads, head_dim, tokens), BF16),
            jax.ShapeDtypeStruct((local_heads, 1, length), F32),
        ],
        compiler_params=KERNEL,
        cost_estimate=LIGHT,
    )(
        projected.reshape(3, local_heads, head_dim, length),
        scale_vec.reshape(head_dim, 1),
        segments.reshape(length, 1),
        segments.reshape(1, length),
    )
    return attended.reshape(owners, local_heads * head_dim, tokens), log_total


def attend_back_kernel(
    token_rows,
    proj_ref,
    grad_ref,
    lse_ref,
    scale_ref,
    col_ref,
    row_ref,
    out_ref,
    scale_grad_ref,
    keys_acc,
    values_acc,
):
    length = proj_ref.shape[-1]
    scale = scale_ref[...]
    query_pre = proj_ref[0, 0]
    queries = (query_pre * scale).astype(BF16)
    keys_t = proj_ref[1, 0].astype(BF16)
    keys = proj_ref[1, 0].T.astype(BF16)
    values = proj_ref[2, 0].T.astype(BF16)
    keys_acc[...] = jnp.zeros_like(keys_acc)
    values_acc[...] = jnp.zeros_like(values_acc)
    scale_grad = jnp.zeros((scale.shape[0], 1), F32)
    for first, parts in token_places(length, grad_ref.shape[0], token_rows):
        end = first + Q_ROWS
        block = queries[:, first:end]
        grad = jnp.concatenate(
            [grad_ref[owner, 0, :, at : at + token_rows] for _, owner, at in parts], axis=1
        )
        scores = jnp.dot(keys[:end], block, preferred_element_type=F32)
        allowed = allowed_keys(col_ref[...], row_ref[:, first:end], first)
        scores = jnp.where(allowed, scores, MASKED_SCORE)
        probs = jnp.exp(scores - lse_ref[0, :, first:end])
        probs_grad = jnp.dot(values[:end], grad, preferred_element_type=F32)
        row_dot = jnp.sum(probs_grad * probs, axis=0, keepdims=True)
        scores_low = (probs * (probs_grad - row_dot)).astype(BF16)
        values_acc[:, :end] += lax.dot_general(
            grad, probs.astype(BF16), NT, preferred_element_type=F32
        )
        keys_acc[:, :end] += lax.dot_general(
            block, scores_low, NT, preferred_element_type=F32
        )
        query_bar = jnp.dot(keys_t[:, :end], scores_low, preferred_element_type=F32)
        query_bar = query_bar.astype(BF16).astype(F32)
        scale_grad += jnp.sum(query_bar * query_pre[:, first:end], axis=1, keepdims=True)
        out_ref[0, 0, :, first:end] = (query_bar * scale).astype(BF16)
    out_ref[1, 0] = keys_acc[...].astype(BF16)
    out_ref[2, 0] = values_acc[...].astype(BF16)
    spread = jnp.broadcast_to(scale_grad, scale_grad_ref.shape)

    @pl.when(pl.program_id(0) == 0)
    def _():
        scale_grad_ref[...] = spread

    @pl.when(pl.program_id(0) > 0)
    def _():
        scale_grad_ref[...] += spread


def attend_back_rows(projected, attended_grad, log_total, scale_vec, segments, token_rows):
    head_dim = scale_vec.shape[0]
    length = projected.shape[1]
    local_heads = projected.shape[0] // 3 // head_dim
    owners, _, tokens = attended_grad.shape
    lanes = 128
    grads, scale_grad = pl.pallas_call(
        functools.partial(attend_back_kernel, token_rows),
        grid=(local_heads,),
        in_specs=[
            pl.BlockSpec((3, 1, head_dim, length), lambda h: (0, h, 0, 0)),
            pl.BlockSpec((owners, 1, head_dim, tokens), lambda h: (0, h, 0, 0)),
            pl.BlockSpec((1, 1, length), lambda h: (h, 0, 0)),
            pl.BlockSpec((head_dim, 1), lambda h: (0, 0)),
            pl.BlockSpec((length, 1), lambda h: (0, 0)),
            pl.BlockSpec((1, length), lambda h: (0, 0)),
        ],
        out_specs=[
            pl.BlockSpec((3, 1, head_dim, length), lambda h: (0, h, 0, 0)),
            pl.BlockSpec((head_dim, lanes), lambda h: (0, 0)),
        ],
        out_shape=[
            pltpu.HBM((3, local_heads, head_dim, length), BF16),
            pltpu.HBM((head_dim, lanes), F32),
        ],
        scratch_shapes=[
            pltpu.VMEM((head_dim, length), F32),
            pltpu.VMEM((head_dim, length), F32),
        ],
        compiler_params=KERNEL,
        cost_estimate=LIGHT,
    )(
        *in_hbm(
            projected.reshape(3, local_heads, head_dim, length),
            attended_grad.reshape(owners, local_heads, head_dim, tokens),
        ),
        log_total,
        scale_vec.reshape(head_dim, 1),
        segments.reshape(length, 1),
        segments.reshape(1, length),
    )
    return grads.reshape(3 * local_heads * head_dim, length), scale_grad[:, 0]


def dense_grad_kernel(
    core_ref, attended_ref, normed_ref, active_ref, out_bar, up_bar, down_bar,
    own_ref, other_ref, normed_t, active_t,
):
    tile = pl.program_id(0)
    rows, width = own_ref.shape[1] * own_ref.shape[3] * 2, out_bar.shape[1]

    @pl.when(tile == 0)
    def _():
        normed_t[...] = normed_ref[...].astype(F32).T.astype(BF16)
        active_t[...] = active_ref[...].astype(F32).T.astype(BF16)

    start = pl.multiple_of(tile * rows, rows)
    first_core = core_ref[2] == 0
    lefts = (attended_ref, normed_t, active_t)
    for i, (left, right) in enumerate(zip(lefts, (out_bar, up_bar, down_bar))):
        grad = jnp.dot(left[pl.ds(start, rows), :], right[...], preferred_element_type=F32)
        grad = grad.reshape(2, 2, rows // 4, width)
        one, two = grad[:, 0], grad[:, 1]
        own_ref[0, :, 0, :, i * width : (i + 1) * width] = jnp.where(
            first_core, one, two
        ).astype(BF16)
        other_ref[0, :, 0, :, i * width : (i + 1) * width] = jnp.where(
            first_core, two, one
        ).astype(BF16)


def dense_grads(attended_t, normed, active, out_bar, up_bar, down_bar):
    width, tokens = attended_t.shape
    own = width // 32
    whole = pl.BlockSpec((tokens, width), lambda i, core: (0, 0))
    rows = pl.BlockSpec((1, 2, 1, own, 3 * width), lambda i, core: (i % 2, 0, i // 2, 0, 0))
    shape = pltpu.HBM((2, 2, 4, own, 3 * width), BF16)
    return pl.pallas_call(
        dense_grad_kernel,
        grid_spec=pltpu.PrefetchScalarGridSpec(
            num_scalar_prefetch=1,
            grid=(8,),
            in_specs=[pl.BlockSpec((width, tokens), lambda i, core: (0, 0))] + [whole] * 5,
            out_specs=[rows, rows],
            scratch_shapes=[pltpu.VMEM((width, tokens), BF16)] * 2,
        ),
        out_shape=[shape, shape],
        compiler_params=KERNEL,
        cost_estimate=LIGHT,
    )(place(), *in_hbm(attended_t, normed, active, out_bar, up_bar, down_bar))


def place():
    head = lax.axis_index("head")
    return jnp.stack([lax.axis_index("blk"), head // 2, head % 2]).astype(jnp.int32)


def assemble_kernel(place_ref, *refs):
    pieces, whole_ref = refs[:10], refs[10]
    half = whole_ref.shape[-1] // 2
    blk, row, core = place_ref[0], place_ref[1], place_ref[2]
    for i in range(2):
        at_core = core if i == 0 else 1 - core
        own, across, beside, one, two = pieces[5 * i : 5 * i + 5]
        whole_ref[0, blk, row, at_core] = own[0]
        whole_ref[0, 1 - blk, row, at_core] = across[0]
        whole_ref[0, blk, 1 - row, at_core] = beside[0]
        whole_ref[0, 1 - blk, 1 - row, at_core, :, :half] = one[0]
        whole_ref[0, 1 - blk, 1 - row, at_core, :, half:] = two[0]


def assemble(pieces):
    batch, own, columns = pieces[0].shape
    specs = [
        pl.BlockSpec((1, own, piece.shape[-1]), lambda i, at: (i, 0, 0))
        for piece in pieces
    ]
    whole = pl.pallas_call(
        assemble_kernel,
        grid_spec=pltpu.PrefetchScalarGridSpec(
            num_scalar_prefetch=1,
            grid=(batch,),
            in_specs=specs,
            out_specs=pl.BlockSpec((1, 2, 2, 2, own, columns), lambda i, at: (i, 0, 0, 0, 0, 0)),
        ),
        out_shape=jax.ShapeDtypeStruct((batch, 2, 2, 2, own, columns), BF16),
        compiler_params=KERNEL,
        cost_estimate=LIGHT,
    )(place(), *pieces)
    return whole.reshape(-1, columns)


def assemble_columns_kernel(place_ref, along_ref, across_ref, whole_ref, *extra_ref):
    blk = place_ref[0]
    columns = whole_ref.shape[-1]
    whole_ref[0, blk] = along_ref[0, :, :columns]
    whole_ref[0, 1 - blk] = across_ref[0, :, :columns]
    for extra in extra_ref:
        extra[0, blk] = along_ref[0, :, columns:]
        extra[0, 1 - blk] = across_ref[0, :, columns:]


def assemble_columns(along, across, columns):
    batch, own, both = along.shape
    rows = pl.BlockSpec((1, own, both), lambda i, at: (i, 0, 0))
    shapes = [(batch, 2, own, columns)]
    if both > columns:
        shapes.append((batch, 2, own, both - columns))
    parts = pl.pallas_call(
        assemble_columns_kernel,
        grid_spec=pltpu.PrefetchScalarGridSpec(
            num_scalar_prefetch=1,
            grid=(batch,),
            in_specs=[rows, rows],
            out_specs=[pl.BlockSpec((1,) + s[1:], lambda i, at: (i, 0, 0, 0)) for s in shapes],
        ),
        out_shape=[pltpu.HBM(s, BF16) for s in shapes],
        compiler_params=KERNEL,
        cost_estimate=LIGHT,
    )(place(), *in_hbm(along, across))
    return [part.reshape(-1, part.shape[-1]) for part in parts]


def assemble_wide_kernel(place_ref, along_ref, across_ref, whole_ref):
    blk = place_ref[0]
    own, columns = along_ref.shape[1], whole_ref.shape[-1]
    for i in range(along_ref.shape[-1] // columns):
        place, part = slice(i * own, (i + 1) * own), slice(i * columns, (i + 1) * columns)
        whole_ref[0, blk, place, :] = along_ref[0, :, part]
        whole_ref[0, 1 - blk, place, :] = across_ref[0, :, part]


def assemble_wide(along, across, columns):
    batch, own, wide = along.shape
    rows = own * (wide // columns)
    piece = pl.BlockSpec((1, own, wide), lambda i, at: (i, 0, 0))
    whole = pl.pallas_call(
        assemble_wide_kernel,
        grid_spec=pltpu.PrefetchScalarGridSpec(
            num_scalar_prefetch=1,
            grid=(batch,),
            in_specs=[piece, piece],
            out_specs=pl.BlockSpec((1, 2, rows, columns), lambda i, at: (i, 0, 0, 0)),
        ),
        out_shape=pltpu.HBM((batch, 2, rows, columns), BF16),
        compiler_params=KERNEL,
        cost_estimate=LIGHT,
    )(place(), *in_hbm(along, across))
    return whole.reshape(-1, columns)


def project_kernel(with_norm, place_ref, *refs):
    pieces, (gain_ref, weight_ref, normed_ref, projected_ref) = refs[:4], refs[4:]
    head = place_ref[1] * 2 + place_ref[2]
    rows = pieces[0].shape[0]
    for i, piece in enumerate(pieces):
        value = piece[...]
        if with_norm:
            stream = value.astype(F32)
            factor = lax.rsqrt(jnp.mean(stream * stream, axis=-1, keepdims=True) + EPSILON)
            value = (stream * factor * gain_ref[...]).astype(BF16)
        normed_ref[pl.ds(pl.multiple_of((head ^ i) * rows, rows), rows), :] = value
    projected = jnp.dot(normed_ref[...], weight_ref[...], preferred_element_type=F32)
    projected_ref[...] = projected.T


def project(pieces, gain, weight, with_norm, token_rows):
    tokens, width = pieces[0].shape
    length, columns = 4 * tokens, weight.shape[1]
    groups = tokens // token_rows
    piece = pl.BlockSpec((token_rows, width), lambda g, at: (g, 0))
    return pl.pallas_call(
        functools.partial(project_kernel, with_norm),
        grid_spec=pltpu.PrefetchScalarGridSpec(
            num_scalar_prefetch=1,
            grid=(groups,),
            in_specs=[piece] * 4
            + [
                pl.BlockSpec((1, width), lambda g, at: (0, 0)),
                pl.BlockSpec((width, columns), lambda g, at: (0, 0)),
            ],
            out_specs=[
                pl.BlockSpec((4 * token_rows, width), lambda g, at: (g, 0)),
                pl.BlockSpec((columns, 4 * token_rows), lambda g, at: (0, g)),
            ],
        ),
        out_shape=[
            pltpu.HBM((length, width), BF16),
            pltpu.HBM((columns, length), F32),
        ],
        compiler_params=KERNEL,
        cost_estimate=LIGHT,
    )(place(), *in_hbm(*pieces), gain.reshape(1, width), *in_hbm(weight))


def project_back_kernel(
    place_ref, bars_ref, weight_ref, normed_ref, own_ref, other_ref, grad_ref, bars_t
):
    @pl.when(pl.program_id(0) == 0)
    def _():
        bars_t[...] = bars_ref[...].astype(F32).T.astype(BF16)

    upper = lax.dot_general(bars_t[...], weight_ref[...], NT, preferred_element_type=F32)
    upper = upper.reshape(2, 2, 2, -1, upper.shape[-1])
    first_core = place_ref[2] == 0
    one, two = upper[:, :, 0], upper[:, :, 1]
    own_ref[...] = jnp.where(first_core, one, two)
    other_ref[...] = jnp.where(first_core, two, one).astype(BF16)
    grad = lax.dot_general(normed_ref[...], bars_t[...], TN, preferred_element_type=F32)
    grad_ref[...] = grad.astype(BF16)


def project_back(bars, weight, normed, token_rows):
    columns, length = bars.shape
    width = weight.shape[0]
    tile = width // 2
    quarter = pl.BlockSpec((2, 2, token_rows, tile), lambda i, at: (0, 0, 0, i))
    return pl.pallas_call(
        project_back_kernel,
        grid_spec=pltpu.PrefetchScalarGridSpec(
            num_scalar_prefetch=1,
            grid=(2,),
            in_specs=[
                pl.BlockSpec((columns, length), lambda i, at: (0, 0)),
                pl.BlockSpec((tile, columns), lambda i, at: (i, 0)),
                pl.BlockSpec((length, tile), lambda i, at: (0, i)),
            ],
            out_specs=[quarter, quarter, pl.BlockSpec((tile, columns), lambda i, at: (i, 0))],
            scratch_shapes=[pltpu.VMEM((length, columns), BF16)],
        ),
        out_shape=[
            pltpu.HBM((2, 2, token_rows, width), F32),
            pltpu.HBM((2, 2, token_rows, width), BF16),
            pltpu.HBM((width, columns), BF16),
        ],
        compiler_params=KERNEL,
        cost_estimate=LIGHT,
    )(place(), *in_hbm(bars, weight, normed))


def rows_back_kernel(place_ref, bars_ref, weight_ref, own_ref, other_ref, bars_t):
    @pl.when(pl.program_id(0) == 0)
    def _():
        bars_t[...] = bars_ref[...].astype(F32).T.astype(BF16)

    upper = lax.dot_general(bars_t[...], weight_ref[...], NT, preferred_element_type=F32)
    upper = upper.reshape(2, 2, 2, -1, upper.shape[-1])
    first_core = place_ref[2] == 0
    one, two = upper[:, :, 0], upper[:, :, 1]
    own_ref[...] = jnp.where(first_core, one, two)
    other_ref[...] = jnp.where(first_core, two, one).astype(BF16)


def rows_back(bars, weight, token_rows):
    columns, length = bars.shape
    width = weight.shape[0]
    tile = width // 2
    quarter = pl.BlockSpec((2, 2, token_rows, tile), lambda i, at: (0, 0, 0, i))
    return pl.pallas_call(
        rows_back_kernel,
        grid_spec=pltpu.PrefetchScalarGridSpec(
            num_scalar_prefetch=1,
            grid=(2,),
            in_specs=[
                pl.BlockSpec((columns, length), lambda i, at: (0, 0)),
                pl.BlockSpec((tile, columns), lambda i, at: (i, 0)),
            ],
            out_specs=[quarter, quarter],
            scratch_shapes=[pltpu.VMEM((length, columns), BF16)],
        ),
        out_shape=[
            pltpu.HBM((2, 2, token_rows, width), F32),
            pltpu.HBM((2, 2, token_rows, width), BF16),
        ],
        compiler_params=KERNEL,
        cost_estimate=LIGHT,
    )(place(), *in_hbm(bars, weight))


def weight_back_kernel(bars_ref, normed_ref, grad_ref):
    grad = jnp.dot(bars_ref[...], normed_ref[...], preferred_element_type=F32)
    grad_ref[...] = grad.T.astype(BF16)


def weight_back(bars, normed):
    columns, length = bars.shape
    width = normed.shape[1]
    tile = width // 5
    return pl.pallas_call(
        weight_back_kernel,
        grid=(5,),
        in_specs=[
            pl.BlockSpec((columns, length), lambda i: (0, 0)),
            pl.BlockSpec((length, tile), lambda i: (0, i)),
        ],
        out_specs=pl.BlockSpec((tile, columns), lambda i: (i, 0)),
        out_shape=pltpu.HBM((width, columns), BF16),
        compiler_params=KERNEL,
        cost_estimate=LIGHT,
    )(*in_hbm(bars, normed))


def tied(*arrays):
    return lax.optimization_barrier(arrays)


def swapped(array, axis, mask):
    size = lax.axis_size(axis)
    return lax.ppermute(array, axis, [(i, i ^ mask) for i in range(size)])


def pick(array, index, axis=0):
    return lax.dynamic_index_in_dim(array, index, axis, keepdims=False)


def swap_halves(array):
    me = lax.axis_index("blk")
    got = swapped(pick(array, 1 - me), "blk", 1)
    kept = pick(array, me)
    return jnp.stack([jnp.where(me == 0, kept, got), jnp.where(me == 0, got, kept)])


def scatter_row(halves):
    row = lax.axis_index("head") // 2
    got = swapped(pick(halves, 1 - row, 1).astype(BF16), "head", 2).astype(F32)
    return (pick(halves, row, 1) + got).reshape(-1, halves.shape[-1])


def over_head(parts):
    return lax.all_to_all(parts, "head", split_axis=0, concat_axis=0, tiled=True)


def qkv_columns(rows, extra):
    own, width = rows.shape
    part = width // 3 // 4
    sent = rows.reshape(own, 3, 4, part).transpose(2, 0, 1, 3).reshape(4, own, 3 * part)
    if extra is not None:
        sent = jnp.concatenate([sent, jnp.broadcast_to(extra[None], (4,) + extra.shape)], axis=2)
    return over_head(sent)


def along_batch(piece):
    return lax.all_gather(piece, "batch", axis=0, tiled=False)


def other_core(array):
    return swapped(array, "head", 1)


def to_beside(across):
    return swapped(across[..., : across.shape[-1] // 2], "head", 2)


def to_across(beside):
    return swapped(beside[..., beside.shape[-1] // 2 :], "blk", 1)


def over_batch(parts):
    return lax.psum_scatter(parts.astype(BF16), "batch", scatter_dimension=0, tiled=False)


def across_sum(halves):
    blk = lax.axis_index("blk")
    got = swapped(pick(halves, 1 - blk), "blk", 1).astype(F32)
    return (pick(halves, blk).astype(F32) + got).astype(BF16)


def columns_to_rows(summed):
    moved = over_head(summed.reshape(4, -1, summed.shape[-1]))
    rows = moved.shape[1]
    return moved.reshape(4, rows, 3, -1).transpose(1, 2, 0, 3).reshape(rows, -1).astype(F32)


def diagonal_rows(cored):
    blk, row = place()[:2]
    rows = pick(pick(cored, 1 - blk), 1 - row)
    half = rows.shape[-1] // 2
    return rows[..., :half], rows[..., half:]


def neighbour_rows(cored, one, two):
    blk, row = place()[:2]
    half = one.shape[-1]
    across = pick(pick(cored, 1 - blk), row)
    beside = pick(pick(cored, blk), 1 - row)
    across = jnp.concatenate(
        [across[..., :half], across[..., half:].astype(F32) + two.astype(F32)], axis=-1
    ).astype(BF16)
    beside = jnp.concatenate(
        [beside[..., :half].astype(F32) + one.astype(F32), beside[..., half:]], axis=-1
    ).astype(BF16)
    return across, beside


def sent_beside_and_across(across, beside):
    return swapped(across, "blk", 1), swapped(beside, "head", 2)


def heads_grad(weight, out_bar):
    return dot_cols(weight, out_bar).astype(BF16).reshape(4, -1, out_bar.shape[0])


def own_sum(cored, across, beside):
    blk, row = place()[:2]
    own = pick(pick(cored, blk), row)
    return own.astype(F32) + across.astype(F32) + beside.astype(F32)


def sum_all(array):
    for axis, mask in (("head", 1), ("head", 2), ("blk", 1), ("batch", 1), ("batch", 2)):
        array = array + swapped(array, axis, mask)
    return array


def gain_back(weight, weight_grad, gain):
    return jnp.sum(weight.astype(F32) * weight_grad, axis=-1) / gain.astype(F32)


def lower_of(upper, stream, factor, gain):
    return norm_back(upper, stream, factor, gain)[0]


def spread_device(
    tokens,
    segments,
    qkv_weight,
    out_weight,
    up_weight,
    down_weight,
    attn_gain,
    mlp_gain,
    scale_param,
    cotangent,
):
    layers, head_dim = scale_param.shape
    _, token_rows, width = tokens.shape
    scale_vecs = SCALE_BASE / math.sqrt(head_dim) * jax.nn.softplus(scale_param)
    segments = pick(segments, lax.axis_index("blk"))
    own_gains = jnp.concatenate([attn_gain, mlp_gain], axis=0)

    part3 = 3 * width // 4
    dense_own = [
        jnp.concatenate([out_weight[i], up_weight[i], down_weight[i]], axis=1) for i in (0, 1)
    ]

    first = swap_halves(tokens).reshape(-1, width)
    columns = qkv_columns(qkv_weight[0], own_gains.T)
    columns, first = tied(columns.reshape(-1, columns.shape[-1]), first)
    stream = first.astype(F32)
    along = along_batch(columns)
    far, near = swapped(first, "head", 2), other_core(first)
    both = other_core(far)
    along, near, far, both, dense_near = tied(along, near, far, both, dense_own[0])
    token_pieces = (first, near, far, both)
    dense_near = along_batch(dense_near)
    qkv_across = swapped(along, "blk", 1)
    next_columns = jnp.concatenate(list(qkv_columns(qkv_weight[1], None)), axis=1)
    qkv_across, dense_near, next_columns = tied(qkv_across, dense_near, next_columns)
    across, beside = swapped(dense_near, "blk", 1), swapped(dense_near, "head", 2)
    next_both = along_batch(jnp.stack([next_columns, dense_own[1]]))
    weight, gains = assemble_columns(along, qkv_across, part3)
    qkvs = [weight]
    gains = gains.T.astype(F32)

    kept, denses = [], []
    for layer in range(layers):
        normed, factor_one = normalize(stream, gains[layer])
        if layer == 1:
            normed = normed.astype(BF16)
            far, near = swapped(normed, "head", 2), other_core(normed)
            far, next_across, dense_next = tied(far, next_across, dense_next)
            across, beside = swapped(dense_next, "blk", 1), swapped(dense_next, "head", 2)
            token_pieces = (normed, near, far, other_core(far))
            qkvs.append(assemble_wide(next_along, next_across, part3))
        normed_all, projected = project(
            token_pieces, gains[layer], qkvs[layer], layer == 0, token_rows
        )
        attended, log_total = attend_rows(
            projected, scale_vecs[layer], segments, 4, token_rows
        )
        attended, across, beside = tied(attended, across, beside)
        one, two = to_beside(across), to_across(beside)
        if layer == 0:
            two, next_both = tied(two, next_both)
            next_along, dense_next = next_both[:, 0], next_both[:, 1]
            next_across = swapped(next_along, "blk", 1)
            attended_t, one, two = tied(over_head(attended), one, two)
        else:
            dense_near = dense_next
            attended_t, one, two, cotangent = tied(over_head(attended), one, two, cotangent)
            upper = swap_halves(cotangent)
        pieces = (dense_near, across, beside, one, two)
        pieces += tuple(other_core(piece) for piece in pieces)
        attended_t = attended_t.reshape(width, -1)
        denses.append(assemble(pieces))
        dense = denses[layer]
        out_w, up_w, down_w = dense[:, :width], dense[:, width:-width], dense[:, -width:]
        middle = stream + dot_rows(attended_t, out_w)
        if layer == 1:
            middle, upper = tied(middle, upper)
        normed_two, factor_two = normalize(middle, gains[layers + layer])
        normed_two = normed_two.astype(BF16)
        hidden = dot(normed_two, up_w)
        active = (hidden * jax.nn.sigmoid(hidden)).astype(BF16)
        kept.append(
            (
                stream, factor_one, normed_all, projected, log_total, attended_t, middle,
                factor_two, normed_two, hidden, active,
            )
        )
        stream = middle + dot(active, down_w)
    layer_out = swap_halves(stream.astype(BF16).reshape(tokens.shape))
    upper = upper.reshape(-1, width).astype(F32)

    scale_grads = [None] * layers
    for layer in reversed(range(layers)):
        (
            stream, factor_one, normed_all, projected, log_total, attended_t, middle,
            factor_two, normed_two, hidden, active,
        ) = kept[layer]
        qkv, dense = qkvs[layer], denses[layer]
        out_w, up_w, down_w = dense[:, :width], dense[:, width:-width], dense[:, -width:]
        down_bar = upper.astype(BF16)
        gate = jax.nn.sigmoid(hidden)
        up_bar = (
            dot_cols(down_bar, down_w) * gate * (1.0 + hidden * (1.0 - gate))
        ).astype(BF16)
        middle_grad = upper + lower_of(
            dot_cols(up_bar, up_w), middle, factor_two, gains[layers + layer]
        )
        out_bar = middle_grad.astype(BF16)
        if layer == 0:
            attended_grad = over_head(heads_grad(out_w, out_bar))
            grads, others = dense_grads(attended_t, normed_two, active, out_bar, up_bar, down_bar)
            attended_grad, others, z_sum, across, beside = tied(
                attended_grad, others, z_sum, across, beside
            )
            others = other_core(others)
            attended_grad, summed = tied(attended_grad, own_sum(cored, across, beside))
            summed = over_batch(summed)
            z_across = across_sum(z_sum)
        else:
            attended_grad = over_head(heads_grad(out_w, out_bar))
            grads, others = dense_grads(attended_t, normed_two, active, out_bar, up_bar, down_bar)
            attended_grad, others, layer_out = tied(attended_grad, others, layer_out)
            others = other_core(others)
        bars, scale_grads[layer] = attend_back_rows(
            projected, attended_grad, log_total, scale_vecs[layer], segments, token_rows
        )
        if layer == 0:
            bars, others, z_across = tied(bars, others, z_across)
            qkv_grad = weight_back(bars, normed_all)
            bars, qkv_grad = tied(bars, qkv_grad)
            z_sum = over_batch(qkv_grad.reshape(4, 2, -1, qkv_grad.shape[-1]))
            cored = (grads.astype(F32) + others.astype(F32)).astype(BF16)
            bars, rows = tied(bars, diagonal_rows(cored))
            diagonal = sent_beside_and_across(*rows)
            halves, to_core = rows_back(bars, qkv, token_rows)
            halves, to_core, diagonal, summed = tied(halves, to_core, diagonal, summed)
            qkv_rows = columns_to_rows(z_across)
            halves, to_core, rows = tied(halves, to_core, neighbour_rows(cored, *diagonal))
            sent = sent_beside_and_across(*rows)
            halves = halves + other_core(to_core).astype(F32)
            sent, z_sum, qkv_rows = tied(sent, z_sum, qkv_rows)
            own, z_sum = tied(own_sum(cored, *sent), z_sum)
            dense_first = over_batch(own)
            normed_grad = scatter_row(halves)
            normed_grad, scale_grads[0] = tied(normed_grad, scale_grads[0])
            dense_grad = [dense_first, summed]
            qkv_grads = [columns_to_rows(across_sum(z_sum)), qkv_rows]
        else:
            bars, others = tied(bars, others)
            cored = (grads.astype(F32) + others.astype(F32)).astype(BF16)
            bars, rows = tied(bars, diagonal_rows(cored))
            diagonal = sent_beside_and_across(*rows)
            halves, to_core, qkv_grad = project_back(bars, qkv, normed_all, token_rows)
            z_sum = over_batch(qkv_grad.reshape(4, 2, -1, qkv_grad.shape[-1]))
            to_core, halves, diagonal = tied(to_core, halves, diagonal)
            to_core, rows = tied(to_core, neighbour_rows(cored, *diagonal))
            across = swapped(rows[0], "blk", 1)
            halves = halves + other_core(to_core).astype(F32)
            normed_grad = scatter_row(halves)
            normed_grad, beside = tied(normed_grad, rows[1])
            beside = swapped(beside, "head", 2)
        upper = middle_grad + lower_of(normed_grad, stream, factor_one, gains[layer])
    input_grad = swap_halves(upper.astype(BF16).reshape(tokens.shape)).astype(F32)
    scale_total = sum_all(jnp.stack(scale_grads))
    scale_grad = scale_total * (SCALE_BASE / math.sqrt(head_dim)) * jax.nn.sigmoid(scale_param)
    dense_all = jnp.stack([part.astype(F32) for part in dense_grad])
    qkv_all = jnp.stack(qkv_grads)
    up_all = dense_all[:, :, width:-width]
    return (
        layer_out,
        input_grad,
        qkv_all,
        dense_all[:, :, :width],
        up_all,
        dense_all[:, :, -width:],
        gain_back(qkv_weight, qkv_all, attn_gain),
        gain_back(up_weight, up_all, mlp_gain),
        scale_grad,
    )


def per_device(*args):
    tokens, segments = args[0], args[1]
    sizes = tuple(lax.axis_size(axis) for axis in ALL)
    heads = tokens.shape[2] // args[8].shape[1]
    spread = (
        sizes == (4, 2, 4)
        and tokens.shape[0] == 2
        and args[2].shape[0] == 2
        and tokens.shape[1] % 128 == 0
        and Q_ROWS % tokens.shape[1] == 0
        and segments.shape[1] <= WINDOW
        and segments.shape[1] % Q_ROWS == 0
        and heads % 4 == 0
        and tokens.shape[2] % 256 == 0
    )
    return spread_device(*args) if spread else general_device(*args)


def solution(mesh):
    rows = P(None, ALL, None)
    by_token = P("batch", ("blk", "head"), None)
    return jax.shard_map(
        per_device,
        mesh=mesh,
        in_specs=(
            by_token, P("batch", None), rows, rows, rows, rows, P(None, ALL), P(None, ALL), P(),
            by_token,
        ),
        out_specs=(
            by_token, by_token, rows, rows, rows, rows, P(None, ALL), P(None, ALL), P(),
        ),
        check_vma=False,
    )
```

```python
import functools
import math

import jax
import jax.numpy as jnp
from jax import lax
from jax.experimental import pallas as pl
from jax.experimental.pallas import tpu as pltpu
from jax.sharding import PartitionSpec as P

WINDOW = 1024
EPSILON = 1e-06
SCALE_BASE = 1.4426950408889634
MASKED_SCORE = -1e30

ALL = ("batch", "blk", "head")
REST = ("batch", "blk")
F32 = jnp.float32
BF16 = jnp.bfloat16


def shifted(block, axis, distance):
    devices = range(lax.axis_size(axis))
    route = [(i - distance, i) for i in devices if i - distance in devices]
    return lax.ppermute(block, axis, route)


NT = (((1,), (1,)), ((), ()))
TN = (((0,), (0,)), ((), ()))


def dot(left, right):
    return jnp.dot(left, right, preferred_element_type=F32)


def dot_rows(left, right):
    return lax.dot_general(left, right, (((0,), (0,)), ((), ())), preferred_element_type=F32)


def dot_cols(left, right):
    return lax.dot_general(left, right, (((1,), (1,)), ((), ())), preferred_element_type=F32)


def normalize(stream, gain):
    factor = lax.rsqrt(jnp.mean(stream * stream, axis=-1, keepdims=True) + EPSILON)
    return stream * factor * gain, factor


def norm_back(upper, stream, factor, gain):
    inner = upper * gain
    gain_grad = jnp.sum(upper * stream * factor, axis=0)
    lower = factor * inner - stream * factor * factor * factor * jnp.mean(
        inner * stream, axis=-1, keepdims=True
    )
    return lower, gain_grad


class Plan:
    def __init__(self, tokens):
        self.seqs, self.rows, self.width = tokens.shape
        self.heads = lax.axis_size("head")
        self.blks = lax.axis_size("blk")
        self.block = self.rows * self.heads
        self.whole = self.seqs % self.blks == 0
        if self.whole:
            self.groups, self.own_seqs = self.blks, self.seqs // self.blks
            self.reach = 0
        else:
            self.groups, self.own_seqs = 1, self.seqs
            self.reach = min((WINDOW - 1) // self.block + 1, self.blks - 1)
        self.length = self.groups * self.block
        self.tokens = self.seqs * self.rows


def to_plan(plan, array):
    if plan.whole and plan.blks > 1:
        array = lax.all_to_all(array, "blk", split_axis=0, concat_axis=0, tiled=True)
    return array.reshape(plan.tokens, plan.width)


def from_plan(plan, flat):
    array = flat.reshape(plan.seqs, plan.rows, plan.width)
    if plan.whole and plan.blks > 1:
        array = lax.all_to_all(array, "blk", split_axis=0, concat_axis=0, tiled=True)
    return array


def in_sequence(plan, by_head, width):
    parts = by_head.reshape(plan.heads, plan.groups, plan.own_seqs, plan.rows, width)
    return parts.transpose(2, 1, 0, 3, 4).reshape(-1, width)


def by_owner(plan, rows, width):
    parts = rows.reshape(plan.own_seqs, plan.groups, plan.heads, plan.rows, width)
    return parts.transpose(2, 1, 0, 3, 4).reshape(plan.heads, plan.tokens, width)


def gather_tokens(plan, rows):
    moved = lax.all_gather(rows, "head", axis=0, tiled=False)
    return in_sequence(plan, moved, rows.shape[-1])


def scatter_tokens(plan, rows):
    width = rows.shape[-1]
    return lax.psum_scatter(
        by_owner(plan, rows.astype(BF16), width), "head", scatter_dimension=0, tiled=False
    ).astype(F32)


def heads_to_tokens(plan, rows):
    part = rows.shape[-1]
    moved = lax.all_to_all(
        by_owner(plan, rows, part), "head", split_axis=0, concat_axis=0, tiled=True
    )
    return moved.transpose(1, 0, 2).reshape(plan.tokens, plan.heads * part)


def tokens_to_heads(plan, rows):
    part = rows.shape[-1] // plan.heads
    sent = rows.reshape(plan.tokens, plan.heads, part).transpose(1, 0, 2)
    moved = lax.all_to_all(sent, "head", split_axis=0, concat_axis=0, tiled=True)
    return in_sequence(plan, moved, part)


def gather_qkv(rows):
    own, width = rows.shape
    heads = lax.axis_size("head")
    part = width // 3 // heads
    sent = rows.reshape(own, 3, heads, part).transpose(2, 0, 1, 3).reshape(heads, own, 3 * part)
    moved = lax.all_to_all(sent, "head", split_axis=0, concat_axis=0, tiled=True)
    full = lax.all_gather(moved, REST, axis=0, tiled=True)
    return full.reshape(-1, 3 * part)


def scatter_qkv(grad):
    heads = lax.axis_size("head")
    part = grad.shape[1] // 3
    summed = lax.psum_scatter(grad.astype(BF16), REST, scatter_dimension=0, tiled=True)
    own = summed.shape[0] // heads
    moved = lax.all_to_all(
        summed.reshape(heads, own, 3 * part), "head", split_axis=0, concat_axis=0, tiled=True
    )
    return (
        moved.reshape(heads, own, 3, part)
        .transpose(1, 2, 0, 3)
        .reshape(own, 3 * heads * part)
        .astype(F32)
    )


def window_mask(plan, segments, block_index):
    key_count = plan.length + plan.reach * plan.block
    if plan.whole:
        query_segs, key_segs = segments, segments
    else:
        leading = jnp.full((plan.own_seqs, plan.reach * plan.block), -1, jnp.int32)
        padded = jnp.concatenate([leading, segments], axis=1)
        start = block_index * plan.block
        query_segs = lax.dynamic_slice_in_dim(segments, start, plan.block, 1)
        key_segs = lax.dynamic_slice_in_dim(padded, start, key_count, 1)
    query_place = jnp.arange(plan.length, dtype=jnp.int32)[:, None] + plan.reach * plan.block
    key_place = jnp.arange(key_count, dtype=jnp.int32)[None, :]
    near = (key_place <= query_place) & (query_place - key_place < WINDOW)
    return (key_segs[:, None, :] == query_segs[:, :, None]) & near[None]


def with_earlier(plan, own):
    arrived = [own]
    for _ in range(plan.reach):
        arrived.append(shifted(arrived[-1], "blk", 1))
    return jnp.concatenate(arrived[::-1], axis=1) if plan.reach else own


def to_earlier(plan, grads):
    if not plan.reach:
        return grads
    block = plan.block
    total = grads[:, :block]
    for step in range(1, plan.reach + 1):
        total = (
            shifted(total.astype(BF16), "blk", -1).astype(F32)
            + grads[:, step * block : (step + 1) * block]
        )
    return total


def scores_of(queries, keys, allowed):
    scores = jnp.einsum("sqhd,skhd->shqk", queries, keys, preferred_element_type=F32)
    return jnp.where(allowed[:, None], scores, MASKED_SCORE)


def attend(queries, keys, values, allowed):
    scores = scores_of(queries, keys, allowed)
    top_score = jnp.max(scores, axis=-1, keepdims=True)
    exp_terms = jnp.exp(scores - top_score)
    totals = jnp.sum(exp_terms, axis=-1, keepdims=True)
    probs_low = (exp_terms / totals).astype(BF16)
    attended = jnp.einsum("shqk,skhd->sqhd", probs_low, values, preferred_element_type=F32)
    return attended, top_score + jnp.log(totals)


def attend_back(queries, keys, values, allowed, log_total, attended_grad):
    probs = jnp.exp(scores_of(queries, keys, allowed) - log_total)
    probs_low = probs.astype(BF16)
    values_grad = jnp.einsum(
        "shqk,sqhd->skhd", probs_low, attended_grad, preferred_element_type=F32
    )
    probs_grad = jnp.einsum("sqhd,skhd->shqk", attended_grad, values, preferred_element_type=F32)
    row_dot = jnp.sum(probs_grad * probs, axis=-1, keepdims=True)
    scores_low = (probs * (probs_grad - row_dot)).astype(BF16)
    queries_grad = jnp.einsum("shqk,skhd->sqhd", scores_low, keys, preferred_element_type=F32)
    keys_grad = jnp.einsum("shqk,sqhd->skhd", scores_low, queries, preferred_element_type=F32)
    return queries_grad, keys_grad, values_grad


def forward(plan, stream, qkv, dense, gains, scale_vec, allowed):
    width = plan.width
    head_dim = scale_vec.shape[0]
    part = qkv.shape[1] // 3
    local_heads = part // head_dim
    split = (plan.own_seqs, plan.length, local_heads, head_dim)
    out_w, up_w, down_w = dense[:, :width], dense[:, width:-width], dense[:, -width:]
    normed, factor_one = normalize(stream, gains[0])
    normed_all = gather_tokens(plan, normed.astype(BF16))
    projected = dot(normed_all, qkv)
    query_pre = projected[:, :part].reshape(split)
    queries = (query_pre * scale_vec).astype(BF16)
    keys = with_earlier(plan, projected[:, part : 2 * part].astype(BF16).reshape(split))
    values = with_earlier(plan, projected[:, 2 * part :].astype(BF16).reshape(split))
    attended_part, log_total = attend(queries, keys, values, allowed)
    attended = heads_to_tokens(plan, attended_part.astype(BF16).reshape(-1, part))
    middle = stream + dot(attended, out_w)
    normed_two, factor_two = normalize(middle, gains[1])
    normed_two = normed_two.astype(BF16)
    hidden = dot(normed_two, up_w)
    active = (hidden * jax.nn.sigmoid(hidden)).astype(BF16)
    result = middle + dot(active, down_w)
    kept = (
        stream, factor_one, normed_all, query_pre, queries, keys, values, log_total,
        attended, middle, factor_two, normed_two, hidden, active,
    )
    return result, kept


def backward(plan, upper, kept, qkv, dense, gains, scale_vec, allowed):
    (
        stream, factor_one, normed_all, query_pre, queries, keys, values, log_total,
        attended, middle, factor_two, normed_two, hidden, active,
    ) = kept
    width = plan.width
    head_dim = scale_vec.shape[0]
    part = qkv.shape[1] // 3
    out_w, up_w, down_w = dense[:, :width], dense[:, width:-width], dense[:, -width:]
    upper_low = upper.astype(BF16)
    down_grad = dot_rows(active, upper_low)
    active_grad = dot_cols(upper_low, down_w)
    gate = jax.nn.sigmoid(hidden)
    hidden_low = (active_grad * gate * (1.0 + hidden * (1.0 - gate))).astype(BF16)
    up_grad = dot_rows(normed_two, hidden_low)
    extra_two, mlp_gain_grad = norm_back(dot_cols(hidden_low, up_w), middle, factor_two, gains[1])
    middle_grad = upper + extra_two
    middle_low = middle_grad.astype(BF16)
    out_grad = dot_rows(attended, middle_low)
    dense_grad = jnp.concatenate([out_grad, up_grad, down_grad], axis=1).astype(BF16)
    dense_own = lax.psum_scatter(dense_grad, ALL, scatter_dimension=0, tiled=True)
    attended_grad = tokens_to_heads(plan, dot_cols(middle_low, out_w).astype(BF16))
    queries_grad, keys_grad, values_grad = attend_back(
        queries, keys, values, allowed, log_total, attended_grad.reshape(queries.shape)
    )
    query_bar = queries_grad.astype(BF16).astype(F32)
    scale_vec_grad = jnp.sum((query_bar * query_pre).reshape(-1, head_dim), axis=0)
    query_low = (query_bar * scale_vec).astype(BF16).reshape(-1, part)
    keys_low = to_earlier(plan, keys_grad).astype(BF16).reshape(-1, part)
    values_low = to_earlier(plan, values_grad).astype(BF16).reshape(-1, part)
    projected_low = jnp.concatenate([query_low, keys_low, values_low], axis=1)
    normed_grad = scatter_tokens(plan, dot_cols(projected_low, qkv))
    qkv_own = scatter_qkv(dot_rows(normed_all, projected_low))
    extra_one, attn_gain_grad = norm_back(normed_grad, stream, factor_one, gains[0])
    lower = middle_grad + extra_one
    return lower, qkv_own, dense_own, (attn_gain_grad, mlp_gain_grad), scale_vec_grad


def general_device(
    tokens,
    segments,
    qkv_weight,
    out_weight,
    up_weight,
    down_weight,
    attn_gain,
    mlp_gain,
    scale_param,
    cotangent,
):
    plan = Plan(tokens)
    layers, head_dim = scale_param.shape
    block_index = lax.axis_index("blk")
    scale_vecs = SCALE_BASE / math.sqrt(head_dim) * jax.nn.softplus(scale_param)
    own_gains = jnp.concatenate([attn_gain, mlp_gain], axis=0)
    gains = (
        lax.all_gather(own_gains.reshape(1, -1), ALL, axis=0, tiled=True)
        .reshape(-1, 2 * layers, attn_gain.shape[1])
        .transpose(1, 0, 2)
        .reshape(2 * layers, plan.width)
        .astype(F32)
    )
    if plan.whole:
        segments = lax.dynamic_slice_in_dim(
            segments, block_index * plan.own_seqs, plan.own_seqs, 0
        )
    allowed = window_mask(plan, segments, block_index)
    stream = to_plan(plan, tokens).astype(F32)
    qkvs, denses, kept = [], [], []
    for layer in range(layers):
        qkvs.append(gather_qkv(qkv_weight[layer]))
        own = jnp.concatenate([out_weight[layer], up_weight[layer], down_weight[layer]], axis=1)
        denses.append(lax.all_gather(own, ALL, axis=0, tiled=True))
        layer_gains = (gains[layer], gains[layers + layer])
        stream, saved = forward(
            plan, stream, qkvs[layer], denses[layer], layer_gains, scale_vecs[layer], allowed
        )
        kept.append(saved)
    layer_out = from_plan(plan, stream.astype(BF16))
    upper = to_plan(plan, cotangent).astype(F32)
    qkv_grads, dense_grads = [None] * layers, [None] * layers
    gain_grads, scale_grads = [None] * layers, [None] * layers
    for layer in reversed(range(layers)):
        layer_gains = (gains[layer], gains[layers + layer])
        upper, qkv_grads[layer], dense_grads[layer], gain_grads[layer], scale_grads[layer] = (
            backward(
                plan, upper, kept[layer], qkvs[layer], denses[layer], layer_gains,
                scale_vecs[layer], allowed,
            )
        )
    input_grad = from_plan(plan, upper.astype(BF16)).astype(F32)
    small = jnp.concatenate(
        [g[0] for g in gain_grads] + [g[1] for g in gain_grads] + scale_grads, axis=0
    )
    total = lax.psum(small, ALL)
    gain_total = total[: 2 * layers * plan.width].reshape(2 * layers, plan.width)
    owner = lax.axis_index(ALL)
    gain_rows = attn_gain.shape[1]
    own_total = lax.dynamic_slice_in_dim(gain_total, owner * gain_rows, gain_rows, 1)
    scale_total = total[2 * layers * plan.width :].reshape(layers, head_dim)
    scale_grad = scale_total * (SCALE_BASE / math.sqrt(head_dim)) * jax.nn.sigmoid(scale_param)
    dense_all = jnp.stack(dense_grads).astype(F32)
    width = plan.width
    return (
        layer_out,
        input_grad,
        jnp.stack(qkv_grads),
        dense_all[:, :, :width],
        dense_all[:, :, width:-width],
        dense_all[:, :, -width:],
        own_total[:layers],
        own_total[layers:],
        scale_grad,
    )


Q_ROWS = 256
KERNEL = pltpu.CompilerParams(vmem_limit_bytes=32 * 1024 * 1024)
LIGHT = pl.CostEstimate(flops=1 << 20, bytes_accessed=1 << 20, transcendentals=0)


def in_hbm(*arrays):
    return [pltpu.with_memory_space_constraint(array, pltpu.HBM) for array in arrays]


def allowed_keys(col, row, first):
    count = first + row.shape[1]
    key_place = lax.broadcasted_iota(jnp.int32, (count, row.shape[1]), 0)
    query_place = lax.broadcasted_iota(jnp.int32, (count, row.shape[1]), 1) + first
    return (col[:count] == row) & (key_place <= query_place)


def token_places(length, heads, token_rows):
    for first in range(0, length, Q_ROWS):
        parts = []
        for start in range(0, Q_ROWS, token_rows):
            place = (first + start) // token_rows
            parts.append((start, place % heads, place // heads * token_rows))
        yield first, parts


def attend_kernel(token_rows, proj_ref, scale_ref, col_ref, row_ref, out_ref, lse_ref):
    length = proj_ref.shape[-1]
    queries = (proj_ref[0, 0] * scale_ref[...]).astype(BF16)
    keys = proj_ref[1, 0].T.astype(BF16)
    values = proj_ref[2, 0].astype(BF16)
    for first, parts in token_places(length, out_ref.shape[0], token_rows):
        end = first + Q_ROWS
        scores = jnp.dot(keys[:end], queries[:, first:end], preferred_element_type=F32)
        allowed = allowed_keys(col_ref[...], row_ref[:, first:end], first)
        scores = jnp.where(allowed, scores, MASKED_SCORE)
        top = jnp.max(scores, axis=0, keepdims=True)
        terms = jnp.exp(scores - top)
        total = jnp.sum(terms, axis=0, keepdims=True)
        probs = (terms * (1.0 / total)).astype(BF16)
        attended = jnp.dot(values[:, :end], probs, preferred_element_type=F32).astype(BF16)
        lse_ref[0, :, first:end] = top + jnp.log(total)
        for start, owner, offset in parts:
            out_ref[owner, 0, :, offset : offset + token_rows] = attended[
                :, start : start + token_rows
            ]


def attend_rows(projected, scale_vec, segments, owners, token_rows):
    head_dim = scale_vec.shape[0]
    length = projected.shape[1]
    local_heads = projected.shape[0] // 3 // head_dim
    tokens = length // owners
    attended, log_total = pl.pallas_call(
        functools.partial(attend_kernel, token_rows),
        grid=(local_heads,),
        in_specs=[
            pl.BlockSpec((3, 1, head_dim, length), lambda h: (0, h, 0, 0)),
            pl.BlockSpec((head_dim, 1), lambda h: (0, 0)),
            pl.BlockSpec((length, 1), lambda h: (0, 0)),
            pl.BlockSpec((1, length), lambda h: (0, 0)),
        ],
        out_specs=[
            pl.BlockSpec((owners, 1, head_dim, tokens), lambda h: (0, h, 0, 0)),
            pl.BlockSpec((1, 1, length), lambda h: (h, 0, 0)),
        ],
        out_shape=[
            jax.ShapeDtypeStruct((owners, local_heads, head_dim, tokens), BF16),
            jax.ShapeDtypeStruct((local_heads, 1, length), F32),
        ],
        compiler_params=KERNEL,
        cost_estimate=LIGHT,
    )(
        projected.reshape(3, local_heads, head_dim, length),
        scale_vec.reshape(head_dim, 1),
        segments.reshape(length, 1),
        segments.reshape(1, length),
    )
    return attended.reshape(owners, local_heads * head_dim, tokens), log_total


def attend_back_kernel(
    token_rows,
    proj_ref,
    grad_ref,
    lse_ref,
    scale_ref,
    col_ref,
    row_ref,
    out_ref,
    scale_grad_ref,
    keys_acc,
    values_acc,
):
    length = proj_ref.shape[-1]
    scale = scale_ref[...]
    query_pre = proj_ref[0, 0]
    queries = (query_pre * scale).astype(BF16)
    keys_t = proj_ref[1, 0].astype(BF16)
    keys = proj_ref[1, 0].T.astype(BF16)
    values = proj_ref[2, 0].T.astype(BF16)
    keys_acc[...] = jnp.zeros_like(keys_acc)
    values_acc[...] = jnp.zeros_like(values_acc)
    scale_grad = jnp.zeros((scale.shape[0], 1), F32)
    for first, parts in token_places(length, grad_ref.shape[0], token_rows):
        end = first + Q_ROWS
        block = queries[:, first:end]
        grad = jnp.concatenate(
            [grad_ref[owner, 0, :, at : at + token_rows] for _, owner, at in parts], axis=1
        )
        scores = jnp.dot(keys[:end], block, preferred_element_type=F32)
        allowed = allowed_keys(col_ref[...], row_ref[:, first:end], first)
        scores = jnp.where(allowed, scores, MASKED_SCORE)
        probs = jnp.exp(scores - lse_ref[0, :, first:end])
        probs_grad = jnp.dot(values[:end], grad, preferred_element_type=F32)
        row_dot = jnp.sum(probs_grad * probs, axis=0, keepdims=True)
        scores_low = (probs * (probs_grad - row_dot)).astype(BF16)
        values_acc[:, :end] += lax.dot_general(
            grad, probs.astype(BF16), NT, preferred_element_type=F32
        )
        keys_acc[:, :end] += lax.dot_general(
            block, scores_low, NT, preferred_element_type=F32
        )
        query_bar = jnp.dot(keys_t[:, :end], scores_low, preferred_element_type=F32)
        query_bar = query_bar.astype(BF16).astype(F32)
        scale_grad += jnp.sum(query_bar * query_pre[:, first:end], axis=1, keepdims=True)
        out_ref[0, 0, :, first:end] = (query_bar * scale).astype(BF16)
    out_ref[1, 0] = keys_acc[...].astype(BF16)
    out_ref[2, 0] = values_acc[...].astype(BF16)
    spread = jnp.broadcast_to(scale_grad, scale_grad_ref.shape)

    @pl.when(pl.program_id(0) == 0)
    def _():
        scale_grad_ref[...] = spread

    @pl.when(pl.program_id(0) > 0)
    def _():
        scale_grad_ref[...] += spread


def attend_back_rows(projected, attended_grad, log_total, scale_vec, segments, token_rows):
    head_dim = scale_vec.shape[0]
    length = projected.shape[1]
    local_heads = projected.shape[0] // 3 // head_dim
    owners, _, tokens = attended_grad.shape
    lanes = 128
    grads, scale_grad = pl.pallas_call(
        functools.partial(attend_back_kernel, token_rows),
        grid=(local_heads,),
        in_specs=[
            pl.BlockSpec((3, 1, head_dim, length), lambda h: (0, h, 0, 0)),
            pl.BlockSpec((owners, 1, head_dim, tokens), lambda h: (0, h, 0, 0)),
            pl.BlockSpec((1, 1, length), lambda h: (h, 0, 0)),
            pl.BlockSpec((head_dim, 1), lambda h: (0, 0)),
            pl.BlockSpec((length, 1), lambda h: (0, 0)),
            pl.BlockSpec((1, length), lambda h: (0, 0)),
        ],
        out_specs=[
            pl.BlockSpec((3, 1, head_dim, length), lambda h: (0, h, 0, 0)),
            pl.BlockSpec((head_dim, lanes), lambda h: (0, 0)),
        ],
        out_shape=[
            pltpu.HBM((3, local_heads, head_dim, length), BF16),
            pltpu.HBM((head_dim, lanes), F32),
        ],
        scratch_shapes=[
            pltpu.VMEM((head_dim, length), F32),
            pltpu.VMEM((head_dim, length), F32),
        ],
        compiler_params=KERNEL,
        cost_estimate=LIGHT,
    )(
        *in_hbm(
            projected.reshape(3, local_heads, head_dim, length),
            attended_grad.reshape(owners, local_heads, head_dim, tokens),
        ),
        log_total,
        scale_vec.reshape(head_dim, 1),
        segments.reshape(length, 1),
        segments.reshape(1, length),
    )
    return grads.reshape(3 * local_heads * head_dim, length), scale_grad[:, 0]


def dense_grad_kernel(
    core_ref, attended_ref, normed_ref, active_ref, out_bar, up_bar, down_bar,
    own_ref, other_ref, normed_t, active_t,
):
    tile = pl.program_id(0)
    rows, width = own_ref.shape[1] * own_ref.shape[3] * 2, out_bar.shape[1]

    @pl.when(tile == 0)
    def _():
        normed_t[...] = normed_ref[...].astype(F32).T.astype(BF16)
        active_t[...] = active_ref[...].astype(F32).T.astype(BF16)

    start = pl.multiple_of(tile * rows, rows)
    first_core = core_ref[2] == 0
    lefts = (attended_ref, normed_t, active_t)
    for i, (left, right) in enumerate(zip(lefts, (out_bar, up_bar, down_bar))):
        grad = jnp.dot(left[pl.ds(start, rows), :], right[...], preferred_element_type=F32)
        grad = grad.reshape(2, 2, rows // 4, width)
        one, two = grad[:, 0], grad[:, 1]
        own_ref[0, :, 0, :, i * width : (i + 1) * width] = jnp.where(
            first_core, one, two
        ).astype(BF16)
        other_ref[0, :, 0, :, i * width : (i + 1) * width] = jnp.where(
            first_core, two, one
        ).astype(BF16)


def dense_grads(attended_t, normed, active, out_bar, up_bar, down_bar):
    width, tokens = attended_t.shape
    own = width // 32
    whole = pl.BlockSpec((tokens, width), lambda i, core: (0, 0))
    rows = pl.BlockSpec((1, 2, 1, own, 3 * width), lambda i, core: (i % 2, 0, i // 2, 0, 0))
    shape = pltpu.HBM((2, 2, 4, own, 3 * width), BF16)
    return pl.pallas_call(
        dense_grad_kernel,
        grid_spec=pltpu.PrefetchScalarGridSpec(
            num_scalar_prefetch=1,
            grid=(8,),
            in_specs=[pl.BlockSpec((width, tokens), lambda i, core: (0, 0))] + [whole] * 5,
            out_specs=[rows, rows],
            scratch_shapes=[pltpu.VMEM((width, tokens), BF16)] * 2,
        ),
        out_shape=[shape, shape],
        compiler_params=KERNEL,
        cost_estimate=LIGHT,
    )(place(), *in_hbm(attended_t, normed, active, out_bar, up_bar, down_bar))


def place():
    head = lax.axis_index("head")
    return jnp.stack([lax.axis_index("blk"), head // 2, head % 2]).astype(jnp.int32)


def assemble_kernel(place_ref, *refs):
    pieces, whole_ref = refs[:10], refs[10]
    half = whole_ref.shape[-1] // 2
    blk, row, core = place_ref[0], place_ref[1], place_ref[2]
    for i in range(2):
        at_core = core if i == 0 else 1 - core
        own, across, beside, one, two = pieces[5 * i : 5 * i + 5]
        whole_ref[0, blk, row, at_core] = own[0]
        whole_ref[0, 1 - blk, row, at_core] = across[0]
        whole_ref[0, blk, 1 - row, at_core] = beside[0]
        whole_ref[0, 1 - blk, 1 - row, at_core, :, :half] = one[0]
        whole_ref[0, 1 - blk, 1 - row, at_core, :, half:] = two[0]


def assemble(pieces):
    batch, own, columns = pieces[0].shape
    specs = [
        pl.BlockSpec((1, own, piece.shape[-1]), lambda i, at: (i, 0, 0))
        for piece in pieces
    ]
    whole = pl.pallas_call(
        assemble_kernel,
        grid_spec=pltpu.PrefetchScalarGridSpec(
            num_scalar_prefetch=1,
            grid=(batch,),
            in_specs=specs,
            out_specs=pl.BlockSpec((1, 2, 2, 2, own, columns), lambda i, at: (i, 0, 0, 0, 0, 0)),
        ),
        out_shape=jax.ShapeDtypeStruct((batch, 2, 2, 2, own, columns), BF16),
        compiler_params=KERNEL,
        cost_estimate=LIGHT,
    )(place(), *pieces)
    return whole.reshape(-1, columns)


def assemble_columns_kernel(place_ref, along_ref, across_ref, whole_ref, *extra_ref):
    blk = place_ref[0]
    columns = whole_ref.shape[-1]
    whole_ref[0, blk] = along_ref[0, :, :columns]
    whole_ref[0, 1 - blk] = across_ref[0, :, :columns]
    for extra in extra_ref:
        extra[0, blk] = along_ref[0, :, columns:]
        extra[0, 1 - blk] = across_ref[0, :, columns:]


def assemble_columns(along, across, columns):
    batch, own, both = along.shape
    rows = pl.BlockSpec((1, own, both), lambda i, at: (i, 0, 0))
    shapes = [(batch, 2, own, columns)]
    if both > columns:
        shapes.append((batch, 2, own, both - columns))
    parts = pl.pallas_call(
        assemble_columns_kernel,
        grid_spec=pltpu.PrefetchScalarGridSpec(
            num_scalar_prefetch=1,
            grid=(batch,),
            in_specs=[rows, rows],
            out_specs=[pl.BlockSpec((1,) + s[1:], lambda i, at: (i, 0, 0, 0)) for s in shapes],
        ),
        out_shape=[pltpu.HBM(s, BF16) for s in shapes],
        compiler_params=KERNEL,
        cost_estimate=LIGHT,
    )(place(), *in_hbm(along, across))
    return [part.reshape(-1, part.shape[-1]) for part in parts]


def assemble_wide_kernel(place_ref, along_ref, across_ref, whole_ref):
    blk = place_ref[0]
    own, columns = along_ref.shape[1], whole_ref.shape[-1]
    for i in range(along_ref.shape[-1] // columns):
        place, part = slice(i * own, (i + 1) * own), slice(i * columns, (i + 1) * columns)
        whole_ref[0, blk, place, :] = along_ref[0, :, part]
        whole_ref[0, 1 - blk, place, :] = across_ref[0, :, part]


def assemble_wide(along, across, columns):
    batch, own, wide = along.shape
    rows = own * (wide // columns)
    piece = pl.BlockSpec((1, own, wide), lambda i, at: (i, 0, 0))
    whole = pl.pallas_call(
        assemble_wide_kernel,
        grid_spec=pltpu.PrefetchScalarGridSpec(
            num_scalar_prefetch=1,
            grid=(batch,),
            in_specs=[piece, piece],
            out_specs=pl.BlockSpec((1, 2, rows, columns), lambda i, at: (i, 0, 0, 0)),
        ),
        out_shape=pltpu.HBM((batch, 2, rows, columns), BF16),
        compiler_params=KERNEL,
        cost_estimate=LIGHT,
    )(place(), *in_hbm(along, across))
    return whole.reshape(-1, columns)


def project_kernel(with_norm, place_ref, *refs):
    pieces, (gain_ref, weight_ref, normed_ref, projected_ref) = refs[:4], refs[4:]
    head = place_ref[1] * 2 + place_ref[2]
    rows = pieces[0].shape[0]
    for i, piece in enumerate(pieces):
        value = piece[...]
        if with_norm:
            stream = value.astype(F32)
            factor = lax.rsqrt(jnp.mean(stream * stream, axis=-1, keepdims=True) + EPSILON)
            value = (stream * factor * gain_ref[...]).astype(BF16)
        normed_ref[pl.ds(pl.multiple_of((head ^ i) * rows, rows), rows), :] = value
    projected = jnp.dot(normed_ref[...], weight_ref[...], preferred_element_type=F32)
    projected_ref[...] = projected.T


def project(pieces, gain, weight, with_norm, token_rows):
    tokens, width = pieces[0].shape
    length, columns = 4 * tokens, weight.shape[1]
    groups = tokens // token_rows
    piece = pl.BlockSpec((token_rows, width), lambda g, at: (g, 0))
    return pl.pallas_call(
        functools.partial(project_kernel, with_norm),
        grid_spec=pltpu.PrefetchScalarGridSpec(
            num_scalar_prefetch=1,
            grid=(groups,),
            in_specs=[piece] * 4
            + [
                pl.BlockSpec((1, width), lambda g, at: (0, 0)),
                pl.BlockSpec((width, columns), lambda g, at: (0, 0)),
            ],
            out_specs=[
                pl.BlockSpec((4 * token_rows, width), lambda g, at: (g, 0)),
                pl.BlockSpec((columns, 4 * token_rows), lambda g, at: (0, g)),
            ],
        ),
        out_shape=[
            pltpu.HBM((length, width), BF16),
            pltpu.HBM((columns, length), F32),
        ],
        compiler_params=KERNEL,
        cost_estimate=LIGHT,
    )(place(), *in_hbm(*pieces), gain.reshape(1, width), *in_hbm(weight))


def project_back_kernel(
    place_ref, bars_ref, weight_ref, normed_ref, own_ref, other_ref, grad_ref, bars_t
):
    @pl.when(pl.program_id(0) == 0)
    def _():
        bars_t[...] = bars_ref[...].astype(F32).T.astype(BF16)

    upper = lax.dot_general(bars_t[...], weight_ref[...], NT, preferred_element_type=F32)
    upper = upper.reshape(2, 2, 2, -1, upper.shape[-1])
    first_core = place_ref[2] == 0
    one, two = upper[:, :, 0], upper[:, :, 1]
    own_ref[...] = jnp.where(first_core, one, two)
    other_ref[...] = jnp.where(first_core, two, one).astype(BF16)
    grad = lax.dot_general(normed_ref[...], bars_t[...], TN, preferred_element_type=F32)
    grad_ref[...] = grad.astype(BF16)


def project_back(bars, weight, normed, token_rows):
    columns, length = bars.shape
    width = weight.shape[0]
    tile = width // 2
    quarter = pl.BlockSpec((2, 2, token_rows, tile), lambda i, at: (0, 0, 0, i))
    return pl.pallas_call(
        project_back_kernel,
        grid_spec=pltpu.PrefetchScalarGridSpec(
            num_scalar_prefetch=1,
            grid=(2,),
            in_specs=[
                pl.BlockSpec((columns, length), lambda i, at: (0, 0)),
                pl.BlockSpec((tile, columns), lambda i, at: (i, 0)),
                pl.BlockSpec((length, tile), lambda i, at: (0, i)),
            ],
            out_specs=[quarter, quarter, pl.BlockSpec((tile, columns), lambda i, at: (i, 0))],
            scratch_shapes=[pltpu.VMEM((length, columns), BF16)],
        ),
        out_shape=[
            pltpu.HBM((2, 2, token_rows, width), F32),
            pltpu.HBM((2, 2, token_rows, width), BF16),
            pltpu.HBM((width, columns), BF16),
        ],
        compiler_params=KERNEL,
        cost_estimate=LIGHT,
    )(place(), *in_hbm(bars, weight, normed))


def rows_back_kernel(place_ref, bars_ref, weight_ref, own_ref, other_ref, bars_t):
    @pl.when(pl.program_id(0) == 0)
    def _():
        bars_t[...] = bars_ref[...].astype(F32).T.astype(BF16)

    upper = lax.dot_general(bars_t[...], weight_ref[...], NT, preferred_element_type=F32)
    upper = upper.reshape(2, 2, 2, -1, upper.shape[-1])
    first_core = place_ref[2] == 0
    one, two = upper[:, :, 0], upper[:, :, 1]
    own_ref[...] = jnp.where(first_core, one, two)
    other_ref[...] = jnp.where(first_core, two, one).astype(BF16)


def rows_back(bars, weight, token_rows):
    columns, length = bars.shape
    width = weight.shape[0]
    tile = width // 2
    quarter = pl.BlockSpec((2, 2, token_rows, tile), lambda i, at: (0, 0, 0, i))
    return pl.pallas_call(
        rows_back_kernel,
        grid_spec=pltpu.PrefetchScalarGridSpec(
            num_scalar_prefetch=1,
            grid=(2,),
            in_specs=[
                pl.BlockSpec((columns, length), lambda i, at: (0, 0)),
                pl.BlockSpec((tile, columns), lambda i, at: (i, 0)),
            ],
            out_specs=[quarter, quarter],
            scratch_shapes=[pltpu.VMEM((length, columns), BF16)],
        ),
        out_shape=[
            pltpu.HBM((2, 2, token_rows, width), F32),
            pltpu.HBM((2, 2, token_rows, width), BF16),
        ],
        compiler_params=KERNEL,
        cost_estimate=LIGHT,
    )(place(), *in_hbm(bars, weight))


def weight_back_kernel(bars_ref, normed_ref, grad_ref):
    grad = jnp.dot(bars_ref[...], normed_ref[...], preferred_element_type=F32)
    grad_ref[...] = grad.T.astype(BF16)


def weight_back(bars, normed):
    columns, length = bars.shape
    width = normed.shape[1]
    tile = width // 5
    return pl.pallas_call(
        weight_back_kernel,
        grid=(5,),
        in_specs=[
            pl.BlockSpec((columns, length), lambda i: (0, 0)),
            pl.BlockSpec((length, tile), lambda i: (0, i)),
        ],
        out_specs=pl.BlockSpec((tile, columns), lambda i: (i, 0)),
        out_shape=pltpu.HBM((width, columns), BF16),
        compiler_params=KERNEL,
        cost_estimate=LIGHT,
    )(*in_hbm(bars, normed))


def tied(*arrays):
    return lax.optimization_barrier(arrays)


def swapped(array, axis, mask):
    size = lax.axis_size(axis)
    return lax.ppermute(array, axis, [(i, i ^ mask) for i in range(size)])


def pick(array, index, axis=0):
    return lax.dynamic_index_in_dim(array, index, axis, keepdims=False)


def swap_halves(array):
    me = lax.axis_index("blk")
    got = swapped(pick(array, 1 - me), "blk", 1)
    kept = pick(array, me)
    return jnp.stack([jnp.where(me == 0, kept, got), jnp.where(me == 0, got, kept)])


def scatter_row(halves):
    row = lax.axis_index("head") // 2
    got = swapped(pick(halves, 1 - row, 1).astype(BF16), "head", 2).astype(F32)
    return (pick(halves, row, 1) + got).reshape(-1, halves.shape[-1])


def over_head(parts):
    return lax.all_to_all(parts, "head", split_axis=0, concat_axis=0, tiled=True)


def qkv_columns(rows, extra):
    own, width = rows.shape
    part = width // 3 // 4
    sent = rows.reshape(own, 3, 4, part).transpose(2, 0, 1, 3).reshape(4, own, 3 * part)
    if extra is not None:
        sent = jnp.concatenate([sent, jnp.broadcast_to(extra[None], (4,) + extra.shape)], axis=2)
    return over_head(sent)


def along_batch(piece):
    return lax.all_gather(piece, "batch", axis=0, tiled=False)


def other_core(array):
    return swapped(array, "head", 1)


def to_beside(across):
    return swapped(across[..., : across.shape[-1] // 2], "head", 2)


def to_across(beside):
    return swapped(beside[..., beside.shape[-1] // 2 :], "blk", 1)


def over_batch(parts):
    return lax.psum_scatter(parts.astype(BF16), "batch", scatter_dimension=0, tiled=False)


def across_sum(halves):
    blk = lax.axis_index("blk")
    got = swapped(pick(halves, 1 - blk), "blk", 1).astype(F32)
    return (pick(halves, blk).astype(F32) + got).astype(BF16)


def columns_to_rows(moved):
    rows = moved.shape[1]
    return moved.reshape(4, rows, 3, -1).transpose(1, 2, 0, 3).reshape(rows, -1).astype(F32)


def diagonal_rows(cored):
    blk, row = place()[:2]
    rows = pick(pick(cored, 1 - blk), 1 - row)
    half = rows.shape[-1] // 2
    return rows[..., :half], rows[..., half:]


def neighbour_rows(cored, one, two):
    blk, row = place()[:2]
    half = one.shape[-1]
    across = pick(pick(cored, 1 - blk), row)
    beside = pick(pick(cored, blk), 1 - row)
    across = jnp.concatenate(
        [across[..., :half], across[..., half:].astype(F32) + two.astype(F32)], axis=-1
    ).astype(BF16)
    beside = jnp.concatenate(
        [beside[..., :half].astype(F32) + one.astype(F32), beside[..., half:]], axis=-1
    ).astype(BF16)
    return across, beside


def sent_beside_and_across(across, beside):
    return swapped(across, "blk", 1), swapped(beside, "head", 2)


def heads_grad(weight, out_bar):
    return dot_cols(weight, out_bar).astype(BF16).reshape(4, -1, out_bar.shape[0])


def own_sum(cored, across, beside):
    blk, row = place()[:2]
    own = pick(pick(cored, blk), row)
    return own.astype(F32) + across.astype(F32) + beside.astype(F32)


def sum_over(array, *hops):
    for axis, mask in hops:
        array = array + swapped(array, axis, mask)
    return array


def gain_back(weight, weight_grad, gain):
    return jnp.sum(weight.astype(F32) * weight_grad, axis=-1) / gain.astype(F32)


def lower_of(upper, stream, factor, gain):
    return norm_back(upper, stream, factor, gain)[0]


def spread_device(
    tokens,
    segments,
    qkv_weight,
    out_weight,
    up_weight,
    down_weight,
    attn_gain,
    mlp_gain,
    scale_param,
    cotangent,
):
    layers, head_dim = scale_param.shape
    _, token_rows, width = tokens.shape
    scale_vecs = SCALE_BASE / math.sqrt(head_dim) * jax.nn.softplus(scale_param)
    segments = pick(segments, lax.axis_index("blk"))
    own_gains = jnp.concatenate([attn_gain, mlp_gain], axis=0)

    part3 = 3 * width // 4
    dense_own = [
        jnp.concatenate([out_weight[i], up_weight[i], down_weight[i]], axis=1) for i in (0, 1)
    ]

    first = swap_halves(tokens).reshape(-1, width)
    columns = qkv_columns(qkv_weight[0], own_gains.T)
    columns, first = tied(columns.reshape(-1, columns.shape[-1]), first)
    stream = first.astype(F32)
    along = along_batch(columns)
    far, near = swapped(first, "head", 2), other_core(first)
    both = other_core(far)
    upper = swap_halves(cotangent)
    along, near, far, both, dense_near, upper = tied(
        along, near, far, both, dense_own[0], upper
    )
    token_pieces = (first, near, far, both)
    dense_near = along_batch(dense_near)
    qkv_across = swapped(along, "blk", 1)
    next_columns = jnp.concatenate(list(qkv_columns(qkv_weight[1], None)), axis=1)
    qkv_across, dense_near, next_columns = tied(qkv_across, dense_near, next_columns)
    across, beside = swapped(dense_near, "blk", 1), swapped(dense_near, "head", 2)
    next_both = along_batch(jnp.stack([next_columns, dense_own[1]]))
    weight, gains = assemble_columns(along, qkv_across, part3)
    qkvs = [weight]
    gains = gains.T.astype(F32)

    kept, denses = [], []
    for layer in range(layers):
        normed, factor_one = normalize(stream, gains[layer])
        if layer == 1:
            normed = normed.astype(BF16)
            far, near = swapped(normed, "head", 2), other_core(normed)
            far, next_across, dense_next = tied(far, next_across, dense_next)
            across, beside = swapped(dense_next, "blk", 1), swapped(dense_next, "head", 2)
            token_pieces = (normed, near, far, other_core(far))
            qkvs.append(assemble_wide(next_along, next_across, part3))
        normed_all, projected = project(
            token_pieces, gains[layer], qkvs[layer], layer == 0, token_rows
        )
        attended, log_total = attend_rows(
            projected, scale_vecs[layer], segments, 4, token_rows
        )
        attended, across, beside = tied(attended, across, beside)
        one, two = to_beside(across), to_across(beside)
        if layer == 0:
            two, next_both = tied(two, next_both)
            next_along, dense_next = next_both[:, 0], next_both[:, 1]
            next_across = swapped(next_along, "blk", 1)
            attended_t, one, two = tied(over_head(attended), one, two)
        else:
            dense_near = dense_next
            attended_t, one, two = tied(over_head(attended), one, two)
        pieces = (dense_near, across, beside, one, two)
        pieces += tuple(other_core(piece) for piece in pieces)
        attended_t = attended_t.reshape(width, -1)
        denses.append(assemble(pieces))
        dense = denses[layer]
        out_w, up_w, down_w = dense[:, :width], dense[:, width:-width], dense[:, -width:]
        middle = stream + dot_rows(attended_t, out_w)
        normed_two, factor_two = normalize(middle, gains[layers + layer])
        normed_two = normed_two.astype(BF16)
        hidden = dot(normed_two, up_w)
        active = (hidden * jax.nn.sigmoid(hidden)).astype(BF16)
        kept.append(
            (
                stream, factor_one, normed_all, projected, log_total, attended_t, middle,
                factor_two, normed_two, hidden, active,
            )
        )
        stream = middle + dot(active, down_w)
    layer_out = swap_halves(stream.astype(BF16).reshape(tokens.shape))
    upper = upper.reshape(-1, width).astype(F32)

    scale_grads = [None] * layers
    for layer in reversed(range(layers)):
        (
            stream, factor_one, normed_all, projected, log_total, attended_t, middle,
            factor_two, normed_two, hidden, active,
        ) = kept[layer]
        qkv, dense = qkvs[layer], denses[layer]
        out_w, up_w, down_w = dense[:, :width], dense[:, width:-width], dense[:, -width:]
        down_bar = upper.astype(BF16)
        gate = jax.nn.sigmoid(hidden)
        up_bar = (
            dot_cols(down_bar, down_w) * gate * (1.0 + hidden * (1.0 - gate))
        ).astype(BF16)
        middle_grad = upper + lower_of(
            dot_cols(up_bar, up_w), middle, factor_two, gains[layers + layer]
        )
        out_bar = middle_grad.astype(BF16)
        if layer == 0:
            attended_grad = over_head(heads_grad(out_w, out_bar))
            grads, others = dense_grads(attended_t, normed_two, active, out_bar, up_bar, down_bar)
            attended_grad, others, z_sum, across, beside = tied(
                attended_grad, others, z_sum, across, beside
            )
            others = other_core(others)
            attended_grad, summed = tied(attended_grad, own_sum(cored, across, beside))
            summed = over_batch(summed)
            z_across = across_sum(z_sum)
        else:
            attended_grad = over_head(heads_grad(out_w, out_bar))
            grads, others = dense_grads(attended_t, normed_two, active, out_bar, up_bar, down_bar)
            attended_grad, others, layer_out = tied(attended_grad, others, layer_out)
            others = other_core(others)
        bars, scale_grads[layer] = attend_back_rows(
            projected, attended_grad, log_total, scale_vecs[layer], segments, token_rows
        )
        if layer == 0:
            bars, others, z_across = tied(bars, others, z_across)
            moved = over_head(z_across.reshape(4, -1, z_across.shape[-1]))
            qkv_grad = weight_back(bars, normed_all)
            bars, qkv_grad, moved = tied(bars, qkv_grad, moved)
            z_sum = over_batch(qkv_grad.reshape(4, 2, -1, qkv_grad.shape[-1]))
            cored = (grads.astype(F32) + others.astype(F32)).astype(BF16)
            bars, rows = tied(bars, diagonal_rows(cored))
            diagonal = sent_beside_and_across(*rows)
            halves, to_core = rows_back(bars, qkv, token_rows)
            halves, to_core, diagonal, summed = tied(halves, to_core, diagonal, summed)
            halves, to_core, rows = tied(halves, to_core, neighbour_rows(cored, *diagonal))
            sent = sent_beside_and_across(*rows)
            halves = halves + other_core(to_core).astype(F32)
            scale_sum = sum_over(jnp.stack(scale_grads), ("head", 1), ("batch", 1), ("batch", 2))
            halves, sent, z_sum, scale_sum = tied(halves, sent, z_sum, scale_sum)
            halves, own = tied(halves, own_sum(cored, *sent))
            dense_first = over_batch(own)
            normed_grad = scatter_row(halves)
            dense_grad = [dense_first, summed]
            z_across = across_sum(z_sum)
            z_across = over_head(z_across.reshape(4, -1, z_across.shape[-1]))
            qkv_grads = [columns_to_rows(z_across), columns_to_rows(moved)]
        else:
            bars, others = tied(bars, others)
            cored = (grads.astype(F32) + others.astype(F32)).astype(BF16)
            bars, rows = tied(bars, diagonal_rows(cored))
            diagonal = sent_beside_and_across(*rows)
            halves, to_core, qkv_grad = project_back(bars, qkv, normed_all, token_rows)
            z_sum = over_batch(qkv_grad.reshape(4, 2, -1, qkv_grad.shape[-1]))
            to_core, halves, diagonal = tied(to_core, halves, diagonal)
            to_core, rows = tied(to_core, neighbour_rows(cored, *diagonal))
            across = swapped(rows[0], "blk", 1)
            halves = halves + other_core(to_core).astype(F32)
            normed_grad = scatter_row(halves)
            normed_grad, beside = tied(normed_grad, rows[1])
            beside = swapped(beside, "head", 2)
        upper = middle_grad + lower_of(normed_grad, stream, factor_one, gains[layer])
    input_grad = swap_halves(upper.astype(BF16).reshape(tokens.shape)).astype(F32)
    scale_total = sum_over(scale_sum, ("head", 2), ("blk", 1))
    scale_grad = scale_total * (SCALE_BASE / math.sqrt(head_dim)) * jax.nn.sigmoid(scale_param)
    dense_all = jnp.stack([part.astype(F32) for part in dense_grad])
    qkv_all = jnp.stack(qkv_grads)
    up_all = dense_all[:, :, width:-width]
    return (
        layer_out,
        input_grad,
        qkv_all,
        dense_all[:, :, :width],
        up_all,
        dense_all[:, :, -width:],
        gain_back(qkv_weight, qkv_all, attn_gain),
        gain_back(up_weight, up_all, mlp_gain),
        scale_grad,
    )


def per_device(*args):
    tokens, segments = args[0], args[1]
    sizes = tuple(lax.axis_size(axis) for axis in ALL)
    heads = tokens.shape[2] // args[8].shape[1]
    spread = (
        sizes == (4, 2, 4)
        and tokens.shape[0] == 2
        and args[2].shape[0] == 2
        and tokens.shape[1] % 128 == 0
        and Q_ROWS % tokens.shape[1] == 0
        and segments.shape[1] <= WINDOW
        and segments.shape[1] % Q_ROWS == 0
        and heads % 4 == 0
        and tokens.shape[2] % 256 == 0
    )
    return spread_device(*args) if spread else general_device(*args)


def solution(mesh):
    rows = P(None, ALL, None)
    by_token = P("batch", ("blk", "head"), None)
    return jax.shard_map(
        per_device,
        mesh=mesh,
        in_specs=(
            by_token, P("batch", None), rows, rows, rows, rows, P(None, ALL), P(None, ALL), P(),
            by_token,
        ),
        out_specs=(
            by_token, by_token, rows, rows, rows, rows, P(None, ALL), P(None, ALL), P(),
        ),
        check_vma=False,
    )
```

```python
import functools
import math

import jax
import jax.numpy as jnp
from jax import lax
from jax.experimental import pallas as pl
from jax.experimental.pallas import tpu as pltpu
from jax.sharding import PartitionSpec as P

WINDOW = 1024
EPSILON = 1e-06
SCALE_BASE = 1.4426950408889634
MASKED_SCORE = -1e30

ALL = ("batch", "blk", "head")
REST = ("batch", "blk")
F32 = jnp.float32
BF16 = jnp.bfloat16


def shifted(block, axis, distance):
    devices = range(lax.axis_size(axis))
    route = [(i - distance, i) for i in devices if i - distance in devices]
    return lax.ppermute(block, axis, route)


NT = (((1,), (1,)), ((), ()))
TN = (((0,), (0,)), ((), ()))


def dot(left, right):
    return jnp.dot(left, right, preferred_element_type=F32)


def dot_rows(left, right):
    return lax.dot_general(left, right, (((0,), (0,)), ((), ())), preferred_element_type=F32)


def dot_cols(left, right):
    return lax.dot_general(left, right, (((1,), (1,)), ((), ())), preferred_element_type=F32)


def normalize(stream, gain):
    factor = lax.rsqrt(jnp.mean(stream * stream, axis=-1, keepdims=True) + EPSILON)
    return stream * factor * gain, factor


def norm_back(upper, stream, factor, gain):
    inner = upper * gain
    gain_grad = jnp.sum(upper * stream * factor, axis=0)
    lower = factor * inner - stream * factor * factor * factor * jnp.mean(
        inner * stream, axis=-1, keepdims=True
    )
    return lower, gain_grad


class Plan:
    def __init__(self, tokens):
        self.seqs, self.rows, self.width = tokens.shape
        self.heads = lax.axis_size("head")
        self.blks = lax.axis_size("blk")
        self.block = self.rows * self.heads
        self.whole = self.seqs % self.blks == 0
        if self.whole:
            self.groups, self.own_seqs = self.blks, self.seqs // self.blks
            self.reach = 0
        else:
            self.groups, self.own_seqs = 1, self.seqs
            self.reach = min((WINDOW - 1) // self.block + 1, self.blks - 1)
        self.length = self.groups * self.block
        self.tokens = self.seqs * self.rows


def to_plan(plan, array):
    if plan.whole and plan.blks > 1:
        array = lax.all_to_all(array, "blk", split_axis=0, concat_axis=0, tiled=True)
    return array.reshape(plan.tokens, plan.width)


def from_plan(plan, flat):
    array = flat.reshape(plan.seqs, plan.rows, plan.width)
    if plan.whole and plan.blks > 1:
        array = lax.all_to_all(array, "blk", split_axis=0, concat_axis=0, tiled=True)
    return array


def in_sequence(plan, by_head, width):
    parts = by_head.reshape(plan.heads, plan.groups, plan.own_seqs, plan.rows, width)
    return parts.transpose(2, 1, 0, 3, 4).reshape(-1, width)


def by_owner(plan, rows, width):
    parts = rows.reshape(plan.own_seqs, plan.groups, plan.heads, plan.rows, width)
    return parts.transpose(2, 1, 0, 3, 4).reshape(plan.heads, plan.tokens, width)


def gather_tokens(plan, rows):
    moved = lax.all_gather(rows, "head", axis=0, tiled=False)
    return in_sequence(plan, moved, rows.shape[-1])


def scatter_tokens(plan, rows):
    width = rows.shape[-1]
    return lax.psum_scatter(
        by_owner(plan, rows.astype(BF16), width), "head", scatter_dimension=0, tiled=False
    ).astype(F32)


def heads_to_tokens(plan, rows):
    part = rows.shape[-1]
    moved = lax.all_to_all(
        by_owner(plan, rows, part), "head", split_axis=0, concat_axis=0, tiled=True
    )
    return moved.transpose(1, 0, 2).reshape(plan.tokens, plan.heads * part)


def tokens_to_heads(plan, rows):
    part = rows.shape[-1] // plan.heads
    sent = rows.reshape(plan.tokens, plan.heads, part).transpose(1, 0, 2)
    moved = lax.all_to_all(sent, "head", split_axis=0, concat_axis=0, tiled=True)
    return in_sequence(plan, moved, part)


def gather_qkv(rows):
    own, width = rows.shape
    heads = lax.axis_size("head")
    part = width // 3 // heads
    sent = rows.reshape(own, 3, heads, part).transpose(2, 0, 1, 3).reshape(heads, own, 3 * part)
    moved = lax.all_to_all(sent, "head", split_axis=0, concat_axis=0, tiled=True)
    full = lax.all_gather(moved, REST, axis=0, tiled=True)
    return full.reshape(-1, 3 * part)


def scatter_qkv(grad):
    heads = lax.axis_size("head")
    part = grad.shape[1] // 3
    summed = lax.psum_scatter(grad.astype(BF16), REST, scatter_dimension=0, tiled=True)
    own = summed.shape[0] // heads
    moved = lax.all_to_all(
        summed.reshape(heads, own, 3 * part), "head", split_axis=0, concat_axis=0, tiled=True
    )
    return (
        moved.reshape(heads, own, 3, part)
        .transpose(1, 2, 0, 3)
        .reshape(own, 3 * heads * part)
        .astype(F32)
    )


def window_mask(plan, segments, block_index):
    key_count = plan.length + plan.reach * plan.block
    if plan.whole:
        query_segs, key_segs = segments, segments
    else:
        leading = jnp.full((plan.own_seqs, plan.reach * plan.block), -1, jnp.int32)
        padded = jnp.concatenate([leading, segments], axis=1)
        start = block_index * plan.block
        query_segs = lax.dynamic_slice_in_dim(segments, start, plan.block, 1)
        key_segs = lax.dynamic_slice_in_dim(padded, start, key_count, 1)
    query_place = jnp.arange(plan.length, dtype=jnp.int32)[:, None] + plan.reach * plan.block
    key_place = jnp.arange(key_count, dtype=jnp.int32)[None, :]
    near = (key_place <= query_place) & (query_place - key_place < WINDOW)
    return (key_segs[:, None, :] == query_segs[:, :, None]) & near[None]


def with_earlier(plan, own):
    arrived = [own]
    for _ in range(plan.reach):
        arrived.append(shifted(arrived[-1], "blk", 1))
    return jnp.concatenate(arrived[::-1], axis=1) if plan.reach else own


def to_earlier(plan, grads):
    if not plan.reach:
        return grads
    block = plan.block
    total = grads[:, :block]
    for step in range(1, plan.reach + 1):
        total = (
            shifted(total.astype(BF16), "blk", -1).astype(F32)
            + grads[:, step * block : (step + 1) * block]
        )
    return total


def scores_of(queries, keys, allowed):
    scores = jnp.einsum("sqhd,skhd->shqk", queries, keys, preferred_element_type=F32)
    return jnp.where(allowed[:, None], scores, MASKED_SCORE)


def attend(queries, keys, values, allowed):
    scores = scores_of(queries, keys, allowed)
    top_score = jnp.max(scores, axis=-1, keepdims=True)
    exp_terms = jnp.exp(scores - top_score)
    totals = jnp.sum(exp_terms, axis=-1, keepdims=True)
    probs_low = (exp_terms / totals).astype(BF16)
    attended = jnp.einsum("shqk,skhd->sqhd", probs_low, values, preferred_element_type=F32)
    return attended, top_score + jnp.log(totals)


def attend_back(queries, keys, values, allowed, log_total, attended_grad):
    probs = jnp.exp(scores_of(queries, keys, allowed) - log_total)
    probs_low = probs.astype(BF16)
    values_grad = jnp.einsum(
        "shqk,sqhd->skhd", probs_low, attended_grad, preferred_element_type=F32
    )
    probs_grad = jnp.einsum("sqhd,skhd->shqk", attended_grad, values, preferred_element_type=F32)
    row_dot = jnp.sum(probs_grad * probs, axis=-1, keepdims=True)
    scores_low = (probs * (probs_grad - row_dot)).astype(BF16)
    queries_grad = jnp.einsum("shqk,skhd->sqhd", scores_low, keys, preferred_element_type=F32)
    keys_grad = jnp.einsum("shqk,sqhd->skhd", scores_low, queries, preferred_element_type=F32)
    return queries_grad, keys_grad, values_grad


def forward(plan, stream, qkv, dense, gains, scale_vec, allowed):
    width = plan.width
    head_dim = scale_vec.shape[0]
    part = qkv.shape[1] // 3
    local_heads = part // head_dim
    split = (plan.own_seqs, plan.length, local_heads, head_dim)
    out_w, up_w, down_w = dense[:, :width], dense[:, width:-width], dense[:, -width:]
    normed, factor_one = normalize(stream, gains[0])
    normed_all = gather_tokens(plan, normed.astype(BF16))
    projected = dot(normed_all, qkv)
    query_pre = projected[:, :part].reshape(split)
    queries = (query_pre * scale_vec).astype(BF16)
    keys = with_earlier(plan, projected[:, part : 2 * part].astype(BF16).reshape(split))
    values = with_earlier(plan, projected[:, 2 * part :].astype(BF16).reshape(split))
    attended_part, log_total = attend(queries, keys, values, allowed)
    attended = heads_to_tokens(plan, attended_part.astype(BF16).reshape(-1, part))
    middle = stream + dot(attended, out_w)
    normed_two, factor_two = normalize(middle, gains[1])
    normed_two = normed_two.astype(BF16)
    hidden = dot(normed_two, up_w)
    active = (hidden * jax.nn.sigmoid(hidden)).astype(BF16)
    result = middle + dot(active, down_w)
    kept = (
        stream, factor_one, normed_all, query_pre, queries, keys, values, log_total,
        attended, middle, factor_two, normed_two, hidden, active,
    )
    return result, kept


def backward(plan, upper, kept, qkv, dense, gains, scale_vec, allowed):
    (
        stream, factor_one, normed_all, query_pre, queries, keys, values, log_total,
        attended, middle, factor_two, normed_two, hidden, active,
    ) = kept
    width = plan.width
    head_dim = scale_vec.shape[0]
    part = qkv.shape[1] // 3
    out_w, up_w, down_w = dense[:, :width], dense[:, width:-width], dense[:, -width:]
    upper_low = upper.astype(BF16)
    down_grad = dot_rows(active, upper_low)
    active_grad = dot_cols(upper_low, down_w)
    gate = jax.nn.sigmoid(hidden)
    hidden_low = (active_grad * gate * (1.0 + hidden * (1.0 - gate))).astype(BF16)
    up_grad = dot_rows(normed_two, hidden_low)
    extra_two, mlp_gain_grad = norm_back(dot_cols(hidden_low, up_w), middle, factor_two, gains[1])
    middle_grad = upper + extra_two
    middle_low = middle_grad.astype(BF16)
    out_grad = dot_rows(attended, middle_low)
    dense_grad = jnp.concatenate([out_grad, up_grad, down_grad], axis=1).astype(BF16)
    dense_own = lax.psum_scatter(dense_grad, ALL, scatter_dimension=0, tiled=True)
    attended_grad = tokens_to_heads(plan, dot_cols(middle_low, out_w).astype(BF16))
    queries_grad, keys_grad, values_grad = attend_back(
        queries, keys, values, allowed, log_total, attended_grad.reshape(queries.shape)
    )
    query_bar = queries_grad.astype(BF16).astype(F32)
    scale_vec_grad = jnp.sum((query_bar * query_pre).reshape(-1, head_dim), axis=0)
    query_low = (query_bar * scale_vec).astype(BF16).reshape(-1, part)
    keys_low = to_earlier(plan, keys_grad).astype(BF16).reshape(-1, part)
    values_low = to_earlier(plan, values_grad).astype(BF16).reshape(-1, part)
    projected_low = jnp.concatenate([query_low, keys_low, values_low], axis=1)
    normed_grad = scatter_tokens(plan, dot_cols(projected_low, qkv))
    qkv_own = scatter_qkv(dot_rows(normed_all, projected_low))
    extra_one, attn_gain_grad = norm_back(normed_grad, stream, factor_one, gains[0])
    lower = middle_grad + extra_one
    return lower, qkv_own, dense_own, (attn_gain_grad, mlp_gain_grad), scale_vec_grad


def general_device(
    tokens,
    segments,
    qkv_weight,
    out_weight,
    up_weight,
    down_weight,
    attn_gain,
    mlp_gain,
    scale_param,
    cotangent,
):
    plan = Plan(tokens)
    layers, head_dim = scale_param.shape
    block_index = lax.axis_index("blk")
    scale_vecs = SCALE_BASE / math.sqrt(head_dim) * jax.nn.softplus(scale_param)
    own_gains = jnp.concatenate([attn_gain, mlp_gain], axis=0)
    gains = (
        lax.all_gather(own_gains.reshape(1, -1), ALL, axis=0, tiled=True)
        .reshape(-1, 2 * layers, attn_gain.shape[1])
        .transpose(1, 0, 2)
        .reshape(2 * layers, plan.width)
        .astype(F32)
    )
    if plan.whole:
        segments = lax.dynamic_slice_in_dim(
            segments, block_index * plan.own_seqs, plan.own_seqs, 0
        )
    allowed = window_mask(plan, segments, block_index)
    stream = to_plan(plan, tokens).astype(F32)
    qkvs, denses, kept = [], [], []
    for layer in range(layers):
        qkvs.append(gather_qkv(qkv_weight[layer]))
        own = jnp.concatenate([out_weight[layer], up_weight[layer], down_weight[layer]], axis=1)
        denses.append(lax.all_gather(own, ALL, axis=0, tiled=True))
        layer_gains = (gains[layer], gains[layers + layer])
        stream, saved = forward(
            plan, stream, qkvs[layer], denses[layer], layer_gains, scale_vecs[layer], allowed
        )
        kept.append(saved)
    layer_out = from_plan(plan, stream.astype(BF16))
    upper = to_plan(plan, cotangent).astype(F32)
    qkv_grads, dense_grads = [None] * layers, [None] * layers
    gain_grads, scale_grads = [None] * layers, [None] * layers
    for layer in reversed(range(layers)):
        layer_gains = (gains[layer], gains[layers + layer])
        upper, qkv_grads[layer], dense_grads[layer], gain_grads[layer], scale_grads[layer] = (
            backward(
                plan, upper, kept[layer], qkvs[layer], denses[layer], layer_gains,
                scale_vecs[layer], allowed,
            )
        )
    input_grad = from_plan(plan, upper.astype(BF16)).astype(F32)
    small = jnp.concatenate(
        [g[0] for g in gain_grads] + [g[1] for g in gain_grads] + scale_grads, axis=0
    )
    total = lax.psum(small, ALL)
    gain_total = total[: 2 * layers * plan.width].reshape(2 * layers, plan.width)
    owner = lax.axis_index(ALL)
    gain_rows = attn_gain.shape[1]
    own_total = lax.dynamic_slice_in_dim(gain_total, owner * gain_rows, gain_rows, 1)
    scale_total = total[2 * layers * plan.width :].reshape(layers, head_dim)
    scale_grad = scale_total * (SCALE_BASE / math.sqrt(head_dim)) * jax.nn.sigmoid(scale_param)
    dense_all = jnp.stack(dense_grads).astype(F32)
    width = plan.width
    return (
        layer_out,
        input_grad,
        jnp.stack(qkv_grads),
        dense_all[:, :, :width],
        dense_all[:, :, width:-width],
        dense_all[:, :, -width:],
        own_total[:layers],
        own_total[layers:],
        scale_grad,
    )


Q_ROWS = 256
KERNEL = pltpu.CompilerParams(vmem_limit_bytes=32 * 1024 * 1024)
LIGHT = pl.CostEstimate(flops=1 << 20, bytes_accessed=1 << 20, transcendentals=0)


def in_hbm(*arrays):
    return [pltpu.with_memory_space_constraint(array, pltpu.HBM) for array in arrays]


def allowed_keys(col, row, first):
    count = first + row.shape[1]
    key_place = lax.broadcasted_iota(jnp.int32, (count, row.shape[1]), 0)
    query_place = lax.broadcasted_iota(jnp.int32, (count, row.shape[1]), 1) + first
    return (col[:count] == row) & (key_place <= query_place)


def token_places(length, heads, token_rows):
    for first in range(0, length, Q_ROWS):
        parts = []
        for start in range(0, Q_ROWS, token_rows):
            place = (first + start) // token_rows
            parts.append((start, place % heads, place // heads * token_rows))
        yield first, parts


def attend_kernel(token_rows, proj_ref, scale_ref, col_ref, row_ref, out_ref, lse_ref):
    length = proj_ref.shape[-1]
    queries = (proj_ref[0, 0] * scale_ref[...]).astype(BF16)
    keys = proj_ref[1, 0].T.astype(BF16)
    values = proj_ref[2, 0].astype(BF16)
    for first, parts in token_places(length, out_ref.shape[0], token_rows):
        end = first + Q_ROWS
        scores = jnp.dot(keys[:end], queries[:, first:end], preferred_element_type=F32)
        allowed = allowed_keys(col_ref[...], row_ref[:, first:end], first)
        scores = jnp.where(allowed, scores, MASKED_SCORE)
        top = jnp.max(scores, axis=0, keepdims=True)
        terms = jnp.exp(scores - top)
        total = jnp.sum(terms, axis=0, keepdims=True)
        probs = (terms * (1.0 / total)).astype(BF16)
        attended = jnp.dot(values[:, :end], probs, preferred_element_type=F32).astype(BF16)
        lse_ref[0, :, first:end] = top + jnp.log(total)
        for start, owner, offset in parts:
            out_ref[owner, 0, :, offset : offset + token_rows] = attended[
                :, start : start + token_rows
            ]


def attend_rows(projected, scale_vec, segments, owners, token_rows):
    head_dim = scale_vec.shape[0]
    length = projected.shape[1]
    local_heads = projected.shape[0] // 3 // head_dim
    tokens = length // owners
    attended, log_total = pl.pallas_call(
        functools.partial(attend_kernel, token_rows),
        grid=(local_heads,),
        in_specs=[
            pl.BlockSpec((3, 1, head_dim, length), lambda h: (0, h, 0, 0)),
            pl.BlockSpec((head_dim, 1), lambda h: (0, 0)),
            pl.BlockSpec((length, 1), lambda h: (0, 0)),
            pl.BlockSpec((1, length), lambda h: (0, 0)),
        ],
        out_specs=[
            pl.BlockSpec((owners, 1, head_dim, tokens), lambda h: (0, h, 0, 0)),
            pl.BlockSpec((1, 1, length), lambda h: (h, 0, 0)),
        ],
        out_shape=[
            jax.ShapeDtypeStruct((owners, local_heads, head_dim, tokens), BF16),
            jax.ShapeDtypeStruct((local_heads, 1, length), F32),
        ],
        compiler_params=KERNEL,
        cost_estimate=LIGHT,
    )(
        projected.reshape(3, local_heads, head_dim, length),
        scale_vec.reshape(head_dim, 1),
        segments.reshape(length, 1),
        segments.reshape(1, length),
    )
    return attended.reshape(owners, local_heads * head_dim, tokens), log_total


def attend_back_kernel(
    token_rows,
    proj_ref,
    grad_ref,
    lse_ref,
    scale_ref,
    col_ref,
    row_ref,
    out_ref,
    scale_grad_ref,
    keys_acc,
    values_acc,
):
    length = proj_ref.shape[-1]
    scale = scale_ref[...]
    query_pre = proj_ref[0, 0]
    queries = (query_pre * scale).astype(BF16)
    keys_t = proj_ref[1, 0].astype(BF16)
    keys = proj_ref[1, 0].T.astype(BF16)
    values = proj_ref[2, 0].T.astype(BF16)
    keys_acc[...] = jnp.zeros_like(keys_acc)
    values_acc[...] = jnp.zeros_like(values_acc)
    scale_grad = jnp.zeros((scale.shape[0], 1), F32)
    for first, parts in token_places(length, grad_ref.shape[0], token_rows):
        end = first + Q_ROWS
        block = queries[:, first:end]
        grad = jnp.concatenate(
            [grad_ref[owner, 0, :, at : at + token_rows] for _, owner, at in parts], axis=1
        )
        scores = jnp.dot(keys[:end], block, preferred_element_type=F32)
        allowed = allowed_keys(col_ref[...], row_ref[:, first:end], first)
        scores = jnp.where(allowed, scores, MASKED_SCORE)
        probs = jnp.exp(scores - lse_ref[0, :, first:end])
        probs_grad = jnp.dot(values[:end], grad, preferred_element_type=F32)
        row_dot = jnp.sum(probs_grad * probs, axis=0, keepdims=True)
        scores_low = (probs * (probs_grad - row_dot)).astype(BF16)
        values_acc[:, :end] += lax.dot_general(
            grad, probs.astype(BF16), NT, preferred_element_type=F32
        )
        keys_acc[:, :end] += lax.dot_general(
            block, scores_low, NT, preferred_element_type=F32
        )
        query_bar = jnp.dot(keys_t[:, :end], scores_low, preferred_element_type=F32)
        query_bar = query_bar.astype(BF16).astype(F32)
        scale_grad += jnp.sum(query_bar * query_pre[:, first:end], axis=1, keepdims=True)
        out_ref[0, 0, :, first:end] = (query_bar * scale).astype(BF16)
    out_ref[1, 0] = keys_acc[...].astype(BF16)
    out_ref[2, 0] = values_acc[...].astype(BF16)
    spread = jnp.broadcast_to(scale_grad, scale_grad_ref.shape)

    @pl.when(pl.program_id(0) == 0)
    def _():
        scale_grad_ref[...] = spread

    @pl.when(pl.program_id(0) > 0)
    def _():
        scale_grad_ref[...] += spread


def attend_back_rows(projected, attended_grad, log_total, scale_vec, segments, token_rows):
    head_dim = scale_vec.shape[0]
    length = projected.shape[1]
    local_heads = projected.shape[0] // 3 // head_dim
    owners, _, tokens = attended_grad.shape
    lanes = 128
    grads, scale_grad = pl.pallas_call(
        functools.partial(attend_back_kernel, token_rows),
        grid=(local_heads,),
        in_specs=[
            pl.BlockSpec((3, 1, head_dim, length), lambda h: (0, h, 0, 0)),
            pl.BlockSpec((owners, 1, head_dim, tokens), lambda h: (0, h, 0, 0)),
            pl.BlockSpec((1, 1, length), lambda h: (h, 0, 0)),
            pl.BlockSpec((head_dim, 1), lambda h: (0, 0)),
            pl.BlockSpec((length, 1), lambda h: (0, 0)),
            pl.BlockSpec((1, length), lambda h: (0, 0)),
        ],
        out_specs=[
            pl.BlockSpec((3, 1, head_dim, length), lambda h: (0, h, 0, 0)),
            pl.BlockSpec((head_dim, lanes), lambda h: (0, 0)),
        ],
        out_shape=[
            pltpu.HBM((3, local_heads, head_dim, length), BF16),
            pltpu.HBM((head_dim, lanes), F32),
        ],
        scratch_shapes=[
            pltpu.VMEM((head_dim, length), F32),
            pltpu.VMEM((head_dim, length), F32),
        ],
        compiler_params=KERNEL,
        cost_estimate=LIGHT,
    )(
        *in_hbm(
            projected.reshape(3, local_heads, head_dim, length),
            attended_grad.reshape(owners, local_heads, head_dim, tokens),
        ),
        log_total,
        scale_vec.reshape(head_dim, 1),
        segments.reshape(length, 1),
        segments.reshape(1, length),
    )
    return grads.reshape(3 * local_heads * head_dim, length), scale_grad[:, 0]


def dense_grad_kernel(
    core_ref, attended_ref, normed_ref, active_ref, out_bar, up_bar, down_bar,
    own_ref, other_ref, normed_t, active_t,
):
    tile = pl.program_id(0)
    rows, width = 8 * own_ref.shape[3], out_bar.shape[1]

    @pl.when(tile == 0)
    def _():
        normed_t[...] = normed_ref[...].astype(F32).T.astype(BF16)
        active_t[...] = active_ref[...].astype(F32).T.astype(BF16)

    start = pl.multiple_of(tile * rows, rows)
    first_core = core_ref[2] == 0
    lefts = (attended_ref, normed_t, active_t)
    for i, (left, right) in enumerate(zip(lefts, (out_bar, up_bar, down_bar))):
        grad = jnp.dot(left[pl.ds(start, rows), :], right[...], preferred_element_type=F32)
        grad = grad.reshape(2, 2, 2, rows // 8, width)
        one, two = grad[:, :, 0], grad[:, :, 1]
        own_ref[:, :, 0, :, i * width : (i + 1) * width] = jnp.where(
            first_core, one, two
        ).astype(BF16)
        other_ref[:, :, 0, :, i * width : (i + 1) * width] = jnp.where(
            first_core, two, one
        ).astype(BF16)


def dense_grads(attended_t, normed, active, out_bar, up_bar, down_bar):
    width, tokens = attended_t.shape
    own = width // 32
    whole = pl.BlockSpec((tokens, width), lambda i, core: (0, 0))
    rows = pl.BlockSpec((2, 2, 1, own, 3 * width), lambda i, core: (0, 0, i, 0, 0))
    shape = pltpu.HBM((2, 2, 4, own, 3 * width), BF16)
    return pl.pallas_call(
        dense_grad_kernel,
        grid_spec=pltpu.PrefetchScalarGridSpec(
            num_scalar_prefetch=1,
            grid=(4,),
            in_specs=[pl.BlockSpec((width, tokens), lambda i, core: (0, 0))] + [whole] * 5,
            out_specs=[rows, rows],
            scratch_shapes=[pltpu.VMEM((width, tokens), BF16)] * 2,
        ),
        out_shape=[shape, shape],
        compiler_params=KERNEL,
        cost_estimate=LIGHT,
    )(place(), *in_hbm(attended_t, normed, active, out_bar, up_bar, down_bar))


def place():
    head = lax.axis_index("head")
    return jnp.stack([lax.axis_index("blk"), head // 2, head % 2]).astype(jnp.int32)


def assemble_kernel(place_ref, *refs):
    pieces, whole_ref = refs[:10], refs[10]
    half = whole_ref.shape[-1] // 2
    blk, row, core = place_ref[0], place_ref[1], place_ref[2]
    for i in range(2):
        at_core = core if i == 0 else 1 - core
        own, across, beside, one, two = pieces[5 * i : 5 * i + 5]
        whole_ref[0, blk, row, at_core] = own[0]
        whole_ref[0, 1 - blk, row, at_core] = across[0]
        whole_ref[0, blk, 1 - row, at_core] = beside[0]
        whole_ref[0, 1 - blk, 1 - row, at_core, :, :half] = one[0]
        whole_ref[0, 1 - blk, 1 - row, at_core, :, half:] = two[0]


def assemble(pieces):
    batch, own, columns = pieces[0].shape
    specs = [
        pl.BlockSpec((1, own, piece.shape[-1]), lambda i, at: (i, 0, 0))
        for piece in pieces
    ]
    whole = pl.pallas_call(
        assemble_kernel,
        grid_spec=pltpu.PrefetchScalarGridSpec(
            num_scalar_prefetch=1,
            grid=(batch,),
            in_specs=specs,
            out_specs=pl.BlockSpec((1, 2, 2, 2, own, columns), lambda i, at: (i, 0, 0, 0, 0, 0)),
        ),
        out_shape=jax.ShapeDtypeStruct((batch, 2, 2, 2, own, columns), BF16),
        compiler_params=KERNEL,
        cost_estimate=LIGHT,
    )(place(), *pieces)
    return whole.reshape(-1, columns)


def assemble_columns_kernel(place_ref, along_ref, across_ref, whole_ref, *extra_ref):
    blk = place_ref[0]
    columns = whole_ref.shape[-1]
    whole_ref[0, blk] = along_ref[0, :, :columns]
    whole_ref[0, 1 - blk] = across_ref[0, :, :columns]
    for extra in extra_ref:
        extra[0, blk] = along_ref[0, :, columns:]
        extra[0, 1 - blk] = across_ref[0, :, columns:]


def assemble_columns(along, across, columns):
    batch, own, both = along.shape
    rows = pl.BlockSpec((1, own, both), lambda i, at: (i, 0, 0))
    shapes = [(batch, 2, own, columns)]
    if both > columns:
        shapes.append((batch, 2, own, both - columns))
    parts = pl.pallas_call(
        assemble_columns_kernel,
        grid_spec=pltpu.PrefetchScalarGridSpec(
            num_scalar_prefetch=1,
            grid=(batch,),
            in_specs=[rows, rows],
            out_specs=[pl.BlockSpec((1,) + s[1:], lambda i, at: (i, 0, 0, 0)) for s in shapes],
        ),
        out_shape=[pltpu.HBM(s, BF16) for s in shapes],
        compiler_params=KERNEL,
        cost_estimate=LIGHT,
    )(place(), *in_hbm(along, across))
    return [part.reshape(-1, part.shape[-1]) for part in parts]


def assemble_wide_kernel(place_ref, along_ref, across_ref, whole_ref):
    blk = place_ref[0]
    own, columns = along_ref.shape[1], whole_ref.shape[-1]
    for i in range(along_ref.shape[-1] // columns):
        place, part = slice(i * own, (i + 1) * own), slice(i * columns, (i + 1) * columns)
        whole_ref[0, blk, place, :] = along_ref[0, :, part]
        whole_ref[0, 1 - blk, place, :] = across_ref[0, :, part]


def assemble_wide(along, across, columns):
    batch, own, wide = along.shape
    rows = own * (wide // columns)
    piece = pl.BlockSpec((1, own, wide), lambda i, at: (i, 0, 0))
    whole = pl.pallas_call(
        assemble_wide_kernel,
        grid_spec=pltpu.PrefetchScalarGridSpec(
            num_scalar_prefetch=1,
            grid=(batch,),
            in_specs=[piece, piece],
            out_specs=pl.BlockSpec((1, 2, rows, columns), lambda i, at: (i, 0, 0, 0)),
        ),
        out_shape=pltpu.HBM((batch, 2, rows, columns), BF16),
        compiler_params=KERNEL,
        cost_estimate=LIGHT,
    )(place(), *in_hbm(along, across))
    return whole.reshape(-1, columns)


def project_kernel(with_norm, place_ref, *refs):
    pieces, (gain_ref, weight_ref, normed_ref, projected_ref) = refs[:4], refs[4:]
    head = place_ref[1] * 2 + place_ref[2]
    rows = pieces[0].shape[0]
    for i, piece in enumerate(pieces):
        value = piece[...]
        if with_norm:
            stream = value.astype(F32)
            factor = lax.rsqrt(jnp.mean(stream * stream, axis=-1, keepdims=True) + EPSILON)
            value = (stream * factor * gain_ref[...]).astype(BF16)
        normed_ref[pl.ds(pl.multiple_of((head ^ i) * rows, rows), rows), :] = value
    projected = jnp.dot(normed_ref[...], weight_ref[...], preferred_element_type=F32)
    projected_ref[...] = projected.T


def project(pieces, gain, weight, with_norm, token_rows):
    tokens, width = pieces[0].shape
    length, columns = 4 * tokens, weight.shape[1]
    groups = tokens // token_rows
    piece = pl.BlockSpec((token_rows, width), lambda g, at: (g, 0))
    return pl.pallas_call(
        functools.partial(project_kernel, with_norm),
        grid_spec=pltpu.PrefetchScalarGridSpec(
            num_scalar_prefetch=1,
            grid=(groups,),
            in_specs=[piece] * 4
            + [
                pl.BlockSpec((1, width), lambda g, at: (0, 0)),
                pl.BlockSpec((width, columns), lambda g, at: (0, 0)),
            ],
            out_specs=[
                pl.BlockSpec((4 * token_rows, width), lambda g, at: (g, 0)),
                pl.BlockSpec((columns, 4 * token_rows), lambda g, at: (0, g)),
            ],
        ),
        out_shape=[
            pltpu.HBM((length, width), BF16),
            pltpu.HBM((columns, length), F32),
        ],
        compiler_params=KERNEL,
        cost_estimate=LIGHT,
    )(place(), *in_hbm(*pieces), gain.reshape(1, width), *in_hbm(weight))


def project_back_kernel(
    place_ref, bars_ref, weight_ref, normed_ref, own_ref, other_ref, grad_ref, bars_t
):
    @pl.when(pl.program_id(0) == 0)
    def _():
        bars_t[...] = bars_ref[...].astype(F32).T.astype(BF16)

    upper = lax.dot_general(bars_t[...], weight_ref[...], NT, preferred_element_type=F32)
    upper = upper.reshape(2, 2, 2, -1, upper.shape[-1])
    first_core = place_ref[2] == 0
    one, two = upper[:, :, 0], upper[:, :, 1]
    own_ref[...] = jnp.where(first_core, one, two)
    other_ref[...] = jnp.where(first_core, two, one).astype(BF16)
    grad = lax.dot_general(normed_ref[...], bars_t[...], TN, preferred_element_type=F32)
    grad_ref[...] = grad.astype(BF16)


def project_back(bars, weight, normed, token_rows):
    columns, length = bars.shape
    width = weight.shape[0]
    tile = width // 2
    quarter = pl.BlockSpec((2, 2, token_rows, tile), lambda i, at: (0, 0, 0, i))
    return pl.pallas_call(
        project_back_kernel,
        grid_spec=pltpu.PrefetchScalarGridSpec(
            num_scalar_prefetch=1,
            grid=(2,),
            in_specs=[
                pl.BlockSpec((columns, length), lambda i, at: (0, 0)),
                pl.BlockSpec((tile, columns), lambda i, at: (i, 0)),
                pl.BlockSpec((length, tile), lambda i, at: (0, i)),
            ],
            out_specs=[quarter, quarter, pl.BlockSpec((tile, columns), lambda i, at: (i, 0))],
            scratch_shapes=[pltpu.VMEM((length, columns), BF16)],
        ),
        out_shape=[
            pltpu.HBM((2, 2, token_rows, width), F32),
            pltpu.HBM((2, 2, token_rows, width), BF16),
            pltpu.HBM((width, columns), BF16),
        ],
        compiler_params=KERNEL,
        cost_estimate=LIGHT,
    )(place(), *in_hbm(bars, weight, normed))


def rows_back_kernel(place_ref, bars_ref, weight_ref, own_ref, other_ref, bars_t):
    @pl.when(pl.program_id(0) == 0)
    def _():
        bars_t[...] = bars_ref[...].astype(F32).T.astype(BF16)

    upper = lax.dot_general(bars_t[...], weight_ref[...], NT, preferred_element_type=F32)
    upper = upper.reshape(2, 2, 2, -1, upper.shape[-1])
    first_core = place_ref[2] == 0
    one, two = upper[:, :, 0], upper[:, :, 1]
    own_ref[...] = jnp.where(first_core, one, two)
    other_ref[...] = jnp.where(first_core, two, one).astype(BF16)


def rows_back(bars, weight, token_rows):
    columns, length = bars.shape
    width = weight.shape[0]
    tile = width // 2
    quarter = pl.BlockSpec((2, 2, token_rows, tile), lambda i, at: (0, 0, 0, i))
    return pl.pallas_call(
        rows_back_kernel,
        grid_spec=pltpu.PrefetchScalarGridSpec(
            num_scalar_prefetch=1,
            grid=(2,),
            in_specs=[
                pl.BlockSpec((columns, length), lambda i, at: (0, 0)),
                pl.BlockSpec((tile, columns), lambda i, at: (i, 0)),
            ],
            out_specs=[quarter, quarter],
            scratch_shapes=[pltpu.VMEM((length, columns), BF16)],
        ),
        out_shape=[
            pltpu.HBM((2, 2, token_rows, width), F32),
            pltpu.HBM((2, 2, token_rows, width), BF16),
        ],
        compiler_params=KERNEL,
        cost_estimate=LIGHT,
    )(place(), *in_hbm(bars, weight))


def weight_back_kernel(bars_ref, normed_ref, grad_ref):
    grad = jnp.dot(bars_ref[...], normed_ref[...], preferred_element_type=F32)
    grad_ref[...] = grad.T.astype(BF16)


def weight_back(bars, normed):
    columns, length = bars.shape
    width = normed.shape[1]
    tile = width // 5
    return pl.pallas_call(
        weight_back_kernel,
        grid=(5,),
        in_specs=[
            pl.BlockSpec((columns, length), lambda i: (0, 0)),
            pl.BlockSpec((length, tile), lambda i: (0, i)),
        ],
        out_specs=pl.BlockSpec((tile, columns), lambda i: (i, 0)),
        out_shape=pltpu.HBM((width, columns), BF16),
        compiler_params=KERNEL,
        cost_estimate=LIGHT,
    )(*in_hbm(bars, normed))


def tied(*arrays):
    return lax.optimization_barrier(arrays)


def swapped(array, axis, mask):
    size = lax.axis_size(axis)
    return lax.ppermute(array, axis, [(i, i ^ mask) for i in range(size)])


def pick(array, index, axis=0):
    return lax.dynamic_index_in_dim(array, index, axis, keepdims=False)


def swap_halves(array):
    me = lax.axis_index("blk")
    got = swapped(pick(array, 1 - me), "blk", 1)
    kept = pick(array, me)
    return jnp.stack([jnp.where(me == 0, kept, got), jnp.where(me == 0, got, kept)])


def scatter_row(halves):
    row = lax.axis_index("head") // 2
    got = swapped(pick(halves, 1 - row, 1).astype(BF16), "head", 2).astype(F32)
    return (pick(halves, row, 1) + got).reshape(-1, halves.shape[-1])


def over_head(parts):
    return lax.all_to_all(parts, "head", split_axis=0, concat_axis=0, tiled=True)


def qkv_columns(rows, extra):
    own, width = rows.shape
    part = width // 3 // 4
    sent = rows.reshape(own, 3, 4, part).transpose(2, 0, 1, 3).reshape(4, own, 3 * part)
    if extra is not None:
        sent = jnp.concatenate([sent, jnp.broadcast_to(extra[None], (4,) + extra.shape)], axis=2)
    return over_head(sent)


def along_batch(piece):
    return lax.all_gather(piece, "batch", axis=0, tiled=False)


def other_core(array):
    return swapped(array, "head", 1)


def to_beside(across):
    return swapped(across[..., : across.shape[-1] // 2], "head", 2)


def to_across(beside):
    return swapped(beside[..., beside.shape[-1] // 2 :], "blk", 1)


def over_batch(parts):
    return lax.psum_scatter(parts.astype(BF16), "batch", scatter_dimension=0, tiled=False)


def across_sum(halves):
    blk = lax.axis_index("blk")
    got = swapped(pick(halves, 1 - blk), "blk", 1).astype(F32)
    return (pick(halves, blk).astype(F32) + got).astype(BF16)


def columns_to_rows(moved):
    rows = moved.shape[1]
    return moved.reshape(4, rows, 3, -1).transpose(1, 2, 0, 3).reshape(rows, -1).astype(F32)


def quarter(parts, blk, row):
    one, two = (pick(pick(part, blk), row).astype(F32) for part in parts)
    return one + two


def diagonal_rows(parts):
    blk, row = place()[:2]
    rows = quarter(parts, 1 - blk, 1 - row).astype(BF16)
    half = rows.shape[-1] // 2
    return rows[..., :half], rows[..., half:]


def neighbour_rows(parts, one, two):
    blk, row = place()[:2]
    half = one.shape[-1]
    across, beside = quarter(parts, 1 - blk, row), quarter(parts, blk, 1 - row)
    across = jnp.concatenate([across[..., :half], across[..., half:] + two.astype(F32)], axis=-1)
    beside = jnp.concatenate([beside[..., :half] + one.astype(F32), beside[..., half:]], axis=-1)
    return across.astype(BF16), beside.astype(BF16)


def sent_beside_and_across(across, beside):
    return swapped(across, "blk", 1), swapped(beside, "head", 2)


def heads_grad(weight, out_bar):
    return dot_cols(weight, out_bar).astype(BF16).reshape(4, -1, out_bar.shape[0])


def own_sum(parts, across, beside):
    blk, row = place()[:2]
    return quarter(parts, blk, row) + across.astype(F32) + beside.astype(F32)


def sum_over(array, *hops):
    for axis, mask in hops:
        array = array + swapped(array, axis, mask)
    return array


def gain_back(weight, weight_grad, gain):
    return jnp.sum(weight.astype(F32) * weight_grad, axis=-1) / gain.astype(F32)


def lower_of(upper, stream, factor, gain):
    return norm_back(upper, stream, factor, gain)[0]


def spread_device(
    tokens,
    segments,
    qkv_weight,
    out_weight,
    up_weight,
    down_weight,
    attn_gain,
    mlp_gain,
    scale_param,
    cotangent,
):
    layers, head_dim = scale_param.shape
    _, token_rows, width = tokens.shape
    scale_vecs = SCALE_BASE / math.sqrt(head_dim) * jax.nn.softplus(scale_param)
    segments = pick(segments, lax.axis_index("blk"))
    own_gains = jnp.concatenate([attn_gain, mlp_gain], axis=0)

    part3 = 3 * width // 4
    dense_own = [
        jnp.concatenate([out_weight[i], up_weight[i], down_weight[i]], axis=1) for i in (0, 1)
    ]

    first = swap_halves(tokens).reshape(-1, width)
    columns = qkv_columns(qkv_weight[0], own_gains.T)
    columns, first = tied(columns.reshape(-1, columns.shape[-1]), first)
    stream = first.astype(F32)
    along = along_batch(columns)
    far, near = swapped(first, "head", 2), other_core(first)
    both = other_core(far)
    upper = swap_halves(cotangent)
    along, near, far, both, dense_near, upper = tied(
        along, near, far, both, dense_own[0], upper
    )
    token_pieces = (first, near, far, both)
    dense_near = along_batch(dense_near)
    qkv_across = swapped(along, "blk", 1)
    next_columns = jnp.concatenate(list(qkv_columns(qkv_weight[1], None)), axis=1)
    qkv_across, dense_near, next_columns = tied(qkv_across, dense_near, next_columns)
    across, beside = swapped(dense_near, "blk", 1), swapped(dense_near, "head", 2)
    next_both = along_batch(jnp.stack([next_columns, dense_own[1]]))
    weight, gains = assemble_columns(along, qkv_across, part3)
    qkvs = [weight]
    gains = gains.T.astype(F32)

    kept, denses = [], []
    for layer in range(layers):
        normed, factor_one = normalize(stream, gains[layer])
        if layer == 1:
            normed = normed.astype(BF16)
            far, near = swapped(normed, "head", 2), other_core(normed)
            far, next_across, dense_next = tied(far, next_across, dense_next)
            across, beside = swapped(dense_next, "blk", 1), swapped(dense_next, "head", 2)
            token_pieces = (normed, near, far, other_core(far))
            qkvs.append(assemble_wide(next_along, next_across, part3))
        normed_all, projected = project(
            token_pieces, gains[layer], qkvs[layer], layer == 0, token_rows
        )
        attended, log_total = attend_rows(
            projected, scale_vecs[layer], segments, 4, token_rows
        )
        attended, across, beside = tied(attended, across, beside)
        one, two = to_beside(across), to_across(beside)
        if layer == 0:
            two, next_both = tied(two, next_both)
            next_along, dense_next = next_both[:, 0], next_both[:, 1]
            next_across = swapped(next_along, "blk", 1)
            attended_t, one, two = tied(over_head(attended), one, two)
        else:
            dense_near = dense_next
            attended_t, one, two = tied(over_head(attended), one, two)
        pieces = (dense_near, across, beside, one, two)
        pieces += tuple(other_core(piece) for piece in pieces)
        attended_t = attended_t.reshape(width, -1)
        denses.append(assemble(pieces))
        dense = denses[layer]
        out_w, up_w, down_w = dense[:, :width], dense[:, width:-width], dense[:, -width:]
        middle = stream + dot_rows(attended_t, out_w)
        normed_two, factor_two = normalize(middle, gains[layers + layer])
        normed_two = normed_two.astype(BF16)
        hidden = dot(normed_two, up_w)
        active = (hidden * jax.nn.sigmoid(hidden)).astype(BF16)
        kept.append(
            (
                stream, factor_one, normed_all, projected, log_total, attended_t, middle,
                factor_two, normed_two, hidden, active,
            )
        )
        stream = middle + dot(active, down_w)
    layer_out = swap_halves(stream.astype(BF16).reshape(tokens.shape))
    upper = upper.reshape(-1, width).astype(F32)

    scale_grads = [None] * layers
    for layer in reversed(range(layers)):
        (
            stream, factor_one, normed_all, projected, log_total, attended_t, middle,
            factor_two, normed_two, hidden, active,
        ) = kept[layer]
        qkv, dense = qkvs[layer], denses[layer]
        out_w, up_w, down_w = dense[:, :width], dense[:, width:-width], dense[:, -width:]
        down_bar = upper.astype(BF16)
        gate = jax.nn.sigmoid(hidden)
        up_bar = (
            dot_cols(down_bar, down_w) * gate * (1.0 + hidden * (1.0 - gate))
        ).astype(BF16)
        middle_grad = upper + lower_of(
            dot_cols(up_bar, up_w), middle, factor_two, gains[layers + layer]
        )
        out_bar = middle_grad.astype(BF16)
        if layer == 0:
            attended_grad = over_head(heads_grad(out_w, out_bar))
            grads, others = dense_grads(attended_t, normed_two, active, out_bar, up_bar, down_bar)
            attended_grad, others, z_sum, across, beside = tied(
                attended_grad, others, z_sum, across, beside
            )
            others = other_core(others)
            attended_grad, summed = tied(attended_grad, own_sum(cored, across, beside))
            summed = over_batch(summed)
            z_across = across_sum(z_sum)
        else:
            attended_grad = over_head(heads_grad(out_w, out_bar))
            grads, others = dense_grads(attended_t, normed_two, active, out_bar, up_bar, down_bar)
            attended_grad, others, layer_out = tied(attended_grad, others, layer_out)
            others = other_core(others)
        bars, scale_grads[layer] = attend_back_rows(
            projected, attended_grad, log_total, scale_vecs[layer], segments, token_rows
        )
        if layer == 0:
            bars, others, z_across = tied(bars, others, z_across)
            moved = over_head(z_across.reshape(4, -1, z_across.shape[-1]))
            qkv_grad = weight_back(bars, normed_all)
            bars, qkv_grad, moved = tied(bars, qkv_grad, moved)
            z_sum = over_batch(qkv_grad.reshape(4, 2, -1, qkv_grad.shape[-1]))
            cored = (grads, others)
            bars, rows = tied(bars, diagonal_rows(cored))
            diagonal = sent_beside_and_across(*rows)
            halves, to_core = rows_back(bars, qkv, token_rows)
            halves, to_core, diagonal, summed = tied(halves, to_core, diagonal, summed)
            halves, to_core, rows = tied(halves, to_core, neighbour_rows(cored, *diagonal))
            sent = sent_beside_and_across(*rows)
            halves = halves + other_core(to_core).astype(F32)
            scale_sum = sum_over(jnp.stack(scale_grads), ("head", 1), ("batch", 1), ("batch", 2))
            halves, sent, z_sum, scale_sum = tied(halves, sent, z_sum, scale_sum)
            halves, own = tied(halves, own_sum(cored, *sent))
            dense_first = over_batch(own)
            normed_grad = scatter_row(halves)
            z_across, dense_first = tied(across_sum(z_sum), dense_first)
            z_across = over_head(z_across.reshape(4, -1, z_across.shape[-1]))
            dense_grad = [dense_first, summed]
            qkv_grads = [columns_to_rows(z_across), columns_to_rows(moved)]
        else:
            bars, others = tied(bars, others)
            cored = (grads, others)
            bars, rows = tied(bars, diagonal_rows(cored))
            diagonal = sent_beside_and_across(*rows)
            halves, to_core, qkv_grad = project_back(bars, qkv, normed_all, token_rows)
            z_sum = over_batch(qkv_grad.reshape(4, 2, -1, qkv_grad.shape[-1]))
            to_core, halves, diagonal = tied(to_core, halves, diagonal)
            to_core, rows = tied(to_core, neighbour_rows(cored, *diagonal))
            across = swapped(rows[0], "blk", 1)
            halves = halves + other_core(to_core).astype(F32)
            normed_grad = scatter_row(halves)
            normed_grad, beside = tied(normed_grad, rows[1])
            beside = swapped(beside, "head", 2)
        upper = middle_grad + lower_of(normed_grad, stream, factor_one, gains[layer])
    input_grad = swap_halves(upper.astype(BF16).reshape(tokens.shape)).astype(F32)
    scale_total = sum_over(scale_sum, ("head", 2), ("blk", 1))
    scale_grad = scale_total * (SCALE_BASE / math.sqrt(head_dim)) * jax.nn.sigmoid(scale_param)
    dense_all = jnp.stack([part.astype(F32) for part in dense_grad])
    qkv_all = jnp.stack(qkv_grads)
    up_all = dense_all[:, :, width:-width]
    return (
        layer_out,
        input_grad,
        qkv_all,
        dense_all[:, :, :width],
        up_all,
        dense_all[:, :, -width:],
        gain_back(qkv_weight, qkv_all, attn_gain),
        gain_back(up_weight, up_all, mlp_gain),
        scale_grad,
    )


def per_device(*args):
    tokens, segments = args[0], args[1]
    sizes = tuple(lax.axis_size(axis) for axis in ALL)
    heads = tokens.shape[2] // args[8].shape[1]
    spread = (
        sizes == (4, 2, 4)
        and tokens.shape[0] == 2
        and args[2].shape[0] == 2
        and tokens.shape[1] % 128 == 0
        and Q_ROWS % tokens.shape[1] == 0
        and segments.shape[1] <= WINDOW
        and segments.shape[1] % Q_ROWS == 0
        and heads % 4 == 0
        and tokens.shape[2] % 256 == 0
    )
    return spread_device(*args) if spread else general_device(*args)


def solution(mesh):
    rows = P(None, ALL, None)
    by_token = P("batch", ("blk", "head"), None)
    return jax.shard_map(
        per_device,
        mesh=mesh,
        in_specs=(
            by_token, P("batch", None), rows, rows, rows, rows, P(None, ALL), P(None, ALL), P(),
            by_token,
        ),
        out_specs=(
            by_token, by_token, rows, rows, rows, rows, P(None, ALL), P(None, ALL), P(),
        ),
        check_vma=False,
    )
```

```python
import functools
import math

import jax
import jax.numpy as jnp
from jax import lax
from jax.experimental import pallas as pl
from jax.experimental.pallas import tpu as pltpu
from jax.sharding import PartitionSpec as P

WINDOW = 1024
EPSILON = 1e-06
SCALE_BASE = 1.4426950408889634
MASKED_SCORE = -1e30

ALL = ("batch", "blk", "head")
REST = ("batch", "blk")
F32 = jnp.float32
BF16 = jnp.bfloat16


def shifted(block, axis, distance):
    devices = range(lax.axis_size(axis))
    route = [(i - distance, i) for i in devices if i - distance in devices]
    return lax.ppermute(block, axis, route)


NT = (((1,), (1,)), ((), ()))
TN = (((0,), (0,)), ((), ()))


def dot(left, right):
    return jnp.dot(left, right, preferred_element_type=F32)


def dot_rows(left, right):
    return lax.dot_general(left, right, (((0,), (0,)), ((), ())), preferred_element_type=F32)


def dot_cols(left, right):
    return lax.dot_general(left, right, (((1,), (1,)), ((), ())), preferred_element_type=F32)


def normalize(stream, gain):
    factor = lax.rsqrt(jnp.mean(stream * stream, axis=-1, keepdims=True) + EPSILON)
    return stream * factor * gain, factor


def norm_back(upper, stream, factor, gain):
    inner = upper * gain
    gain_grad = jnp.sum(upper * stream * factor, axis=0)
    lower = factor * inner - stream * factor * factor * factor * jnp.mean(
        inner * stream, axis=-1, keepdims=True
    )
    return lower, gain_grad


class Plan:
    def __init__(self, tokens):
        self.seqs, self.rows, self.width = tokens.shape
        self.heads = lax.axis_size("head")
        self.blks = lax.axis_size("blk")
        self.block = self.rows * self.heads
        self.whole = self.seqs % self.blks == 0
        if self.whole:
            self.groups, self.own_seqs = self.blks, self.seqs // self.blks
            self.reach = 0
        else:
            self.groups, self.own_seqs = 1, self.seqs
            self.reach = min((WINDOW - 1) // self.block + 1, self.blks - 1)
        self.length = self.groups * self.block
        self.tokens = self.seqs * self.rows


def to_plan(plan, array):
    if plan.whole and plan.blks > 1:
        array = lax.all_to_all(array, "blk", split_axis=0, concat_axis=0, tiled=True)
    return array.reshape(plan.tokens, plan.width)


def from_plan(plan, flat):
    array = flat.reshape(plan.seqs, plan.rows, plan.width)
    if plan.whole and plan.blks > 1:
        array = lax.all_to_all(array, "blk", split_axis=0, concat_axis=0, tiled=True)
    return array


def in_sequence(plan, by_head, width):
    parts = by_head.reshape(plan.heads, plan.groups, plan.own_seqs, plan.rows, width)
    return parts.transpose(2, 1, 0, 3, 4).reshape(-1, width)


def by_owner(plan, rows, width):
    parts = rows.reshape(plan.own_seqs, plan.groups, plan.heads, plan.rows, width)
    return parts.transpose(2, 1, 0, 3, 4).reshape(plan.heads, plan.tokens, width)


def gather_tokens(plan, rows):
    moved = lax.all_gather(rows, "head", axis=0, tiled=False)
    return in_sequence(plan, moved, rows.shape[-1])


def scatter_tokens(plan, rows):
    width = rows.shape[-1]
    return lax.psum_scatter(
        by_owner(plan, rows.astype(BF16), width), "head", scatter_dimension=0, tiled=False
    ).astype(F32)


def heads_to_tokens(plan, rows):
    part = rows.shape[-1]
    moved = lax.all_to_all(
        by_owner(plan, rows, part), "head", split_axis=0, concat_axis=0, tiled=True
    )
    return moved.transpose(1, 0, 2).reshape(plan.tokens, plan.heads * part)


def tokens_to_heads(plan, rows):
    part = rows.shape[-1] // plan.heads
    sent = rows.reshape(plan.tokens, plan.heads, part).transpose(1, 0, 2)
    moved = lax.all_to_all(sent, "head", split_axis=0, concat_axis=0, tiled=True)
    return in_sequence(plan, moved, part)


def gather_qkv(rows):
    own, width = rows.shape
    heads = lax.axis_size("head")
    part = width // 3 // heads
    sent = rows.reshape(own, 3, heads, part).transpose(2, 0, 1, 3).reshape(heads, own, 3 * part)
    moved = lax.all_to_all(sent, "head", split_axis=0, concat_axis=0, tiled=True)
    full = lax.all_gather(moved, REST, axis=0, tiled=True)
    return full.reshape(-1, 3 * part)


def scatter_qkv(grad):
    heads = lax.axis_size("head")
    part = grad.shape[1] // 3
    summed = lax.psum_scatter(grad.astype(BF16), REST, scatter_dimension=0, tiled=True)
    own = summed.shape[0] // heads
    moved = lax.all_to_all(
        summed.reshape(heads, own, 3 * part), "head", split_axis=0, concat_axis=0, tiled=True
    )
    return (
        moved.reshape(heads, own, 3, part)
        .transpose(1, 2, 0, 3)
        .reshape(own, 3 * heads * part)
        .astype(F32)
    )


def window_mask(plan, segments, block_index):
    key_count = plan.length + plan.reach * plan.block
    if plan.whole:
        query_segs, key_segs = segments, segments
    else:
        leading = jnp.full((plan.own_seqs, plan.reach * plan.block), -1, jnp.int32)
        padded = jnp.concatenate([leading, segments], axis=1)
        start = block_index * plan.block
        query_segs = lax.dynamic_slice_in_dim(segments, start, plan.block, 1)
        key_segs = lax.dynamic_slice_in_dim(padded, start, key_count, 1)
    query_place = jnp.arange(plan.length, dtype=jnp.int32)[:, None] + plan.reach * plan.block
    key_place = jnp.arange(key_count, dtype=jnp.int32)[None, :]
    near = (key_place <= query_place) & (query_place - key_place < WINDOW)
    return (key_segs[:, None, :] == query_segs[:, :, None]) & near[None]


def with_earlier(plan, own):
    arrived = [own]
    for _ in range(plan.reach):
        arrived.append(shifted(arrived[-1], "blk", 1))
    return jnp.concatenate(arrived[::-1], axis=1) if plan.reach else own


def to_earlier(plan, grads):
    if not plan.reach:
        return grads
    block = plan.block
    total = grads[:, :block]
    for step in range(1, plan.reach + 1):
        total = (
            shifted(total.astype(BF16), "blk", -1).astype(F32)
            + grads[:, step * block : (step + 1) * block]
        )
    return total


def scores_of(queries, keys, allowed):
    scores = jnp.einsum("sqhd,skhd->shqk", queries, keys, preferred_element_type=F32)
    return jnp.where(allowed[:, None], scores, MASKED_SCORE)


def attend(queries, keys, values, allowed):
    scores = scores_of(queries, keys, allowed)
    top_score = jnp.max(scores, axis=-1, keepdims=True)
    exp_terms = jnp.exp(scores - top_score)
    totals = jnp.sum(exp_terms, axis=-1, keepdims=True)
    probs_low = (exp_terms / totals).astype(BF16)
    attended = jnp.einsum("shqk,skhd->sqhd", probs_low, values, preferred_element_type=F32)
    return attended, top_score + jnp.log(totals)


def attend_back(queries, keys, values, allowed, log_total, attended_grad):
    probs = jnp.exp(scores_of(queries, keys, allowed) - log_total)
    probs_low = probs.astype(BF16)
    values_grad = jnp.einsum(
        "shqk,sqhd->skhd", probs_low, attended_grad, preferred_element_type=F32
    )
    probs_grad = jnp.einsum("sqhd,skhd->shqk", attended_grad, values, preferred_element_type=F32)
    row_dot = jnp.sum(probs_grad * probs, axis=-1, keepdims=True)
    scores_low = (probs * (probs_grad - row_dot)).astype(BF16)
    queries_grad = jnp.einsum("shqk,skhd->sqhd", scores_low, keys, preferred_element_type=F32)
    keys_grad = jnp.einsum("shqk,sqhd->skhd", scores_low, queries, preferred_element_type=F32)
    return queries_grad, keys_grad, values_grad


def forward(plan, stream, qkv, dense, gains, scale_vec, allowed):
    width = plan.width
    head_dim = scale_vec.shape[0]
    part = qkv.shape[1] // 3
    local_heads = part // head_dim
    split = (plan.own_seqs, plan.length, local_heads, head_dim)
    out_w, up_w, down_w = dense[:, :width], dense[:, width:-width], dense[:, -width:]
    normed, factor_one = normalize(stream, gains[0])
    normed_all = gather_tokens(plan, normed.astype(BF16))
    projected = dot(normed_all, qkv)
    query_pre = projected[:, :part].reshape(split)
    queries = (query_pre * scale_vec).astype(BF16)
    keys = with_earlier(plan, projected[:, part : 2 * part].astype(BF16).reshape(split))
    values = with_earlier(plan, projected[:, 2 * part :].astype(BF16).reshape(split))
    attended_part, log_total = attend(queries, keys, values, allowed)
    attended = heads_to_tokens(plan, attended_part.astype(BF16).reshape(-1, part))
    middle = stream + dot(attended, out_w)
    normed_two, factor_two = normalize(middle, gains[1])
    normed_two = normed_two.astype(BF16)
    hidden = dot(normed_two, up_w)
    active = (hidden * jax.nn.sigmoid(hidden)).astype(BF16)
    result = middle + dot(active, down_w)
    kept = (
        stream, factor_one, normed_all, query_pre, queries, keys, values, log_total,
        attended, middle, factor_two, normed_two, hidden, active,
    )
    return result, kept


def backward(plan, upper, kept, qkv, dense, gains, scale_vec, allowed):
    (
        stream, factor_one, normed_all, query_pre, queries, keys, values, log_total,
        attended, middle, factor_two, normed_two, hidden, active,
    ) = kept
    width = plan.width
    head_dim = scale_vec.shape[0]
    part = qkv.shape[1] // 3
    out_w, up_w, down_w = dense[:, :width], dense[:, width:-width], dense[:, -width:]
    upper_low = upper.astype(BF16)
    down_grad = dot_rows(active, upper_low)
    active_grad = dot_cols(upper_low, down_w)
    gate = jax.nn.sigmoid(hidden)
    hidden_low = (active_grad * gate * (1.0 + hidden * (1.0 - gate))).astype(BF16)
    up_grad = dot_rows(normed_two, hidden_low)
    extra_two, mlp_gain_grad = norm_back(dot_cols(hidden_low, up_w), middle, factor_two, gains[1])
    middle_grad = upper + extra_two
    middle_low = middle_grad.astype(BF16)
    out_grad = dot_rows(attended, middle_low)
    dense_grad = jnp.concatenate([out_grad, up_grad, down_grad], axis=1).astype(BF16)
    dense_own = lax.psum_scatter(dense_grad, ALL, scatter_dimension=0, tiled=True)
    attended_grad = tokens_to_heads(plan, dot_cols(middle_low, out_w).astype(BF16))
    queries_grad, keys_grad, values_grad = attend_back(
        queries, keys, values, allowed, log_total, attended_grad.reshape(queries.shape)
    )
    query_bar = queries_grad.astype(BF16).astype(F32)
    scale_vec_grad = jnp.sum((query_bar * query_pre).reshape(-1, head_dim), axis=0)
    query_low = (query_bar * scale_vec).astype(BF16).reshape(-1, part)
    keys_low = to_earlier(plan, keys_grad).astype(BF16).reshape(-1, part)
    values_low = to_earlier(plan, values_grad).astype(BF16).reshape(-1, part)
    projected_low = jnp.concatenate([query_low, keys_low, values_low], axis=1)
    normed_grad = scatter_tokens(plan, dot_cols(projected_low, qkv))
    qkv_own = scatter_qkv(dot_rows(normed_all, projected_low))
    extra_one, attn_gain_grad = norm_back(normed_grad, stream, factor_one, gains[0])
    lower = middle_grad + extra_one
    return lower, qkv_own, dense_own, (attn_gain_grad, mlp_gain_grad), scale_vec_grad


def general_device(
    tokens,
    segments,
    qkv_weight,
    out_weight,
    up_weight,
    down_weight,
    attn_gain,
    mlp_gain,
    scale_param,
    cotangent,
):
    plan = Plan(tokens)
    layers, head_dim = scale_param.shape
    block_index = lax.axis_index("blk")
    scale_vecs = SCALE_BASE / math.sqrt(head_dim) * jax.nn.softplus(scale_param)
    own_gains = jnp.concatenate([attn_gain, mlp_gain], axis=0)
    gains = (
        lax.all_gather(own_gains.reshape(1, -1), ALL, axis=0, tiled=True)
        .reshape(-1, 2 * layers, attn_gain.shape[1])
        .transpose(1, 0, 2)
        .reshape(2 * layers, plan.width)
        .astype(F32)
    )
    if plan.whole:
        segments = lax.dynamic_slice_in_dim(
            segments, block_index * plan.own_seqs, plan.own_seqs, 0
        )
    allowed = window_mask(plan, segments, block_index)
    stream = to_plan(plan, tokens).astype(F32)
    qkvs, denses, kept = [], [], []
    for layer in range(layers):
        qkvs.append(gather_qkv(qkv_weight[layer]))
        own = jnp.concatenate([out_weight[layer], up_weight[layer], down_weight[layer]], axis=1)
        denses.append(lax.all_gather(own, ALL, axis=0, tiled=True))
        layer_gains = (gains[layer], gains[layers + layer])
        stream, saved = forward(
            plan, stream, qkvs[layer], denses[layer], layer_gains, scale_vecs[layer], allowed
        )
        kept.append(saved)
    layer_out = from_plan(plan, stream.astype(BF16))
    upper = to_plan(plan, cotangent).astype(F32)
    qkv_grads, dense_grads = [None] * layers, [None] * layers
    gain_grads, scale_grads = [None] * layers, [None] * layers
    for layer in reversed(range(layers)):
        layer_gains = (gains[layer], gains[layers + layer])
        upper, qkv_grads[layer], dense_grads[layer], gain_grads[layer], scale_grads[layer] = (
            backward(
                plan, upper, kept[layer], qkvs[layer], denses[layer], layer_gains,
                scale_vecs[layer], allowed,
            )
        )
    input_grad = from_plan(plan, upper.astype(BF16)).astype(F32)
    small = jnp.concatenate(
        [g[0] for g in gain_grads] + [g[1] for g in gain_grads] + scale_grads, axis=0
    )
    total = lax.psum(small, ALL)
    gain_total = total[: 2 * layers * plan.width].reshape(2 * layers, plan.width)
    owner = lax.axis_index(ALL)
    gain_rows = attn_gain.shape[1]
    own_total = lax.dynamic_slice_in_dim(gain_total, owner * gain_rows, gain_rows, 1)
    scale_total = total[2 * layers * plan.width :].reshape(layers, head_dim)
    scale_grad = scale_total * (SCALE_BASE / math.sqrt(head_dim)) * jax.nn.sigmoid(scale_param)
    dense_all = jnp.stack(dense_grads).astype(F32)
    width = plan.width
    return (
        layer_out,
        input_grad,
        jnp.stack(qkv_grads),
        dense_all[:, :, :width],
        dense_all[:, :, width:-width],
        dense_all[:, :, -width:],
        own_total[:layers],
        own_total[layers:],
        scale_grad,
    )


Q_ROWS = 256
KERNEL = pltpu.CompilerParams(vmem_limit_bytes=32 * 1024 * 1024)
LIGHT = pl.CostEstimate(flops=1 << 20, bytes_accessed=1 << 20, transcendentals=0)


def in_hbm(*arrays):
    return [pltpu.with_memory_space_constraint(array, pltpu.HBM) for array in arrays]


def allowed_keys(col, row, first):
    count = first + row.shape[1]
    key_place = lax.broadcasted_iota(jnp.int32, (count, row.shape[1]), 0)
    query_place = lax.broadcasted_iota(jnp.int32, (count, row.shape[1]), 1) + first
    return (col[:count] == row) & (key_place <= query_place)


def token_places(length, heads, token_rows):
    for first in range(0, length, Q_ROWS):
        parts = []
        for start in range(0, Q_ROWS, token_rows):
            place = (first + start) // token_rows
            parts.append((start, place % heads, place // heads * token_rows))
        yield first, parts


def attend_kernel(token_rows, proj_ref, scale_ref, col_ref, row_ref, out_ref, lse_ref):
    length = proj_ref.shape[-1]
    queries = (proj_ref[0, 0] * scale_ref[...]).astype(BF16)
    keys = proj_ref[1, 0].T.astype(BF16)
    values = proj_ref[2, 0].astype(BF16)
    for first, parts in token_places(length, out_ref.shape[0], token_rows):
        end = first + Q_ROWS
        scores = jnp.dot(keys[:end], queries[:, first:end], preferred_element_type=F32)
        allowed = allowed_keys(col_ref[...], row_ref[:, first:end], first)
        scores = jnp.where(allowed, scores, MASKED_SCORE)
        top = jnp.max(scores, axis=0, keepdims=True)
        terms = jnp.exp(scores - top)
        total = jnp.sum(terms, axis=0, keepdims=True)
        probs = (terms * (1.0 / total)).astype(BF16)
        attended = jnp.dot(values[:, :end], probs, preferred_element_type=F32).astype(BF16)
        lse_ref[0, :, first:end] = top + jnp.log(total)
        for start, owner, offset in parts:
            out_ref[owner, 0, :, offset : offset + token_rows] = attended[
                :, start : start + token_rows
            ]


def attend_rows(projected, scale_vec, segments, owners, token_rows):
    head_dim = scale_vec.shape[0]
    length = projected.shape[1]
    local_heads = projected.shape[0] // 3 // head_dim
    tokens = length // owners
    attended, log_total = pl.pallas_call(
        functools.partial(attend_kernel, token_rows),
        grid=(local_heads,),
        in_specs=[
            pl.BlockSpec((3, 1, head_dim, length), lambda h: (0, h, 0, 0)),
            pl.BlockSpec((head_dim, 1), lambda h: (0, 0)),
            pl.BlockSpec((length, 1), lambda h: (0, 0)),
            pl.BlockSpec((1, length), lambda h: (0, 0)),
        ],
        out_specs=[
            pl.BlockSpec((owners, 1, head_dim, tokens), lambda h: (0, h, 0, 0)),
            pl.BlockSpec((1, 1, length), lambda h: (h, 0, 0)),
        ],
        out_shape=[
            jax.ShapeDtypeStruct((owners, local_heads, head_dim, tokens), BF16),
            jax.ShapeDtypeStruct((local_heads, 1, length), F32),
        ],
        compiler_params=KERNEL,
        cost_estimate=LIGHT,
    )(
        projected.reshape(3, local_heads, head_dim, length),
        scale_vec.reshape(head_dim, 1),
        segments.reshape(length, 1),
        segments.reshape(1, length),
    )
    return attended.reshape(owners, local_heads * head_dim, tokens), log_total


def attend_back_kernel(
    token_rows,
    proj_ref,
    grad_ref,
    lse_ref,
    scale_ref,
    col_ref,
    row_ref,
    out_ref,
    scale_grad_ref,
    keys_acc,
    values_acc,
):
    length = proj_ref.shape[-1]
    scale = scale_ref[...]
    query_pre = proj_ref[0, 0]
    queries = (query_pre * scale).astype(BF16)
    keys_t = proj_ref[1, 0].astype(BF16)
    keys = proj_ref[1, 0].T.astype(BF16)
    values = proj_ref[2, 0].T.astype(BF16)
    keys_acc[...] = jnp.zeros_like(keys_acc)
    values_acc[...] = jnp.zeros_like(values_acc)
    scale_grad = jnp.zeros((scale.shape[0], 1), F32)
    for first, parts in token_places(length, grad_ref.shape[0], token_rows):
        end = first + Q_ROWS
        block = queries[:, first:end]
        grad = jnp.concatenate(
            [grad_ref[owner, 0, :, at : at + token_rows] for _, owner, at in parts], axis=1
        )
        scores = jnp.dot(keys[:end], block, preferred_element_type=F32)
        allowed = allowed_keys(col_ref[...], row_ref[:, first:end], first)
        scores = jnp.where(allowed, scores, MASKED_SCORE)
        probs = jnp.exp(scores - lse_ref[0, :, first:end])
        probs_grad = jnp.dot(values[:end], grad, preferred_element_type=F32)
        row_dot = jnp.sum(probs_grad * probs, axis=0, keepdims=True)
        scores_low = (probs * (probs_grad - row_dot)).astype(BF16)
        values_acc[:, :end] += lax.dot_general(
            grad, probs.astype(BF16), NT, preferred_element_type=F32
        )
        keys_acc[:, :end] += lax.dot_general(
            block, scores_low, NT, preferred_element_type=F32
        )
        query_bar = jnp.dot(keys_t[:, :end], scores_low, preferred_element_type=F32)
        query_bar = query_bar.astype(BF16).astype(F32)
        scale_grad += jnp.sum(query_bar * query_pre[:, first:end], axis=1, keepdims=True)
        out_ref[0, 0, :, first:end] = (query_bar * scale).astype(BF16)
    out_ref[1, 0] = keys_acc[...].astype(BF16)
    out_ref[2, 0] = values_acc[...].astype(BF16)
    spread = jnp.broadcast_to(scale_grad, scale_grad_ref.shape)

    @pl.when(pl.program_id(0) == 0)
    def _():
        scale_grad_ref[...] = spread

    @pl.when(pl.program_id(0) > 0)
    def _():
        scale_grad_ref[...] += spread


def attend_back_rows(projected, attended_grad, log_total, scale_vec, segments, token_rows):
    head_dim = scale_vec.shape[0]
    length = projected.shape[1]
    local_heads = projected.shape[0] // 3 // head_dim
    owners, _, tokens = attended_grad.shape
    lanes = 128
    grads, scale_grad = pl.pallas_call(
        functools.partial(attend_back_kernel, token_rows),
        grid=(local_heads,),
        in_specs=[
            pl.BlockSpec((3, 1, head_dim, length), lambda h: (0, h, 0, 0)),
            pl.BlockSpec((owners, 1, head_dim, tokens), lambda h: (0, h, 0, 0)),
            pl.BlockSpec((1, 1, length), lambda h: (h, 0, 0)),
            pl.BlockSpec((head_dim, 1), lambda h: (0, 0)),
            pl.BlockSpec((length, 1), lambda h: (0, 0)),
            pl.BlockSpec((1, length), lambda h: (0, 0)),
        ],
        out_specs=[
            pl.BlockSpec((3, 1, head_dim, length), lambda h: (0, h, 0, 0)),
            pl.BlockSpec((head_dim, lanes), lambda h: (0, 0)),
        ],
        out_shape=[
            pltpu.HBM((3, local_heads, head_dim, length), BF16),
            pltpu.HBM((head_dim, lanes), F32),
        ],
        scratch_shapes=[
            pltpu.VMEM((head_dim, length), F32),
            pltpu.VMEM((head_dim, length), F32),
        ],
        compiler_params=KERNEL,
        cost_estimate=LIGHT,
    )(
        *in_hbm(
            projected.reshape(3, local_heads, head_dim, length),
            attended_grad.reshape(owners, local_heads, head_dim, tokens),
        ),
        log_total,
        scale_vec.reshape(head_dim, 1),
        segments.reshape(length, 1),
        segments.reshape(1, length),
    )
    return grads.reshape(3 * local_heads * head_dim, length), scale_grad[:, 0]


def dense_grad_kernel(
    core_ref, attended_ref, normed_ref, active_ref, out_bar, up_bar, down_bar,
    own_ref, other_ref, normed_t, active_t,
):
    tile = pl.program_id(0)
    rows, width = 8 * own_ref.shape[3], out_bar.shape[1]

    @pl.when(tile == 0)
    def _():
        normed_t[...] = normed_ref[...].astype(F32).T.astype(BF16)
        active_t[...] = active_ref[...].astype(F32).T.astype(BF16)

    start = pl.multiple_of(tile * rows, rows)
    first_core = core_ref[2] == 0
    lefts = (attended_ref, normed_t, active_t)
    for i, (left, right) in enumerate(zip(lefts, (out_bar, up_bar, down_bar))):
        grad = jnp.dot(left[pl.ds(start, rows), :], right[...], preferred_element_type=F32)
        grad = grad.reshape(2, 2, 2, rows // 8, width)
        one, two = grad[:, :, 0], grad[:, :, 1]
        own_ref[:, :, 0, :, i * width : (i + 1) * width] = jnp.where(
            first_core, one, two
        ).astype(BF16)
        other_ref[:, :, 0, :, i * width : (i + 1) * width] = jnp.where(
            first_core, two, one
        ).astype(BF16)


def dense_grads(attended_t, normed, active, out_bar, up_bar, down_bar):
    width, tokens = attended_t.shape
    own = width // 32
    whole = pl.BlockSpec((tokens, width), lambda i, core: (0, 0))
    rows = pl.BlockSpec((2, 2, 1, own, 3 * width), lambda i, core: (0, 0, i, 0, 0))
    shape = pltpu.HBM((2, 2, 4, own, 3 * width), BF16)
    return pl.pallas_call(
        dense_grad_kernel,
        grid_spec=pltpu.PrefetchScalarGridSpec(
            num_scalar_prefetch=1,
            grid=(4,),
            in_specs=[pl.BlockSpec((width, tokens), lambda i, core: (0, 0))] + [whole] * 5,
            out_specs=[rows, rows],
            scratch_shapes=[pltpu.VMEM((width, tokens), BF16)] * 2,
        ),
        out_shape=[shape, shape],
        compiler_params=KERNEL,
        cost_estimate=LIGHT,
    )(place(), *in_hbm(attended_t, normed, active, out_bar, up_bar, down_bar))


def place():
    head = lax.axis_index("head")
    return jnp.stack([lax.axis_index("blk"), head // 2, head % 2]).astype(jnp.int32)


def assemble_kernel(place_ref, *refs):
    pieces, whole_ref = refs[:10], refs[10]
    half = whole_ref.shape[-1] // 2
    blk, row, core = place_ref[0], place_ref[1], place_ref[2]
    for i in range(2):
        at_core = core if i == 0 else 1 - core
        own, across, beside, one, two = pieces[5 * i : 5 * i + 5]
        whole_ref[0, blk, row, at_core] = own[0]
        whole_ref[0, 1 - blk, row, at_core] = across[0]
        whole_ref[0, blk, 1 - row, at_core] = beside[0]
        whole_ref[0, 1 - blk, 1 - row, at_core, :, :half] = one[0]
        whole_ref[0, 1 - blk, 1 - row, at_core, :, half:] = two[0]


def assemble(pieces):
    batch, own, columns = pieces[0].shape
    specs = [
        pl.BlockSpec((1, own, piece.shape[-1]), lambda i, at: (i, 0, 0))
        for piece in pieces
    ]
    whole = pl.pallas_call(
        assemble_kernel,
        grid_spec=pltpu.PrefetchScalarGridSpec(
            num_scalar_prefetch=1,
            grid=(batch,),
            in_specs=specs,
            out_specs=pl.BlockSpec((1, 2, 2, 2, own, columns), lambda i, at: (i, 0, 0, 0, 0, 0)),
        ),
        out_shape=jax.ShapeDtypeStruct((batch, 2, 2, 2, own, columns), BF16),
        compiler_params=KERNEL,
        cost_estimate=LIGHT,
    )(place(), *pieces)
    return whole.reshape(-1, columns)


def assemble_columns_kernel(place_ref, along_ref, across_ref, whole_ref, *extra_ref):
    blk = place_ref[0]
    columns = whole_ref.shape[-1]
    whole_ref[0, blk] = along_ref[0, :, :columns]
    whole_ref[0, 1 - blk] = across_ref[0, :, :columns]
    for extra in extra_ref:
        extra[0, blk] = along_ref[0, :, columns:]
        extra[0, 1 - blk] = across_ref[0, :, columns:]


def assemble_columns(along, across, columns):
    batch, own, both = along.shape
    rows = pl.BlockSpec((1, own, both), lambda i, at: (i, 0, 0))
    shapes = [(batch, 2, own, columns)]
    if both > columns:
        shapes.append((batch, 2, own, both - columns))
    parts = pl.pallas_call(
        assemble_columns_kernel,
        grid_spec=pltpu.PrefetchScalarGridSpec(
            num_scalar_prefetch=1,
            grid=(batch,),
            in_specs=[rows, rows],
            out_specs=[pl.BlockSpec((1,) + s[1:], lambda i, at: (i, 0, 0, 0)) for s in shapes],
        ),
        out_shape=[pltpu.HBM(s, BF16) for s in shapes],
        compiler_params=KERNEL,
        cost_estimate=LIGHT,
    )(place(), *in_hbm(along, across))
    return [part.reshape(-1, part.shape[-1]) for part in parts]


def assemble_wide_kernel(place_ref, along_ref, across_ref, whole_ref):
    blk = place_ref[0]
    own, columns = along_ref.shape[1], whole_ref.shape[-1]
    for i in range(along_ref.shape[-1] // columns):
        place, part = slice(i * own, (i + 1) * own), slice(i * columns, (i + 1) * columns)
        whole_ref[0, blk, place, :] = along_ref[0, :, part]
        whole_ref[0, 1 - blk, place, :] = across_ref[0, :, part]


def assemble_wide(along, across, columns):
    batch, own, wide = along.shape
    rows = own * (wide // columns)
    piece = pl.BlockSpec((1, own, wide), lambda i, at: (i, 0, 0))
    whole = pl.pallas_call(
        assemble_wide_kernel,
        grid_spec=pltpu.PrefetchScalarGridSpec(
            num_scalar_prefetch=1,
            grid=(batch,),
            in_specs=[piece, piece],
            out_specs=pl.BlockSpec((1, 2, rows, columns), lambda i, at: (i, 0, 0, 0)),
        ),
        out_shape=pltpu.HBM((batch, 2, rows, columns), BF16),
        compiler_params=KERNEL,
        cost_estimate=LIGHT,
    )(place(), *in_hbm(along, across))
    return whole.reshape(-1, columns)


def project_kernel(with_norm, place_ref, *refs):
    pieces, (gain_ref, weight_ref, normed_ref, projected_ref) = refs[:4], refs[4:]
    head = place_ref[1] * 2 + place_ref[2]
    rows = pieces[0].shape[0]
    for i, piece in enumerate(pieces):
        value = piece[...]
        if with_norm:
            stream = value.astype(F32)
            factor = lax.rsqrt(jnp.mean(stream * stream, axis=-1, keepdims=True) + EPSILON)
            value = (stream * factor * gain_ref[...]).astype(BF16)
        normed_ref[pl.ds(pl.multiple_of((head ^ i) * rows, rows), rows), :] = value
    projected = jnp.dot(normed_ref[...], weight_ref[...], preferred_element_type=F32)
    projected_ref[...] = projected.T


def project(pieces, gain, weight, with_norm, token_rows):
    tokens, width = pieces[0].shape
    length, columns = 4 * tokens, weight.shape[1]
    groups = tokens // token_rows
    piece = pl.BlockSpec((token_rows, width), lambda g, at: (g, 0))
    return pl.pallas_call(
        functools.partial(project_kernel, with_norm),
        grid_spec=pltpu.PrefetchScalarGridSpec(
            num_scalar_prefetch=1,
            grid=(groups,),
            in_specs=[piece] * 4
            + [
                pl.BlockSpec((1, width), lambda g, at: (0, 0)),
                pl.BlockSpec((width, columns), lambda g, at: (0, 0)),
            ],
            out_specs=[
                pl.BlockSpec((4 * token_rows, width), lambda g, at: (g, 0)),
                pl.BlockSpec((columns, 4 * token_rows), lambda g, at: (0, g)),
            ],
        ),
        out_shape=[
            pltpu.HBM((length, width), BF16),
            pltpu.HBM((columns, length), F32),
        ],
        compiler_params=KERNEL,
        cost_estimate=LIGHT,
    )(place(), *in_hbm(*pieces), gain.reshape(1, width), *in_hbm(weight))


def project_back_kernel(
    place_ref, bars_ref, weight_ref, normed_ref, own_ref, other_ref, grad_ref, bars_t
):
    @pl.when(pl.program_id(0) == 0)
    def _():
        bars_t[...] = bars_ref[...].astype(F32).T.astype(BF16)

    upper = lax.dot_general(bars_t[...], weight_ref[...], NT, preferred_element_type=F32)
    upper = upper.reshape(2, 2, 2, -1, upper.shape[-1])
    first_core = place_ref[2] == 0
    one, two = upper[:, :, 0], upper[:, :, 1]
    own_ref[...] = jnp.where(first_core, one, two)
    other_ref[...] = jnp.where(first_core, two, one).astype(BF16)
    grad = lax.dot_general(normed_ref[...], bars_t[...], TN, preferred_element_type=F32)
    grad_ref[...] = grad.astype(BF16)


def project_back(bars, weight, normed, token_rows):
    columns, length = bars.shape
    width = weight.shape[0]
    tile = width // 2
    quarter = pl.BlockSpec((2, 2, token_rows, tile), lambda i, at: (0, 0, 0, i))
    return pl.pallas_call(
        project_back_kernel,
        grid_spec=pltpu.PrefetchScalarGridSpec(
            num_scalar_prefetch=1,
            grid=(2,),
            in_specs=[
                pl.BlockSpec((columns, length), lambda i, at: (0, 0)),
                pl.BlockSpec((tile, columns), lambda i, at: (i, 0)),
                pl.BlockSpec((length, tile), lambda i, at: (0, i)),
            ],
            out_specs=[quarter, quarter, pl.BlockSpec((tile, columns), lambda i, at: (i, 0))],
            scratch_shapes=[pltpu.VMEM((length, columns), BF16)],
        ),
        out_shape=[
            pltpu.HBM((2, 2, token_rows, width), F32),
            pltpu.HBM((2, 2, token_rows, width), BF16),
            pltpu.HBM((width, columns), BF16),
        ],
        compiler_params=KERNEL,
        cost_estimate=LIGHT,
    )(place(), *in_hbm(bars, weight, normed))


def rows_back_kernel(place_ref, bars_ref, weight_ref, own_ref, other_ref, bars_t):
    @pl.when(pl.program_id(0) == 0)
    def _():
        bars_t[...] = bars_ref[...].astype(F32).T.astype(BF16)

    upper = lax.dot_general(bars_t[...], weight_ref[...], NT, preferred_element_type=F32)
    upper = upper.reshape(2, 2, 2, -1, upper.shape[-1])
    first_core = place_ref[2] == 0
    one, two = upper[:, :, 0], upper[:, :, 1]
    own_ref[...] = jnp.where(first_core, one, two)
    other_ref[...] = jnp.where(first_core, two, one).astype(BF16)


def rows_back(bars, weight, token_rows):
    columns, length = bars.shape
    width = weight.shape[0]
    tile = width // 2
    quarter = pl.BlockSpec((2, 2, token_rows, tile), lambda i, at: (0, 0, 0, i))
    return pl.pallas_call(
        rows_back_kernel,
        grid_spec=pltpu.PrefetchScalarGridSpec(
            num_scalar_prefetch=1,
            grid=(2,),
            in_specs=[
                pl.BlockSpec((columns, length), lambda i, at: (0, 0)),
                pl.BlockSpec((tile, columns), lambda i, at: (i, 0)),
            ],
            out_specs=[quarter, quarter],
            scratch_shapes=[pltpu.VMEM((length, columns), BF16)],
        ),
        out_shape=[
            pltpu.HBM((2, 2, token_rows, width), F32),
            pltpu.HBM((2, 2, token_rows, width), BF16),
        ],
        compiler_params=KERNEL,
        cost_estimate=LIGHT,
    )(place(), *in_hbm(bars, weight))


def weight_back_kernel(bars_ref, normed_ref, grad_ref):
    grad = jnp.dot(bars_ref[...], normed_ref[...], preferred_element_type=F32)
    grad_ref[...] = grad.T.astype(BF16)


def weight_back(bars, normed):
    columns, length = bars.shape
    width = normed.shape[1]
    tile = width // 5
    return pl.pallas_call(
        weight_back_kernel,
        grid=(5,),
        in_specs=[
            pl.BlockSpec((columns, length), lambda i: (0, 0)),
            pl.BlockSpec((length, tile), lambda i: (0, i)),
        ],
        out_specs=pl.BlockSpec((tile, columns), lambda i: (i, 0)),
        out_shape=pltpu.HBM((width, columns), BF16),
        compiler_params=KERNEL,
        cost_estimate=LIGHT,
    )(*in_hbm(bars, normed))


def tied(*arrays):
    return lax.optimization_barrier(arrays)


def swapped(array, axis, mask):
    size = lax.axis_size(axis)
    return lax.ppermute(array, axis, [(i, i ^ mask) for i in range(size)])


def pick(array, index, axis=0):
    return lax.dynamic_index_in_dim(array, index, axis, keepdims=False)


def swap_halves(array):
    me = lax.axis_index("blk")
    got = swapped(pick(array, 1 - me), "blk", 1)
    kept = pick(array, me)
    return jnp.stack([jnp.where(me == 0, kept, got), jnp.where(me == 0, got, kept)])


def scatter_row(halves):
    row = lax.axis_index("head") // 2
    got = swapped(pick(halves, 1 - row, 1).astype(BF16), "head", 2).astype(F32)
    return (pick(halves, row, 1) + got).reshape(-1, halves.shape[-1])


def over_head(parts):
    return lax.all_to_all(parts, "head", split_axis=0, concat_axis=0, tiled=True)


def qkv_columns(rows, extra):
    own, width = rows.shape
    part = width // 3 // 4
    sent = rows.reshape(own, 3, 4, part).transpose(2, 0, 1, 3).reshape(4, own, 3 * part)
    if extra is not None:
        sent = jnp.concatenate([sent, jnp.broadcast_to(extra[None], (4,) + extra.shape)], axis=2)
    return over_head(sent)


def along_batch(piece):
    return lax.all_gather(piece, "batch", axis=0, tiled=False)


def other_core(array):
    return swapped(array, "head", 1)


def to_beside(across):
    return swapped(across[..., : across.shape[-1] // 2], "head", 2)


def to_across(beside):
    return swapped(beside[..., beside.shape[-1] // 2 :], "blk", 1)


def over_batch(parts):
    return lax.psum_scatter(parts.astype(BF16), "batch", scatter_dimension=0, tiled=False)


def across_sum(halves):
    blk = lax.axis_index("blk")
    got = swapped(pick(halves, 1 - blk), "blk", 1).astype(F32)
    return (pick(halves, blk).astype(F32) + got).astype(BF16)


def columns_to_rows(moved):
    rows = moved.shape[1]
    return moved.reshape(4, rows, 3, -1).transpose(1, 2, 0, 3).reshape(rows, -1).astype(F32)


def quarter(parts, blk, row):
    one, two = (pick(pick(part, blk), row).astype(F32) for part in parts)
    return one + two


def quarter_kernel(place_ref, one_ref, two_ref, *refs):
    total = one_ref[0, 0, 0].astype(F32) + two_ref[0, 0, 0].astype(F32)
    for ref in refs[:-1]:
        total = total + ref[0].astype(F32)
    refs[-1][0] = total.astype(BF16)


def quarter_rows(parts, flipped, *more):
    _, _, batch, own, columns = parts[0].shape
    rows = pl.BlockSpec((1, own, columns), lambda i, at: (i, 0, 0))

    def quarter_at(i, at):
        return (1 - at[0], 1 - at[1], i, 0, 0) if flipped else (at[0], at[1], i, 0, 0)

    part = pl.BlockSpec((1, 1, 1, own, columns), quarter_at)
    return pl.pallas_call(
        quarter_kernel,
        grid_spec=pltpu.PrefetchScalarGridSpec(
            num_scalar_prefetch=1,
            grid=(batch,),
            in_specs=[part, part] + [rows] * len(more),
            out_specs=rows,
        ),
        out_shape=pltpu.HBM((batch, own, columns), BF16),
        compiler_params=KERNEL,
        cost_estimate=LIGHT,
    )(place(), *in_hbm(*parts, *more))


def diagonal_rows(parts):
    rows = quarter_rows(parts, True)
    half = rows.shape[-1] // 2
    return rows[..., :half], rows[..., half:]


def beside_rows(parts, diagonal):
    blk, row = place()[:2]
    return (quarter(parts, blk, 1 - row) + diagonal.astype(F32)).astype(BF16)


def across_rows(parts):
    blk, row = place()[:2]
    return quarter(parts, 1 - blk, row).astype(BF16)


def neighbour_rows(parts, one, two):
    blk, row = place()[:2]
    half = one.shape[-1]
    across, beside = quarter(parts, 1 - blk, row), quarter(parts, blk, 1 - row)
    across = jnp.concatenate([across[..., :half], across[..., half:] + two.astype(F32)], axis=-1)
    beside = jnp.concatenate([beside[..., :half] + one.astype(F32), beside[..., half:]], axis=-1)
    return across.astype(BF16), beside.astype(BF16)


def sent_beside_and_across(across, beside):
    return swapped(across, "blk", 1), swapped(beside, "head", 2)


def heads_grad(weight, out_bar):
    return dot_cols(weight, out_bar).astype(BF16).reshape(4, -1, out_bar.shape[0])


def own_sum(parts, across, beside):
    return quarter_rows(parts, False, across, beside)


def sum_over(array, *hops):
    for axis, mask in hops:
        array = array + swapped(array, axis, mask)
    return array


def gain_back(weight, weight_grad, gain):
    return jnp.sum(weight.astype(F32) * weight_grad, axis=-1) / gain.astype(F32)


def lower_of(upper, stream, factor, gain):
    return norm_back(upper, stream, factor, gain)[0]


def spread_device(
    tokens,
    segments,
    qkv_weight,
    out_weight,
    up_weight,
    down_weight,
    attn_gain,
    mlp_gain,
    scale_param,
    cotangent,
):
    layers, head_dim = scale_param.shape
    _, token_rows, width = tokens.shape
    scale_vecs = SCALE_BASE / math.sqrt(head_dim) * jax.nn.softplus(scale_param)
    segments = pick(segments, lax.axis_index("blk"))
    own_gains = jnp.concatenate([attn_gain, mlp_gain], axis=0)

    part3 = 3 * width // 4
    dense_own = [
        jnp.concatenate([out_weight[i], up_weight[i], down_weight[i]], axis=1) for i in (0, 1)
    ]

    first = swap_halves(tokens).reshape(-1, width)
    columns = qkv_columns(qkv_weight[0], own_gains.T)
    columns, first = tied(columns.reshape(-1, columns.shape[-1]), first)
    stream = first.astype(F32)
    along = along_batch(columns)
    far, near = swapped(first, "head", 2), other_core(first)
    both = other_core(far)
    upper = swap_halves(cotangent)
    along, near, far, both, dense_near, upper = tied(
        along, near, far, both, dense_own[0], upper
    )
    token_pieces = (first, near, far, both)
    dense_near = along_batch(dense_near)
    qkv_across = swapped(along, "blk", 1)
    next_columns = jnp.concatenate(list(qkv_columns(qkv_weight[1], None)), axis=1)
    qkv_across, dense_near, next_columns = tied(qkv_across, dense_near, next_columns)
    across, beside = swapped(dense_near, "blk", 1), swapped(dense_near, "head", 2)
    next_both = along_batch(jnp.stack([next_columns, dense_own[1]]))
    weight, gains = assemble_columns(along, qkv_across, part3)
    qkvs = [weight]
    gains = gains.T.astype(F32)

    kept, denses = [], []
    for layer in range(layers):
        normed, factor_one = normalize(stream, gains[layer])
        if layer == 1:
            normed = normed.astype(BF16)
            far, near = swapped(normed, "head", 2), other_core(normed)
            far, next_across, dense_next = tied(far, next_across, dense_next)
            across, beside = swapped(dense_next, "blk", 1), swapped(dense_next, "head", 2)
            token_pieces = (normed, near, far, other_core(far))
            qkvs.append(assemble_wide(next_along, next_across, part3))
        normed_all, projected = project(
            token_pieces, gains[layer], qkvs[layer], layer == 0, token_rows
        )
        attended, log_total = attend_rows(
            projected, scale_vecs[layer], segments, 4, token_rows
        )
        attended, across, beside = tied(attended, across, beside)
        one, two = to_beside(across), to_across(beside)
        if layer == 0:
            two, next_both = tied(two, next_both)
            next_along, dense_next = next_both[:, 0], next_both[:, 1]
            next_across = swapped(next_along, "blk", 1)
            attended_t, one, two = tied(over_head(attended), one, two)
        else:
            dense_near = dense_next
            attended_t, one, two = tied(over_head(attended), one, two)
        pieces = (dense_near, across, beside, one, two)
        pieces += tuple(other_core(piece) for piece in pieces)
        attended_t = attended_t.reshape(width, -1)
        denses.append(assemble(pieces))
        dense = denses[layer]
        out_w, up_w, down_w = dense[:, :width], dense[:, width:-width], dense[:, -width:]
        middle = stream + dot_rows(attended_t, out_w)
        normed_two, factor_two = normalize(middle, gains[layers + layer])
        normed_two = normed_two.astype(BF16)
        hidden = dot(normed_two, up_w)
        active = (hidden * jax.nn.sigmoid(hidden)).astype(BF16)
        kept.append(
            (
                stream, factor_one, normed_all, projected, log_total, attended_t, middle,
                factor_two, normed_two, hidden, active,
            )
        )
        stream = middle + dot(active, down_w)
    layer_out = swap_halves(stream.astype(BF16).reshape(tokens.shape))
    upper = upper.reshape(-1, width).astype(F32)

    scale_grads = [None] * layers
    for layer in reversed(range(layers)):
        (
            stream, factor_one, normed_all, projected, log_total, attended_t, middle,
            factor_two, normed_two, hidden, active,
        ) = kept[layer]
        qkv, dense = qkvs[layer], denses[layer]
        out_w, up_w, down_w = dense[:, :width], dense[:, width:-width], dense[:, -width:]
        down_bar = upper.astype(BF16)
        gate = jax.nn.sigmoid(hidden)
        up_bar = (
            dot_cols(down_bar, down_w) * gate * (1.0 + hidden * (1.0 - gate))
        ).astype(BF16)
        middle_grad = upper + lower_of(
            dot_cols(up_bar, up_w), middle, factor_two, gains[layers + layer]
        )
        out_bar = middle_grad.astype(BF16)
        if layer == 0:
            out_bar, diagonal = tied(out_bar, diagonal)
            out_bar, rows = tied(out_bar, beside_rows(cored, diagonal))
            beside = swapped(rows, "head", 2)
            attended_grad = over_head(heads_grad(out_w, out_bar))
            grads, others = dense_grads(attended_t, normed_two, active, out_bar, up_bar, down_bar)
            attended_grad, others, z_sum, across, beside = tied(
                attended_grad, others, z_sum, across, beside
            )
            others = other_core(others)
            attended_grad, summed = tied(attended_grad, own_sum(cored, across, beside))
            summed = over_batch(summed)
            z_across = across_sum(z_sum)
        else:
            attended_grad = over_head(heads_grad(out_w, out_bar))
            grads, others = dense_grads(attended_t, normed_two, active, out_bar, up_bar, down_bar)
            attended_grad, others, layer_out = tied(attended_grad, others, layer_out)
            others = other_core(others)
        bars, scale_grads[layer] = attend_back_rows(
            projected, attended_grad, log_total, scale_vecs[layer], segments, token_rows
        )
        if layer == 0:
            bars, others, z_across = tied(bars, others, z_across)
            moved = over_head(z_across.reshape(4, -1, z_across.shape[-1]))
            qkv_grad = weight_back(bars, normed_all)
            bars, qkv_grad, moved = tied(bars, qkv_grad, moved)
            z_sum = over_batch(qkv_grad.reshape(4, 2, -1, qkv_grad.shape[-1]))
            cored = (grads, others)
            bars, rows = tied(bars, diagonal_rows(cored))
            diagonal = sent_beside_and_across(*rows)
            halves, to_core = rows_back(bars, qkv, token_rows)
            halves, to_core, diagonal, summed = tied(halves, to_core, diagonal, summed)
            halves, to_core, rows = tied(halves, to_core, neighbour_rows(cored, *diagonal))
            sent = sent_beside_and_across(*rows)
            halves = halves + other_core(to_core).astype(F32)
            scale_sum = sum_over(jnp.stack(scale_grads), ("head", 1), ("batch", 1), ("batch", 2))
            halves, sent, z_sum, scale_sum = tied(halves, sent, z_sum, scale_sum)
            halves, own = tied(halves, own_sum(cored, *sent))
            dense_first = over_batch(own)
            normed_grad = scatter_row(halves)
            z_across = across_sum(z_sum)
            z_across = over_head(z_across.reshape(4, -1, z_across.shape[-1]))
            z_across, dense_first = tied(z_across, dense_first)
            dense_grad = [dense_first, summed]
            qkv_grads = [columns_to_rows(z_across), columns_to_rows(moved)]
        else:
            bars, others = tied(bars, others)
            cored = (grads, others)
            halves, to_core, qkv_grad = project_back(bars, qkv, normed_all, token_rows)
            z_sum = over_batch(qkv_grad.reshape(4, 2, -1, qkv_grad.shape[-1]))
            to_core, grads = tied(to_core, grads)
            rows = quarter_rows((grads, others), True)
            halves = halves + other_core(to_core).astype(F32)
            halves, rows = tied(halves, rows)
            diagonal = swapped(rows, "blk", 1)
            normed_grad = scatter_row(halves)
            normed_grad, rows = tied(normed_grad, across_rows(cored))
            across = swapped(rows, "blk", 1)
        upper = middle_grad + lower_of(normed_grad, stream, factor_one, gains[layer])
    input_grad = swap_halves(upper.astype(BF16).reshape(tokens.shape)).astype(F32)
    scale_total = sum_over(scale_sum, ("head", 2), ("blk", 1))
    scale_grad = scale_total * (SCALE_BASE / math.sqrt(head_dim)) * jax.nn.sigmoid(scale_param)
    dense_all = jnp.stack([part.astype(F32) for part in dense_grad])
    qkv_all = jnp.stack(qkv_grads)
    up_all = dense_all[:, :, width:-width]
    return (
        layer_out,
        input_grad,
        qkv_all,
        dense_all[:, :, :width],
        up_all,
        dense_all[:, :, -width:],
        gain_back(qkv_weight, qkv_all, attn_gain),
        gain_back(up_weight, up_all, mlp_gain),
        scale_grad,
    )


def per_device(*args):
    tokens, segments = args[0], args[1]
    sizes = tuple(lax.axis_size(axis) for axis in ALL)
    heads = tokens.shape[2] // args[8].shape[1]
    spread = (
        sizes == (4, 2, 4)
        and tokens.shape[0] == 2
        and args[2].shape[0] == 2
        and tokens.shape[1] % 128 == 0
        and Q_ROWS % tokens.shape[1] == 0
        and segments.shape[1] <= WINDOW
        and segments.shape[1] % Q_ROWS == 0
        and heads % 4 == 0
        and tokens.shape[2] % 256 == 0
    )
    return spread_device(*args) if spread else general_device(*args)


def solution(mesh):
    rows = P(None, ALL, None)
    by_token = P("batch", ("blk", "head"), None)
    return jax.shard_map(
        per_device,
        mesh=mesh,
        in_specs=(
            by_token, P("batch", None), rows, rows, rows, rows, P(None, ALL), P(None, ALL), P(),
            by_token,
        ),
        out_specs=(
            by_token, by_token, rows, rows, rows, rows, P(None, ALL), P(None, ALL), P(),
        ),
        check_vma=False,
    )
```

```python
import functools
import math

import jax
import jax.numpy as jnp
from jax import lax
from jax.experimental import pallas as pl
from jax.experimental.pallas import tpu as pltpu
from jax.sharding import PartitionSpec as P

WINDOW = 1024
EPSILON = 1e-06
SCALE_BASE = 1.4426950408889634
MASKED_SCORE = -1e30

ALL = ("batch", "blk", "head")
REST = ("batch", "blk")
F32 = jnp.float32
BF16 = jnp.bfloat16


def shifted(block, axis, distance):
    devices = range(lax.axis_size(axis))
    route = [(i - distance, i) for i in devices if i - distance in devices]
    return lax.ppermute(block, axis, route)


NT = (((1,), (1,)), ((), ()))
TN = (((0,), (0,)), ((), ()))


def dot(left, right):
    return jnp.dot(left, right, preferred_element_type=F32)


def dot_rows(left, right):
    return lax.dot_general(left, right, (((0,), (0,)), ((), ())), preferred_element_type=F32)


def dot_cols(left, right):
    return lax.dot_general(left, right, (((1,), (1,)), ((), ())), preferred_element_type=F32)


def normalize(stream, gain):
    factor = lax.rsqrt(jnp.mean(stream * stream, axis=-1, keepdims=True) + EPSILON)
    return stream * factor * gain, factor


def norm_back(upper, stream, factor, gain):
    inner = upper * gain
    gain_grad = jnp.sum(upper * stream * factor, axis=0)
    lower = factor * inner - stream * factor * factor * factor * jnp.mean(
        inner * stream, axis=-1, keepdims=True
    )
    return lower, gain_grad


class Plan:
    def __init__(self, tokens):
        self.seqs, self.rows, self.width = tokens.shape
        self.heads = lax.axis_size("head")
        self.blks = lax.axis_size("blk")
        self.block = self.rows * self.heads
        self.whole = self.seqs % self.blks == 0
        if self.whole:
            self.groups, self.own_seqs = self.blks, self.seqs // self.blks
            self.reach = 0
        else:
            self.groups, self.own_seqs = 1, self.seqs
            self.reach = min((WINDOW - 1) // self.block + 1, self.blks - 1)
        self.length = self.groups * self.block
        self.tokens = self.seqs * self.rows


def to_plan(plan, array):
    if plan.whole and plan.blks > 1:
        array = lax.all_to_all(array, "blk", split_axis=0, concat_axis=0, tiled=True)
    return array.reshape(plan.tokens, plan.width)


def from_plan(plan, flat):
    array = flat.reshape(plan.seqs, plan.rows, plan.width)
    if plan.whole and plan.blks > 1:
        array = lax.all_to_all(array, "blk", split_axis=0, concat_axis=0, tiled=True)
    return array


def in_sequence(plan, by_head, width):
    parts = by_head.reshape(plan.heads, plan.groups, plan.own_seqs, plan.rows, width)
    return parts.transpose(2, 1, 0, 3, 4).reshape(-1, width)


def by_owner(plan, rows, width):
    parts = rows.reshape(plan.own_seqs, plan.groups, plan.heads, plan.rows, width)
    return parts.transpose(2, 1, 0, 3, 4).reshape(plan.heads, plan.tokens, width)


def gather_tokens(plan, rows):
    moved = lax.all_gather(rows, "head", axis=0, tiled=False)
    return in_sequence(plan, moved, rows.shape[-1])


def scatter_tokens(plan, rows):
    width = rows.shape[-1]
    return lax.psum_scatter(
        by_owner(plan, rows.astype(BF16), width), "head", scatter_dimension=0, tiled=False
    ).astype(F32)


def heads_to_tokens(plan, rows):
    part = rows.shape[-1]
    moved = lax.all_to_all(
        by_owner(plan, rows, part), "head", split_axis=0, concat_axis=0, tiled=True
    )
    return moved.transpose(1, 0, 2).reshape(plan.tokens, plan.heads * part)


def tokens_to_heads(plan, rows):
    part = rows.shape[-1] // plan.heads
    sent = rows.reshape(plan.tokens, plan.heads, part).transpose(1, 0, 2)
    moved = lax.all_to_all(sent, "head", split_axis=0, concat_axis=0, tiled=True)
    return in_sequence(plan, moved, part)


def gather_qkv(rows):
    own, width = rows.shape
    heads = lax.axis_size("head")
    part = width // 3 // heads
    sent = rows.reshape(own, 3, heads, part).transpose(2, 0, 1, 3).reshape(heads, own, 3 * part)
    moved = lax.all_to_all(sent, "head", split_axis=0, concat_axis=0, tiled=True)
    full = lax.all_gather(moved, REST, axis=0, tiled=True)
    return full.reshape(-1, 3 * part)


def scatter_qkv(grad):
    heads = lax.axis_size("head")
    part = grad.shape[1] // 3
    summed = lax.psum_scatter(grad.astype(BF16), REST, scatter_dimension=0, tiled=True)
    own = summed.shape[0] // heads
    moved = lax.all_to_all(
        summed.reshape(heads, own, 3 * part), "head", split_axis=0, concat_axis=0, tiled=True
    )
    return (
        moved.reshape(heads, own, 3, part)
        .transpose(1, 2, 0, 3)
        .reshape(own, 3 * heads * part)
        .astype(F32)
    )


def window_mask(plan, segments, block_index):
    key_count = plan.length + plan.reach * plan.block
    if plan.whole:
        query_segs, key_segs = segments, segments
    else:
        leading = jnp.full((plan.own_seqs, plan.reach * plan.block), -1, jnp.int32)
        padded = jnp.concatenate([leading, segments], axis=1)
        start = block_index * plan.block
        query_segs = lax.dynamic_slice_in_dim(segments, start, plan.block, 1)
        key_segs = lax.dynamic_slice_in_dim(padded, start, key_count, 1)
    query_place = jnp.arange(plan.length, dtype=jnp.int32)[:, None] + plan.reach * plan.block
    key_place = jnp.arange(key_count, dtype=jnp.int32)[None, :]
    near = (key_place <= query_place) & (query_place - key_place < WINDOW)
    return (key_segs[:, None, :] == query_segs[:, :, None]) & near[None]


def with_earlier(plan, own):
    arrived = [own]
    for _ in range(plan.reach):
        arrived.append(shifted(arrived[-1], "blk", 1))
    return jnp.concatenate(arrived[::-1], axis=1) if plan.reach else own


def to_earlier(plan, grads):
    if not plan.reach:
        return grads
    block = plan.block
    total = grads[:, :block]
    for step in range(1, plan.reach + 1):
        total = (
            shifted(total.astype(BF16), "blk", -1).astype(F32)
            + grads[:, step * block : (step + 1) * block]
        )
    return total


def scores_of(queries, keys, allowed):
    scores = jnp.einsum("sqhd,skhd->shqk", queries, keys, preferred_element_type=F32)
    return jnp.where(allowed[:, None], scores, MASKED_SCORE)


def attend(queries, keys, values, allowed):
    scores = scores_of(queries, keys, allowed)
    top_score = jnp.max(scores, axis=-1, keepdims=True)
    exp_terms = jnp.exp(scores - top_score)
    totals = jnp.sum(exp_terms, axis=-1, keepdims=True)
    probs_low = (exp_terms / totals).astype(BF16)
    attended = jnp.einsum("shqk,skhd->sqhd", probs_low, values, preferred_element_type=F32)
    return attended, top_score + jnp.log(totals)


def attend_back(queries, keys, values, allowed, log_total, attended_grad):
    probs = jnp.exp(scores_of(queries, keys, allowed) - log_total)
    probs_low = probs.astype(BF16)
    values_grad = jnp.einsum(
        "shqk,sqhd->skhd", probs_low, attended_grad, preferred_element_type=F32
    )
    probs_grad = jnp.einsum("sqhd,skhd->shqk", attended_grad, values, preferred_element_type=F32)
    row_dot = jnp.sum(probs_grad * probs, axis=-1, keepdims=True)
    scores_low = (probs * (probs_grad - row_dot)).astype(BF16)
    queries_grad = jnp.einsum("shqk,skhd->sqhd", scores_low, keys, preferred_element_type=F32)
    keys_grad = jnp.einsum("shqk,sqhd->skhd", scores_low, queries, preferred_element_type=F32)
    return queries_grad, keys_grad, values_grad


def forward(plan, stream, qkv, dense, gains, scale_vec, allowed):
    width = plan.width
    head_dim = scale_vec.shape[0]
    part = qkv.shape[1] // 3
    local_heads = part // head_dim
    split = (plan.own_seqs, plan.length, local_heads, head_dim)
    out_w, up_w, down_w = dense[:, :width], dense[:, width:-width], dense[:, -width:]
    normed, factor_one = normalize(stream, gains[0])
    normed_all = gather_tokens(plan, normed.astype(BF16))
    projected = dot(normed_all, qkv)
    query_pre = projected[:, :part].reshape(split)
    queries = (query_pre * scale_vec).astype(BF16)
    keys = with_earlier(plan, projected[:, part : 2 * part].astype(BF16).reshape(split))
    values = with_earlier(plan, projected[:, 2 * part :].astype(BF16).reshape(split))
    attended_part, log_total = attend(queries, keys, values, allowed)
    attended = heads_to_tokens(plan, attended_part.astype(BF16).reshape(-1, part))
    middle = stream + dot(attended, out_w)
    normed_two, factor_two = normalize(middle, gains[1])
    normed_two = normed_two.astype(BF16)
    hidden = dot(normed_two, up_w)
    active = (hidden * jax.nn.sigmoid(hidden)).astype(BF16)
    result = middle + dot(active, down_w)
    kept = (
        stream, factor_one, normed_all, query_pre, queries, keys, values, log_total,
        attended, middle, factor_two, normed_two, hidden, active,
    )
    return result, kept


def backward(plan, upper, kept, qkv, dense, gains, scale_vec, allowed):
    (
        stream, factor_one, normed_all, query_pre, queries, keys, values, log_total,
        attended, middle, factor_two, normed_two, hidden, active,
    ) = kept
    width = plan.width
    head_dim = scale_vec.shape[0]
    part = qkv.shape[1] // 3
    out_w, up_w, down_w = dense[:, :width], dense[:, width:-width], dense[:, -width:]
    upper_low = upper.astype(BF16)
    down_grad = dot_rows(active, upper_low)
    active_grad = dot_cols(upper_low, down_w)
    gate = jax.nn.sigmoid(hidden)
    hidden_low = (active_grad * gate * (1.0 + hidden * (1.0 - gate))).astype(BF16)
    up_grad = dot_rows(normed_two, hidden_low)
    extra_two, mlp_gain_grad = norm_back(dot_cols(hidden_low, up_w), middle, factor_two, gains[1])
    middle_grad = upper + extra_two
    middle_low = middle_grad.astype(BF16)
    out_grad = dot_rows(attended, middle_low)
    dense_grad = jnp.concatenate([out_grad, up_grad, down_grad], axis=1).astype(BF16)
    dense_own = lax.psum_scatter(dense_grad, ALL, scatter_dimension=0, tiled=True)
    attended_grad = tokens_to_heads(plan, dot_cols(middle_low, out_w).astype(BF16))
    queries_grad, keys_grad, values_grad = attend_back(
        queries, keys, values, allowed, log_total, attended_grad.reshape(queries.shape)
    )
    query_bar = queries_grad.astype(BF16).astype(F32)
    scale_vec_grad = jnp.sum((query_bar * query_pre).reshape(-1, head_dim), axis=0)
    query_low = (query_bar * scale_vec).astype(BF16).reshape(-1, part)
    keys_low = to_earlier(plan, keys_grad).astype(BF16).reshape(-1, part)
    values_low = to_earlier(plan, values_grad).astype(BF16).reshape(-1, part)
    projected_low = jnp.concatenate([query_low, keys_low, values_low], axis=1)
    normed_grad = scatter_tokens(plan, dot_cols(projected_low, qkv))
    qkv_own = scatter_qkv(dot_rows(normed_all, projected_low))
    extra_one, attn_gain_grad = norm_back(normed_grad, stream, factor_one, gains[0])
    lower = middle_grad + extra_one
    return lower, qkv_own, dense_own, (attn_gain_grad, mlp_gain_grad), scale_vec_grad


def general_device(
    tokens,
    segments,
    qkv_weight,
    out_weight,
    up_weight,
    down_weight,
    attn_gain,
    mlp_gain,
    scale_param,
    cotangent,
):
    plan = Plan(tokens)
    layers, head_dim = scale_param.shape
    block_index = lax.axis_index("blk")
    scale_vecs = SCALE_BASE / math.sqrt(head_dim) * jax.nn.softplus(scale_param)
    own_gains = jnp.concatenate([attn_gain, mlp_gain], axis=0)
    gains = (
        lax.all_gather(own_gains.reshape(1, -1), ALL, axis=0, tiled=True)
        .reshape(-1, 2 * layers, attn_gain.shape[1])
        .transpose(1, 0, 2)
        .reshape(2 * layers, plan.width)
        .astype(F32)
    )
    if plan.whole:
        segments = lax.dynamic_slice_in_dim(
            segments, block_index * plan.own_seqs, plan.own_seqs, 0
        )
    allowed = window_mask(plan, segments, block_index)
    stream = to_plan(plan, tokens).astype(F32)
    qkvs, denses, kept = [], [], []
    for layer in range(layers):
        qkvs.append(gather_qkv(qkv_weight[layer]))
        own = jnp.concatenate([out_weight[layer], up_weight[layer], down_weight[layer]], axis=1)
        denses.append(lax.all_gather(own, ALL, axis=0, tiled=True))
        layer_gains = (gains[layer], gains[layers + layer])
        stream, saved = forward(
            plan, stream, qkvs[layer], denses[layer], layer_gains, scale_vecs[layer], allowed
        )
        kept.append(saved)
    layer_out = from_plan(plan, stream.astype(BF16))
    upper = to_plan(plan, cotangent).astype(F32)
    qkv_grads, dense_grads = [None] * layers, [None] * layers
    gain_grads, scale_grads = [None] * layers, [None] * layers
    for layer in reversed(range(layers)):
        layer_gains = (gains[layer], gains[layers + layer])
        upper, qkv_grads[layer], dense_grads[layer], gain_grads[layer], scale_grads[layer] = (
            backward(
                plan, upper, kept[layer], qkvs[layer], denses[layer], layer_gains,
                scale_vecs[layer], allowed,
            )
        )
    input_grad = from_plan(plan, upper.astype(BF16)).astype(F32)
    small = jnp.concatenate(
        [g[0] for g in gain_grads] + [g[1] for g in gain_grads] + scale_grads, axis=0
    )
    total = lax.psum(small, ALL)
    gain_total = total[: 2 * layers * plan.width].reshape(2 * layers, plan.width)
    owner = lax.axis_index(ALL)
    gain_rows = attn_gain.shape[1]
    own_total = lax.dynamic_slice_in_dim(gain_total, owner * gain_rows, gain_rows, 1)
    scale_total = total[2 * layers * plan.width :].reshape(layers, head_dim)
    scale_grad = scale_total * (SCALE_BASE / math.sqrt(head_dim)) * jax.nn.sigmoid(scale_param)
    dense_all = jnp.stack(dense_grads).astype(F32)
    width = plan.width
    return (
        layer_out,
        input_grad,
        jnp.stack(qkv_grads),
        dense_all[:, :, :width],
        dense_all[:, :, width:-width],
        dense_all[:, :, -width:],
        own_total[:layers],
        own_total[layers:],
        scale_grad,
    )


Q_ROWS = 256
KERNEL = pltpu.CompilerParams(vmem_limit_bytes=32 * 1024 * 1024)
LIGHT = pl.CostEstimate(flops=1 << 20, bytes_accessed=1 << 20, transcendentals=0)


def in_hbm(*arrays):
    return [pltpu.with_memory_space_constraint(array, pltpu.HBM) for array in arrays]


def allowed_keys(col, row, first):
    count = first + row.shape[1]
    key_place = lax.broadcasted_iota(jnp.int32, (count, row.shape[1]), 0)
    query_place = lax.broadcasted_iota(jnp.int32, (count, row.shape[1]), 1) + first
    return (col[:count] == row) & (key_place <= query_place)


def token_places(length, heads, token_rows):
    for first in range(0, length, Q_ROWS):
        parts = []
        for start in range(0, Q_ROWS, token_rows):
            place = (first + start) // token_rows
            parts.append((start, place % heads, place // heads * token_rows))
        yield first, parts


def attend_kernel(token_rows, proj_ref, scale_ref, col_ref, row_ref, out_ref, lse_ref):
    length = proj_ref.shape[-1]
    queries = (proj_ref[0, 0] * scale_ref[...]).astype(BF16)
    keys = proj_ref[1, 0].T.astype(BF16)
    values = proj_ref[2, 0].astype(BF16)
    for first, parts in token_places(length, out_ref.shape[0], token_rows):
        end = first + Q_ROWS
        scores = jnp.dot(keys[:end], queries[:, first:end], preferred_element_type=F32)
        allowed = allowed_keys(col_ref[...], row_ref[:, first:end], first)
        scores = jnp.where(allowed, scores, MASKED_SCORE)
        top = jnp.max(scores, axis=0, keepdims=True)
        terms = jnp.exp(scores - top)
        total = jnp.sum(terms, axis=0, keepdims=True)
        probs = (terms * (1.0 / total)).astype(BF16)
        attended = jnp.dot(values[:, :end], probs, preferred_element_type=F32).astype(BF16)
        lse_ref[0, :, first:end] = top + jnp.log(total)
        for start, owner, offset in parts:
            out_ref[owner, 0, :, offset : offset + token_rows] = attended[
                :, start : start + token_rows
            ]


def attend_rows(projected, scale_vec, segments, owners, token_rows):
    head_dim = scale_vec.shape[0]
    length = projected.shape[1]
    local_heads = projected.shape[0] // 3 // head_dim
    tokens = length // owners
    attended, log_total = pl.pallas_call(
        functools.partial(attend_kernel, token_rows),
        grid=(local_heads,),
        in_specs=[
            pl.BlockSpec((3, 1, head_dim, length), lambda h: (0, h, 0, 0)),
            pl.BlockSpec((head_dim, 1), lambda h: (0, 0)),
            pl.BlockSpec((length, 1), lambda h: (0, 0)),
            pl.BlockSpec((1, length), lambda h: (0, 0)),
        ],
        out_specs=[
            pl.BlockSpec((owners, 1, head_dim, tokens), lambda h: (0, h, 0, 0)),
            pl.BlockSpec((1, 1, length), lambda h: (h, 0, 0)),
        ],
        out_shape=[
            jax.ShapeDtypeStruct((owners, local_heads, head_dim, tokens), BF16),
            jax.ShapeDtypeStruct((local_heads, 1, length), F32),
        ],
        compiler_params=KERNEL,
        cost_estimate=LIGHT,
    )(
        projected.reshape(3, local_heads, head_dim, length),
        scale_vec.reshape(head_dim, 1),
        segments.reshape(length, 1),
        segments.reshape(1, length),
    )
    return attended.reshape(owners, local_heads * head_dim, tokens), log_total


def attend_back_kernel(
    token_rows,
    proj_ref,
    grad_ref,
    lse_ref,
    scale_ref,
    col_ref,
    row_ref,
    out_ref,
    scale_grad_ref,
    keys_acc,
    values_acc,
):
    length = proj_ref.shape[-1]
    scale = scale_ref[...]
    query_pre = proj_ref[0, 0]
    queries = (query_pre * scale).astype(BF16)
    keys_t = proj_ref[1, 0].astype(BF16)
    keys = proj_ref[1, 0].T.astype(BF16)
    values = proj_ref[2, 0].T.astype(BF16)
    keys_acc[...] = jnp.zeros_like(keys_acc)
    values_acc[...] = jnp.zeros_like(values_acc)
    scale_grad = jnp.zeros((scale.shape[0], 1), F32)
    for first, parts in token_places(length, grad_ref.shape[0], token_rows):
        end = first + Q_ROWS
        block = queries[:, first:end]
        grad = jnp.concatenate(
            [grad_ref[owner, 0, :, at : at + token_rows] for _, owner, at in parts], axis=1
        )
        scores = jnp.dot(keys[:end], block, preferred_element_type=F32)
        allowed = allowed_keys(col_ref[...], row_ref[:, first:end], first)
        scores = jnp.where(allowed, scores, MASKED_SCORE)
        probs = jnp.exp(scores - lse_ref[0, :, first:end])
        probs_grad = jnp.dot(values[:end], grad, preferred_element_type=F32)
        row_dot = jnp.sum(probs_grad * probs, axis=0, keepdims=True)
        scores_low = (probs * (probs_grad - row_dot)).astype(BF16)
        values_acc[:, :end] += lax.dot_general(
            grad, probs.astype(BF16), NT, preferred_element_type=F32
        )
        keys_acc[:, :end] += lax.dot_general(
            block, scores_low, NT, preferred_element_type=F32
        )
        query_bar = jnp.dot(keys_t[:, :end], scores_low, preferred_element_type=F32)
        query_bar = query_bar.astype(BF16).astype(F32)
        scale_grad += jnp.sum(query_bar * query_pre[:, first:end], axis=1, keepdims=True)
        out_ref[0, 0, :, first:end] = (query_bar * scale).astype(BF16)
    out_ref[1, 0] = keys_acc[...].astype(BF16)
    out_ref[2, 0] = values_acc[...].astype(BF16)
    spread = jnp.broadcast_to(scale_grad, scale_grad_ref.shape)

    @pl.when(pl.program_id(0) == 0)
    def _():
        scale_grad_ref[...] = spread

    @pl.when(pl.program_id(0) > 0)
    def _():
        scale_grad_ref[...] += spread


def attend_back_rows(projected, attended_grad, log_total, scale_vec, segments, token_rows):
    head_dim = scale_vec.shape[0]
    length = projected.shape[1]
    local_heads = projected.shape[0] // 3 // head_dim
    owners, _, tokens = attended_grad.shape
    lanes = 128
    grads, scale_grad = pl.pallas_call(
        functools.partial(attend_back_kernel, token_rows),
        grid=(local_heads,),
        in_specs=[
            pl.BlockSpec((3, 1, head_dim, length), lambda h: (0, h, 0, 0)),
            pl.BlockSpec((owners, 1, head_dim, tokens), lambda h: (0, h, 0, 0)),
            pl.BlockSpec((1, 1, length), lambda h: (h, 0, 0)),
            pl.BlockSpec((head_dim, 1), lambda h: (0, 0)),
            pl.BlockSpec((length, 1), lambda h: (0, 0)),
            pl.BlockSpec((1, length), lambda h: (0, 0)),
        ],
        out_specs=[
            pl.BlockSpec((3, 1, head_dim, length), lambda h: (0, h, 0, 0)),
            pl.BlockSpec((head_dim, lanes), lambda h: (0, 0)),
        ],
        out_shape=[
            pltpu.HBM((3, local_heads, head_dim, length), BF16),
            pltpu.HBM((head_dim, lanes), F32),
        ],
        scratch_shapes=[
            pltpu.VMEM((head_dim, length), F32),
            pltpu.VMEM((head_dim, length), F32),
        ],
        compiler_params=KERNEL,
        cost_estimate=LIGHT,
    )(
        *in_hbm(
            projected.reshape(3, local_heads, head_dim, length),
            attended_grad.reshape(owners, local_heads, head_dim, tokens),
        ),
        log_total,
        scale_vec.reshape(head_dim, 1),
        segments.reshape(length, 1),
        segments.reshape(1, length),
    )
    return grads.reshape(3 * local_heads * head_dim, length), scale_grad[:, 0]


def dense_grad_kernel(
    core_ref, attended_ref, normed_ref, active_ref, out_bar, up_bar, down_bar,
    own_ref, other_ref, normed_t, active_t,
):
    tile = pl.program_id(0)
    rows, width = 8 * own_ref.shape[3], out_bar.shape[1]

    @pl.when(tile == 0)
    def _():
        normed_t[...] = normed_ref[...].astype(F32).T.astype(BF16)
        active_t[...] = active_ref[...].astype(F32).T.astype(BF16)

    start = pl.multiple_of(tile * rows, rows)
    first_core = core_ref[2] == 0
    lefts = (attended_ref, normed_t, active_t)
    for i, (left, right) in enumerate(zip(lefts, (out_bar, up_bar, down_bar))):
        grad = jnp.dot(left[pl.ds(start, rows), :], right[...], preferred_element_type=F32)
        grad = grad.reshape(2, 2, 2, rows // 8, width)
        one, two = grad[:, :, 0], grad[:, :, 1]
        own_ref[:, :, 0, :, i * width : (i + 1) * width] = jnp.where(
            first_core, one, two
        ).astype(BF16)
        other_ref[:, :, 0, :, i * width : (i + 1) * width] = jnp.where(
            first_core, two, one
        ).astype(BF16)


def dense_grads(attended_t, normed, active, out_bar, up_bar, down_bar):
    width, tokens = attended_t.shape
    own = width // 32
    whole = pl.BlockSpec((tokens, width), lambda i, core: (0, 0))
    rows = pl.BlockSpec((2, 2, 1, own, 3 * width), lambda i, core: (0, 0, i, 0, 0))
    shape = pltpu.HBM((2, 2, 4, own, 3 * width), BF16)
    return pl.pallas_call(
        dense_grad_kernel,
        grid_spec=pltpu.PrefetchScalarGridSpec(
            num_scalar_prefetch=1,
            grid=(4,),
            in_specs=[pl.BlockSpec((width, tokens), lambda i, core: (0, 0))] + [whole] * 5,
            out_specs=[rows, rows],
            scratch_shapes=[pltpu.VMEM((width, tokens), BF16)] * 2,
        ),
        out_shape=[shape, shape],
        compiler_params=KERNEL,
        cost_estimate=LIGHT,
    )(place(), *in_hbm(attended_t, normed, active, out_bar, up_bar, down_bar))


def place():
    head = lax.axis_index("head")
    return jnp.stack([lax.axis_index("blk"), head // 2, head % 2]).astype(jnp.int32)


def assemble_kernel(place_ref, *refs):
    pieces, whole_ref = refs[:10], refs[10]
    half = whole_ref.shape[-1] // 2
    blk, row, core = place_ref[0], place_ref[1], place_ref[2]
    for i in range(2):
        at_core = core if i == 0 else 1 - core
        own, across, beside, one, two = pieces[5 * i : 5 * i + 5]
        whole_ref[0, blk, row, at_core] = own[0]
        whole_ref[0, 1 - blk, row, at_core] = across[0]
        whole_ref[0, blk, 1 - row, at_core] = beside[0]
        whole_ref[0, 1 - blk, 1 - row, at_core, :, :half] = one[0]
        whole_ref[0, 1 - blk, 1 - row, at_core, :, half:] = two[0]


def assemble(pieces):
    batch, own, columns = pieces[0].shape
    specs = [
        pl.BlockSpec((1, own, piece.shape[-1]), lambda i, at: (i, 0, 0))
        for piece in pieces
    ]
    whole = pl.pallas_call(
        assemble_kernel,
        grid_spec=pltpu.PrefetchScalarGridSpec(
            num_scalar_prefetch=1,
            grid=(batch,),
            in_specs=specs,
            out_specs=pl.BlockSpec((1, 2, 2, 2, own, columns), lambda i, at: (i, 0, 0, 0, 0, 0)),
        ),
        out_shape=jax.ShapeDtypeStruct((batch, 2, 2, 2, own, columns), BF16),
        compiler_params=KERNEL,
        cost_estimate=LIGHT,
    )(place(), *pieces)
    return whole.reshape(-1, columns)


def assemble_columns_kernel(place_ref, along_ref, across_ref, whole_ref, *extra_ref):
    blk = place_ref[0]
    columns = whole_ref.shape[-1]
    whole_ref[0, blk] = along_ref[0, :, :columns]
    whole_ref[0, 1 - blk] = across_ref[0, :, :columns]
    for extra in extra_ref:
        extra[0, blk] = along_ref[0, :, columns:]
        extra[0, 1 - blk] = across_ref[0, :, columns:]


def assemble_columns(along, across, columns):
    batch, own, both = along.shape
    rows = pl.BlockSpec((1, own, both), lambda i, at: (i, 0, 0))
    shapes = [(batch, 2, own, columns)]
    if both > columns:
        shapes.append((batch, 2, own, both - columns))
    parts = pl.pallas_call(
        assemble_columns_kernel,
        grid_spec=pltpu.PrefetchScalarGridSpec(
            num_scalar_prefetch=1,
            grid=(batch,),
            in_specs=[rows, rows],
            out_specs=[pl.BlockSpec((1,) + s[1:], lambda i, at: (i, 0, 0, 0)) for s in shapes],
        ),
        out_shape=[pltpu.HBM(s, BF16) for s in shapes],
        compiler_params=KERNEL,
        cost_estimate=LIGHT,
    )(place(), *in_hbm(along, across))
    return [part.reshape(-1, part.shape[-1]) for part in parts]


def assemble_wide_kernel(place_ref, along_ref, across_ref, whole_ref):
    blk = place_ref[0]
    own, columns = along_ref.shape[1], whole_ref.shape[-1]
    for i in range(along_ref.shape[-1] // columns):
        place, part = slice(i * own, (i + 1) * own), slice(i * columns, (i + 1) * columns)
        whole_ref[0, blk, place, :] = along_ref[0, :, part]
        whole_ref[0, 1 - blk, place, :] = across_ref[0, :, part]


def assemble_wide(along, across, columns):
    batch, own, wide = along.shape
    rows = own * (wide // columns)
    piece = pl.BlockSpec((1, own, wide), lambda i, at: (i, 0, 0))
    whole = pl.pallas_call(
        assemble_wide_kernel,
        grid_spec=pltpu.PrefetchScalarGridSpec(
            num_scalar_prefetch=1,
            grid=(batch,),
            in_specs=[piece, piece],
            out_specs=pl.BlockSpec((1, 2, rows, columns), lambda i, at: (i, 0, 0, 0)),
        ),
        out_shape=pltpu.HBM((batch, 2, rows, columns), BF16),
        compiler_params=KERNEL,
        cost_estimate=LIGHT,
    )(place(), *in_hbm(along, across))
    return whole.reshape(-1, columns)


def project_kernel(with_norm, place_ref, *refs):
    pieces, (gain_ref, weight_ref, normed_ref, projected_ref) = refs[:4], refs[4:]
    head = place_ref[1] * 2 + place_ref[2]
    rows = pieces[0].shape[0]
    for i, piece in enumerate(pieces):
        value = piece[...]
        if with_norm:
            stream = value.astype(F32)
            factor = lax.rsqrt(jnp.mean(stream * stream, axis=-1, keepdims=True) + EPSILON)
            value = (stream * factor * gain_ref[...]).astype(BF16)
        normed_ref[pl.ds(pl.multiple_of((head ^ i) * rows, rows), rows), :] = value
    projected = jnp.dot(normed_ref[...], weight_ref[...], preferred_element_type=F32)
    projected_ref[...] = projected.T


def project(pieces, gain, weight, with_norm, token_rows):
    tokens, width = pieces[0].shape
    length, columns = 4 * tokens, weight.shape[1]
    groups = tokens // token_rows
    piece = pl.BlockSpec((token_rows, width), lambda g, at: (g, 0))
    return pl.pallas_call(
        functools.partial(project_kernel, with_norm),
        grid_spec=pltpu.PrefetchScalarGridSpec(
            num_scalar_prefetch=1,
            grid=(groups,),
            in_specs=[piece] * 4
            + [
                pl.BlockSpec((1, width), lambda g, at: (0, 0)),
                pl.BlockSpec((width, columns), lambda g, at: (0, 0)),
            ],
            out_specs=[
                pl.BlockSpec((4 * token_rows, width), lambda g, at: (g, 0)),
                pl.BlockSpec((columns, 4 * token_rows), lambda g, at: (0, g)),
            ],
        ),
        out_shape=[
            pltpu.HBM((length, width), BF16),
            pltpu.HBM((columns, length), F32),
        ],
        compiler_params=KERNEL,
        cost_estimate=LIGHT,
    )(place(), *in_hbm(*pieces), gain.reshape(1, width), *in_hbm(weight))


def project_back_kernel(
    place_ref, bars_ref, weight_ref, normed_ref, own_ref, other_ref, grad_ref, bars_t
):
    @pl.when(pl.program_id(0) == 0)
    def _():
        bars_t[...] = bars_ref[...].astype(F32).T.astype(BF16)

    upper = lax.dot_general(bars_t[...], weight_ref[...], NT, preferred_element_type=F32)
    upper = upper.reshape(2, 2, 2, -1, upper.shape[-1])
    first_core = place_ref[2] == 0
    one, two = upper[:, :, 0], upper[:, :, 1]
    own_ref[...] = jnp.where(first_core, one, two)
    other_ref[...] = jnp.where(first_core, two, one).astype(BF16)
    grad = lax.dot_general(normed_ref[...], bars_t[...], TN, preferred_element_type=F32)
    grad_ref[...] = grad.astype(BF16)


def project_back(bars, weight, normed, token_rows):
    columns, length = bars.shape
    width = weight.shape[0]
    tile = width // 2
    quarter = pl.BlockSpec((2, 2, token_rows, tile), lambda i, at: (0, 0, 0, i))
    return pl.pallas_call(
        project_back_kernel,
        grid_spec=pltpu.PrefetchScalarGridSpec(
            num_scalar_prefetch=1,
            grid=(2,),
            in_specs=[
                pl.BlockSpec((columns, length), lambda i, at: (0, 0)),
                pl.BlockSpec((tile, columns), lambda i, at: (i, 0)),
                pl.BlockSpec((length, tile), lambda i, at: (0, i)),
            ],
            out_specs=[quarter, quarter, pl.BlockSpec((tile, columns), lambda i, at: (i, 0))],
            scratch_shapes=[pltpu.VMEM((length, columns), BF16)],
        ),
        out_shape=[
            pltpu.HBM((2, 2, token_rows, width), F32),
            pltpu.HBM((2, 2, token_rows, width), BF16),
            pltpu.HBM((width, columns), BF16),
        ],
        compiler_params=KERNEL,
        cost_estimate=LIGHT,
    )(place(), *in_hbm(bars, weight, normed))


def rows_back_kernel(place_ref, bars_ref, weight_ref, own_ref, other_ref, bars_t):
    @pl.when(pl.program_id(0) == 0)
    def _():
        bars_t[...] = bars_ref[...].astype(F32).T.astype(BF16)

    upper = lax.dot_general(bars_t[...], weight_ref[...], NT, preferred_element_type=F32)
    upper = upper.reshape(2, 2, 2, -1, upper.shape[-1])
    first_core = place_ref[2] == 0
    one, two = upper[:, :, 0], upper[:, :, 1]
    own_ref[...] = jnp.where(first_core, one, two)
    other_ref[...] = jnp.where(first_core, two, one).astype(BF16)


def rows_back(bars, weight, token_rows):
    columns, length = bars.shape
    width = weight.shape[0]
    tile = width // 2
    quarter = pl.BlockSpec((2, 2, token_rows, tile), lambda i, at: (0, 0, 0, i))
    return pl.pallas_call(
        rows_back_kernel,
        grid_spec=pltpu.PrefetchScalarGridSpec(
            num_scalar_prefetch=1,
            grid=(2,),
            in_specs=[
                pl.BlockSpec((columns, length), lambda i, at: (0, 0)),
                pl.BlockSpec((tile, columns), lambda i, at: (i, 0)),
            ],
            out_specs=[quarter, quarter],
            scratch_shapes=[pltpu.VMEM((length, columns), BF16)],
        ),
        out_shape=[
            pltpu.HBM((2, 2, token_rows, width), F32),
            pltpu.HBM((2, 2, token_rows, width), BF16),
        ],
        compiler_params=KERNEL,
        cost_estimate=LIGHT,
    )(place(), *in_hbm(bars, weight))


def weight_back_kernel(bars_ref, normed_ref, grad_ref):
    grad = jnp.dot(bars_ref[...], normed_ref[...], preferred_element_type=F32)
    grad_ref[...] = grad.T.astype(BF16)


def weight_back(bars, normed):
    columns, length = bars.shape
    width = normed.shape[1]
    tile = width // 5
    return pl.pallas_call(
        weight_back_kernel,
        grid=(5,),
        in_specs=[
            pl.BlockSpec((columns, length), lambda i: (0, 0)),
            pl.BlockSpec((length, tile), lambda i: (0, i)),
        ],
        out_specs=pl.BlockSpec((tile, columns), lambda i: (i, 0)),
        out_shape=pltpu.HBM((width, columns), BF16),
        compiler_params=KERNEL,
        cost_estimate=LIGHT,
    )(*in_hbm(bars, normed))


def tied(*arrays):
    return lax.optimization_barrier(arrays)


def swapped(array, axis, mask):
    size = lax.axis_size(axis)
    return lax.ppermute(array, axis, [(i, i ^ mask) for i in range(size)])


def pick(array, index, axis=0):
    return lax.dynamic_index_in_dim(array, index, axis, keepdims=False)


def swap_halves(array):
    me = lax.axis_index("blk")
    got = swapped(pick(array, 1 - me), "blk", 1)
    kept = pick(array, me)
    return jnp.stack([jnp.where(me == 0, kept, got), jnp.where(me == 0, got, kept)])


def scatter_row(halves):
    row = lax.axis_index("head") // 2
    got = swapped(pick(halves, 1 - row, 1).astype(BF16), "head", 2).astype(F32)
    return (pick(halves, row, 1) + got).reshape(-1, halves.shape[-1])


def over_head(parts):
    return lax.all_to_all(parts, "head", split_axis=0, concat_axis=0, tiled=True)


def qkv_columns(rows, extra):
    own, width = rows.shape
    part = width // 3 // 4
    sent = rows.reshape(own, 3, 4, part).transpose(2, 0, 1, 3).reshape(4, own, 3 * part)
    if extra is not None:
        sent = jnp.concatenate([sent, jnp.broadcast_to(extra[None], (4,) + extra.shape)], axis=2)
    return over_head(sent)


def along_batch(piece):
    return lax.all_gather(piece, "batch", axis=0, tiled=False)


def other_core(array):
    return swapped(array, "head", 1)


def to_beside(across):
    return swapped(across[..., : across.shape[-1] // 2], "head", 2)


def to_across(beside):
    return swapped(beside[..., beside.shape[-1] // 2 :], "blk", 1)


def over_batch(parts):
    return lax.psum_scatter(parts.astype(BF16), "batch", scatter_dimension=0, tiled=False)


def across_sum(halves):
    blk = lax.axis_index("blk")
    got = swapped(pick(halves, 1 - blk), "blk", 1).astype(F32)
    return (pick(halves, blk).astype(F32) + got).astype(BF16)


def columns_to_rows(moved):
    rows = moved.shape[1]
    return moved.reshape(4, rows, 3, -1).transpose(1, 2, 0, 3).reshape(rows, -1).astype(F32)


def quarter(parts, blk, row):
    one, two = (pick(pick(part, blk), row).astype(F32) for part in parts)
    return one + two


def diagonal_rows(parts):
    blk, row = place()[:2]
    rows = quarter(parts, 1 - blk, 1 - row).astype(BF16)
    half = rows.shape[-1] // 2
    return rows[..., :half], rows[..., half:]


def neighbour_rows(parts, one, two):
    blk, row = place()[:2]
    half = one.shape[-1]
    across, beside = quarter(parts, 1 - blk, row), quarter(parts, blk, 1 - row)
    across = jnp.concatenate([across[..., :half], across[..., half:] + two.astype(F32)], axis=-1)
    beside = jnp.concatenate([beside[..., :half] + one.astype(F32), beside[..., half:]], axis=-1)
    return across.astype(BF16), beside.astype(BF16)


def sent_beside_and_across(across, beside):
    return swapped(across, "blk", 1), swapped(beside, "head", 2)


def heads_grad(weight, out_bar):
    return dot_cols(weight, out_bar).astype(BF16).reshape(4, -1, out_bar.shape[0])


def own_sum(parts, across, beside):
    blk, row = place()[:2]
    return quarter(parts, blk, row) + across.astype(F32) + beside.astype(F32)


def sum_over(array, *hops):
    for axis, mask in hops:
        array = array + swapped(array, axis, mask)
    return array


def gain_back(weight, weight_grad, gain):
    return jnp.sum(weight.astype(F32) * weight_grad, axis=-1) / gain.astype(F32)


def lower_of(upper, stream, factor, gain):
    return norm_back(upper, stream, factor, gain)[0]


def spread_device(
    tokens,
    segments,
    qkv_weight,
    out_weight,
    up_weight,
    down_weight,
    attn_gain,
    mlp_gain,
    scale_param,
    cotangent,
):
    layers, head_dim = scale_param.shape
    _, token_rows, width = tokens.shape
    scale_vecs = SCALE_BASE / math.sqrt(head_dim) * jax.nn.softplus(scale_param)
    segments = pick(segments, lax.axis_index("blk"))
    own_gains = jnp.concatenate([attn_gain, mlp_gain], axis=0)

    part3 = 3 * width // 4
    dense_own = [
        jnp.concatenate([out_weight[i], up_weight[i], down_weight[i]], axis=1) for i in (0, 1)
    ]

    first = swap_halves(tokens).reshape(-1, width)
    columns = qkv_columns(qkv_weight[0], own_gains.T)
    columns, first = tied(columns.reshape(-1, columns.shape[-1]), first)
    stream = first.astype(F32)
    along = along_batch(columns)
    far, near = swapped(first, "head", 2), other_core(first)
    both = other_core(far)
    upper = swap_halves(cotangent)
    along, near, far, both, dense_near, upper = tied(
        along, near, far, both, dense_own[0], upper
    )
    token_pieces = (first, near, far, both)
    dense_near = along_batch(dense_near)
    qkv_across = swapped(along, "blk", 1)
    next_columns = jnp.concatenate(list(qkv_columns(qkv_weight[1], None)), axis=1)
    qkv_across, dense_near, next_columns = tied(qkv_across, dense_near, next_columns)
    across, beside = swapped(dense_near, "blk", 1), swapped(dense_near, "head", 2)
    next_both = along_batch(jnp.stack([next_columns, dense_own[1]]))
    weight, gains = assemble_columns(along, qkv_across, part3)
    qkvs = [weight]
    gains = gains.T.astype(F32)

    kept, denses = [], []
    for layer in range(layers):
        normed, factor_one = normalize(stream, gains[layer])
        if layer == 1:
            normed = normed.astype(BF16)
            far, near = swapped(normed, "head", 2), other_core(normed)
            far, next_across, dense_next = tied(far, next_across, dense_next)
            across, beside = swapped(dense_next, "blk", 1), swapped(dense_next, "head", 2)
            token_pieces = (normed, near, far, other_core(far))
            qkvs.append(assemble_wide(next_along, next_across, part3))
        normed_all, projected = project(
            token_pieces, gains[layer], qkvs[layer], layer == 0, token_rows
        )
        attended, log_total = attend_rows(
            projected, scale_vecs[layer], segments, 4, token_rows
        )
        attended, across, beside = tied(attended, across, beside)
        one, two = to_beside(across), to_across(beside)
        if layer == 0:
            two, next_both = tied(two, next_both)
            next_along, dense_next = next_both[:, 0], next_both[:, 1]
            next_across = swapped(next_along, "blk", 1)
            attended_t, one, two = tied(over_head(attended), one, two)
        else:
            dense_near = dense_next
            attended_t, one, two = tied(over_head(attended), one, two)
        pieces = (dense_near, across, beside, one, two)
        pieces += tuple(other_core(piece) for piece in pieces)
        attended_t = attended_t.reshape(width, -1)
        denses.append(assemble(pieces))
        dense = denses[layer]
        out_w, up_w, down_w = dense[:, :width], dense[:, width:-width], dense[:, -width:]
        middle = stream + dot_rows(attended_t, out_w)
        normed_two, factor_two = normalize(middle, gains[layers + layer])
        normed_two = normed_two.astype(BF16)
        hidden = dot(normed_two, up_w)
        active = (hidden * jax.nn.sigmoid(hidden)).astype(BF16)
        kept.append(
            (
                stream, factor_one, normed_all, projected, log_total, attended_t, middle,
                factor_two, normed_two, hidden, active,
            )
        )
        stream = middle + dot(active, down_w)
    layer_out = swap_halves(stream.astype(BF16).reshape(tokens.shape))
    upper = upper.reshape(-1, width).astype(F32)

    scale_grads = [None] * layers
    for layer in reversed(range(layers)):
        (
            stream, factor_one, normed_all, projected, log_total, attended_t, middle,
            factor_two, normed_two, hidden, active,
        ) = kept[layer]
        qkv, dense = qkvs[layer], denses[layer]
        out_w, up_w, down_w = dense[:, :width], dense[:, width:-width], dense[:, -width:]
        down_bar = upper.astype(BF16)
        gate = jax.nn.sigmoid(hidden)
        up_bar = (
            dot_cols(down_bar, down_w) * gate * (1.0 + hidden * (1.0 - gate))
        ).astype(BF16)
        middle_grad = upper + lower_of(
            dot_cols(up_bar, up_w), middle, factor_two, gains[layers + layer]
        )
        out_bar = middle_grad.astype(BF16)
        if layer == 0:
            attended_grad = over_head(heads_grad(out_w, out_bar))
            grads, others = dense_grads(attended_t, normed_two, active, out_bar, up_bar, down_bar)
            others, diagonal = tied(others, diagonal)
            others, rows = tied(others, neighbour_rows(cored, *diagonal))
            sent = sent_beside_and_across(*rows)
            attended_grad, others, z_sum = tied(attended_grad, others, z_sum)
            others = other_core(others)
            last = cored
            z_across = across_sum(z_sum)
        else:
            attended_grad = over_head(heads_grad(out_w, out_bar))
            grads, others = dense_grads(attended_t, normed_two, active, out_bar, up_bar, down_bar)
            attended_grad, others, layer_out = tied(attended_grad, others, layer_out)
            others = other_core(others)
        bars, scale_grads[layer] = attend_back_rows(
            projected, attended_grad, log_total, scale_vecs[layer], segments, token_rows
        )
        if layer == 0:
            bars, others, z_across = tied(bars, others, z_across)
            moved = over_head(z_across.reshape(4, -1, z_across.shape[-1]))
            qkv_grad = weight_back(bars, normed_all)
            bars, qkv_grad = tied(bars, qkv_grad)
            z_sum = over_batch(qkv_grad.reshape(4, 2, -1, qkv_grad.shape[-1]))
            cored = (grads, others)
            bars, rows = tied(bars, diagonal_rows(cored))
            diagonal = sent_beside_and_across(*rows)
            halves, to_core = rows_back(bars, qkv, token_rows)
            halves, to_core, diagonal, sent = tied(halves, to_core, diagonal, sent)
            halves, summed = tied(halves, own_sum(last, *sent))
            summed = over_batch(summed)
            halves, to_core, rows = tied(halves, to_core, neighbour_rows(cored, *diagonal))
            sent = sent_beside_and_across(*rows)
            halves = halves + other_core(to_core).astype(F32)
            scale_sum = sum_over(jnp.stack(scale_grads), ("head", 1), ("batch", 1), ("batch", 2))
            halves, sent, z_sum, scale_sum, moved = tied(halves, sent, z_sum, scale_sum, moved)
            halves, own = tied(halves, own_sum(cored, *sent))
            dense_first = over_batch(own)
            normed_grad = scatter_row(halves)
            z_across = across_sum(z_sum)
            z_across = over_head(z_across.reshape(4, -1, z_across.shape[-1]))
            z_across, dense_first = tied(z_across, dense_first)
            dense_grad = [dense_first, summed]
            qkv_grads = [columns_to_rows(z_across), columns_to_rows(moved)]
        else:
            bars, others = tied(bars, others)
            cored = (grads, others)
            halves, to_core, qkv_grad = project_back(bars, qkv, normed_all, token_rows)
            z_sum = over_batch(qkv_grad.reshape(4, 2, -1, qkv_grad.shape[-1]))
            to_core, others = tied(to_core, others)
            halves = halves + other_core(to_core).astype(F32)
            halves, rows = tied(halves, diagonal_rows((grads, others)))
            diagonal = sent_beside_and_across(*rows)
            normed_grad = scatter_row(halves)
        upper = middle_grad + lower_of(normed_grad, stream, factor_one, gains[layer])
    input_grad = swap_halves(upper.astype(BF16).reshape(tokens.shape)).astype(F32)
    scale_total = sum_over(scale_sum, ("head", 2), ("blk", 1))
    scale_grad = scale_total * (SCALE_BASE / math.sqrt(head_dim)) * jax.nn.sigmoid(scale_param)
    dense_all = jnp.stack([part.astype(F32) for part in dense_grad])
    qkv_all = jnp.stack(qkv_grads)
    up_all = dense_all[:, :, width:-width]
    return (
        layer_out,
        input_grad,
        qkv_all,
        dense_all[:, :, :width],
        up_all,
        dense_all[:, :, -width:],
        gain_back(qkv_weight, qkv_all, attn_gain),
        gain_back(up_weight, up_all, mlp_gain),
        scale_grad,
    )


def per_device(*args):
    tokens, segments = args[0], args[1]
    sizes = tuple(lax.axis_size(axis) for axis in ALL)
    heads = tokens.shape[2] // args[8].shape[1]
    spread = (
        sizes == (4, 2, 4)
        and tokens.shape[0] == 2
        and args[2].shape[0] == 2
        and tokens.shape[1] % 128 == 0
        and Q_ROWS % tokens.shape[1] == 0
        and segments.shape[1] <= WINDOW
        and segments.shape[1] % Q_ROWS == 0
        and heads % 4 == 0
        and tokens.shape[2] % 256 == 0
    )
    return spread_device(*args) if spread else general_device(*args)


def solution(mesh):
    rows = P(None, ALL, None)
    by_token = P("batch", ("blk", "head"), None)
    return jax.shard_map(
        per_device,
        mesh=mesh,
        in_specs=(
            by_token, P("batch", None), rows, rows, rows, rows, P(None, ALL), P(None, ALL), P(),
            by_token,
        ),
        out_specs=(
            by_token, by_token, rows, rows, rows, rows, P(None, ALL), P(None, ALL), P(),
        ),
        check_vma=False,
    )
```

```python
import functools
import math

import jax
import jax.numpy as jnp
from jax import lax
from jax.experimental import pallas as pl
from jax.experimental.pallas import tpu as pltpu
from jax.sharding import PartitionSpec as P

WINDOW = 1024
EPSILON = 1e-06
SCALE_BASE = 1.4426950408889634
MASKED_SCORE = -1e30

ALL = ("batch", "blk", "head")
REST = ("batch", "blk")
F32 = jnp.float32
BF16 = jnp.bfloat16


def shifted(block, axis, distance):
    devices = range(lax.axis_size(axis))
    route = [(i - distance, i) for i in devices if i - distance in devices]
    return lax.ppermute(block, axis, route)


NT = (((1,), (1,)), ((), ()))
TN = (((0,), (0,)), ((), ()))


def dot(left, right):
    return jnp.dot(left, right, preferred_element_type=F32)


def dot_rows(left, right):
    return lax.dot_general(left, right, (((0,), (0,)), ((), ())), preferred_element_type=F32)


def dot_cols(left, right):
    return lax.dot_general(left, right, (((1,), (1,)), ((), ())), preferred_element_type=F32)


def normalize(stream, gain):
    factor = lax.rsqrt(jnp.mean(stream * stream, axis=-1, keepdims=True) + EPSILON)
    return stream * factor * gain, factor


def norm_back(upper, stream, factor, gain):
    inner = upper * gain
    gain_grad = jnp.sum(upper * stream * factor, axis=0)
    lower = factor * inner - stream * factor * factor * factor * jnp.mean(
        inner * stream, axis=-1, keepdims=True
    )
    return lower, gain_grad


class Plan:
    def __init__(self, tokens):
        self.seqs, self.rows, self.width = tokens.shape
        self.heads = lax.axis_size("head")
        self.blks = lax.axis_size("blk")
        self.block = self.rows * self.heads
        self.whole = self.seqs % self.blks == 0
        if self.whole:
            self.groups, self.own_seqs = self.blks, self.seqs // self.blks
            self.reach = 0
        else:
            self.groups, self.own_seqs = 1, self.seqs
            self.reach = min((WINDOW - 1) // self.block + 1, self.blks - 1)
        self.length = self.groups * self.block
        self.tokens = self.seqs * self.rows


def to_plan(plan, array):
    if plan.whole and plan.blks > 1:
        array = lax.all_to_all(array, "blk", split_axis=0, concat_axis=0, tiled=True)
    return array.reshape(plan.tokens, plan.width)


def from_plan(plan, flat):
    array = flat.reshape(plan.seqs, plan.rows, plan.width)
    if plan.whole and plan.blks > 1:
        array = lax.all_to_all(array, "blk", split_axis=0, concat_axis=0, tiled=True)
    return array


def in_sequence(plan, by_head, width):
    parts = by_head.reshape(plan.heads, plan.groups, plan.own_seqs, plan.rows, width)
    return parts.transpose(2, 1, 0, 3, 4).reshape(-1, width)


def by_owner(plan, rows, width):
    parts = rows.reshape(plan.own_seqs, plan.groups, plan.heads, plan.rows, width)
    return parts.transpose(2, 1, 0, 3, 4).reshape(plan.heads, plan.tokens, width)


def gather_tokens(plan, rows):
    moved = lax.all_gather(rows, "head", axis=0, tiled=False)
    return in_sequence(plan, moved, rows.shape[-1])


def scatter_tokens(plan, rows):
    width = rows.shape[-1]
    return lax.psum_scatter(
        by_owner(plan, rows.astype(BF16), width), "head", scatter_dimension=0, tiled=False
    ).astype(F32)


def heads_to_tokens(plan, rows):
    part = rows.shape[-1]
    moved = lax.all_to_all(
        by_owner(plan, rows, part), "head", split_axis=0, concat_axis=0, tiled=True
    )
    return moved.transpose(1, 0, 2).reshape(plan.tokens, plan.heads * part)


def tokens_to_heads(plan, rows):
    part = rows.shape[-1] // plan.heads
    sent = rows.reshape(plan.tokens, plan.heads, part).transpose(1, 0, 2)
    moved = lax.all_to_all(sent, "head", split_axis=0, concat_axis=0, tiled=True)
    return in_sequence(plan, moved, part)


def gather_qkv(rows):
    own, width = rows.shape
    heads = lax.axis_size("head")
    part = width // 3 // heads
    sent = rows.reshape(own, 3, heads, part).transpose(2, 0, 1, 3).reshape(heads, own, 3 * part)
    moved = lax.all_to_all(sent, "head", split_axis=0, concat_axis=0, tiled=True)
    full = lax.all_gather(moved, REST, axis=0, tiled=True)
    return full.reshape(-1, 3 * part)


def scatter_qkv(grad):
    heads = lax.axis_size("head")
    part = grad.shape[1] // 3
    summed = lax.psum_scatter(grad.astype(BF16), REST, scatter_dimension=0, tiled=True)
    own = summed.shape[0] // heads
    moved = lax.all_to_all(
        summed.reshape(heads, own, 3 * part), "head", split_axis=0, concat_axis=0, tiled=True
    )
    return (
        moved.reshape(heads, own, 3, part)
        .transpose(1, 2, 0, 3)
        .reshape(own, 3 * heads * part)
        .astype(F32)
    )


def window_mask(plan, segments, block_index):
    key_count = plan.length + plan.reach * plan.block
    if plan.whole:
        query_segs, key_segs = segments, segments
    else:
        leading = jnp.full((plan.own_seqs, plan.reach * plan.block), -1, jnp.int32)
        padded = jnp.concatenate([leading, segments], axis=1)
        start = block_index * plan.block
        query_segs = lax.dynamic_slice_in_dim(segments, start, plan.block, 1)
        key_segs = lax.dynamic_slice_in_dim(padded, start, key_count, 1)
    query_place = jnp.arange(plan.length, dtype=jnp.int32)[:, None] + plan.reach * plan.block
    key_place = jnp.arange(key_count, dtype=jnp.int32)[None, :]
    near = (key_place <= query_place) & (query_place - key_place < WINDOW)
    return (key_segs[:, None, :] == query_segs[:, :, None]) & near[None]


def with_earlier(plan, own):
    arrived = [own]
    for _ in range(plan.reach):
        arrived.append(shifted(arrived[-1], "blk", 1))
    return jnp.concatenate(arrived[::-1], axis=1) if plan.reach else own


def to_earlier(plan, grads):
    if not plan.reach:
        return grads
    block = plan.block
    total = grads[:, :block]
    for step in range(1, plan.reach + 1):
        total = (
            shifted(total.astype(BF16), "blk", -1).astype(F32)
            + grads[:, step * block : (step + 1) * block]
        )
    return total


def scores_of(queries, keys, allowed):
    scores = jnp.einsum("sqhd,skhd->shqk", queries, keys, preferred_element_type=F32)
    return jnp.where(allowed[:, None], scores, MASKED_SCORE)


def attend(queries, keys, values, allowed):
    scores = scores_of(queries, keys, allowed)
    top_score = jnp.max(scores, axis=-1, keepdims=True)
    exp_terms = jnp.exp(scores - top_score)
    totals = jnp.sum(exp_terms, axis=-1, keepdims=True)
    probs_low = (exp_terms / totals).astype(BF16)
    attended = jnp.einsum("shqk,skhd->sqhd", probs_low, values, preferred_element_type=F32)
    return attended, top_score + jnp.log(totals)


def attend_back(queries, keys, values, allowed, log_total, attended_grad):
    probs = jnp.exp(scores_of(queries, keys, allowed) - log_total)
    probs_low = probs.astype(BF16)
    values_grad = jnp.einsum(
        "shqk,sqhd->skhd", probs_low, attended_grad, preferred_element_type=F32
    )
    probs_grad = jnp.einsum("sqhd,skhd->shqk", attended_grad, values, preferred_element_type=F32)
    row_dot = jnp.sum(probs_grad * probs, axis=-1, keepdims=True)
    scores_low = (probs * (probs_grad - row_dot)).astype(BF16)
    queries_grad = jnp.einsum("shqk,skhd->sqhd", scores_low, keys, preferred_element_type=F32)
    keys_grad = jnp.einsum("shqk,sqhd->skhd", scores_low, queries, preferred_element_type=F32)
    return queries_grad, keys_grad, values_grad


def forward(plan, stream, qkv, dense, gains, scale_vec, allowed):
    width = plan.width
    head_dim = scale_vec.shape[0]
    part = qkv.shape[1] // 3
    local_heads = part // head_dim
    split = (plan.own_seqs, plan.length, local_heads, head_dim)
    out_w, up_w, down_w = dense[:, :width], dense[:, width:-width], dense[:, -width:]
    normed, factor_one = normalize(stream, gains[0])
    normed_all = gather_tokens(plan, normed.astype(BF16))
    projected = dot(normed_all, qkv)
    query_pre = projected[:, :part].reshape(split)
    queries = (query_pre * scale_vec).astype(BF16)
    keys = with_earlier(plan, projected[:, part : 2 * part].astype(BF16).reshape(split))
    values = with_earlier(plan, projected[:, 2 * part :].astype(BF16).reshape(split))
    attended_part, log_total = attend(queries, keys, values, allowed)
    attended = heads_to_tokens(plan, attended_part.astype(BF16).reshape(-1, part))
    middle = stream + dot(attended, out_w)
    normed_two, factor_two = normalize(middle, gains[1])
    normed_two = normed_two.astype(BF16)
    hidden = dot(normed_two, up_w)
    active = (hidden * jax.nn.sigmoid(hidden)).astype(BF16)
    result = middle + dot(active, down_w)
    kept = (
        stream, factor_one, normed_all, query_pre, queries, keys, values, log_total,
        attended, middle, factor_two, normed_two, hidden, active,
    )
    return result, kept


def backward(plan, upper, kept, qkv, dense, gains, scale_vec, allowed):
    (
        stream, factor_one, normed_all, query_pre, queries, keys, values, log_total,
        attended, middle, factor_two, normed_two, hidden, active,
    ) = kept
    width = plan.width
    head_dim = scale_vec.shape[0]
    part = qkv.shape[1] // 3
    out_w, up_w, down_w = dense[:, :width], dense[:, width:-width], dense[:, -width:]
    upper_low = upper.astype(BF16)
    down_grad = dot_rows(active, upper_low)
    active_grad = dot_cols(upper_low, down_w)
    gate = jax.nn.sigmoid(hidden)
    hidden_low = (active_grad * gate * (1.0 + hidden * (1.0 - gate))).astype(BF16)
    up_grad = dot_rows(normed_two, hidden_low)
    extra_two, mlp_gain_grad = norm_back(dot_cols(hidden_low, up_w), middle, factor_two, gains[1])
    middle_grad = upper + extra_two
    middle_low = middle_grad.astype(BF16)
    out_grad = dot_rows(attended, middle_low)
    dense_grad = jnp.concatenate([out_grad, up_grad, down_grad], axis=1).astype(BF16)
    dense_own = lax.psum_scatter(dense_grad, ALL, scatter_dimension=0, tiled=True)
    attended_grad = tokens_to_heads(plan, dot_cols(middle_low, out_w).astype(BF16))
    queries_grad, keys_grad, values_grad = attend_back(
        queries, keys, values, allowed, log_total, attended_grad.reshape(queries.shape)
    )
    query_bar = queries_grad.astype(BF16).astype(F32)
    scale_vec_grad = jnp.sum((query_bar * query_pre).reshape(-1, head_dim), axis=0)
    query_low = (query_bar * scale_vec).astype(BF16).reshape(-1, part)
    keys_low = to_earlier(plan, keys_grad).astype(BF16).reshape(-1, part)
    values_low = to_earlier(plan, values_grad).astype(BF16).reshape(-1, part)
    projected_low = jnp.concatenate([query_low, keys_low, values_low], axis=1)
    normed_grad = scatter_tokens(plan, dot_cols(projected_low, qkv))
    qkv_own = scatter_qkv(dot_rows(normed_all, projected_low))
    extra_one, attn_gain_grad = norm_back(normed_grad, stream, factor_one, gains[0])
    lower = middle_grad + extra_one
    return lower, qkv_own, dense_own, (attn_gain_grad, mlp_gain_grad), scale_vec_grad


def general_device(
    tokens,
    segments,
    qkv_weight,
    out_weight,
    up_weight,
    down_weight,
    attn_gain,
    mlp_gain,
    scale_param,
    cotangent,
):
    plan = Plan(tokens)
    layers, head_dim = scale_param.shape
    block_index = lax.axis_index("blk")
    scale_vecs = SCALE_BASE / math.sqrt(head_dim) * jax.nn.softplus(scale_param)
    own_gains = jnp.concatenate([attn_gain, mlp_gain], axis=0)
    gains = (
        lax.all_gather(own_gains.reshape(1, -1), ALL, axis=0, tiled=True)
        .reshape(-1, 2 * layers, attn_gain.shape[1])
        .transpose(1, 0, 2)
        .reshape(2 * layers, plan.width)
        .astype(F32)
    )
    if plan.whole:
        segments = lax.dynamic_slice_in_dim(
            segments, block_index * plan.own_seqs, plan.own_seqs, 0
        )
    allowed = window_mask(plan, segments, block_index)
    stream = to_plan(plan, tokens).astype(F32)
    qkvs, denses, kept = [], [], []
    for layer in range(layers):
        qkvs.append(gather_qkv(qkv_weight[layer]))
        own = jnp.concatenate([out_weight[layer], up_weight[layer], down_weight[layer]], axis=1)
        denses.append(lax.all_gather(own, ALL, axis=0, tiled=True))
        layer_gains = (gains[layer], gains[layers + layer])
        stream, saved = forward(
            plan, stream, qkvs[layer], denses[layer], layer_gains, scale_vecs[layer], allowed
        )
        kept.append(saved)
    layer_out = from_plan(plan, stream.astype(BF16))
    upper = to_plan(plan, cotangent).astype(F32)
    qkv_grads, dense_grads = [None] * layers, [None] * layers
    gain_grads, scale_grads = [None] * layers, [None] * layers
    for layer in reversed(range(layers)):
        layer_gains = (gains[layer], gains[layers + layer])
        upper, qkv_grads[layer], dense_grads[layer], gain_grads[layer], scale_grads[layer] = (
            backward(
                plan, upper, kept[layer], qkvs[layer], denses[layer], layer_gains,
                scale_vecs[layer], allowed,
            )
        )
    input_grad = from_plan(plan, upper.astype(BF16)).astype(F32)
    small = jnp.concatenate(
        [g[0] for g in gain_grads] + [g[1] for g in gain_grads] + scale_grads, axis=0
    )
    total = lax.psum(small, ALL)
    gain_total = total[: 2 * layers * plan.width].reshape(2 * layers, plan.width)
    owner = lax.axis_index(ALL)
    gain_rows = attn_gain.shape[1]
    own_total = lax.dynamic_slice_in_dim(gain_total, owner * gain_rows, gain_rows, 1)
    scale_total = total[2 * layers * plan.width :].reshape(layers, head_dim)
    scale_grad = scale_total * (SCALE_BASE / math.sqrt(head_dim)) * jax.nn.sigmoid(scale_param)
    dense_all = jnp.stack(dense_grads).astype(F32)
    width = plan.width
    return (
        layer_out,
        input_grad,
        jnp.stack(qkv_grads),
        dense_all[:, :, :width],
        dense_all[:, :, width:-width],
        dense_all[:, :, -width:],
        own_total[:layers],
        own_total[layers:],
        scale_grad,
    )


Q_ROWS = 256
KERNEL = pltpu.CompilerParams(vmem_limit_bytes=32 * 1024 * 1024)
LIGHT = pl.CostEstimate(flops=1 << 20, bytes_accessed=1 << 20, transcendentals=0)


def in_hbm(*arrays):
    return [pltpu.with_memory_space_constraint(array, pltpu.HBM) for array in arrays]


def allowed_keys(col, row, first):
    count = first + row.shape[1]
    key_place = lax.broadcasted_iota(jnp.int32, (count, row.shape[1]), 0)
    query_place = lax.broadcasted_iota(jnp.int32, (count, row.shape[1]), 1) + first
    return (col[:count] == row) & (key_place <= query_place)


def allowed_piece(col, row, start, first):
    same = col == row
    if start + col.shape[0] <= first:
        return same
    key_place = lax.broadcasted_iota(jnp.int32, same.shape, 0) + start
    return same & (key_place <= lax.broadcasted_iota(jnp.int32, same.shape, 1) + first)


def token_places(length, heads, token_rows, block_rows=Q_ROWS):
    for first in range(0, length, block_rows):
        parts = []
        for start in range(0, block_rows, token_rows):
            place = (first + start) // token_rows
            parts.append((start, place % heads, place // heads * token_rows))
        yield first, parts


FORWARD_ROWS, FORWARD_KEYS = 1024, 512


def attend_kernel(token_rows, proj_ref, scale_ref, col_ref, row_ref, out_ref, lse_ref):
    length = proj_ref.shape[-1]
    queries = (proj_ref[0, 0] * scale_ref[...]).astype(BF16)
    keys = proj_ref[1, 0].T.astype(BF16)
    values = proj_ref[2, 0].astype(BF16)
    for first, parts in token_places(length, out_ref.shape[0], token_rows, FORWARD_ROWS):
        end = first + FORWARD_ROWS
        block, row = queries[:, first:end], row_ref[:, first:end]
        pieces = []
        for start in range(0, end, FORWARD_KEYS):
            scores = jnp.dot(keys[start : start + FORWARD_KEYS], block, preferred_element_type=F32)
            allowed = allowed_piece(col_ref[start : start + FORWARD_KEYS], row, start, first)
            pieces.append(jnp.where(allowed, scores, MASKED_SCORE))
        top = functools.reduce(
            jnp.maximum, [jnp.max(piece, axis=0, keepdims=True) for piece in pieces]
        )
        total, attended = 0.0, 0.0
        for i, piece in enumerate(pieces):
            terms = jnp.exp(piece - top)
            total += jnp.sum(terms, axis=0, keepdims=True)
            attended += jnp.dot(
                values[:, i * FORWARD_KEYS : (i + 1) * FORWARD_KEYS],
                terms.astype(BF16),
                preferred_element_type=F32,
            )
        attended = (attended * (1.0 / total)).astype(BF16)
        lse_ref[0, :, first:end] = top + jnp.log(total)
        for start, owner, offset in parts:
            out_ref[owner, 0, :, offset : offset + token_rows] = attended[
                :, start : start + token_rows
            ]


def attend_rows(projected, scale_vec, segments, owners, token_rows):
    head_dim = scale_vec.shape[0]
    length = projected.shape[1]
    local_heads = projected.shape[0] // 3 // head_dim
    tokens = length // owners
    attended, log_total = pl.pallas_call(
        functools.partial(attend_kernel, token_rows),
        grid=(local_heads,),
        in_specs=[
            pl.BlockSpec((3, 1, head_dim, length), lambda h: (0, h, 0, 0)),
            pl.BlockSpec((head_dim, 1), lambda h: (0, 0)),
            pl.BlockSpec((length, 1), lambda h: (0, 0)),
            pl.BlockSpec((1, length), lambda h: (0, 0)),
        ],
        out_specs=[
            pl.BlockSpec((owners, 1, head_dim, tokens), lambda h: (0, h, 0, 0)),
            pl.BlockSpec((1, 1, length), lambda h: (h, 0, 0)),
        ],
        out_shape=[
            jax.ShapeDtypeStruct((owners, local_heads, head_dim, tokens), BF16),
            jax.ShapeDtypeStruct((local_heads, 1, length), F32),
        ],
        compiler_params=KERNEL,
        cost_estimate=LIGHT,
    )(
        projected.reshape(3, local_heads, head_dim, length),
        scale_vec.reshape(head_dim, 1),
        segments.reshape(length, 1),
        segments.reshape(1, length),
    )
    return attended.reshape(owners, local_heads * head_dim, tokens), log_total


def attend_back_kernel(
    token_rows,
    proj_ref,
    grad_ref,
    lse_ref,
    scale_ref,
    col_ref,
    row_ref,
    out_ref,
    scale_grad_ref,
    keys_acc,
    values_acc,
):
    length = proj_ref.shape[-1]
    scale = scale_ref[...]
    query_pre = proj_ref[0, 0]
    queries = (query_pre * scale).astype(BF16)
    keys_t = proj_ref[1, 0].astype(BF16)
    keys = proj_ref[1, 0].T.astype(BF16)
    values = proj_ref[2, 0].T.astype(BF16)
    keys_acc[...] = jnp.zeros_like(keys_acc)
    values_acc[...] = jnp.zeros_like(values_acc)
    scale_grad = jnp.zeros((scale.shape[0], 1), F32)
    for first, parts in token_places(length, grad_ref.shape[0], token_rows):
        end = first + Q_ROWS
        block = queries[:, first:end]
        grad = jnp.concatenate(
            [grad_ref[owner, 0, :, at : at + token_rows] for _, owner, at in parts], axis=1
        )
        scores = jnp.dot(keys[:end], block, preferred_element_type=F32)
        allowed = allowed_keys(col_ref[...], row_ref[:, first:end], first)
        scores = jnp.where(allowed, scores, MASKED_SCORE)
        probs = jnp.exp(scores - lse_ref[0, :, first:end])
        probs_grad = jnp.dot(values[:end], grad, preferred_element_type=F32)
        row_dot = jnp.sum(probs_grad * probs, axis=0, keepdims=True)
        scores_low = (probs * (probs_grad - row_dot)).astype(BF16)
        values_acc[:, :end] += lax.dot_general(
            grad, probs.astype(BF16), NT, preferred_element_type=F32
        )
        keys_acc[:, :end] += lax.dot_general(
            block, scores_low, NT, preferred_element_type=F32
        )
        query_bar = jnp.dot(keys_t[:, :end], scores_low, preferred_element_type=F32)
        query_bar = query_bar.astype(BF16).astype(F32)
        scale_grad += jnp.sum(query_bar * query_pre[:, first:end], axis=1, keepdims=True)
        out_ref[0, 0, :, first:end] = (query_bar * scale).astype(BF16)
    out_ref[1, 0] = keys_acc[...].astype(BF16)
    out_ref[2, 0] = values_acc[...].astype(BF16)
    spread = jnp.broadcast_to(scale_grad, scale_grad_ref.shape)

    @pl.when(pl.program_id(0) == 0)
    def _():
        scale_grad_ref[...] = spread

    @pl.when(pl.program_id(0) > 0)
    def _():
        scale_grad_ref[...] += spread


def attend_back_rows(projected, attended_grad, log_total, scale_vec, segments, token_rows):
    head_dim = scale_vec.shape[0]
    length = projected.shape[1]
    local_heads = projected.shape[0] // 3 // head_dim
    owners, _, tokens = attended_grad.shape
    lanes = 128
    grads, scale_grad = pl.pallas_call(
        functools.partial(attend_back_kernel, token_rows),
        grid=(local_heads,),
        in_specs=[
            pl.BlockSpec((3, 1, head_dim, length), lambda h: (0, h, 0, 0)),
            pl.BlockSpec((owners, 1, head_dim, tokens), lambda h: (0, h, 0, 0)),
            pl.BlockSpec((1, 1, length), lambda h: (h, 0, 0)),
            pl.BlockSpec((head_dim, 1), lambda h: (0, 0)),
            pl.BlockSpec((length, 1), lambda h: (0, 0)),
            pl.BlockSpec((1, length), lambda h: (0, 0)),
        ],
        out_specs=[
            pl.BlockSpec((3, 1, head_dim, length), lambda h: (0, h, 0, 0)),
            pl.BlockSpec((head_dim, lanes), lambda h: (0, 0)),
        ],
        out_shape=[
            pltpu.HBM((3, local_heads, head_dim, length), BF16),
            pltpu.HBM((head_dim, lanes), F32),
        ],
        scratch_shapes=[
            pltpu.VMEM((head_dim, length), F32),
            pltpu.VMEM((head_dim, length), F32),
        ],
        compiler_params=KERNEL,
        cost_estimate=LIGHT,
    )(
        *in_hbm(
            projected.reshape(3, local_heads, head_dim, length),
            attended_grad.reshape(owners, local_heads, head_dim, tokens),
        ),
        log_total,
        scale_vec.reshape(head_dim, 1),
        segments.reshape(length, 1),
        segments.reshape(1, length),
    )
    return grads.reshape(3 * local_heads * head_dim, length), scale_grad[:, 0]


def dense_grad_kernel(
    core_ref, attended_ref, normed_ref, active_ref, out_bar, up_bar, down_bar,
    own_ref, other_ref, normed_t, active_t,
):
    tile = pl.program_id(0)
    rows, width = 8 * own_ref.shape[3], out_bar.shape[1]

    @pl.when(tile == 0)
    def _():
        normed_t[...] = normed_ref[...].astype(F32).T.astype(BF16)
        active_t[...] = active_ref[...].astype(F32).T.astype(BF16)

    start = pl.multiple_of(tile * rows, rows)
    first_core = core_ref[2] == 0
    lefts = (attended_ref, normed_t, active_t)
    for i, (left, right) in enumerate(zip(lefts, (out_bar, up_bar, down_bar))):
        grad = jnp.dot(left[pl.ds(start, rows), :], right[...], preferred_element_type=F32)
        grad = grad.reshape(2, 2, 2, rows // 8, width)
        one, two = grad[:, :, 0], grad[:, :, 1]
        own_ref[:, :, 0, :, i * width : (i + 1) * width] = jnp.where(
            first_core, one, two
        ).astype(BF16)
        other_ref[:, :, 0, :, i * width : (i + 1) * width] = jnp.where(
            first_core, two, one
        ).astype(BF16)


def dense_grads(attended_t, normed, active, out_bar, up_bar, down_bar):
    width, tokens = attended_t.shape
    own = width // 32
    whole = pl.BlockSpec((tokens, width), lambda i, core: (0, 0))
    rows = pl.BlockSpec((2, 2, 1, own, 3 * width), lambda i, core: (0, 0, i, 0, 0))
    shape = pltpu.HBM((2, 2, 4, own, 3 * width), BF16)
    return pl.pallas_call(
        dense_grad_kernel,
        grid_spec=pltpu.PrefetchScalarGridSpec(
            num_scalar_prefetch=1,
            grid=(4,),
            in_specs=[pl.BlockSpec((width, tokens), lambda i, core: (0, 0))] + [whole] * 5,
            out_specs=[rows, rows],
            scratch_shapes=[pltpu.VMEM((width, tokens), BF16)] * 2,
        ),
        out_shape=[shape, shape],
        compiler_params=KERNEL,
        cost_estimate=LIGHT,
    )(place(), *in_hbm(attended_t, normed, active, out_bar, up_bar, down_bar))


def place():
    head = lax.axis_index("head")
    return jnp.stack([lax.axis_index("blk"), head // 2, head % 2]).astype(jnp.int32)


def assemble_kernel(place_ref, *refs):
    pieces, whole_ref = refs[:10], refs[10]
    half = whole_ref.shape[-1] // 2
    blk, row, core = place_ref[0], place_ref[1], place_ref[2]
    for i in range(2):
        at_core = core if i == 0 else 1 - core
        own, across, beside, one, two = pieces[5 * i : 5 * i + 5]
        whole_ref[0, blk, row, at_core] = own[0]
        whole_ref[0, 1 - blk, row, at_core] = across[0]
        whole_ref[0, blk, 1 - row, at_core] = beside[0]
        whole_ref[0, 1 - blk, 1 - row, at_core, :, :half] = one[0]
        whole_ref[0, 1 - blk, 1 - row, at_core, :, half:] = two[0]


def assemble(pieces):
    batch, own, columns = pieces[0].shape
    specs = [
        pl.BlockSpec((1, own, piece.shape[-1]), lambda i, at: (i, 0, 0))
        for piece in pieces
    ]
    whole = pl.pallas_call(
        assemble_kernel,
        grid_spec=pltpu.PrefetchScalarGridSpec(
            num_scalar_prefetch=1,
            grid=(batch,),
            in_specs=specs,
            out_specs=pl.BlockSpec((1, 2, 2, 2, own, columns), lambda i, at: (i, 0, 0, 0, 0, 0)),
        ),
        out_shape=jax.ShapeDtypeStruct((batch, 2, 2, 2, own, columns), BF16),
        compiler_params=KERNEL,
        cost_estimate=LIGHT,
    )(place(), *pieces)
    return whole.reshape(-1, columns)


def assemble_columns_kernel(place_ref, along_ref, across_ref, whole_ref, *extra_ref):
    blk = place_ref[0]
    columns = whole_ref.shape[-1]
    whole_ref[0, blk] = along_ref[0, :, :columns]
    whole_ref[0, 1 - blk] = across_ref[0, :, :columns]
    for extra in extra_ref:
        extra[0, blk] = along_ref[0, :, columns:]
        extra[0, 1 - blk] = across_ref[0, :, columns:]


def assemble_columns(along, across, columns):
    batch, own, both = along.shape
    rows = pl.BlockSpec((1, own, both), lambda i, at: (i, 0, 0))
    shapes = [(batch, 2, own, columns)]
    if both > columns:
        shapes.append((batch, 2, own, both - columns))
    parts = pl.pallas_call(
        assemble_columns_kernel,
        grid_spec=pltpu.PrefetchScalarGridSpec(
            num_scalar_prefetch=1,
            grid=(batch,),
            in_specs=[rows, rows],
            out_specs=[pl.BlockSpec((1,) + s[1:], lambda i, at: (i, 0, 0, 0)) for s in shapes],
        ),
        out_shape=[pltpu.HBM(s, BF16) for s in shapes],
        compiler_params=KERNEL,
        cost_estimate=LIGHT,
    )(place(), *in_hbm(along, across))
    return [part.reshape(-1, part.shape[-1]) for part in parts]


def assemble_wide_kernel(place_ref, along_ref, across_ref, whole_ref):
    blk = place_ref[0]
    own, columns = along_ref.shape[1], whole_ref.shape[-1]
    for i in range(along_ref.shape[-1] // columns):
        place, part = slice(i * own, (i + 1) * own), slice(i * columns, (i + 1) * columns)
        whole_ref[0, blk, place, :] = along_ref[0, :, part]
        whole_ref[0, 1 - blk, place, :] = across_ref[0, :, part]


def assemble_wide(along, across, columns):
    batch, own, wide = along.shape
    rows = own * (wide // columns)
    piece = pl.BlockSpec((1, own, wide), lambda i, at: (i, 0, 0))
    whole = pl.pallas_call(
        assemble_wide_kernel,
        grid_spec=pltpu.PrefetchScalarGridSpec(
            num_scalar_prefetch=1,
            grid=(batch,),
            in_specs=[piece, piece],
            out_specs=pl.BlockSpec((1, 2, rows, columns), lambda i, at: (i, 0, 0, 0)),
        ),
        out_shape=pltpu.HBM((batch, 2, rows, columns), BF16),
        compiler_params=KERNEL,
        cost_estimate=LIGHT,
    )(place(), *in_hbm(along, across))
    return whole.reshape(-1, columns)


def project_kernel(with_norm, place_ref, *refs):
    pieces, (gain_ref, weight_ref, normed_ref, projected_ref) = refs[:4], refs[4:]
    head = place_ref[1] * 2 + place_ref[2]
    rows = pieces[0].shape[0]
    for i, piece in enumerate(pieces):
        value = piece[...]
        if with_norm:
            stream = value.astype(F32)
            factor = lax.rsqrt(jnp.mean(stream * stream, axis=-1, keepdims=True) + EPSILON)
            value = (stream * factor * gain_ref[...]).astype(BF16)
        normed_ref[pl.ds(pl.multiple_of((head ^ i) * rows, rows), rows), :] = value
    projected = jnp.dot(normed_ref[...], weight_ref[...], preferred_element_type=F32)
    projected_ref[...] = projected.T


def project(pieces, gain, weight, with_norm, token_rows):
    tokens, width = pieces[0].shape
    length, columns = 4 * tokens, weight.shape[1]
    groups = tokens // token_rows
    piece = pl.BlockSpec((token_rows, width), lambda g, at: (g, 0))
    return pl.pallas_call(
        functools.partial(project_kernel, with_norm),
        grid_spec=pltpu.PrefetchScalarGridSpec(
            num_scalar_prefetch=1,
            grid=(groups,),
            in_specs=[piece] * 4
            + [
                pl.BlockSpec((1, width), lambda g, at: (0, 0)),
                pl.BlockSpec((width, columns), lambda g, at: (0, 0)),
            ],
            out_specs=[
                pl.BlockSpec((4 * token_rows, width), lambda g, at: (g, 0)),
                pl.BlockSpec((columns, 4 * token_rows), lambda g, at: (0, g)),
            ],
        ),
        out_shape=[
            pltpu.HBM((length, width), BF16),
            jax.ShapeDtypeStruct((columns, length), F32),
        ],
        compiler_params=KERNEL,
        cost_estimate=LIGHT,
    )(place(), *in_hbm(*pieces), gain.reshape(1, width), *in_hbm(weight))


def project_back_kernel(
    place_ref, bars_ref, weight_ref, normed_ref, own_ref, other_ref, grad_ref, bars_t
):
    @pl.when(pl.program_id(0) == 0)
    def _():
        bars_t[...] = bars_ref[...].astype(F32).T.astype(BF16)

    upper = lax.dot_general(bars_t[...], weight_ref[...], NT, preferred_element_type=F32)
    upper = upper.reshape(2, 2, 2, -1, upper.shape[-1])
    first_core = place_ref[2] == 0
    one, two = upper[:, :, 0], upper[:, :, 1]
    own_ref[...] = jnp.where(first_core, one, two)
    other_ref[...] = jnp.where(first_core, two, one).astype(BF16)
    grad = lax.dot_general(normed_ref[...], bars_t[...], TN, preferred_element_type=F32)
    grad_ref[...] = grad.astype(BF16)


def project_back(bars, weight, normed, token_rows):
    columns, length = bars.shape
    width = weight.shape[0]
    tile = width // 2
    quarter = pl.BlockSpec((2, 2, token_rows, tile), lambda i, at: (0, 0, 0, i))
    return pl.pallas_call(
        project_back_kernel,
        grid_spec=pltpu.PrefetchScalarGridSpec(
            num_scalar_prefetch=1,
            grid=(2,),
            in_specs=[
                pl.BlockSpec((columns, length), lambda i, at: (0, 0)),
                pl.BlockSpec((tile, columns), lambda i, at: (i, 0)),
                pl.BlockSpec((length, tile), lambda i, at: (0, i)),
            ],
            out_specs=[quarter, quarter, pl.BlockSpec((tile, columns), lambda i, at: (i, 0))],
            scratch_shapes=[pltpu.VMEM((length, columns), BF16)],
        ),
        out_shape=[
            pltpu.HBM((2, 2, token_rows, width), F32),
            pltpu.HBM((2, 2, token_rows, width), BF16),
            pltpu.HBM((width, columns), BF16),
        ],
        compiler_params=KERNEL,
        cost_estimate=LIGHT,
    )(place(), *in_hbm(bars, weight, normed))


def rows_back_kernel(place_ref, bars_ref, weight_ref, own_ref, other_ref, bars_t):
    @pl.when(pl.program_id(0) == 0)
    def _():
        bars_t[...] = bars_ref[...].astype(F32).T.astype(BF16)

    upper = lax.dot_general(bars_t[...], weight_ref[...], NT, preferred_element_type=F32)
    upper = upper.reshape(2, 2, 2, -1, upper.shape[-1])
    first_core = place_ref[2] == 0
    one, two = upper[:, :, 0], upper[:, :, 1]
    own_ref[...] = jnp.where(first_core, one, two)
    other_ref[...] = jnp.where(first_core, two, one).astype(BF16)


def rows_back(bars, weight, token_rows):
    columns, length = bars.shape
    width = weight.shape[0]
    tile = width // 2
    quarter = pl.BlockSpec((2, 2, token_rows, tile), lambda i, at: (0, 0, 0, i))
    return pl.pallas_call(
        rows_back_kernel,
        grid_spec=pltpu.PrefetchScalarGridSpec(
            num_scalar_prefetch=1,
            grid=(2,),
            in_specs=[
                pl.BlockSpec((columns, length), lambda i, at: (0, 0)),
                pl.BlockSpec((tile, columns), lambda i, at: (i, 0)),
            ],
            out_specs=[quarter, quarter],
            scratch_shapes=[pltpu.VMEM((length, columns), BF16)],
        ),
        out_shape=[
            pltpu.HBM((2, 2, token_rows, width), F32),
            pltpu.HBM((2, 2, token_rows, width), BF16),
        ],
        compiler_params=KERNEL,
        cost_estimate=LIGHT,
    )(place(), *in_hbm(bars, weight))


def weight_back_kernel(bars_ref, normed_ref, grad_ref):
    grad = jnp.dot(bars_ref[...], normed_ref[...], preferred_element_type=F32)
    grad_ref[...] = grad.T.astype(BF16)


def weight_back(bars, normed):
    columns, length = bars.shape
    width = normed.shape[1]
    tile = width // 5
    return pl.pallas_call(
        weight_back_kernel,
        grid=(5,),
        in_specs=[
            pl.BlockSpec((columns, length), lambda i: (0, 0)),
            pl.BlockSpec((length, tile), lambda i: (0, i)),
        ],
        out_specs=pl.BlockSpec((tile, columns), lambda i: (i, 0)),
        out_shape=pltpu.HBM((width, columns), BF16),
        compiler_params=KERNEL,
        cost_estimate=LIGHT,
    )(*in_hbm(bars, normed))


def tied(*arrays):
    return lax.optimization_barrier(arrays)


def swapped(array, axis, mask):
    size = lax.axis_size(axis)
    return lax.ppermute(array, axis, [(i, i ^ mask) for i in range(size)])


def pick(array, index, axis=0):
    return lax.dynamic_index_in_dim(array, index, axis, keepdims=False)


def swap_halves(array):
    me = lax.axis_index("blk")
    got = swapped(pick(array, 1 - me), "blk", 1)
    kept = pick(array, me)
    return jnp.stack([jnp.where(me == 0, kept, got), jnp.where(me == 0, got, kept)])


def scatter_row(halves):
    row = lax.axis_index("head") // 2
    got = swapped(pick(halves, 1 - row, 1).astype(BF16), "head", 2).astype(F32)
    return (pick(halves, row, 1) + got).reshape(-1, halves.shape[-1])


def over_head(parts):
    return lax.all_to_all(parts, "head", split_axis=0, concat_axis=0, tiled=True)


def qkv_columns(rows, extra):
    own, width = rows.shape
    part = width // 3 // 4
    sent = rows.reshape(own, 3, 4, part).transpose(2, 0, 1, 3).reshape(4, own, 3 * part)
    if extra is not None:
        sent = jnp.concatenate([sent, jnp.broadcast_to(extra[None], (4,) + extra.shape)], axis=2)
    return over_head(sent)


def along_batch(piece):
    return lax.all_gather(piece, "batch", axis=0, tiled=False)


def other_core(array):
    return swapped(array, "head", 1)


def to_beside(across):
    return swapped(across[..., : across.shape[-1] // 2], "head", 2)


def to_across(beside):
    return swapped(beside[..., beside.shape[-1] // 2 :], "blk", 1)


def over_batch(parts):
    return lax.psum_scatter(parts.astype(BF16), "batch", scatter_dimension=0, tiled=False)


def across_sum(halves):
    blk = lax.axis_index("blk")
    got = swapped(pick(halves, 1 - blk), "blk", 1).astype(F32)
    return (pick(halves, blk).astype(F32) + got).astype(BF16)


def columns_to_rows(moved):
    rows = moved.shape[1]
    return moved.reshape(4, rows, 3, -1).transpose(1, 2, 0, 3).reshape(rows, -1).astype(F32)


def quarter(parts, blk, row):
    one, two = (pick(pick(part, blk), row).astype(F32) for part in parts)
    return one + two


def diagonal_rows(parts):
    blk, row = place()[:2]
    rows = quarter(parts, 1 - blk, 1 - row).astype(BF16)
    half = rows.shape[-1] // 2
    return rows[..., :half], rows[..., half:]


def neighbour_rows(parts, one, two):
    blk, row = place()[:2]
    half = one.shape[-1]
    across, beside = quarter(parts, 1 - blk, row), quarter(parts, blk, 1 - row)
    across = jnp.concatenate([across[..., :half], across[..., half:] + two.astype(F32)], axis=-1)
    beside = jnp.concatenate([beside[..., :half] + one.astype(F32), beside[..., half:]], axis=-1)
    return across.astype(BF16), beside.astype(BF16)


def sent_beside_and_across(across, beside):
    return swapped(across, "blk", 1), swapped(beside, "head", 2)


def heads_grad(weight, out_bar):
    return dot_cols(weight, out_bar).astype(BF16).reshape(4, -1, out_bar.shape[0])


def own_quarter(parts):
    blk, row = place()[:2]
    return quarter(parts, blk, row)


def own_sum(own, *more):
    return sum((part.astype(F32) for part in more), own).astype(BF16)


def sum_over(array, *hops):
    for axis, mask in hops:
        array = array + swapped(array, axis, mask)
    return array


def gain_back(weight, weight_grad, gain):
    return jnp.sum(weight.astype(F32) * weight_grad, axis=-1) / gain.astype(F32)


def lower_of(upper, stream, factor, gain):
    return norm_back(upper, stream, factor, gain)[0]


def spread_device(
    tokens,
    segments,
    qkv_weight,
    out_weight,
    up_weight,
    down_weight,
    attn_gain,
    mlp_gain,
    scale_param,
    cotangent,
):
    layers, head_dim = scale_param.shape
    _, token_rows, width = tokens.shape
    scale_vecs = SCALE_BASE / math.sqrt(head_dim) * jax.nn.softplus(scale_param)
    segments = pick(segments, lax.axis_index("blk"))
    own_gains = jnp.concatenate([attn_gain, mlp_gain], axis=0)

    part3 = 3 * width // 4
    dense_own = [
        jnp.concatenate([out_weight[i], up_weight[i], down_weight[i]], axis=1) for i in (0, 1)
    ]

    first = swap_halves(tokens).reshape(-1, width)
    columns = qkv_columns(qkv_weight[0], own_gains.T)
    columns, first, cotangent = tied(columns.reshape(-1, columns.shape[-1]), first, cotangent)
    stream = first.astype(F32)
    along = along_batch(columns)
    far, near = swapped(first, "head", 2), other_core(first)
    both = other_core(far)
    upper = swap_halves(cotangent)
    along, near, far, both, dense_near, upper = tied(
        along, near, far, both, dense_own[0], upper
    )
    token_pieces = (first, near, far, both)
    dense_near = along_batch(dense_near)
    qkv_across = swapped(along, "blk", 1)
    next_columns = jnp.concatenate(list(qkv_columns(qkv_weight[1], None)), axis=1)
    qkv_across, dense_near, next_columns = tied(qkv_across, dense_near, next_columns)
    across, beside = swapped(dense_near, "blk", 1), swapped(dense_near, "head", 2)
    next_both = along_batch(jnp.stack([next_columns, dense_own[1]]))
    weight, gains = assemble_columns(along, qkv_across, part3)
    qkvs = [weight]
    gains = gains.T.astype(F32)

    kept, denses = [], []
    for layer in range(layers):
        normed, factor_one = normalize(stream, gains[layer])
        if layer == 1:
            normed = normed.astype(BF16)
            far, near = swapped(normed, "head", 2), other_core(normed)
            far, next_across, dense_next = tied(far, next_across, dense_next)
            across, beside = swapped(dense_next, "blk", 1), swapped(dense_next, "head", 2)
            token_pieces = (normed, near, far, other_core(far))
            qkvs.append(assemble_wide(next_along, next_across, part3))
        normed_all, projected = project(
            token_pieces, gains[layer], qkvs[layer], layer == 0, token_rows
        )
        attended, log_total = attend_rows(
            projected, scale_vecs[layer], segments, 4, token_rows
        )
        attended, across, beside = tied(attended, across, beside)
        one, two = to_beside(across), to_across(beside)
        if layer == 0:
            two, next_both = tied(two, next_both)
            next_along, dense_next = next_both[:, 0], next_both[:, 1]
            next_across = swapped(next_along, "blk", 1)
            attended_t, one, two = tied(over_head(attended), one, two)
        else:
            dense_near = dense_next
            attended_t, one, two = tied(over_head(attended), one, two)
        pieces = (dense_near, across, beside, one, two)
        pieces += tuple(other_core(piece) for piece in pieces)
        attended_t = attended_t.reshape(width, -1)
        denses.append(assemble(pieces))
        dense = denses[layer]
        out_w, up_w, down_w = dense[:, :width], dense[:, width:-width], dense[:, -width:]
        middle = stream + dot_rows(attended_t, out_w)
        normed_two, factor_two = normalize(middle, gains[layers + layer])
        normed_two = normed_two.astype(BF16)
        hidden = dot(normed_two, up_w)
        active = (hidden * jax.nn.sigmoid(hidden)).astype(BF16)
        kept.append(
            (
                stream, factor_one, normed_all, projected, log_total, attended_t, middle,
                factor_two, normed_two, hidden, active,
            )
        )
        stream = middle + dot(active, down_w)
    layer_out = swap_halves(stream.astype(BF16).reshape(tokens.shape))
    upper = upper.reshape(-1, width).astype(F32)

    scale_grads = [None] * layers
    for layer in reversed(range(layers)):
        (
            stream, factor_one, normed_all, projected, log_total, attended_t, middle,
            factor_two, normed_two, hidden, active,
        ) = kept[layer]
        qkv, dense = qkvs[layer], denses[layer]
        out_w, up_w, down_w = dense[:, :width], dense[:, width:-width], dense[:, -width:]
        down_bar = upper.astype(BF16)
        gate = jax.nn.sigmoid(hidden)
        up_bar = (
            dot_cols(down_bar, down_w) * gate * (1.0 + hidden * (1.0 - gate))
        ).astype(BF16)
        middle_grad = upper + lower_of(
            dot_cols(up_bar, up_w), middle, factor_two, gains[layers + layer]
        )
        out_bar = middle_grad.astype(BF16)
        if layer == 0:
            attended_grad = over_head(heads_grad(out_w, out_bar))
            grads, others = dense_grads(attended_t, normed_two, active, out_bar, up_bar, down_bar)
            others, across = tied(others, across)
            others, own = tied(others, own_quarter(cored) + across.astype(F32))
            attended_grad, others, z_sum, beside = tied(attended_grad, others, z_sum, beside)
            others = other_core(others)
            attended_grad, summed = tied(attended_grad, own_sum(own, beside))
            summed = over_batch(summed)
            z_across = across_sum(z_sum)
        else:
            attended_grad = over_head(heads_grad(out_w, out_bar))
            grads, others = dense_grads(attended_t, normed_two, active, out_bar, up_bar, down_bar)
            attended_grad, others, layer_out = tied(attended_grad, others, layer_out)
            others = other_core(others)
        bars, scale_grads[layer] = attend_back_rows(
            projected, attended_grad, log_total, scale_vecs[layer], segments, token_rows
        )
        if layer == 0:
            bars, others, z_across = tied(bars, others, z_across)
            moved = over_head(z_across.reshape(4, -1, z_across.shape[-1]))
            qkv_grad = weight_back(bars, normed_all)
            bars, qkv_grad, moved = tied(bars, qkv_grad, moved)
            z_sum = over_batch(qkv_grad.reshape(4, 2, -1, qkv_grad.shape[-1]))
            cored = (grads, others)
            bars, rows = tied(bars, diagonal_rows(cored))
            diagonal = sent_beside_and_across(*rows)
            halves, to_core = rows_back(bars, qkv, token_rows)
            halves, to_core, diagonal, summed = tied(halves, to_core, diagonal, summed)
            halves, to_core, rows = tied(halves, to_core, neighbour_rows(cored, *diagonal))
            sent = sent_beside_and_across(*rows)
            halves = halves + other_core(to_core).astype(F32)
            scale_sum = sum_over(jnp.stack(scale_grads), ("head", 1), ("batch", 1), ("batch", 2))
            own = own_quarter(cored)
            halves, sent, z_sum, scale_sum, own = tied(halves, sent, z_sum, scale_sum, own)
            halves, own = tied(halves, own_sum(own, *sent))
            dense_first = over_batch(own)
            normed_grad = scatter_row(halves)
            z_across = across_sum(z_sum)
            z_across = over_head(z_across.reshape(4, -1, z_across.shape[-1]))
            dense_grad = [dense_first, summed]
            qkv_grads = [columns_to_rows(z_across), columns_to_rows(moved)]
        else:
            bars, others = tied(bars, others)
            cored = (grads, others)
            bars, rows = tied(bars, diagonal_rows(cored))
            diagonal = sent_beside_and_across(*rows)
            halves, to_core, qkv_grad = project_back(bars, qkv, normed_all, token_rows)
            z_sum = over_batch(qkv_grad.reshape(4, 2, -1, qkv_grad.shape[-1]))
            to_core, halves, diagonal = tied(to_core, halves, diagonal)
            to_core, rows = tied(to_core, neighbour_rows(cored, *diagonal))
            across = swapped(rows[0], "blk", 1)
            halves = halves + other_core(to_core).astype(F32)
            normed_grad = scatter_row(halves)
            normed_grad, beside = tied(normed_grad, rows[1])
            beside = swapped(beside, "head", 2)
        upper = middle_grad + lower_of(normed_grad, stream, factor_one, gains[layer])
    input_grad = swap_halves(upper.astype(BF16).reshape(tokens.shape)).astype(F32)
    scale_total = sum_over(scale_sum, ("head", 2))
    scale_total, dense_grad[0] = tied(scale_total, dense_grad[0])
    scale_total = sum_over(scale_total, ("blk", 1))
    scale_grad = scale_total * (SCALE_BASE / math.sqrt(head_dim)) * jax.nn.sigmoid(scale_param)
    dense_all = jnp.stack([part.astype(F32) for part in dense_grad])
    qkv_all = jnp.stack(qkv_grads)
    up_all = dense_all[:, :, width:-width]
    return (
        layer_out,
        input_grad,
        qkv_all,
        dense_all[:, :, :width],
        up_all,
        dense_all[:, :, -width:],
        gain_back(qkv_weight, qkv_all, attn_gain),
        gain_back(up_weight, up_all, mlp_gain),
        scale_grad,
    )


def per_device(*args):
    tokens, segments = args[0], args[1]
    sizes = tuple(lax.axis_size(axis) for axis in ALL)
    heads = tokens.shape[2] // args[8].shape[1]
    spread = (
        sizes == (4, 2, 4)
        and tokens.shape[0] == 2
        and args[2].shape[0] == 2
        and tokens.shape[1] % 128 == 0
        and Q_ROWS % tokens.shape[1] == 0
        and segments.shape[1] <= WINDOW
        and segments.shape[1] % FORWARD_ROWS == 0
        and heads % 4 == 0
        and tokens.shape[2] % 256 == 0
    )
    return spread_device(*args) if spread else general_device(*args)


def solution(mesh):
    rows = P(None, ALL, None)
    by_token = P("batch", ("blk", "head"), None)
    return jax.shard_map(
        per_device,
        mesh=mesh,
        in_specs=(
            by_token, P("batch", None), rows, rows, rows, rows, P(None, ALL), P(None, ALL), P(),
            by_token,
        ),
        out_specs=(
            by_token, by_token, rows, rows, rows, rows, P(None, ALL), P(None, ALL), P(),
        ),
        check_vma=False,
    )
```

```python
import functools
import math

import jax
import jax.numpy as jnp
from jax import lax
from jax.experimental import pallas as pl
from jax.experimental.pallas import tpu as pltpu
from jax.sharding import PartitionSpec as P

WINDOW = 1024
EPSILON = 1e-06
SCALE_BASE = 1.4426950408889634
MASKED_SCORE = -1e30

ALL = ("batch", "blk", "head")
REST = ("batch", "blk")
F32 = jnp.float32
BF16 = jnp.bfloat16


def shifted(block, axis, distance):
    devices = range(lax.axis_size(axis))
    route = [(i - distance, i) for i in devices if i - distance in devices]
    return lax.ppermute(block, axis, route)


NT = (((1,), (1,)), ((), ()))
TN = (((0,), (0,)), ((), ()))


def dot(left, right):
    return jnp.dot(left, right, preferred_element_type=F32)


def dot_rows(left, right):
    return lax.dot_general(left, right, (((0,), (0,)), ((), ())), preferred_element_type=F32)


def dot_cols(left, right):
    return lax.dot_general(left, right, (((1,), (1,)), ((), ())), preferred_element_type=F32)


def normalize(stream, gain):
    factor = lax.rsqrt(jnp.mean(stream * stream, axis=-1, keepdims=True) + EPSILON)
    return stream * factor * gain, factor


def norm_back(upper, stream, factor, gain):
    inner = upper * gain
    gain_grad = jnp.sum(upper * stream * factor, axis=0)
    lower = factor * inner - stream * factor * factor * factor * jnp.mean(
        inner * stream, axis=-1, keepdims=True
    )
    return lower, gain_grad


class Plan:
    def __init__(self, tokens):
        self.seqs, self.rows, self.width = tokens.shape
        self.heads = lax.axis_size("head")
        self.blks = lax.axis_size("blk")
        self.block = self.rows * self.heads
        self.whole = self.seqs % self.blks == 0
        if self.whole:
            self.groups, self.own_seqs = self.blks, self.seqs // self.blks
            self.reach = 0
        else:
            self.groups, self.own_seqs = 1, self.seqs
            self.reach = min((WINDOW - 1) // self.block + 1, self.blks - 1)
        self.length = self.groups * self.block
        self.tokens = self.seqs * self.rows


def to_plan(plan, array):
    if plan.whole and plan.blks > 1:
        array = lax.all_to_all(array, "blk", split_axis=0, concat_axis=0, tiled=True)
    return array.reshape(plan.tokens, plan.width)


def from_plan(plan, flat):
    array = flat.reshape(plan.seqs, plan.rows, plan.width)
    if plan.whole and plan.blks > 1:
        array = lax.all_to_all(array, "blk", split_axis=0, concat_axis=0, tiled=True)
    return array


def in_sequence(plan, by_head, width):
    parts = by_head.reshape(plan.heads, plan.groups, plan.own_seqs, plan.rows, width)
    return parts.transpose(2, 1, 0, 3, 4).reshape(-1, width)


def by_owner(plan, rows, width):
    parts = rows.reshape(plan.own_seqs, plan.groups, plan.heads, plan.rows, width)
    return parts.transpose(2, 1, 0, 3, 4).reshape(plan.heads, plan.tokens, width)


def gather_tokens(plan, rows):
    moved = lax.all_gather(rows, "head", axis=0, tiled=False)
    return in_sequence(plan, moved, rows.shape[-1])


def scatter_tokens(plan, rows):
    width = rows.shape[-1]
    return lax.psum_scatter(
        by_owner(plan, rows.astype(BF16), width), "head", scatter_dimension=0, tiled=False
    ).astype(F32)


def heads_to_tokens(plan, rows):
    part = rows.shape[-1]
    moved = lax.all_to_all(
        by_owner(plan, rows, part), "head", split_axis=0, concat_axis=0, tiled=True
    )
    return moved.transpose(1, 0, 2).reshape(plan.tokens, plan.heads * part)


def tokens_to_heads(plan, rows):
    part = rows.shape[-1] // plan.heads
    sent = rows.reshape(plan.tokens, plan.heads, part).transpose(1, 0, 2)
    moved = lax.all_to_all(sent, "head", split_axis=0, concat_axis=0, tiled=True)
    return in_sequence(plan, moved, part)


def gather_qkv(rows):
    own, width = rows.shape
    heads = lax.axis_size("head")
    part = width // 3 // heads
    sent = rows.reshape(own, 3, heads, part).transpose(2, 0, 1, 3).reshape(heads, own, 3 * part)
    moved = lax.all_to_all(sent, "head", split_axis=0, concat_axis=0, tiled=True)
    full = lax.all_gather(moved, REST, axis=0, tiled=True)
    return full.reshape(-1, 3 * part)


def scatter_qkv(grad):
    heads = lax.axis_size("head")
    part = grad.shape[1] // 3
    summed = lax.psum_scatter(grad.astype(BF16), REST, scatter_dimension=0, tiled=True)
    own = summed.shape[0] // heads
    moved = lax.all_to_all(
        summed.reshape(heads, own, 3 * part), "head", split_axis=0, concat_axis=0, tiled=True
    )
    return (
        moved.reshape(heads, own, 3, part)
        .transpose(1, 2, 0, 3)
        .reshape(own, 3 * heads * part)
        .astype(F32)
    )


def window_mask(plan, segments, block_index):
    key_count = plan.length + plan.reach * plan.block
    if plan.whole:
        query_segs, key_segs = segments, segments
    else:
        leading = jnp.full((plan.own_seqs, plan.reach * plan.block), -1, jnp.int32)
        padded = jnp.concatenate([leading, segments], axis=1)
        start = block_index * plan.block
        query_segs = lax.dynamic_slice_in_dim(segments, start, plan.block, 1)
        key_segs = lax.dynamic_slice_in_dim(padded, start, key_count, 1)
    query_place = jnp.arange(plan.length, dtype=jnp.int32)[:, None] + plan.reach * plan.block
    key_place = jnp.arange(key_count, dtype=jnp.int32)[None, :]
    near = (key_place <= query_place) & (query_place - key_place < WINDOW)
    return (key_segs[:, None, :] == query_segs[:, :, None]) & near[None]


def with_earlier(plan, own):
    arrived = [own]
    for _ in range(plan.reach):
        arrived.append(shifted(arrived[-1], "blk", 1))
    return jnp.concatenate(arrived[::-1], axis=1) if plan.reach else own


def to_earlier(plan, grads):
    if not plan.reach:
        return grads
    block = plan.block
    total = grads[:, :block]
    for step in range(1, plan.reach + 1):
        total = (
            shifted(total.astype(BF16), "blk", -1).astype(F32)
            + grads[:, step * block : (step + 1) * block]
        )
    return total


def scores_of(queries, keys, allowed):
    scores = jnp.einsum("sqhd,skhd->shqk", queries, keys, preferred_element_type=F32)
    return jnp.where(allowed[:, None], scores, MASKED_SCORE)


def attend(queries, keys, values, allowed):
    scores = scores_of(queries, keys, allowed)
    top_score = jnp.max(scores, axis=-1, keepdims=True)
    exp_terms = jnp.exp(scores - top_score)
    totals = jnp.sum(exp_terms, axis=-1, keepdims=True)
    probs_low = (exp_terms / totals).astype(BF16)
    attended = jnp.einsum("shqk,skhd->sqhd", probs_low, values, preferred_element_type=F32)
    return attended, top_score + jnp.log(totals)


def attend_back(queries, keys, values, allowed, log_total, attended_grad):
    probs = jnp.exp(scores_of(queries, keys, allowed) - log_total)
    probs_low = probs.astype(BF16)
    values_grad = jnp.einsum(
        "shqk,sqhd->skhd", probs_low, attended_grad, preferred_element_type=F32
    )
    probs_grad = jnp.einsum("sqhd,skhd->shqk", attended_grad, values, preferred_element_type=F32)
    row_dot = jnp.sum(probs_grad * probs, axis=-1, keepdims=True)
    scores_low = (probs * (probs_grad - row_dot)).astype(BF16)
    queries_grad = jnp.einsum("shqk,skhd->sqhd", scores_low, keys, preferred_element_type=F32)
    keys_grad = jnp.einsum("shqk,sqhd->skhd", scores_low, queries, preferred_element_type=F32)
    return queries_grad, keys_grad, values_grad


def forward(plan, stream, qkv, dense, gains, scale_vec, allowed):
    width = plan.width
    head_dim = scale_vec.shape[0]
    part = qkv.shape[1] // 3
    local_heads = part // head_dim
    split = (plan.own_seqs, plan.length, local_heads, head_dim)
    out_w, up_w, down_w = dense[:, :width], dense[:, width:-width], dense[:, -width:]
    normed, factor_one = normalize(stream, gains[0])
    normed_all = gather_tokens(plan, normed.astype(BF16))
    projected = dot(normed_all, qkv)
    query_pre = projected[:, :part].reshape(split)
    queries = (query_pre * scale_vec).astype(BF16)
    keys = with_earlier(plan, projected[:, part : 2 * part].astype(BF16).reshape(split))
    values = with_earlier(plan, projected[:, 2 * part :].astype(BF16).reshape(split))
    attended_part, log_total = attend(queries, keys, values, allowed)
    attended = heads_to_tokens(plan, attended_part.astype(BF16).reshape(-1, part))
    middle = stream + dot(attended, out_w)
    normed_two, factor_two = normalize(middle, gains[1])
    normed_two = normed_two.astype(BF16)
    hidden = dot(normed_two, up_w)
    active = (hidden * jax.nn.sigmoid(hidden)).astype(BF16)
    result = middle + dot(active, down_w)
    kept = (
        stream, factor_one, normed_all, query_pre, queries, keys, values, log_total,
        attended, middle, factor_two, normed_two, hidden, active,
    )
    return result, kept


def backward(plan, upper, kept, qkv, dense, gains, scale_vec, allowed):
    (
        stream, factor_one, normed_all, query_pre, queries, keys, values, log_total,
        attended, middle, factor_two, normed_two, hidden, active,
    ) = kept
    width = plan.width
    head_dim = scale_vec.shape[0]
    part = qkv.shape[1] // 3
    out_w, up_w, down_w = dense[:, :width], dense[:, width:-width], dense[:, -width:]
    upper_low = upper.astype(BF16)
    down_grad = dot_rows(active, upper_low)
    active_grad = dot_cols(upper_low, down_w)
    gate = jax.nn.sigmoid(hidden)
    hidden_low = (active_grad * gate * (1.0 + hidden * (1.0 - gate))).astype(BF16)
    up_grad = dot_rows(normed_two, hidden_low)
    extra_two, mlp_gain_grad = norm_back(dot_cols(hidden_low, up_w), middle, factor_two, gains[1])
    middle_grad = upper + extra_two
    middle_low = middle_grad.astype(BF16)
    out_grad = dot_rows(attended, middle_low)
    dense_grad = jnp.concatenate([out_grad, up_grad, down_grad], axis=1).astype(BF16)
    dense_own = lax.psum_scatter(dense_grad, ALL, scatter_dimension=0, tiled=True)
    attended_grad = tokens_to_heads(plan, dot_cols(middle_low, out_w).astype(BF16))
    queries_grad, keys_grad, values_grad = attend_back(
        queries, keys, values, allowed, log_total, attended_grad.reshape(queries.shape)
    )
    query_bar = queries_grad.astype(BF16).astype(F32)
    scale_vec_grad = jnp.sum((query_bar * query_pre).reshape(-1, head_dim), axis=0)
    query_low = (query_bar * scale_vec).astype(BF16).reshape(-1, part)
    keys_low = to_earlier(plan, keys_grad).astype(BF16).reshape(-1, part)
    values_low = to_earlier(plan, values_grad).astype(BF16).reshape(-1, part)
    projected_low = jnp.concatenate([query_low, keys_low, values_low], axis=1)
    normed_grad = scatter_tokens(plan, dot_cols(projected_low, qkv))
    qkv_own = scatter_qkv(dot_rows(normed_all, projected_low))
    extra_one, attn_gain_grad = norm_back(normed_grad, stream, factor_one, gains[0])
    lower = middle_grad + extra_one
    return lower, qkv_own, dense_own, (attn_gain_grad, mlp_gain_grad), scale_vec_grad


def general_device(
    tokens,
    segments,
    qkv_weight,
    out_weight,
    up_weight,
    down_weight,
    attn_gain,
    mlp_gain,
    scale_param,
    cotangent,
):
    plan = Plan(tokens)
    layers, head_dim = scale_param.shape
    block_index = lax.axis_index("blk")
    scale_vecs = SCALE_BASE / math.sqrt(head_dim) * jax.nn.softplus(scale_param)
    own_gains = jnp.concatenate([attn_gain, mlp_gain], axis=0)
    gains = (
        lax.all_gather(own_gains.reshape(1, -1), ALL, axis=0, tiled=True)
        .reshape(-1, 2 * layers, attn_gain.shape[1])
        .transpose(1, 0, 2)
        .reshape(2 * layers, plan.width)
        .astype(F32)
    )
    if plan.whole:
        segments = lax.dynamic_slice_in_dim(
            segments, block_index * plan.own_seqs, plan.own_seqs, 0
        )
    allowed = window_mask(plan, segments, block_index)
    stream = to_plan(plan, tokens).astype(F32)
    qkvs, denses, kept = [], [], []
    for layer in range(layers):
        qkvs.append(gather_qkv(qkv_weight[layer]))
        own = jnp.concatenate([out_weight[layer], up_weight[layer], down_weight[layer]], axis=1)
        denses.append(lax.all_gather(own, ALL, axis=0, tiled=True))
        layer_gains = (gains[layer], gains[layers + layer])
        stream, saved = forward(
            plan, stream, qkvs[layer], denses[layer], layer_gains, scale_vecs[layer], allowed
        )
        kept.append(saved)
    layer_out = from_plan(plan, stream.astype(BF16))
    upper = to_plan(plan, cotangent).astype(F32)
    qkv_grads, dense_grads = [None] * layers, [None] * layers
    gain_grads, scale_grads = [None] * layers, [None] * layers
    for layer in reversed(range(layers)):
        layer_gains = (gains[layer], gains[layers + layer])
        upper, qkv_grads[layer], dense_grads[layer], gain_grads[layer], scale_grads[layer] = (
            backward(
                plan, upper, kept[layer], qkvs[layer], denses[layer], layer_gains,
                scale_vecs[layer], allowed,
            )
        )
    input_grad = from_plan(plan, upper.astype(BF16)).astype(F32)
    small = jnp.concatenate(
        [g[0] for g in gain_grads] + [g[1] for g in gain_grads] + scale_grads, axis=0
    )
    total = lax.psum(small, ALL)
    gain_total = total[: 2 * layers * plan.width].reshape(2 * layers, plan.width)
    owner = lax.axis_index(ALL)
    gain_rows = attn_gain.shape[1]
    own_total = lax.dynamic_slice_in_dim(gain_total, owner * gain_rows, gain_rows, 1)
    scale_total = total[2 * layers * plan.width :].reshape(layers, head_dim)
    scale_grad = scale_total * (SCALE_BASE / math.sqrt(head_dim)) * jax.nn.sigmoid(scale_param)
    dense_all = jnp.stack(dense_grads).astype(F32)
    width = plan.width
    return (
        layer_out,
        input_grad,
        jnp.stack(qkv_grads),
        dense_all[:, :, :width],
        dense_all[:, :, width:-width],
        dense_all[:, :, -width:],
        own_total[:layers],
        own_total[layers:],
        scale_grad,
    )


Q_ROWS = 256
KERNEL = pltpu.CompilerParams(vmem_limit_bytes=32 * 1024 * 1024)
LIGHT = pl.CostEstimate(flops=1 << 20, bytes_accessed=1 << 20, transcendentals=0)


def in_hbm(*arrays):
    return [pltpu.with_memory_space_constraint(array, pltpu.HBM) for array in arrays]


def allowed_keys(col, row, first):
    count = first + row.shape[1]
    key_place = lax.broadcasted_iota(jnp.int32, (count, row.shape[1]), 0)
    query_place = lax.broadcasted_iota(jnp.int32, (count, row.shape[1]), 1) + first
    return (col[:count] == row) & (key_place <= query_place)


def allowed_piece(col, row, start, first):
    same = col == row
    if start + col.shape[0] <= first:
        return same
    key_place = lax.broadcasted_iota(jnp.int32, same.shape, 0) + start
    return same & (key_place <= lax.broadcasted_iota(jnp.int32, same.shape, 1) + first)


def token_places(length, heads, token_rows, block_rows=Q_ROWS):
    for first in range(0, length, block_rows):
        parts = []
        for start in range(0, block_rows, token_rows):
            place = (first + start) // token_rows
            parts.append((start, place % heads, place // heads * token_rows))
        yield first, parts


FORWARD_ROWS, FORWARD_KEYS = 1024, 512


def attend_kernel(token_rows, proj_ref, scale_ref, col_ref, row_ref, out_ref, lse_ref):
    length = proj_ref.shape[-1]
    queries = (proj_ref[0, 0] * scale_ref[...]).astype(BF16)
    keys = proj_ref[1, 0].T.astype(BF16)
    values = proj_ref[2, 0].astype(BF16)
    for first, parts in token_places(length, out_ref.shape[0], token_rows, FORWARD_ROWS):
        end = first + FORWARD_ROWS
        block, row = queries[:, first:end], row_ref[:, first:end]
        pieces = []
        for start in range(0, end, FORWARD_KEYS):
            scores = jnp.dot(keys[start : start + FORWARD_KEYS], block, preferred_element_type=F32)
            allowed = allowed_piece(col_ref[start : start + FORWARD_KEYS], row, start, first)
            pieces.append(jnp.where(allowed, scores, MASKED_SCORE))
        top = functools.reduce(
            jnp.maximum, [jnp.max(piece, axis=0, keepdims=True) for piece in pieces]
        )
        total, attended = 0.0, 0.0
        for i, piece in enumerate(pieces):
            terms = jnp.exp(piece - top)
            total += jnp.sum(terms, axis=0, keepdims=True)
            attended += jnp.dot(
                values[:, i * FORWARD_KEYS : (i + 1) * FORWARD_KEYS],
                terms.astype(BF16),
                preferred_element_type=F32,
            )
        attended = (attended * (1.0 / total)).astype(BF16)
        lse_ref[0, :, first:end] = top + jnp.log(total)
        for start, owner, offset in parts:
            out_ref[owner, 0, :, offset : offset + token_rows] = attended[
                :, start : start + token_rows
            ]


def attend_rows(projected, scale_vec, segments, owners, token_rows):
    head_dim = scale_vec.shape[0]
    length = projected.shape[1]
    local_heads = projected.shape[0] // 3 // head_dim
    tokens = length // owners
    attended, log_total = pl.pallas_call(
        functools.partial(attend_kernel, token_rows),
        grid=(local_heads,),
        in_specs=[
            pl.BlockSpec((3, 1, head_dim, length), lambda h: (0, h, 0, 0)),
            pl.BlockSpec((head_dim, 1), lambda h: (0, 0)),
            pl.BlockSpec((length, 1), lambda h: (0, 0)),
            pl.BlockSpec((1, length), lambda h: (0, 0)),
        ],
        out_specs=[
            pl.BlockSpec((owners, 1, head_dim, tokens), lambda h: (0, h, 0, 0)),
            pl.BlockSpec((1, 1, length), lambda h: (h, 0, 0)),
        ],
        out_shape=[
            jax.ShapeDtypeStruct((owners, local_heads, head_dim, tokens), BF16),
            jax.ShapeDtypeStruct((local_heads, 1, length), F32),
        ],
        compiler_params=KERNEL,
        cost_estimate=LIGHT,
    )(
        projected.reshape(3, local_heads, head_dim, length),
        scale_vec.reshape(head_dim, 1),
        segments.reshape(length, 1),
        segments.reshape(1, length),
    )
    return attended.reshape(owners, local_heads * head_dim, tokens), log_total


def attend_back_kernel(
    token_rows,
    proj_ref,
    grad_ref,
    lse_ref,
    scale_ref,
    col_ref,
    row_ref,
    out_ref,
    scale_grad_ref,
    keys_acc,
    values_acc,
):
    length = proj_ref.shape[-1]
    scale = scale_ref[...]
    query_pre = proj_ref[0, 0]
    queries = (query_pre * scale).astype(BF16)
    keys_t = proj_ref[1, 0].astype(BF16)
    keys = proj_ref[1, 0].T.astype(BF16)
    values = proj_ref[2, 0].T.astype(BF16)
    keys_acc[...] = jnp.zeros_like(keys_acc)
    values_acc[...] = jnp.zeros_like(values_acc)
    scale_grad = jnp.zeros((scale.shape[0], 1), F32)
    for first, parts in token_places(length, grad_ref.shape[0], token_rows):
        end = first + Q_ROWS
        block = queries[:, first:end]
        grad = jnp.concatenate(
            [grad_ref[owner, 0, :, at : at + token_rows] for _, owner, at in parts], axis=1
        )
        scores = jnp.dot(keys[:end], block, preferred_element_type=F32)
        allowed = allowed_keys(col_ref[...], row_ref[:, first:end], first)
        scores = jnp.where(allowed, scores, MASKED_SCORE)
        probs = jnp.exp(scores - lse_ref[0, :, first:end])
        probs_grad = jnp.dot(values[:end], grad, preferred_element_type=F32)
        row_dot = jnp.sum(probs_grad * probs, axis=0, keepdims=True)
        scores_low = (probs * (probs_grad - row_dot)).astype(BF16)
        values_acc[:, :end] += lax.dot_general(
            grad, probs.astype(BF16), NT, preferred_element_type=F32
        )
        keys_acc[:, :end] += lax.dot_general(
            block, scores_low, NT, preferred_element_type=F32
        )
        query_bar = jnp.dot(keys_t[:, :end], scores_low, preferred_element_type=F32)
        query_bar = query_bar.astype(BF16).astype(F32)
        scale_grad += jnp.sum(query_bar * query_pre[:, first:end], axis=1, keepdims=True)
        out_ref[0, 0, :, first:end] = (query_bar * scale).astype(BF16)
    out_ref[1, 0] = keys_acc[...].astype(BF16)
    out_ref[2, 0] = values_acc[...].astype(BF16)
    spread = jnp.broadcast_to(scale_grad, scale_grad_ref.shape)

    @pl.when(pl.program_id(0) == 0)
    def _():
        scale_grad_ref[...] = spread

    @pl.when(pl.program_id(0) > 0)
    def _():
        scale_grad_ref[...] += spread


def attend_back_rows(projected, attended_grad, log_total, scale_vec, segments, token_rows):
    head_dim = scale_vec.shape[0]
    length = projected.shape[1]
    local_heads = projected.shape[0] // 3 // head_dim
    owners, _, tokens = attended_grad.shape
    lanes = 128
    grads, scale_grad = pl.pallas_call(
        functools.partial(attend_back_kernel, token_rows),
        grid=(local_heads,),
        in_specs=[
            pl.BlockSpec((3, 1, head_dim, length), lambda h: (0, h, 0, 0)),
            pl.BlockSpec((owners, 1, head_dim, tokens), lambda h: (0, h, 0, 0)),
            pl.BlockSpec((1, 1, length), lambda h: (h, 0, 0)),
            pl.BlockSpec((head_dim, 1), lambda h: (0, 0)),
            pl.BlockSpec((length, 1), lambda h: (0, 0)),
            pl.BlockSpec((1, length), lambda h: (0, 0)),
        ],
        out_specs=[
            pl.BlockSpec((3, 1, head_dim, length), lambda h: (0, h, 0, 0)),
            pl.BlockSpec((head_dim, lanes), lambda h: (0, 0)),
        ],
        out_shape=[
            pltpu.HBM((3, local_heads, head_dim, length), BF16),
            pltpu.HBM((head_dim, lanes), F32),
        ],
        scratch_shapes=[
            pltpu.VMEM((head_dim, length), F32),
            pltpu.VMEM((head_dim, length), F32),
        ],
        compiler_params=KERNEL,
        cost_estimate=LIGHT,
    )(
        *in_hbm(
            projected.reshape(3, local_heads, head_dim, length),
            attended_grad.reshape(owners, local_heads, head_dim, tokens),
        ),
        log_total,
        scale_vec.reshape(head_dim, 1),
        segments.reshape(length, 1),
        segments.reshape(1, length),
    )
    return grads.reshape(3 * local_heads * head_dim, length), scale_grad[:, 0]


def dense_grad_kernel(
    core_ref, attended_ref, normed_ref, active_ref, out_bar, up_bar, down_bar,
    own_ref, other_ref, normed_t, active_t,
):
    tile = pl.program_id(0)
    rows, width = 8 * own_ref.shape[3], out_bar.shape[1]

    @pl.when(tile == 0)
    def _():
        normed_t[...] = normed_ref[...].astype(F32).T.astype(BF16)
        active_t[...] = active_ref[...].astype(F32).T.astype(BF16)

    start = pl.multiple_of(tile * rows, rows)
    first_core = core_ref[2] == 0
    lefts = (attended_ref, normed_t, active_t)
    for i, (left, right) in enumerate(zip(lefts, (out_bar, up_bar, down_bar))):
        grad = jnp.dot(left[pl.ds(start, rows), :], right[...], preferred_element_type=F32)
        grad = grad.reshape(2, 2, 2, rows // 8, width)
        one, two = grad[:, :, 0], grad[:, :, 1]
        own_ref[:, :, 0, :, i * width : (i + 1) * width] = jnp.where(
            first_core, one, two
        ).astype(BF16)
        other_ref[:, :, 0, :, i * width : (i + 1) * width] = jnp.where(
            first_core, two, one
        ).astype(BF16)


def dense_grads(attended_t, normed, active, out_bar, up_bar, down_bar):
    width, tokens = attended_t.shape
    own = width // 32
    whole = pl.BlockSpec((tokens, width), lambda i, core: (0, 0))
    rows = pl.BlockSpec((2, 2, 1, own, 3 * width), lambda i, core: (0, 0, i, 0, 0))
    shape = pltpu.HBM((2, 2, 4, own, 3 * width), BF16)
    return pl.pallas_call(
        dense_grad_kernel,
        grid_spec=pltpu.PrefetchScalarGridSpec(
            num_scalar_prefetch=1,
            grid=(4,),
            in_specs=[pl.BlockSpec((width, tokens), lambda i, core: (0, 0))] + [whole] * 5,
            out_specs=[rows, rows],
            scratch_shapes=[pltpu.VMEM((width, tokens), BF16)] * 2,
        ),
        out_shape=[shape, shape],
        compiler_params=KERNEL,
        cost_estimate=LIGHT,
    )(place(), *in_hbm(attended_t, normed, active, out_bar, up_bar, down_bar))


def place():
    head = lax.axis_index("head")
    return jnp.stack([lax.axis_index("blk"), head // 2, head % 2]).astype(jnp.int32)


def assemble_kernel(place_ref, *refs):
    pieces, whole_ref = refs[:10], refs[10]
    half = whole_ref.shape[-1] // 2
    blk, row, core = place_ref[0], place_ref[1], place_ref[2]
    for i in range(2):
        at_core = core if i == 0 else 1 - core
        own, across, beside, one, two = pieces[5 * i : 5 * i + 5]
        whole_ref[0, blk, row, at_core] = own[0]
        whole_ref[0, 1 - blk, row, at_core] = across[0]
        whole_ref[0, blk, 1 - row, at_core] = beside[0]
        whole_ref[0, 1 - blk, 1 - row, at_core, :, :half] = one[0]
        whole_ref[0, 1 - blk, 1 - row, at_core, :, half:] = two[0]


def assemble(pieces):
    batch, own, columns = pieces[0].shape
    specs = [
        pl.BlockSpec((1, own, piece.shape[-1]), lambda i, at: (i, 0, 0))
        for piece in pieces
    ]
    whole = pl.pallas_call(
        assemble_kernel,
        grid_spec=pltpu.PrefetchScalarGridSpec(
            num_scalar_prefetch=1,
            grid=(batch,),
            in_specs=specs,
            out_specs=pl.BlockSpec((1, 2, 2, 2, own, columns), lambda i, at: (i, 0, 0, 0, 0, 0)),
        ),
        out_shape=jax.ShapeDtypeStruct((batch, 2, 2, 2, own, columns), BF16),
        compiler_params=KERNEL,
        cost_estimate=LIGHT,
    )(place(), *pieces)
    return whole.reshape(-1, columns)


def assemble_columns_kernel(place_ref, along_ref, across_ref, whole_ref, *extra_ref):
    blk = place_ref[0]
    columns = whole_ref.shape[-1]
    whole_ref[0, blk] = along_ref[0, :, :columns]
    whole_ref[0, 1 - blk] = across_ref[0, :, :columns]
    for extra in extra_ref:
        extra[0, blk] = along_ref[0, :, columns:]
        extra[0, 1 - blk] = across_ref[0, :, columns:]


def assemble_columns(along, across, columns):
    batch, own, both = along.shape
    rows = pl.BlockSpec((1, own, both), lambda i, at: (i, 0, 0))
    shapes = [(batch, 2, own, columns)]
    if both > columns:
        shapes.append((batch, 2, own, both - columns))
    parts = pl.pallas_call(
        assemble_columns_kernel,
        grid_spec=pltpu.PrefetchScalarGridSpec(
            num_scalar_prefetch=1,
            grid=(batch,),
            in_specs=[rows, rows],
            out_specs=[pl.BlockSpec((1,) + s[1:], lambda i, at: (i, 0, 0, 0)) for s in shapes],
        ),
        out_shape=[pltpu.HBM(s, BF16) for s in shapes],
        compiler_params=KERNEL,
        cost_estimate=LIGHT,
    )(place(), *in_hbm(along, across))
    return [part.reshape(-1, part.shape[-1]) for part in parts]


def assemble_wide_kernel(place_ref, along_ref, across_ref, whole_ref):
    blk = place_ref[0]
    own, columns = along_ref.shape[1], whole_ref.shape[-1]
    for i in range(along_ref.shape[-1] // columns):
        place, part = slice(i * own, (i + 1) * own), slice(i * columns, (i + 1) * columns)
        whole_ref[0, blk, place, :] = along_ref[0, :, part]
        whole_ref[0, 1 - blk, place, :] = across_ref[0, :, part]


def assemble_wide(along, across, columns):
    batch, own, wide = along.shape
    rows = own * (wide // columns)
    piece = pl.BlockSpec((1, own, wide), lambda i, at: (i, 0, 0))
    whole = pl.pallas_call(
        assemble_wide_kernel,
        grid_spec=pltpu.PrefetchScalarGridSpec(
            num_scalar_prefetch=1,
            grid=(batch,),
            in_specs=[piece, piece],
            out_specs=pl.BlockSpec((1, 2, rows, columns), lambda i, at: (i, 0, 0, 0)),
        ),
        out_shape=pltpu.HBM((batch, 2, rows, columns), BF16),
        compiler_params=KERNEL,
        cost_estimate=LIGHT,
    )(place(), *in_hbm(along, across))
    return whole.reshape(-1, columns)


def project_kernel(with_norm, place_ref, *refs):
    pieces, (gain_ref, weight_ref, normed_ref, projected_ref) = refs[:4], refs[4:]
    head = place_ref[1] * 2 + place_ref[2]
    rows = pieces[0].shape[0]
    for i, piece in enumerate(pieces):
        value = piece[...]
        if with_norm:
            stream = value.astype(F32)
            factor = lax.rsqrt(jnp.mean(stream * stream, axis=-1, keepdims=True) + EPSILON)
            value = (stream * factor * gain_ref[...]).astype(BF16)
        normed_ref[pl.ds(pl.multiple_of((head ^ i) * rows, rows), rows), :] = value
    projected = jnp.dot(normed_ref[...], weight_ref[...], preferred_element_type=F32)
    projected_ref[...] = projected.T


def project(pieces, gain, weight, with_norm, token_rows):
    tokens, width = pieces[0].shape
    length, columns = 4 * tokens, weight.shape[1]
    groups = tokens // token_rows
    piece = pl.BlockSpec((token_rows, width), lambda g, at: (g, 0))
    return pl.pallas_call(
        functools.partial(project_kernel, with_norm),
        grid_spec=pltpu.PrefetchScalarGridSpec(
            num_scalar_prefetch=1,
            grid=(groups,),
            in_specs=[piece] * 4
            + [
                pl.BlockSpec((1, width), lambda g, at: (0, 0)),
                pl.BlockSpec((width, columns), lambda g, at: (0, 0)),
            ],
            out_specs=[
                pl.BlockSpec((4 * token_rows, width), lambda g, at: (g, 0)),
                pl.BlockSpec((columns, 4 * token_rows), lambda g, at: (0, g)),
            ],
        ),
        out_shape=[
            pltpu.HBM((length, width), BF16),
            jax.ShapeDtypeStruct((columns, length), F32),
        ],
        compiler_params=KERNEL,
        cost_estimate=LIGHT,
    )(place(), *in_hbm(*pieces), gain.reshape(1, width), *in_hbm(weight))


def project_back_kernel(
    place_ref, bars_ref, weight_ref, normed_ref, own_ref, other_ref, grad_ref, bars_t
):
    @pl.when(pl.program_id(0) == 0)
    def _():
        bars_t[...] = bars_ref[...].astype(F32).T.astype(BF16)

    upper = lax.dot_general(bars_t[...], weight_ref[...], NT, preferred_element_type=F32)
    upper = upper.reshape(2, 2, 2, -1, upper.shape[-1])
    first_core = place_ref[2] == 0
    one, two = upper[:, :, 0], upper[:, :, 1]
    own_ref[...] = jnp.where(first_core, one, two)
    other_ref[...] = jnp.where(first_core, two, one).astype(BF16)
    grad = lax.dot_general(normed_ref[...], bars_t[...], TN, preferred_element_type=F32)
    grad_ref[...] = grad.astype(BF16)


def project_back(bars, weight, normed, token_rows):
    columns, length = bars.shape
    width = weight.shape[0]
    tile = width // 2
    quarter = pl.BlockSpec((2, 2, token_rows, tile), lambda i, at: (0, 0, 0, i))
    return pl.pallas_call(
        project_back_kernel,
        grid_spec=pltpu.PrefetchScalarGridSpec(
            num_scalar_prefetch=1,
            grid=(2,),
            in_specs=[
                pl.BlockSpec((columns, length), lambda i, at: (0, 0)),
                pl.BlockSpec((tile, columns), lambda i, at: (i, 0)),
                pl.BlockSpec((length, tile), lambda i, at: (0, i)),
            ],
            out_specs=[quarter, quarter, pl.BlockSpec((tile, columns), lambda i, at: (i, 0))],
            scratch_shapes=[pltpu.VMEM((length, columns), BF16)],
        ),
        out_shape=[
            pltpu.HBM((2, 2, token_rows, width), F32),
            pltpu.HBM((2, 2, token_rows, width), BF16),
            pltpu.HBM((width, columns), BF16),
        ],
        compiler_params=KERNEL,
        cost_estimate=LIGHT,
    )(place(), *in_hbm(bars, weight, normed))


def rows_back_kernel(place_ref, bars_ref, weight_ref, own_ref, other_ref, bars_t):
    @pl.when(pl.program_id(0) == 0)
    def _():
        bars_t[...] = bars_ref[...].astype(F32).T.astype(BF16)

    upper = lax.dot_general(bars_t[...], weight_ref[...], NT, preferred_element_type=F32)
    upper = upper.reshape(2, 2, 2, -1, upper.shape[-1])
    first_core = place_ref[2] == 0
    one, two = upper[:, :, 0], upper[:, :, 1]
    own_ref[...] = jnp.where(first_core, one, two)
    other_ref[...] = jnp.where(first_core, two, one).astype(BF16)


def rows_back(bars, weight, token_rows):
    columns, length = bars.shape
    width = weight.shape[0]
    tile = width // 2
    quarter = pl.BlockSpec((2, 2, token_rows, tile), lambda i, at: (0, 0, 0, i))
    return pl.pallas_call(
        rows_back_kernel,
        grid_spec=pltpu.PrefetchScalarGridSpec(
            num_scalar_prefetch=1,
            grid=(2,),
            in_specs=[
                pl.BlockSpec((columns, length), lambda i, at: (0, 0)),
                pl.BlockSpec((tile, columns), lambda i, at: (i, 0)),
            ],
            out_specs=[quarter, quarter],
            scratch_shapes=[pltpu.VMEM((length, columns), BF16)],
        ),
        out_shape=[
            pltpu.HBM((2, 2, token_rows, width), F32),
            pltpu.HBM((2, 2, token_rows, width), BF16),
        ],
        compiler_params=KERNEL,
        cost_estimate=LIGHT,
    )(place(), *in_hbm(bars, weight))


def weight_back_kernel(bars_ref, normed_ref, grad_ref):
    grad = jnp.dot(bars_ref[...], normed_ref[...], preferred_element_type=F32)
    grad_ref[...] = grad.T.astype(BF16)


def weight_back(bars, normed):
    columns, length = bars.shape
    width = normed.shape[1]
    tile = width // 5
    return pl.pallas_call(
        weight_back_kernel,
        grid=(5,),
        in_specs=[
            pl.BlockSpec((columns, length), lambda i: (0, 0)),
            pl.BlockSpec((length, tile), lambda i: (0, i)),
        ],
        out_specs=pl.BlockSpec((tile, columns), lambda i: (i, 0)),
        out_shape=pltpu.HBM((width, columns), BF16),
        compiler_params=KERNEL,
        cost_estimate=LIGHT,
    )(*in_hbm(bars, normed))


def tied(*arrays):
    return lax.optimization_barrier(arrays)


def swapped(array, axis, mask):
    size = lax.axis_size(axis)
    return lax.ppermute(array, axis, [(i, i ^ mask) for i in range(size)])


def pick(array, index, axis=0):
    return lax.dynamic_index_in_dim(array, index, axis, keepdims=False)


def swap_halves(array):
    me = lax.axis_index("blk")
    got = swapped(pick(array, 1 - me), "blk", 1)
    kept = pick(array, me)
    return jnp.stack([jnp.where(me == 0, kept, got), jnp.where(me == 0, got, kept)])


def scatter_row(halves):
    row = lax.axis_index("head") // 2
    got = swapped(pick(halves, 1 - row, 1).astype(BF16), "head", 2).astype(F32)
    return (pick(halves, row, 1) + got).reshape(-1, halves.shape[-1])


def over_head(parts):
    return lax.all_to_all(parts, "head", split_axis=0, concat_axis=0, tiled=True)


def qkv_columns(rows, extra):
    own, width = rows.shape
    part = width // 3 // 4
    sent = rows.reshape(own, 3, 4, part).transpose(2, 0, 1, 3).reshape(4, own, 3 * part)
    if extra is not None:
        sent = jnp.concatenate([sent, jnp.broadcast_to(extra[None], (4,) + extra.shape)], axis=2)
    return over_head(sent)


def along_batch(piece):
    return lax.all_gather(piece, "batch", axis=0, tiled=False)


def other_core(array):
    return swapped(array, "head", 1)


def to_beside(across):
    return swapped(across[..., : across.shape[-1] // 2], "head", 2)


def to_across(beside):
    return swapped(beside[..., beside.shape[-1] // 2 :], "blk", 1)


def over_batch(parts):
    return lax.psum_scatter(parts.astype(BF16), "batch", scatter_dimension=0, tiled=False)


def across_sum(halves):
    blk = lax.axis_index("blk")
    got = swapped(pick(halves, 1 - blk), "blk", 1).astype(F32)
    return (pick(halves, blk).astype(F32) + got).astype(BF16)


def columns_to_rows(moved):
    rows = moved.shape[1]
    return moved.reshape(4, rows, 3, -1).transpose(1, 2, 0, 3).reshape(rows, -1).astype(F32)


def quarter(parts, blk, row):
    one, two = (pick(pick(part, blk), row).astype(F32) for part in parts)
    return one + two


def diagonal_rows(parts):
    blk, row = place()[:2]
    rows = quarter(parts, 1 - blk, 1 - row).astype(BF16)
    half = rows.shape[-1] // 2
    return rows[..., :half], rows[..., half:]


def neighbour_rows(parts, one, two):
    blk, row = place()[:2]
    half = one.shape[-1]
    across, beside = quarter(parts, 1 - blk, row), quarter(parts, blk, 1 - row)
    across = jnp.concatenate([across[..., :half], across[..., half:] + two.astype(F32)], axis=-1)
    beside = jnp.concatenate([beside[..., :half] + one.astype(F32), beside[..., half:]], axis=-1)
    return across.astype(BF16), beside.astype(BF16)


def sent_beside_and_across(across, beside):
    return swapped(across, "blk", 1), swapped(beside, "head", 2)


def heads_grad(weight, out_bar):
    return dot_cols(weight, out_bar).astype(BF16).reshape(4, -1, out_bar.shape[0])


def own_quarter(parts):
    blk, row = place()[:2]
    return quarter(parts, blk, row)


def own_sum(own, *more):
    return sum((part.astype(F32) for part in more), own).astype(BF16)


def sum_over(array, *hops):
    for axis, mask in hops:
        array = array + swapped(array, axis, mask)
    return array


def gain_back(weight, weight_grad, gain):
    return jnp.sum(weight.astype(F32) * weight_grad, axis=-1) / gain.astype(F32)


def lower_of(upper, stream, factor, gain):
    return norm_back(upper, stream, factor, gain)[0]


def spread_device(
    tokens,
    segments,
    qkv_weight,
    out_weight,
    up_weight,
    down_weight,
    attn_gain,
    mlp_gain,
    scale_param,
    cotangent,
):
    layers, head_dim = scale_param.shape
    _, token_rows, width = tokens.shape
    scale_vecs = SCALE_BASE / math.sqrt(head_dim) * jax.nn.softplus(scale_param)
    segments = pick(segments, lax.axis_index("blk"))
    own_gains = jnp.concatenate([attn_gain, mlp_gain], axis=0)

    part3 = 3 * width // 4
    dense_own = [
        jnp.concatenate([out_weight[i], up_weight[i], down_weight[i]], axis=1) for i in (0, 1)
    ]

    first = swap_halves(tokens).reshape(-1, width)
    columns = qkv_columns(qkv_weight[0], own_gains.T)
    columns, first, cotangent = tied(columns.reshape(-1, columns.shape[-1]), first, cotangent)
    stream = first.astype(F32)
    along = along_batch(columns)
    far, near = swapped(first, "head", 2), other_core(first)
    both = other_core(far)
    upper = swap_halves(cotangent)
    along, near, far, both, dense_near, upper = tied(
        along, near, far, both, dense_own[0], upper
    )
    token_pieces = (first, near, far, both)
    dense_near = along_batch(dense_near)
    qkv_across = swapped(along, "blk", 1)
    next_columns = jnp.concatenate(list(qkv_columns(qkv_weight[1], None)), axis=1)
    qkv_across, dense_near, next_columns = tied(qkv_across, dense_near, next_columns)
    across, beside = swapped(dense_near, "blk", 1), swapped(dense_near, "head", 2)
    next_both = along_batch(jnp.stack([next_columns, dense_own[1]]))
    weight, gains = assemble_columns(along, qkv_across, part3)
    qkvs = [weight]
    gains = gains.T.astype(F32)

    kept, denses = [], []
    for layer in range(layers):
        normed, factor_one = normalize(stream, gains[layer])
        if layer == 1:
            normed = normed.astype(BF16)
            far, near = swapped(normed, "head", 2), other_core(normed)
            far, next_across, dense_next = tied(far, next_across, dense_next)
            across, beside = swapped(dense_next, "blk", 1), swapped(dense_next, "head", 2)
            token_pieces = (normed, near, far, other_core(far))
            qkvs.append(assemble_wide(next_along, next_across, part3))
        normed_all, projected = project(
            token_pieces, gains[layer], qkvs[layer], layer == 0, token_rows
        )
        attended, log_total = attend_rows(
            projected, scale_vecs[layer], segments, 4, token_rows
        )
        attended, across, beside = tied(attended, across, beside)
        one, two = to_beside(across), to_across(beside)
        if layer == 0:
            two, next_both = tied(two, next_both)
            next_along, dense_next = next_both[:, 0], next_both[:, 1]
            next_across = swapped(next_along, "blk", 1)
            attended_t, one, two = tied(over_head(attended), one, two)
        else:
            dense_near = dense_next
            attended_t, one, two = tied(over_head(attended), one, two)
        pieces = (dense_near, across, beside, one, two)
        pieces += tuple(other_core(piece) for piece in pieces)
        attended_t = attended_t.reshape(width, -1)
        denses.append(assemble(pieces))
        dense = denses[layer]
        out_w, up_w, down_w = dense[:, :width], dense[:, width:-width], dense[:, -width:]
        middle = stream + dot_rows(attended_t, out_w)
        normed_two, factor_two = normalize(middle, gains[layers + layer])
        normed_two = normed_two.astype(BF16)
        hidden = dot(normed_two, up_w)
        active = (hidden * jax.nn.sigmoid(hidden)).astype(BF16)
        kept.append(
            (
                stream, factor_one, normed_all, projected, log_total, attended_t, middle,
                factor_two, normed_two, hidden, active,
            )
        )
        stream = middle + dot(active, down_w)
    layer_out = swap_halves(stream.astype(BF16).reshape(tokens.shape))
    upper = upper.reshape(-1, width).astype(F32)

    scale_grads = [None] * layers
    for layer in reversed(range(layers)):
        (
            stream, factor_one, normed_all, projected, log_total, attended_t, middle,
            factor_two, normed_two, hidden, active,
        ) = kept[layer]
        qkv, dense = qkvs[layer], denses[layer]
        out_w, up_w, down_w = dense[:, :width], dense[:, width:-width], dense[:, -width:]
        down_bar = upper.astype(BF16)
        gate = jax.nn.sigmoid(hidden)
        up_bar = (
            dot_cols(down_bar, down_w) * gate * (1.0 + hidden * (1.0 - gate))
        ).astype(BF16)
        middle_grad = upper + lower_of(
            dot_cols(up_bar, up_w), middle, factor_two, gains[layers + layer]
        )
        out_bar = middle_grad.astype(BF16)
        if layer == 0:
            attended_grad = over_head(heads_grad(out_w, out_bar))
            grads, others = dense_grads(attended_t, normed_two, active, out_bar, up_bar, down_bar)
            others, across = tied(others, across)
            others, own = tied(others, own_quarter(cored) + across.astype(F32))
            attended_grad, others, z_sum, beside = tied(attended_grad, others, z_sum, beside)
            others = other_core(others)
            attended_grad, summed = tied(attended_grad, own_sum(own, beside))
            summed = over_batch(summed)
            earlier = across_sum(z_sum)
        else:
            attended_grad = over_head(heads_grad(out_w, out_bar))
            grads, others = dense_grads(attended_t, normed_two, active, out_bar, up_bar, down_bar)
            attended_grad, others, layer_out = tied(attended_grad, others, layer_out)
            others = other_core(others)
        bars, scale_grads[layer] = attend_back_rows(
            projected, attended_grad, log_total, scale_vecs[layer], segments, token_rows
        )
        if layer == 0:
            bars, earlier = tied(bars, earlier)
            qkv_grad = weight_back(bars, normed_all)
            bars, qkv_grad, others = tied(bars, qkv_grad, others)
            z_sum = over_batch(qkv_grad.reshape(4, 2, -1, qkv_grad.shape[-1]))
            cored = (grads, others)
            bars, rows = tied(bars, diagonal_rows(cored))
            diagonal = sent_beside_and_across(*rows)
            halves, to_core = rows_back(bars, qkv, token_rows)
            halves, to_core, diagonal, summed = tied(halves, to_core, diagonal, summed)
            halves, to_core, rows = tied(halves, to_core, neighbour_rows(cored, *diagonal))
            sent = sent_beside_and_across(*rows)
            halves = halves + other_core(to_core).astype(F32)
            scale_sum = sum_over(jnp.stack(scale_grads), ("head", 1), ("batch", 1), ("batch", 2))
            own = own_quarter(cored)
            halves, sent, z_sum, scale_sum, own = tied(halves, sent, z_sum, scale_sum, own)
            halves, own, earlier = tied(halves, own_sum(own, *sent), earlier)
            moved = over_head(earlier.reshape(4, -1, earlier.shape[-1]))
            dense_first = over_batch(own)
            normed_grad = scatter_row(halves)
            z_across, scale_sum, dense_first = tied(across_sum(z_sum), scale_sum, dense_first)
            z_across = over_head(z_across.reshape(4, -1, z_across.shape[-1]))
            dense_grad = [dense_first, summed]
            qkv_grads = [columns_to_rows(z_across), columns_to_rows(moved)]
        else:
            bars, others = tied(bars, others)
            cored = (grads, others)
            bars, rows = tied(bars, diagonal_rows(cored))
            diagonal = sent_beside_and_across(*rows)
            halves, to_core, qkv_grad = project_back(bars, qkv, normed_all, token_rows)
            z_sum = over_batch(qkv_grad.reshape(4, 2, -1, qkv_grad.shape[-1]))
            to_core, halves, diagonal = tied(to_core, halves, diagonal)
            to_core, rows = tied(to_core, neighbour_rows(cored, *diagonal))
            across = swapped(rows[0], "blk", 1)
            halves = halves + other_core(to_core).astype(F32)
            normed_grad = scatter_row(halves)
            normed_grad, beside = tied(normed_grad, rows[1])
            beside = swapped(beside, "head", 2)
        upper = middle_grad + lower_of(normed_grad, stream, factor_one, gains[layer])
    input_grad = swap_halves(upper.astype(BF16).reshape(tokens.shape)).astype(F32)
    scale_total = sum_over(scale_sum, ("head", 2), ("blk", 1))
    scale_grad = scale_total * (SCALE_BASE / math.sqrt(head_dim)) * jax.nn.sigmoid(scale_param)
    dense_all = jnp.stack([part.astype(F32) for part in dense_grad])
    qkv_all = jnp.stack(qkv_grads)
    up_all = dense_all[:, :, width:-width]
    return (
        layer_out,
        input_grad,
        qkv_all,
        dense_all[:, :, :width],
        up_all,
        dense_all[:, :, -width:],
        gain_back(qkv_weight, qkv_all, attn_gain),
        gain_back(up_weight, up_all, mlp_gain),
        scale_grad,
    )


def per_device(*args):
    tokens, segments = args[0], args[1]
    sizes = tuple(lax.axis_size(axis) for axis in ALL)
    heads = tokens.shape[2] // args[8].shape[1]
    spread = (
        sizes == (4, 2, 4)
        and tokens.shape[0] == 2
        and args[2].shape[0] == 2
        and tokens.shape[1] % 128 == 0
        and Q_ROWS % tokens.shape[1] == 0
        and segments.shape[1] <= WINDOW
        and segments.shape[1] % FORWARD_ROWS == 0
        and heads % 4 == 0
        and tokens.shape[2] % 256 == 0
    )
    return spread_device(*args) if spread else general_device(*args)


def solution(mesh):
    rows = P(None, ALL, None)
    by_token = P("batch", ("blk", "head"), None)
    return jax.shard_map(
        per_device,
        mesh=mesh,
        in_specs=(
            by_token, P("batch", None), rows, rows, rows, rows, P(None, ALL), P(None, ALL), P(),
            by_token,
        ),
        out_specs=(
            by_token, by_token, rows, rows, rows, rows, P(None, ALL), P(None, ALL), P(),
        ),
        check_vma=False,
    )
```

```python
import functools
import math

import jax
import jax.numpy as jnp
from jax import lax
from jax.experimental import pallas as pl
from jax.experimental.pallas import tpu as pltpu
from jax.sharding import PartitionSpec as P

WINDOW = 1024
EPSILON = 1e-06
SCALE_BASE = 1.4426950408889634
MASKED_SCORE = -1e30

ALL = ("batch", "blk", "head")
REST = ("batch", "blk")
F32 = jnp.float32
BF16 = jnp.bfloat16


def shifted(block, axis, distance):
    devices = range(lax.axis_size(axis))
    route = [(i - distance, i) for i in devices if i - distance in devices]
    return lax.ppermute(block, axis, route)


NT = (((1,), (1,)), ((), ()))
TN = (((0,), (0,)), ((), ()))


def dot(left, right):
    return jnp.dot(left, right, preferred_element_type=F32)


def dot_rows(left, right):
    return lax.dot_general(left, right, (((0,), (0,)), ((), ())), preferred_element_type=F32)


def dot_cols(left, right):
    return lax.dot_general(left, right, (((1,), (1,)), ((), ())), preferred_element_type=F32)


def normalize(stream, gain):
    factor = lax.rsqrt(jnp.mean(stream * stream, axis=-1, keepdims=True) + EPSILON)
    return stream * factor * gain, factor


def norm_back(upper, stream, factor, gain):
    inner = upper * gain
    gain_grad = jnp.sum(upper * stream * factor, axis=0)
    lower = factor * inner - stream * factor * factor * factor * jnp.mean(
        inner * stream, axis=-1, keepdims=True
    )
    return lower, gain_grad


class Plan:
    def __init__(self, tokens):
        self.seqs, self.rows, self.width = tokens.shape
        self.heads = lax.axis_size("head")
        self.blks = lax.axis_size("blk")
        self.block = self.rows * self.heads
        self.whole = self.seqs % self.blks == 0
        if self.whole:
            self.groups, self.own_seqs = self.blks, self.seqs // self.blks
            self.reach = 0
        else:
            self.groups, self.own_seqs = 1, self.seqs
            self.reach = min((WINDOW - 1) // self.block + 1, self.blks - 1)
        self.length = self.groups * self.block
        self.tokens = self.seqs * self.rows


def to_plan(plan, array):
    if plan.whole and plan.blks > 1:
        array = lax.all_to_all(array, "blk", split_axis=0, concat_axis=0, tiled=True)
    return array.reshape(plan.tokens, plan.width)


def from_plan(plan, flat):
    array = flat.reshape(plan.seqs, plan.rows, plan.width)
    if plan.whole and plan.blks > 1:
        array = lax.all_to_all(array, "blk", split_axis=0, concat_axis=0, tiled=True)
    return array


def in_sequence(plan, by_head, width):
    parts = by_head.reshape(plan.heads, plan.groups, plan.own_seqs, plan.rows, width)
    return parts.transpose(2, 1, 0, 3, 4).reshape(-1, width)


def by_owner(plan, rows, width):
    parts = rows.reshape(plan.own_seqs, plan.groups, plan.heads, plan.rows, width)
    return parts.transpose(2, 1, 0, 3, 4).reshape(plan.heads, plan.tokens, width)


def gather_tokens(plan, rows):
    moved = lax.all_gather(rows, "head", axis=0, tiled=False)
    return in_sequence(plan, moved, rows.shape[-1])


def scatter_tokens(plan, rows):
    width = rows.shape[-1]
    return lax.psum_scatter(
        by_owner(plan, rows.astype(BF16), width), "head", scatter_dimension=0, tiled=False
    ).astype(F32)


def heads_to_tokens(plan, rows):
    part = rows.shape[-1]
    moved = lax.all_to_all(
        by_owner(plan, rows, part), "head", split_axis=0, concat_axis=0, tiled=True
    )
    return moved.transpose(1, 0, 2).reshape(plan.tokens, plan.heads * part)


def tokens_to_heads(plan, rows):
    part = rows.shape[-1] // plan.heads
    sent = rows.reshape(plan.tokens, plan.heads, part).transpose(1, 0, 2)
    moved = lax.all_to_all(sent, "head", split_axis=0, concat_axis=0, tiled=True)
    return in_sequence(plan, moved, part)


def gather_qkv(rows):
    own, width = rows.shape
    heads = lax.axis_size("head")
    part = width // 3 // heads
    sent = rows.reshape(own, 3, heads, part).transpose(2, 0, 1, 3).reshape(heads, own, 3 * part)
    moved = lax.all_to_all(sent, "head", split_axis=0, concat_axis=0, tiled=True)
    full = lax.all_gather(moved, REST, axis=0, tiled=True)
    return full.reshape(-1, 3 * part)


def scatter_qkv(grad):
    heads = lax.axis_size("head")
    part = grad.shape[1] // 3
    summed = lax.psum_scatter(grad.astype(BF16), REST, scatter_dimension=0, tiled=True)
    own = summed.shape[0] // heads
    moved = lax.all_to_all(
        summed.reshape(heads, own, 3 * part), "head", split_axis=0, concat_axis=0, tiled=True
    )
    return (
        moved.reshape(heads, own, 3, part)
        .transpose(1, 2, 0, 3)
        .reshape(own, 3 * heads * part)
        .astype(F32)
    )


def window_mask(plan, segments, block_index):
    key_count = plan.length + plan.reach * plan.block
    if plan.whole:
        query_segs, key_segs = segments, segments
    else:
        leading = jnp.full((plan.own_seqs, plan.reach * plan.block), -1, jnp.int32)
        padded = jnp.concatenate([leading, segments], axis=1)
        start = block_index * plan.block
        query_segs = lax.dynamic_slice_in_dim(segments, start, plan.block, 1)
        key_segs = lax.dynamic_slice_in_dim(padded, start, key_count, 1)
    query_place = jnp.arange(plan.length, dtype=jnp.int32)[:, None] + plan.reach * plan.block
    key_place = jnp.arange(key_count, dtype=jnp.int32)[None, :]
    near = (key_place <= query_place) & (query_place - key_place < WINDOW)
    return (key_segs[:, None, :] == query_segs[:, :, None]) & near[None]


def with_earlier(plan, own):
    arrived = [own]
    for _ in range(plan.reach):
        arrived.append(shifted(arrived[-1], "blk", 1))
    return jnp.concatenate(arrived[::-1], axis=1) if plan.reach else own


def to_earlier(plan, grads):
    if not plan.reach:
        return grads
    block = plan.block
    total = grads[:, :block]
    for step in range(1, plan.reach + 1):
        total = (
            shifted(total.astype(BF16), "blk", -1).astype(F32)
            + grads[:, step * block : (step + 1) * block]
        )
    return total


def scores_of(queries, keys, allowed):
    scores = jnp.einsum("sqhd,skhd->shqk", queries, keys, preferred_element_type=F32)
    return jnp.where(allowed[:, None], scores, MASKED_SCORE)


def attend(queries, keys, values, allowed):
    scores = scores_of(queries, keys, allowed)
    top_score = jnp.max(scores, axis=-1, keepdims=True)
    exp_terms = jnp.exp(scores - top_score)
    totals = jnp.sum(exp_terms, axis=-1, keepdims=True)
    probs_low = (exp_terms / totals).astype(BF16)
    attended = jnp.einsum("shqk,skhd->sqhd", probs_low, values, preferred_element_type=F32)
    return attended, top_score + jnp.log(totals)


def attend_back(queries, keys, values, allowed, log_total, attended_grad):
    probs = jnp.exp(scores_of(queries, keys, allowed) - log_total)
    probs_low = probs.astype(BF16)
    values_grad = jnp.einsum(
        "shqk,sqhd->skhd", probs_low, attended_grad, preferred_element_type=F32
    )
    probs_grad = jnp.einsum("sqhd,skhd->shqk", attended_grad, values, preferred_element_type=F32)
    row_dot = jnp.sum(probs_grad * probs, axis=-1, keepdims=True)
    scores_low = (probs * (probs_grad - row_dot)).astype(BF16)
    queries_grad = jnp.einsum("shqk,skhd->sqhd", scores_low, keys, preferred_element_type=F32)
    keys_grad = jnp.einsum("shqk,sqhd->skhd", scores_low, queries, preferred_element_type=F32)
    return queries_grad, keys_grad, values_grad


def forward(plan, stream, qkv, dense, gains, scale_vec, allowed):
    width = plan.width
    head_dim = scale_vec.shape[0]
    part = qkv.shape[1] // 3
    local_heads = part // head_dim
    split = (plan.own_seqs, plan.length, local_heads, head_dim)
    out_w, up_w, down_w = dense[:, :width], dense[:, width:-width], dense[:, -width:]
    normed, factor_one = normalize(stream, gains[0])
    normed_all = gather_tokens(plan, normed.astype(BF16))
    projected = dot(normed_all, qkv)
    query_pre = projected[:, :part].reshape(split)
    queries = (query_pre * scale_vec).astype(BF16)
    keys = with_earlier(plan, projected[:, part : 2 * part].astype(BF16).reshape(split))
    values = with_earlier(plan, projected[:, 2 * part :].astype(BF16).reshape(split))
    attended_part, log_total = attend(queries, keys, values, allowed)
    attended = heads_to_tokens(plan, attended_part.astype(BF16).reshape(-1, part))
    middle = stream + dot(attended, out_w)
    normed_two, factor_two = normalize(middle, gains[1])
    normed_two = normed_two.astype(BF16)
    hidden = dot(normed_two, up_w)
    active = (hidden * jax.nn.sigmoid(hidden)).astype(BF16)
    result = middle + dot(active, down_w)
    kept = (
        stream, factor_one, normed_all, query_pre, queries, keys, values, log_total,
        attended, middle, factor_two, normed_two, hidden, active,
    )
    return result, kept


def backward(plan, upper, kept, qkv, dense, gains, scale_vec, allowed):
    (
        stream, factor_one, normed_all, query_pre, queries, keys, values, log_total,
        attended, middle, factor_two, normed_two, hidden, active,
    ) = kept
    width = plan.width
    head_dim = scale_vec.shape[0]
    part = qkv.shape[1] // 3
    out_w, up_w, down_w = dense[:, :width], dense[:, width:-width], dense[:, -width:]
    upper_low = upper.astype(BF16)
    down_grad = dot_rows(active, upper_low)
    active_grad = dot_cols(upper_low, down_w)
    gate = jax.nn.sigmoid(hidden)
    hidden_low = (active_grad * gate * (1.0 + hidden * (1.0 - gate))).astype(BF16)
    up_grad = dot_rows(normed_two, hidden_low)
    extra_two, mlp_gain_grad = norm_back(dot_cols(hidden_low, up_w), middle, factor_two, gains[1])
    middle_grad = upper + extra_two
    middle_low = middle_grad.astype(BF16)
    out_grad = dot_rows(attended, middle_low)
    dense_grad = jnp.concatenate([out_grad, up_grad, down_grad], axis=1).astype(BF16)
    dense_own = lax.psum_scatter(dense_grad, ALL, scatter_dimension=0, tiled=True)
    attended_grad = tokens_to_heads(plan, dot_cols(middle_low, out_w).astype(BF16))
    queries_grad, keys_grad, values_grad = attend_back(
        queries, keys, values, allowed, log_total, attended_grad.reshape(queries.shape)
    )
    query_bar = queries_grad.astype(BF16).astype(F32)
    scale_vec_grad = jnp.sum((query_bar * query_pre).reshape(-1, head_dim), axis=0)
    query_low = (query_bar * scale_vec).astype(BF16).reshape(-1, part)
    keys_low = to_earlier(plan, keys_grad).astype(BF16).reshape(-1, part)
    values_low = to_earlier(plan, values_grad).astype(BF16).reshape(-1, part)
    projected_low = jnp.concatenate([query_low, keys_low, values_low], axis=1)
    normed_grad = scatter_tokens(plan, dot_cols(projected_low, qkv))
    qkv_own = scatter_qkv(dot_rows(normed_all, projected_low))
    extra_one, attn_gain_grad = norm_back(normed_grad, stream, factor_one, gains[0])
    lower = middle_grad + extra_one
    return lower, qkv_own, dense_own, (attn_gain_grad, mlp_gain_grad), scale_vec_grad


def general_device(
    tokens,
    segments,
    qkv_weight,
    out_weight,
    up_weight,
    down_weight,
    attn_gain,
    mlp_gain,
    scale_param,
    cotangent,
):
    plan = Plan(tokens)
    layers, head_dim = scale_param.shape
    block_index = lax.axis_index("blk")
    scale_vecs = SCALE_BASE / math.sqrt(head_dim) * jax.nn.softplus(scale_param)
    own_gains = jnp.concatenate([attn_gain, mlp_gain], axis=0)
    gains = (
        lax.all_gather(own_gains.reshape(1, -1), ALL, axis=0, tiled=True)
        .reshape(-1, 2 * layers, attn_gain.shape[1])
        .transpose(1, 0, 2)
        .reshape(2 * layers, plan.width)
        .astype(F32)
    )
    if plan.whole:
        segments = lax.dynamic_slice_in_dim(
            segments, block_index * plan.own_seqs, plan.own_seqs, 0
        )
    allowed = window_mask(plan, segments, block_index)
    stream = to_plan(plan, tokens).astype(F32)
    qkvs, denses, kept = [], [], []
    for layer in range(layers):
        qkvs.append(gather_qkv(qkv_weight[layer]))
        own = jnp.concatenate([out_weight[layer], up_weight[layer], down_weight[layer]], axis=1)
        denses.append(lax.all_gather(own, ALL, axis=0, tiled=True))
        layer_gains = (gains[layer], gains[layers + layer])
        stream, saved = forward(
            plan, stream, qkvs[layer], denses[layer], layer_gains, scale_vecs[layer], allowed
        )
        kept.append(saved)
    layer_out = from_plan(plan, stream.astype(BF16))
    upper = to_plan(plan, cotangent).astype(F32)
    qkv_grads, dense_grads = [None] * layers, [None] * layers
    gain_grads, scale_grads = [None] * layers, [None] * layers
    for layer in reversed(range(layers)):
        layer_gains = (gains[layer], gains[layers + layer])
        upper, qkv_grads[layer], dense_grads[layer], gain_grads[layer], scale_grads[layer] = (
            backward(
                plan, upper, kept[layer], qkvs[layer], denses[layer], layer_gains,
                scale_vecs[layer], allowed,
            )
        )
    input_grad = from_plan(plan, upper.astype(BF16)).astype(F32)
    small = jnp.concatenate(
        [g[0] for g in gain_grads] + [g[1] for g in gain_grads] + scale_grads, axis=0
    )
    total = lax.psum(small, ALL)
    gain_total = total[: 2 * layers * plan.width].reshape(2 * layers, plan.width)
    owner = lax.axis_index(ALL)
    gain_rows = attn_gain.shape[1]
    own_total = lax.dynamic_slice_in_dim(gain_total, owner * gain_rows, gain_rows, 1)
    scale_total = total[2 * layers * plan.width :].reshape(layers, head_dim)
    scale_grad = scale_total * (SCALE_BASE / math.sqrt(head_dim)) * jax.nn.sigmoid(scale_param)
    dense_all = jnp.stack(dense_grads).astype(F32)
    width = plan.width
    return (
        layer_out,
        input_grad,
        jnp.stack(qkv_grads),
        dense_all[:, :, :width],
        dense_all[:, :, width:-width],
        dense_all[:, :, -width:],
        own_total[:layers],
        own_total[layers:],
        scale_grad,
    )


Q_ROWS = 256
KERNEL = pltpu.CompilerParams(vmem_limit_bytes=32 * 1024 * 1024)
LIGHT = pl.CostEstimate(flops=1 << 20, bytes_accessed=1 << 20, transcendentals=0)
HEAVY = pl.CostEstimate(flops=10**11, bytes_accessed=3 * 10**8, transcendentals=0)


def in_hbm(*arrays):
    return [pltpu.with_memory_space_constraint(array, pltpu.HBM) for array in arrays]


def allowed_keys(col, row, first):
    count = first + row.shape[1]
    key_place = lax.broadcasted_iota(jnp.int32, (count, row.shape[1]), 0)
    query_place = lax.broadcasted_iota(jnp.int32, (count, row.shape[1]), 1) + first
    return (col[:count] == row) & (key_place <= query_place)


def allowed_piece(col, row, start, first):
    same = col == row
    if start + col.shape[0] <= first:
        return same
    key_place = lax.broadcasted_iota(jnp.int32, same.shape, 0) + start
    return same & (key_place <= lax.broadcasted_iota(jnp.int32, same.shape, 1) + first)


def token_places(length, heads, token_rows, block_rows=Q_ROWS):
    for first in range(0, length, block_rows):
        parts = []
        for start in range(0, block_rows, token_rows):
            place = (first + start) // token_rows
            parts.append((start, place % heads, place // heads * token_rows))
        yield first, parts


FORWARD_ROWS, FORWARD_KEYS = 1024, 512


def attend_kernel(token_rows, proj_ref, scale_ref, col_ref, row_ref, out_ref, lse_ref):
    length = proj_ref.shape[-1]
    queries = (proj_ref[0, 0] * scale_ref[...]).astype(BF16)
    keys = proj_ref[1, 0].T.astype(BF16)
    values = proj_ref[2, 0].astype(BF16)
    for first, parts in token_places(length, out_ref.shape[0], token_rows, FORWARD_ROWS):
        end = first + FORWARD_ROWS
        block, row = queries[:, first:end], row_ref[:, first:end]
        pieces = []
        for start in range(0, end, FORWARD_KEYS):
            scores = jnp.dot(keys[start : start + FORWARD_KEYS], block, preferred_element_type=F32)
            allowed = allowed_piece(col_ref[start : start + FORWARD_KEYS], row, start, first)
            pieces.append(jnp.where(allowed, scores, MASKED_SCORE))
        top = functools.reduce(
            jnp.maximum, [jnp.max(piece, axis=0, keepdims=True) for piece in pieces]
        )
        total, attended = 0.0, 0.0
        for i, piece in enumerate(pieces):
            terms = jnp.exp(piece - top)
            total += jnp.sum(terms, axis=0, keepdims=True)
            attended += jnp.dot(
                values[:, i * FORWARD_KEYS : (i + 1) * FORWARD_KEYS],
                terms.astype(BF16),
                preferred_element_type=F32,
            )
        attended = (attended * (1.0 / total)).astype(BF16)
        lse_ref[0, :, first:end] = top + jnp.log(total)
        for start, owner, offset in parts:
            out_ref[owner, 0, :, offset : offset + token_rows] = attended[
                :, start : start + token_rows
            ]


def attend_rows(projected, scale_vec, segments, owners, token_rows):
    head_dim = scale_vec.shape[0]
    length = projected.shape[1]
    local_heads = projected.shape[0] // 3 // head_dim
    tokens = length // owners
    attended, log_total = pl.pallas_call(
        functools.partial(attend_kernel, token_rows),
        grid=(local_heads,),
        in_specs=[
            pl.BlockSpec((3, 1, head_dim, length), lambda h: (0, h, 0, 0)),
            pl.BlockSpec((head_dim, 1), lambda h: (0, 0)),
            pl.BlockSpec((length, 1), lambda h: (0, 0)),
            pl.BlockSpec((1, length), lambda h: (0, 0)),
        ],
        out_specs=[
            pl.BlockSpec((owners, 1, head_dim, tokens), lambda h: (0, h, 0, 0)),
            pl.BlockSpec((1, 1, length), lambda h: (h, 0, 0)),
        ],
        out_shape=[
            jax.ShapeDtypeStruct((owners, local_heads, head_dim, tokens), BF16),
            jax.ShapeDtypeStruct((local_heads, 1, length), F32),
        ],
        compiler_params=KERNEL,
        cost_estimate=LIGHT,
    )(
        projected.reshape(3, local_heads, head_dim, length),
        scale_vec.reshape(head_dim, 1),
        segments.reshape(length, 1),
        segments.reshape(1, length),
    )
    return attended.reshape(owners, local_heads * head_dim, tokens), log_total


def attend_back_kernel(
    token_rows,
    proj_ref,
    grad_ref,
    lse_ref,
    scale_ref,
    col_ref,
    row_ref,
    out_ref,
    scale_grad_ref,
    keys_acc,
    values_acc,
):
    length = proj_ref.shape[-1]
    scale = scale_ref[...]
    query_pre = proj_ref[0, 0]
    queries = (query_pre * scale).astype(BF16)
    keys_t = proj_ref[1, 0].astype(BF16)
    keys = proj_ref[1, 0].T.astype(BF16)
    values = proj_ref[2, 0].T.astype(BF16)
    keys_acc[...] = jnp.zeros_like(keys_acc)
    values_acc[...] = jnp.zeros_like(values_acc)
    scale_grad = jnp.zeros((scale.shape[0], 1), F32)
    for first, parts in token_places(length, grad_ref.shape[0], token_rows):
        end = first + Q_ROWS
        block = queries[:, first:end]
        grad = jnp.concatenate(
            [grad_ref[owner, 0, :, at : at + token_rows] for _, owner, at in parts], axis=1
        )
        scores = jnp.dot(keys[:end], block, preferred_element_type=F32)
        allowed = allowed_keys(col_ref[...], row_ref[:, first:end], first)
        scores = jnp.where(allowed, scores, MASKED_SCORE)
        probs = jnp.exp(scores - lse_ref[0, :, first:end])
        probs_grad = jnp.dot(values[:end], grad, preferred_element_type=F32)
        row_dot = jnp.sum(probs_grad * probs, axis=0, keepdims=True)
        scores_low = (probs * (probs_grad - row_dot)).astype(BF16)
        values_acc[:, :end] += lax.dot_general(
            grad, probs.astype(BF16), NT, preferred_element_type=F32
        )
        keys_acc[:, :end] += lax.dot_general(
            block, scores_low, NT, preferred_element_type=F32
        )
        query_bar = jnp.dot(keys_t[:, :end], scores_low, preferred_element_type=F32)
        query_bar = query_bar.astype(BF16).astype(F32)
        scale_grad += jnp.sum(query_bar * query_pre[:, first:end], axis=1, keepdims=True)
        out_ref[0, 0, :, first:end] = (query_bar * scale).astype(BF16)
    out_ref[1, 0] = keys_acc[...].astype(BF16)
    out_ref[2, 0] = values_acc[...].astype(BF16)
    spread = jnp.broadcast_to(scale_grad, scale_grad_ref.shape)

    @pl.when(pl.program_id(0) == 0)
    def _():
        scale_grad_ref[...] = spread

    @pl.when(pl.program_id(0) > 0)
    def _():
        scale_grad_ref[...] += spread


def attend_back_rows(projected, attended_grad, log_total, scale_vec, segments, token_rows):
    head_dim = scale_vec.shape[0]
    length = projected.shape[1]
    local_heads = projected.shape[0] // 3 // head_dim
    owners, _, tokens = attended_grad.shape
    lanes = 128
    grads, scale_grad = pl.pallas_call(
        functools.partial(attend_back_kernel, token_rows),
        grid=(local_heads,),
        in_specs=[
            pl.BlockSpec((3, 1, head_dim, length), lambda h: (0, h, 0, 0)),
            pl.BlockSpec((owners, 1, head_dim, tokens), lambda h: (0, h, 0, 0)),
            pl.BlockSpec((1, 1, length), lambda h: (h, 0, 0)),
            pl.BlockSpec((head_dim, 1), lambda h: (0, 0)),
            pl.BlockSpec((length, 1), lambda h: (0, 0)),
            pl.BlockSpec((1, length), lambda h: (0, 0)),
        ],
        out_specs=[
            pl.BlockSpec((3, 1, head_dim, length), lambda h: (0, h, 0, 0)),
            pl.BlockSpec((head_dim, lanes), lambda h: (0, 0)),
        ],
        out_shape=[
            pltpu.HBM((3, local_heads, head_dim, length), BF16),
            pltpu.HBM((head_dim, lanes), F32),
        ],
        scratch_shapes=[
            pltpu.VMEM((head_dim, length), F32),
            pltpu.VMEM((head_dim, length), F32),
        ],
        compiler_params=KERNEL,
        cost_estimate=LIGHT,
    )(
        *in_hbm(
            projected.reshape(3, local_heads, head_dim, length),
            attended_grad.reshape(owners, local_heads, head_dim, tokens),
        ),
        log_total,
        scale_vec.reshape(head_dim, 1),
        segments.reshape(length, 1),
        segments.reshape(1, length),
    )
    return grads.reshape(3 * local_heads * head_dim, length), scale_grad[:, 0]


def dense_grad_kernel(
    core_ref, attended_ref, normed_ref, active_ref, out_bar, up_bar, down_bar,
    own_ref, other_ref, normed_t, active_t,
):
    tile = pl.program_id(0)
    rows, width = 8 * own_ref.shape[3], out_bar.shape[1]

    @pl.when(tile == 0)
    def _():
        normed_t[...] = normed_ref[...].astype(F32).T.astype(BF16)
        active_t[...] = active_ref[...].astype(F32).T.astype(BF16)

    start = pl.multiple_of(tile * rows, rows)
    first_core = core_ref[2] == 0
    lefts = (attended_ref, normed_t, active_t)
    for i, (left, right) in enumerate(zip(lefts, (out_bar, up_bar, down_bar))):
        grad = jnp.dot(left[pl.ds(start, rows), :], right[...], preferred_element_type=F32)
        grad = grad.reshape(2, 2, 2, rows // 8, width)
        one, two = grad[:, :, 0], grad[:, :, 1]
        own_ref[:, :, 0, :, i * width : (i + 1) * width] = jnp.where(
            first_core, one, two
        ).astype(BF16)
        other_ref[:, :, 0, :, i * width : (i + 1) * width] = jnp.where(
            first_core, two, one
        ).astype(BF16)


def dense_grads(attended_t, normed, active, out_bar, up_bar, down_bar):
    width, tokens = attended_t.shape
    own = width // 32
    whole = pl.BlockSpec((tokens, width), lambda i, core: (0, 0))
    rows = pl.BlockSpec((2, 2, 1, own, 3 * width), lambda i, core: (0, 0, i, 0, 0))
    shape = pltpu.HBM((2, 2, 4, own, 3 * width), BF16)
    return pl.pallas_call(
        dense_grad_kernel,
        grid_spec=pltpu.PrefetchScalarGridSpec(
            num_scalar_prefetch=1,
            grid=(4,),
            in_specs=[pl.BlockSpec((width, tokens), lambda i, core: (0, 0))] + [whole] * 5,
            out_specs=[rows, rows],
            scratch_shapes=[pltpu.VMEM((width, tokens), BF16)] * 2,
        ),
        out_shape=[shape, shape],
        compiler_params=KERNEL,
        cost_estimate=LIGHT,
    )(place(), *in_hbm(attended_t, normed, active, out_bar, up_bar, down_bar))


def widen_kernel(in_ref, out_ref):
    out_ref[...] = in_ref[...].astype(F32)


def widened(rows):
    return pl.pallas_call(
        widen_kernel,
        out_shape=jax.ShapeDtypeStruct(rows.shape, F32),
        compiler_params=KERNEL,
        cost_estimate=HEAVY,
    )(rows)


def place():
    head = lax.axis_index("head")
    return jnp.stack([lax.axis_index("blk"), head // 2, head % 2]).astype(jnp.int32)


def assemble_kernel(place_ref, *refs):
    pieces, whole_ref = refs[:10], refs[10]
    half = whole_ref.shape[-1] // 2
    blk, row, core = place_ref[0], place_ref[1], place_ref[2]
    for i in range(2):
        at_core = core if i == 0 else 1 - core
        own, across, beside, one, two = pieces[5 * i : 5 * i + 5]
        whole_ref[0, blk, row, at_core] = own[0]
        whole_ref[0, 1 - blk, row, at_core] = across[0]
        whole_ref[0, blk, 1 - row, at_core] = beside[0]
        whole_ref[0, 1 - blk, 1 - row, at_core, :, :half] = one[0]
        whole_ref[0, 1 - blk, 1 - row, at_core, :, half:] = two[0]


def assemble(pieces):
    batch, own, columns = pieces[0].shape
    specs = [
        pl.BlockSpec((1, own, piece.shape[-1]), lambda i, at: (i, 0, 0))
        for piece in pieces
    ]
    whole = pl.pallas_call(
        assemble_kernel,
        grid_spec=pltpu.PrefetchScalarGridSpec(
            num_scalar_prefetch=1,
            grid=(batch,),
            in_specs=specs,
            out_specs=pl.BlockSpec((1, 2, 2, 2, own, columns), lambda i, at: (i, 0, 0, 0, 0, 0)),
        ),
        out_shape=jax.ShapeDtypeStruct((batch, 2, 2, 2, own, columns), BF16),
        compiler_params=KERNEL,
        cost_estimate=LIGHT,
    )(place(), *pieces)
    return whole.reshape(-1, columns)


def assemble_columns_kernel(place_ref, along_ref, across_ref, whole_ref, *extra_ref):
    blk = place_ref[0]
    columns = whole_ref.shape[-1]
    whole_ref[0, blk] = along_ref[0, :, :columns]
    whole_ref[0, 1 - blk] = across_ref[0, :, :columns]
    for extra in extra_ref:
        extra[0, blk] = along_ref[0, :, columns:]
        extra[0, 1 - blk] = across_ref[0, :, columns:]


def assemble_columns(along, across, columns):
    batch, own, both = along.shape
    rows = pl.BlockSpec((1, own, both), lambda i, at: (i, 0, 0))
    shapes = [(batch, 2, own, columns)]
    if both > columns:
        shapes.append((batch, 2, own, both - columns))
    parts = pl.pallas_call(
        assemble_columns_kernel,
        grid_spec=pltpu.PrefetchScalarGridSpec(
            num_scalar_prefetch=1,
            grid=(batch,),
            in_specs=[rows, rows],
            out_specs=[pl.BlockSpec((1,) + s[1:], lambda i, at: (i, 0, 0, 0)) for s in shapes],
        ),
        out_shape=[pltpu.HBM(s, BF16) for s in shapes],
        compiler_params=KERNEL,
        cost_estimate=LIGHT,
    )(place(), *in_hbm(along, across))
    return [part.reshape(-1, part.shape[-1]) for part in parts]


def assemble_wide_kernel(place_ref, along_ref, across_ref, whole_ref):
    blk = place_ref[0]
    own, columns = along_ref.shape[1], whole_ref.shape[-1]
    for i in range(along_ref.shape[-1] // columns):
        place, part = slice(i * own, (i + 1) * own), slice(i * columns, (i + 1) * columns)
        whole_ref[0, blk, place, :] = along_ref[0, :, part]
        whole_ref[0, 1 - blk, place, :] = across_ref[0, :, part]


def assemble_wide(along, across, columns):
    batch, own, wide = along.shape
    rows = own * (wide // columns)
    piece = pl.BlockSpec((1, own, wide), lambda i, at: (i, 0, 0))
    whole = pl.pallas_call(
        assemble_wide_kernel,
        grid_spec=pltpu.PrefetchScalarGridSpec(
            num_scalar_prefetch=1,
            grid=(batch,),
            in_specs=[piece, piece],
            out_specs=pl.BlockSpec((1, 2, rows, columns), lambda i, at: (i, 0, 0, 0)),
        ),
        out_shape=pltpu.HBM((batch, 2, rows, columns), BF16),
        compiler_params=KERNEL,
        cost_estimate=LIGHT,
    )(place(), *in_hbm(along, across))
    return whole.reshape(-1, columns)


def project_kernel(with_norm, place_ref, *refs):
    pieces, (gain_ref, weight_ref, normed_ref, projected_ref) = refs[:4], refs[4:]
    head = place_ref[1] * 2 + place_ref[2]
    rows = pieces[0].shape[0]
    for i, piece in enumerate(pieces):
        value = piece[...]
        if with_norm:
            stream = value.astype(F32)
            factor = lax.rsqrt(jnp.mean(stream * stream, axis=-1, keepdims=True) + EPSILON)
            value = (stream * factor * gain_ref[...]).astype(BF16)
        normed_ref[pl.ds(pl.multiple_of((head ^ i) * rows, rows), rows), :] = value
    projected = jnp.dot(normed_ref[...], weight_ref[...], preferred_element_type=F32)
    projected_ref[...] = projected.T


def project(pieces, gain, weight, with_norm, token_rows):
    tokens, width = pieces[0].shape
    length, columns = 4 * tokens, weight.shape[1]
    groups = tokens // token_rows
    piece = pl.BlockSpec((token_rows, width), lambda g, at: (g, 0))
    return pl.pallas_call(
        functools.partial(project_kernel, with_norm),
        grid_spec=pltpu.PrefetchScalarGridSpec(
            num_scalar_prefetch=1,
            grid=(groups,),
            in_specs=[piece] * 4
            + [
                pl.BlockSpec((1, width), lambda g, at: (0, 0)),
                pl.BlockSpec((width, columns), lambda g, at: (0, 0)),
            ],
            out_specs=[
                pl.BlockSpec((4 * token_rows, width), lambda g, at: (g, 0)),
                pl.BlockSpec((columns, 4 * token_rows), lambda g, at: (0, g)),
            ],
        ),
        out_shape=[
            pltpu.HBM((length, width), BF16),
            jax.ShapeDtypeStruct((columns, length), F32),
        ],
        compiler_params=KERNEL,
        cost_estimate=LIGHT,
    )(place(), *in_hbm(*pieces), gain.reshape(1, width), *in_hbm(weight))


def project_back_kernel(
    place_ref, bars_ref, weight_ref, normed_ref, own_ref, other_ref, grad_ref, bars_t
):
    @pl.when(pl.program_id(0) == 0)
    def _():
        bars_t[...] = bars_ref[...].astype(F32).T.astype(BF16)

    upper = lax.dot_general(bars_t[...], weight_ref[...], NT, preferred_element_type=F32)
    upper = upper.reshape(2, 2, 2, -1, upper.shape[-1])
    first_core = place_ref[2] == 0
    one, two = upper[:, :, 0], upper[:, :, 1]
    own_ref[...] = jnp.where(first_core, one, two)
    other_ref[...] = jnp.where(first_core, two, one).astype(BF16)
    grad = lax.dot_general(normed_ref[...], bars_t[...], TN, preferred_element_type=F32)
    grad_ref[...] = grad.astype(BF16)


def project_back(bars, weight, normed, token_rows):
    columns, length = bars.shape
    width = weight.shape[0]
    tile = width // 2
    quarter = pl.BlockSpec((2, 2, token_rows, tile), lambda i, at: (0, 0, 0, i))
    return pl.pallas_call(
        project_back_kernel,
        grid_spec=pltpu.PrefetchScalarGridSpec(
            num_scalar_prefetch=1,
            grid=(2,),
            in_specs=[
                pl.BlockSpec((columns, length), lambda i, at: (0, 0)),
                pl.BlockSpec((tile, columns), lambda i, at: (i, 0)),
                pl.BlockSpec((length, tile), lambda i, at: (0, i)),
            ],
            out_specs=[quarter, quarter, pl.BlockSpec((tile, columns), lambda i, at: (i, 0))],
            scratch_shapes=[pltpu.VMEM((length, columns), BF16)],
        ),
        out_shape=[
            pltpu.HBM((2, 2, token_rows, width), F32),
            pltpu.HBM((2, 2, token_rows, width), BF16),
            pltpu.HBM((width, columns), BF16),
        ],
        compiler_params=KERNEL,
        cost_estimate=LIGHT,
    )(place(), *in_hbm(bars, weight, normed))


def rows_back_kernel(place_ref, bars_ref, weight_ref, own_ref, other_ref, bars_t):
    @pl.when(pl.program_id(0) == 0)
    def _():
        bars_t[...] = bars_ref[...].astype(F32).T.astype(BF16)

    upper = lax.dot_general(bars_t[...], weight_ref[...], NT, preferred_element_type=F32)
    upper = upper.reshape(2, 2, 2, -1, upper.shape[-1])
    first_core = place_ref[2] == 0
    one, two = upper[:, :, 0], upper[:, :, 1]
    own_ref[...] = jnp.where(first_core, one, two)
    other_ref[...] = jnp.where(first_core, two, one).astype(BF16)


def rows_back(bars, weight, token_rows):
    columns, length = bars.shape
    width = weight.shape[0]
    tile = width // 2
    quarter = pl.BlockSpec((2, 2, token_rows, tile), lambda i, at: (0, 0, 0, i))
    return pl.pallas_call(
        rows_back_kernel,
        grid_spec=pltpu.PrefetchScalarGridSpec(
            num_scalar_prefetch=1,
            grid=(2,),
            in_specs=[
                pl.BlockSpec((columns, length), lambda i, at: (0, 0)),
                pl.BlockSpec((tile, columns), lambda i, at: (i, 0)),
            ],
            out_specs=[quarter, quarter],
            scratch_shapes=[pltpu.VMEM((length, columns), BF16)],
        ),
        out_shape=[
            pltpu.HBM((2, 2, token_rows, width), F32),
            pltpu.HBM((2, 2, token_rows, width), BF16),
        ],
        compiler_params=KERNEL,
        cost_estimate=LIGHT,
    )(place(), *in_hbm(bars, weight))


def weight_back_kernel(bars_ref, normed_ref, grad_ref):
    grad = jnp.dot(bars_ref[...], normed_ref[...], preferred_element_type=F32)
    grad_ref[...] = grad.T.astype(BF16)


def weight_back(bars, normed):
    columns, length = bars.shape
    width = normed.shape[1]
    tile = width // 5
    return pl.pallas_call(
        weight_back_kernel,
        grid=(5,),
        in_specs=[
            pl.BlockSpec((columns, length), lambda i: (0, 0)),
            pl.BlockSpec((length, tile), lambda i: (0, i)),
        ],
        out_specs=pl.BlockSpec((tile, columns), lambda i: (i, 0)),
        out_shape=pltpu.HBM((width, columns), BF16),
        compiler_params=KERNEL,
        cost_estimate=LIGHT,
    )(*in_hbm(bars, normed))


def tied(*arrays):
    return lax.optimization_barrier(arrays)


def swapped(array, axis, mask):
    size = lax.axis_size(axis)
    return lax.ppermute(array, axis, [(i, i ^ mask) for i in range(size)])


def pick(array, index, axis=0):
    return lax.dynamic_index_in_dim(array, index, axis, keepdims=False)


def swap_halves(array):
    me = lax.axis_index("blk")
    got = swapped(pick(array, 1 - me), "blk", 1)
    kept = pick(array, me)
    return jnp.stack([jnp.where(me == 0, kept, got), jnp.where(me == 0, got, kept)])


def scatter_row(halves):
    row = lax.axis_index("head") // 2
    got = swapped(pick(halves, 1 - row, 1).astype(BF16), "head", 2).astype(F32)
    return (pick(halves, row, 1) + got).reshape(-1, halves.shape[-1])


def over_head(parts):
    return lax.all_to_all(parts, "head", split_axis=0, concat_axis=0, tiled=True)


def qkv_columns(rows, extra):
    own, width = rows.shape
    part = width // 3 // 4
    sent = rows.reshape(own, 3, 4, part).transpose(2, 0, 1, 3).reshape(4, own, 3 * part)
    if extra is not None:
        sent = jnp.concatenate([sent, jnp.broadcast_to(extra[None], (4,) + extra.shape)], axis=2)
    return over_head(sent)


def along_batch(piece):
    return lax.all_gather(piece, "batch", axis=0, tiled=False)


def other_core(array):
    return swapped(array, "head", 1)


def to_beside(across):
    return swapped(across[..., : across.shape[-1] // 2], "head", 2)


def to_across(beside):
    return swapped(beside[..., beside.shape[-1] // 2 :], "blk", 1)


def over_batch(parts):
    return lax.psum_scatter(parts.astype(BF16), "batch", scatter_dimension=0, tiled=False)


def across_sum(halves):
    blk = lax.axis_index("blk")
    got = swapped(pick(halves, 1 - blk), "blk", 1).astype(F32)
    return (pick(halves, blk).astype(F32) + got).astype(BF16)


def columns_to_rows(moved):
    rows = moved.shape[1]
    return moved.reshape(4, rows, 3, -1).transpose(1, 2, 0, 3).reshape(rows, -1).astype(F32)


def quarter(parts, blk, row):
    one, two = (pick(pick(part, blk), row).astype(F32) for part in parts)
    return one + two


def diagonal_rows(parts):
    blk, row = place()[:2]
    rows = quarter(parts, 1 - blk, 1 - row).astype(BF16)
    half = rows.shape[-1] // 2
    return rows[..., :half], rows[..., half:]


def neighbour_rows(parts, one, two):
    blk, row = place()[:2]
    half = one.shape[-1]
    across, beside = quarter(parts, 1 - blk, row), quarter(parts, blk, 1 - row)
    across = jnp.concatenate([across[..., :half], across[..., half:] + two.astype(F32)], axis=-1)
    beside = jnp.concatenate([beside[..., :half] + one.astype(F32), beside[..., half:]], axis=-1)
    return across.astype(BF16), beside.astype(BF16)


def sent_beside_and_across(across, beside):
    return swapped(across, "blk", 1), swapped(beside, "head", 2)


def heads_grad(weight, out_bar):
    return dot_cols(weight, out_bar).astype(BF16).reshape(4, -1, out_bar.shape[0])


def own_quarter(parts):
    blk, row = place()[:2]
    return quarter(parts, blk, row)


def own_sum(own, *more):
    return sum((part.astype(F32) for part in more), own).astype(BF16)


def sum_over(array, *hops):
    for axis, mask in hops:
        array = array + swapped(array, axis, mask)
    return array


def gain_back(weight, weight_grad, gain):
    return jnp.sum(weight.astype(F32) * weight_grad, axis=-1) / gain.astype(F32)


def lower_of(upper, stream, factor, gain):
    return norm_back(upper, stream, factor, gain)[0]


def spread_device(
    tokens,
    segments,
    qkv_weight,
    out_weight,
    up_weight,
    down_weight,
    attn_gain,
    mlp_gain,
    scale_param,
    cotangent,
):
    layers, head_dim = scale_param.shape
    _, token_rows, width = tokens.shape
    scale_vecs = SCALE_BASE / math.sqrt(head_dim) * jax.nn.softplus(scale_param)
    segments = pick(segments, lax.axis_index("blk"))
    own_gains = jnp.concatenate([attn_gain, mlp_gain], axis=0)

    part3 = 3 * width // 4
    dense_own = [
        jnp.concatenate([out_weight[i], up_weight[i], down_weight[i]], axis=1) for i in (0, 1)
    ]

    first = swap_halves(tokens).reshape(-1, width)
    columns = qkv_columns(qkv_weight[0], own_gains.T)
    columns, first, cotangent = tied(columns.reshape(-1, columns.shape[-1]), first, cotangent)
    stream = first.astype(F32)
    along = along_batch(columns)
    far, near = swapped(first, "head", 2), other_core(first)
    both = other_core(far)
    upper = swap_halves(cotangent)
    along, near, far, both, dense_near, upper = tied(
        along, near, far, both, dense_own[0], upper
    )
    token_pieces = (first, near, far, both)
    dense_near = along_batch(dense_near)
    qkv_across = swapped(along, "blk", 1)
    next_columns = jnp.concatenate(list(qkv_columns(qkv_weight[1], None)), axis=1)
    qkv_across, dense_near, next_columns = tied(qkv_across, dense_near, next_columns)
    across, beside = swapped(dense_near, "blk", 1), swapped(dense_near, "head", 2)
    next_both = along_batch(jnp.stack([next_columns, dense_own[1]]))
    weight, gains = assemble_columns(along, qkv_across, part3)
    qkvs = [weight]
    gains = gains.T.astype(F32)

    kept, denses = [], []
    for layer in range(layers):
        normed, factor_one = normalize(stream, gains[layer])
        if layer == 1:
            normed = normed.astype(BF16)
            far, near = swapped(normed, "head", 2), other_core(normed)
            far, next_across, dense_next = tied(far, next_across, dense_next)
            across, beside = swapped(dense_next, "blk", 1), swapped(dense_next, "head", 2)
            token_pieces = (normed, near, far, other_core(far))
            qkvs.append(assemble_wide(next_along, next_across, part3))
        normed_all, projected = project(
            token_pieces, gains[layer], qkvs[layer], layer == 0, token_rows
        )
        attended, log_total = attend_rows(
            projected, scale_vecs[layer], segments, 4, token_rows
        )
        attended, across, beside = tied(attended, across, beside)
        one, two = to_beside(across), to_across(beside)
        if layer == 0:
            two, next_both = tied(two, next_both)
            next_along, dense_next = next_both[:, 0], next_both[:, 1]
            next_across = swapped(next_along, "blk", 1)
            attended_t, one, two = tied(over_head(attended), one, two)
        else:
            dense_near = dense_next
            attended_t, one, two = tied(over_head(attended), one, two)
        pieces = (dense_near, across, beside, one, two)
        pieces += tuple(other_core(piece) for piece in pieces)
        attended_t = attended_t.reshape(width, -1)
        denses.append(assemble(pieces))
        dense = denses[layer]
        out_w, up_w, down_w = dense[:, :width], dense[:, width:-width], dense[:, -width:]
        middle = stream + dot_rows(attended_t, out_w)
        normed_two, factor_two = normalize(middle, gains[layers + layer])
        normed_two = normed_two.astype(BF16)
        hidden = dot(normed_two, up_w)
        active = (hidden * jax.nn.sigmoid(hidden)).astype(BF16)
        kept.append(
            (
                stream, factor_one, normed_all, projected, log_total, attended_t, middle,
                factor_two, normed_two, hidden, active,
            )
        )
        stream = middle + dot(active, down_w)
    layer_out = swap_halves(stream.astype(BF16).reshape(tokens.shape))
    upper = upper.reshape(-1, width).astype(F32)

    scale_grads = [None] * layers
    for layer in reversed(range(layers)):
        (
            stream, factor_one, normed_all, projected, log_total, attended_t, middle,
            factor_two, normed_two, hidden, active,
        ) = kept[layer]
        qkv, dense = qkvs[layer], denses[layer]
        out_w, up_w, down_w = dense[:, :width], dense[:, width:-width], dense[:, -width:]
        down_bar = upper.astype(BF16)
        gate = jax.nn.sigmoid(hidden)
        up_bar = (
            dot_cols(down_bar, down_w) * gate * (1.0 + hidden * (1.0 - gate))
        ).astype(BF16)
        middle_grad = upper + lower_of(
            dot_cols(up_bar, up_w), middle, factor_two, gains[layers + layer]
        )
        out_bar = middle_grad.astype(BF16)
        if layer == 0:
            attended_grad = over_head(heads_grad(out_w, out_bar))
            grads, others = dense_grads(attended_t, normed_two, active, out_bar, up_bar, down_bar)
            others, across = tied(others, across)
            others, own = tied(others, own_quarter(cored) + across.astype(F32))
            attended_grad, others, z_sum, beside = tied(attended_grad, others, z_sum, beside)
            others = other_core(others)
            attended_grad, summed = tied(attended_grad, own_sum(own, beside))
            summed = over_batch(summed)
            earlier = across_sum(z_sum)
        else:
            attended_grad = over_head(heads_grad(out_w, out_bar))
            grads, others = dense_grads(attended_t, normed_two, active, out_bar, up_bar, down_bar)
            attended_grad, others, layer_out = tied(attended_grad, others, layer_out)
            others = other_core(others)
        bars, scale_grads[layer] = attend_back_rows(
            projected, attended_grad, log_total, scale_vecs[layer], segments, token_rows
        )
        if layer == 0:
            bars, earlier = tied(bars, earlier)
            qkv_grad = weight_back(bars, normed_all)
            bars, qkv_grad, others = tied(bars, qkv_grad, others)
            z_sum = over_batch(qkv_grad.reshape(4, 2, -1, qkv_grad.shape[-1]))
            cored = (grads, others)
            bars, rows = tied(bars, diagonal_rows(cored))
            diagonal = sent_beside_and_across(*rows)
            halves, to_core = rows_back(bars, qkv, token_rows)
            scale_sum = sum_over(jnp.stack(scale_grads), ("head", 1))
            halves, to_core, diagonal, summed, scale_sum = tied(
                halves, to_core, diagonal, summed, scale_sum
            )
            halves, to_core, rows, scale_sum = tied(
                halves, to_core, neighbour_rows(cored, *diagonal), scale_sum
            )
            sent = sent_beside_and_across(*rows)
            halves = halves + other_core(to_core).astype(F32)
            scale_sum = sum_over(scale_sum, ("batch", 1), ("batch", 2))
            own = own_quarter(cored)
            halves, sent, z_sum, scale_sum, own = tied(halves, sent, z_sum, scale_sum, own)
            halves, own, earlier = tied(halves, own_sum(own, *sent), earlier)
            moved = over_head(earlier.reshape(4, -1, earlier.shape[-1]))
            dense_first = widened(over_batch(own))
            normed_grad = scatter_row(halves)
            z_across = across_sum(z_sum)
            z_across = over_head(z_across.reshape(4, -1, z_across.shape[-1]))
            dense_grad = [dense_first, summed]
            qkv_grads = [columns_to_rows(z_across), columns_to_rows(moved)]
        else:
            bars, others = tied(bars, others)
            cored = (grads, others)
            bars, rows = tied(bars, diagonal_rows(cored))
            diagonal = sent_beside_and_across(*rows)
            halves, to_core, qkv_grad = project_back(bars, qkv, normed_all, token_rows)
            z_sum = over_batch(qkv_grad.reshape(4, 2, -1, qkv_grad.shape[-1]))
            to_core, halves, diagonal = tied(to_core, halves, diagonal)
            to_core, rows = tied(to_core, neighbour_rows(cored, *diagonal))
            across = swapped(rows[0], "blk", 1)
            halves = halves + other_core(to_core).astype(F32)
            normed_grad = scatter_row(halves)
            normed_grad, beside = tied(normed_grad, rows[1])
            beside = swapped(beside, "head", 2)
        upper = middle_grad + lower_of(normed_grad, stream, factor_one, gains[layer])
    input_grad = swap_halves(upper.astype(BF16).reshape(tokens.shape)).astype(F32)
    scale_total = sum_over(scale_sum, ("head", 2), ("blk", 1))
    scale_grad = scale_total * (SCALE_BASE / math.sqrt(head_dim)) * jax.nn.sigmoid(scale_param)
    dense_all = jnp.stack([part.astype(F32) for part in dense_grad])
    qkv_all = jnp.stack(qkv_grads)
    up_all = dense_all[:, :, width:-width]
    return (
        layer_out,
        input_grad,
        qkv_all,
        dense_all[:, :, :width],
        up_all,
        dense_all[:, :, -width:],
        gain_back(qkv_weight, qkv_all, attn_gain),
        gain_back(up_weight, up_all, mlp_gain),
        scale_grad,
    )


def per_device(*args):
    tokens, segments = args[0], args[1]
    sizes = tuple(lax.axis_size(axis) for axis in ALL)
    heads = tokens.shape[2] // args[8].shape[1]
    spread = (
        sizes == (4, 2, 4)
        and tokens.shape[0] == 2
        and args[2].shape[0] == 2
        and tokens.shape[1] % 128 == 0
        and Q_ROWS % tokens.shape[1] == 0
        and segments.shape[1] <= WINDOW
        and segments.shape[1] % FORWARD_ROWS == 0
        and heads % 4 == 0
        and tokens.shape[2] % 256 == 0
    )
    return spread_device(*args) if spread else general_device(*args)


def solution(mesh):
    rows = P(None, ALL, None)
    by_token = P("batch", ("blk", "head"), None)
    return jax.shard_map(
        per_device,
        mesh=mesh,
        in_specs=(
            by_token, P("batch", None), rows, rows, rows, rows, P(None, ALL), P(None, ALL), P(),
            by_token,
        ),
        out_specs=(
            by_token, by_token, rows, rows, rows, rows, P(None, ALL), P(None, ALL), P(),
        ),
        check_vma=False,
    )
```

```python
import functools
import math

import jax
import jax.numpy as jnp
from jax import lax
from jax.experimental import pallas as pl
from jax.experimental.pallas import tpu as pltpu
from jax.sharding import PartitionSpec as P

WINDOW = 1024
EPSILON = 1e-06
SCALE_BASE = 1.4426950408889634
MASKED_SCORE = -1e30

ALL = ("batch", "blk", "head")
REST = ("batch", "blk")
F32 = jnp.float32
BF16 = jnp.bfloat16


def shifted(block, axis, distance):
    devices = range(lax.axis_size(axis))
    route = [(i - distance, i) for i in devices if i - distance in devices]
    return lax.ppermute(block, axis, route)


NT = (((1,), (1,)), ((), ()))
TN = (((0,), (0,)), ((), ()))


def dot(left, right):
    return jnp.dot(left, right, preferred_element_type=F32)


def dot_rows(left, right):
    return lax.dot_general(left, right, (((0,), (0,)), ((), ())), preferred_element_type=F32)


def dot_cols(left, right):
    return lax.dot_general(left, right, (((1,), (1,)), ((), ())), preferred_element_type=F32)


def normalize(stream, gain):
    factor = lax.rsqrt(jnp.mean(stream * stream, axis=-1, keepdims=True) + EPSILON)
    return stream * factor * gain, factor


def norm_back(upper, stream, factor, gain):
    inner = upper * gain
    gain_grad = jnp.sum(upper * stream * factor, axis=0)
    lower = factor * inner - stream * factor * factor * factor * jnp.mean(
        inner * stream, axis=-1, keepdims=True
    )
    return lower, gain_grad


class Plan:
    def __init__(self, tokens):
        self.seqs, self.rows, self.width = tokens.shape
        self.heads = lax.axis_size("head")
        self.blks = lax.axis_size("blk")
        self.block = self.rows * self.heads
        self.whole = self.seqs % self.blks == 0
        if self.whole:
            self.groups, self.own_seqs = self.blks, self.seqs // self.blks
            self.reach = 0
        else:
            self.groups, self.own_seqs = 1, self.seqs
            self.reach = min((WINDOW - 1) // self.block + 1, self.blks - 1)
        self.length = self.groups * self.block
        self.tokens = self.seqs * self.rows


def to_plan(plan, array):
    if plan.whole and plan.blks > 1:
        array = lax.all_to_all(array, "blk", split_axis=0, concat_axis=0, tiled=True)
    return array.reshape(plan.tokens, plan.width)


def from_plan(plan, flat):
    array = flat.reshape(plan.seqs, plan.rows, plan.width)
    if plan.whole and plan.blks > 1:
        array = lax.all_to_all(array, "blk", split_axis=0, concat_axis=0, tiled=True)
    return array


def in_sequence(plan, by_head, width):
    parts = by_head.reshape(plan.heads, plan.groups, plan.own_seqs, plan.rows, width)
    return parts.transpose(2, 1, 0, 3, 4).reshape(-1, width)


def by_owner(plan, rows, width):
    parts = rows.reshape(plan.own_seqs, plan.groups, plan.heads, plan.rows, width)
    return parts.transpose(2, 1, 0, 3, 4).reshape(plan.heads, plan.tokens, width)


def gather_tokens(plan, rows):
    moved = lax.all_gather(rows, "head", axis=0, tiled=False)
    return in_sequence(plan, moved, rows.shape[-1])


def scatter_tokens(plan, rows):
    width = rows.shape[-1]
    return lax.psum_scatter(
        by_owner(plan, rows.astype(BF16), width), "head", scatter_dimension=0, tiled=False
    ).astype(F32)


def heads_to_tokens(plan, rows):
    part = rows.shape[-1]
    moved = lax.all_to_all(
        by_owner(plan, rows, part), "head", split_axis=0, concat_axis=0, tiled=True
    )
    return moved.transpose(1, 0, 2).reshape(plan.tokens, plan.heads * part)


def tokens_to_heads(plan, rows):
    part = rows.shape[-1] // plan.heads
    sent = rows.reshape(plan.tokens, plan.heads, part).transpose(1, 0, 2)
    moved = lax.all_to_all(sent, "head", split_axis=0, concat_axis=0, tiled=True)
    return in_sequence(plan, moved, part)


def gather_qkv(rows):
    own, width = rows.shape
    heads = lax.axis_size("head")
    part = width // 3 // heads
    sent = rows.reshape(own, 3, heads, part).transpose(2, 0, 1, 3).reshape(heads, own, 3 * part)
    moved = lax.all_to_all(sent, "head", split_axis=0, concat_axis=0, tiled=True)
    full = lax.all_gather(moved, REST, axis=0, tiled=True)
    return full.reshape(-1, 3 * part)


def scatter_qkv(grad):
    heads = lax.axis_size("head")
    part = grad.shape[1] // 3
    summed = lax.psum_scatter(grad.astype(BF16), REST, scatter_dimension=0, tiled=True)
    own = summed.shape[0] // heads
    moved = lax.all_to_all(
        summed.reshape(heads, own, 3 * part), "head", split_axis=0, concat_axis=0, tiled=True
    )
    return (
        moved.reshape(heads, own, 3, part)
        .transpose(1, 2, 0, 3)
        .reshape(own, 3 * heads * part)
        .astype(F32)
    )


def window_mask(plan, segments, block_index):
    key_count = plan.length + plan.reach * plan.block
    if plan.whole:
        query_segs, key_segs = segments, segments
    else:
        leading = jnp.full((plan.own_seqs, plan.reach * plan.block), -1, jnp.int32)
        padded = jnp.concatenate([leading, segments], axis=1)
        start = block_index * plan.block
        query_segs = lax.dynamic_slice_in_dim(segments, start, plan.block, 1)
        key_segs = lax.dynamic_slice_in_dim(padded, start, key_count, 1)
    query_place = jnp.arange(plan.length, dtype=jnp.int32)[:, None] + plan.reach * plan.block
    key_place = jnp.arange(key_count, dtype=jnp.int32)[None, :]
    near = (key_place <= query_place) & (query_place - key_place < WINDOW)
    return (key_segs[:, None, :] == query_segs[:, :, None]) & near[None]


def with_earlier(plan, own):
    arrived = [own]
    for _ in range(plan.reach):
        arrived.append(shifted(arrived[-1], "blk", 1))
    return jnp.concatenate(arrived[::-1], axis=1) if plan.reach else own


def to_earlier(plan, grads):
    if not plan.reach:
        return grads
    block = plan.block
    total = grads[:, :block]
    for step in range(1, plan.reach + 1):
        total = (
            shifted(total.astype(BF16), "blk", -1).astype(F32)
            + grads[:, step * block : (step + 1) * block]
        )
    return total


def scores_of(queries, keys, allowed):
    scores = jnp.einsum("sqhd,skhd->shqk", queries, keys, preferred_element_type=F32)
    return jnp.where(allowed[:, None], scores, MASKED_SCORE)


def attend(queries, keys, values, allowed):
    scores = scores_of(queries, keys, allowed)
    top_score = jnp.max(scores, axis=-1, keepdims=True)
    exp_terms = jnp.exp(scores - top_score)
    totals = jnp.sum(exp_terms, axis=-1, keepdims=True)
    probs_low = (exp_terms / totals).astype(BF16)
    attended = jnp.einsum("shqk,skhd->sqhd", probs_low, values, preferred_element_type=F32)
    return attended, top_score + jnp.log(totals)


def attend_back(queries, keys, values, allowed, log_total, attended_grad):
    probs = jnp.exp(scores_of(queries, keys, allowed) - log_total)
    probs_low = probs.astype(BF16)
    values_grad = jnp.einsum(
        "shqk,sqhd->skhd", probs_low, attended_grad, preferred_element_type=F32
    )
    probs_grad = jnp.einsum("sqhd,skhd->shqk", attended_grad, values, preferred_element_type=F32)
    row_dot = jnp.sum(probs_grad * probs, axis=-1, keepdims=True)
    scores_low = (probs * (probs_grad - row_dot)).astype(BF16)
    queries_grad = jnp.einsum("shqk,skhd->sqhd", scores_low, keys, preferred_element_type=F32)
    keys_grad = jnp.einsum("shqk,sqhd->skhd", scores_low, queries, preferred_element_type=F32)
    return queries_grad, keys_grad, values_grad


def forward(plan, stream, qkv, dense, gains, scale_vec, allowed):
    width = plan.width
    head_dim = scale_vec.shape[0]
    part = qkv.shape[1] // 3
    local_heads = part // head_dim
    split = (plan.own_seqs, plan.length, local_heads, head_dim)
    out_w, up_w, down_w = dense[:, :width], dense[:, width:-width], dense[:, -width:]
    normed, factor_one = normalize(stream, gains[0])
    normed_all = gather_tokens(plan, normed.astype(BF16))
    projected = dot(normed_all, qkv)
    query_pre = projected[:, :part].reshape(split)
    queries = (query_pre * scale_vec).astype(BF16)
    keys = with_earlier(plan, projected[:, part : 2 * part].astype(BF16).reshape(split))
    values = with_earlier(plan, projected[:, 2 * part :].astype(BF16).reshape(split))
    attended_part, log_total = attend(queries, keys, values, allowed)
    attended = heads_to_tokens(plan, attended_part.astype(BF16).reshape(-1, part))
    middle = stream + dot(attended, out_w)
    normed_two, factor_two = normalize(middle, gains[1])
    normed_two = normed_two.astype(BF16)
    hidden = dot(normed_two, up_w)
    active = (hidden * jax.nn.sigmoid(hidden)).astype(BF16)
    result = middle + dot(active, down_w)
    kept = (
        stream, factor_one, normed_all, query_pre, queries, keys, values, log_total,
        attended, middle, factor_two, normed_two, hidden, active,
    )
    return result, kept


def backward(plan, upper, kept, qkv, dense, gains, scale_vec, allowed):
    (
        stream, factor_one, normed_all, query_pre, queries, keys, values, log_total,
        attended, middle, factor_two, normed_two, hidden, active,
    ) = kept
    width = plan.width
    head_dim = scale_vec.shape[0]
    part = qkv.shape[1] // 3
    out_w, up_w, down_w = dense[:, :width], dense[:, width:-width], dense[:, -width:]
    upper_low = upper.astype(BF16)
    down_grad = dot_rows(active, upper_low)
    active_grad = dot_cols(upper_low, down_w)
    gate = jax.nn.sigmoid(hidden)
    hidden_low = (active_grad * gate * (1.0 + hidden * (1.0 - gate))).astype(BF16)
    up_grad = dot_rows(normed_two, hidden_low)
    extra_two, mlp_gain_grad = norm_back(dot_cols(hidden_low, up_w), middle, factor_two, gains[1])
    middle_grad = upper + extra_two
    middle_low = middle_grad.astype(BF16)
    out_grad = dot_rows(attended, middle_low)
    dense_grad = jnp.concatenate([out_grad, up_grad, down_grad], axis=1).astype(BF16)
    dense_own = lax.psum_scatter(dense_grad, ALL, scatter_dimension=0, tiled=True)
    attended_grad = tokens_to_heads(plan, dot_cols(middle_low, out_w).astype(BF16))
    queries_grad, keys_grad, values_grad = attend_back(
        queries, keys, values, allowed, log_total, attended_grad.reshape(queries.shape)
    )
    query_bar = queries_grad.astype(BF16).astype(F32)
    scale_vec_grad = jnp.sum((query_bar * query_pre).reshape(-1, head_dim), axis=0)
    query_low = (query_bar * scale_vec).astype(BF16).reshape(-1, part)
    keys_low = to_earlier(plan, keys_grad).astype(BF16).reshape(-1, part)
    values_low = to_earlier(plan, values_grad).astype(BF16).reshape(-1, part)
    projected_low = jnp.concatenate([query_low, keys_low, values_low], axis=1)
    normed_grad = scatter_tokens(plan, dot_cols(projected_low, qkv))
    qkv_own = scatter_qkv(dot_rows(normed_all, projected_low))
    extra_one, attn_gain_grad = norm_back(normed_grad, stream, factor_one, gains[0])
    lower = middle_grad + extra_one
    return lower, qkv_own, dense_own, (attn_gain_grad, mlp_gain_grad), scale_vec_grad


def general_device(
    tokens,
    segments,
    qkv_weight,
    out_weight,
    up_weight,
    down_weight,
    attn_gain,
    mlp_gain,
    scale_param,
    cotangent,
):
    plan = Plan(tokens)
    layers, head_dim = scale_param.shape
    block_index = lax.axis_index("blk")
    scale_vecs = SCALE_BASE / math.sqrt(head_dim) * jax.nn.softplus(scale_param)
    own_gains = jnp.concatenate([attn_gain, mlp_gain], axis=0)
    gains = (
        lax.all_gather(own_gains.reshape(1, -1), ALL, axis=0, tiled=True)
        .reshape(-1, 2 * layers, attn_gain.shape[1])
        .transpose(1, 0, 2)
        .reshape(2 * layers, plan.width)
        .astype(F32)
    )
    if plan.whole:
        segments = lax.dynamic_slice_in_dim(
            segments, block_index * plan.own_seqs, plan.own_seqs, 0
        )
    allowed = window_mask(plan, segments, block_index)
    stream = to_plan(plan, tokens).astype(F32)
    qkvs, denses, kept = [], [], []
    for layer in range(layers):
        qkvs.append(gather_qkv(qkv_weight[layer]))
        own = jnp.concatenate([out_weight[layer], up_weight[layer], down_weight[layer]], axis=1)
        denses.append(lax.all_gather(own, ALL, axis=0, tiled=True))
        layer_gains = (gains[layer], gains[layers + layer])
        stream, saved = forward(
            plan, stream, qkvs[layer], denses[layer], layer_gains, scale_vecs[layer], allowed
        )
        kept.append(saved)
    layer_out = from_plan(plan, stream.astype(BF16))
    upper = to_plan(plan, cotangent).astype(F32)
    qkv_grads, dense_grads = [None] * layers, [None] * layers
    gain_grads, scale_grads = [None] * layers, [None] * layers
    for layer in reversed(range(layers)):
        layer_gains = (gains[layer], gains[layers + layer])
        upper, qkv_grads[layer], dense_grads[layer], gain_grads[layer], scale_grads[layer] = (
            backward(
                plan, upper, kept[layer], qkvs[layer], denses[layer], layer_gains,
                scale_vecs[layer], allowed,
            )
        )
    input_grad = from_plan(plan, upper.astype(BF16)).astype(F32)
    small = jnp.concatenate(
        [g[0] for g in gain_grads] + [g[1] for g in gain_grads] + scale_grads, axis=0
    )
    total = lax.psum(small, ALL)
    gain_total = total[: 2 * layers * plan.width].reshape(2 * layers, plan.width)
    owner = lax.axis_index(ALL)
    gain_rows = attn_gain.shape[1]
    own_total = lax.dynamic_slice_in_dim(gain_total, owner * gain_rows, gain_rows, 1)
    scale_total = total[2 * layers * plan.width :].reshape(layers, head_dim)
    scale_grad = scale_total * (SCALE_BASE / math.sqrt(head_dim)) * jax.nn.sigmoid(scale_param)
    dense_all = jnp.stack(dense_grads).astype(F32)
    width = plan.width
    return (
        layer_out,
        input_grad,
        jnp.stack(qkv_grads),
        dense_all[:, :, :width],
        dense_all[:, :, width:-width],
        dense_all[:, :, -width:],
        own_total[:layers],
        own_total[layers:],
        scale_grad,
    )


Q_ROWS = 256
KERNEL = pltpu.CompilerParams(vmem_limit_bytes=32 * 1024 * 1024)
LIGHT = pl.CostEstimate(flops=1 << 20, bytes_accessed=1 << 20, transcendentals=0)


def in_hbm(*arrays):
    return [pltpu.with_memory_space_constraint(array, pltpu.HBM) for array in arrays]


def allowed_keys(col, row, first):
    count = first + row.shape[1]
    key_place = lax.broadcasted_iota(jnp.int32, (count, row.shape[1]), 0)
    query_place = lax.broadcasted_iota(jnp.int32, (count, row.shape[1]), 1) + first
    return (col[:count] == row) & (key_place <= query_place)


def allowed_piece(col, row, start, first):
    same = col == row
    if start + col.shape[0] <= first:
        return same
    key_place = lax.broadcasted_iota(jnp.int32, same.shape, 0) + start
    return same & (key_place <= lax.broadcasted_iota(jnp.int32, same.shape, 1) + first)


def token_places(length, heads, token_rows, block_rows=Q_ROWS):
    for first in range(0, length, block_rows):
        parts = []
        for start in range(0, block_rows, token_rows):
            place = (first + start) // token_rows
            parts.append((start, place % heads, place // heads * token_rows))
        yield first, parts


FORWARD_ROWS, FORWARD_KEYS = 1024, 512


def attend_kernel(token_rows, proj_ref, scale_ref, col_ref, row_ref, out_ref, lse_ref):
    length = proj_ref.shape[-1]
    queries = (proj_ref[0, 0] * scale_ref[...]).astype(BF16)
    keys = proj_ref[1, 0].T.astype(BF16)
    values = proj_ref[2, 0].astype(BF16)
    for first, parts in token_places(length, out_ref.shape[0], token_rows, FORWARD_ROWS):
        end = first + FORWARD_ROWS
        block, row = queries[:, first:end], row_ref[:, first:end]
        pieces = []
        for start in range(0, end, FORWARD_KEYS):
            scores = jnp.dot(keys[start : start + FORWARD_KEYS], block, preferred_element_type=F32)
            allowed = allowed_piece(col_ref[start : start + FORWARD_KEYS], row, start, first)
            pieces.append(jnp.where(allowed, scores, MASKED_SCORE))
        top = functools.reduce(
            jnp.maximum, [jnp.max(piece, axis=0, keepdims=True) for piece in pieces]
        )
        total, attended = 0.0, 0.0
        for i, piece in enumerate(pieces):
            terms = jnp.exp(piece - top)
            total += jnp.sum(terms, axis=0, keepdims=True)
            attended += jnp.dot(
                values[:, i * FORWARD_KEYS : (i + 1) * FORWARD_KEYS],
                terms.astype(BF16),
                preferred_element_type=F32,
            )
        attended = (attended * (1.0 / total)).astype(BF16)
        lse_ref[0, :, first:end] = top + jnp.log(total)
        for start, owner, offset in parts:
            out_ref[owner, 0, :, offset : offset + token_rows] = attended[
                :, start : start + token_rows
            ]


def attend_rows(projected, scale_vec, segments, owners, token_rows):
    head_dim = scale_vec.shape[0]
    length = projected.shape[1]
    local_heads = projected.shape[0] // 3 // head_dim
    tokens = length // owners
    attended, log_total = pl.pallas_call(
        functools.partial(attend_kernel, token_rows),
        grid=(local_heads,),
        in_specs=[
            pl.BlockSpec((3, 1, head_dim, length), lambda h: (0, h, 0, 0)),
            pl.BlockSpec((head_dim, 1), lambda h: (0, 0)),
            pl.BlockSpec((length, 1), lambda h: (0, 0)),
            pl.BlockSpec((1, length), lambda h: (0, 0)),
        ],
        out_specs=[
            pl.BlockSpec((owners, 1, head_dim, tokens), lambda h: (0, h, 0, 0)),
            pl.BlockSpec((1, 1, length), lambda h: (h, 0, 0)),
        ],
        out_shape=[
            jax.ShapeDtypeStruct((owners, local_heads, head_dim, tokens), BF16),
            jax.ShapeDtypeStruct((local_heads, 1, length), F32),
        ],
        compiler_params=KERNEL,
        cost_estimate=LIGHT,
    )(
        projected.reshape(3, local_heads, head_dim, length),
        scale_vec.reshape(head_dim, 1),
        segments.reshape(length, 1),
        segments.reshape(1, length),
    )
    return attended.reshape(owners, local_heads * head_dim, tokens), log_total


def attend_back_kernel(
    token_rows,
    proj_ref,
    grad_ref,
    lse_ref,
    scale_ref,
    col_ref,
    row_ref,
    out_ref,
    scale_grad_ref,
    keys_acc,
    values_acc,
):
    length = proj_ref.shape[-1]
    scale = scale_ref[...]
    query_pre = proj_ref[0, 0]
    queries = (query_pre * scale).astype(BF16)
    keys_t = proj_ref[1, 0].astype(BF16)
    keys = proj_ref[1, 0].T.astype(BF16)
    values = proj_ref[2, 0].T.astype(BF16)
    keys_acc[...] = jnp.zeros_like(keys_acc)
    values_acc[...] = jnp.zeros_like(values_acc)
    scale_grad = jnp.zeros((scale.shape[0], 1), F32)
    for first, parts in token_places(length, grad_ref.shape[0], token_rows):
        end = first + Q_ROWS
        block = queries[:, first:end]
        grad = jnp.concatenate(
            [grad_ref[owner, 0, :, at : at + token_rows] for _, owner, at in parts], axis=1
        )
        scores = jnp.dot(keys[:end], block, preferred_element_type=F32)
        allowed = allowed_keys(col_ref[...], row_ref[:, first:end], first)
        scores = jnp.where(allowed, scores, MASKED_SCORE)
        probs = jnp.exp(scores - lse_ref[0, :, first:end])
        probs_grad = jnp.dot(values[:end], grad, preferred_element_type=F32)
        row_dot = jnp.sum(probs_grad * probs, axis=0, keepdims=True)
        scores_low = (probs * (probs_grad - row_dot)).astype(BF16)
        values_acc[:, :end] += lax.dot_general(
            grad, probs.astype(BF16), NT, preferred_element_type=F32
        )
        keys_acc[:, :end] += lax.dot_general(
            block, scores_low, NT, preferred_element_type=F32
        )
        query_bar = jnp.dot(keys_t[:, :end], scores_low, preferred_element_type=F32)
        query_bar = query_bar.astype(BF16).astype(F32)
        scale_grad += jnp.sum(query_bar * query_pre[:, first:end], axis=1, keepdims=True)
        out_ref[0, 0, :, first:end] = (query_bar * scale).astype(BF16)
    out_ref[1, 0] = keys_acc[...].astype(BF16)
    out_ref[2, 0] = values_acc[...].astype(BF16)
    spread = jnp.broadcast_to(scale_grad, scale_grad_ref.shape)

    @pl.when(pl.program_id(0) == 0)
    def _():
        scale_grad_ref[...] = spread

    @pl.when(pl.program_id(0) > 0)
    def _():
        scale_grad_ref[...] += spread


def attend_back_rows(projected, attended_grad, log_total, scale_vec, segments, token_rows):
    head_dim = scale_vec.shape[0]
    length = projected.shape[1]
    local_heads = projected.shape[0] // 3 // head_dim
    owners, _, tokens = attended_grad.shape
    lanes = 128
    grads, scale_grad = pl.pallas_call(
        functools.partial(attend_back_kernel, token_rows),
        grid=(local_heads,),
        in_specs=[
            pl.BlockSpec((3, 1, head_dim, length), lambda h: (0, h, 0, 0)),
            pl.BlockSpec((owners, 1, head_dim, tokens), lambda h: (0, h, 0, 0)),
            pl.BlockSpec((1, 1, length), lambda h: (h, 0, 0)),
            pl.BlockSpec((head_dim, 1), lambda h: (0, 0)),
            pl.BlockSpec((length, 1), lambda h: (0, 0)),
            pl.BlockSpec((1, length), lambda h: (0, 0)),
        ],
        out_specs=[
            pl.BlockSpec((3, 1, head_dim, length), lambda h: (0, h, 0, 0)),
            pl.BlockSpec((head_dim, lanes), lambda h: (0, 0)),
        ],
        out_shape=[
            pltpu.HBM((3, local_heads, head_dim, length), BF16),
            pltpu.HBM((head_dim, lanes), F32),
        ],
        scratch_shapes=[
            pltpu.VMEM((head_dim, length), F32),
            pltpu.VMEM((head_dim, length), F32),
        ],
        compiler_params=KERNEL,
        cost_estimate=LIGHT,
    )(
        *in_hbm(
            projected.reshape(3, local_heads, head_dim, length),
            attended_grad.reshape(owners, local_heads, head_dim, tokens),
        ),
        log_total,
        scale_vec.reshape(head_dim, 1),
        segments.reshape(length, 1),
        segments.reshape(1, length),
    )
    return grads.reshape(3 * local_heads * head_dim, length), scale_grad[:, 0]


def dense_grad_kernel(
    core_ref, attended_ref, normed_ref, active_ref, out_bar, up_bar, down_bar,
    own_ref, other_ref, normed_t, active_t,
):
    tile = pl.program_id(0)
    rows, width = 8 * own_ref.shape[3], out_bar.shape[1]

    @pl.when(tile == 0)
    def _():
        normed_t[...] = normed_ref[...].astype(F32).T.astype(BF16)
        active_t[...] = active_ref[...].astype(F32).T.astype(BF16)

    start = pl.multiple_of(tile * rows, rows)
    first_core = core_ref[2] == 0
    lefts = (attended_ref, normed_t, active_t)
    for i, (left, right) in enumerate(zip(lefts, (out_bar, up_bar, down_bar))):
        grad = jnp.dot(left[pl.ds(start, rows), :], right[...], preferred_element_type=F32)
        grad = grad.reshape(2, 2, 2, rows // 8, width)
        one, two = grad[:, :, 0], grad[:, :, 1]
        own_ref[:, :, 0, :, i * width : (i + 1) * width] = jnp.where(
            first_core, one, two
        ).astype(BF16)
        other_ref[:, :, 0, :, i * width : (i + 1) * width] = jnp.where(
            first_core, two, one
        ).astype(BF16)


def dense_grads(attended_t, normed, active, out_bar, up_bar, down_bar):
    width, tokens = attended_t.shape
    own = width // 32
    whole = pl.BlockSpec((tokens, width), lambda i, core: (0, 0))
    rows = pl.BlockSpec((2, 2, 1, own, 3 * width), lambda i, core: (0, 0, i, 0, 0))
    shape = pltpu.HBM((2, 2, 4, own, 3 * width), BF16)
    return pl.pallas_call(
        dense_grad_kernel,
        grid_spec=pltpu.PrefetchScalarGridSpec(
            num_scalar_prefetch=1,
            grid=(4,),
            in_specs=[pl.BlockSpec((width, tokens), lambda i, core: (0, 0))] + [whole] * 5,
            out_specs=[rows, rows],
            scratch_shapes=[pltpu.VMEM((width, tokens), BF16)] * 2,
        ),
        out_shape=[shape, shape],
        compiler_params=KERNEL,
        cost_estimate=LIGHT,
    )(place(), *in_hbm(attended_t, normed, active, out_bar, up_bar, down_bar))


def place():
    head = lax.axis_index("head")
    return jnp.stack([lax.axis_index("blk"), head // 2, head % 2]).astype(jnp.int32)


def assemble_kernel(place_ref, *refs):
    pieces, whole_ref = refs[:10], refs[10]
    half = whole_ref.shape[-1] // 2
    blk, row, core = place_ref[0], place_ref[1], place_ref[2]
    for i in range(2):
        at_core = core if i == 0 else 1 - core
        own, across, beside, one, two = pieces[5 * i : 5 * i + 5]
        whole_ref[0, blk, row, at_core] = own[0]
        whole_ref[0, 1 - blk, row, at_core] = across[0]
        whole_ref[0, blk, 1 - row, at_core] = beside[0]
        whole_ref[0, 1 - blk, 1 - row, at_core, :, :half] = one[0]
        whole_ref[0, 1 - blk, 1 - row, at_core, :, half:] = two[0]


def assemble(pieces):
    batch, own, columns = pieces[0].shape
    specs = [
        pl.BlockSpec((1, own, piece.shape[-1]), lambda i, at: (i, 0, 0))
        for piece in pieces
    ]
    whole = pl.pallas_call(
        assemble_kernel,
        grid_spec=pltpu.PrefetchScalarGridSpec(
            num_scalar_prefetch=1,
            grid=(batch,),
            in_specs=specs,
            out_specs=pl.BlockSpec((1, 2, 2, 2, own, columns), lambda i, at: (i, 0, 0, 0, 0, 0)),
        ),
        out_shape=jax.ShapeDtypeStruct((batch, 2, 2, 2, own, columns), BF16),
        compiler_params=KERNEL,
        cost_estimate=LIGHT,
    )(place(), *pieces)
    return whole.reshape(-1, columns)


def assemble_columns_kernel(place_ref, along_ref, across_ref, whole_ref, *extra_ref):
    blk = place_ref[0]
    columns = whole_ref.shape[-1]
    whole_ref[0, blk] = along_ref[0, :, :columns]
    whole_ref[0, 1 - blk] = across_ref[0, :, :columns]
    for extra in extra_ref:
        extra[0, blk] = along_ref[0, :, columns:]
        extra[0, 1 - blk] = across_ref[0, :, columns:]


def assemble_columns(along, across, columns):
    batch, own, both = along.shape
    rows = pl.BlockSpec((1, own, both), lambda i, at: (i, 0, 0))
    shapes = [(batch, 2, own, columns)]
    if both > columns:
        shapes.append((batch, 2, own, both - columns))
    parts = pl.pallas_call(
        assemble_columns_kernel,
        grid_spec=pltpu.PrefetchScalarGridSpec(
            num_scalar_prefetch=1,
            grid=(batch,),
            in_specs=[rows, rows],
            out_specs=[pl.BlockSpec((1,) + s[1:], lambda i, at: (i, 0, 0, 0)) for s in shapes],
        ),
        out_shape=[pltpu.HBM(s, BF16) for s in shapes],
        compiler_params=KERNEL,
        cost_estimate=LIGHT,
    )(place(), *in_hbm(along, across))
    return [part.reshape(-1, part.shape[-1]) for part in parts]


def assemble_wide_kernel(place_ref, along_ref, across_ref, whole_ref):
    blk = place_ref[0]
    own, columns = along_ref.shape[1], whole_ref.shape[-1]
    for i in range(along_ref.shape[-1] // columns):
        place, part = slice(i * own, (i + 1) * own), slice(i * columns, (i + 1) * columns)
        whole_ref[0, blk, place, :] = along_ref[0, :, part]
        whole_ref[0, 1 - blk, place, :] = across_ref[0, :, part]


def assemble_wide(along, across, columns):
    batch, own, wide = along.shape
    rows = own * (wide // columns)
    piece = pl.BlockSpec((1, own, wide), lambda i, at: (i, 0, 0))
    whole = pl.pallas_call(
        assemble_wide_kernel,
        grid_spec=pltpu.PrefetchScalarGridSpec(
            num_scalar_prefetch=1,
            grid=(batch,),
            in_specs=[piece, piece],
            out_specs=pl.BlockSpec((1, 2, rows, columns), lambda i, at: (i, 0, 0, 0)),
        ),
        out_shape=pltpu.HBM((batch, 2, rows, columns), BF16),
        compiler_params=KERNEL,
        cost_estimate=LIGHT,
    )(place(), *in_hbm(along, across))
    return whole.reshape(-1, columns)


def project_kernel(with_norm, place_ref, *refs):
    pieces, (gain_ref, weight_ref, normed_ref, projected_ref) = refs[:4], refs[4:]
    head = place_ref[1] * 2 + place_ref[2]
    rows = pieces[0].shape[0]
    for i, piece in enumerate(pieces):
        value = piece[...]
        if with_norm:
            stream = value.astype(F32)
            factor = lax.rsqrt(jnp.mean(stream * stream, axis=-1, keepdims=True) + EPSILON)
            value = (stream * factor * gain_ref[...]).astype(BF16)
        normed_ref[pl.ds(pl.multiple_of((head ^ i) * rows, rows), rows), :] = value
    projected = jnp.dot(normed_ref[...], weight_ref[...], preferred_element_type=F32)
    projected_ref[...] = projected.T


def project(pieces, gain, weight, with_norm, token_rows):
    tokens, width = pieces[0].shape
    length, columns = 4 * tokens, weight.shape[1]
    groups = tokens // token_rows
    piece = pl.BlockSpec((token_rows, width), lambda g, at: (g, 0))
    return pl.pallas_call(
        functools.partial(project_kernel, with_norm),
        grid_spec=pltpu.PrefetchScalarGridSpec(
            num_scalar_prefetch=1,
            grid=(groups,),
            in_specs=[piece] * 4
            + [
                pl.BlockSpec((1, width), lambda g, at: (0, 0)),
                pl.BlockSpec((width, columns), lambda g, at: (0, 0)),
            ],
            out_specs=[
                pl.BlockSpec((4 * token_rows, width), lambda g, at: (g, 0)),
                pl.BlockSpec((columns, 4 * token_rows), lambda g, at: (0, g)),
            ],
        ),
        out_shape=[
            pltpu.HBM((length, width), BF16),
            jax.ShapeDtypeStruct((columns, length), F32),
        ],
        compiler_params=KERNEL,
        cost_estimate=LIGHT,
    )(place(), *in_hbm(*pieces), gain.reshape(1, width), *in_hbm(weight))


def project_back_kernel(
    place_ref, bars_ref, weight_ref, normed_ref, own_ref, other_ref, grad_ref, bars_t
):
    @pl.when(pl.program_id(0) == 0)
    def _():
        bars_t[...] = bars_ref[...].astype(F32).T.astype(BF16)

    upper = lax.dot_general(bars_t[...], weight_ref[...], NT, preferred_element_type=F32)
    upper = upper.reshape(2, 2, 2, -1, upper.shape[-1])
    first_core = place_ref[2] == 0
    one, two = upper[:, :, 0], upper[:, :, 1]
    own_ref[...] = jnp.where(first_core, one, two)
    other_ref[...] = jnp.where(first_core, two, one).astype(BF16)
    grad = lax.dot_general(normed_ref[...], bars_t[...], TN, preferred_element_type=F32)
    grad_ref[...] = grad.astype(BF16)


def project_back(bars, weight, normed, token_rows):
    columns, length = bars.shape
    width = weight.shape[0]
    tile = width // 2
    quarter = pl.BlockSpec((2, 2, token_rows, tile), lambda i, at: (0, 0, 0, i))
    return pl.pallas_call(
        project_back_kernel,
        grid_spec=pltpu.PrefetchScalarGridSpec(
            num_scalar_prefetch=1,
            grid=(2,),
            in_specs=[
                pl.BlockSpec((columns, length), lambda i, at: (0, 0)),
                pl.BlockSpec((tile, columns), lambda i, at: (i, 0)),
                pl.BlockSpec((length, tile), lambda i, at: (0, i)),
            ],
            out_specs=[quarter, quarter, pl.BlockSpec((tile, columns), lambda i, at: (i, 0))],
            scratch_shapes=[pltpu.VMEM((length, columns), BF16)],
        ),
        out_shape=[
            pltpu.HBM((2, 2, token_rows, width), F32),
            pltpu.HBM((2, 2, token_rows, width), BF16),
            pltpu.HBM((width, columns), BF16),
        ],
        compiler_params=KERNEL,
        cost_estimate=LIGHT,
    )(place(), *in_hbm(bars, weight, normed))


def rows_back_kernel(place_ref, bars_ref, weight_ref, own_ref, other_ref, bars_t):
    @pl.when(pl.program_id(0) == 0)
    def _():
        bars_t[...] = bars_ref[...].astype(F32).T.astype(BF16)

    upper = lax.dot_general(bars_t[...], weight_ref[...], NT, preferred_element_type=F32)
    upper = upper.reshape(2, 2, 2, -1, upper.shape[-1])
    first_core = place_ref[2] == 0
    one, two = upper[:, :, 0], upper[:, :, 1]
    own_ref[...] = jnp.where(first_core, one, two)
    other_ref[...] = jnp.where(first_core, two, one).astype(BF16)


def rows_back(bars, weight, token_rows):
    columns, length = bars.shape
    width = weight.shape[0]
    tile = width // 2
    quarter = pl.BlockSpec((2, 2, token_rows, tile), lambda i, at: (0, 0, 0, i))
    return pl.pallas_call(
        rows_back_kernel,
        grid_spec=pltpu.PrefetchScalarGridSpec(
            num_scalar_prefetch=1,
            grid=(2,),
            in_specs=[
                pl.BlockSpec((columns, length), lambda i, at: (0, 0)),
                pl.BlockSpec((tile, columns), lambda i, at: (i, 0)),
            ],
            out_specs=[quarter, quarter],
            scratch_shapes=[pltpu.VMEM((length, columns), BF16)],
        ),
        out_shape=[
            pltpu.HBM((2, 2, token_rows, width), F32),
            pltpu.HBM((2, 2, token_rows, width), BF16),
        ],
        compiler_params=KERNEL,
        cost_estimate=LIGHT,
    )(place(), *in_hbm(bars, weight))


def weight_back_kernel(bars_ref, normed_ref, grad_ref):
    grad = jnp.dot(bars_ref[...], normed_ref[...], preferred_element_type=F32)
    grad_ref[...] = grad.T.astype(BF16)


def weight_back(bars, normed):
    columns, length = bars.shape
    width = normed.shape[1]
    tile = width // 5
    return pl.pallas_call(
        weight_back_kernel,
        grid=(5,),
        in_specs=[
            pl.BlockSpec((columns, length), lambda i: (0, 0)),
            pl.BlockSpec((length, tile), lambda i: (0, i)),
        ],
        out_specs=pl.BlockSpec((tile, columns), lambda i: (i, 0)),
        out_shape=pltpu.HBM((width, columns), BF16),
        compiler_params=KERNEL,
        cost_estimate=LIGHT,
    )(*in_hbm(bars, normed))


def tied(*arrays):
    return lax.optimization_barrier(arrays)


def swapped(array, axis, mask):
    size = lax.axis_size(axis)
    return lax.ppermute(array, axis, [(i, i ^ mask) for i in range(size)])


def pick(array, index, axis=0):
    return lax.dynamic_index_in_dim(array, index, axis, keepdims=False)


def swap_halves(array):
    me = lax.axis_index("blk")
    got = swapped(pick(array, 1 - me), "blk", 1)
    kept = pick(array, me)
    return jnp.stack([jnp.where(me == 0, kept, got), jnp.where(me == 0, got, kept)])


def scatter_row(halves):
    row = lax.axis_index("head") // 2
    got = swapped(pick(halves, 1 - row, 1).astype(BF16), "head", 2).astype(F32)
    return (pick(halves, row, 1) + got).reshape(-1, halves.shape[-1])


def over_head(parts):
    return lax.all_to_all(parts, "head", split_axis=0, concat_axis=0, tiled=True)


def qkv_columns(rows, extra):
    own, width = rows.shape
    part = width // 3 // 4
    sent = rows.reshape(own, 3, 4, part).transpose(2, 0, 1, 3).reshape(4, own, 3 * part)
    if extra is not None:
        sent = jnp.concatenate([sent, jnp.broadcast_to(extra[None], (4,) + extra.shape)], axis=2)
    return over_head(sent)


def along_batch(piece):
    return lax.all_gather(piece, "batch", axis=0, tiled=False)


def other_core(array):
    return swapped(array, "head", 1)


def to_beside(across):
    return swapped(across[..., : across.shape[-1] // 2], "head", 2)


def to_across(beside):
    return swapped(beside[..., beside.shape[-1] // 2 :], "blk", 1)


def over_batch(parts):
    return lax.psum_scatter(parts.astype(BF16), "batch", scatter_dimension=0, tiled=False)


def across_sum(halves):
    blk = lax.axis_index("blk")
    got = swapped(pick(halves, 1 - blk), "blk", 1).astype(F32)
    return (pick(halves, blk).astype(F32) + got).astype(BF16)


def columns_to_rows(moved):
    rows = moved.shape[1]
    return moved.reshape(4, rows, 3, -1).transpose(1, 2, 0, 3).reshape(rows, -1).astype(F32)


def quarter(parts, blk, row):
    one, two = (pick(pick(part, blk), row).astype(F32) for part in parts)
    return one + two


def diagonal_rows(parts):
    blk, row = place()[:2]
    rows = quarter(parts, 1 - blk, 1 - row).astype(BF16)
    half = rows.shape[-1] // 2
    return rows[..., :half], rows[..., half:]


def neighbour_rows(parts, one, two):
    blk, row = place()[:2]
    half = one.shape[-1]
    across, beside = quarter(parts, 1 - blk, row), quarter(parts, blk, 1 - row)
    across = jnp.concatenate([across[..., :half], across[..., half:] + two.astype(F32)], axis=-1)
    beside = jnp.concatenate([beside[..., :half] + one.astype(F32), beside[..., half:]], axis=-1)
    return across.astype(BF16), beside.astype(BF16)


def sent_beside_and_across(across, beside):
    return swapped(across, "blk", 1), swapped(beside, "head", 2)


def heads_grad(weight, out_bar):
    return dot_cols(weight, out_bar).astype(BF16).reshape(4, -1, out_bar.shape[0])


def own_quarter(parts):
    blk, row = place()[:2]
    return quarter(parts, blk, row)


def own_sum(own, *more):
    return sum((part.astype(F32) for part in more), own).astype(BF16)


def sum_over(array, *hops):
    for axis, mask in hops:
        array = array + swapped(array, axis, mask)
    return array


def gain_back(weight, weight_grad, gain):
    return jnp.sum(weight.astype(F32) * weight_grad, axis=-1) / gain.astype(F32)


def lower_of(upper, stream, factor, gain):
    return norm_back(upper, stream, factor, gain)[0]


def spread_device(
    tokens,
    segments,
    qkv_weight,
    out_weight,
    up_weight,
    down_weight,
    attn_gain,
    mlp_gain,
    scale_param,
    cotangent,
):
    layers, head_dim = scale_param.shape
    _, token_rows, width = tokens.shape
    scale_vecs = SCALE_BASE / math.sqrt(head_dim) * jax.nn.softplus(scale_param)
    segments = pick(segments, lax.axis_index("blk"))
    own_gains = jnp.concatenate([attn_gain, mlp_gain], axis=0)

    part3 = 3 * width // 4
    dense_own = [
        jnp.concatenate([out_weight[i], up_weight[i], down_weight[i]], axis=1) for i in (0, 1)
    ]

    first = swap_halves(tokens).reshape(-1, width)
    columns = qkv_columns(qkv_weight[0], own_gains.T)
    columns, first, cotangent = tied(columns.reshape(-1, columns.shape[-1]), first, cotangent)
    stream = first.astype(F32)
    along = along_batch(columns)
    far, near = swapped(first, "head", 2), other_core(first)
    both = other_core(far)
    upper = swap_halves(cotangent)
    along, near, far, both, dense_near, upper = tied(
        along, near, far, both, dense_own[0], upper
    )
    token_pieces = (first, near, far, both)
    dense_near = along_batch(dense_near)
    qkv_across = swapped(along, "blk", 1)
    next_columns = jnp.concatenate(list(qkv_columns(qkv_weight[1], None)), axis=1)
    qkv_across, dense_near, next_columns = tied(qkv_across, dense_near, next_columns)
    across, beside = swapped(dense_near, "blk", 1), swapped(dense_near, "head", 2)
    next_both = along_batch(jnp.stack([next_columns, dense_own[1]]))
    weight, gains = assemble_columns(along, qkv_across, part3)
    qkvs = [weight]
    gains = gains.T.astype(F32)

    kept, denses = [], []
    for layer in range(layers):
        normed, factor_one = normalize(stream, gains[layer])
        if layer == 1:
            normed = normed.astype(BF16)
            far, near = swapped(normed, "head", 2), other_core(normed)
            far, next_across, dense_next = tied(far, next_across, dense_next)
            across, beside = swapped(dense_next, "blk", 1), swapped(dense_next, "head", 2)
            token_pieces = (normed, near, far, other_core(far))
            qkvs.append(assemble_wide(next_along, next_across, part3))
        normed_all, projected = project(
            token_pieces, gains[layer], qkvs[layer], layer == 0, token_rows
        )
        attended, log_total = attend_rows(
            projected, scale_vecs[layer], segments, 4, token_rows
        )
        attended, across, beside = tied(attended, across, beside)
        one, two = to_beside(across), to_across(beside)
        if layer == 0:
            two, next_both = tied(two, next_both)
            next_along, dense_next = next_both[:, 0], next_both[:, 1]
            next_across = swapped(next_along, "blk", 1)
            attended_t, one, two = tied(over_head(attended), one, two)
        else:
            dense_near = dense_next
            attended_t, one, two = tied(over_head(attended), one, two)
        pieces = (dense_near, across, beside, one, two)
        pieces += tuple(other_core(piece) for piece in pieces)
        attended_t = attended_t.reshape(width, -1)
        denses.append(assemble(pieces))
        dense = denses[layer]
        out_w, up_w, down_w = dense[:, :width], dense[:, width:-width], dense[:, -width:]
        middle = stream + dot_rows(attended_t, out_w)
        normed_two, factor_two = normalize(middle, gains[layers + layer])
        normed_two = normed_two.astype(BF16)
        hidden = dot(normed_two, up_w)
        active = (hidden * jax.nn.sigmoid(hidden)).astype(BF16)
        kept.append(
            (
                stream, factor_one, normed_all, projected, log_total, attended_t, middle,
                factor_two, normed_two, hidden, active,
            )
        )
        stream = middle + dot(active, down_w)
    layer_out = swap_halves(stream.astype(BF16).reshape(tokens.shape))
    upper = upper.reshape(-1, width).astype(F32)

    scale_grads = [None] * layers
    for layer in reversed(range(layers)):
        (
            stream, factor_one, normed_all, projected, log_total, attended_t, middle,
            factor_two, normed_two, hidden, active,
        ) = kept[layer]
        qkv, dense = qkvs[layer], denses[layer]
        out_w, up_w, down_w = dense[:, :width], dense[:, width:-width], dense[:, -width:]
        down_bar = upper.astype(BF16)
        gate = jax.nn.sigmoid(hidden)
        up_bar = (
            dot_cols(down_bar, down_w) * gate * (1.0 + hidden * (1.0 - gate))
        ).astype(BF16)
        middle_grad = upper + lower_of(
            dot_cols(up_bar, up_w), middle, factor_two, gains[layers + layer]
        )
        out_bar = middle_grad.astype(BF16)
        if layer == 0:
            attended_grad = over_head(heads_grad(out_w, out_bar))
            grads, others = dense_grads(attended_t, normed_two, active, out_bar, up_bar, down_bar)
            others, across = tied(others, across)
            others, own = tied(others, own_quarter(cored) + across.astype(F32))
            attended_grad, others, z_sum, beside = tied(attended_grad, others, z_sum, beside)
            others = other_core(others)
            attended_grad, summed = tied(attended_grad, own_sum(own, beside))
            summed = over_batch(summed)
            earlier = across_sum(z_sum)
        else:
            attended_grad = over_head(heads_grad(out_w, out_bar))
            grads, others = dense_grads(attended_t, normed_two, active, out_bar, up_bar, down_bar)
            attended_grad, others, layer_out = tied(attended_grad, others, layer_out)
            others = other_core(others)
        bars, scale_grads[layer] = attend_back_rows(
            projected, attended_grad, log_total, scale_vecs[layer], segments, token_rows
        )
        if layer == 0:
            bars, earlier = tied(bars, earlier)
            qkv_grad = weight_back(bars, normed_all)
            bars, qkv_grad, others = tied(bars, qkv_grad, others)
            z_sum = over_batch(qkv_grad.reshape(4, 2, -1, qkv_grad.shape[-1]))
            cored = (grads, others)
            bars, rows = tied(bars, diagonal_rows(cored))
            diagonal = sent_beside_and_across(*rows)
            halves, to_core = rows_back(bars, qkv, token_rows)
            scale_sum = sum_over(jnp.stack(scale_grads), ("head", 1))
            halves, to_core, diagonal, summed, scale_sum = tied(
                halves, to_core, diagonal, summed, scale_sum
            )
            scale_sum = sum_over(scale_sum, ("head", 2))
            halves, to_core, rows, scale_sum = tied(
                halves, to_core, neighbour_rows(cored, *diagonal), scale_sum
            )
            sent = sent_beside_and_across(*rows)
            halves = halves + other_core(to_core).astype(F32)
            scale_sum = sum_over(scale_sum, ("batch", 1), ("batch", 2), ("blk", 1))
            own = own_quarter(cored)
            halves, sent, z_sum, scale_sum, own = tied(halves, sent, z_sum, scale_sum, own)
            halves, own, earlier = tied(halves, own_sum(own, *sent), earlier)
            moved = over_head(earlier.reshape(4, -1, earlier.shape[-1]))
            dense_first = over_batch(own)
            normed_grad = scatter_row(halves)
            z_across, dense_first = tied(across_sum(z_sum), dense_first)
            z_across = over_head(z_across.reshape(4, -1, z_across.shape[-1]))
            dense_grad = [dense_first, summed]
            qkv_grads = [columns_to_rows(z_across), columns_to_rows(moved)]
        else:
            bars, others = tied(bars, others)
            cored = (grads, others)
            bars, rows = tied(bars, diagonal_rows(cored))
            diagonal = sent_beside_and_across(*rows)
            halves, to_core, qkv_grad = project_back(bars, qkv, normed_all, token_rows)
            z_sum = over_batch(qkv_grad.reshape(4, 2, -1, qkv_grad.shape[-1]))
            to_core, halves, diagonal = tied(to_core, halves, diagonal)
            to_core, rows = tied(to_core, neighbour_rows(cored, *diagonal))
            across = swapped(rows[0], "blk", 1)
            halves = halves + other_core(to_core).astype(F32)
            normed_grad = scatter_row(halves)
            normed_grad, beside = tied(normed_grad, rows[1])
            beside = swapped(beside, "head", 2)
        upper = middle_grad + lower_of(normed_grad, stream, factor_one, gains[layer])
    input_grad = swap_halves(upper.astype(BF16).reshape(tokens.shape)).astype(F32)
    scale_grad = scale_sum * (SCALE_BASE / math.sqrt(head_dim)) * jax.nn.sigmoid(scale_param)
    dense_all = jnp.stack([part.astype(F32) for part in dense_grad])
    qkv_all = jnp.stack(qkv_grads)
    up_all = dense_all[:, :, width:-width]
    return (
        layer_out,
        input_grad,
        qkv_all,
        dense_all[:, :, :width],
        up_all,
        dense_all[:, :, -width:],
        gain_back(qkv_weight, qkv_all, attn_gain),
        gain_back(up_weight, up_all, mlp_gain),
        scale_grad,
    )


def per_device(*args):
    tokens, segments = args[0], args[1]
    sizes = tuple(lax.axis_size(axis) for axis in ALL)
    heads = tokens.shape[2] // args[8].shape[1]
    spread = (
        sizes == (4, 2, 4)
        and tokens.shape[0] == 2
        and args[2].shape[0] == 2
        and tokens.shape[1] % 128 == 0
        and Q_ROWS % tokens.shape[1] == 0
        and segments.shape[1] <= WINDOW
        and segments.shape[1] % FORWARD_ROWS == 0
        and heads % 4 == 0
        and tokens.shape[2] % 256 == 0
    )
    return spread_device(*args) if spread else general_device(*args)


def solution(mesh):
    rows = P(None, ALL, None)
    by_token = P("batch", ("blk", "head"), None)
    return jax.shard_map(
        per_device,
        mesh=mesh,
        in_specs=(
            by_token, P("batch", None), rows, rows, rows, rows, P(None, ALL), P(None, ALL), P(),
            by_token,
        ),
        out_specs=(
            by_token, by_token, rows, rows, rows, rows, P(None, ALL), P(None, ALL), P(),
        ),
        check_vma=False,
    )
```

```python
import functools
import math

import jax
import jax.numpy as jnp
from jax import lax
from jax.experimental import pallas as pl
from jax.experimental.pallas import tpu as pltpu
from jax.sharding import PartitionSpec as P

WINDOW = 1024
EPSILON = 1e-06
SCALE_BASE = 1.4426950408889634
MASKED_SCORE = -1e30

ALL = ("batch", "blk", "head")
REST = ("batch", "blk")
F32 = jnp.float32
BF16 = jnp.bfloat16


def shifted(block, axis, distance):
    devices = range(lax.axis_size(axis))
    route = [(i - distance, i) for i in devices if i - distance in devices]
    return lax.ppermute(block, axis, route)


NT = (((1,), (1,)), ((), ()))
TN = (((0,), (0,)), ((), ()))


def dot(left, right):
    return jnp.dot(left, right, preferred_element_type=F32)


def dot_rows(left, right):
    return lax.dot_general(left, right, (((0,), (0,)), ((), ())), preferred_element_type=F32)


def dot_cols(left, right):
    return lax.dot_general(left, right, (((1,), (1,)), ((), ())), preferred_element_type=F32)


def normalize(stream, gain):
    factor = lax.rsqrt(jnp.mean(stream * stream, axis=-1, keepdims=True) + EPSILON)
    return stream * factor * gain, factor


def norm_back(upper, stream, factor, gain):
    inner = upper * gain
    gain_grad = jnp.sum(upper * stream * factor, axis=0)
    lower = factor * inner - stream * factor * factor * factor * jnp.mean(
        inner * stream, axis=-1, keepdims=True
    )
    return lower, gain_grad


class Plan:
    def __init__(self, tokens):
        self.seqs, self.rows, self.width = tokens.shape
        self.heads = lax.axis_size("head")
        self.blks = lax.axis_size("blk")
        self.block = self.rows * self.heads
        self.whole = self.seqs % self.blks == 0
        if self.whole:
            self.groups, self.own_seqs = self.blks, self.seqs // self.blks
            self.reach = 0
        else:
            self.groups, self.own_seqs = 1, self.seqs
            self.reach = min((WINDOW - 1) // self.block + 1, self.blks - 1)
        self.length = self.groups * self.block
        self.tokens = self.seqs * self.rows


def to_plan(plan, array):
    if plan.whole and plan.blks > 1:
        array = lax.all_to_all(array, "blk", split_axis=0, concat_axis=0, tiled=True)
    return array.reshape(plan.tokens, plan.width)


def from_plan(plan, flat):
    array = flat.reshape(plan.seqs, plan.rows, plan.width)
    if plan.whole and plan.blks > 1:
        array = lax.all_to_all(array, "blk", split_axis=0, concat_axis=0, tiled=True)
    return array


def in_sequence(plan, by_head, width):
    parts = by_head.reshape(plan.heads, plan.groups, plan.own_seqs, plan.rows, width)
    return parts.transpose(2, 1, 0, 3, 4).reshape(-1, width)


def by_owner(plan, rows, width):
    parts = rows.reshape(plan.own_seqs, plan.groups, plan.heads, plan.rows, width)
    return parts.transpose(2, 1, 0, 3, 4).reshape(plan.heads, plan.tokens, width)


def gather_tokens(plan, rows):
    moved = lax.all_gather(rows, "head", axis=0, tiled=False)
    return in_sequence(plan, moved, rows.shape[-1])


def scatter_tokens(plan, rows):
    width = rows.shape[-1]
    return lax.psum_scatter(
        by_owner(plan, rows.astype(BF16), width), "head", scatter_dimension=0, tiled=False
    ).astype(F32)


def heads_to_tokens(plan, rows):
    part = rows.shape[-1]
    moved = lax.all_to_all(
        by_owner(plan, rows, part), "head", split_axis=0, concat_axis=0, tiled=True
    )
    return moved.transpose(1, 0, 2).reshape(plan.tokens, plan.heads * part)


def tokens_to_heads(plan, rows):
    part = rows.shape[-1] // plan.heads
    sent = rows.reshape(plan.tokens, plan.heads, part).transpose(1, 0, 2)
    moved = lax.all_to_all(sent, "head", split_axis=0, concat_axis=0, tiled=True)
    return in_sequence(plan, moved, part)


def gather_qkv(rows):
    own, width = rows.shape
    heads = lax.axis_size("head")
    part = width // 3 // heads
    sent = rows.reshape(own, 3, heads, part).transpose(2, 0, 1, 3).reshape(heads, own, 3 * part)
    moved = lax.all_to_all(sent, "head", split_axis=0, concat_axis=0, tiled=True)
    full = lax.all_gather(moved, REST, axis=0, tiled=True)
    return full.reshape(-1, 3 * part)


def scatter_qkv(grad):
    heads = lax.axis_size("head")
    part = grad.shape[1] // 3
    summed = lax.psum_scatter(grad.astype(BF16), REST, scatter_dimension=0, tiled=True)
    own = summed.shape[0] // heads
    moved = lax.all_to_all(
        summed.reshape(heads, own, 3 * part), "head", split_axis=0, concat_axis=0, tiled=True
    )
    return (
        moved.reshape(heads, own, 3, part)
        .transpose(1, 2, 0, 3)
        .reshape(own, 3 * heads * part)
        .astype(F32)
    )


def window_mask(plan, segments, block_index):
    key_count = plan.length + plan.reach * plan.block
    if plan.whole:
        query_segs, key_segs = segments, segments
    else:
        leading = jnp.full((plan.own_seqs, plan.reach * plan.block), -1, jnp.int32)
        padded = jnp.concatenate([leading, segments], axis=1)
        start = block_index * plan.block
        query_segs = lax.dynamic_slice_in_dim(segments, start, plan.block, 1)
        key_segs = lax.dynamic_slice_in_dim(padded, start, key_count, 1)
    query_place = jnp.arange(plan.length, dtype=jnp.int32)[:, None] + plan.reach * plan.block
    key_place = jnp.arange(key_count, dtype=jnp.int32)[None, :]
    near = (key_place <= query_place) & (query_place - key_place < WINDOW)
    return (key_segs[:, None, :] == query_segs[:, :, None]) & near[None]


def with_earlier(plan, own):
    arrived = [own]
    for _ in range(plan.reach):
        arrived.append(shifted(arrived[-1], "blk", 1))
    return jnp.concatenate(arrived[::-1], axis=1) if plan.reach else own


def to_earlier(plan, grads):
    if not plan.reach:
        return grads
    block = plan.block
    total = grads[:, :block]
    for step in range(1, plan.reach + 1):
        total = (
            shifted(total.astype(BF16), "blk", -1).astype(F32)
            + grads[:, step * block : (step + 1) * block]
        )
    return total


def scores_of(queries, keys, allowed):
    scores = jnp.einsum("sqhd,skhd->shqk", queries, keys, preferred_element_type=F32)
    return jnp.where(allowed[:, None], scores, MASKED_SCORE)


def attend(queries, keys, values, allowed):
    scores = scores_of(queries, keys, allowed)
    top_score = jnp.max(scores, axis=-1, keepdims=True)
    exp_terms = jnp.exp(scores - top_score)
    totals = jnp.sum(exp_terms, axis=-1, keepdims=True)
    probs_low = (exp_terms / totals).astype(BF16)
    attended = jnp.einsum("shqk,skhd->sqhd", probs_low, values, preferred_element_type=F32)
    return attended, top_score + jnp.log(totals)


def attend_back(queries, keys, values, allowed, log_total, attended_grad):
    probs = jnp.exp(scores_of(queries, keys, allowed) - log_total)
    probs_low = probs.astype(BF16)
    values_grad = jnp.einsum(
        "shqk,sqhd->skhd", probs_low, attended_grad, preferred_element_type=F32
    )
    probs_grad = jnp.einsum("sqhd,skhd->shqk", attended_grad, values, preferred_element_type=F32)
    row_dot = jnp.sum(probs_grad * probs, axis=-1, keepdims=True)
    scores_low = (probs * (probs_grad - row_dot)).astype(BF16)
    queries_grad = jnp.einsum("shqk,skhd->sqhd", scores_low, keys, preferred_element_type=F32)
    keys_grad = jnp.einsum("shqk,sqhd->skhd", scores_low, queries, preferred_element_type=F32)
    return queries_grad, keys_grad, values_grad


def forward(plan, stream, qkv, dense, gains, scale_vec, allowed):
    width = plan.width
    head_dim = scale_vec.shape[0]
    part = qkv.shape[1] // 3
    local_heads = part // head_dim
    split = (plan.own_seqs, plan.length, local_heads, head_dim)
    out_w, up_w, down_w = dense[:, :width], dense[:, width:-width], dense[:, -width:]
    normed, factor_one = normalize(stream, gains[0])
    normed_all = gather_tokens(plan, normed.astype(BF16))
    projected = dot(normed_all, qkv)
    query_pre = projected[:, :part].reshape(split)
    queries = (query_pre * scale_vec).astype(BF16)
    keys = with_earlier(plan, projected[:, part : 2 * part].astype(BF16).reshape(split))
    values = with_earlier(plan, projected[:, 2 * part :].astype(BF16).reshape(split))
    attended_part, log_total = attend(queries, keys, values, allowed)
    attended = heads_to_tokens(plan, attended_part.astype(BF16).reshape(-1, part))
    middle = stream + dot(attended, out_w)
    normed_two, factor_two = normalize(middle, gains[1])
    normed_two = normed_two.astype(BF16)
    hidden = dot(normed_two, up_w)
    active = (hidden * jax.nn.sigmoid(hidden)).astype(BF16)
    result = middle + dot(active, down_w)
    kept = (
        stream, factor_one, normed_all, query_pre, queries, keys, values, log_total,
        attended, middle, factor_two, normed_two, hidden, active,
    )
    return result, kept


def backward(plan, upper, kept, qkv, dense, gains, scale_vec, allowed):
    (
        stream, factor_one, normed_all, query_pre, queries, keys, values, log_total,
        attended, middle, factor_two, normed_two, hidden, active,
    ) = kept
    width = plan.width
    head_dim = scale_vec.shape[0]
    part = qkv.shape[1] // 3
    out_w, up_w, down_w = dense[:, :width], dense[:, width:-width], dense[:, -width:]
    upper_low = upper.astype(BF16)
    down_grad = dot_rows(active, upper_low)
    active_grad = dot_cols(upper_low, down_w)
    gate = jax.nn.sigmoid(hidden)
    hidden_low = (active_grad * gate * (1.0 + hidden * (1.0 - gate))).astype(BF16)
    up_grad = dot_rows(normed_two, hidden_low)
    extra_two, mlp_gain_grad = norm_back(dot_cols(hidden_low, up_w), middle, factor_two, gains[1])
    middle_grad = upper + extra_two
    middle_low = middle_grad.astype(BF16)
    out_grad = dot_rows(attended, middle_low)
    dense_grad = jnp.concatenate([out_grad, up_grad, down_grad], axis=1).astype(BF16)
    dense_own = lax.psum_scatter(dense_grad, ALL, scatter_dimension=0, tiled=True)
    attended_grad = tokens_to_heads(plan, dot_cols(middle_low, out_w).astype(BF16))
    queries_grad, keys_grad, values_grad = attend_back(
        queries, keys, values, allowed, log_total, attended_grad.reshape(queries.shape)
    )
    query_bar = queries_grad.astype(BF16).astype(F32)
    scale_vec_grad = jnp.sum((query_bar * query_pre).reshape(-1, head_dim), axis=0)
    query_low = (query_bar * scale_vec).astype(BF16).reshape(-1, part)
    keys_low = to_earlier(plan, keys_grad).astype(BF16).reshape(-1, part)
    values_low = to_earlier(plan, values_grad).astype(BF16).reshape(-1, part)
    projected_low = jnp.concatenate([query_low, keys_low, values_low], axis=1)
    normed_grad = scatter_tokens(plan, dot_cols(projected_low, qkv))
    qkv_own = scatter_qkv(dot_rows(normed_all, projected_low))
    extra_one, attn_gain_grad = norm_back(normed_grad, stream, factor_one, gains[0])
    lower = middle_grad + extra_one
    return lower, qkv_own, dense_own, (attn_gain_grad, mlp_gain_grad), scale_vec_grad


def general_device(
    tokens,
    segments,
    qkv_weight,
    out_weight,
    up_weight,
    down_weight,
    attn_gain,
    mlp_gain,
    scale_param,
    cotangent,
):
    plan = Plan(tokens)
    layers, head_dim = scale_param.shape
    block_index = lax.axis_index("blk")
    scale_vecs = SCALE_BASE / math.sqrt(head_dim) * jax.nn.softplus(scale_param)
    own_gains = jnp.concatenate([attn_gain, mlp_gain], axis=0)
    gains = (
        lax.all_gather(own_gains.reshape(1, -1), ALL, axis=0, tiled=True)
        .reshape(-1, 2 * layers, attn_gain.shape[1])
        .transpose(1, 0, 2)
        .reshape(2 * layers, plan.width)
        .astype(F32)
    )
    if plan.whole:
        segments = lax.dynamic_slice_in_dim(
            segments, block_index * plan.own_seqs, plan.own_seqs, 0
        )
    allowed = window_mask(plan, segments, block_index)
    stream = to_plan(plan, tokens).astype(F32)
    qkvs, denses, kept = [], [], []
    for layer in range(layers):
        qkvs.append(gather_qkv(qkv_weight[layer]))
        own = jnp.concatenate([out_weight[layer], up_weight[layer], down_weight[layer]], axis=1)
        denses.append(lax.all_gather(own, ALL, axis=0, tiled=True))
        layer_gains = (gains[layer], gains[layers + layer])
        stream, saved = forward(
            plan, stream, qkvs[layer], denses[layer], layer_gains, scale_vecs[layer], allowed
        )
        kept.append(saved)
    layer_out = from_plan(plan, stream.astype(BF16))
    upper = to_plan(plan, cotangent).astype(F32)
    qkv_grads, dense_grads = [None] * layers, [None] * layers
    gain_grads, scale_grads = [None] * layers, [None] * layers
    for layer in reversed(range(layers)):
        layer_gains = (gains[layer], gains[layers + layer])
        upper, qkv_grads[layer], dense_grads[layer], gain_grads[layer], scale_grads[layer] = (
            backward(
                plan, upper, kept[layer], qkvs[layer], denses[layer], layer_gains,
                scale_vecs[layer], allowed,
            )
        )
    input_grad = from_plan(plan, upper.astype(BF16)).astype(F32)
    small = jnp.concatenate(
        [g[0] for g in gain_grads] + [g[1] for g in gain_grads] + scale_grads, axis=0
    )
    total = lax.psum(small, ALL)
    gain_total = total[: 2 * layers * plan.width].reshape(2 * layers, plan.width)
    owner = lax.axis_index(ALL)
    gain_rows = attn_gain.shape[1]
    own_total = lax.dynamic_slice_in_dim(gain_total, owner * gain_rows, gain_rows, 1)
    scale_total = total[2 * layers * plan.width :].reshape(layers, head_dim)
    scale_grad = scale_total * (SCALE_BASE / math.sqrt(head_dim)) * jax.nn.sigmoid(scale_param)
    dense_all = jnp.stack(dense_grads).astype(F32)
    width = plan.width
    return (
        layer_out,
        input_grad,
        jnp.stack(qkv_grads),
        dense_all[:, :, :width],
        dense_all[:, :, width:-width],
        dense_all[:, :, -width:],
        own_total[:layers],
        own_total[layers:],
        scale_grad,
    )


Q_ROWS = 256
KERNEL = pltpu.CompilerParams(vmem_limit_bytes=32 * 1024 * 1024)
LIGHT = pl.CostEstimate(flops=1 << 20, bytes_accessed=1 << 20, transcendentals=0)


def in_hbm(*arrays):
    return [pltpu.with_memory_space_constraint(array, pltpu.HBM) for array in arrays]


def allowed_keys(col, row, first):
    count = first + row.shape[1]
    key_place = lax.broadcasted_iota(jnp.int32, (count, row.shape[1]), 0)
    query_place = lax.broadcasted_iota(jnp.int32, (count, row.shape[1]), 1) + first
    return (col[:count] == row) & (key_place <= query_place)


def allowed_piece(col, row, start, first):
    same = col == row
    if start + col.shape[0] <= first:
        return same
    key_place = lax.broadcasted_iota(jnp.int32, same.shape, 0) + start
    return same & (key_place <= lax.broadcasted_iota(jnp.int32, same.shape, 1) + first)


def token_places(length, heads, token_rows, block_rows=Q_ROWS):
    for first in range(0, length, block_rows):
        parts = []
        for start in range(0, block_rows, token_rows):
            place = (first + start) // token_rows
            parts.append((start, place % heads, place // heads * token_rows))
        yield first, parts


FORWARD_ROWS, FORWARD_KEYS = 1024, 512


def attend_kernel(token_rows, proj_ref, scale_ref, col_ref, row_ref, out_ref, lse_ref):
    length = proj_ref.shape[-1]
    queries = (proj_ref[0, 0] * scale_ref[...]).astype(BF16)
    keys = proj_ref[1, 0].T.astype(BF16)
    values = proj_ref[2, 0].astype(BF16)
    for first, parts in token_places(length, out_ref.shape[0], token_rows, FORWARD_ROWS):
        end = first + FORWARD_ROWS
        block, row = queries[:, first:end], row_ref[:, first:end]
        pieces = []
        for start in range(0, end, FORWARD_KEYS):
            scores = jnp.dot(keys[start : start + FORWARD_KEYS], block, preferred_element_type=F32)
            allowed = allowed_piece(col_ref[start : start + FORWARD_KEYS], row, start, first)
            pieces.append(jnp.where(allowed, scores, MASKED_SCORE))
        top = functools.reduce(
            jnp.maximum, [jnp.max(piece, axis=0, keepdims=True) for piece in pieces]
        )
        total, attended = 0.0, 0.0
        for i, piece in enumerate(pieces):
            terms = jnp.exp(piece - top)
            total += jnp.sum(terms, axis=0, keepdims=True)
            attended += jnp.dot(
                values[:, i * FORWARD_KEYS : (i + 1) * FORWARD_KEYS],
                terms.astype(BF16),
                preferred_element_type=F32,
            )
        attended = (attended * (1.0 / total)).astype(BF16)
        lse_ref[0, :, first:end] = top + jnp.log(total)
        for start, owner, offset in parts:
            out_ref[owner, 0, :, offset : offset + token_rows] = attended[
                :, start : start + token_rows
            ]


def attend_rows(projected, scale_vec, segments, owners, token_rows):
    head_dim = scale_vec.shape[0]
    length = projected.shape[1]
    local_heads = projected.shape[0] // 3 // head_dim
    tokens = length // owners
    attended, log_total = pl.pallas_call(
        functools.partial(attend_kernel, token_rows),
        grid=(local_heads,),
        in_specs=[
            pl.BlockSpec((3, 1, head_dim, length), lambda h: (0, h, 0, 0)),
            pl.BlockSpec((head_dim, 1), lambda h: (0, 0)),
            pl.BlockSpec((length, 1), lambda h: (0, 0)),
            pl.BlockSpec((1, length), lambda h: (0, 0)),
        ],
        out_specs=[
            pl.BlockSpec((owners, 1, head_dim, tokens), lambda h: (0, h, 0, 0)),
            pl.BlockSpec((1, 1, length), lambda h: (h, 0, 0)),
        ],
        out_shape=[
            jax.ShapeDtypeStruct((owners, local_heads, head_dim, tokens), BF16),
            jax.ShapeDtypeStruct((local_heads, 1, length), F32),
        ],
        compiler_params=KERNEL,
        cost_estimate=LIGHT,
    )(
        projected.reshape(3, local_heads, head_dim, length),
        scale_vec.reshape(head_dim, 1),
        segments.reshape(length, 1),
        segments.reshape(1, length),
    )
    return attended.reshape(owners, local_heads * head_dim, tokens), log_total


def attend_back_kernel(
    token_rows,
    proj_ref,
    grad_ref,
    lse_ref,
    scale_ref,
    col_ref,
    row_ref,
    out_ref,
    scale_grad_ref,
    keys_acc,
    values_acc,
):
    length = proj_ref.shape[-1]
    scale = scale_ref[...]
    query_pre = proj_ref[0, 0]
    queries = (query_pre * scale).astype(BF16)
    keys_t = proj_ref[1, 0].astype(BF16)
    keys = proj_ref[1, 0].T.astype(BF16)
    values = proj_ref[2, 0].T.astype(BF16)
    keys_acc[...] = jnp.zeros_like(keys_acc)
    values_acc[...] = jnp.zeros_like(values_acc)
    scale_grad = jnp.zeros((scale.shape[0], 1), F32)
    for first, parts in token_places(length, grad_ref.shape[0], token_rows):
        end = first + Q_ROWS
        block = queries[:, first:end]
        grad = jnp.concatenate(
            [grad_ref[owner, 0, :, at : at + token_rows] for _, owner, at in parts], axis=1
        )
        scores = jnp.dot(keys[:end], block, preferred_element_type=F32)
        allowed = allowed_keys(col_ref[...], row_ref[:, first:end], first)
        scores = jnp.where(allowed, scores, MASKED_SCORE)
        probs = jnp.exp(scores - lse_ref[0, :, first:end])
        probs_grad = jnp.dot(values[:end], grad, preferred_element_type=F32)
        row_dot = jnp.sum(probs_grad * probs, axis=0, keepdims=True)
        scores_low = (probs * (probs_grad - row_dot)).astype(BF16)
        values_acc[:, :end] += lax.dot_general(
            grad, probs.astype(BF16), NT, preferred_element_type=F32
        )
        keys_acc[:, :end] += lax.dot_general(
            block, scores_low, NT, preferred_element_type=F32
        )
        query_bar = jnp.dot(keys_t[:, :end], scores_low, preferred_element_type=F32)
        query_bar = query_bar.astype(BF16).astype(F32)
        scale_grad += jnp.sum(query_bar * query_pre[:, first:end], axis=1, keepdims=True)
        out_ref[0, 0, :, first:end] = (query_bar * scale).astype(BF16)
    out_ref[1, 0] = keys_acc[...].astype(BF16)
    out_ref[2, 0] = values_acc[...].astype(BF16)
    spread = jnp.broadcast_to(scale_grad, scale_grad_ref.shape)

    @pl.when(pl.program_id(0) == 0)
    def _():
        scale_grad_ref[...] = spread

    @pl.when(pl.program_id(0) > 0)
    def _():
        scale_grad_ref[...] += spread


def attend_back_rows(projected, attended_grad, log_total, scale_vec, segments, token_rows):
    head_dim = scale_vec.shape[0]
    length = projected.shape[1]
    local_heads = projected.shape[0] // 3 // head_dim
    owners, _, tokens = attended_grad.shape
    lanes = 128
    grads, scale_grad = pl.pallas_call(
        functools.partial(attend_back_kernel, token_rows),
        grid=(local_heads,),
        in_specs=[
            pl.BlockSpec((3, 1, head_dim, length), lambda h: (0, h, 0, 0)),
            pl.BlockSpec((owners, 1, head_dim, tokens), lambda h: (0, h, 0, 0)),
            pl.BlockSpec((1, 1, length), lambda h: (h, 0, 0)),
            pl.BlockSpec((head_dim, 1), lambda h: (0, 0)),
            pl.BlockSpec((length, 1), lambda h: (0, 0)),
            pl.BlockSpec((1, length), lambda h: (0, 0)),
        ],
        out_specs=[
            pl.BlockSpec((3, 1, head_dim, length), lambda h: (0, h, 0, 0)),
            pl.BlockSpec((head_dim, lanes), lambda h: (0, 0)),
        ],
        out_shape=[
            pltpu.HBM((3, local_heads, head_dim, length), BF16),
            pltpu.HBM((head_dim, lanes), F32),
        ],
        scratch_shapes=[
            pltpu.VMEM((head_dim, length), F32),
            pltpu.VMEM((head_dim, length), F32),
        ],
        compiler_params=KERNEL,
        cost_estimate=LIGHT,
    )(
        *in_hbm(
            projected.reshape(3, local_heads, head_dim, length),
            attended_grad.reshape(owners, local_heads, head_dim, tokens),
        ),
        log_total,
        scale_vec.reshape(head_dim, 1),
        segments.reshape(length, 1),
        segments.reshape(1, length),
    )
    return grads.reshape(3 * local_heads * head_dim, length), scale_grad[:, 0]


def dense_grad_kernel(
    core_ref, attended_ref, normed_ref, active_ref, out_bar, up_bar, down_bar,
    own_ref, other_ref, normed_t, active_t,
):
    tile = pl.program_id(0)
    rows, width = 8 * own_ref.shape[3], out_bar.shape[1]

    @pl.when(tile == 0)
    def _():
        normed_t[...] = normed_ref[...].astype(F32).T.astype(BF16)
        active_t[...] = active_ref[...].astype(F32).T.astype(BF16)

    start = pl.multiple_of(tile * rows, rows)
    first_core = core_ref[2] == 0
    lefts = (attended_ref, normed_t, active_t)
    for i, (left, right) in enumerate(zip(lefts, (out_bar, up_bar, down_bar))):
        grad = jnp.dot(left[pl.ds(start, rows), :], right[...], preferred_element_type=F32)
        grad = grad.reshape(2, 2, 2, rows // 8, width)
        one, two = grad[:, :, 0], grad[:, :, 1]
        own_ref[:, :, 0, :, i * width : (i + 1) * width] = jnp.where(
            first_core, one, two
        ).astype(BF16)
        other_ref[:, :, 0, :, i * width : (i + 1) * width] = jnp.where(
            first_core, two, one
        ).astype(BF16)


def dense_grads(attended_t, normed, active, out_bar, up_bar, down_bar):
    width, tokens = attended_t.shape
    own = width // 32
    whole = pl.BlockSpec((tokens, width), lambda i, core: (0, 0))
    rows = pl.BlockSpec((2, 2, 1, own, 3 * width), lambda i, core: (0, 0, i, 0, 0))
    shape = pltpu.HBM((2, 2, 4, own, 3 * width), BF16)
    return pl.pallas_call(
        dense_grad_kernel,
        grid_spec=pltpu.PrefetchScalarGridSpec(
            num_scalar_prefetch=1,
            grid=(4,),
            in_specs=[pl.BlockSpec((width, tokens), lambda i, core: (0, 0))] + [whole] * 5,
            out_specs=[rows, rows],
            scratch_shapes=[pltpu.VMEM((width, tokens), BF16)] * 2,
        ),
        out_shape=[shape, shape],
        compiler_params=KERNEL,
        cost_estimate=LIGHT,
    )(place(), *in_hbm(attended_t, normed, active, out_bar, up_bar, down_bar))


def place():
    head = lax.axis_index("head")
    return jnp.stack([lax.axis_index("blk"), head // 2, head % 2]).astype(jnp.int32)


def assemble_kernel(place_ref, *refs):
    pieces, whole_ref = refs[:10], refs[10]
    half = whole_ref.shape[-1] // 2
    blk, row, core = place_ref[0], place_ref[1], place_ref[2]
    for i in range(2):
        at_core = core if i == 0 else 1 - core
        own, across, beside, one, two = pieces[5 * i : 5 * i + 5]
        whole_ref[0, blk, row, at_core] = own[0]
        whole_ref[0, 1 - blk, row, at_core] = across[0]
        whole_ref[0, blk, 1 - row, at_core] = beside[0]
        whole_ref[0, 1 - blk, 1 - row, at_core, :, :half] = one[0]
        whole_ref[0, 1 - blk, 1 - row, at_core, :, half:] = two[0]


def assemble(pieces):
    batch, own, columns = pieces[0].shape
    specs = [
        pl.BlockSpec((1, own, piece.shape[-1]), lambda i, at: (i, 0, 0))
        for piece in pieces
    ]
    whole = pl.pallas_call(
        assemble_kernel,
        grid_spec=pltpu.PrefetchScalarGridSpec(
            num_scalar_prefetch=1,
            grid=(batch,),
            in_specs=specs,
            out_specs=pl.BlockSpec((1, 2, 2, 2, own, columns), lambda i, at: (i, 0, 0, 0, 0, 0)),
        ),
        out_shape=jax.ShapeDtypeStruct((batch, 2, 2, 2, own, columns), BF16),
        compiler_params=KERNEL,
        cost_estimate=LIGHT,
    )(place(), *pieces)
    return whole.reshape(-1, columns)


def assemble_columns_kernel(place_ref, along_ref, across_ref, whole_ref, *extra_ref):
    blk = place_ref[0]
    columns = whole_ref.shape[-1]
    whole_ref[0, blk] = along_ref[0, :, :columns]
    whole_ref[0, 1 - blk] = across_ref[0, :, :columns]
    for extra in extra_ref:
        extra[0, blk] = along_ref[0, :, columns:]
        extra[0, 1 - blk] = across_ref[0, :, columns:]


def assemble_columns(along, across, columns):
    batch, own, both = along.shape
    rows = pl.BlockSpec((1, own, both), lambda i, at: (i, 0, 0))
    shapes = [(batch, 2, own, columns)]
    if both > columns:
        shapes.append((batch, 2, own, both - columns))
    parts = pl.pallas_call(
        assemble_columns_kernel,
        grid_spec=pltpu.PrefetchScalarGridSpec(
            num_scalar_prefetch=1,
            grid=(batch,),
            in_specs=[rows, rows],
            out_specs=[pl.BlockSpec((1,) + s[1:], lambda i, at: (i, 0, 0, 0)) for s in shapes],
        ),
        out_shape=[pltpu.HBM(s, BF16) for s in shapes],
        compiler_params=KERNEL,
        cost_estimate=LIGHT,
    )(place(), *in_hbm(along, across))
    return [part.reshape(-1, part.shape[-1]) for part in parts]


def assemble_wide_kernel(place_ref, along_ref, across_ref, whole_ref):
    blk = place_ref[0]
    own, columns = along_ref.shape[1], whole_ref.shape[-1]
    for i in range(along_ref.shape[-1] // columns):
        place, part = slice(i * own, (i + 1) * own), slice(i * columns, (i + 1) * columns)
        whole_ref[0, blk, place, :] = along_ref[0, :, part]
        whole_ref[0, 1 - blk, place, :] = across_ref[0, :, part]


def assemble_wide(along, across, columns):
    batch, own, wide = along.shape
    rows = own * (wide // columns)
    piece = pl.BlockSpec((1, own, wide), lambda i, at: (i, 0, 0))
    whole = pl.pallas_call(
        assemble_wide_kernel,
        grid_spec=pltpu.PrefetchScalarGridSpec(
            num_scalar_prefetch=1,
            grid=(batch,),
            in_specs=[piece, piece],
            out_specs=pl.BlockSpec((1, 2, rows, columns), lambda i, at: (i, 0, 0, 0)),
        ),
        out_shape=pltpu.HBM((batch, 2, rows, columns), BF16),
        compiler_params=KERNEL,
        cost_estimate=LIGHT,
    )(place(), *in_hbm(along, across))
    return whole.reshape(-1, columns)


def project_kernel(with_norm, place_ref, *refs):
    pieces, (gain_ref, weight_ref, normed_ref, projected_ref) = refs[:4], refs[4:]
    head = place_ref[1] * 2 + place_ref[2]
    rows = pieces[0].shape[0]
    for i, piece in enumerate(pieces):
        value = piece[...]
        if with_norm:
            stream = value.astype(F32)
            factor = lax.rsqrt(jnp.mean(stream * stream, axis=-1, keepdims=True) + EPSILON)
            value = (stream * factor * gain_ref[...]).astype(BF16)
        normed_ref[pl.ds(pl.multiple_of((head ^ i) * rows, rows), rows), :] = value
    projected = jnp.dot(normed_ref[...], weight_ref[...], preferred_element_type=F32)
    projected_ref[...] = projected.T


def project(pieces, gain, weight, with_norm, token_rows):
    tokens, width = pieces[0].shape
    length, columns = 4 * tokens, weight.shape[1]
    groups = tokens // token_rows
    piece = pl.BlockSpec((token_rows, width), lambda g, at: (g, 0))
    return pl.pallas_call(
        functools.partial(project_kernel, with_norm),
        grid_spec=pltpu.PrefetchScalarGridSpec(
            num_scalar_prefetch=1,
            grid=(groups,),
            in_specs=[piece] * 4
            + [
                pl.BlockSpec((1, width), lambda g, at: (0, 0)),
                pl.BlockSpec((width, columns), lambda g, at: (0, 0)),
            ],
            out_specs=[
                pl.BlockSpec((4 * token_rows, width), lambda g, at: (g, 0)),
                pl.BlockSpec((columns, 4 * token_rows), lambda g, at: (0, g)),
            ],
        ),
        out_shape=[
            pltpu.HBM((length, width), BF16),
            jax.ShapeDtypeStruct((columns, length), F32),
        ],
        compiler_params=KERNEL,
        cost_estimate=LIGHT,
    )(place(), *in_hbm(*pieces), gain.reshape(1, width), *in_hbm(weight))


def project_back_kernel(
    place_ref, bars_ref, weight_ref, normed_ref, own_ref, other_ref, grad_ref, bars_t
):
    @pl.when(pl.program_id(0) == 0)
    def _():
        bars_t[...] = bars_ref[...].astype(F32).T.astype(BF16)

    upper = lax.dot_general(bars_t[...], weight_ref[...], NT, preferred_element_type=F32)
    upper = upper.reshape(2, 2, 2, -1, upper.shape[-1])
    first_core = place_ref[2] == 0
    one, two = upper[:, :, 0], upper[:, :, 1]
    own_ref[...] = jnp.where(first_core, one, two)
    other_ref[...] = jnp.where(first_core, two, one).astype(BF16)
    grad = lax.dot_general(normed_ref[...], bars_t[...], TN, preferred_element_type=F32)
    grad_ref[...] = grad.astype(BF16)


def project_back(bars, weight, normed, token_rows):
    columns, length = bars.shape
    width = weight.shape[0]
    tile = width // 2
    quarter = pl.BlockSpec((2, 2, token_rows, tile), lambda i, at: (0, 0, 0, i))
    return pl.pallas_call(
        project_back_kernel,
        grid_spec=pltpu.PrefetchScalarGridSpec(
            num_scalar_prefetch=1,
            grid=(2,),
            in_specs=[
                pl.BlockSpec((columns, length), lambda i, at: (0, 0)),
                pl.BlockSpec((tile, columns), lambda i, at: (i, 0)),
                pl.BlockSpec((length, tile), lambda i, at: (0, i)),
            ],
            out_specs=[quarter, quarter, pl.BlockSpec((tile, columns), lambda i, at: (i, 0))],
            scratch_shapes=[pltpu.VMEM((length, columns), BF16)],
        ),
        out_shape=[
            pltpu.HBM((2, 2, token_rows, width), F32),
            pltpu.HBM((2, 2, token_rows, width), BF16),
            pltpu.HBM((width, columns), BF16),
        ],
        compiler_params=KERNEL,
        cost_estimate=LIGHT,
    )(place(), *in_hbm(bars, weight, normed))


def rows_back_kernel(place_ref, bars_ref, weight_ref, own_ref, other_ref, bars_t):
    @pl.when(pl.program_id(0) == 0)
    def _():
        bars_t[...] = bars_ref[...].astype(F32).T.astype(BF16)

    upper = lax.dot_general(bars_t[...], weight_ref[...], NT, preferred_element_type=F32)
    upper = upper.reshape(2, 2, 2, -1, upper.shape[-1])
    first_core = place_ref[2] == 0
    one, two = upper[:, :, 0], upper[:, :, 1]
    own_ref[...] = jnp.where(first_core, one, two)
    other_ref[...] = jnp.where(first_core, two, one).astype(BF16)


def rows_back(bars, weight, token_rows):
    columns, length = bars.shape
    width = weight.shape[0]
    tile = width // 2
    quarter = pl.BlockSpec((2, 2, token_rows, tile), lambda i, at: (0, 0, 0, i))
    return pl.pallas_call(
        rows_back_kernel,
        grid_spec=pltpu.PrefetchScalarGridSpec(
            num_scalar_prefetch=1,
            grid=(2,),
            in_specs=[
                pl.BlockSpec((columns, length), lambda i, at: (0, 0)),
                pl.BlockSpec((tile, columns), lambda i, at: (i, 0)),
            ],
            out_specs=[quarter, quarter],
            scratch_shapes=[pltpu.VMEM((length, columns), BF16)],
        ),
        out_shape=[
            pltpu.HBM((2, 2, token_rows, width), F32),
            pltpu.HBM((2, 2, token_rows, width), BF16),
        ],
        compiler_params=KERNEL,
        cost_estimate=LIGHT,
    )(place(), *in_hbm(bars, weight))


def weight_back_kernel(bars_ref, normed_ref, grad_ref):
    grad = jnp.dot(bars_ref[...], normed_ref[...], preferred_element_type=F32)
    grad_ref[...] = grad.T.astype(BF16)


def weight_back(bars, normed):
    columns, length = bars.shape
    width = normed.shape[1]
    tile = width // 5
    return pl.pallas_call(
        weight_back_kernel,
        grid=(5,),
        in_specs=[
            pl.BlockSpec((columns, length), lambda i: (0, 0)),
            pl.BlockSpec((length, tile), lambda i: (0, i)),
        ],
        out_specs=pl.BlockSpec((tile, columns), lambda i: (i, 0)),
        out_shape=pltpu.HBM((width, columns), BF16),
        compiler_params=KERNEL,
        cost_estimate=LIGHT,
    )(*in_hbm(bars, normed))


def tied(*arrays):
    return lax.optimization_barrier(arrays)


def swapped(array, axis, mask):
    size = lax.axis_size(axis)
    return lax.ppermute(array, axis, [(i, i ^ mask) for i in range(size)])


def pick(array, index, axis=0):
    return lax.dynamic_index_in_dim(array, index, axis, keepdims=False)


def swap_halves(array):
    me = lax.axis_index("blk")
    got = swapped(pick(array, 1 - me), "blk", 1)
    kept = pick(array, me)
    return jnp.stack([jnp.where(me == 0, kept, got), jnp.where(me == 0, got, kept)])


def scatter_row(halves):
    row = lax.axis_index("head") // 2
    got = swapped(pick(halves, 1 - row, 1).astype(BF16), "head", 2).astype(F32)
    return (pick(halves, row, 1) + got).reshape(-1, halves.shape[-1])


def over_head(parts):
    return lax.all_to_all(parts, "head", split_axis=0, concat_axis=0, tiled=True)


def qkv_columns(rows, extra):
    own, width = rows.shape
    part = width // 3 // 4
    sent = rows.reshape(own, 3, 4, part).transpose(2, 0, 1, 3).reshape(4, own, 3 * part)
    if extra is not None:
        sent = jnp.concatenate([sent, jnp.broadcast_to(extra[None], (4,) + extra.shape)], axis=2)
    return over_head(sent)


def along_batch(piece):
    return lax.all_gather(piece, "batch", axis=0, tiled=False)


def other_core(array):
    return swapped(array, "head", 1)


def to_beside(across):
    return swapped(across[..., : across.shape[-1] // 2], "head", 2)


def to_across(beside):
    return swapped(beside[..., beside.shape[-1] // 2 :], "blk", 1)


def over_batch(parts):
    return lax.psum_scatter(parts.astype(BF16), "batch", scatter_dimension=0, tiled=False)


def across_sum(halves):
    blk = lax.axis_index("blk")
    got = swapped(pick(halves, 1 - blk), "blk", 1).astype(F32)
    return (pick(halves, blk).astype(F32) + got).astype(BF16)


def columns_to_rows(moved):
    rows = moved.shape[1]
    return moved.reshape(4, rows, 3, -1).transpose(1, 2, 0, 3).reshape(rows, -1).astype(F32)


def quarter(parts, blk, row):
    one, two = (pick(pick(part, blk), row).astype(F32) for part in parts)
    return one + two


def diagonal_rows(parts):
    blk, row = place()[:2]
    rows = quarter(parts, 1 - blk, 1 - row).astype(BF16)
    half = rows.shape[-1] // 2
    return rows[..., :half], rows[..., half:]


def neighbour_rows(parts, one, two):
    blk, row = place()[:2]
    half = one.shape[-1]
    across, beside = quarter(parts, 1 - blk, row), quarter(parts, blk, 1 - row)
    across = jnp.concatenate([across[..., :half], across[..., half:] + two.astype(F32)], axis=-1)
    beside = jnp.concatenate([beside[..., :half] + one.astype(F32), beside[..., half:]], axis=-1)
    return across.astype(BF16), beside.astype(BF16)


def sent_beside_and_across(across, beside):
    return swapped(across, "blk", 1), swapped(beside, "head", 2)


def heads_grad(weight, out_bar):
    return dot_cols(weight, out_bar).astype(BF16).reshape(4, -1, out_bar.shape[0])


def own_quarter(parts):
    blk, row = place()[:2]
    return quarter(parts, blk, row)


def own_sum(own, *more):
    return sum((part.astype(F32) for part in more), own).astype(BF16)


def sum_over(array, *hops):
    for axis, mask in hops:
        array = array + swapped(array, axis, mask)
    return array


def gain_back(weight, weight_grad, gain):
    return jnp.sum(weight.astype(F32) * weight_grad, axis=-1) / gain.astype(F32)


def lower_of(upper, stream, factor, gain):
    return norm_back(upper, stream, factor, gain)[0]


def spread_device(
    tokens,
    segments,
    qkv_weight,
    out_weight,
    up_weight,
    down_weight,
    attn_gain,
    mlp_gain,
    scale_param,
    cotangent,
):
    layers, head_dim = scale_param.shape
    _, token_rows, width = tokens.shape
    scale_vecs = SCALE_BASE / math.sqrt(head_dim) * jax.nn.softplus(scale_param)
    segments = pick(segments, lax.axis_index("blk"))
    own_gains = jnp.concatenate([attn_gain, mlp_gain], axis=0)

    part3 = 3 * width // 4
    dense_own = [
        jnp.concatenate([out_weight[i], up_weight[i], down_weight[i]], axis=1) for i in (0, 1)
    ]

    first = swap_halves(tokens).reshape(-1, width)
    columns = qkv_columns(qkv_weight[0], own_gains.T)
    columns, first, cotangent = tied(columns.reshape(-1, columns.shape[-1]), first, cotangent)
    stream = first.astype(F32)
    along = along_batch(columns)
    far, near = swapped(first, "head", 2), other_core(first)
    both = other_core(far)
    upper = swap_halves(cotangent)
    along, near, far, both, dense_near, upper = tied(
        along, near, far, both, dense_own[0], upper
    )
    token_pieces = (first, near, far, both)
    dense_near = along_batch(dense_near)
    qkv_across = swapped(along, "blk", 1)
    next_columns = jnp.concatenate(list(qkv_columns(qkv_weight[1], None)), axis=1)
    qkv_across, dense_near, next_columns = tied(qkv_across, dense_near, next_columns)
    across, beside = swapped(dense_near, "blk", 1), swapped(dense_near, "head", 2)
    next_both = along_batch(jnp.stack([next_columns, dense_own[1]]))
    weight, gains = assemble_columns(along, qkv_across, part3)
    qkvs = [weight]
    gains = gains.T.astype(F32)

    kept, denses = [], []
    for layer in range(layers):
        normed, factor_one = normalize(stream, gains[layer])
        if layer == 1:
            normed = normed.astype(BF16)
            far, near = swapped(normed, "head", 2), other_core(normed)
            far, next_across, dense_next = tied(far, next_across, dense_next)
            across, beside = swapped(dense_next, "blk", 1), swapped(dense_next, "head", 2)
            token_pieces = (normed, near, far, other_core(far))
            qkvs.append(assemble_wide(next_along, next_across, part3))
        normed_all, projected = project(
            token_pieces, gains[layer], qkvs[layer], layer == 0, token_rows
        )
        attended, log_total = attend_rows(
            projected, scale_vecs[layer], segments, 4, token_rows
        )
        attended_t, across, beside = tied(over_head(attended), across, beside)
        one, two = to_beside(across), to_across(beside)
        if layer == 0:
            two, next_both = tied(two, next_both)
            next_along, dense_next = next_both[:, 0], next_both[:, 1]
            next_across = swapped(next_along, "blk", 1)
        else:
            dense_near = dense_next
        pieces = (dense_near, across, beside, one, two)
        pieces += tuple(other_core(piece) for piece in pieces)
        attended_t = attended_t.reshape(width, -1)
        denses.append(assemble(pieces))
        dense = denses[layer]
        out_w, up_w, down_w = dense[:, :width], dense[:, width:-width], dense[:, -width:]
        middle = stream + dot_rows(attended_t, out_w)
        normed_two, factor_two = normalize(middle, gains[layers + layer])
        normed_two = normed_two.astype(BF16)
        hidden = dot(normed_two, up_w)
        active = (hidden * jax.nn.sigmoid(hidden)).astype(BF16)
        kept.append(
            (
                stream, factor_one, normed_all, projected, log_total, attended_t, middle,
                factor_two, normed_two, hidden, active,
            )
        )
        stream = middle + dot(active, down_w)
    layer_out = swap_halves(stream.astype(BF16).reshape(tokens.shape))
    upper = upper.reshape(-1, width).astype(F32)

    scale_grads = [None] * layers
    for layer in reversed(range(layers)):
        (
            stream, factor_one, normed_all, projected, log_total, attended_t, middle,
            factor_two, normed_two, hidden, active,
        ) = kept[layer]
        qkv, dense = qkvs[layer], denses[layer]
        out_w, up_w, down_w = dense[:, :width], dense[:, width:-width], dense[:, -width:]
        down_bar = upper.astype(BF16)
        gate = jax.nn.sigmoid(hidden)
        up_bar = (
            dot_cols(down_bar, down_w) * gate * (1.0 + hidden * (1.0 - gate))
        ).astype(BF16)
        middle_grad = upper + lower_of(
            dot_cols(up_bar, up_w), middle, factor_two, gains[layers + layer]
        )
        out_bar = middle_grad.astype(BF16)
        if layer == 0:
            attended_grad = over_head(heads_grad(out_w, out_bar))
            grads, others = dense_grads(attended_t, normed_two, active, out_bar, up_bar, down_bar)
            others, across = tied(others, across)
            others, own = tied(others, own_quarter(cored) + across.astype(F32))
            attended_grad, others, z_sum, beside = tied(attended_grad, others, z_sum, beside)
            others = other_core(others)
            attended_grad, summed = tied(attended_grad, own_sum(own, beside))
            summed = over_batch(summed)
            earlier = across_sum(z_sum)
        else:
            attended_grad = over_head(heads_grad(out_w, out_bar))
            grads, others = dense_grads(attended_t, normed_two, active, out_bar, up_bar, down_bar)
            attended_grad, others, layer_out = tied(attended_grad, others, layer_out)
            others = other_core(others)
        bars, scale_grads[layer] = attend_back_rows(
            projected, attended_grad, log_total, scale_vecs[layer], segments, token_rows
        )
        if layer == 0:
            bars, earlier = tied(bars, earlier)
            qkv_grad = weight_back(bars, normed_all)
            bars, qkv_grad, others = tied(bars, qkv_grad, others)
            z_sum = over_batch(qkv_grad.reshape(4, 2, -1, qkv_grad.shape[-1]))
            cored = (grads, others)
            bars, rows = tied(bars, diagonal_rows(cored))
            diagonal = sent_beside_and_across(*rows)
            halves, to_core = rows_back(bars, qkv, token_rows)
            scale_sum = sum_over(jnp.stack(scale_grads), ("head", 1))
            halves, to_core, diagonal, summed, scale_sum = tied(
                halves, to_core, diagonal, summed, scale_sum
            )
            scale_sum = sum_over(scale_sum, ("head", 2))
            halves, to_core, rows, scale_sum = tied(
                halves, to_core, neighbour_rows(cored, *diagonal), scale_sum
            )
            sent = sent_beside_and_across(*rows)
            halves = halves + other_core(to_core).astype(F32)
            scale_sum = sum_over(scale_sum, ("batch", 1), ("batch", 2), ("blk", 1))
            own = own_quarter(cored)
            halves, sent, z_sum, scale_sum, own = tied(halves, sent, z_sum, scale_sum, own)
            halves, own, earlier = tied(halves, own_sum(own, *sent), earlier)
            moved = over_head(earlier.reshape(4, -1, earlier.shape[-1]))
            dense_first = over_batch(own)
            normed_grad = scatter_row(halves)
            z_across, dense_first = tied(across_sum(z_sum), dense_first)
            z_across = over_head(z_across.reshape(4, -1, z_across.shape[-1]))
            dense_grad = [dense_first, summed]
            qkv_grads = [columns_to_rows(z_across), columns_to_rows(moved)]
        else:
            bars, others = tied(bars, others)
            cored = (grads, others)
            bars, rows = tied(bars, diagonal_rows(cored))
            diagonal = sent_beside_and_across(*rows)
            halves, to_core, qkv_grad = project_back(bars, qkv, normed_all, token_rows)
            z_sum = over_batch(qkv_grad.reshape(4, 2, -1, qkv_grad.shape[-1]))
            to_core, halves, diagonal = tied(to_core, halves, diagonal)
            to_core, rows = tied(to_core, neighbour_rows(cored, *diagonal))
            across = swapped(rows[0], "blk", 1)
            halves = halves + other_core(to_core).astype(F32)
            normed_grad = scatter_row(halves)
            normed_grad, beside = tied(normed_grad, rows[1])
            beside = swapped(beside, "head", 2)
        upper = middle_grad + lower_of(normed_grad, stream, factor_one, gains[layer])
    input_grad = swap_halves(upper.astype(BF16).reshape(tokens.shape)).astype(F32)
    scale_grad = scale_sum * (SCALE_BASE / math.sqrt(head_dim)) * jax.nn.sigmoid(scale_param)
    dense_all = jnp.stack([part.astype(F32) for part in dense_grad])
    qkv_all = jnp.stack(qkv_grads)
    up_all = dense_all[:, :, width:-width]
    return (
        layer_out,
        input_grad,
        qkv_all,
        dense_all[:, :, :width],
        up_all,
        dense_all[:, :, -width:],
        gain_back(qkv_weight, qkv_all, attn_gain),
        gain_back(up_weight, up_all, mlp_gain),
        scale_grad,
    )


def per_device(*args):
    tokens, segments = args[0], args[1]
    sizes = tuple(lax.axis_size(axis) for axis in ALL)
    heads = tokens.shape[2] // args[8].shape[1]
    spread = (
        sizes == (4, 2, 4)
        and tokens.shape[0] == 2
        and args[2].shape[0] == 2
        and tokens.shape[1] % 128 == 0
        and Q_ROWS % tokens.shape[1] == 0
        and segments.shape[1] <= WINDOW
        and segments.shape[1] % FORWARD_ROWS == 0
        and heads % 4 == 0
        and tokens.shape[2] % 256 == 0
    )
    return spread_device(*args) if spread else general_device(*args)


def solution(mesh):
    rows = P(None, ALL, None)
    by_token = P("batch", ("blk", "head"), None)
    return jax.shard_map(
        per_device,
        mesh=mesh,
        in_specs=(
            by_token, P("batch", None), rows, rows, rows, rows, P(None, ALL), P(None, ALL), P(),
            by_token,
        ),
        out_specs=(
            by_token, by_token, rows, rows, rows, rows, P(None, ALL), P(None, ALL), P(),
        ),
        check_vma=False,
    )
```

```python
import functools
import math

import jax
import jax.numpy as jnp
from jax import lax
from jax.experimental import pallas as pl
from jax.experimental.pallas import tpu as pltpu
from jax.sharding import PartitionSpec as P

WINDOW = 1024
EPSILON = 1e-06
SCALE_BASE = 1.4426950408889634
MASKED_SCORE = -1e30

ALL = ("batch", "blk", "head")
REST = ("batch", "blk")
F32 = jnp.float32
BF16 = jnp.bfloat16


def shifted(block, axis, distance):
    devices = range(lax.axis_size(axis))
    route = [(i - distance, i) for i in devices if i - distance in devices]
    return lax.ppermute(block, axis, route)


NT = (((1,), (1,)), ((), ()))
TN = (((0,), (0,)), ((), ()))


def dot(left, right):
    return jnp.dot(left, right, preferred_element_type=F32)


def dot_rows(left, right):
    return lax.dot_general(left, right, (((0,), (0,)), ((), ())), preferred_element_type=F32)


def dot_cols(left, right):
    return lax.dot_general(left, right, (((1,), (1,)), ((), ())), preferred_element_type=F32)


def normalize(stream, gain):
    factor = lax.rsqrt(jnp.mean(stream * stream, axis=-1, keepdims=True) + EPSILON)
    return stream * factor * gain, factor


def norm_back(upper, stream, factor, gain):
    inner = upper * gain
    gain_grad = jnp.sum(upper * stream * factor, axis=0)
    lower = factor * inner - stream * factor * factor * factor * jnp.mean(
        inner * stream, axis=-1, keepdims=True
    )
    return lower, gain_grad


class Plan:
    def __init__(self, tokens):
        self.seqs, self.rows, self.width = tokens.shape
        self.heads = lax.axis_size("head")
        self.blks = lax.axis_size("blk")
        self.block = self.rows * self.heads
        self.whole = self.seqs % self.blks == 0
        if self.whole:
            self.groups, self.own_seqs = self.blks, self.seqs // self.blks
            self.reach = 0
        else:
            self.groups, self.own_seqs = 1, self.seqs
            self.reach = min((WINDOW - 1) // self.block + 1, self.blks - 1)
        self.length = self.groups * self.block
        self.tokens = self.seqs * self.rows


def to_plan(plan, array):
    if plan.whole and plan.blks > 1:
        array = lax.all_to_all(array, "blk", split_axis=0, concat_axis=0, tiled=True)
    return array.reshape(plan.tokens, plan.width)


def from_plan(plan, flat):
    array = flat.reshape(plan.seqs, plan.rows, plan.width)
    if plan.whole and plan.blks > 1:
        array = lax.all_to_all(array, "blk", split_axis=0, concat_axis=0, tiled=True)
    return array


def in_sequence(plan, by_head, width):
    parts = by_head.reshape(plan.heads, plan.groups, plan.own_seqs, plan.rows, width)
    return parts.transpose(2, 1, 0, 3, 4).reshape(-1, width)


def by_owner(plan, rows, width):
    parts = rows.reshape(plan.own_seqs, plan.groups, plan.heads, plan.rows, width)
    return parts.transpose(2, 1, 0, 3, 4).reshape(plan.heads, plan.tokens, width)


def gather_tokens(plan, rows):
    moved = lax.all_gather(rows, "head", axis=0, tiled=False)
    return in_sequence(plan, moved, rows.shape[-1])


def scatter_tokens(plan, rows):
    width = rows.shape[-1]
    return lax.psum_scatter(
        by_owner(plan, rows.astype(BF16), width), "head", scatter_dimension=0, tiled=False
    ).astype(F32)


def heads_to_tokens(plan, rows):
    part = rows.shape[-1]
    moved = lax.all_to_all(
        by_owner(plan, rows, part), "head", split_axis=0, concat_axis=0, tiled=True
    )
    return moved.transpose(1, 0, 2).reshape(plan.tokens, plan.heads * part)


def tokens_to_heads(plan, rows):
    part = rows.shape[-1] // plan.heads
    sent = rows.reshape(plan.tokens, plan.heads, part).transpose(1, 0, 2)
    moved = lax.all_to_all(sent, "head", split_axis=0, concat_axis=0, tiled=True)
    return in_sequence(plan, moved, part)


def gather_qkv(rows):
    own, width = rows.shape
    heads = lax.axis_size("head")
    part = width // 3 // heads
    sent = rows.reshape(own, 3, heads, part).transpose(2, 0, 1, 3).reshape(heads, own, 3 * part)
    moved = lax.all_to_all(sent, "head", split_axis=0, concat_axis=0, tiled=True)
    full = lax.all_gather(moved, REST, axis=0, tiled=True)
    return full.reshape(-1, 3 * part)


def scatter_qkv(grad):
    heads = lax.axis_size("head")
    part = grad.shape[1] // 3
    summed = lax.psum_scatter(grad.astype(BF16), REST, scatter_dimension=0, tiled=True)
    own = summed.shape[0] // heads
    moved = lax.all_to_all(
        summed.reshape(heads, own, 3 * part), "head", split_axis=0, concat_axis=0, tiled=True
    )
    return (
        moved.reshape(heads, own, 3, part)
        .transpose(1, 2, 0, 3)
        .reshape(own, 3 * heads * part)
        .astype(F32)
    )


def window_mask(plan, segments, block_index):
    key_count = plan.length + plan.reach * plan.block
    if plan.whole:
        query_segs, key_segs = segments, segments
    else:
        leading = jnp.full((plan.own_seqs, plan.reach * plan.block), -1, jnp.int32)
        padded = jnp.concatenate([leading, segments], axis=1)
        start = block_index * plan.block
        query_segs = lax.dynamic_slice_in_dim(segments, start, plan.block, 1)
        key_segs = lax.dynamic_slice_in_dim(padded, start, key_count, 1)
    query_place = jnp.arange(plan.length, dtype=jnp.int32)[:, None] + plan.reach * plan.block
    key_place = jnp.arange(key_count, dtype=jnp.int32)[None, :]
    near = (key_place <= query_place) & (query_place - key_place < WINDOW)
    return (key_segs[:, None, :] == query_segs[:, :, None]) & near[None]


def with_earlier(plan, own):
    arrived = [own]
    for _ in range(plan.reach):
        arrived.append(shifted(arrived[-1], "blk", 1))
    return jnp.concatenate(arrived[::-1], axis=1) if plan.reach else own


def to_earlier(plan, grads):
    if not plan.reach:
        return grads
    block = plan.block
    total = grads[:, :block]
    for step in range(1, plan.reach + 1):
        total = (
            shifted(total.astype(BF16), "blk", -1).astype(F32)
            + grads[:, step * block : (step + 1) * block]
        )
    return total


def scores_of(queries, keys, allowed):
    scores = jnp.einsum("sqhd,skhd->shqk", queries, keys, preferred_element_type=F32)
    return jnp.where(allowed[:, None], scores, MASKED_SCORE)


def attend(queries, keys, values, allowed):
    scores = scores_of(queries, keys, allowed)
    top_score = jnp.max(scores, axis=-1, keepdims=True)
    exp_terms = jnp.exp(scores - top_score)
    totals = jnp.sum(exp_terms, axis=-1, keepdims=True)
    probs_low = (exp_terms / totals).astype(BF16)
    attended = jnp.einsum("shqk,skhd->sqhd", probs_low, values, preferred_element_type=F32)
    return attended, top_score + jnp.log(totals)


def attend_back(queries, keys, values, allowed, log_total, attended_grad):
    probs = jnp.exp(scores_of(queries, keys, allowed) - log_total)
    probs_low = probs.astype(BF16)
    values_grad = jnp.einsum(
        "shqk,sqhd->skhd", probs_low, attended_grad, preferred_element_type=F32
    )
    probs_grad = jnp.einsum("sqhd,skhd->shqk", attended_grad, values, preferred_element_type=F32)
    row_dot = jnp.sum(probs_grad * probs, axis=-1, keepdims=True)
    scores_low = (probs * (probs_grad - row_dot)).astype(BF16)
    queries_grad = jnp.einsum("shqk,skhd->sqhd", scores_low, keys, preferred_element_type=F32)
    keys_grad = jnp.einsum("shqk,sqhd->skhd", scores_low, queries, preferred_element_type=F32)
    return queries_grad, keys_grad, values_grad


def forward(plan, stream, qkv, dense, gains, scale_vec, allowed):
    width = plan.width
    head_dim = scale_vec.shape[0]
    part = qkv.shape[1] // 3
    local_heads = part // head_dim
    split = (plan.own_seqs, plan.length, local_heads, head_dim)
    out_w, up_w, down_w = dense[:, :width], dense[:, width:-width], dense[:, -width:]
    normed, factor_one = normalize(stream, gains[0])
    normed_all = gather_tokens(plan, normed.astype(BF16))
    projected = dot(normed_all, qkv)
    query_pre = projected[:, :part].reshape(split)
    queries = (query_pre * scale_vec).astype(BF16)
    keys = with_earlier(plan, projected[:, part : 2 * part].astype(BF16).reshape(split))
    values = with_earlier(plan, projected[:, 2 * part :].astype(BF16).reshape(split))
    attended_part, log_total = attend(queries, keys, values, allowed)
    attended = heads_to_tokens(plan, attended_part.astype(BF16).reshape(-1, part))
    middle = stream + dot(attended, out_w)
    normed_two, factor_two = normalize(middle, gains[1])
    normed_two = normed_two.astype(BF16)
    hidden = dot(normed_two, up_w)
    active = (hidden * jax.nn.sigmoid(hidden)).astype(BF16)
    result = middle + dot(active, down_w)
    kept = (
        stream, factor_one, normed_all, query_pre, queries, keys, values, log_total,
        attended, middle, factor_two, normed_two, hidden, active,
    )
    return result, kept


def backward(plan, upper, kept, qkv, dense, gains, scale_vec, allowed):
    (
        stream, factor_one, normed_all, query_pre, queries, keys, values, log_total,
        attended, middle, factor_two, normed_two, hidden, active,
    ) = kept
    width = plan.width
    head_dim = scale_vec.shape[0]
    part = qkv.shape[1] // 3
    out_w, up_w, down_w = dense[:, :width], dense[:, width:-width], dense[:, -width:]
    upper_low = upper.astype(BF16)
    down_grad = dot_rows(active, upper_low)
    active_grad = dot_cols(upper_low, down_w)
    gate = jax.nn.sigmoid(hidden)
    hidden_low = (active_grad * gate * (1.0 + hidden * (1.0 - gate))).astype(BF16)
    up_grad = dot_rows(normed_two, hidden_low)
    extra_two, mlp_gain_grad = norm_back(dot_cols(hidden_low, up_w), middle, factor_two, gains[1])
    middle_grad = upper + extra_two
    middle_low = middle_grad.astype(BF16)
    out_grad = dot_rows(attended, middle_low)
    dense_grad = jnp.concatenate([out_grad, up_grad, down_grad], axis=1).astype(BF16)
    dense_own = lax.psum_scatter(dense_grad, ALL, scatter_dimension=0, tiled=True)
    attended_grad = tokens_to_heads(plan, dot_cols(middle_low, out_w).astype(BF16))
    queries_grad, keys_grad, values_grad = attend_back(
        queries, keys, values, allowed, log_total, attended_grad.reshape(queries.shape)
    )
    query_bar = queries_grad.astype(BF16).astype(F32)
    scale_vec_grad = jnp.sum((query_bar * query_pre).reshape(-1, head_dim), axis=0)
    query_low = (query_bar * scale_vec).astype(BF16).reshape(-1, part)
    keys_low = to_earlier(plan, keys_grad).astype(BF16).reshape(-1, part)
    values_low = to_earlier(plan, values_grad).astype(BF16).reshape(-1, part)
    projected_low = jnp.concatenate([query_low, keys_low, values_low], axis=1)
    normed_grad = scatter_tokens(plan, dot_cols(projected_low, qkv))
    qkv_own = scatter_qkv(dot_rows(normed_all, projected_low))
    extra_one, attn_gain_grad = norm_back(normed_grad, stream, factor_one, gains[0])
    lower = middle_grad + extra_one
    return lower, qkv_own, dense_own, (attn_gain_grad, mlp_gain_grad), scale_vec_grad


def general_device(
    tokens,
    segments,
    qkv_weight,
    out_weight,
    up_weight,
    down_weight,
    attn_gain,
    mlp_gain,
    scale_param,
    cotangent,
):
    plan = Plan(tokens)
    layers, head_dim = scale_param.shape
    block_index = lax.axis_index("blk")
    scale_vecs = SCALE_BASE / math.sqrt(head_dim) * jax.nn.softplus(scale_param)
    own_gains = jnp.concatenate([attn_gain, mlp_gain], axis=0)
    gains = (
        lax.all_gather(own_gains.reshape(1, -1), ALL, axis=0, tiled=True)
        .reshape(-1, 2 * layers, attn_gain.shape[1])
        .transpose(1, 0, 2)
        .reshape(2 * layers, plan.width)
        .astype(F32)
    )
    if plan.whole:
        segments = lax.dynamic_slice_in_dim(
            segments, block_index * plan.own_seqs, plan.own_seqs, 0
        )
    allowed = window_mask(plan, segments, block_index)
    stream = to_plan(plan, tokens).astype(F32)
    qkvs, denses, kept = [], [], []
    for layer in range(layers):
        qkvs.append(gather_qkv(qkv_weight[layer]))
        own = jnp.concatenate([out_weight[layer], up_weight[layer], down_weight[layer]], axis=1)
        denses.append(lax.all_gather(own, ALL, axis=0, tiled=True))
        layer_gains = (gains[layer], gains[layers + layer])
        stream, saved = forward(
            plan, stream, qkvs[layer], denses[layer], layer_gains, scale_vecs[layer], allowed
        )
        kept.append(saved)
    layer_out = from_plan(plan, stream.astype(BF16))
    upper = to_plan(plan, cotangent).astype(F32)
    qkv_grads, dense_grads = [None] * layers, [None] * layers
    gain_grads, scale_grads = [None] * layers, [None] * layers
    for layer in reversed(range(layers)):
        layer_gains = (gains[layer], gains[layers + layer])
        upper, qkv_grads[layer], dense_grads[layer], gain_grads[layer], scale_grads[layer] = (
            backward(
                plan, upper, kept[layer], qkvs[layer], denses[layer], layer_gains,
                scale_vecs[layer], allowed,
            )
        )
    input_grad = from_plan(plan, upper.astype(BF16)).astype(F32)
    small = jnp.concatenate(
        [g[0] for g in gain_grads] + [g[1] for g in gain_grads] + scale_grads, axis=0
    )
    total = lax.psum(small, ALL)
    gain_total = total[: 2 * layers * plan.width].reshape(2 * layers, plan.width)
    owner = lax.axis_index(ALL)
    gain_rows = attn_gain.shape[1]
    own_total = lax.dynamic_slice_in_dim(gain_total, owner * gain_rows, gain_rows, 1)
    scale_total = total[2 * layers * plan.width :].reshape(layers, head_dim)
    scale_grad = scale_total * (SCALE_BASE / math.sqrt(head_dim)) * jax.nn.sigmoid(scale_param)
    dense_all = jnp.stack(dense_grads).astype(F32)
    width = plan.width
    return (
        layer_out,
        input_grad,
        jnp.stack(qkv_grads),
        dense_all[:, :, :width],
        dense_all[:, :, width:-width],
        dense_all[:, :, -width:],
        own_total[:layers],
        own_total[layers:],
        scale_grad,
    )


Q_ROWS = 256
KERNEL = pltpu.CompilerParams(vmem_limit_bytes=32 * 1024 * 1024)
LIGHT = pl.CostEstimate(flops=1 << 20, bytes_accessed=1 << 20, transcendentals=0)


def in_hbm(*arrays):
    return [pltpu.with_memory_space_constraint(array, pltpu.HBM) for array in arrays]


def allowed_keys(col, row, first):
    count = first + row.shape[1]
    key_place = lax.broadcasted_iota(jnp.int32, (count, row.shape[1]), 0)
    query_place = lax.broadcasted_iota(jnp.int32, (count, row.shape[1]), 1) + first
    return (col[:count] == row) & (key_place <= query_place)


def allowed_piece(col, row, start, first):
    same = col == row
    if start + col.shape[0] <= first:
        return same
    key_place = lax.broadcasted_iota(jnp.int32, same.shape, 0) + start
    return same & (key_place <= lax.broadcasted_iota(jnp.int32, same.shape, 1) + first)


def token_places(length, heads, token_rows, block_rows=Q_ROWS):
    for first in range(0, length, block_rows):
        parts = []
        for start in range(0, block_rows, token_rows):
            place = (first + start) // token_rows
            parts.append((start, place % heads, place // heads * token_rows))
        yield first, parts


FORWARD_ROWS, FORWARD_KEYS = 1024, 512


def attend_kernel(token_rows, proj_ref, scale_ref, col_ref, row_ref, out_ref, lse_ref):
    length = proj_ref.shape[-1]
    queries = (proj_ref[0, 0] * scale_ref[...]).astype(BF16)
    keys = proj_ref[1, 0].T.astype(BF16)
    values = proj_ref[2, 0].astype(BF16)
    for first, parts in token_places(length, out_ref.shape[0], token_rows, FORWARD_ROWS):
        end = first + FORWARD_ROWS
        block, row = queries[:, first:end], row_ref[:, first:end]
        pieces = []
        for start in range(0, end, FORWARD_KEYS):
            scores = jnp.dot(keys[start : start + FORWARD_KEYS], block, preferred_element_type=F32)
            allowed = allowed_piece(col_ref[start : start + FORWARD_KEYS], row, start, first)
            pieces.append(jnp.where(allowed, scores, MASKED_SCORE))
        top = functools.reduce(
            jnp.maximum, [jnp.max(piece, axis=0, keepdims=True) for piece in pieces]
        )
        total, attended = 0.0, 0.0
        for i, piece in enumerate(pieces):
            terms = jnp.exp(piece - top)
            total += jnp.sum(terms, axis=0, keepdims=True)
            attended += jnp.dot(
                values[:, i * FORWARD_KEYS : (i + 1) * FORWARD_KEYS],
                terms.astype(BF16),
                preferred_element_type=F32,
            )
        attended = (attended * (1.0 / total)).astype(BF16)
        lse_ref[0, :, first:end] = top + jnp.log(total)
        for start, owner, offset in parts:
            out_ref[owner, 0, :, offset : offset + token_rows] = attended[
                :, start : start + token_rows
            ]


def attend_rows(projected, scale_vec, segments, owners, token_rows):
    head_dim = scale_vec.shape[0]
    length = projected.shape[1]
    local_heads = projected.shape[0] // 3 // head_dim
    tokens = length // owners
    attended, log_total = pl.pallas_call(
        functools.partial(attend_kernel, token_rows),
        grid=(local_heads,),
        in_specs=[
            pl.BlockSpec((3, 1, head_dim, length), lambda h: (0, h, 0, 0)),
            pl.BlockSpec((head_dim, 1), lambda h: (0, 0)),
            pl.BlockSpec((length, 1), lambda h: (0, 0)),
            pl.BlockSpec((1, length), lambda h: (0, 0)),
        ],
        out_specs=[
            pl.BlockSpec((owners, 1, head_dim, tokens), lambda h: (0, h, 0, 0)),
            pl.BlockSpec((1, 1, length), lambda h: (h, 0, 0)),
        ],
        out_shape=[
            jax.ShapeDtypeStruct((owners, local_heads, head_dim, tokens), BF16),
            jax.ShapeDtypeStruct((local_heads, 1, length), F32),
        ],
        compiler_params=KERNEL,
        cost_estimate=LIGHT,
    )(
        projected.reshape(3, local_heads, head_dim, length),
        scale_vec.reshape(head_dim, 1),
        segments.reshape(length, 1),
        segments.reshape(1, length),
    )
    return attended.reshape(owners, local_heads * head_dim, tokens), log_total


def attend_back_kernel(
    token_rows,
    proj_ref,
    grad_ref,
    lse_ref,
    scale_ref,
    col_ref,
    row_ref,
    out_ref,
    scale_grad_ref,
    keys_acc,
    values_acc,
):
    length = proj_ref.shape[-1]
    scale = scale_ref[...]
    query_pre = proj_ref[0, 0]
    queries = (query_pre * scale).astype(BF16)
    keys_t = proj_ref[1, 0].astype(BF16)
    keys = proj_ref[1, 0].T.astype(BF16)
    values = proj_ref[2, 0].T.astype(BF16)
    keys_acc[...] = jnp.zeros_like(keys_acc)
    values_acc[...] = jnp.zeros_like(values_acc)
    scale_grad = jnp.zeros((scale.shape[0], 1), F32)
    for first, parts in token_places(length, grad_ref.shape[0], token_rows):
        end = first + Q_ROWS
        block = queries[:, first:end]
        grad = jnp.concatenate(
            [grad_ref[owner, 0, :, at : at + token_rows] for _, owner, at in parts], axis=1
        )
        scores = jnp.dot(keys[:end], block, preferred_element_type=F32)
        allowed = allowed_keys(col_ref[...], row_ref[:, first:end], first)
        scores = jnp.where(allowed, scores, MASKED_SCORE)
        probs = jnp.exp(scores - lse_ref[0, :, first:end])
        probs_grad = jnp.dot(values[:end], grad, preferred_element_type=F32)
        row_dot = jnp.sum(probs_grad * probs, axis=0, keepdims=True)
        scores_low = (probs * (probs_grad - row_dot)).astype(BF16)
        values_acc[:, :end] += lax.dot_general(
            grad, probs.astype(BF16), NT, preferred_element_type=F32
        )
        keys_acc[:, :end] += lax.dot_general(
            block, scores_low, NT, preferred_element_type=F32
        )
        query_bar = jnp.dot(keys_t[:, :end], scores_low, preferred_element_type=F32)
        query_bar = query_bar.astype(BF16).astype(F32)
        scale_grad += jnp.sum(query_bar * query_pre[:, first:end], axis=1, keepdims=True)
        out_ref[0, 0, :, first:end] = (query_bar * scale).astype(BF16)
    out_ref[1, 0] = keys_acc[...].astype(BF16)
    out_ref[2, 0] = values_acc[...].astype(BF16)
    spread = jnp.broadcast_to(scale_grad, scale_grad_ref.shape)

    @pl.when(pl.program_id(0) == 0)
    def _():
        scale_grad_ref[...] = spread

    @pl.when(pl.program_id(0) > 0)
    def _():
        scale_grad_ref[...] += spread


def attend_back_rows(projected, attended_grad, log_total, scale_vec, segments, token_rows):
    head_dim = scale_vec.shape[0]
    length = projected.shape[1]
    local_heads = projected.shape[0] // 3 // head_dim
    owners, _, tokens = attended_grad.shape
    lanes = 128
    grads, scale_grad = pl.pallas_call(
        functools.partial(attend_back_kernel, token_rows),
        grid=(local_heads,),
        in_specs=[
            pl.BlockSpec((3, 1, head_dim, length), lambda h: (0, h, 0, 0)),
            pl.BlockSpec((owners, 1, head_dim, tokens), lambda h: (0, h, 0, 0)),
            pl.BlockSpec((1, 1, length), lambda h: (h, 0, 0)),
            pl.BlockSpec((head_dim, 1), lambda h: (0, 0)),
            pl.BlockSpec((length, 1), lambda h: (0, 0)),
            pl.BlockSpec((1, length), lambda h: (0, 0)),
        ],
        out_specs=[
            pl.BlockSpec((3, 1, head_dim, length), lambda h: (0, h, 0, 0)),
            pl.BlockSpec((head_dim, lanes), lambda h: (0, 0)),
        ],
        out_shape=[
            pltpu.HBM((3, local_heads, head_dim, length), BF16),
            pltpu.HBM((head_dim, lanes), F32),
        ],
        scratch_shapes=[
            pltpu.VMEM((head_dim, length), F32),
            pltpu.VMEM((head_dim, length), F32),
        ],
        compiler_params=KERNEL,
        cost_estimate=LIGHT,
    )(
        *in_hbm(
            projected.reshape(3, local_heads, head_dim, length),
            attended_grad.reshape(owners, local_heads, head_dim, tokens),
        ),
        log_total,
        scale_vec.reshape(head_dim, 1),
        segments.reshape(length, 1),
        segments.reshape(1, length),
    )
    return grads.reshape(3 * local_heads * head_dim, length), scale_grad[:, 0]


def dense_grad_kernel(
    core_ref, attended_ref, normed_ref, active_ref, out_bar, up_bar, down_bar,
    own_ref, other_ref, normed_t, active_t,
):
    tile = pl.program_id(0)
    rows, width = 8 * own_ref.shape[3], out_bar.shape[1]

    @pl.when(tile == 0)
    def _():
        normed_t[...] = normed_ref[...].astype(F32).T.astype(BF16)
        active_t[...] = active_ref[...].astype(F32).T.astype(BF16)

    start = pl.multiple_of(tile * rows, rows)
    first_core = core_ref[2] == 0
    lefts = (attended_ref, normed_t, active_t)
    for i, (left, right) in enumerate(zip(lefts, (out_bar, up_bar, down_bar))):
        grad = jnp.dot(left[pl.ds(start, rows), :], right[...], preferred_element_type=F32)
        grad = grad.reshape(2, 2, 2, rows // 8, width)
        one, two = grad[:, :, 0], grad[:, :, 1]
        own_ref[:, :, 0, :, i * width : (i + 1) * width] = jnp.where(
            first_core, one, two
        ).astype(BF16)
        other_ref[:, :, 0, :, i * width : (i + 1) * width] = jnp.where(
            first_core, two, one
        ).astype(BF16)


def dense_grads(attended_t, normed, active, out_bar, up_bar, down_bar):
    width, tokens = attended_t.shape
    own = width // 32
    whole = pl.BlockSpec((tokens, width), lambda i, core: (0, 0))
    rows = pl.BlockSpec((2, 2, 1, own, 3 * width), lambda i, core: (0, 0, i, 0, 0))
    shape = pltpu.HBM((2, 2, 4, own, 3 * width), BF16)
    return pl.pallas_call(
        dense_grad_kernel,
        grid_spec=pltpu.PrefetchScalarGridSpec(
            num_scalar_prefetch=1,
            grid=(4,),
            in_specs=[pl.BlockSpec((width, tokens), lambda i, core: (0, 0))] + [whole] * 5,
            out_specs=[rows, rows],
            scratch_shapes=[pltpu.VMEM((width, tokens), BF16)] * 2,
        ),
        out_shape=[shape, shape],
        compiler_params=KERNEL,
        cost_estimate=LIGHT,
    )(place(), *in_hbm(attended_t, normed, active, out_bar, up_bar, down_bar))


def place():
    head = lax.axis_index("head")
    return jnp.stack([lax.axis_index("blk"), head // 2, head % 2]).astype(jnp.int32)


def assemble_kernel(place_ref, *refs):
    pieces, whole_ref = refs[:10], refs[10]
    split = pieces[3].shape[-1]
    blk, row, core = place_ref[0], place_ref[1], place_ref[2]
    for i in range(2):
        at_core = core if i == 0 else 1 - core
        own, across, beside, one, two = pieces[5 * i : 5 * i + 5]
        whole_ref[0, blk, row, at_core] = own[0]
        whole_ref[0, 1 - blk, row, at_core] = across[0]
        whole_ref[0, blk, 1 - row, at_core] = beside[0]
        whole_ref[0, 1 - blk, 1 - row, at_core, :, :split] = one[0]
        whole_ref[0, 1 - blk, 1 - row, at_core, :, split:] = two[0]


def assemble(pieces):
    batch, own, columns = pieces[0].shape
    specs = [
        pl.BlockSpec((1, own, piece.shape[-1]), lambda i, at: (i, 0, 0))
        for piece in pieces
    ]
    whole = pl.pallas_call(
        assemble_kernel,
        grid_spec=pltpu.PrefetchScalarGridSpec(
            num_scalar_prefetch=1,
            grid=(batch,),
            in_specs=specs,
            out_specs=pl.BlockSpec((1, 2, 2, 2, own, columns), lambda i, at: (i, 0, 0, 0, 0, 0)),
        ),
        out_shape=jax.ShapeDtypeStruct((batch, 2, 2, 2, own, columns), BF16),
        compiler_params=KERNEL,
        cost_estimate=LIGHT,
    )(place(), *pieces)
    return whole.reshape(-1, columns)


def assemble_columns_kernel(place_ref, along_ref, across_ref, whole_ref, *extra_ref):
    blk = place_ref[0]
    columns = whole_ref.shape[-1]
    whole_ref[0, blk] = along_ref[0, :, :columns]
    whole_ref[0, 1 - blk] = across_ref[0, :, :columns]
    for extra in extra_ref:
        extra[0, blk] = along_ref[0, :, columns:]
        extra[0, 1 - blk] = across_ref[0, :, columns:]


def assemble_columns(along, across, columns):
    batch, own, both = along.shape
    rows = pl.BlockSpec((1, own, both), lambda i, at: (i, 0, 0))
    shapes = [(batch, 2, own, columns)]
    if both > columns:
        shapes.append((batch, 2, own, both - columns))
    parts = pl.pallas_call(
        assemble_columns_kernel,
        grid_spec=pltpu.PrefetchScalarGridSpec(
            num_scalar_prefetch=1,
            grid=(batch,),
            in_specs=[rows, rows],
            out_specs=[pl.BlockSpec((1,) + s[1:], lambda i, at: (i, 0, 0, 0)) for s in shapes],
        ),
        out_shape=[pltpu.HBM(s, BF16) for s in shapes],
        compiler_params=KERNEL,
        cost_estimate=LIGHT,
    )(place(), *in_hbm(along, across))
    return [part.reshape(-1, part.shape[-1]) for part in parts]


def assemble_wide_kernel(place_ref, along_ref, across_ref, whole_ref):
    blk = place_ref[0]
    own, columns = along_ref.shape[1], whole_ref.shape[-1]
    for i in range(along_ref.shape[-1] // columns):
        place, part = slice(i * own, (i + 1) * own), slice(i * columns, (i + 1) * columns)
        whole_ref[0, blk, place, :] = along_ref[0, :, part]
        whole_ref[0, 1 - blk, place, :] = across_ref[0, :, part]


def assemble_wide(along, across, columns):
    batch, own, wide = along.shape
    rows = own * (wide // columns)
    piece = pl.BlockSpec((1, own, wide), lambda i, at: (i, 0, 0))
    whole = pl.pallas_call(
        assemble_wide_kernel,
        grid_spec=pltpu.PrefetchScalarGridSpec(
            num_scalar_prefetch=1,
            grid=(batch,),
            in_specs=[piece, piece],
            out_specs=pl.BlockSpec((1, 2, rows, columns), lambda i, at: (i, 0, 0, 0)),
        ),
        out_shape=pltpu.HBM((batch, 2, rows, columns), BF16),
        compiler_params=KERNEL,
        cost_estimate=LIGHT,
    )(place(), *in_hbm(along, across))
    return whole.reshape(-1, columns)


def project_kernel(with_norm, place_ref, *refs):
    pieces, (gain_ref, weight_ref, normed_ref, projected_ref) = refs[:4], refs[4:]
    head = place_ref[1] * 2 + place_ref[2]
    rows = pieces[0].shape[0]
    for i, piece in enumerate(pieces):
        value = piece[...]
        if with_norm:
            stream = value.astype(F32)
            factor = lax.rsqrt(jnp.mean(stream * stream, axis=-1, keepdims=True) + EPSILON)
            value = (stream * factor * gain_ref[...]).astype(BF16)
        normed_ref[pl.ds(pl.multiple_of((head ^ i) * rows, rows), rows), :] = value
    projected = jnp.dot(normed_ref[...], weight_ref[...], preferred_element_type=F32)
    projected_ref[...] = projected.T


def project(pieces, gain, weight, with_norm, token_rows):
    tokens, width = pieces[0].shape
    length, columns = 4 * tokens, weight.shape[1]
    groups = tokens // token_rows
    piece = pl.BlockSpec((token_rows, width), lambda g, at: (g, 0))
    return pl.pallas_call(
        functools.partial(project_kernel, with_norm),
        grid_spec=pltpu.PrefetchScalarGridSpec(
            num_scalar_prefetch=1,
            grid=(groups,),
            in_specs=[piece] * 4
            + [
                pl.BlockSpec((1, width), lambda g, at: (0, 0)),
                pl.BlockSpec((width, columns), lambda g, at: (0, 0)),
            ],
            out_specs=[
                pl.BlockSpec((4 * token_rows, width), lambda g, at: (g, 0)),
                pl.BlockSpec((columns, 4 * token_rows), lambda g, at: (0, g)),
            ],
        ),
        out_shape=[
            pltpu.HBM((length, width), BF16),
            jax.ShapeDtypeStruct((columns, length), F32),
        ],
        compiler_params=KERNEL,
        cost_estimate=LIGHT,
    )(place(), *in_hbm(*pieces), gain.reshape(1, width), *in_hbm(weight))


def project_back_kernel(
    place_ref, bars_ref, weight_ref, normed_ref, own_ref, other_ref, grad_ref, bars_t
):
    @pl.when(pl.program_id(0) == 0)
    def _():
        bars_t[...] = bars_ref[...].astype(F32).T.astype(BF16)

    upper = lax.dot_general(bars_t[...], weight_ref[...], NT, preferred_element_type=F32)
    upper = upper.reshape(2, 2, 2, -1, upper.shape[-1])
    first_core = place_ref[2] == 0
    one, two = upper[:, :, 0], upper[:, :, 1]
    own_ref[...] = jnp.where(first_core, one, two)
    other_ref[...] = jnp.where(first_core, two, one).astype(BF16)
    grad = lax.dot_general(normed_ref[...], bars_t[...], TN, preferred_element_type=F32)
    grad_ref[...] = grad.astype(BF16)


def project_back(bars, weight, normed, token_rows):
    columns, length = bars.shape
    width = weight.shape[0]
    tile = width // 2
    quarter = pl.BlockSpec((2, 2, token_rows, tile), lambda i, at: (0, 0, 0, i))
    return pl.pallas_call(
        project_back_kernel,
        grid_spec=pltpu.PrefetchScalarGridSpec(
            num_scalar_prefetch=1,
            grid=(2,),
            in_specs=[
                pl.BlockSpec((columns, length), lambda i, at: (0, 0)),
                pl.BlockSpec((tile, columns), lambda i, at: (i, 0)),
                pl.BlockSpec((length, tile), lambda i, at: (0, i)),
            ],
            out_specs=[quarter, quarter, pl.BlockSpec((tile, columns), lambda i, at: (i, 0))],
            scratch_shapes=[pltpu.VMEM((length, columns), BF16)],
        ),
        out_shape=[
            pltpu.HBM((2, 2, token_rows, width), F32),
            pltpu.HBM((2, 2, token_rows, width), BF16),
            pltpu.HBM((width, columns), BF16),
        ],
        compiler_params=KERNEL,
        cost_estimate=LIGHT,
    )(place(), *in_hbm(bars, weight, normed))


def rows_back_kernel(place_ref, bars_ref, weight_ref, own_ref, other_ref, bars_t):
    @pl.when(pl.program_id(0) == 0)
    def _():
        bars_t[...] = bars_ref[...].astype(F32).T.astype(BF16)

    upper = lax.dot_general(bars_t[...], weight_ref[...], NT, preferred_element_type=F32)
    upper = upper.reshape(2, 2, 2, -1, upper.shape[-1])
    first_core = place_ref[2] == 0
    one, two = upper[:, :, 0], upper[:, :, 1]
    own_ref[...] = jnp.where(first_core, one, two)
    other_ref[...] = jnp.where(first_core, two, one).astype(BF16)


def rows_back(bars, weight, token_rows):
    columns, length = bars.shape
    width = weight.shape[0]
    tile = width // 2
    quarter = pl.BlockSpec((2, 2, token_rows, tile), lambda i, at: (0, 0, 0, i))
    return pl.pallas_call(
        rows_back_kernel,
        grid_spec=pltpu.PrefetchScalarGridSpec(
            num_scalar_prefetch=1,
            grid=(2,),
            in_specs=[
                pl.BlockSpec((columns, length), lambda i, at: (0, 0)),
                pl.BlockSpec((tile, columns), lambda i, at: (i, 0)),
            ],
            out_specs=[quarter, quarter],
            scratch_shapes=[pltpu.VMEM((length, columns), BF16)],
        ),
        out_shape=[
            pltpu.HBM((2, 2, token_rows, width), F32),
            pltpu.HBM((2, 2, token_rows, width), BF16),
        ],
        compiler_params=KERNEL,
        cost_estimate=LIGHT,
    )(place(), *in_hbm(bars, weight))


def weight_back_kernel(bars_ref, normed_ref, grad_ref):
    grad = jnp.dot(bars_ref[...], normed_ref[...], preferred_element_type=F32)
    grad_ref[...] = grad.T.astype(BF16)


def weight_back(bars, normed):
    columns, length = bars.shape
    width = normed.shape[1]
    tile = width // 5
    return pl.pallas_call(
        weight_back_kernel,
        grid=(5,),
        in_specs=[
            pl.BlockSpec((columns, length), lambda i: (0, 0)),
            pl.BlockSpec((length, tile), lambda i: (0, i)),
        ],
        out_specs=pl.BlockSpec((tile, columns), lambda i: (i, 0)),
        out_shape=pltpu.HBM((width, columns), BF16),
        compiler_params=KERNEL,
        cost_estimate=LIGHT,
    )(*in_hbm(bars, normed))


def tied(*arrays):
    return lax.optimization_barrier(arrays)


def swapped(array, axis, mask):
    size = lax.axis_size(axis)
    return lax.ppermute(array, axis, [(i, i ^ mask) for i in range(size)])


def pick(array, index, axis=0):
    return lax.dynamic_index_in_dim(array, index, axis, keepdims=False)


def swap_halves(array):
    me = lax.axis_index("blk")
    got = swapped(pick(array, 1 - me), "blk", 1)
    kept = pick(array, me)
    return jnp.stack([jnp.where(me == 0, kept, got), jnp.where(me == 0, got, kept)])


def scatter_row(halves):
    row = lax.axis_index("head") // 2
    got = swapped(pick(halves, 1 - row, 1).astype(BF16), "head", 2).astype(F32)
    return (pick(halves, row, 1) + got).reshape(-1, halves.shape[-1])


def over_head(parts):
    return lax.all_to_all(parts, "head", split_axis=0, concat_axis=0, tiled=True)


def qkv_columns(rows, extra):
    own, width = rows.shape
    part = width // 3 // 4
    sent = rows.reshape(own, 3, 4, part).transpose(2, 0, 1, 3).reshape(4, own, 3 * part)
    if extra is not None:
        sent = jnp.concatenate([sent, jnp.broadcast_to(extra[None], (4,) + extra.shape)], axis=2)
    return over_head(sent)


def along_batch(piece):
    return lax.all_gather(piece, "batch", axis=0, tiled=False)


def other_core(array):
    return swapped(array, "head", 1)


def to_beside(across):
    return swapped(across[..., : across.shape[-1] // 3], "head", 2)


def to_across(beside):
    return swapped(beside[..., beside.shape[-1] // 3 :], "blk", 1)


def over_batch(parts):
    return lax.psum_scatter(parts.astype(BF16), "batch", scatter_dimension=0, tiled=False)


def across_sum(halves):
    blk = lax.axis_index("blk")
    got = swapped(pick(halves, 1 - blk), "blk", 1).astype(F32)
    return (pick(halves, blk).astype(F32) + got).astype(BF16)


def columns_to_rows(moved):
    rows = moved.shape[1]
    return moved.reshape(4, rows, 3, -1).transpose(1, 2, 0, 3).reshape(rows, -1).astype(F32)


def quarter(parts, blk, row):
    one, two = (pick(pick(part, blk), row).astype(F32) for part in parts)
    return one + two


def diagonal_rows(parts):
    blk, row = place()[:2]
    rows = quarter(parts, 1 - blk, 1 - row).astype(BF16)
    half = rows.shape[-1] // 2
    return rows[..., :half], rows[..., half:]


def neighbour_rows(parts, one, two):
    blk, row = place()[:2]
    half = one.shape[-1]
    across, beside = quarter(parts, 1 - blk, row), quarter(parts, blk, 1 - row)
    across = jnp.concatenate([across[..., :half], across[..., half:] + two.astype(F32)], axis=-1)
    beside = jnp.concatenate([beside[..., :half] + one.astype(F32), beside[..., half:]], axis=-1)
    return across.astype(BF16), beside.astype(BF16)


def sent_beside_and_across(across, beside):
    return swapped(across, "blk", 1), swapped(beside, "head", 2)


def heads_grad(weight, out_bar):
    return dot_cols(weight, out_bar).astype(BF16).reshape(4, -1, out_bar.shape[0])


def own_quarter(parts):
    blk, row = place()[:2]
    return quarter(parts, blk, row)


def own_sum(own, *more):
    return sum((part.astype(F32) for part in more), own).astype(BF16)


def sum_over(array, *hops):
    for axis, mask in hops:
        array = array + swapped(array, axis, mask)
    return array


def gain_back(weight, weight_grad, gain):
    return jnp.sum(weight.astype(F32) * weight_grad, axis=-1) / gain.astype(F32)


def lower_of(upper, stream, factor, gain):
    return norm_back(upper, stream, factor, gain)[0]


def spread_device(
    tokens,
    segments,
    qkv_weight,
    out_weight,
    up_weight,
    down_weight,
    attn_gain,
    mlp_gain,
    scale_param,
    cotangent,
):
    layers, head_dim = scale_param.shape
    _, token_rows, width = tokens.shape
    scale_vecs = SCALE_BASE / math.sqrt(head_dim) * jax.nn.softplus(scale_param)
    segments = pick(segments, lax.axis_index("blk"))
    own_gains = jnp.concatenate([attn_gain, mlp_gain], axis=0)

    part3 = 3 * width // 4
    dense_own = [
        jnp.concatenate([out_weight[i], up_weight[i], down_weight[i]], axis=1) for i in (0, 1)
    ]

    first = swap_halves(tokens).reshape(-1, width)
    columns = qkv_columns(qkv_weight[0], own_gains.T)
    columns, first, cotangent = tied(columns.reshape(-1, columns.shape[-1]), first, cotangent)
    stream = first.astype(F32)
    along = along_batch(columns)
    far, near = swapped(first, "head", 2), other_core(first)
    both = other_core(far)
    upper = swap_halves(cotangent)
    along, near, far, both, dense_near, upper = tied(
        along, near, far, both, dense_own[0], upper
    )
    token_pieces = (first, near, far, both)
    dense_near = along_batch(dense_near)
    qkv_across = swapped(along, "blk", 1)
    next_columns = jnp.concatenate(list(qkv_columns(qkv_weight[1], None)), axis=1)
    qkv_across, dense_near, next_columns = tied(qkv_across, dense_near, next_columns)
    across, beside = swapped(dense_near, "blk", 1), swapped(dense_near, "head", 2)
    next_both = along_batch(jnp.stack([next_columns, dense_own[1]]))
    weight, gains = assemble_columns(along, qkv_across, part3)
    qkvs = [weight]
    gains = gains.T.astype(F32)

    kept, denses = [], []
    for layer in range(layers):
        normed, factor_one = normalize(stream, gains[layer])
        if layer == 1:
            normed = normed.astype(BF16)
            far, near = swapped(normed, "head", 2), other_core(normed)
            far, next_across, dense_next = tied(far, next_across, dense_next)
            across, beside = swapped(dense_next, "blk", 1), swapped(dense_next, "head", 2)
            token_pieces = (normed, near, far, other_core(far))
            qkvs.append(assemble_wide(next_along, next_across, part3))
        normed_all, projected = project(
            token_pieces, gains[layer], qkvs[layer], layer == 0, token_rows
        )
        attended, log_total = attend_rows(
            projected, scale_vecs[layer], segments, 4, token_rows
        )
        attended, across, beside = tied(attended, across, beside)
        one, two = to_beside(across), to_across(beside)
        if layer == 0:
            two, next_both = tied(two, next_both)
            next_along, dense_next = next_both[:, 0], next_both[:, 1]
            next_across = swapped(next_along, "blk", 1)
            attended_t, one, two = tied(over_head(attended), one, two)
        else:
            dense_near = dense_next
            attended_t, one, two = tied(over_head(attended), one, two)
        pieces = (dense_near, across, beside, one, two)
        pieces += tuple(other_core(piece) for piece in pieces)
        attended_t = attended_t.reshape(width, -1)
        denses.append(assemble(pieces))
        dense = denses[layer]
        out_w, up_w, down_w = dense[:, :width], dense[:, width:-width], dense[:, -width:]
        middle = stream + dot_rows(attended_t, out_w)
        normed_two, factor_two = normalize(middle, gains[layers + layer])
        normed_two = normed_two.astype(BF16)
        hidden = dot(normed_two, up_w)
        active = (hidden * jax.nn.sigmoid(hidden)).astype(BF16)
        kept.append(
            (
                stream, factor_one, normed_all, projected, log_total, attended_t, middle,
                factor_two, normed_two, hidden, active,
            )
        )
        stream = middle + dot(active, down_w)
    layer_out = swap_halves(stream.astype(BF16).reshape(tokens.shape))
    upper = upper.reshape(-1, width).astype(F32)

    scale_grads = [None] * layers
    for layer in reversed(range(layers)):
        (
            stream, factor_one, normed_all, projected, log_total, attended_t, middle,
            factor_two, normed_two, hidden, active,
        ) = kept[layer]
        qkv, dense = qkvs[layer], denses[layer]
        out_w, up_w, down_w = dense[:, :width], dense[:, width:-width], dense[:, -width:]
        down_bar = upper.astype(BF16)
        gate = jax.nn.sigmoid(hidden)
        up_bar = (
            dot_cols(down_bar, down_w) * gate * (1.0 + hidden * (1.0 - gate))
        ).astype(BF16)
        middle_grad = upper + lower_of(
            dot_cols(up_bar, up_w), middle, factor_two, gains[layers + layer]
        )
        out_bar = middle_grad.astype(BF16)
        if layer == 0:
            attended_grad = over_head(heads_grad(out_w, out_bar))
            grads, others = dense_grads(attended_t, normed_two, active, out_bar, up_bar, down_bar)
            others, across = tied(others, across)
            others, own = tied(others, own_quarter(cored) + across.astype(F32))
            attended_grad, others, z_sum, beside = tied(attended_grad, others, z_sum, beside)
            others = other_core(others)
            attended_grad, summed = tied(attended_grad, own_sum(own, beside))
            summed = over_batch(summed)
            earlier = across_sum(z_sum)
        else:
            attended_grad = over_head(heads_grad(out_w, out_bar))
            grads, others = dense_grads(attended_t, normed_two, active, out_bar, up_bar, down_bar)
            attended_grad, others, layer_out = tied(attended_grad, others, layer_out)
            others = other_core(others)
        bars, scale_grads[layer] = attend_back_rows(
            projected, attended_grad, log_total, scale_vecs[layer], segments, token_rows
        )
        if layer == 0:
            bars, earlier = tied(bars, earlier)
            qkv_grad = weight_back(bars, normed_all)
            bars, qkv_grad, others = tied(bars, qkv_grad, others)
            z_sum = over_batch(qkv_grad.reshape(4, 2, -1, qkv_grad.shape[-1]))
            cored = (grads, others)
            bars, rows = tied(bars, diagonal_rows(cored))
            diagonal = sent_beside_and_across(*rows)
            halves, to_core = rows_back(bars, qkv, token_rows)
            scale_sum = sum_over(jnp.stack(scale_grads), ("head", 1))
            halves, to_core, diagonal, summed, scale_sum = tied(
                halves, to_core, diagonal, summed, scale_sum
            )
            scale_sum = sum_over(scale_sum, ("head", 2))
            halves, to_core, rows, scale_sum = tied(
                halves, to_core, neighbour_rows(cored, *diagonal), scale_sum
            )
            sent = sent_beside_and_across(*rows)
            halves = halves + other_core(to_core).astype(F32)
            scale_sum = sum_over(scale_sum, ("batch", 1), ("batch", 2), ("blk", 1))
            own = own_quarter(cored)
            halves, sent, z_sum, scale_sum, own = tied(halves, sent, z_sum, scale_sum, own)
            halves, own, earlier = tied(halves, own_sum(own, *sent), earlier)
            moved = over_head(earlier.reshape(4, -1, earlier.shape[-1]))
            dense_first = over_batch(own)
            normed_grad = scatter_row(halves)
            z_across, dense_first = tied(across_sum(z_sum), dense_first)
            z_across = over_head(z_across.reshape(4, -1, z_across.shape[-1]))
            dense_grad = [dense_first, summed]
            qkv_grads = [columns_to_rows(z_across), columns_to_rows(moved)]
        else:
            bars, others = tied(bars, others)
            cored = (grads, others)
            bars, rows = tied(bars, diagonal_rows(cored))
            diagonal = sent_beside_and_across(*rows)
            halves, to_core, qkv_grad = project_back(bars, qkv, normed_all, token_rows)
            z_sum = over_batch(qkv_grad.reshape(4, 2, -1, qkv_grad.shape[-1]))
            to_core, halves, diagonal = tied(to_core, halves, diagonal)
            to_core, rows = tied(to_core, neighbour_rows(cored, *diagonal))
            across = swapped(rows[0], "blk", 1)
            halves = halves + other_core(to_core).astype(F32)
            normed_grad = scatter_row(halves)
            normed_grad, beside = tied(normed_grad, rows[1])
            beside = swapped(beside, "head", 2)
        upper = middle_grad + lower_of(normed_grad, stream, factor_one, gains[layer])
    input_grad = swap_halves(upper.astype(BF16).reshape(tokens.shape)).astype(F32)
    scale_grad = scale_sum * (SCALE_BASE / math.sqrt(head_dim)) * jax.nn.sigmoid(scale_param)
    dense_all = jnp.stack([part.astype(F32) for part in dense_grad])
    qkv_all = jnp.stack(qkv_grads)
    up_all = dense_all[:, :, width:-width]
    return (
        layer_out,
        input_grad,
        qkv_all,
        dense_all[:, :, :width],
        up_all,
        dense_all[:, :, -width:],
        gain_back(qkv_weight, qkv_all, attn_gain),
        gain_back(up_weight, up_all, mlp_gain),
        scale_grad,
    )


def per_device(*args):
    tokens, segments = args[0], args[1]
    sizes = tuple(lax.axis_size(axis) for axis in ALL)
    heads = tokens.shape[2] // args[8].shape[1]
    spread = (
        sizes == (4, 2, 4)
        and tokens.shape[0] == 2
        and args[2].shape[0] == 2
        and tokens.shape[1] % 128 == 0
        and Q_ROWS % tokens.shape[1] == 0
        and segments.shape[1] <= WINDOW
        and segments.shape[1] % FORWARD_ROWS == 0
        and heads % 4 == 0
        and tokens.shape[2] % 256 == 0
    )
    return spread_device(*args) if spread else general_device(*args)


def solution(mesh):
    rows = P(None, ALL, None)
    by_token = P("batch", ("blk", "head"), None)
    return jax.shard_map(
        per_device,
        mesh=mesh,
        in_specs=(
            by_token, P("batch", None), rows, rows, rows, rows, P(None, ALL), P(None, ALL), P(),
            by_token,
        ),
        out_specs=(
            by_token, by_token, rows, rows, rows, rows, P(None, ALL), P(None, ALL), P(),
        ),
        check_vma=False,
    )
```

```python
import functools
import math

import jax
import jax.numpy as jnp
from jax import lax
from jax.experimental import pallas as pl
from jax.experimental.pallas import tpu as pltpu
from jax.sharding import PartitionSpec as P

WINDOW = 1024
EPSILON = 1e-06
SCALE_BASE = 1.4426950408889634
MASKED_SCORE = -1e30

ALL = ("batch", "blk", "head")
REST = ("batch", "blk")
F32 = jnp.float32
BF16 = jnp.bfloat16


def shifted(block, axis, distance):
    devices = range(lax.axis_size(axis))
    route = [(i - distance, i) for i in devices if i - distance in devices]
    return lax.ppermute(block, axis, route)


NT = (((1,), (1,)), ((), ()))
TN = (((0,), (0,)), ((), ()))


def dot(left, right):
    return jnp.dot(left, right, preferred_element_type=F32)


def dot_rows(left, right):
    return lax.dot_general(left, right, (((0,), (0,)), ((), ())), preferred_element_type=F32)


def dot_cols(left, right):
    return lax.dot_general(left, right, (((1,), (1,)), ((), ())), preferred_element_type=F32)


def normalize(stream, gain):
    factor = lax.rsqrt(jnp.mean(stream * stream, axis=-1, keepdims=True) + EPSILON)
    return stream * factor * gain, factor


def norm_back(upper, stream, factor, gain):
    inner = upper * gain
    gain_grad = jnp.sum(upper * stream * factor, axis=0)
    lower = factor * inner - stream * factor * factor * factor * jnp.mean(
        inner * stream, axis=-1, keepdims=True
    )
    return lower, gain_grad


class Plan:
    def __init__(self, tokens):
        self.seqs, self.rows, self.width = tokens.shape
        self.heads = lax.axis_size("head")
        self.blks = lax.axis_size("blk")
        self.block = self.rows * self.heads
        self.whole = self.seqs % self.blks == 0
        if self.whole:
            self.groups, self.own_seqs = self.blks, self.seqs // self.blks
            self.reach = 0
        else:
            self.groups, self.own_seqs = 1, self.seqs
            self.reach = min((WINDOW - 1) // self.block + 1, self.blks - 1)
        self.length = self.groups * self.block
        self.tokens = self.seqs * self.rows


def to_plan(plan, array):
    if plan.whole and plan.blks > 1:
        array = lax.all_to_all(array, "blk", split_axis=0, concat_axis=0, tiled=True)
    return array.reshape(plan.tokens, plan.width)


def from_plan(plan, flat):
    array = flat.reshape(plan.seqs, plan.rows, plan.width)
    if plan.whole and plan.blks > 1:
        array = lax.all_to_all(array, "blk", split_axis=0, concat_axis=0, tiled=True)
    return array


def in_sequence(plan, by_head, width):
    parts = by_head.reshape(plan.heads, plan.groups, plan.own_seqs, plan.rows, width)
    return parts.transpose(2, 1, 0, 3, 4).reshape(-1, width)


def by_owner(plan, rows, width):
    parts = rows.reshape(plan.own_seqs, plan.groups, plan.heads, plan.rows, width)
    return parts.transpose(2, 1, 0, 3, 4).reshape(plan.heads, plan.tokens, width)


def gather_tokens(plan, rows):
    moved = lax.all_gather(rows, "head", axis=0, tiled=False)
    return in_sequence(plan, moved, rows.shape[-1])


def scatter_tokens(plan, rows):
    width = rows.shape[-1]
    return lax.psum_scatter(
        by_owner(plan, rows.astype(BF16), width), "head", scatter_dimension=0, tiled=False
    ).astype(F32)


def heads_to_tokens(plan, rows):
    part = rows.shape[-1]
    moved = lax.all_to_all(
        by_owner(plan, rows, part), "head", split_axis=0, concat_axis=0, tiled=True
    )
    return moved.transpose(1, 0, 2).reshape(plan.tokens, plan.heads * part)


def tokens_to_heads(plan, rows):
    part = rows.shape[-1] // plan.heads
    sent = rows.reshape(plan.tokens, plan.heads, part).transpose(1, 0, 2)
    moved = lax.all_to_all(sent, "head", split_axis=0, concat_axis=0, tiled=True)
    return in_sequence(plan, moved, part)


def gather_qkv(rows):
    own, width = rows.shape
    heads = lax.axis_size("head")
    part = width // 3 // heads
    sent = rows.reshape(own, 3, heads, part).transpose(2, 0, 1, 3).reshape(heads, own, 3 * part)
    moved = lax.all_to_all(sent, "head", split_axis=0, concat_axis=0, tiled=True)
    full = lax.all_gather(moved, REST, axis=0, tiled=True)
    return full.reshape(-1, 3 * part)


def scatter_qkv(grad):
    heads = lax.axis_size("head")
    part = grad.shape[1] // 3
    summed = lax.psum_scatter(grad.astype(BF16), REST, scatter_dimension=0, tiled=True)
    own = summed.shape[0] // heads
    moved = lax.all_to_all(
        summed.reshape(heads, own, 3 * part), "head", split_axis=0, concat_axis=0, tiled=True
    )
    return (
        moved.reshape(heads, own, 3, part)
        .transpose(1, 2, 0, 3)
        .reshape(own, 3 * heads * part)
        .astype(F32)
    )


def window_mask(plan, segments, block_index):
    key_count = plan.length + plan.reach * plan.block
    if plan.whole:
        query_segs, key_segs = segments, segments
    else:
        leading = jnp.full((plan.own_seqs, plan.reach * plan.block), -1, jnp.int32)
        padded = jnp.concatenate([leading, segments], axis=1)
        start = block_index * plan.block
        query_segs = lax.dynamic_slice_in_dim(segments, start, plan.block, 1)
        key_segs = lax.dynamic_slice_in_dim(padded, start, key_count, 1)
    query_place = jnp.arange(plan.length, dtype=jnp.int32)[:, None] + plan.reach * plan.block
    key_place = jnp.arange(key_count, dtype=jnp.int32)[None, :]
    near = (key_place <= query_place) & (query_place - key_place < WINDOW)
    return (key_segs[:, None, :] == query_segs[:, :, None]) & near[None]


def with_earlier(plan, own):
    arrived = [own]
    for _ in range(plan.reach):
        arrived.append(shifted(arrived[-1], "blk", 1))
    return jnp.concatenate(arrived[::-1], axis=1) if plan.reach else own


def to_earlier(plan, grads):
    if not plan.reach:
        return grads
    block = plan.block
    total = grads[:, :block]
    for step in range(1, plan.reach + 1):
        total = (
            shifted(total.astype(BF16), "blk", -1).astype(F32)
            + grads[:, step * block : (step + 1) * block]
        )
    return total


def scores_of(queries, keys, allowed):
    scores = jnp.einsum("sqhd,skhd->shqk", queries, keys, preferred_element_type=F32)
    return jnp.where(allowed[:, None], scores, MASKED_SCORE)


def attend(queries, keys, values, allowed):
    scores = scores_of(queries, keys, allowed)
    top_score = jnp.max(scores, axis=-1, keepdims=True)
    exp_terms = jnp.exp(scores - top_score)
    totals = jnp.sum(exp_terms, axis=-1, keepdims=True)
    probs_low = (exp_terms / totals).astype(BF16)
    attended = jnp.einsum("shqk,skhd->sqhd", probs_low, values, preferred_element_type=F32)
    return attended, top_score + jnp.log(totals)


def attend_back(queries, keys, values, allowed, log_total, attended_grad):
    probs = jnp.exp(scores_of(queries, keys, allowed) - log_total)
    probs_low = probs.astype(BF16)
    values_grad = jnp.einsum(
        "shqk,sqhd->skhd", probs_low, attended_grad, preferred_element_type=F32
    )
    probs_grad = jnp.einsum("sqhd,skhd->shqk", attended_grad, values, preferred_element_type=F32)
    row_dot = jnp.sum(probs_grad * probs, axis=-1, keepdims=True)
    scores_low = (probs * (probs_grad - row_dot)).astype(BF16)
    queries_grad = jnp.einsum("shqk,skhd->sqhd", scores_low, keys, preferred_element_type=F32)
    keys_grad = jnp.einsum("shqk,sqhd->skhd", scores_low, queries, preferred_element_type=F32)
    return queries_grad, keys_grad, values_grad


def forward(plan, stream, qkv, dense, gains, scale_vec, allowed):
    width = plan.width
    head_dim = scale_vec.shape[0]
    part = qkv.shape[1] // 3
    local_heads = part // head_dim
    split = (plan.own_seqs, plan.length, local_heads, head_dim)
    out_w, up_w, down_w = dense[:, :width], dense[:, width:-width], dense[:, -width:]
    normed, factor_one = normalize(stream, gains[0])
    normed_all = gather_tokens(plan, normed.astype(BF16))
    projected = dot(normed_all, qkv)
    query_pre = projected[:, :part].reshape(split)
    queries = (query_pre * scale_vec).astype(BF16)
    keys = with_earlier(plan, projected[:, part : 2 * part].astype(BF16).reshape(split))
    values = with_earlier(plan, projected[:, 2 * part :].astype(BF16).reshape(split))
    attended_part, log_total = attend(queries, keys, values, allowed)
    attended = heads_to_tokens(plan, attended_part.astype(BF16).reshape(-1, part))
    middle = stream + dot(attended, out_w)
    normed_two, factor_two = normalize(middle, gains[1])
    normed_two = normed_two.astype(BF16)
    hidden = dot(normed_two, up_w)
    active = (hidden * jax.nn.sigmoid(hidden)).astype(BF16)
    result = middle + dot(active, down_w)
    kept = (
        stream, factor_one, normed_all, query_pre, queries, keys, values, log_total,
        attended, middle, factor_two, normed_two, hidden, active,
    )
    return result, kept


def backward(plan, upper, kept, qkv, dense, gains, scale_vec, allowed):
    (
        stream, factor_one, normed_all, query_pre, queries, keys, values, log_total,
        attended, middle, factor_two, normed_two, hidden, active,
    ) = kept
    width = plan.width
    head_dim = scale_vec.shape[0]
    part = qkv.shape[1] // 3
    out_w, up_w, down_w = dense[:, :width], dense[:, width:-width], dense[:, -width:]
    upper_low = upper.astype(BF16)
    down_grad = dot_rows(active, upper_low)
    active_grad = dot_cols(upper_low, down_w)
    gate = jax.nn.sigmoid(hidden)
    hidden_low = (active_grad * gate * (1.0 + hidden * (1.0 - gate))).astype(BF16)
    up_grad = dot_rows(normed_two, hidden_low)
    extra_two, mlp_gain_grad = norm_back(dot_cols(hidden_low, up_w), middle, factor_two, gains[1])
    middle_grad = upper + extra_two
    middle_low = middle_grad.astype(BF16)
    out_grad = dot_rows(attended, middle_low)
    dense_grad = jnp.concatenate([out_grad, up_grad, down_grad], axis=1).astype(BF16)
    dense_own = lax.psum_scatter(dense_grad, ALL, scatter_dimension=0, tiled=True)
    attended_grad = tokens_to_heads(plan, dot_cols(middle_low, out_w).astype(BF16))
    queries_grad, keys_grad, values_grad = attend_back(
        queries, keys, values, allowed, log_total, attended_grad.reshape(queries.shape)
    )
    query_bar = queries_grad.astype(BF16).astype(F32)
    scale_vec_grad = jnp.sum((query_bar * query_pre).reshape(-1, head_dim), axis=0)
    query_low = (query_bar * scale_vec).astype(BF16).reshape(-1, part)
    keys_low = to_earlier(plan, keys_grad).astype(BF16).reshape(-1, part)
    values_low = to_earlier(plan, values_grad).astype(BF16).reshape(-1, part)
    projected_low = jnp.concatenate([query_low, keys_low, values_low], axis=1)
    normed_grad = scatter_tokens(plan, dot_cols(projected_low, qkv))
    qkv_own = scatter_qkv(dot_rows(normed_all, projected_low))
    extra_one, attn_gain_grad = norm_back(normed_grad, stream, factor_one, gains[0])
    lower = middle_grad + extra_one
    return lower, qkv_own, dense_own, (attn_gain_grad, mlp_gain_grad), scale_vec_grad


def general_device(
    tokens,
    segments,
    qkv_weight,
    out_weight,
    up_weight,
    down_weight,
    attn_gain,
    mlp_gain,
    scale_param,
    cotangent,
):
    plan = Plan(tokens)
    layers, head_dim = scale_param.shape
    block_index = lax.axis_index("blk")
    scale_vecs = SCALE_BASE / math.sqrt(head_dim) * jax.nn.softplus(scale_param)
    own_gains = jnp.concatenate([attn_gain, mlp_gain], axis=0)
    gains = (
        lax.all_gather(own_gains.reshape(1, -1), ALL, axis=0, tiled=True)
        .reshape(-1, 2 * layers, attn_gain.shape[1])
        .transpose(1, 0, 2)
        .reshape(2 * layers, plan.width)
        .astype(F32)
    )
    if plan.whole:
        segments = lax.dynamic_slice_in_dim(
            segments, block_index * plan.own_seqs, plan.own_seqs, 0
        )
    allowed = window_mask(plan, segments, block_index)
    stream = to_plan(plan, tokens).astype(F32)
    qkvs, denses, kept = [], [], []
    for layer in range(layers):
        qkvs.append(gather_qkv(qkv_weight[layer]))
        own = jnp.concatenate([out_weight[layer], up_weight[layer], down_weight[layer]], axis=1)
        denses.append(lax.all_gather(own, ALL, axis=0, tiled=True))
        layer_gains = (gains[layer], gains[layers + layer])
        stream, saved = forward(
            plan, stream, qkvs[layer], denses[layer], layer_gains, scale_vecs[layer], allowed
        )
        kept.append(saved)
    layer_out = from_plan(plan, stream.astype(BF16))
    upper = to_plan(plan, cotangent).astype(F32)
    qkv_grads, dense_grads = [None] * layers, [None] * layers
    gain_grads, scale_grads = [None] * layers, [None] * layers
    for layer in reversed(range(layers)):
        layer_gains = (gains[layer], gains[layers + layer])
        upper, qkv_grads[layer], dense_grads[layer], gain_grads[layer], scale_grads[layer] = (
            backward(
                plan, upper, kept[layer], qkvs[layer], denses[layer], layer_gains,
                scale_vecs[layer], allowed,
            )
        )
    input_grad = from_plan(plan, upper.astype(BF16)).astype(F32)
    small = jnp.concatenate(
        [g[0] for g in gain_grads] + [g[1] for g in gain_grads] + scale_grads, axis=0
    )
    total = lax.psum(small, ALL)
    gain_total = total[: 2 * layers * plan.width].reshape(2 * layers, plan.width)
    owner = lax.axis_index(ALL)
    gain_rows = attn_gain.shape[1]
    own_total = lax.dynamic_slice_in_dim(gain_total, owner * gain_rows, gain_rows, 1)
    scale_total = total[2 * layers * plan.width :].reshape(layers, head_dim)
    scale_grad = scale_total * (SCALE_BASE / math.sqrt(head_dim)) * jax.nn.sigmoid(scale_param)
    dense_all = jnp.stack(dense_grads).astype(F32)
    width = plan.width
    return (
        layer_out,
        input_grad,
        jnp.stack(qkv_grads),
        dense_all[:, :, :width],
        dense_all[:, :, width:-width],
        dense_all[:, :, -width:],
        own_total[:layers],
        own_total[layers:],
        scale_grad,
    )


Q_ROWS = 256
KERNEL = pltpu.CompilerParams(vmem_limit_bytes=32 * 1024 * 1024)
LIGHT = pl.CostEstimate(flops=1 << 20, bytes_accessed=1 << 20, transcendentals=0)


def in_hbm(*arrays):
    return [pltpu.with_memory_space_constraint(array, pltpu.HBM) for array in arrays]


def allowed_keys(col, row, first):
    count = first + row.shape[1]
    key_place = lax.broadcasted_iota(jnp.int32, (count, row.shape[1]), 0)
    query_place = lax.broadcasted_iota(jnp.int32, (count, row.shape[1]), 1) + first
    return (col[:count] == row) & (key_place <= query_place)


def allowed_piece(col, row, start, first):
    same = col == row
    if start + col.shape[0] <= first:
        return same
    key_place = lax.broadcasted_iota(jnp.int32, same.shape, 0) + start
    return same & (key_place <= lax.broadcasted_iota(jnp.int32, same.shape, 1) + first)


def token_places(length, heads, token_rows, block_rows=Q_ROWS):
    for first in range(0, length, block_rows):
        parts = []
        for start in range(0, block_rows, token_rows):
            place = (first + start) // token_rows
            parts.append((start, place % heads, place // heads * token_rows))
        yield first, parts


FORWARD_ROWS, FORWARD_KEYS = 1024, 512


def attend_kernel(token_rows, proj_ref, scale_ref, col_ref, row_ref, out_ref, lse_ref):
    length = proj_ref.shape[-1]
    queries = (proj_ref[0, 0] * scale_ref[...]).astype(BF16)
    keys = proj_ref[1, 0].T.astype(BF16)
    values = proj_ref[2, 0].astype(BF16)
    for first, parts in token_places(length, out_ref.shape[0], token_rows, FORWARD_ROWS):
        end = first + FORWARD_ROWS
        block, row = queries[:, first:end], row_ref[:, first:end]
        pieces = []
        for start in range(0, end, FORWARD_KEYS):
            scores = jnp.dot(keys[start : start + FORWARD_KEYS], block, preferred_element_type=F32)
            allowed = allowed_piece(col_ref[start : start + FORWARD_KEYS], row, start, first)
            pieces.append(jnp.where(allowed, scores, MASKED_SCORE))
        top = functools.reduce(
            jnp.maximum, [jnp.max(piece, axis=0, keepdims=True) for piece in pieces]
        )
        total, attended = 0.0, 0.0
        for i, piece in enumerate(pieces):
            terms = jnp.exp(piece - top)
            total += jnp.sum(terms, axis=0, keepdims=True)
            attended += jnp.dot(
                values[:, i * FORWARD_KEYS : (i + 1) * FORWARD_KEYS],
                terms.astype(BF16),
                preferred_element_type=F32,
            )
        attended = (attended * (1.0 / total)).astype(BF16)
        lse_ref[0, :, first:end] = top + jnp.log(total)
        for start, owner, offset in parts:
            out_ref[owner, 0, :, offset : offset + token_rows] = attended[
                :, start : start + token_rows
            ]


def attend_rows(projected, scale_vec, segments, owners, token_rows):
    head_dim = scale_vec.shape[0]
    length = projected.shape[1]
    local_heads = projected.shape[0] // 3 // head_dim
    tokens = length // owners
    attended, log_total = pl.pallas_call(
        functools.partial(attend_kernel, token_rows),
        grid=(local_heads,),
        in_specs=[
            pl.BlockSpec((3, 1, head_dim, length), lambda h: (0, h, 0, 0)),
            pl.BlockSpec((head_dim, 1), lambda h: (0, 0)),
            pl.BlockSpec((length, 1), lambda h: (0, 0)),
            pl.BlockSpec((1, length), lambda h: (0, 0)),
        ],
        out_specs=[
            pl.BlockSpec((owners, 1, head_dim, tokens), lambda h: (0, h, 0, 0)),
            pl.BlockSpec((1, 1, length), lambda h: (h, 0, 0)),
        ],
        out_shape=[
            jax.ShapeDtypeStruct((owners, local_heads, head_dim, tokens), BF16),
            jax.ShapeDtypeStruct((local_heads, 1, length), F32),
        ],
        compiler_params=KERNEL,
        cost_estimate=LIGHT,
    )(
        projected.reshape(3, local_heads, head_dim, length),
        scale_vec.reshape(head_dim, 1),
        segments.reshape(length, 1),
        segments.reshape(1, length),
    )
    return attended.reshape(owners, local_heads * head_dim, tokens), log_total


def attend_back_kernel(
    token_rows,
    proj_ref,
    grad_ref,
    lse_ref,
    scale_ref,
    col_ref,
    row_ref,
    out_ref,
    scale_grad_ref,
    keys_acc,
    values_acc,
):
    length = proj_ref.shape[-1]
    scale = scale_ref[...]
    query_pre = proj_ref[0, 0]
    queries = (query_pre * scale).astype(BF16)
    keys_t = proj_ref[1, 0].astype(BF16)
    keys = proj_ref[1, 0].T.astype(BF16)
    values = proj_ref[2, 0].T.astype(BF16)
    keys_acc[...] = jnp.zeros_like(keys_acc)
    values_acc[...] = jnp.zeros_like(values_acc)
    scale_grad = jnp.zeros((scale.shape[0], 1), F32)
    for first, parts in token_places(length, grad_ref.shape[0], token_rows):
        end = first + Q_ROWS
        block = queries[:, first:end]
        grad = jnp.concatenate(
            [grad_ref[owner, 0, :, at : at + token_rows] for _, owner, at in parts], axis=1
        )
        scores = jnp.dot(keys[:end], block, preferred_element_type=F32)
        allowed = allowed_keys(col_ref[...], row_ref[:, first:end], first)
        scores = jnp.where(allowed, scores, MASKED_SCORE)
        probs = jnp.exp(scores - lse_ref[0, :, first:end])
        probs_grad = jnp.dot(values[:end], grad, preferred_element_type=F32)
        row_dot = jnp.sum(probs_grad * probs, axis=0, keepdims=True)
        scores_low = (probs * (probs_grad - row_dot)).astype(BF16)
        values_acc[:, :end] += lax.dot_general(
            grad, probs.astype(BF16), NT, preferred_element_type=F32
        )
        keys_acc[:, :end] += lax.dot_general(
            block, scores_low, NT, preferred_element_type=F32
        )
        query_bar = jnp.dot(keys_t[:, :end], scores_low, preferred_element_type=F32)
        query_bar = query_bar.astype(BF16).astype(F32)
        scale_grad += jnp.sum(query_bar * query_pre[:, first:end], axis=1, keepdims=True)
        out_ref[0, 0, :, first:end] = (query_bar * scale).astype(BF16)
    out_ref[1, 0] = keys_acc[...].astype(BF16)
    out_ref[2, 0] = values_acc[...].astype(BF16)
    spread = jnp.broadcast_to(scale_grad, scale_grad_ref.shape)

    @pl.when(pl.program_id(0) == 0)
    def _():
        scale_grad_ref[...] = spread

    @pl.when(pl.program_id(0) > 0)
    def _():
        scale_grad_ref[...] += spread


def attend_back_rows(projected, attended_grad, log_total, scale_vec, segments, token_rows):
    head_dim = scale_vec.shape[0]
    length = projected.shape[1]
    local_heads = projected.shape[0] // 3 // head_dim
    owners, _, tokens = attended_grad.shape
    lanes = 128
    grads, scale_grad = pl.pallas_call(
        functools.partial(attend_back_kernel, token_rows),
        grid=(local_heads,),
        in_specs=[
            pl.BlockSpec((3, 1, head_dim, length), lambda h: (0, h, 0, 0)),
            pl.BlockSpec((owners, 1, head_dim, tokens), lambda h: (0, h, 0, 0)),
            pl.BlockSpec((1, 1, length), lambda h: (h, 0, 0)),
            pl.BlockSpec((head_dim, 1), lambda h: (0, 0)),
            pl.BlockSpec((length, 1), lambda h: (0, 0)),
            pl.BlockSpec((1, length), lambda h: (0, 0)),
        ],
        out_specs=[
            pl.BlockSpec((3, 1, head_dim, length), lambda h: (0, h, 0, 0)),
            pl.BlockSpec((head_dim, lanes), lambda h: (0, 0)),
        ],
        out_shape=[
            pltpu.HBM((3, local_heads, head_dim, length), BF16),
            pltpu.HBM((head_dim, lanes), F32),
        ],
        scratch_shapes=[
            pltpu.VMEM((head_dim, length), F32),
            pltpu.VMEM((head_dim, length), F32),
        ],
        compiler_params=KERNEL,
        cost_estimate=LIGHT,
    )(
        *in_hbm(
            projected.reshape(3, local_heads, head_dim, length),
            attended_grad.reshape(owners, local_heads, head_dim, tokens),
        ),
        log_total,
        scale_vec.reshape(head_dim, 1),
        segments.reshape(length, 1),
        segments.reshape(1, length),
    )
    return grads.reshape(3 * local_heads * head_dim, length), scale_grad[:, 0]


def dense_grad_kernel(
    core_ref, attended_ref, normed_ref, active_ref, out_bar, up_bar, down_bar,
    own_ref, other_ref, normed_t, active_t,
):
    tile = pl.program_id(0)
    rows, width = 8 * own_ref.shape[3], out_bar.shape[1]

    @pl.when(tile == 0)
    def _():
        normed_t[...] = normed_ref[...].astype(F32).T.astype(BF16)
        active_t[...] = active_ref[...].astype(F32).T.astype(BF16)

    start = pl.multiple_of(tile * rows, rows)
    first_core = core_ref[2] == 0
    lefts = (attended_ref, normed_t, active_t)
    for i, (left, right) in enumerate(zip(lefts, (out_bar, up_bar, down_bar))):
        grad = jnp.dot(left[pl.ds(start, rows), :], right[...], preferred_element_type=F32)
        grad = grad.reshape(2, 2, 2, rows // 8, width)
        one, two = grad[:, :, 0], grad[:, :, 1]
        own_ref[:, :, 0, :, i * width : (i + 1) * width] = jnp.where(
            first_core, one, two
        ).astype(BF16)
        other_ref[:, :, 0, :, i * width : (i + 1) * width] = jnp.where(
            first_core, two, one
        ).astype(BF16)


def dense_grads(attended_t, normed, active, out_bar, up_bar, down_bar):
    width, tokens = attended_t.shape
    own = width // 32
    whole = pl.BlockSpec((tokens, width), lambda i, core: (0, 0))
    rows = pl.BlockSpec((2, 2, 1, own, 3 * width), lambda i, core: (0, 0, i, 0, 0))
    shape = pltpu.HBM((2, 2, 4, own, 3 * width), BF16)
    return pl.pallas_call(
        dense_grad_kernel,
        grid_spec=pltpu.PrefetchScalarGridSpec(
            num_scalar_prefetch=1,
            grid=(4,),
            in_specs=[pl.BlockSpec((width, tokens), lambda i, core: (0, 0))] + [whole] * 5,
            out_specs=[rows, rows],
            scratch_shapes=[pltpu.VMEM((width, tokens), BF16)] * 2,
        ),
        out_shape=[shape, shape],
        compiler_params=KERNEL,
        cost_estimate=LIGHT,
    )(place(), *in_hbm(attended_t, normed, active, out_bar, up_bar, down_bar))


def place():
    head = lax.axis_index("head")
    return jnp.stack([lax.axis_index("blk"), head // 2, head % 2]).astype(jnp.int32)


def assemble_kernel(place_ref, *refs):
    pieces, whole_ref = refs[:10], refs[10]
    half = whole_ref.shape[-1] // 2
    blk, row, core = place_ref[0], place_ref[1], place_ref[2]
    for i in range(2):
        at_core = core if i == 0 else 1 - core
        own, across, beside, one, two = pieces[5 * i : 5 * i + 5]
        whole_ref[0, blk, row, at_core] = own[0]
        whole_ref[0, 1 - blk, row, at_core] = across[0]
        whole_ref[0, blk, 1 - row, at_core] = beside[0]
        whole_ref[0, 1 - blk, 1 - row, at_core, :, :half] = one[0]
        whole_ref[0, 1 - blk, 1 - row, at_core, :, half:] = two[0]


def assemble(pieces):
    batch, own, columns = pieces[0].shape
    specs = [
        pl.BlockSpec((1, own, piece.shape[-1]), lambda i, at: (i, 0, 0))
        for piece in pieces
    ]
    whole = pl.pallas_call(
        assemble_kernel,
        grid_spec=pltpu.PrefetchScalarGridSpec(
            num_scalar_prefetch=1,
            grid=(batch,),
            in_specs=specs,
            out_specs=pl.BlockSpec((1, 2, 2, 2, own, columns), lambda i, at: (i, 0, 0, 0, 0, 0)),
        ),
        out_shape=jax.ShapeDtypeStruct((batch, 2, 2, 2, own, columns), BF16),
        compiler_params=KERNEL,
        cost_estimate=LIGHT,
    )(place(), *pieces)
    return whole.reshape(-1, columns)


def assemble_columns_kernel(place_ref, along_ref, across_ref, whole_ref, *extra_ref):
    blk = place_ref[0]
    columns = whole_ref.shape[-1]
    whole_ref[0, blk] = along_ref[0, :, :columns]
    whole_ref[0, 1 - blk] = across_ref[0, :, :columns]
    for extra in extra_ref:
        extra[0, blk] = along_ref[0, :, columns:]
        extra[0, 1 - blk] = across_ref[0, :, columns:]


def assemble_columns(along, across, columns):
    batch, own, both = along.shape
    rows = pl.BlockSpec((1, own, both), lambda i, at: (i, 0, 0))
    shapes = [(batch, 2, own, columns)]
    if both > columns:
        shapes.append((batch, 2, own, both - columns))
    parts = pl.pallas_call(
        assemble_columns_kernel,
        grid_spec=pltpu.PrefetchScalarGridSpec(
            num_scalar_prefetch=1,
            grid=(batch,),
            in_specs=[rows, rows],
            out_specs=[pl.BlockSpec((1,) + s[1:], lambda i, at: (i, 0, 0, 0)) for s in shapes],
        ),
        out_shape=[pltpu.HBM(s, BF16) for s in shapes],
        compiler_params=KERNEL,
        cost_estimate=LIGHT,
    )(place(), *in_hbm(along, across))
    return [part.reshape(-1, part.shape[-1]) for part in parts]


def assemble_wide_kernel(place_ref, along_ref, across_ref, whole_ref):
    blk = place_ref[0]
    own, columns = along_ref.shape[1], whole_ref.shape[-1]
    for i in range(along_ref.shape[-1] // columns):
        place, part = slice(i * own, (i + 1) * own), slice(i * columns, (i + 1) * columns)
        whole_ref[0, blk, place, :] = along_ref[0, :, part]
        whole_ref[0, 1 - blk, place, :] = across_ref[0, :, part]


def assemble_wide(along, across, columns):
    batch, own, wide = along.shape
    rows = own * (wide // columns)
    piece = pl.BlockSpec((1, own, wide), lambda i, at: (i, 0, 0))
    whole = pl.pallas_call(
        assemble_wide_kernel,
        grid_spec=pltpu.PrefetchScalarGridSpec(
            num_scalar_prefetch=1,
            grid=(batch,),
            in_specs=[piece, piece],
            out_specs=pl.BlockSpec((1, 2, rows, columns), lambda i, at: (i, 0, 0, 0)),
        ),
        out_shape=pltpu.HBM((batch, 2, rows, columns), BF16),
        compiler_params=KERNEL,
        cost_estimate=LIGHT,
    )(place(), *in_hbm(along, across))
    return whole.reshape(-1, columns)


def project_kernel(with_norm, place_ref, *refs):
    pieces, (gain_ref, weight_ref, normed_ref, projected_ref) = refs[:4], refs[4:]
    head = place_ref[1] * 2 + place_ref[2]
    rows = pieces[0].shape[0]
    for i, piece in enumerate(pieces):
        value = piece[...]
        if with_norm:
            stream = value.astype(F32)
            factor = lax.rsqrt(jnp.mean(stream * stream, axis=-1, keepdims=True) + EPSILON)
            value = (stream * factor * gain_ref[...]).astype(BF16)
        normed_ref[pl.ds(pl.multiple_of((head ^ i) * rows, rows), rows), :] = value
    projected = jnp.dot(normed_ref[...], weight_ref[...], preferred_element_type=F32)
    projected_ref[...] = projected.T


def project(pieces, gain, weight, with_norm, token_rows):
    tokens, width = pieces[0].shape
    length, columns = 4 * tokens, weight.shape[1]
    groups = tokens // token_rows
    piece = pl.BlockSpec((token_rows, width), lambda g, at: (g, 0))
    return pl.pallas_call(
        functools.partial(project_kernel, with_norm),
        grid_spec=pltpu.PrefetchScalarGridSpec(
            num_scalar_prefetch=1,
            grid=(groups,),
            in_specs=[piece] * 4
            + [
                pl.BlockSpec((1, width), lambda g, at: (0, 0)),
                pl.BlockSpec((width, columns), lambda g, at: (0, 0)),
            ],
            out_specs=[
                pl.BlockSpec((4 * token_rows, width), lambda g, at: (g, 0)),
                pl.BlockSpec((columns, 4 * token_rows), lambda g, at: (0, g)),
            ],
        ),
        out_shape=[
            pltpu.HBM((length, width), BF16),
            jax.ShapeDtypeStruct((columns, length), F32),
        ],
        compiler_params=KERNEL,
        cost_estimate=LIGHT,
    )(place(), *in_hbm(*pieces), gain.reshape(1, width), *in_hbm(weight))


def project_back_kernel(
    place_ref, bars_ref, weight_ref, normed_ref, own_ref, other_ref, grad_ref, bars_t
):
    @pl.when(pl.program_id(0) == 0)
    def _():
        bars_t[...] = bars_ref[...].astype(F32).T.astype(BF16)

    upper = lax.dot_general(bars_t[...], weight_ref[...], NT, preferred_element_type=F32)
    upper = upper.reshape(2, 2, 2, -1, upper.shape[-1])
    first_core = place_ref[2] == 0
    one, two = upper[:, :, 0], upper[:, :, 1]
    own_ref[...] = jnp.where(first_core, one, two)
    other_ref[...] = jnp.where(first_core, two, one).astype(BF16)
    grad = lax.dot_general(normed_ref[...], bars_t[...], TN, preferred_element_type=F32)
    grad_ref[...] = grad.astype(BF16)


def project_back(bars, weight, normed, token_rows):
    columns, length = bars.shape
    width = weight.shape[0]
    tile = width // 2
    quarter = pl.BlockSpec((2, 2, token_rows, tile), lambda i, at: (0, 0, 0, i))
    return pl.pallas_call(
        project_back_kernel,
        grid_spec=pltpu.PrefetchScalarGridSpec(
            num_scalar_prefetch=1,
            grid=(2,),
            in_specs=[
                pl.BlockSpec((columns, length), lambda i, at: (0, 0)),
                pl.BlockSpec((tile, columns), lambda i, at: (i, 0)),
                pl.BlockSpec((length, tile), lambda i, at: (0, i)),
            ],
            out_specs=[quarter, quarter, pl.BlockSpec((tile, columns), lambda i, at: (i, 0))],
            scratch_shapes=[pltpu.VMEM((length, columns), BF16)],
        ),
        out_shape=[
            pltpu.HBM((2, 2, token_rows, width), F32),
            pltpu.HBM((2, 2, token_rows, width), BF16),
            pltpu.HBM((width, columns), BF16),
        ],
        compiler_params=KERNEL,
        cost_estimate=LIGHT,
    )(place(), *in_hbm(bars, weight, normed))


def rows_back_kernel(place_ref, bars_ref, weight_ref, own_ref, other_ref, bars_t):
    @pl.when(pl.program_id(0) == 0)
    def _():
        bars_t[...] = bars_ref[...].astype(F32).T.astype(BF16)

    upper = lax.dot_general(bars_t[...], weight_ref[...], NT, preferred_element_type=F32)
    upper = upper.reshape(2, 2, 2, -1, upper.shape[-1])
    first_core = place_ref[2] == 0
    one, two = upper[:, :, 0], upper[:, :, 1]
    own_ref[...] = jnp.where(first_core, one, two)
    other_ref[...] = jnp.where(first_core, two, one).astype(BF16)


def rows_back(bars, weight, token_rows):
    columns, length = bars.shape
    width = weight.shape[0]
    tile = width // 2
    quarter = pl.BlockSpec((2, 2, token_rows, tile), lambda i, at: (0, 0, 0, i))
    return pl.pallas_call(
        rows_back_kernel,
        grid_spec=pltpu.PrefetchScalarGridSpec(
            num_scalar_prefetch=1,
            grid=(2,),
            in_specs=[
                pl.BlockSpec((columns, length), lambda i, at: (0, 0)),
                pl.BlockSpec((tile, columns), lambda i, at: (i, 0)),
            ],
            out_specs=[quarter, quarter],
            scratch_shapes=[pltpu.VMEM((length, columns), BF16)],
        ),
        out_shape=[
            pltpu.HBM((2, 2, token_rows, width), F32),
            pltpu.HBM((2, 2, token_rows, width), BF16),
        ],
        compiler_params=KERNEL,
        cost_estimate=LIGHT,
    )(place(), *in_hbm(bars, weight))


def weight_back_kernel(bars_ref, normed_ref, grad_ref):
    grad = jnp.dot(bars_ref[...], normed_ref[...], preferred_element_type=F32)
    grad_ref[...] = grad.T.astype(BF16)


def weight_back(bars, normed):
    columns, length = bars.shape
    width = normed.shape[1]
    tile = width // 5
    return pl.pallas_call(
        weight_back_kernel,
        grid=(5,),
        in_specs=[
            pl.BlockSpec((columns, length), lambda i: (0, 0)),
            pl.BlockSpec((length, tile), lambda i: (0, i)),
        ],
        out_specs=pl.BlockSpec((tile, columns), lambda i: (i, 0)),
        out_shape=pltpu.HBM((width, columns), BF16),
        compiler_params=KERNEL,
        cost_estimate=LIGHT,
    )(*in_hbm(bars, normed))


def tied(*arrays):
    return lax.optimization_barrier(arrays)


def swapped(array, axis, mask):
    size = lax.axis_size(axis)
    return lax.ppermute(array, axis, [(i, i ^ mask) for i in range(size)])


def pick(array, index, axis=0):
    return lax.dynamic_index_in_dim(array, index, axis, keepdims=False)


def swap_halves(array):
    me = lax.axis_index("blk")
    got = swapped(pick(array, 1 - me), "blk", 1)
    kept = pick(array, me)
    return jnp.stack([jnp.where(me == 0, kept, got), jnp.where(me == 0, got, kept)])


def scatter_row(halves):
    row = lax.axis_index("head") // 2
    got = swapped(pick(halves, 1 - row, 1).astype(BF16), "head", 2).astype(F32)
    return (pick(halves, row, 1) + got).reshape(-1, halves.shape[-1])


def over_head(parts):
    return lax.all_to_all(parts, "head", split_axis=0, concat_axis=0, tiled=True)


def qkv_columns(rows, extra):
    own, width = rows.shape
    part = width // 3 // 4
    sent = rows.reshape(own, 3, 4, part).transpose(2, 0, 1, 3).reshape(4, own, 3 * part)
    if extra is not None:
        sent = jnp.concatenate([sent, jnp.broadcast_to(extra[None], (4,) + extra.shape)], axis=2)
    return over_head(sent)


def along_batch(piece):
    return lax.all_gather(piece, "batch", axis=0, tiled=False)


def other_core(array):
    return swapped(array, "head", 1)


def to_beside(across):
    return swapped(across[..., : across.shape[-1] // 2], "head", 2)


def to_across(beside):
    return swapped(beside[..., beside.shape[-1] // 2 :], "blk", 1)


def over_batch(parts):
    return lax.psum_scatter(parts.astype(BF16), "batch", scatter_dimension=0, tiled=False)


def across_sum(halves):
    blk = lax.axis_index("blk")
    got = swapped(pick(halves, 1 - blk), "blk", 1).astype(F32)
    return (pick(halves, blk).astype(F32) + got).astype(BF16)


def columns_to_rows(moved):
    rows = moved.shape[1]
    return moved.reshape(4, rows, 3, -1).transpose(1, 2, 0, 3).reshape(rows, -1).astype(F32)


def quarter(parts, blk, row):
    one, two = (pick(pick(part, blk), row).astype(F32) for part in parts)
    return one + two


def diagonal_rows(parts):
    blk, row = place()[:2]
    rows = quarter(parts, 1 - blk, 1 - row).astype(BF16)
    half = rows.shape[-1] // 2
    return rows[..., :half], rows[..., half:]


def neighbour_rows(parts, one, two):
    blk, row = place()[:2]
    half = one.shape[-1]
    across, beside = quarter(parts, 1 - blk, row), quarter(parts, blk, 1 - row)
    across = jnp.concatenate([across[..., :half], across[..., half:] + two.astype(F32)], axis=-1)
    beside = jnp.concatenate([beside[..., :half] + one.astype(F32), beside[..., half:]], axis=-1)
    return across.astype(BF16), beside.astype(BF16)


def sent_beside_and_across(across, beside):
    return swapped(across, "blk", 1), swapped(beside, "head", 2)


def heads_grad(weight, out_bar):
    return dot_cols(weight, out_bar).astype(BF16).reshape(4, -1, out_bar.shape[0])


def own_quarter(parts):
    blk, row = place()[:2]
    return quarter(parts, blk, row)


def own_sum(own, *more):
    return sum((part.astype(F32) for part in more), own).astype(BF16)


def sum_over(array, *hops):
    for axis, mask in hops:
        array = array + swapped(array, axis, mask)
    return array


def gain_back(weight, weight_grad, gain):
    return jnp.sum(weight.astype(F32) * weight_grad, axis=-1) / gain.astype(F32)


def lower_of(upper, stream, factor, gain):
    return norm_back(upper, stream, factor, gain)[0]


def spread_device(
    tokens,
    segments,
    qkv_weight,
    out_weight,
    up_weight,
    down_weight,
    attn_gain,
    mlp_gain,
    scale_param,
    cotangent,
):
    layers, head_dim = scale_param.shape
    _, token_rows, width = tokens.shape
    scale_vecs = SCALE_BASE / math.sqrt(head_dim) * jax.nn.softplus(scale_param)
    segments = pick(segments, lax.axis_index("blk"))
    own_gains = jnp.concatenate([attn_gain, mlp_gain], axis=0)

    part3 = 3 * width // 4
    dense_own = [
        jnp.concatenate([out_weight[i], up_weight[i], down_weight[i]], axis=1) for i in (0, 1)
    ]

    columns = qkv_columns(qkv_weight[0], own_gains.T)
    columns, tokens, cotangent = tied(columns.reshape(-1, columns.shape[-1]), tokens, cotangent)
    along = along_batch(columns)
    first = swap_halves(tokens).reshape(-1, width)
    stream = first.astype(F32)
    far, near = swapped(first, "head", 2), other_core(first)
    both = other_core(far)
    upper = swap_halves(cotangent)
    along, near, far, both, dense_near, upper = tied(
        along, near, far, both, dense_own[0], upper
    )
    token_pieces = (first, near, far, both)
    dense_near = along_batch(dense_near)
    qkv_across = swapped(along, "blk", 1)
    next_columns = jnp.concatenate(list(qkv_columns(qkv_weight[1], None)), axis=1)
    qkv_across, dense_near, next_columns = tied(qkv_across, dense_near, next_columns)
    across, beside = swapped(dense_near, "blk", 1), swapped(dense_near, "head", 2)
    next_both = along_batch(jnp.stack([next_columns, dense_own[1]]))
    weight, gains = assemble_columns(along, qkv_across, part3)
    qkvs = [weight]
    gains = gains.T.astype(F32)

    kept, denses = [], []
    for layer in range(layers):
        normed, factor_one = normalize(stream, gains[layer])
        if layer == 1:
            normed = normed.astype(BF16)
            far, near = swapped(normed, "head", 2), other_core(normed)
            far, next_across, dense_next = tied(far, next_across, dense_next)
            across, beside = swapped(dense_next, "blk", 1), swapped(dense_next, "head", 2)
            token_pieces = (normed, near, far, other_core(far))
            qkvs.append(assemble_wide(next_along, next_across, part3))
        normed_all, projected = project(
            token_pieces, gains[layer], qkvs[layer], layer == 0, token_rows
        )
        attended, log_total = attend_rows(
            projected, scale_vecs[layer], segments, 4, token_rows
        )
        attended, across, beside = tied(attended, across, beside)
        one, two = to_beside(across), to_across(beside)
        if layer == 0:
            two, next_both = tied(two, next_both)
            next_along, dense_next = next_both[:, 0], next_both[:, 1]
            next_across = swapped(next_along, "blk", 1)
            attended_t, one, two = tied(over_head(attended), one, two)
        else:
            dense_near = dense_next
            attended_t, one, two = tied(over_head(attended), one, two)
        pieces = (dense_near, across, beside, one, two)
        pieces += tuple(other_core(piece) for piece in pieces)
        attended_t = attended_t.reshape(width, -1)
        denses.append(assemble(pieces))
        dense = denses[layer]
        out_w, up_w, down_w = dense[:, :width], dense[:, width:-width], dense[:, -width:]
        middle = stream + dot_rows(attended_t, out_w)
        normed_two, factor_two = normalize(middle, gains[layers + layer])
        normed_two = normed_two.astype(BF16)
        hidden = dot(normed_two, up_w)
        active = (hidden * jax.nn.sigmoid(hidden)).astype(BF16)
        kept.append(
            (
                stream, factor_one, normed_all, projected, log_total, attended_t, middle,
                factor_two, normed_two, hidden, active,
            )
        )
        stream = middle + dot(active, down_w)
    layer_out = swap_halves(stream.astype(BF16).reshape(tokens.shape))
    upper = upper.reshape(-1, width).astype(F32)

    scale_grads = [None] * layers
    for layer in reversed(range(layers)):
        (
            stream, factor_one, normed_all, projected, log_total, attended_t, middle,
            factor_two, normed_two, hidden, active,
        ) = kept[layer]
        qkv, dense = qkvs[layer], denses[layer]
        out_w, up_w, down_w = dense[:, :width], dense[:, width:-width], dense[:, -width:]
        down_bar = upper.astype(BF16)
        gate = jax.nn.sigmoid(hidden)
        up_bar = (
            dot_cols(down_bar, down_w) * gate * (1.0 + hidden * (1.0 - gate))
        ).astype(BF16)
        middle_grad = upper + lower_of(
            dot_cols(up_bar, up_w), middle, factor_two, gains[layers + layer]
        )
        out_bar = middle_grad.astype(BF16)
        if layer == 0:
            attended_grad = over_head(heads_grad(out_w, out_bar))
            grads, others = dense_grads(attended_t, normed_two, active, out_bar, up_bar, down_bar)
            others, across = tied(others, across)
            others, own = tied(others, own_quarter(cored) + across.astype(F32))
            attended_grad, others, z_sum, beside = tied(attended_grad, others, z_sum, beside)
            others = other_core(others)
            attended_grad, summed = tied(attended_grad, own_sum(own, beside))
            summed = over_batch(summed)
            earlier = across_sum(z_sum)
        else:
            attended_grad = over_head(heads_grad(out_w, out_bar))
            grads, others = dense_grads(attended_t, normed_two, active, out_bar, up_bar, down_bar)
            attended_grad, others, layer_out = tied(attended_grad, others, layer_out)
            others = other_core(others)
        bars, scale_grads[layer] = attend_back_rows(
            projected, attended_grad, log_total, scale_vecs[layer], segments, token_rows
        )
        if layer == 0:
            bars, earlier = tied(bars, earlier)
            qkv_grad = weight_back(bars, normed_all)
            bars, qkv_grad, others = tied(bars, qkv_grad, others)
            z_sum = over_batch(qkv_grad.reshape(4, 2, -1, qkv_grad.shape[-1]))
            cored = (grads, others)
            bars, rows = tied(bars, diagonal_rows(cored))
            diagonal = sent_beside_and_across(*rows)
            halves, to_core = rows_back(bars, qkv, token_rows)
            scale_sum = sum_over(jnp.stack(scale_grads), ("head", 1))
            halves, to_core, diagonal, summed, scale_sum = tied(
                halves, to_core, diagonal, summed, scale_sum
            )
            scale_sum = sum_over(scale_sum, ("head", 2))
            halves, to_core, rows, scale_sum = tied(
                halves, to_core, neighbour_rows(cored, *diagonal), scale_sum
            )
            sent = sent_beside_and_across(*rows)
            halves = halves + other_core(to_core).astype(F32)
            scale_sum = sum_over(scale_sum, ("batch", 1), ("batch", 2), ("blk", 1))
            own = own_quarter(cored)
            halves, sent, z_sum, scale_sum, own = tied(halves, sent, z_sum, scale_sum, own)
            halves, own, earlier = tied(halves, own_sum(own, *sent), earlier)
            moved = over_head(earlier.reshape(4, -1, earlier.shape[-1]))
            dense_first = over_batch(own)
            normed_grad = scatter_row(halves)
            z_across, dense_first = tied(across_sum(z_sum), dense_first)
            z_across = over_head(z_across.reshape(4, -1, z_across.shape[-1]))
            dense_grad = [dense_first, summed]
            qkv_grads = [columns_to_rows(z_across), columns_to_rows(moved)]
        else:
            bars, others = tied(bars, others)
            cored = (grads, others)
            bars, rows = tied(bars, diagonal_rows(cored))
            diagonal = sent_beside_and_across(*rows)
            halves, to_core, qkv_grad = project_back(bars, qkv, normed_all, token_rows)
            z_sum = over_batch(qkv_grad.reshape(4, 2, -1, qkv_grad.shape[-1]))
            to_core, halves, diagonal = tied(to_core, halves, diagonal)
            to_core, rows = tied(to_core, neighbour_rows(cored, *diagonal))
            across = swapped(rows[0], "blk", 1)
            halves = halves + other_core(to_core).astype(F32)
            normed_grad = scatter_row(halves)
            normed_grad, beside = tied(normed_grad, rows[1])
            beside = swapped(beside, "head", 2)
        upper = middle_grad + lower_of(normed_grad, stream, factor_one, gains[layer])
    input_grad = swap_halves(upper.astype(BF16).reshape(tokens.shape)).astype(F32)
    scale_grad = scale_sum * (SCALE_BASE / math.sqrt(head_dim)) * jax.nn.sigmoid(scale_param)
    dense_all = jnp.stack([part.astype(F32) for part in dense_grad])
    qkv_all = jnp.stack(qkv_grads)
    up_all = dense_all[:, :, width:-width]
    return (
        layer_out,
        input_grad,
        qkv_all,
        dense_all[:, :, :width],
        up_all,
        dense_all[:, :, -width:],
        gain_back(qkv_weight, qkv_all, attn_gain),
        gain_back(up_weight, up_all, mlp_gain),
        scale_grad,
    )


def per_device(*args):
    tokens, segments = args[0], args[1]
    sizes = tuple(lax.axis_size(axis) for axis in ALL)
    heads = tokens.shape[2] // args[8].shape[1]
    spread = (
        sizes == (4, 2, 4)
        and tokens.shape[0] == 2
        and args[2].shape[0] == 2
        and tokens.shape[1] % 128 == 0
        and Q_ROWS % tokens.shape[1] == 0
        and segments.shape[1] <= WINDOW
        and segments.shape[1] % FORWARD_ROWS == 0
        and heads % 4 == 0
        and tokens.shape[2] % 256 == 0
    )
    return spread_device(*args) if spread else general_device(*args)


def solution(mesh):
    rows = P(None, ALL, None)
    by_token = P("batch", ("blk", "head"), None)
    return jax.shard_map(
        per_device,
        mesh=mesh,
        in_specs=(
            by_token, P("batch", None), rows, rows, rows, rows, P(None, ALL), P(None, ALL), P(),
            by_token,
        ),
        out_specs=(
            by_token, by_token, rows, rows, rows, rows, P(None, ALL), P(None, ALL), P(),
        ),
        check_vma=False,
    )
```

```python
import functools
import math

import jax
import jax.numpy as jnp
from jax import lax
from jax.experimental import pallas as pl
from jax.experimental.pallas import tpu as pltpu
from jax.sharding import PartitionSpec as P

WINDOW = 1024
EPSILON = 1e-06
SCALE_BASE = 1.4426950408889634
MASKED_SCORE = -1e30

ALL = ("batch", "blk", "head")
REST = ("batch", "blk")
F32 = jnp.float32
BF16 = jnp.bfloat16


def shifted(block, axis, distance):
    devices = range(lax.axis_size(axis))
    route = [(i - distance, i) for i in devices if i - distance in devices]
    return lax.ppermute(block, axis, route)


NT = (((1,), (1,)), ((), ()))
TN = (((0,), (0,)), ((), ()))


def dot(left, right):
    return jnp.dot(left, right, preferred_element_type=F32)


def dot_rows(left, right):
    return lax.dot_general(left, right, (((0,), (0,)), ((), ())), preferred_element_type=F32)


def dot_cols(left, right):
    return lax.dot_general(left, right, (((1,), (1,)), ((), ())), preferred_element_type=F32)


def normalize(stream, gain):
    factor = lax.rsqrt(jnp.mean(stream * stream, axis=-1, keepdims=True) + EPSILON)
    return stream * factor * gain, factor


def norm_back(upper, stream, factor, gain):
    inner = upper * gain
    gain_grad = jnp.sum(upper * stream * factor, axis=0)
    lower = factor * inner - stream * factor * factor * factor * jnp.mean(
        inner * stream, axis=-1, keepdims=True
    )
    return lower, gain_grad


class Plan:
    def __init__(self, tokens):
        self.seqs, self.rows, self.width = tokens.shape
        self.heads = lax.axis_size("head")
        self.blks = lax.axis_size("blk")
        self.block = self.rows * self.heads
        self.whole = self.seqs % self.blks == 0
        if self.whole:
            self.groups, self.own_seqs = self.blks, self.seqs // self.blks
            self.reach = 0
        else:
            self.groups, self.own_seqs = 1, self.seqs
            self.reach = min((WINDOW - 1) // self.block + 1, self.blks - 1)
        self.length = self.groups * self.block
        self.tokens = self.seqs * self.rows


def to_plan(plan, array):
    if plan.whole and plan.blks > 1:
        array = lax.all_to_all(array, "blk", split_axis=0, concat_axis=0, tiled=True)
    return array.reshape(plan.tokens, plan.width)


def from_plan(plan, flat):
    array = flat.reshape(plan.seqs, plan.rows, plan.width)
    if plan.whole and plan.blks > 1:
        array = lax.all_to_all(array, "blk", split_axis=0, concat_axis=0, tiled=True)
    return array


def in_sequence(plan, by_head, width):
    parts = by_head.reshape(plan.heads, plan.groups, plan.own_seqs, plan.rows, width)
    return parts.transpose(2, 1, 0, 3, 4).reshape(-1, width)


def by_owner(plan, rows, width):
    parts = rows.reshape(plan.own_seqs, plan.groups, plan.heads, plan.rows, width)
    return parts.transpose(2, 1, 0, 3, 4).reshape(plan.heads, plan.tokens, width)


def gather_tokens(plan, rows):
    moved = lax.all_gather(rows, "head", axis=0, tiled=False)
    return in_sequence(plan, moved, rows.shape[-1])


def scatter_tokens(plan, rows):
    width = rows.shape[-1]
    return lax.psum_scatter(
        by_owner(plan, rows.astype(BF16), width), "head", scatter_dimension=0, tiled=False
    ).astype(F32)


def heads_to_tokens(plan, rows):
    part = rows.shape[-1]
    moved = lax.all_to_all(
        by_owner(plan, rows, part), "head", split_axis=0, concat_axis=0, tiled=True
    )
    return moved.transpose(1, 0, 2).reshape(plan.tokens, plan.heads * part)


def tokens_to_heads(plan, rows):
    part = rows.shape[-1] // plan.heads
    sent = rows.reshape(plan.tokens, plan.heads, part).transpose(1, 0, 2)
    moved = lax.all_to_all(sent, "head", split_axis=0, concat_axis=0, tiled=True)
    return in_sequence(plan, moved, part)


def gather_qkv(rows):
    own, width = rows.shape
    heads = lax.axis_size("head")
    part = width // 3 // heads
    sent = rows.reshape(own, 3, heads, part).transpose(2, 0, 1, 3).reshape(heads, own, 3 * part)
    moved = lax.all_to_all(sent, "head", split_axis=0, concat_axis=0, tiled=True)
    full = lax.all_gather(moved, REST, axis=0, tiled=True)
    return full.reshape(-1, 3 * part)


def scatter_qkv(grad):
    heads = lax.axis_size("head")
    part = grad.shape[1] // 3
    summed = lax.psum_scatter(grad.astype(BF16), REST, scatter_dimension=0, tiled=True)
    own = summed.shape[0] // heads
    moved = lax.all_to_all(
        summed.reshape(heads, own, 3 * part), "head", split_axis=0, concat_axis=0, tiled=True
    )
    return (
        moved.reshape(heads, own, 3, part)
        .transpose(1, 2, 0, 3)
        .reshape(own, 3 * heads * part)
        .astype(F32)
    )


def window_mask(plan, segments, block_index):
    key_count = plan.length + plan.reach * plan.block
    if plan.whole:
        query_segs, key_segs = segments, segments
    else:
        leading = jnp.full((plan.own_seqs, plan.reach * plan.block), -1, jnp.int32)
        padded = jnp.concatenate([leading, segments], axis=1)
        start = block_index * plan.block
        query_segs = lax.dynamic_slice_in_dim(segments, start, plan.block, 1)
        key_segs = lax.dynamic_slice_in_dim(padded, start, key_count, 1)
    query_place = jnp.arange(plan.length, dtype=jnp.int32)[:, None] + plan.reach * plan.block
    key_place = jnp.arange(key_count, dtype=jnp.int32)[None, :]
    near = (key_place <= query_place) & (query_place - key_place < WINDOW)
    return (key_segs[:, None, :] == query_segs[:, :, None]) & near[None]


def with_earlier(plan, own):
    arrived = [own]
    for _ in range(plan.reach):
        arrived.append(shifted(arrived[-1], "blk", 1))
    return jnp.concatenate(arrived[::-1], axis=1) if plan.reach else own


def to_earlier(plan, grads):
    if not plan.reach:
        return grads
    block = plan.block
    total = grads[:, :block]
    for step in range(1, plan.reach + 1):
        total = (
            shifted(total.astype(BF16), "blk", -1).astype(F32)
            + grads[:, step * block : (step + 1) * block]
        )
    return total


def scores_of(queries, keys, allowed):
    scores = jnp.einsum("sqhd,skhd->shqk", queries, keys, preferred_element_type=F32)
    return jnp.where(allowed[:, None], scores, MASKED_SCORE)


def attend(queries, keys, values, allowed):
    scores = scores_of(queries, keys, allowed)
    top_score = jnp.max(scores, axis=-1, keepdims=True)
    exp_terms = jnp.exp(scores - top_score)
    totals = jnp.sum(exp_terms, axis=-1, keepdims=True)
    probs_low = (exp_terms / totals).astype(BF16)
    attended = jnp.einsum("shqk,skhd->sqhd", probs_low, values, preferred_element_type=F32)
    return attended, top_score + jnp.log(totals)


def attend_back(queries, keys, values, allowed, log_total, attended_grad):
    probs = jnp.exp(scores_of(queries, keys, allowed) - log_total)
    probs_low = probs.astype(BF16)
    values_grad = jnp.einsum(
        "shqk,sqhd->skhd", probs_low, attended_grad, preferred_element_type=F32
    )
    probs_grad = jnp.einsum("sqhd,skhd->shqk", attended_grad, values, preferred_element_type=F32)
    row_dot = jnp.sum(probs_grad * probs, axis=-1, keepdims=True)
    scores_low = (probs * (probs_grad - row_dot)).astype(BF16)
    queries_grad = jnp.einsum("shqk,skhd->sqhd", scores_low, keys, preferred_element_type=F32)
    keys_grad = jnp.einsum("shqk,sqhd->skhd", scores_low, queries, preferred_element_type=F32)
    return queries_grad, keys_grad, values_grad


def forward(plan, stream, qkv, dense, gains, scale_vec, allowed):
    width = plan.width
    head_dim = scale_vec.shape[0]
    part = qkv.shape[1] // 3
    local_heads = part // head_dim
    split = (plan.own_seqs, plan.length, local_heads, head_dim)
    out_w, up_w, down_w = dense[:, :width], dense[:, width:-width], dense[:, -width:]
    normed, factor_one = normalize(stream, gains[0])
    normed_all = gather_tokens(plan, normed.astype(BF16))
    projected = dot(normed_all, qkv)
    query_pre = projected[:, :part].reshape(split)
    queries = (query_pre * scale_vec).astype(BF16)
    keys = with_earlier(plan, projected[:, part : 2 * part].astype(BF16).reshape(split))
    values = with_earlier(plan, projected[:, 2 * part :].astype(BF16).reshape(split))
    attended_part, log_total = attend(queries, keys, values, allowed)
    attended = heads_to_tokens(plan, attended_part.astype(BF16).reshape(-1, part))
    middle = stream + dot(attended, out_w)
    normed_two, factor_two = normalize(middle, gains[1])
    normed_two = normed_two.astype(BF16)
    hidden = dot(normed_two, up_w)
    active = (hidden * jax.nn.sigmoid(hidden)).astype(BF16)
    result = middle + dot(active, down_w)
    kept = (
        stream, factor_one, normed_all, query_pre, queries, keys, values, log_total,
        attended, middle, factor_two, normed_two, hidden, active,
    )
    return result, kept


def backward(plan, upper, kept, qkv, dense, gains, scale_vec, allowed):
    (
        stream, factor_one, normed_all, query_pre, queries, keys, values, log_total,
        attended, middle, factor_two, normed_two, hidden, active,
    ) = kept
    width = plan.width
    head_dim = scale_vec.shape[0]
    part = qkv.shape[1] // 3
    out_w, up_w, down_w = dense[:, :width], dense[:, width:-width], dense[:, -width:]
    upper_low = upper.astype(BF16)
    down_grad = dot_rows(active, upper_low)
    active_grad = dot_cols(upper_low, down_w)
    gate = jax.nn.sigmoid(hidden)
    hidden_low = (active_grad * gate * (1.0 + hidden * (1.0 - gate))).astype(BF16)
    up_grad = dot_rows(normed_two, hidden_low)
    extra_two, mlp_gain_grad = norm_back(dot_cols(hidden_low, up_w), middle, factor_two, gains[1])
    middle_grad = upper + extra_two
    middle_low = middle_grad.astype(BF16)
    out_grad = dot_rows(attended, middle_low)
    dense_grad = jnp.concatenate([out_grad, up_grad, down_grad], axis=1).astype(BF16)
    dense_own = lax.psum_scatter(dense_grad, ALL, scatter_dimension=0, tiled=True)
    attended_grad = tokens_to_heads(plan, dot_cols(middle_low, out_w).astype(BF16))
    queries_grad, keys_grad, values_grad = attend_back(
        queries, keys, values, allowed, log_total, attended_grad.reshape(queries.shape)
    )
    query_bar = queries_grad.astype(BF16).astype(F32)
    scale_vec_grad = jnp.sum((query_bar * query_pre).reshape(-1, head_dim), axis=0)
    query_low = (query_bar * scale_vec).astype(BF16).reshape(-1, part)
    keys_low = to_earlier(plan, keys_grad).astype(BF16).reshape(-1, part)
    values_low = to_earlier(plan, values_grad).astype(BF16).reshape(-1, part)
    projected_low = jnp.concatenate([query_low, keys_low, values_low], axis=1)
    normed_grad = scatter_tokens(plan, dot_cols(projected_low, qkv))
    qkv_own = scatter_qkv(dot_rows(normed_all, projected_low))
    extra_one, attn_gain_grad = norm_back(normed_grad, stream, factor_one, gains[0])
    lower = middle_grad + extra_one
    return lower, qkv_own, dense_own, (attn_gain_grad, mlp_gain_grad), scale_vec_grad


def general_device(
    tokens,
    segments,
    qkv_weight,
    out_weight,
    up_weight,
    down_weight,
    attn_gain,
    mlp_gain,
    scale_param,
    cotangent,
):
    plan = Plan(tokens)
    layers, head_dim = scale_param.shape
    block_index = lax.axis_index("blk")
    scale_vecs = SCALE_BASE / math.sqrt(head_dim) * jax.nn.softplus(scale_param)
    own_gains = jnp.concatenate([attn_gain, mlp_gain], axis=0)
    gains = (
        lax.all_gather(own_gains.reshape(1, -1), ALL, axis=0, tiled=True)
        .reshape(-1, 2 * layers, attn_gain.shape[1])
        .transpose(1, 0, 2)
        .reshape(2 * layers, plan.width)
        .astype(F32)
    )
    if plan.whole:
        segments = lax.dynamic_slice_in_dim(
            segments, block_index * plan.own_seqs, plan.own_seqs, 0
        )
    allowed = window_mask(plan, segments, block_index)
    stream = to_plan(plan, tokens).astype(F32)
    qkvs, denses, kept = [], [], []
    for layer in range(layers):
        qkvs.append(gather_qkv(qkv_weight[layer]))
        own = jnp.concatenate([out_weight[layer], up_weight[layer], down_weight[layer]], axis=1)
        denses.append(lax.all_gather(own, ALL, axis=0, tiled=True))
        layer_gains = (gains[layer], gains[layers + layer])
        stream, saved = forward(
            plan, stream, qkvs[layer], denses[layer], layer_gains, scale_vecs[layer], allowed
        )
        kept.append(saved)
    layer_out = from_plan(plan, stream.astype(BF16))
    upper = to_plan(plan, cotangent).astype(F32)
    qkv_grads, dense_grads = [None] * layers, [None] * layers
    gain_grads, scale_grads = [None] * layers, [None] * layers
    for layer in reversed(range(layers)):
        layer_gains = (gains[layer], gains[layers + layer])
        upper, qkv_grads[layer], dense_grads[layer], gain_grads[layer], scale_grads[layer] = (
            backward(
                plan, upper, kept[layer], qkvs[layer], denses[layer], layer_gains,
                scale_vecs[layer], allowed,
            )
        )
    input_grad = from_plan(plan, upper.astype(BF16)).astype(F32)
    small = jnp.concatenate(
        [g[0] for g in gain_grads] + [g[1] for g in gain_grads] + scale_grads, axis=0
    )
    total = lax.psum(small, ALL)
    gain_total = total[: 2 * layers * plan.width].reshape(2 * layers, plan.width)
    owner = lax.axis_index(ALL)
    gain_rows = attn_gain.shape[1]
    own_total = lax.dynamic_slice_in_dim(gain_total, owner * gain_rows, gain_rows, 1)
    scale_total = total[2 * layers * plan.width :].reshape(layers, head_dim)
    scale_grad = scale_total * (SCALE_BASE / math.sqrt(head_dim)) * jax.nn.sigmoid(scale_param)
    dense_all = jnp.stack(dense_grads).astype(F32)
    width = plan.width
    return (
        layer_out,
        input_grad,
        jnp.stack(qkv_grads),
        dense_all[:, :, :width],
        dense_all[:, :, width:-width],
        dense_all[:, :, -width:],
        own_total[:layers],
        own_total[layers:],
        scale_grad,
    )


Q_ROWS = 256
KERNEL = pltpu.CompilerParams(vmem_limit_bytes=24 * 1024 * 1024)
LIGHT = pl.CostEstimate(flops=1 << 20, bytes_accessed=1 << 20, transcendentals=0)


def in_hbm(*arrays):
    return [pltpu.with_memory_space_constraint(array, pltpu.HBM) for array in arrays]


def allowed_keys(col, row, first):
    count = first + row.shape[1]
    key_place = lax.broadcasted_iota(jnp.int32, (count, row.shape[1]), 0)
    query_place = lax.broadcasted_iota(jnp.int32, (count, row.shape[1]), 1) + first
    return (col[:count] == row) & (key_place <= query_place)


def allowed_piece(col, row, start, first):
    same = col == row
    if start + col.shape[0] <= first:
        return same
    key_place = lax.broadcasted_iota(jnp.int32, same.shape, 0) + start
    return same & (key_place <= lax.broadcasted_iota(jnp.int32, same.shape, 1) + first)


def token_places(length, heads, token_rows, block_rows=Q_ROWS):
    for first in range(0, length, block_rows):
        parts = []
        for start in range(0, block_rows, token_rows):
            place = (first + start) // token_rows
            parts.append((start, place % heads, place // heads * token_rows))
        yield first, parts


FORWARD_ROWS, FORWARD_KEYS = 1024, 512


def attend_kernel(token_rows, proj_ref, scale_ref, col_ref, row_ref, out_ref, lse_ref):
    length = proj_ref.shape[-1]
    queries = (proj_ref[0, 0] * scale_ref[...]).astype(BF16)
    keys = proj_ref[1, 0].T.astype(BF16)
    values = proj_ref[2, 0].astype(BF16)
    for first, parts in token_places(length, out_ref.shape[0], token_rows, FORWARD_ROWS):
        end = first + FORWARD_ROWS
        block, row = queries[:, first:end], row_ref[:, first:end]
        pieces = []
        for start in range(0, end, FORWARD_KEYS):
            scores = jnp.dot(keys[start : start + FORWARD_KEYS], block, preferred_element_type=F32)
            allowed = allowed_piece(col_ref[start : start + FORWARD_KEYS], row, start, first)
            pieces.append(jnp.where(allowed, scores, MASKED_SCORE))
        top = functools.reduce(
            jnp.maximum, [jnp.max(piece, axis=0, keepdims=True) for piece in pieces]
        )
        total, attended = 0.0, 0.0
        for i, piece in enumerate(pieces):
            terms = jnp.exp(piece - top)
            total += jnp.sum(terms, axis=0, keepdims=True)
            attended += jnp.dot(
                values[:, i * FORWARD_KEYS : (i + 1) * FORWARD_KEYS],
                terms.astype(BF16),
                preferred_element_type=F32,
            )
        attended = (attended * (1.0 / total)).astype(BF16)
        lse_ref[0, :, first:end] = top + jnp.log(total)
        for start, owner, offset in parts:
            out_ref[owner, 0, :, offset : offset + token_rows] = attended[
                :, start : start + token_rows
            ]


def attend_rows(projected, scale_vec, segments, owners, token_rows):
    head_dim = scale_vec.shape[0]
    length = projected.shape[1]
    local_heads = projected.shape[0] // 3 // head_dim
    tokens = length // owners
    attended, log_total = pl.pallas_call(
        functools.partial(attend_kernel, token_rows),
        grid=(local_heads,),
        in_specs=[
            pl.BlockSpec((3, 1, head_dim, length), lambda h: (0, h, 0, 0)),
            pl.BlockSpec((head_dim, 1), lambda h: (0, 0)),
            pl.BlockSpec((length, 1), lambda h: (0, 0)),
            pl.BlockSpec((1, length), lambda h: (0, 0)),
        ],
        out_specs=[
            pl.BlockSpec((owners, 1, head_dim, tokens), lambda h: (0, h, 0, 0)),
            pl.BlockSpec((1, 1, length), lambda h: (h, 0, 0)),
        ],
        out_shape=[
            jax.ShapeDtypeStruct((owners, local_heads, head_dim, tokens), BF16),
            jax.ShapeDtypeStruct((local_heads, 1, length), F32),
        ],
        compiler_params=KERNEL,
        cost_estimate=LIGHT,
    )(
        projected.reshape(3, local_heads, head_dim, length),
        scale_vec.reshape(head_dim, 1),
        segments.reshape(length, 1),
        segments.reshape(1, length),
    )
    return attended.reshape(owners, local_heads * head_dim, tokens), log_total


def attend_back_kernel(
    token_rows,
    proj_ref,
    grad_ref,
    lse_ref,
    scale_ref,
    col_ref,
    row_ref,
    out_ref,
    scale_grad_ref,
    keys_acc,
    values_acc,
):
    length = proj_ref.shape[-1]
    scale = scale_ref[...]
    query_pre = proj_ref[0, 0]
    queries = (query_pre * scale).astype(BF16)
    keys_t = proj_ref[1, 0].astype(BF16)
    keys = proj_ref[1, 0].T.astype(BF16)
    values = proj_ref[2, 0].T.astype(BF16)
    keys_acc[...] = jnp.zeros_like(keys_acc)
    values_acc[...] = jnp.zeros_like(values_acc)
    scale_grad = jnp.zeros((scale.shape[0], 1), F32)
    for first, parts in token_places(length, grad_ref.shape[0], token_rows):
        end = first + Q_ROWS
        block = queries[:, first:end]
        grad = jnp.concatenate(
            [grad_ref[owner, 0, :, at : at + token_rows] for _, owner, at in parts], axis=1
        )
        scores = jnp.dot(keys[:end], block, preferred_element_type=F32)
        allowed = allowed_keys(col_ref[...], row_ref[:, first:end], first)
        scores = jnp.where(allowed, scores, MASKED_SCORE)
        probs = jnp.exp(scores - lse_ref[0, :, first:end])
        probs_grad = jnp.dot(values[:end], grad, preferred_element_type=F32)
        row_dot = jnp.sum(probs_grad * probs, axis=0, keepdims=True)
        scores_low = (probs * (probs_grad - row_dot)).astype(BF16)
        values_acc[:, :end] += lax.dot_general(
            grad, probs.astype(BF16), NT, preferred_element_type=F32
        )
        keys_acc[:, :end] += lax.dot_general(
            block, scores_low, NT, preferred_element_type=F32
        )
        query_bar = jnp.dot(keys_t[:, :end], scores_low, preferred_element_type=F32)
        query_bar = query_bar.astype(BF16).astype(F32)
        scale_grad += jnp.sum(query_bar * query_pre[:, first:end], axis=1, keepdims=True)
        out_ref[0, 0, :, first:end] = (query_bar * scale).astype(BF16)
    out_ref[1, 0] = keys_acc[...].astype(BF16)
    out_ref[2, 0] = values_acc[...].astype(BF16)
    spread = jnp.broadcast_to(scale_grad, scale_grad_ref.shape)

    @pl.when(pl.program_id(0) == 0)
    def _():
        scale_grad_ref[...] = spread

    @pl.when(pl.program_id(0) > 0)
    def _():
        scale_grad_ref[...] += spread


def attend_back_rows(projected, attended_grad, log_total, scale_vec, segments, token_rows):
    head_dim = scale_vec.shape[0]
    length = projected.shape[1]
    local_heads = projected.shape[0] // 3 // head_dim
    owners, _, tokens = attended_grad.shape
    lanes = 128
    grads, scale_grad = pl.pallas_call(
        functools.partial(attend_back_kernel, token_rows),
        grid=(local_heads,),
        in_specs=[
            pl.BlockSpec((3, 1, head_dim, length), lambda h: (0, h, 0, 0)),
            pl.BlockSpec((owners, 1, head_dim, tokens), lambda h: (0, h, 0, 0)),
            pl.BlockSpec((1, 1, length), lambda h: (h, 0, 0)),
            pl.BlockSpec((head_dim, 1), lambda h: (0, 0)),
            pl.BlockSpec((length, 1), lambda h: (0, 0)),
            pl.BlockSpec((1, length), lambda h: (0, 0)),
        ],
        out_specs=[
            pl.BlockSpec((3, 1, head_dim, length), lambda h: (0, h, 0, 0)),
            pl.BlockSpec((head_dim, lanes), lambda h: (0, 0)),
        ],
        out_shape=[
            pltpu.HBM((3, local_heads, head_dim, length), BF16),
            pltpu.HBM((head_dim, lanes), F32),
        ],
        scratch_shapes=[
            pltpu.VMEM((head_dim, length), F32),
            pltpu.VMEM((head_dim, length), F32),
        ],
        compiler_params=KERNEL,
        cost_estimate=LIGHT,
    )(
        *in_hbm(
            projected.reshape(3, local_heads, head_dim, length),
            attended_grad.reshape(owners, local_heads, head_dim, tokens),
        ),
        log_total,
        scale_vec.reshape(head_dim, 1),
        segments.reshape(length, 1),
        segments.reshape(1, length),
    )
    return grads.reshape(3 * local_heads * head_dim, length), scale_grad[:, 0]


def dense_grad_kernel(
    core_ref, attended_ref, normed_ref, active_ref, out_bar, up_bar, down_bar,
    own_ref, other_ref, normed_t, active_t,
):
    tile = pl.program_id(0)
    rows, width = 8 * own_ref.shape[3], out_bar.shape[1]

    @pl.when(tile == 0)
    def _():
        normed_t[...] = normed_ref[...].astype(F32).T.astype(BF16)
        active_t[...] = active_ref[...].astype(F32).T.astype(BF16)

    start = pl.multiple_of(tile * rows, rows)
    first_core = core_ref[2] == 0
    lefts = (attended_ref, normed_t, active_t)
    for i, (left, right) in enumerate(zip(lefts, (out_bar, up_bar, down_bar))):
        grad = jnp.dot(left[pl.ds(start, rows), :], right[...], preferred_element_type=F32)
        grad = grad.reshape(2, 2, 2, rows // 8, width)
        one, two = grad[:, :, 0], grad[:, :, 1]
        own_ref[:, :, 0, :, i * width : (i + 1) * width] = jnp.where(
            first_core, one, two
        ).astype(BF16)
        other_ref[:, :, 0, :, i * width : (i + 1) * width] = jnp.where(
            first_core, two, one
        ).astype(BF16)


def dense_grads(attended_t, normed, active, out_bar, up_bar, down_bar):
    width, tokens = attended_t.shape
    own = width // 32
    whole = pl.BlockSpec((tokens, width), lambda i, core: (0, 0))
    rows = pl.BlockSpec((2, 2, 1, own, 3 * width), lambda i, core: (0, 0, i, 0, 0))
    shape = pltpu.HBM((2, 2, 4, own, 3 * width), BF16)
    return pl.pallas_call(
        dense_grad_kernel,
        grid_spec=pltpu.PrefetchScalarGridSpec(
            num_scalar_prefetch=1,
            grid=(4,),
            in_specs=[pl.BlockSpec((width, tokens), lambda i, core: (0, 0))] + [whole] * 5,
            out_specs=[rows, rows],
            scratch_shapes=[pltpu.VMEM((width, tokens), BF16)] * 2,
        ),
        out_shape=[shape, shape],
        compiler_params=KERNEL,
        cost_estimate=LIGHT,
    )(place(), *in_hbm(attended_t, normed, active, out_bar, up_bar, down_bar))


def place():
    head = lax.axis_index("head")
    return jnp.stack([lax.axis_index("blk"), head // 2, head % 2]).astype(jnp.int32)


def assemble_kernel(place_ref, *refs):
    pieces, whole_ref = refs[:10], refs[10]
    half = whole_ref.shape[-1] // 2
    blk, row, core = place_ref[0], place_ref[1], place_ref[2]
    for i in range(2):
        at_core = core if i == 0 else 1 - core
        own, across, beside, one, two = pieces[5 * i : 5 * i + 5]
        whole_ref[0, blk, row, at_core] = own[0]
        whole_ref[0, 1 - blk, row, at_core] = across[0]
        whole_ref[0, blk, 1 - row, at_core] = beside[0]
        whole_ref[0, 1 - blk, 1 - row, at_core, :, :half] = one[0]
        whole_ref[0, 1 - blk, 1 - row, at_core, :, half:] = two[0]


def assemble(pieces):
    batch, own, columns = pieces[0].shape
    specs = [
        pl.BlockSpec((1, own, piece.shape[-1]), lambda i, at: (i, 0, 0))
        for piece in pieces
    ]
    whole = pl.pallas_call(
        assemble_kernel,
        grid_spec=pltpu.PrefetchScalarGridSpec(
            num_scalar_prefetch=1,
            grid=(batch,),
            in_specs=specs,
            out_specs=pl.BlockSpec((1, 2, 2, 2, own, columns), lambda i, at: (i, 0, 0, 0, 0, 0)),
        ),
        out_shape=jax.ShapeDtypeStruct((batch, 2, 2, 2, own, columns), BF16),
        compiler_params=KERNEL,
        cost_estimate=LIGHT,
    )(place(), *pieces)
    return whole.reshape(-1, columns)


def assemble_columns_kernel(place_ref, along_ref, across_ref, whole_ref, *extra_ref):
    blk = place_ref[0]
    columns = whole_ref.shape[-1]
    whole_ref[0, blk] = along_ref[0, :, :columns]
    whole_ref[0, 1 - blk] = across_ref[0, :, :columns]
    for extra in extra_ref:
        extra[0, blk] = along_ref[0, :, columns:]
        extra[0, 1 - blk] = across_ref[0, :, columns:]


def assemble_columns(along, across, columns):
    batch, own, both = along.shape
    rows = pl.BlockSpec((1, own, both), lambda i, at: (i, 0, 0))
    shapes = [(batch, 2, own, columns)]
    if both > columns:
        shapes.append((batch, 2, own, both - columns))
    parts = pl.pallas_call(
        assemble_columns_kernel,
        grid_spec=pltpu.PrefetchScalarGridSpec(
            num_scalar_prefetch=1,
            grid=(batch,),
            in_specs=[rows, rows],
            out_specs=[pl.BlockSpec((1,) + s[1:], lambda i, at: (i, 0, 0, 0)) for s in shapes],
        ),
        out_shape=[pltpu.HBM(s, BF16) for s in shapes],
        compiler_params=KERNEL,
        cost_estimate=LIGHT,
    )(place(), *in_hbm(along, across))
    return [part.reshape(-1, part.shape[-1]) for part in parts]


def assemble_wide_kernel(place_ref, along_ref, across_ref, whole_ref):
    blk = place_ref[0]
    own, columns = along_ref.shape[1], whole_ref.shape[-1]
    for i in range(along_ref.shape[-1] // columns):
        place, part = slice(i * own, (i + 1) * own), slice(i * columns, (i + 1) * columns)
        whole_ref[0, blk, place, :] = along_ref[0, :, part]
        whole_ref[0, 1 - blk, place, :] = across_ref[0, :, part]


def assemble_wide(along, across, columns):
    batch, own, wide = along.shape
    rows = own * (wide // columns)
    piece = pl.BlockSpec((1, own, wide), lambda i, at: (i, 0, 0))
    whole = pl.pallas_call(
        assemble_wide_kernel,
        grid_spec=pltpu.PrefetchScalarGridSpec(
            num_scalar_prefetch=1,
            grid=(batch,),
            in_specs=[piece, piece],
            out_specs=pl.BlockSpec((1, 2, rows, columns), lambda i, at: (i, 0, 0, 0)),
        ),
        out_shape=pltpu.HBM((batch, 2, rows, columns), BF16),
        compiler_params=KERNEL,
        cost_estimate=LIGHT,
    )(place(), *in_hbm(along, across))
    return whole.reshape(-1, columns)


def project_kernel(with_norm, place_ref, *refs):
    pieces, (gain_ref, weight_ref, normed_ref, projected_ref) = refs[:4], refs[4:]
    head = place_ref[1] * 2 + place_ref[2]
    rows = pieces[0].shape[0]
    for i, piece in enumerate(pieces):
        value = piece[...]
        if with_norm:
            stream = value.astype(F32)
            factor = lax.rsqrt(jnp.mean(stream * stream, axis=-1, keepdims=True) + EPSILON)
            value = (stream * factor * gain_ref[...]).astype(BF16)
        normed_ref[pl.ds(pl.multiple_of((head ^ i) * rows, rows), rows), :] = value
    projected = jnp.dot(normed_ref[...], weight_ref[...], preferred_element_type=F32)
    projected_ref[...] = projected.T


def project(pieces, gain, weight, with_norm, token_rows):
    tokens, width = pieces[0].shape
    length, columns = 4 * tokens, weight.shape[1]
    groups = tokens // token_rows
    piece = pl.BlockSpec((token_rows, width), lambda g, at: (g, 0))
    return pl.pallas_call(
        functools.partial(project_kernel, with_norm),
        grid_spec=pltpu.PrefetchScalarGridSpec(
            num_scalar_prefetch=1,
            grid=(groups,),
            in_specs=[piece] * 4
            + [
                pl.BlockSpec((1, width), lambda g, at: (0, 0)),
                pl.BlockSpec((width, columns), lambda g, at: (0, 0)),
            ],
            out_specs=[
                pl.BlockSpec((4 * token_rows, width), lambda g, at: (g, 0)),
                pl.BlockSpec((columns, 4 * token_rows), lambda g, at: (0, g)),
            ],
        ),
        out_shape=[
            pltpu.HBM((length, width), BF16),
            jax.ShapeDtypeStruct((columns, length), F32),
        ],
        compiler_params=KERNEL,
        cost_estimate=LIGHT,
    )(place(), *in_hbm(*pieces), gain.reshape(1, width), *in_hbm(weight))


def project_back_kernel(
    place_ref, bars_ref, weight_ref, normed_ref, own_ref, other_ref, grad_ref, bars_t
):
    @pl.when(pl.program_id(0) == 0)
    def _():
        bars_t[...] = bars_ref[...].astype(F32).T.astype(BF16)

    upper = lax.dot_general(bars_t[...], weight_ref[...], NT, preferred_element_type=F32)
    upper = upper.reshape(2, 2, 2, -1, upper.shape[-1])
    first_core = place_ref[2] == 0
    one, two = upper[:, :, 0], upper[:, :, 1]
    own_ref[...] = jnp.where(first_core, one, two)
    other_ref[...] = jnp.where(first_core, two, one).astype(BF16)
    grad = lax.dot_general(normed_ref[...], bars_t[...], TN, preferred_element_type=F32)
    grad_ref[...] = grad.astype(BF16)


def project_back(bars, weight, normed, token_rows):
    columns, length = bars.shape
    width = weight.shape[0]
    tile = width // 2
    quarter = pl.BlockSpec((2, 2, token_rows, tile), lambda i, at: (0, 0, 0, i))
    return pl.pallas_call(
        project_back_kernel,
        grid_spec=pltpu.PrefetchScalarGridSpec(
            num_scalar_prefetch=1,
            grid=(2,),
            in_specs=[
                pl.BlockSpec((columns, length), lambda i, at: (0, 0)),
                pl.BlockSpec((tile, columns), lambda i, at: (i, 0)),
                pl.BlockSpec((length, tile), lambda i, at: (0, i)),
            ],
            out_specs=[quarter, quarter, pl.BlockSpec((tile, columns), lambda i, at: (i, 0))],
            scratch_shapes=[pltpu.VMEM((length, columns), BF16)],
        ),
        out_shape=[
            pltpu.HBM((2, 2, token_rows, width), F32),
            pltpu.HBM((2, 2, token_rows, width), BF16),
            pltpu.HBM((width, columns), BF16),
        ],
        compiler_params=KERNEL,
        cost_estimate=LIGHT,
    )(place(), *in_hbm(bars, weight, normed))


def rows_back_kernel(place_ref, bars_ref, weight_ref, own_ref, other_ref, bars_t):
    @pl.when(pl.program_id(0) == 0)
    def _():
        bars_t[...] = bars_ref[...].astype(F32).T.astype(BF16)

    upper = lax.dot_general(bars_t[...], weight_ref[...], NT, preferred_element_type=F32)
    upper = upper.reshape(2, 2, 2, -1, upper.shape[-1])
    first_core = place_ref[2] == 0
    one, two = upper[:, :, 0], upper[:, :, 1]
    own_ref[...] = jnp.where(first_core, one, two)
    other_ref[...] = jnp.where(first_core, two, one).astype(BF16)


def rows_back(bars, weight, token_rows):
    columns, length = bars.shape
    width = weight.shape[0]
    tile = width // 2
    quarter = pl.BlockSpec((2, 2, token_rows, tile), lambda i, at: (0, 0, 0, i))
    return pl.pallas_call(
        rows_back_kernel,
        grid_spec=pltpu.PrefetchScalarGridSpec(
            num_scalar_prefetch=1,
            grid=(2,),
            in_specs=[
                pl.BlockSpec((columns, length), lambda i, at: (0, 0)),
                pl.BlockSpec((tile, columns), lambda i, at: (i, 0)),
            ],
            out_specs=[quarter, quarter],
            scratch_shapes=[pltpu.VMEM((length, columns), BF16)],
        ),
        out_shape=[
            pltpu.HBM((2, 2, token_rows, width), F32),
            pltpu.HBM((2, 2, token_rows, width), BF16),
        ],
        compiler_params=KERNEL,
        cost_estimate=LIGHT,
    )(place(), *in_hbm(bars, weight))


def weight_back_kernel(bars_ref, normed_ref, grad_ref):
    grad = jnp.dot(bars_ref[...], normed_ref[...], preferred_element_type=F32)
    grad_ref[...] = grad.T.astype(BF16)


def weight_back(bars, normed):
    columns, length = bars.shape
    width = normed.shape[1]
    tile = width // 5
    return pl.pallas_call(
        weight_back_kernel,
        grid=(5,),
        in_specs=[
            pl.BlockSpec((columns, length), lambda i: (0, 0)),
            pl.BlockSpec((length, tile), lambda i: (0, i)),
        ],
        out_specs=pl.BlockSpec((tile, columns), lambda i: (i, 0)),
        out_shape=pltpu.HBM((width, columns), BF16),
        compiler_params=KERNEL,
        cost_estimate=LIGHT,
    )(*in_hbm(bars, normed))


def tied(*arrays):
    return lax.optimization_barrier(arrays)


def swapped(array, axis, mask):
    size = lax.axis_size(axis)
    return lax.ppermute(array, axis, [(i, i ^ mask) for i in range(size)])


def pick(array, index, axis=0):
    return lax.dynamic_index_in_dim(array, index, axis, keepdims=False)


def swap_halves(array):
    me = lax.axis_index("blk")
    got = swapped(pick(array, 1 - me), "blk", 1)
    kept = pick(array, me)
    return jnp.stack([jnp.where(me == 0, kept, got), jnp.where(me == 0, got, kept)])


def scatter_row(halves):
    row = lax.axis_index("head") // 2
    got = swapped(pick(halves, 1 - row, 1).astype(BF16), "head", 2).astype(F32)
    return (pick(halves, row, 1) + got).reshape(-1, halves.shape[-1])


def over_head(parts):
    return lax.all_to_all(parts, "head", split_axis=0, concat_axis=0, tiled=True)


def qkv_columns(rows, extra):
    own, width = rows.shape
    part = width // 3 // 4
    sent = rows.reshape(own, 3, 4, part).transpose(2, 0, 1, 3).reshape(4, own, 3 * part)
    if extra is not None:
        sent = jnp.concatenate([sent, jnp.broadcast_to(extra[None], (4,) + extra.shape)], axis=2)
    return over_head(sent)


def along_batch(piece):
    return lax.all_gather(piece, "batch", axis=0, tiled=False)


def other_core(array):
    return swapped(array, "head", 1)


def to_beside(across):
    return swapped(across[..., : across.shape[-1] // 2], "head", 2)


def to_across(beside):
    return swapped(beside[..., beside.shape[-1] // 2 :], "blk", 1)


def over_batch(parts):
    return lax.psum_scatter(parts.astype(BF16), "batch", scatter_dimension=0, tiled=False)


def across_sum(halves):
    blk = lax.axis_index("blk")
    got = swapped(pick(halves, 1 - blk), "blk", 1).astype(F32)
    return (pick(halves, blk).astype(F32) + got).astype(BF16)


def columns_to_rows(moved):
    rows = moved.shape[1]
    return moved.reshape(4, rows, 3, -1).transpose(1, 2, 0, 3).reshape(rows, -1).astype(F32)


def quarter(parts, blk, row):
    one, two = (pick(pick(part, blk), row).astype(F32) for part in parts)
    return one + two


def diagonal_rows(parts):
    blk, row = place()[:2]
    rows = quarter(parts, 1 - blk, 1 - row).astype(BF16)
    half = rows.shape[-1] // 2
    return rows[..., :half], rows[..., half:]


def neighbour_rows(parts, one, two):
    blk, row = place()[:2]
    half = one.shape[-1]
    across, beside = quarter(parts, 1 - blk, row), quarter(parts, blk, 1 - row)
    across = jnp.concatenate([across[..., :half], across[..., half:] + two.astype(F32)], axis=-1)
    beside = jnp.concatenate([beside[..., :half] + one.astype(F32), beside[..., half:]], axis=-1)
    return across.astype(BF16), beside.astype(BF16)


def sent_beside_and_across(across, beside):
    return swapped(across, "blk", 1), swapped(beside, "head", 2)


def heads_grad(weight, out_bar):
    return dot_cols(weight, out_bar).astype(BF16).reshape(4, -1, out_bar.shape[0])


def own_quarter(parts):
    blk, row = place()[:2]
    return quarter(parts, blk, row)


def own_sum(own, *more):
    return sum((part.astype(F32) for part in more), own).astype(BF16)


def sum_over(array, *hops):
    for axis, mask in hops:
        array = array + swapped(array, axis, mask)
    return array


def gain_back(weight, weight_grad, gain):
    return jnp.sum(weight.astype(F32) * weight_grad, axis=-1) / gain.astype(F32)


def lower_of(upper, stream, factor, gain):
    return norm_back(upper, stream, factor, gain)[0]


def spread_device(
    tokens,
    segments,
    qkv_weight,
    out_weight,
    up_weight,
    down_weight,
    attn_gain,
    mlp_gain,
    scale_param,
    cotangent,
):
    layers, head_dim = scale_param.shape
    _, token_rows, width = tokens.shape
    scale_vecs = SCALE_BASE / math.sqrt(head_dim) * jax.nn.softplus(scale_param)
    segments = pick(segments, lax.axis_index("blk"))
    own_gains = jnp.concatenate([attn_gain, mlp_gain], axis=0)

    part3 = 3 * width // 4
    dense_own = [
        jnp.concatenate([out_weight[i], up_weight[i], down_weight[i]], axis=1) for i in (0, 1)
    ]

    columns = qkv_columns(qkv_weight[0], own_gains.T)
    columns, tokens, cotangent = tied(columns.reshape(-1, columns.shape[-1]), tokens, cotangent)
    along = along_batch(columns)
    first = swap_halves(tokens).reshape(-1, width)
    stream = first.astype(F32)
    far, near = swapped(first, "head", 2), other_core(first)
    both = other_core(far)
    upper = swap_halves(cotangent)
    along, near, far, both, dense_near, upper = tied(
        along, near, far, both, dense_own[0], upper
    )
    token_pieces = (first, near, far, both)
    dense_near = along_batch(dense_near)
    qkv_across = swapped(along, "blk", 1)
    next_columns = jnp.concatenate(list(qkv_columns(qkv_weight[1], None)), axis=1)
    qkv_across, dense_near, next_columns = tied(qkv_across, dense_near, next_columns)
    across, beside = swapped(dense_near, "blk", 1), swapped(dense_near, "head", 2)
    next_both = along_batch(jnp.stack([next_columns, dense_own[1]]))
    weight, gains = assemble_columns(along, qkv_across, part3)
    qkvs = [weight]
    gains = gains.T.astype(F32)

    kept, denses = [], []
    for layer in range(layers):
        normed, factor_one = normalize(stream, gains[layer])
        if layer == 1:
            normed = normed.astype(BF16)
            far, near = swapped(normed, "head", 2), other_core(normed)
            far, next_across, dense_next = tied(far, next_across, dense_next)
            across, beside = swapped(dense_next, "blk", 1), swapped(dense_next, "head", 2)
            token_pieces = (normed, near, far, other_core(far))
            qkvs.append(assemble_wide(next_along, next_across, part3))
        normed_all, projected = project(
            token_pieces, gains[layer], qkvs[layer], layer == 0, token_rows
        )
        attended, log_total = attend_rows(
            projected, scale_vecs[layer], segments, 4, token_rows
        )
        attended, across, beside = tied(attended, across, beside)
        one, two = to_beside(across), to_across(beside)
        if layer == 0:
            two, next_both = tied(two, next_both)
            next_along, dense_next = next_both[:, 0], next_both[:, 1]
            next_across = swapped(next_along, "blk", 1)
            attended_t, one, two = tied(over_head(attended), one, two)
        else:
            dense_near = dense_next
            attended_t, one, two = tied(over_head(attended), one, two)
        pieces = (dense_near, across, beside, one, two)
        pieces += tuple(other_core(piece) for piece in pieces)
        attended_t = attended_t.reshape(width, -1)
        denses.append(assemble(pieces))
        dense = denses[layer]
        out_w, up_w, down_w = dense[:, :width], dense[:, width:-width], dense[:, -width:]
        middle = stream + dot_rows(attended_t, out_w)
        normed_two, factor_two = normalize(middle, gains[layers + layer])
        normed_two = normed_two.astype(BF16)
        hidden = dot(normed_two, up_w)
        active = (hidden * jax.nn.sigmoid(hidden)).astype(BF16)
        kept.append(
            (
                stream, factor_one, normed_all, projected, log_total, attended_t, middle,
                factor_two, normed_two, hidden, active,
            )
        )
        stream = middle + dot(active, down_w)
    layer_out = swap_halves(stream.astype(BF16).reshape(tokens.shape))
    upper = upper.reshape(-1, width).astype(F32)

    scale_grads = [None] * layers
    for layer in reversed(range(layers)):
        (
            stream, factor_one, normed_all, projected, log_total, attended_t, middle,
            factor_two, normed_two, hidden, active,
        ) = kept[layer]
        qkv, dense = qkvs[layer], denses[layer]
        out_w, up_w, down_w = dense[:, :width], dense[:, width:-width], dense[:, -width:]
        down_bar = upper.astype(BF16)
        gate = jax.nn.sigmoid(hidden)
        up_bar = (
            dot_cols(down_bar, down_w) * gate * (1.0 + hidden * (1.0 - gate))
        ).astype(BF16)
        middle_grad = upper + lower_of(
            dot_cols(up_bar, up_w), middle, factor_two, gains[layers + layer]
        )
        out_bar = middle_grad.astype(BF16)
        if layer == 0:
            attended_grad = over_head(heads_grad(out_w, out_bar))
            grads, others = dense_grads(attended_t, normed_two, active, out_bar, up_bar, down_bar)
            others, across = tied(others, across)
            others, own = tied(others, own_quarter(cored) + across.astype(F32))
            attended_grad, others, z_sum, beside = tied(attended_grad, others, z_sum, beside)
            others = other_core(others)
            attended_grad, summed = tied(attended_grad, own_sum(own, beside))
            summed = over_batch(summed)
            earlier = across_sum(z_sum)
        else:
            attended_grad = over_head(heads_grad(out_w, out_bar))
            grads, others = dense_grads(attended_t, normed_two, active, out_bar, up_bar, down_bar)
            attended_grad, others, layer_out = tied(attended_grad, others, layer_out)
            others = other_core(others)
        bars, scale_grads[layer] = attend_back_rows(
            projected, attended_grad, log_total, scale_vecs[layer], segments, token_rows
        )
        if layer == 0:
            bars, earlier = tied(bars, earlier)
            qkv_grad = weight_back(bars, normed_all)
            bars, qkv_grad, others = tied(bars, qkv_grad, others)
            z_sum = over_batch(qkv_grad.reshape(4, 2, -1, qkv_grad.shape[-1]))
            cored = (grads, others)
            bars, rows = tied(bars, diagonal_rows(cored))
            diagonal = sent_beside_and_across(*rows)
            halves, to_core = rows_back(bars, qkv, token_rows)
            scale_sum = sum_over(jnp.stack(scale_grads), ("head", 1))
            halves, to_core, diagonal, summed, scale_sum = tied(
                halves, to_core, diagonal, summed, scale_sum
            )
            scale_sum = sum_over(scale_sum, ("head", 2))
            halves, to_core, rows, scale_sum = tied(
                halves, to_core, neighbour_rows(cored, *diagonal), scale_sum
            )
            sent = sent_beside_and_across(*rows)
            halves = halves + other_core(to_core).astype(F32)
            scale_sum = sum_over(scale_sum, ("batch", 1), ("batch", 2), ("blk", 1))
            own = own_quarter(cored)
            halves, sent, z_sum, scale_sum, own = tied(halves, sent, z_sum, scale_sum, own)
            halves, own, earlier = tied(halves, own_sum(own, *sent), earlier)
            moved = over_head(earlier.reshape(4, -1, earlier.shape[-1]))
            dense_first = over_batch(own)
            normed_grad = scatter_row(halves)
            z_across, dense_first = tied(across_sum(z_sum), dense_first)
            z_across = over_head(z_across.reshape(4, -1, z_across.shape[-1]))
            dense_grad = [dense_first, summed]
            qkv_grads = [columns_to_rows(z_across), columns_to_rows(moved)]
        else:
            bars, others = tied(bars, others)
            cored = (grads, others)
            bars, rows = tied(bars, diagonal_rows(cored))
            diagonal = sent_beside_and_across(*rows)
            halves, to_core, qkv_grad = project_back(bars, qkv, normed_all, token_rows)
            z_sum = over_batch(qkv_grad.reshape(4, 2, -1, qkv_grad.shape[-1]))
            to_core, halves, diagonal = tied(to_core, halves, diagonal)
            to_core, rows = tied(to_core, neighbour_rows(cored, *diagonal))
            across = swapped(rows[0], "blk", 1)
            halves = halves + other_core(to_core).astype(F32)
            normed_grad = scatter_row(halves)
            normed_grad, beside = tied(normed_grad, rows[1])
            beside = swapped(beside, "head", 2)
        upper = middle_grad + lower_of(normed_grad, stream, factor_one, gains[layer])
    input_grad = swap_halves(upper.astype(BF16).reshape(tokens.shape)).astype(F32)
    scale_grad = scale_sum * (SCALE_BASE / math.sqrt(head_dim)) * jax.nn.sigmoid(scale_param)
    dense_all = jnp.stack([part.astype(F32) for part in dense_grad])
    qkv_all = jnp.stack(qkv_grads)
    up_all = dense_all[:, :, width:-width]
    return (
        layer_out,
        input_grad,
        qkv_all,
        dense_all[:, :, :width],
        up_all,
        dense_all[:, :, -width:],
        gain_back(qkv_weight, qkv_all, attn_gain),
        gain_back(up_weight, up_all, mlp_gain),
        scale_grad,
    )


def per_device(*args):
    tokens, segments = args[0], args[1]
    sizes = tuple(lax.axis_size(axis) for axis in ALL)
    heads = tokens.shape[2] // args[8].shape[1]
    spread = (
        sizes == (4, 2, 4)
        and tokens.shape[0] == 2
        and args[2].shape[0] == 2
        and tokens.shape[1] % 128 == 0
        and Q_ROWS % tokens.shape[1] == 0
        and segments.shape[1] <= WINDOW
        and segments.shape[1] % FORWARD_ROWS == 0
        and heads % 4 == 0
        and tokens.shape[2] % 256 == 0
    )
    return spread_device(*args) if spread else general_device(*args)


def solution(mesh):
    rows = P(None, ALL, None)
    by_token = P("batch", ("blk", "head"), None)
    return jax.shard_map(
        per_device,
        mesh=mesh,
        in_specs=(
            by_token, P("batch", None), rows, rows, rows, rows, P(None, ALL), P(None, ALL), P(),
            by_token,
        ),
        out_specs=(
            by_token, by_token, rows, rows, rows, rows, P(None, ALL), P(None, ALL), P(),
        ),
        check_vma=False,
    )
```

```python
import functools
import math

import jax
import jax.numpy as jnp
from jax import lax
from jax.experimental import pallas as pl
from jax.experimental.pallas import tpu as pltpu
from jax.sharding import PartitionSpec as P

WINDOW = 1024
EPSILON = 1e-06
SCALE_BASE = 1.4426950408889634
MASKED_SCORE = -1e30

ALL = ("batch", "blk", "head")
REST = ("batch", "blk")
F32 = jnp.float32
BF16 = jnp.bfloat16


def shifted(block, axis, distance):
    devices = range(lax.axis_size(axis))
    route = [(i - distance, i) for i in devices if i - distance in devices]
    return lax.ppermute(block, axis, route)


NT = (((1,), (1,)), ((), ()))
TN = (((0,), (0,)), ((), ()))


def dot(left, right):
    return jnp.dot(left, right, preferred_element_type=F32)


def dot_rows(left, right):
    return lax.dot_general(left, right, (((0,), (0,)), ((), ())), preferred_element_type=F32)


def dot_cols(left, right):
    return lax.dot_general(left, right, (((1,), (1,)), ((), ())), preferred_element_type=F32)


def normalize(stream, gain):
    factor = lax.rsqrt(jnp.mean(stream * stream, axis=-1, keepdims=True) + EPSILON)
    return stream * factor * gain, factor


def norm_back(upper, stream, factor, gain):
    inner = upper * gain
    gain_grad = jnp.sum(upper * stream * factor, axis=0)
    lower = factor * inner - stream * factor * factor * factor * jnp.mean(
        inner * stream, axis=-1, keepdims=True
    )
    return lower, gain_grad


class Plan:
    def __init__(self, tokens):
        self.seqs, self.rows, self.width = tokens.shape
        self.heads = lax.axis_size("head")
        self.blks = lax.axis_size("blk")
        self.block = self.rows * self.heads
        self.whole = self.seqs % self.blks == 0
        if self.whole:
            self.groups, self.own_seqs = self.blks, self.seqs // self.blks
            self.reach = 0
        else:
            self.groups, self.own_seqs = 1, self.seqs
            self.reach = min((WINDOW - 1) // self.block + 1, self.blks - 1)
        self.length = self.groups * self.block
        self.tokens = self.seqs * self.rows


def to_plan(plan, array):
    if plan.whole and plan.blks > 1:
        array = lax.all_to_all(array, "blk", split_axis=0, concat_axis=0, tiled=True)
    return array.reshape(plan.tokens, plan.width)


def from_plan(plan, flat):
    array = flat.reshape(plan.seqs, plan.rows, plan.width)
    if plan.whole and plan.blks > 1:
        array = lax.all_to_all(array, "blk", split_axis=0, concat_axis=0, tiled=True)
    return array


def in_sequence(plan, by_head, width):
    parts = by_head.reshape(plan.heads, plan.groups, plan.own_seqs, plan.rows, width)
    return parts.transpose(2, 1, 0, 3, 4).reshape(-1, width)


def by_owner(plan, rows, width):
    parts = rows.reshape(plan.own_seqs, plan.groups, plan.heads, plan.rows, width)
    return parts.transpose(2, 1, 0, 3, 4).reshape(plan.heads, plan.tokens, width)


def gather_tokens(plan, rows):
    moved = lax.all_gather(rows, "head", axis=0, tiled=False)
    return in_sequence(plan, moved, rows.shape[-1])


def scatter_tokens(plan, rows):
    width = rows.shape[-1]
    return lax.psum_scatter(
        by_owner(plan, rows.astype(BF16), width), "head", scatter_dimension=0, tiled=False
    ).astype(F32)


def heads_to_tokens(plan, rows):
    part = rows.shape[-1]
    moved = lax.all_to_all(
        by_owner(plan, rows, part), "head", split_axis=0, concat_axis=0, tiled=True
    )
    return moved.transpose(1, 0, 2).reshape(plan.tokens, plan.heads * part)


def tokens_to_heads(plan, rows):
    part = rows.shape[-1] // plan.heads
    sent = rows.reshape(plan.tokens, plan.heads, part).transpose(1, 0, 2)
    moved = lax.all_to_all(sent, "head", split_axis=0, concat_axis=0, tiled=True)
    return in_sequence(plan, moved, part)


def gather_qkv(rows):
    own, width = rows.shape
    heads = lax.axis_size("head")
    part = width // 3 // heads
    sent = rows.reshape(own, 3, heads, part).transpose(2, 0, 1, 3).reshape(heads, own, 3 * part)
    moved = lax.all_to_all(sent, "head", split_axis=0, concat_axis=0, tiled=True)
    full = lax.all_gather(moved, REST, axis=0, tiled=True)
    return full.reshape(-1, 3 * part)


def scatter_qkv(grad):
    heads = lax.axis_size("head")
    part = grad.shape[1] // 3
    summed = lax.psum_scatter(grad.astype(BF16), REST, scatter_dimension=0, tiled=True)
    own = summed.shape[0] // heads
    moved = lax.all_to_all(
        summed.reshape(heads, own, 3 * part), "head", split_axis=0, concat_axis=0, tiled=True
    )
    return (
        moved.reshape(heads, own, 3, part)
        .transpose(1, 2, 0, 3)
        .reshape(own, 3 * heads * part)
        .astype(F32)
    )


def window_mask(plan, segments, block_index):
    key_count = plan.length + plan.reach * plan.block
    if plan.whole:
        query_segs, key_segs = segments, segments
    else:
        leading = jnp.full((plan.own_seqs, plan.reach * plan.block), -1, jnp.int32)
        padded = jnp.concatenate([leading, segments], axis=1)
        start = block_index * plan.block
        query_segs = lax.dynamic_slice_in_dim(segments, start, plan.block, 1)
        key_segs = lax.dynamic_slice_in_dim(padded, start, key_count, 1)
    query_place = jnp.arange(plan.length, dtype=jnp.int32)[:, None] + plan.reach * plan.block
    key_place = jnp.arange(key_count, dtype=jnp.int32)[None, :]
    near = (key_place <= query_place) & (query_place - key_place < WINDOW)
    return (key_segs[:, None, :] == query_segs[:, :, None]) & near[None]


def with_earlier(plan, own):
    arrived = [own]
    for _ in range(plan.reach):
        arrived.append(shifted(arrived[-1], "blk", 1))
    return jnp.concatenate(arrived[::-1], axis=1) if plan.reach else own


def to_earlier(plan, grads):
    if not plan.reach:
        return grads
    block = plan.block
    total = grads[:, :block]
    for step in range(1, plan.reach + 1):
        total = (
            shifted(total.astype(BF16), "blk", -1).astype(F32)
            + grads[:, step * block : (step + 1) * block]
        )
    return total


def scores_of(queries, keys, allowed):
    scores = jnp.einsum("sqhd,skhd->shqk", queries, keys, preferred_element_type=F32)
    return jnp.where(allowed[:, None], scores, MASKED_SCORE)


def attend(queries, keys, values, allowed):
    scores = scores_of(queries, keys, allowed)
    top_score = jnp.max(scores, axis=-1, keepdims=True)
    exp_terms = jnp.exp(scores - top_score)
    totals = jnp.sum(exp_terms, axis=-1, keepdims=True)
    probs_low = (exp_terms / totals).astype(BF16)
    attended = jnp.einsum("shqk,skhd->sqhd", probs_low, values, preferred_element_type=F32)
    return attended, top_score + jnp.log(totals)


def attend_back(queries, keys, values, allowed, log_total, attended_grad):
    probs = jnp.exp(scores_of(queries, keys, allowed) - log_total)
    probs_low = probs.astype(BF16)
    values_grad = jnp.einsum(
        "shqk,sqhd->skhd", probs_low, attended_grad, preferred_element_type=F32
    )
    probs_grad = jnp.einsum("sqhd,skhd->shqk", attended_grad, values, preferred_element_type=F32)
    row_dot = jnp.sum(probs_grad * probs, axis=-1, keepdims=True)
    scores_low = (probs * (probs_grad - row_dot)).astype(BF16)
    queries_grad = jnp.einsum("shqk,skhd->sqhd", scores_low, keys, preferred_element_type=F32)
    keys_grad = jnp.einsum("shqk,sqhd->skhd", scores_low, queries, preferred_element_type=F32)
    return queries_grad, keys_grad, values_grad


def forward(plan, stream, qkv, dense, gains, scale_vec, allowed):
    width = plan.width
    head_dim = scale_vec.shape[0]
    part = qkv.shape[1] // 3
    local_heads = part // head_dim
    split = (plan.own_seqs, plan.length, local_heads, head_dim)
    out_w, up_w, down_w = dense[:, :width], dense[:, width:-width], dense[:, -width:]
    normed, factor_one = normalize(stream, gains[0])
    normed_all = gather_tokens(plan, normed.astype(BF16))
    projected = dot(normed_all, qkv)
    query_pre = projected[:, :part].reshape(split)
    queries = (query_pre * scale_vec).astype(BF16)
    keys = with_earlier(plan, projected[:, part : 2 * part].astype(BF16).reshape(split))
    values = with_earlier(plan, projected[:, 2 * part :].astype(BF16).reshape(split))
    attended_part, log_total = attend(queries, keys, values, allowed)
    attended = heads_to_tokens(plan, attended_part.astype(BF16).reshape(-1, part))
    middle = stream + dot(attended, out_w)
    normed_two, factor_two = normalize(middle, gains[1])
    normed_two = normed_two.astype(BF16)
    hidden = dot(normed_two, up_w)
    active = (hidden * jax.nn.sigmoid(hidden)).astype(BF16)
    result = middle + dot(active, down_w)
    kept = (
        stream, factor_one, normed_all, query_pre, queries, keys, values, log_total,
        attended, middle, factor_two, normed_two, hidden, active,
    )
    return result, kept


def backward(plan, upper, kept, qkv, dense, gains, scale_vec, allowed):
    (
        stream, factor_one, normed_all, query_pre, queries, keys, values, log_total,
        attended, middle, factor_two, normed_two, hidden, active,
    ) = kept
    width = plan.width
    head_dim = scale_vec.shape[0]
    part = qkv.shape[1] // 3
    out_w, up_w, down_w = dense[:, :width], dense[:, width:-width], dense[:, -width:]
    upper_low = upper.astype(BF16)
    down_grad = dot_rows(active, upper_low)
    active_grad = dot_cols(upper_low, down_w)
    gate = jax.nn.sigmoid(hidden)
    hidden_low = (active_grad * gate * (1.0 + hidden * (1.0 - gate))).astype(BF16)
    up_grad = dot_rows(normed_two, hidden_low)
    extra_two, mlp_gain_grad = norm_back(dot_cols(hidden_low, up_w), middle, factor_two, gains[1])
    middle_grad = upper + extra_two
    middle_low = middle_grad.astype(BF16)
    out_grad = dot_rows(attended, middle_low)
    dense_grad = jnp.concatenate([out_grad, up_grad, down_grad], axis=1).astype(BF16)
    dense_own = lax.psum_scatter(dense_grad, ALL, scatter_dimension=0, tiled=True)
    attended_grad = tokens_to_heads(plan, dot_cols(middle_low, out_w).astype(BF16))
    queries_grad, keys_grad, values_grad = attend_back(
        queries, keys, values, allowed, log_total, attended_grad.reshape(queries.shape)
    )
    query_bar = queries_grad.astype(BF16).astype(F32)
    scale_vec_grad = jnp.sum((query_bar * query_pre).reshape(-1, head_dim), axis=0)
    query_low = (query_bar * scale_vec).astype(BF16).reshape(-1, part)
    keys_low = to_earlier(plan, keys_grad).astype(BF16).reshape(-1, part)
    values_low = to_earlier(plan, values_grad).astype(BF16).reshape(-1, part)
    projected_low = jnp.concatenate([query_low, keys_low, values_low], axis=1)
    normed_grad = scatter_tokens(plan, dot_cols(projected_low, qkv))
    qkv_own = scatter_qkv(dot_rows(normed_all, projected_low))
    extra_one, attn_gain_grad = norm_back(normed_grad, stream, factor_one, gains[0])
    lower = middle_grad + extra_one
    return lower, qkv_own, dense_own, (attn_gain_grad, mlp_gain_grad), scale_vec_grad


def general_device(
    tokens,
    segments,
    qkv_weight,
    out_weight,
    up_weight,
    down_weight,
    attn_gain,
    mlp_gain,
    scale_param,
    cotangent,
):
    plan = Plan(tokens)
    layers, head_dim = scale_param.shape
    block_index = lax.axis_index("blk")
    scale_vecs = SCALE_BASE / math.sqrt(head_dim) * jax.nn.softplus(scale_param)
    own_gains = jnp.concatenate([attn_gain, mlp_gain], axis=0)
    gains = (
        lax.all_gather(own_gains.reshape(1, -1), ALL, axis=0, tiled=True)
        .reshape(-1, 2 * layers, attn_gain.shape[1])
        .transpose(1, 0, 2)
        .reshape(2 * layers, plan.width)
        .astype(F32)
    )
    if plan.whole:
        segments = lax.dynamic_slice_in_dim(
            segments, block_index * plan.own_seqs, plan.own_seqs, 0
        )
    allowed = window_mask(plan, segments, block_index)
    stream = to_plan(plan, tokens).astype(F32)
    qkvs, denses, kept = [], [], []
    for layer in range(layers):
        qkvs.append(gather_qkv(qkv_weight[layer]))
        own = jnp.concatenate([out_weight[layer], up_weight[layer], down_weight[layer]], axis=1)
        denses.append(lax.all_gather(own, ALL, axis=0, tiled=True))
        layer_gains = (gains[layer], gains[layers + layer])
        stream, saved = forward(
            plan, stream, qkvs[layer], denses[layer], layer_gains, scale_vecs[layer], allowed
        )
        kept.append(saved)
    layer_out = from_plan(plan, stream.astype(BF16))
    upper = to_plan(plan, cotangent).astype(F32)
    qkv_grads, dense_grads = [None] * layers, [None] * layers
    gain_grads, scale_grads = [None] * layers, [None] * layers
    for layer in reversed(range(layers)):
        layer_gains = (gains[layer], gains[layers + layer])
        upper, qkv_grads[layer], dense_grads[layer], gain_grads[layer], scale_grads[layer] = (
            backward(
                plan, upper, kept[layer], qkvs[layer], denses[layer], layer_gains,
                scale_vecs[layer], allowed,
            )
        )
    input_grad = from_plan(plan, upper.astype(BF16)).astype(F32)
    small = jnp.concatenate(
        [g[0] for g in gain_grads] + [g[1] for g in gain_grads] + scale_grads, axis=0
    )
    total = lax.psum(small, ALL)
    gain_total = total[: 2 * layers * plan.width].reshape(2 * layers, plan.width)
    owner = lax.axis_index(ALL)
    gain_rows = attn_gain.shape[1]
    own_total = lax.dynamic_slice_in_dim(gain_total, owner * gain_rows, gain_rows, 1)
    scale_total = total[2 * layers * plan.width :].reshape(layers, head_dim)
    scale_grad = scale_total * (SCALE_BASE / math.sqrt(head_dim)) * jax.nn.sigmoid(scale_param)
    dense_all = jnp.stack(dense_grads).astype(F32)
    width = plan.width
    return (
        layer_out,
        input_grad,
        jnp.stack(qkv_grads),
        dense_all[:, :, :width],
        dense_all[:, :, width:-width],
        dense_all[:, :, -width:],
        own_total[:layers],
        own_total[layers:],
        scale_grad,
    )


Q_ROWS = 256
KERNEL = pltpu.CompilerParams(vmem_limit_bytes=32 * 1024 * 1024)
LIGHT = pl.CostEstimate(flops=1 << 20, bytes_accessed=1 << 20, transcendentals=0)


def in_hbm(*arrays):
    return [pltpu.with_memory_space_constraint(array, pltpu.HBM) for array in arrays]


def allowed_keys(col, row, first):
    count = first + row.shape[1]
    key_place = lax.broadcasted_iota(jnp.int32, (count, row.shape[1]), 0)
    query_place = lax.broadcasted_iota(jnp.int32, (count, row.shape[1]), 1) + first
    return (col[:count] == row) & (key_place <= query_place)


def allowed_piece(col, row, start, first):
    same = col == row
    if start + col.shape[0] <= first:
        return same
    key_place = lax.broadcasted_iota(jnp.int32, same.shape, 0) + start
    return same & (key_place <= lax.broadcasted_iota(jnp.int32, same.shape, 1) + first)


def token_places(length, heads, token_rows, block_rows=Q_ROWS):
    for first in range(0, length, block_rows):
        parts = []
        for start in range(0, block_rows, token_rows):
            place = (first + start) // token_rows
            parts.append((start, place % heads, place // heads * token_rows))
        yield first, parts


FORWARD_ROWS, FORWARD_KEYS = 1024, 512


def attend_kernel(token_rows, proj_ref, scale_ref, col_ref, row_ref, out_ref, lse_ref):
    length = proj_ref.shape[-1]
    queries = (proj_ref[0, 0] * scale_ref[...]).astype(BF16)
    keys = proj_ref[1, 0].T.astype(BF16)
    values = proj_ref[2, 0].astype(BF16)
    for first, parts in token_places(length, out_ref.shape[0], token_rows, FORWARD_ROWS):
        end = first + FORWARD_ROWS
        block, row = queries[:, first:end], row_ref[:, first:end]
        pieces = []
        for start in range(0, end, FORWARD_KEYS):
            scores = jnp.dot(keys[start : start + FORWARD_KEYS], block, preferred_element_type=F32)
            allowed = allowed_piece(col_ref[start : start + FORWARD_KEYS], row, start, first)
            pieces.append(jnp.where(allowed, scores, MASKED_SCORE))
        top = functools.reduce(
            jnp.maximum, [jnp.max(piece, axis=0, keepdims=True) for piece in pieces]
        )
        total, attended = 0.0, 0.0
        for i, piece in enumerate(pieces):
            terms = jnp.exp(piece - top)
            total += jnp.sum(terms, axis=0, keepdims=True)
            attended += jnp.dot(
                values[:, i * FORWARD_KEYS : (i + 1) * FORWARD_KEYS],
                terms.astype(BF16),
                preferred_element_type=F32,
            )
        attended = (attended * (1.0 / total)).astype(BF16)
        lse_ref[0, :, first:end] = top + jnp.log(total)
        for start, owner, offset in parts:
            out_ref[owner, 0, :, offset : offset + token_rows] = attended[
                :, start : start + token_rows
            ]


def attend_rows(projected, scale_vec, segments, owners, token_rows):
    head_dim = scale_vec.shape[0]
    length = projected.shape[1]
    local_heads = projected.shape[0] // 3 // head_dim
    tokens = length // owners
    attended, log_total = pl.pallas_call(
        functools.partial(attend_kernel, token_rows),
        grid=(local_heads,),
        in_specs=[
            pl.BlockSpec((3, 1, head_dim, length), lambda h: (0, h, 0, 0)),
            pl.BlockSpec((head_dim, 1), lambda h: (0, 0)),
            pl.BlockSpec((length, 1), lambda h: (0, 0)),
            pl.BlockSpec((1, length), lambda h: (0, 0)),
        ],
        out_specs=[
            pl.BlockSpec((owners, 1, head_dim, tokens), lambda h: (0, h, 0, 0)),
            pl.BlockSpec((1, 1, length), lambda h: (h, 0, 0)),
        ],
        out_shape=[
            jax.ShapeDtypeStruct((owners, local_heads, head_dim, tokens), BF16),
            jax.ShapeDtypeStruct((local_heads, 1, length), F32),
        ],
        compiler_params=KERNEL,
        cost_estimate=LIGHT,
    )(
        projected.reshape(3, local_heads, head_dim, length),
        scale_vec.reshape(head_dim, 1),
        segments.reshape(length, 1),
        segments.reshape(1, length),
    )
    return attended.reshape(owners, local_heads * head_dim, tokens), log_total


def attend_back_kernel(
    token_rows,
    proj_ref,
    grad_ref,
    lse_ref,
    scale_ref,
    col_ref,
    row_ref,
    out_ref,
    scale_grad_ref,
    keys_acc,
    values_acc,
):
    length = proj_ref.shape[-1]
    scale = scale_ref[...]
    query_pre = proj_ref[0, 0]
    queries = (query_pre * scale).astype(BF16)
    keys_t = proj_ref[1, 0].astype(BF16)
    keys = proj_ref[1, 0].T.astype(BF16)
    values = proj_ref[2, 0].T.astype(BF16)
    keys_acc[...] = jnp.zeros_like(keys_acc)
    values_acc[...] = jnp.zeros_like(values_acc)
    scale_grad = jnp.zeros((scale.shape[0], 1), F32)
    for first, parts in token_places(length, grad_ref.shape[0], token_rows):
        end = first + Q_ROWS
        block = queries[:, first:end]
        grad = jnp.concatenate(
            [grad_ref[owner, 0, :, at : at + token_rows] for _, owner, at in parts], axis=1
        )
        scores = jnp.dot(keys[:end], block, preferred_element_type=F32)
        allowed = allowed_keys(col_ref[...], row_ref[:, first:end], first)
        scores = jnp.where(allowed, scores, MASKED_SCORE)
        probs = jnp.exp(scores - lse_ref[0, :, first:end])
        probs_grad = jnp.dot(values[:end], grad, preferred_element_type=F32)
        row_dot = jnp.sum(probs_grad * probs, axis=0, keepdims=True)
        scores_low = (probs * (probs_grad - row_dot)).astype(BF16)
        values_acc[:, :end] += lax.dot_general(
            grad, probs.astype(BF16), NT, preferred_element_type=F32
        )
        keys_acc[:, :end] += lax.dot_general(
            block, scores_low, NT, preferred_element_type=F32
        )
        query_bar = jnp.dot(keys_t[:, :end], scores_low, preferred_element_type=F32)
        query_bar = query_bar.astype(BF16).astype(F32)
        scale_grad += jnp.sum(query_bar * query_pre[:, first:end], axis=1, keepdims=True)
        out_ref[0, 0, :, first:end] = (query_bar * scale).astype(BF16)
    out_ref[1, 0] = keys_acc[...].astype(BF16)
    out_ref[2, 0] = values_acc[...].astype(BF16)
    spread = jnp.broadcast_to(scale_grad, scale_grad_ref.shape)

    @pl.when(pl.program_id(0) == 0)
    def _():
        scale_grad_ref[...] = spread

    @pl.when(pl.program_id(0) > 0)
    def _():
        scale_grad_ref[...] += spread


def attend_back_rows(projected, attended_grad, log_total, scale_vec, segments, token_rows):
    head_dim = scale_vec.shape[0]
    length = projected.shape[1]
    local_heads = projected.shape[0] // 3 // head_dim
    owners, _, tokens = attended_grad.shape
    lanes = 128
    grads, scale_grad = pl.pallas_call(
        functools.partial(attend_back_kernel, token_rows),
        grid=(local_heads,),
        in_specs=[
            pl.BlockSpec((3, 1, head_dim, length), lambda h: (0, h, 0, 0)),
            pl.BlockSpec((owners, 1, head_dim, tokens), lambda h: (0, h, 0, 0)),
            pl.BlockSpec((1, 1, length), lambda h: (h, 0, 0)),
            pl.BlockSpec((head_dim, 1), lambda h: (0, 0)),
            pl.BlockSpec((length, 1), lambda h: (0, 0)),
            pl.BlockSpec((1, length), lambda h: (0, 0)),
        ],
        out_specs=[
            pl.BlockSpec((3, 1, head_dim, length), lambda h: (0, h, 0, 0)),
            pl.BlockSpec((head_dim, lanes), lambda h: (0, 0)),
        ],
        out_shape=[
            pltpu.HBM((3, local_heads, head_dim, length), BF16),
            pltpu.HBM((head_dim, lanes), F32),
        ],
        scratch_shapes=[
            pltpu.VMEM((head_dim, length), F32),
            pltpu.VMEM((head_dim, length), F32),
        ],
        compiler_params=KERNEL,
        cost_estimate=LIGHT,
    )(
        *in_hbm(
            projected.reshape(3, local_heads, head_dim, length),
            attended_grad.reshape(owners, local_heads, head_dim, tokens),
        ),
        log_total,
        scale_vec.reshape(head_dim, 1),
        segments.reshape(length, 1),
        segments.reshape(1, length),
    )
    return grads.reshape(3 * local_heads * head_dim, length), scale_grad[:, 0]


def dense_grad_kernel(
    core_ref, attended_ref, normed_ref, active_ref, out_bar, up_bar, down_bar,
    own_ref, other_ref, normed_t, active_t,
):
    tile = pl.program_id(0)
    rows, width = 8 * own_ref.shape[3], out_bar.shape[1]

    @pl.when(tile == 0)
    def _():
        normed_t[...] = normed_ref[...].astype(F32).T.astype(BF16)
        active_t[...] = active_ref[...].astype(F32).T.astype(BF16)

    start = pl.multiple_of(tile * rows, rows)
    first_core = core_ref[2] == 0
    lefts = (attended_ref, normed_t, active_t)
    for i, (left, right) in enumerate(zip(lefts, (out_bar, up_bar, down_bar))):
        grad = jnp.dot(left[pl.ds(start, rows), :], right[...], preferred_element_type=F32)
        grad = grad.reshape(2, 2, 2, rows // 8, width)
        one, two = grad[:, :, 0], grad[:, :, 1]
        own_ref[:, :, 0, :, i * width : (i + 1) * width] = jnp.where(
            first_core, one, two
        ).astype(BF16)
        other_ref[:, :, 0, :, i * width : (i + 1) * width] = jnp.where(
            first_core, two, one
        ).astype(BF16)


def dense_grads(attended_t, normed, active, out_bar, up_bar, down_bar):
    width, tokens = attended_t.shape
    own = width // 32
    whole = pl.BlockSpec((tokens, width), lambda i, core: (0, 0))
    rows = pl.BlockSpec((2, 2, 1, own, 3 * width), lambda i, core: (0, 0, i, 0, 0))
    shape = pltpu.HBM((2, 2, 4, own, 3 * width), BF16)
    return pl.pallas_call(
        dense_grad_kernel,
        grid_spec=pltpu.PrefetchScalarGridSpec(
            num_scalar_prefetch=1,
            grid=(4,),
            in_specs=[pl.BlockSpec((width, tokens), lambda i, core: (0, 0))] + [whole] * 5,
            out_specs=[rows, rows],
            scratch_shapes=[pltpu.VMEM((width, tokens), BF16)] * 2,
        ),
        out_shape=[shape, shape],
        compiler_params=KERNEL,
        cost_estimate=LIGHT,
    )(place(), *in_hbm(attended_t, normed, active, out_bar, up_bar, down_bar))


def place():
    head = lax.axis_index("head")
    return jnp.stack([lax.axis_index("blk"), head // 2, head % 2]).astype(jnp.int32)


def assemble_kernel(place_ref, *refs):
    pieces, whole_ref = refs[:10], refs[10]
    half = whole_ref.shape[-1] // 2
    blk, row, core = place_ref[0], place_ref[1], place_ref[2]
    for i in range(2):
        at_core = core if i == 0 else 1 - core
        own, across, beside, one, two = pieces[5 * i : 5 * i + 5]
        whole_ref[0, blk, row, at_core] = own[0]
        whole_ref[0, 1 - blk, row, at_core] = across[0]
        whole_ref[0, blk, 1 - row, at_core] = beside[0]
        whole_ref[0, 1 - blk, 1 - row, at_core, :, :half] = one[0]
        whole_ref[0, 1 - blk, 1 - row, at_core, :, half:] = two[0]


def assemble(pieces):
    batch, own, columns = pieces[0].shape
    specs = [
        pl.BlockSpec((1, own, piece.shape[-1]), lambda i, at: (i, 0, 0))
        for piece in pieces
    ]
    whole = pl.pallas_call(
        assemble_kernel,
        grid_spec=pltpu.PrefetchScalarGridSpec(
            num_scalar_prefetch=1,
            grid=(batch,),
            in_specs=specs,
            out_specs=pl.BlockSpec((1, 2, 2, 2, own, columns), lambda i, at: (i, 0, 0, 0, 0, 0)),
        ),
        out_shape=jax.ShapeDtypeStruct((batch, 2, 2, 2, own, columns), BF16),
        compiler_params=KERNEL,
        cost_estimate=LIGHT,
    )(place(), *pieces)
    return whole.reshape(-1, columns)


def assemble_columns_kernel(place_ref, along_ref, across_ref, whole_ref, *extra_ref):
    blk = place_ref[0]
    columns = whole_ref.shape[-1]
    whole_ref[0, blk] = along_ref[0, :, :columns]
    whole_ref[0, 1 - blk] = across_ref[0, :, :columns]
    for extra in extra_ref:
        extra[0, blk] = along_ref[0, :, columns:]
        extra[0, 1 - blk] = across_ref[0, :, columns:]


def assemble_columns(along, across, columns):
    batch, own, both = along.shape
    rows = pl.BlockSpec((1, own, both), lambda i, at: (i, 0, 0))
    shapes = [(batch, 2, own, columns)]
    if both > columns:
        shapes.append((batch, 2, own, both - columns))
    parts = pl.pallas_call(
        assemble_columns_kernel,
        grid_spec=pltpu.PrefetchScalarGridSpec(
            num_scalar_prefetch=1,
            grid=(batch,),
            in_specs=[rows, rows],
            out_specs=[pl.BlockSpec((1,) + s[1:], lambda i, at: (i, 0, 0, 0)) for s in shapes],
        ),
        out_shape=[pltpu.HBM(s, BF16) for s in shapes],
        compiler_params=KERNEL,
        cost_estimate=LIGHT,
    )(place(), *in_hbm(along, across))
    return [part.reshape(-1, part.shape[-1]) for part in parts]


def assemble_wide_kernel(place_ref, along_ref, across_ref, whole_ref):
    blk = place_ref[0]
    own, columns = along_ref.shape[1], whole_ref.shape[-1]
    for i in range(along_ref.shape[-1] // columns):
        place, part = slice(i * own, (i + 1) * own), slice(i * columns, (i + 1) * columns)
        whole_ref[0, blk, place, :] = along_ref[0, :, part]
        whole_ref[0, 1 - blk, place, :] = across_ref[0, :, part]


def assemble_wide(along, across, columns):
    batch, own, wide = along.shape
    rows = own * (wide // columns)
    piece = pl.BlockSpec((1, own, wide), lambda i, at: (i, 0, 0))
    whole = pl.pallas_call(
        assemble_wide_kernel,
        grid_spec=pltpu.PrefetchScalarGridSpec(
            num_scalar_prefetch=1,
            grid=(batch,),
            in_specs=[piece, piece],
            out_specs=pl.BlockSpec((1, 2, rows, columns), lambda i, at: (i, 0, 0, 0)),
        ),
        out_shape=pltpu.HBM((batch, 2, rows, columns), BF16),
        compiler_params=KERNEL,
        cost_estimate=LIGHT,
    )(place(), *in_hbm(along, across))
    return whole.reshape(-1, columns)


def project_kernel(with_norm, place_ref, *refs):
    pieces, (gain_ref, weight_ref, normed_ref, projected_ref) = refs[:4], refs[4:]
    head = place_ref[1] * 2 + place_ref[2]
    rows = pieces[0].shape[0]
    for i, piece in enumerate(pieces):
        value = piece[...]
        if with_norm:
            stream = value.astype(F32)
            factor = lax.rsqrt(jnp.mean(stream * stream, axis=-1, keepdims=True) + EPSILON)
            value = (stream * factor * gain_ref[...]).astype(BF16)
        normed_ref[pl.ds(pl.multiple_of((head ^ i) * rows, rows), rows), :] = value
    projected = jnp.dot(normed_ref[...], weight_ref[...], preferred_element_type=F32)
    projected_ref[...] = projected.T


def project(pieces, gain, weight, with_norm, token_rows):
    tokens, width = pieces[0].shape
    length, columns = 4 * tokens, weight.shape[1]
    groups = tokens // token_rows
    piece = pl.BlockSpec((token_rows, width), lambda g, at: (g, 0))
    return pl.pallas_call(
        functools.partial(project_kernel, with_norm),
        grid_spec=pltpu.PrefetchScalarGridSpec(
            num_scalar_prefetch=1,
            grid=(groups,),
            in_specs=[piece] * 4
            + [
                pl.BlockSpec((1, width), lambda g, at: (0, 0)),
                pl.BlockSpec((width, columns), lambda g, at: (0, 0)),
            ],
            out_specs=[
                pl.BlockSpec((4 * token_rows, width), lambda g, at: (g, 0)),
                pl.BlockSpec((columns, 4 * token_rows), lambda g, at: (0, g)),
            ],
        ),
        out_shape=[
            pltpu.HBM((length, width), BF16),
            jax.ShapeDtypeStruct((columns, length), F32),
        ],
        compiler_params=KERNEL,
        cost_estimate=LIGHT,
    )(place(), *in_hbm(*pieces), gain.reshape(1, width), *in_hbm(weight))


def project_back_kernel(
    place_ref, bars_ref, weight_ref, normed_ref, own_ref, other_ref, grad_ref, bars_t
):
    @pl.when(pl.program_id(0) == 0)
    def _():
        bars_t[...] = bars_ref[...].astype(F32).T.astype(BF16)

    upper = lax.dot_general(bars_t[...], weight_ref[...], NT, preferred_element_type=F32)
    upper = upper.reshape(2, 2, 2, -1, upper.shape[-1])
    first_core = place_ref[2] == 0
    one, two = upper[:, :, 0], upper[:, :, 1]
    own_ref[...] = jnp.where(first_core, one, two)
    other_ref[...] = jnp.where(first_core, two, one).astype(BF16)
    grad = lax.dot_general(normed_ref[...], bars_t[...], TN, preferred_element_type=F32)
    grad_ref[...] = grad.astype(BF16)


def project_back(bars, weight, normed, token_rows):
    columns, length = bars.shape
    width = weight.shape[0]
    tile = width // 2
    quarter = pl.BlockSpec((2, 2, token_rows, tile), lambda i, at: (0, 0, 0, i))
    return pl.pallas_call(
        project_back_kernel,
        grid_spec=pltpu.PrefetchScalarGridSpec(
            num_scalar_prefetch=1,
            grid=(2,),
            in_specs=[
                pl.BlockSpec((columns, length), lambda i, at: (0, 0)),
                pl.BlockSpec((tile, columns), lambda i, at: (i, 0)),
                pl.BlockSpec((length, tile), lambda i, at: (0, i)),
            ],
            out_specs=[quarter, quarter, pl.BlockSpec((tile, columns), lambda i, at: (i, 0))],
            scratch_shapes=[pltpu.VMEM((length, columns), BF16)],
        ),
        out_shape=[
            pltpu.HBM((2, 2, token_rows, width), F32),
            pltpu.HBM((2, 2, token_rows, width), BF16),
            pltpu.HBM((width, columns), BF16),
        ],
        compiler_params=KERNEL,
        cost_estimate=LIGHT,
    )(place(), *in_hbm(bars, weight, normed))


def rows_back_kernel(place_ref, bars_ref, weight_ref, own_ref, other_ref, bars_t):
    @pl.when(pl.program_id(0) == 0)
    def _():
        bars_t[...] = bars_ref[...].astype(F32).T.astype(BF16)

    upper = lax.dot_general(bars_t[...], weight_ref[...], NT, preferred_element_type=F32)
    upper = upper.reshape(2, 2, 2, -1, upper.shape[-1])
    first_core = place_ref[2] == 0
    one, two = upper[:, :, 0], upper[:, :, 1]
    own_ref[...] = jnp.where(first_core, one, two)
    other_ref[...] = jnp.where(first_core, two, one).astype(BF16)


def rows_back(bars, weight, token_rows):
    columns, length = bars.shape
    width = weight.shape[0]
    tile = width // 2
    quarter = pl.BlockSpec((2, 2, token_rows, tile), lambda i, at: (0, 0, 0, i))
    return pl.pallas_call(
        rows_back_kernel,
        grid_spec=pltpu.PrefetchScalarGridSpec(
            num_scalar_prefetch=1,
            grid=(2,),
            in_specs=[
                pl.BlockSpec((columns, length), lambda i, at: (0, 0)),
                pl.BlockSpec((tile, columns), lambda i, at: (i, 0)),
            ],
            out_specs=[quarter, quarter],
            scratch_shapes=[pltpu.VMEM((length, columns), BF16)],
        ),
        out_shape=[
            pltpu.HBM((2, 2, token_rows, width), F32),
            pltpu.HBM((2, 2, token_rows, width), BF16),
        ],
        compiler_params=KERNEL,
        cost_estimate=LIGHT,
    )(place(), *in_hbm(bars, weight))


def weight_back_kernel(bars_ref, normed_ref, grad_ref):
    grad = jnp.dot(bars_ref[...], normed_ref[...], preferred_element_type=F32)
    grad_ref[...] = grad.T.astype(BF16)


def weight_back(bars, normed):
    columns, length = bars.shape
    width = normed.shape[1]
    tile = width // 5
    return pl.pallas_call(
        weight_back_kernel,
        grid=(5,),
        in_specs=[
            pl.BlockSpec((columns, length), lambda i: (0, 0)),
            pl.BlockSpec((length, tile), lambda i: (0, i)),
        ],
        out_specs=pl.BlockSpec((tile, columns), lambda i: (i, 0)),
        out_shape=pltpu.HBM((width, columns), BF16),
        compiler_params=KERNEL,
        cost_estimate=LIGHT,
    )(*in_hbm(bars, normed))


def tied(*arrays):
    return lax.optimization_barrier(arrays)


def swapped(array, axis, mask):
    size = lax.axis_size(axis)
    return lax.ppermute(array, axis, [(i, i ^ mask) for i in range(size)])


def pick(array, index, axis=0):
    return lax.dynamic_index_in_dim(array, index, axis, keepdims=False)


def swap_halves(array):
    me = lax.axis_index("blk")
    got = swapped(pick(array, 1 - me), "blk", 1)
    kept = pick(array, me)
    return jnp.stack([jnp.where(me == 0, kept, got), jnp.where(me == 0, got, kept)])


def scatter_row(halves):
    row = lax.axis_index("head") // 2
    got = swapped(pick(halves, 1 - row, 1).astype(BF16), "head", 2).astype(F32)
    return (pick(halves, row, 1) + got).reshape(-1, halves.shape[-1])


def over_head(parts):
    return lax.all_to_all(parts, "head", split_axis=0, concat_axis=0, tiled=True)


def qkv_columns(rows, extra):
    own, width = rows.shape
    part = width // 3 // 4
    sent = rows.reshape(own, 3, 4, part).transpose(2, 0, 1, 3).reshape(4, own, 3 * part)
    if extra is not None:
        sent = jnp.concatenate([sent, jnp.broadcast_to(extra[None], (4,) + extra.shape)], axis=2)
    return over_head(sent)


def along_batch(piece):
    return lax.all_gather(piece, "batch", axis=0, tiled=False)


def other_core(array):
    return swapped(array, "head", 1)


def to_beside(across):
    return swapped(across[..., : across.shape[-1] // 2], "head", 2)


def to_across(beside):
    return swapped(beside[..., beside.shape[-1] // 2 :], "blk", 1)


def over_batch(parts):
    return lax.psum_scatter(parts.astype(BF16), "batch", scatter_dimension=0, tiled=False)


def across_sum(halves):
    blk = lax.axis_index("blk")
    got = swapped(pick(halves, 1 - blk), "blk", 1).astype(F32)
    return (pick(halves, blk).astype(F32) + got).astype(BF16)


def columns_to_rows(moved):
    rows = moved.shape[1]
    return moved.reshape(4, rows, 3, -1).transpose(1, 2, 0, 3).reshape(rows, -1).astype(F32)


def quarter(parts, blk, row):
    one, two = (pick(pick(part, blk), row).astype(F32) for part in parts)
    return one + two


def diagonal_rows(parts):
    blk, row = place()[:2]
    rows = quarter(parts, 1 - blk, 1 - row).astype(BF16)
    half = rows.shape[-1] // 2
    return rows[..., :half], rows[..., half:]


def neighbour_rows(parts, one, two):
    blk, row = place()[:2]
    half = one.shape[-1]
    across, beside = quarter(parts, 1 - blk, row), quarter(parts, blk, 1 - row)
    across = jnp.concatenate([across[..., :half], across[..., half:] + two.astype(F32)], axis=-1)
    beside = jnp.concatenate([beside[..., :half] + one.astype(F32), beside[..., half:]], axis=-1)
    return across.astype(BF16), beside.astype(BF16)


def sent_beside_and_across(across, beside):
    return swapped(across, "blk", 1), swapped(beside, "head", 2)


def heads_grad(weight, out_bar):
    return dot_cols(weight, out_bar).astype(BF16).reshape(4, -1, out_bar.shape[0])


def own_quarter(parts):
    blk, row = place()[:2]
    return quarter(parts, blk, row)


def own_sum(own, *more):
    return sum((part.astype(F32) for part in more), own).astype(BF16)


def sum_over(array, *hops):
    for axis, mask in hops:
        array = array + swapped(array, axis, mask)
    return array


def gain_back(weight, weight_grad, gain):
    return jnp.sum(weight.astype(F32) * weight_grad, axis=-1) / gain.astype(F32)


def lower_of(upper, stream, factor, gain):
    return norm_back(upper, stream, factor, gain)[0]


def spread_device(
    tokens,
    segments,
    qkv_weight,
    out_weight,
    up_weight,
    down_weight,
    attn_gain,
    mlp_gain,
    scale_param,
    cotangent,
):
    layers, head_dim = scale_param.shape
    _, token_rows, width = tokens.shape
    scale_vecs = SCALE_BASE / math.sqrt(head_dim) * jax.nn.softplus(scale_param)
    segments = pick(segments, lax.axis_index("blk"))
    own_gains = jnp.concatenate([attn_gain, mlp_gain], axis=0)

    part3 = 3 * width // 4
    dense_own = [
        jnp.concatenate([out_weight[i], up_weight[i], down_weight[i]], axis=1) for i in (0, 1)
    ]

    columns = qkv_columns(qkv_weight[0], own_gains.T)
    columns, tokens, cotangent = tied(columns.reshape(-1, columns.shape[-1]), tokens, cotangent)
    along = along_batch(columns)
    first = swap_halves(tokens).reshape(-1, width)
    stream = first.astype(F32)
    far, near = swapped(first, "head", 2), other_core(first)
    both = other_core(far)
    upper = swap_halves(cotangent)
    along, near, far, both, dense_near, upper = tied(
        along, near, far, both, dense_own[0], upper
    )
    token_pieces = (first, near, far, both)
    dense_near = along_batch(dense_near)
    qkv_across = swapped(along, "blk", 1)
    next_columns = jnp.concatenate(list(qkv_columns(qkv_weight[1], None)), axis=1)
    qkv_across, dense_near, next_columns = tied(qkv_across, dense_near, next_columns)
    across, beside = swapped(dense_near, "blk", 1), swapped(dense_near, "head", 2)
    next_both = along_batch(jnp.stack([next_columns, dense_own[1]]))
    weight, gains = assemble_columns(along, qkv_across, part3)
    qkvs = [weight]
    gains = gains.T.astype(F32)

    kept, denses = [], []
    for layer in range(layers):
        normed, factor_one = normalize(stream, gains[layer])
        if layer == 1:
            normed = normed.astype(BF16)
            far, near = swapped(normed, "head", 2), other_core(normed)
            far, next_across, dense_next = tied(far, next_across, dense_next)
            across, beside = swapped(dense_next, "blk", 1), swapped(dense_next, "head", 2)
            token_pieces = (normed, near, far, other_core(far))
            qkvs.append(assemble_wide(next_along, next_across, part3))
        normed_all, projected = project(
            token_pieces, gains[layer], qkvs[layer], layer == 0, token_rows
        )
        attended, log_total = attend_rows(
            projected, scale_vecs[layer], segments, 4, token_rows
        )
        attended, across, beside = tied(attended, across, beside)
        one, two = to_beside(across), to_across(beside)
        if layer == 0:
            two, next_both = tied(two, next_both)
            next_along, dense_next = next_both[:, 0], next_both[:, 1]
            next_across = swapped(next_along, "blk", 1)
            attended_t, one, two = tied(over_head(attended), one, two)
        else:
            dense_near = dense_next
            attended_t, one, two = tied(over_head(attended), one, two)
        pieces = (dense_near, across, beside, one, two)
        pieces += tuple(other_core(piece) for piece in pieces)
        attended_t = attended_t.reshape(width, -1)
        denses.append(assemble(pieces))
        dense = denses[layer]
        out_w, up_w, down_w = dense[:, :width], dense[:, width:-width], dense[:, -width:]
        middle = stream + dot_rows(attended_t, out_w)
        normed_two, factor_two = normalize(middle, gains[layers + layer])
        normed_two = normed_two.astype(BF16)
        hidden = dot(normed_two, up_w)
        active = (hidden * jax.nn.sigmoid(hidden)).astype(BF16)
        kept.append(
            (
                stream, factor_one, normed_all, projected, log_total, attended_t, middle,
                factor_two, normed_two, hidden, active,
            )
        )
        stream = middle + dot(active, down_w)
    layer_out = swap_halves(stream.astype(BF16).reshape(tokens.shape))
    upper = upper.reshape(-1, width).astype(F32)

    scale_grads = [None] * layers
    for layer in reversed(range(layers)):
        (
            stream, factor_one, normed_all, projected, log_total, attended_t, middle,
            factor_two, normed_two, hidden, active,
        ) = kept[layer]
        qkv, dense = qkvs[layer], denses[layer]
        out_w, up_w, down_w = dense[:, :width], dense[:, width:-width], dense[:, -width:]
        down_bar = upper.astype(BF16)
        gate = jax.nn.sigmoid(hidden)
        up_bar = (
            dot_cols(down_bar, down_w) * gate * (1.0 + hidden * (1.0 - gate))
        ).astype(BF16)
        middle_grad = upper + lower_of(
            dot_cols(up_bar, up_w), middle, factor_two, gains[layers + layer]
        )
        out_bar = middle_grad.astype(BF16)
        if layer == 0:
            attended_grad = over_head(heads_grad(out_w, out_bar))
            grads, others = dense_grads(attended_t, normed_two, active, out_bar, up_bar, down_bar)
            others, across = tied(others, across)
            others, own = tied(others, own_quarter(cored) + across.astype(F32))
            attended_grad, others, z_sum, beside = tied(attended_grad, others, z_sum, beside)
            others = other_core(others)
            attended_grad, summed = tied(attended_grad, own_sum(own, beside))
            summed = over_batch(summed)
            earlier = across_sum(z_sum)
        else:
            attended_grad = over_head(heads_grad(out_w, out_bar))
            grads, others = dense_grads(attended_t, normed_two, active, out_bar, up_bar, down_bar)
            attended_grad, others, layer_out = tied(attended_grad, others, layer_out)
            others = other_core(others)
        bars, scale_grads[layer] = attend_back_rows(
            projected, attended_grad, log_total, scale_vecs[layer], segments, token_rows
        )
        if layer == 0:
            bars, earlier = tied(bars, earlier)
            qkv_grad = weight_back(bars, normed_all)
            bars, qkv_grad, others = tied(bars, qkv_grad, others)
            z_sum = over_batch(qkv_grad.reshape(4, 2, -1, qkv_grad.shape[-1]))
            cored = (grads, others)
            bars, rows = tied(bars, diagonal_rows(cored))
            diagonal = sent_beside_and_across(*rows)
            halves, to_core = rows_back(bars, qkv, token_rows)
            scale_sum = sum_over(jnp.stack(scale_grads), ("head", 1))
            halves, to_core, diagonal, summed, scale_sum = tied(
                halves, to_core, diagonal, summed, scale_sum
            )
            scale_sum = sum_over(scale_sum, ("head", 2))
            halves, to_core, rows, scale_sum = tied(
                halves, to_core, neighbour_rows(cored, *diagonal), scale_sum
            )
            sent = sent_beside_and_across(*rows)
            halves = halves + other_core(to_core).astype(F32)
            scale_sum = sum_over(scale_sum, ("batch", 1), ("batch", 2), ("blk", 1))
            own = own_quarter(cored)
            halves, sent, z_sum, scale_sum, own = tied(halves, sent, z_sum, scale_sum, own)
            halves, own, earlier = tied(halves, own_sum(own, *sent), earlier)
            moved = over_head(earlier.reshape(4, -1, earlier.shape[-1]))
            dense_first = over_batch(own)
            normed_grad = scatter_row(halves)
            z_across = across_sum(z_sum)
            z_across = over_head(z_across.reshape(4, -1, z_across.shape[-1]))
            dense_grad = [dense_first, summed]
            qkv_grads = [columns_to_rows(z_across), columns_to_rows(moved)]
        else:
            bars, others = tied(bars, others)
            cored = (grads, others)
            bars, rows = tied(bars, diagonal_rows(cored))
            diagonal = sent_beside_and_across(*rows)
            halves, to_core, qkv_grad = project_back(bars, qkv, normed_all, token_rows)
            z_sum = over_batch(qkv_grad.reshape(4, 2, -1, qkv_grad.shape[-1]))
            to_core, halves, diagonal = tied(to_core, halves, diagonal)
            to_core, rows = tied(to_core, neighbour_rows(cored, *diagonal))
            across = swapped(rows[0], "blk", 1)
            halves = halves + other_core(to_core).astype(F32)
            normed_grad = scatter_row(halves)
            normed_grad, beside = tied(normed_grad, rows[1])
            beside = swapped(beside, "head", 2)
        upper = middle_grad + lower_of(normed_grad, stream, factor_one, gains[layer])
    upper, dense_grad[0] = tied(upper.astype(BF16), dense_grad[0])
    input_grad = swap_halves(upper.reshape(tokens.shape)).astype(F32)
    scale_grad = scale_sum * (SCALE_BASE / math.sqrt(head_dim)) * jax.nn.sigmoid(scale_param)
    dense_all = jnp.stack([part.astype(F32) for part in dense_grad])
    qkv_all = jnp.stack(qkv_grads)
    up_all = dense_all[:, :, width:-width]
    return (
        layer_out,
        input_grad,
        qkv_all,
        dense_all[:, :, :width],
        up_all,
        dense_all[:, :, -width:],
        gain_back(qkv_weight, qkv_all, attn_gain),
        gain_back(up_weight, up_all, mlp_gain),
        scale_grad,
    )


def per_device(*args):
    tokens, segments = args[0], args[1]
    sizes = tuple(lax.axis_size(axis) for axis in ALL)
    heads = tokens.shape[2] // args[8].shape[1]
    spread = (
        sizes == (4, 2, 4)
        and tokens.shape[0] == 2
        and args[2].shape[0] == 2
        and tokens.shape[1] % 128 == 0
        and Q_ROWS % tokens.shape[1] == 0
        and segments.shape[1] <= WINDOW
        and segments.shape[1] % FORWARD_ROWS == 0
        and heads % 4 == 0
        and tokens.shape[2] % 256 == 0
    )
    return spread_device(*args) if spread else general_device(*args)


def solution(mesh):
    rows = P(None, ALL, None)
    by_token = P("batch", ("blk", "head"), None)
    return jax.shard_map(
        per_device,
        mesh=mesh,
        in_specs=(
            by_token, P("batch", None), rows, rows, rows, rows, P(None, ALL), P(None, ALL), P(),
            by_token,
        ),
        out_specs=(
            by_token, by_token, rows, rows, rows, rows, P(None, ALL), P(None, ALL), P(),
        ),
        check_vma=False,
    )
```

```python
import functools
import math

import jax
import jax.numpy as jnp
from jax import lax
from jax.experimental import pallas as pl
from jax.experimental.pallas import tpu as pltpu
from jax.sharding import PartitionSpec as P

WINDOW = 1024
EPSILON = 1e-06
SCALE_BASE = 1.4426950408889634
MASKED_SCORE = -1e30

ALL = ("batch", "blk", "head")
REST = ("batch", "blk")
F32 = jnp.float32
BF16 = jnp.bfloat16


def shifted(block, axis, distance):
    devices = range(lax.axis_size(axis))
    route = [(i - distance, i) for i in devices if i - distance in devices]
    return lax.ppermute(block, axis, route)


NT = (((1,), (1,)), ((), ()))
TN = (((0,), (0,)), ((), ()))


def dot(left, right):
    return jnp.dot(left, right, preferred_element_type=F32)


def dot_rows(left, right):
    return lax.dot_general(left, right, (((0,), (0,)), ((), ())), preferred_element_type=F32)


def dot_cols(left, right):
    return lax.dot_general(left, right, (((1,), (1,)), ((), ())), preferred_element_type=F32)


def normalize(stream, gain):
    factor = lax.rsqrt(jnp.mean(stream * stream, axis=-1, keepdims=True) + EPSILON)
    return stream * factor * gain, factor


def norm_back(upper, stream, factor, gain):
    inner = upper * gain
    gain_grad = jnp.sum(upper * stream * factor, axis=0)
    lower = factor * inner - stream * factor * factor * factor * jnp.mean(
        inner * stream, axis=-1, keepdims=True
    )
    return lower, gain_grad


class Plan:
    def __init__(self, tokens):
        self.seqs, self.rows, self.width = tokens.shape
        self.heads = lax.axis_size("head")
        self.blks = lax.axis_size("blk")
        self.block = self.rows * self.heads
        self.whole = self.seqs % self.blks == 0
        if self.whole:
            self.groups, self.own_seqs = self.blks, self.seqs // self.blks
            self.reach = 0
        else:
            self.groups, self.own_seqs = 1, self.seqs
            self.reach = min((WINDOW - 1) // self.block + 1, self.blks - 1)
        self.length = self.groups * self.block
        self.tokens = self.seqs * self.rows


def to_plan(plan, array):
    if plan.whole and plan.blks > 1:
        array = lax.all_to_all(array, "blk", split_axis=0, concat_axis=0, tiled=True)
    return array.reshape(plan.tokens, plan.width)


def from_plan(plan, flat):
    array = flat.reshape(plan.seqs, plan.rows, plan.width)
    if plan.whole and plan.blks > 1:
        array = lax.all_to_all(array, "blk", split_axis=0, concat_axis=0, tiled=True)
    return array


def in_sequence(plan, by_head, width):
    parts = by_head.reshape(plan.heads, plan.groups, plan.own_seqs, plan.rows, width)
    return parts.transpose(2, 1, 0, 3, 4).reshape(-1, width)


def by_owner(plan, rows, width):
    parts = rows.reshape(plan.own_seqs, plan.groups, plan.heads, plan.rows, width)
    return parts.transpose(2, 1, 0, 3, 4).reshape(plan.heads, plan.tokens, width)


def gather_tokens(plan, rows):
    moved = lax.all_gather(rows, "head", axis=0, tiled=False)
    return in_sequence(plan, moved, rows.shape[-1])


def scatter_tokens(plan, rows):
    width = rows.shape[-1]
    return lax.psum_scatter(
        by_owner(plan, rows.astype(BF16), width), "head", scatter_dimension=0, tiled=False
    ).astype(F32)


def heads_to_tokens(plan, rows):
    part = rows.shape[-1]
    moved = lax.all_to_all(
        by_owner(plan, rows, part), "head", split_axis=0, concat_axis=0, tiled=True
    )
    return moved.transpose(1, 0, 2).reshape(plan.tokens, plan.heads * part)


def tokens_to_heads(plan, rows):
    part = rows.shape[-1] // plan.heads
    sent = rows.reshape(plan.tokens, plan.heads, part).transpose(1, 0, 2)
    moved = lax.all_to_all(sent, "head", split_axis=0, concat_axis=0, tiled=True)
    return in_sequence(plan, moved, part)


def gather_qkv(rows):
    own, width = rows.shape
    heads = lax.axis_size("head")
    part = width // 3 // heads
    sent = rows.reshape(own, 3, heads, part).transpose(2, 0, 1, 3).reshape(heads, own, 3 * part)
    moved = lax.all_to_all(sent, "head", split_axis=0, concat_axis=0, tiled=True)
    full = lax.all_gather(moved, REST, axis=0, tiled=True)
    return full.reshape(-1, 3 * part)


def scatter_qkv(grad):
    heads = lax.axis_size("head")
    part = grad.shape[1] // 3
    summed = lax.psum_scatter(grad.astype(BF16), REST, scatter_dimension=0, tiled=True)
    own = summed.shape[0] // heads
    moved = lax.all_to_all(
        summed.reshape(heads, own, 3 * part), "head", split_axis=0, concat_axis=0, tiled=True
    )
    return (
        moved.reshape(heads, own, 3, part)
        .transpose(1, 2, 0, 3)
        .reshape(own, 3 * heads * part)
        .astype(F32)
    )


def window_mask(plan, segments, block_index):
    key_count = plan.length + plan.reach * plan.block
    if plan.whole:
        query_segs, key_segs = segments, segments
    else:
        leading = jnp.full((plan.own_seqs, plan.reach * plan.block), -1, jnp.int32)
        padded = jnp.concatenate([leading, segments], axis=1)
        start = block_index * plan.block
        query_segs = lax.dynamic_slice_in_dim(segments, start, plan.block, 1)
        key_segs = lax.dynamic_slice_in_dim(padded, start, key_count, 1)
    query_place = jnp.arange(plan.length, dtype=jnp.int32)[:, None] + plan.reach * plan.block
    key_place = jnp.arange(key_count, dtype=jnp.int32)[None, :]
    near = (key_place <= query_place) & (query_place - key_place < WINDOW)
    return (key_segs[:, None, :] == query_segs[:, :, None]) & near[None]


def with_earlier(plan, own):
    arrived = [own]
    for _ in range(plan.reach):
        arrived.append(shifted(arrived[-1], "blk", 1))
    return jnp.concatenate(arrived[::-1], axis=1) if plan.reach else own


def to_earlier(plan, grads):
    if not plan.reach:
        return grads
    block = plan.block
    total = grads[:, :block]
    for step in range(1, plan.reach + 1):
        total = (
            shifted(total.astype(BF16), "blk", -1).astype(F32)
            + grads[:, step * block : (step + 1) * block]
        )
    return total


def scores_of(queries, keys, allowed):
    scores = jnp.einsum("sqhd,skhd->shqk", queries, keys, preferred_element_type=F32)
    return jnp.where(allowed[:, None], scores, MASKED_SCORE)


def attend(queries, keys, values, allowed):
    scores = scores_of(queries, keys, allowed)
    top_score = jnp.max(scores, axis=-1, keepdims=True)
    exp_terms = jnp.exp(scores - top_score)
    totals = jnp.sum(exp_terms, axis=-1, keepdims=True)
    probs_low = (exp_terms / totals).astype(BF16)
    attended = jnp.einsum("shqk,skhd->sqhd", probs_low, values, preferred_element_type=F32)
    return attended, top_score + jnp.log(totals)


def attend_back(queries, keys, values, allowed, log_total, attended_grad):
    probs = jnp.exp(scores_of(queries, keys, allowed) - log_total)
    probs_low = probs.astype(BF16)
    values_grad = jnp.einsum(
        "shqk,sqhd->skhd", probs_low, attended_grad, preferred_element_type=F32
    )
    probs_grad = jnp.einsum("sqhd,skhd->shqk", attended_grad, values, preferred_element_type=F32)
    row_dot = jnp.sum(probs_grad * probs, axis=-1, keepdims=True)
    scores_low = (probs * (probs_grad - row_dot)).astype(BF16)
    queries_grad = jnp.einsum("shqk,skhd->sqhd", scores_low, keys, preferred_element_type=F32)
    keys_grad = jnp.einsum("shqk,sqhd->skhd", scores_low, queries, preferred_element_type=F32)
    return queries_grad, keys_grad, values_grad


def forward(plan, stream, qkv, dense, gains, scale_vec, allowed):
    width = plan.width
    head_dim = scale_vec.shape[0]
    part = qkv.shape[1] // 3
    local_heads = part // head_dim
    split = (plan.own_seqs, plan.length, local_heads, head_dim)
    out_w, up_w, down_w = dense[:, :width], dense[:, width:-width], dense[:, -width:]
    normed, factor_one = normalize(stream, gains[0])
    normed_all = gather_tokens(plan, normed.astype(BF16))
    projected = dot(normed_all, qkv)
    query_pre = projected[:, :part].reshape(split)
    queries = (query_pre * scale_vec).astype(BF16)
    keys = with_earlier(plan, projected[:, part : 2 * part].astype(BF16).reshape(split))
    values = with_earlier(plan, projected[:, 2 * part :].astype(BF16).reshape(split))
    attended_part, log_total = attend(queries, keys, values, allowed)
    attended = heads_to_tokens(plan, attended_part.astype(BF16).reshape(-1, part))
    middle = stream + dot(attended, out_w)
    normed_two, factor_two = normalize(middle, gains[1])
    normed_two = normed_two.astype(BF16)
    hidden = dot(normed_two, up_w)
    active = (hidden * jax.nn.sigmoid(hidden)).astype(BF16)
    result = middle + dot(active, down_w)
    kept = (
        stream, factor_one, normed_all, query_pre, queries, keys, values, log_total,
        attended, middle, factor_two, normed_two, hidden, active,
    )
    return result, kept


def backward(plan, upper, kept, qkv, dense, gains, scale_vec, allowed):
    (
        stream, factor_one, normed_all, query_pre, queries, keys, values, log_total,
        attended, middle, factor_two, normed_two, hidden, active,
    ) = kept
    width = plan.width
    head_dim = scale_vec.shape[0]
    part = qkv.shape[1] // 3
    out_w, up_w, down_w = dense[:, :width], dense[:, width:-width], dense[:, -width:]
    upper_low = upper.astype(BF16)
    down_grad = dot_rows(active, upper_low)
    active_grad = dot_cols(upper_low, down_w)
    gate = jax.nn.sigmoid(hidden)
    hidden_low = (active_grad * gate * (1.0 + hidden * (1.0 - gate))).astype(BF16)
    up_grad = dot_rows(normed_two, hidden_low)
    extra_two, mlp_gain_grad = norm_back(dot_cols(hidden_low, up_w), middle, factor_two, gains[1])
    middle_grad = upper + extra_two
    middle_low = middle_grad.astype(BF16)
    out_grad = dot_rows(attended, middle_low)
    dense_grad = jnp.concatenate([out_grad, up_grad, down_grad], axis=1).astype(BF16)
    dense_own = lax.psum_scatter(dense_grad, ALL, scatter_dimension=0, tiled=True)
    attended_grad = tokens_to_heads(plan, dot_cols(middle_low, out_w).astype(BF16))
    queries_grad, keys_grad, values_grad = attend_back(
        queries, keys, values, allowed, log_total, attended_grad.reshape(queries.shape)
    )
    query_bar = queries_grad.astype(BF16).astype(F32)
    scale_vec_grad = jnp.sum((query_bar * query_pre).reshape(-1, head_dim), axis=0)
    query_low = (query_bar * scale_vec).astype(BF16).reshape(-1, part)
    keys_low = to_earlier(plan, keys_grad).astype(BF16).reshape(-1, part)
    values_low = to_earlier(plan, values_grad).astype(BF16).reshape(-1, part)
    projected_low = jnp.concatenate([query_low, keys_low, values_low], axis=1)
    normed_grad = scatter_tokens(plan, dot_cols(projected_low, qkv))
    qkv_own = scatter_qkv(dot_rows(normed_all, projected_low))
    extra_one, attn_gain_grad = norm_back(normed_grad, stream, factor_one, gains[0])
    lower = middle_grad + extra_one
    return lower, qkv_own, dense_own, (attn_gain_grad, mlp_gain_grad), scale_vec_grad


def general_device(
    tokens,
    segments,
    qkv_weight,
    out_weight,
    up_weight,
    down_weight,
    attn_gain,
    mlp_gain,
    scale_param,
    cotangent,
):
    plan = Plan(tokens)
    layers, head_dim = scale_param.shape
    block_index = lax.axis_index("blk")
    scale_vecs = SCALE_BASE / math.sqrt(head_dim) * jax.nn.softplus(scale_param)
    own_gains = jnp.concatenate([attn_gain, mlp_gain], axis=0)
    gains = (
        lax.all_gather(own_gains.reshape(1, -1), ALL, axis=0, tiled=True)
        .reshape(-1, 2 * layers, attn_gain.shape[1])
        .transpose(1, 0, 2)
        .reshape(2 * layers, plan.width)
        .astype(F32)
    )
    if plan.whole:
        segments = lax.dynamic_slice_in_dim(
            segments, block_index * plan.own_seqs, plan.own_seqs, 0
        )
    allowed = window_mask(plan, segments, block_index)
    stream = to_plan(plan, tokens).astype(F32)
    qkvs, denses, kept = [], [], []
    for layer in range(layers):
        qkvs.append(gather_qkv(qkv_weight[layer]))
        own = jnp.concatenate([out_weight[layer], up_weight[layer], down_weight[layer]], axis=1)
        denses.append(lax.all_gather(own, ALL, axis=0, tiled=True))
        layer_gains = (gains[layer], gains[layers + layer])
        stream, saved = forward(
            plan, stream, qkvs[layer], denses[layer], layer_gains, scale_vecs[layer], allowed
        )
        kept.append(saved)
    layer_out = from_plan(plan, stream.astype(BF16))
    upper = to_plan(plan, cotangent).astype(F32)
    qkv_grads, dense_grads = [None] * layers, [None] * layers
    gain_grads, scale_grads = [None] * layers, [None] * layers
    for layer in reversed(range(layers)):
        layer_gains = (gains[layer], gains[layers + layer])
        upper, qkv_grads[layer], dense_grads[layer], gain_grads[layer], scale_grads[layer] = (
            backward(
                plan, upper, kept[layer], qkvs[layer], denses[layer], layer_gains,
                scale_vecs[layer], allowed,
            )
        )
    input_grad = from_plan(plan, upper.astype(BF16)).astype(F32)
    small = jnp.concatenate(
        [g[0] for g in gain_grads] + [g[1] for g in gain_grads] + scale_grads, axis=0
    )
    total = lax.psum(small, ALL)
    gain_total = total[: 2 * layers * plan.width].reshape(2 * layers, plan.width)
    owner = lax.axis_index(ALL)
    gain_rows = attn_gain.shape[1]
    own_total = lax.dynamic_slice_in_dim(gain_total, owner * gain_rows, gain_rows, 1)
    scale_total = total[2 * layers * plan.width :].reshape(layers, head_dim)
    scale_grad = scale_total * (SCALE_BASE / math.sqrt(head_dim)) * jax.nn.sigmoid(scale_param)
    dense_all = jnp.stack(dense_grads).astype(F32)
    width = plan.width
    return (
        layer_out,
        input_grad,
        jnp.stack(qkv_grads),
        dense_all[:, :, :width],
        dense_all[:, :, width:-width],
        dense_all[:, :, -width:],
        own_total[:layers],
        own_total[layers:],
        scale_grad,
    )


Q_ROWS = 256
KERNEL = pltpu.CompilerParams(vmem_limit_bytes=32 * 1024 * 1024)
LIGHT = pl.CostEstimate(flops=1 << 20, bytes_accessed=1 << 20, transcendentals=0)


def in_hbm(*arrays):
    return [pltpu.with_memory_space_constraint(array, pltpu.HBM) for array in arrays]


def allowed_keys(col, row, first):
    count = first + row.shape[1]
    key_place = lax.broadcasted_iota(jnp.int32, (count, row.shape[1]), 0)
    query_place = lax.broadcasted_iota(jnp.int32, (count, row.shape[1]), 1) + first
    return (col[:count] == row) & (key_place <= query_place)


def allowed_piece(col, row, start, first):
    same = col == row
    if start + col.shape[0] <= first:
        return same
    key_place = lax.broadcasted_iota(jnp.int32, same.shape, 0) + start
    return same & (key_place <= lax.broadcasted_iota(jnp.int32, same.shape, 1) + first)


def token_places(length, heads, token_rows, block_rows=Q_ROWS):
    for first in range(0, length, block_rows):
        parts = []
        for start in range(0, block_rows, token_rows):
            place = (first + start) // token_rows
            parts.append((start, place % heads, place // heads * token_rows))
        yield first, parts


FORWARD_ROWS, FORWARD_KEYS = 1024, 512


def attend_kernel(token_rows, proj_ref, scale_ref, col_ref, row_ref, out_ref, lse_ref):
    length = proj_ref.shape[-1]
    queries = (proj_ref[0, 0] * scale_ref[...]).astype(BF16)
    keys = proj_ref[1, 0].T.astype(BF16)
    values = proj_ref[2, 0].astype(BF16)
    for first, parts in token_places(length, out_ref.shape[0], token_rows, FORWARD_ROWS):
        end = first + FORWARD_ROWS
        block, row = queries[:, first:end], row_ref[:, first:end]
        pieces = []
        for start in range(0, end, FORWARD_KEYS):
            scores = jnp.dot(keys[start : start + FORWARD_KEYS], block, preferred_element_type=F32)
            allowed = allowed_piece(col_ref[start : start + FORWARD_KEYS], row, start, first)
            pieces.append(jnp.where(allowed, scores, MASKED_SCORE))
        top = functools.reduce(
            jnp.maximum, [jnp.max(piece, axis=0, keepdims=True) for piece in pieces]
        )
        total, attended = 0.0, 0.0
        for i, piece in enumerate(pieces):
            terms = jnp.exp(piece - top)
            total += jnp.sum(terms, axis=0, keepdims=True)
            attended += jnp.dot(
                values[:, i * FORWARD_KEYS : (i + 1) * FORWARD_KEYS],
                terms.astype(BF16),
                preferred_element_type=F32,
            )
        attended = (attended * (1.0 / total)).astype(BF16)
        lse_ref[0, :, first:end] = top + jnp.log(total)
        for start, owner, offset in parts:
            out_ref[owner, 0, :, offset : offset + token_rows] = attended[
                :, start : start + token_rows
            ]


def attend_rows(projected, scale_vec, segments, owners, token_rows):
    head_dim = scale_vec.shape[0]
    length = projected.shape[1]
    local_heads = projected.shape[0] // 3 // head_dim
    tokens = length // owners
    attended, log_total = pl.pallas_call(
        functools.partial(attend_kernel, token_rows),
        grid=(local_heads,),
        in_specs=[
            pl.BlockSpec((3, 1, head_dim, length), lambda h: (0, h, 0, 0)),
            pl.BlockSpec((head_dim, 1), lambda h: (0, 0)),
            pl.BlockSpec((length, 1), lambda h: (0, 0)),
            pl.BlockSpec((1, length), lambda h: (0, 0)),
        ],
        out_specs=[
            pl.BlockSpec((owners, 1, head_dim, tokens), lambda h: (0, h, 0, 0)),
            pl.BlockSpec((1, 1, length), lambda h: (h, 0, 0)),
        ],
        out_shape=[
            jax.ShapeDtypeStruct((owners, local_heads, head_dim, tokens), BF16),
            jax.ShapeDtypeStruct((local_heads, 1, length), F32),
        ],
        compiler_params=KERNEL,
        cost_estimate=LIGHT,
    )(
        projected.reshape(3, local_heads, head_dim, length),
        scale_vec.reshape(head_dim, 1),
        segments.reshape(length, 1),
        segments.reshape(1, length),
    )
    return attended.reshape(owners, local_heads * head_dim, tokens), log_total


def attend_back_kernel(
    token_rows,
    proj_ref,
    grad_ref,
    lse_ref,
    scale_ref,
    col_ref,
    row_ref,
    out_ref,
    scale_grad_ref,
    keys_acc,
    values_acc,
):
    length = proj_ref.shape[-1]
    scale = scale_ref[...]
    query_pre = proj_ref[0, 0]
    queries = (query_pre * scale).astype(BF16)
    keys_t = proj_ref[1, 0].astype(BF16)
    keys = proj_ref[1, 0].T.astype(BF16)
    values = proj_ref[2, 0].T.astype(BF16)
    keys_acc[...] = jnp.zeros_like(keys_acc)
    values_acc[...] = jnp.zeros_like(values_acc)
    scale_grad = jnp.zeros((scale.shape[0], 1), F32)
    for first, parts in token_places(length, grad_ref.shape[0], token_rows):
        end = first + Q_ROWS
        block = queries[:, first:end]
        grad = jnp.concatenate(
            [grad_ref[owner, 0, :, at : at + token_rows] for _, owner, at in parts], axis=1
        )
        scores = jnp.dot(keys[:end], block, preferred_element_type=F32)
        allowed = allowed_keys(col_ref[...], row_ref[:, first:end], first)
        scores = jnp.where(allowed, scores, MASKED_SCORE)
        probs = jnp.exp(scores - lse_ref[0, :, first:end])
        probs_grad = jnp.dot(values[:end], grad, preferred_element_type=F32)
        row_dot = jnp.sum(probs_grad * probs, axis=0, keepdims=True)
        scores_low = (probs * (probs_grad - row_dot)).astype(BF16)
        values_acc[:, :end] += lax.dot_general(
            grad, probs.astype(BF16), NT, preferred_element_type=F32
        )
        keys_acc[:, :end] += lax.dot_general(
            block, scores_low, NT, preferred_element_type=F32
        )
        query_bar = jnp.dot(keys_t[:, :end], scores_low, preferred_element_type=F32)
        query_bar = query_bar.astype(BF16).astype(F32)
        scale_grad += jnp.sum(query_bar * query_pre[:, first:end], axis=1, keepdims=True)
        out_ref[0, 0, :, first:end] = (query_bar * scale).astype(BF16)
    out_ref[1, 0] = keys_acc[...].astype(BF16)
    out_ref[2, 0] = values_acc[...].astype(BF16)
    spread = jnp.broadcast_to(scale_grad, scale_grad_ref.shape)

    @pl.when(pl.program_id(0) == 0)
    def _():
        scale_grad_ref[...] = spread

    @pl.when(pl.program_id(0) > 0)
    def _():
        scale_grad_ref[...] += spread


def attend_back_rows(projected, attended_grad, log_total, scale_vec, segments, token_rows):
    head_dim = scale_vec.shape[0]
    length = projected.shape[1]
    local_heads = projected.shape[0] // 3 // head_dim
    owners, _, tokens = attended_grad.shape
    lanes = 128
    grads, scale_grad = pl.pallas_call(
        functools.partial(attend_back_kernel, token_rows),
        grid=(local_heads,),
        in_specs=[
            pl.BlockSpec((3, 1, head_dim, length), lambda h: (0, h, 0, 0)),
            pl.BlockSpec((owners, 1, head_dim, tokens), lambda h: (0, h, 0, 0)),
            pl.BlockSpec((1, 1, length), lambda h: (h, 0, 0)),
            pl.BlockSpec((head_dim, 1), lambda h: (0, 0)),
            pl.BlockSpec((length, 1), lambda h: (0, 0)),
            pl.BlockSpec((1, length), lambda h: (0, 0)),
        ],
        out_specs=[
            pl.BlockSpec((3, 1, head_dim, length), lambda h: (0, h, 0, 0)),
            pl.BlockSpec((head_dim, lanes), lambda h: (0, 0)),
        ],
        out_shape=[
            pltpu.HBM((3, local_heads, head_dim, length), BF16),
            pltpu.HBM((head_dim, lanes), F32),
        ],
        scratch_shapes=[
            pltpu.VMEM((head_dim, length), F32),
            pltpu.VMEM((head_dim, length), F32),
        ],
        compiler_params=KERNEL,
        cost_estimate=LIGHT,
    )(
        *in_hbm(
            projected.reshape(3, local_heads, head_dim, length),
            attended_grad.reshape(owners, local_heads, head_dim, tokens),
        ),
        log_total,
        scale_vec.reshape(head_dim, 1),
        segments.reshape(length, 1),
        segments.reshape(1, length),
    )
    return grads.reshape(3 * local_heads * head_dim, length), scale_grad[:, 0]


def dense_grad_kernel(
    core_ref, attended_ref, normed_ref, active_ref, out_bar, up_bar, down_bar,
    own_ref, other_ref, normed_t, active_t,
):
    tile = pl.program_id(0)
    rows, width = 8 * own_ref.shape[3], out_bar.shape[1]

    @pl.when(tile == 0)
    def _():
        normed_t[...] = normed_ref[...].astype(F32).T.astype(BF16)
        active_t[...] = active_ref[...].astype(F32).T.astype(BF16)

    start = pl.multiple_of(tile * rows, rows)
    first_core = core_ref[2] == 0
    lefts = (attended_ref, normed_t, active_t)
    for i, (left, right) in enumerate(zip(lefts, (out_bar, up_bar, down_bar))):
        grad = jnp.dot(left[pl.ds(start, rows), :], right[...], preferred_element_type=F32)
        grad = grad.reshape(2, 2, 2, rows // 8, width)
        one, two = grad[:, :, 0], grad[:, :, 1]
        own_ref[:, :, 0, :, i * width : (i + 1) * width] = jnp.where(
            first_core, one, two
        ).astype(BF16)
        other_ref[:, :, 0, :, i * width : (i + 1) * width] = jnp.where(
            first_core, two, one
        ).astype(BF16)


def dense_grads(attended_t, normed, active, out_bar, up_bar, down_bar):
    width, tokens = attended_t.shape
    own = width // 32
    whole = pl.BlockSpec((tokens, width), lambda i, core: (0, 0))
    rows = pl.BlockSpec((2, 2, 1, own, 3 * width), lambda i, core: (0, 0, i, 0, 0))
    shape = pltpu.HBM((2, 2, 4, own, 3 * width), BF16)
    return pl.pallas_call(
        dense_grad_kernel,
        grid_spec=pltpu.PrefetchScalarGridSpec(
            num_scalar_prefetch=1,
            grid=(4,),
            in_specs=[pl.BlockSpec((width, tokens), lambda i, core: (0, 0))] + [whole] * 5,
            out_specs=[rows, rows],
            scratch_shapes=[pltpu.VMEM((width, tokens), BF16)] * 2,
        ),
        out_shape=[shape, shape],
        compiler_params=KERNEL,
        cost_estimate=LIGHT,
    )(place(), *in_hbm(attended_t, normed, active, out_bar, up_bar, down_bar))


def place():
    head = lax.axis_index("head")
    return jnp.stack([lax.axis_index("blk"), head // 2, head % 2]).astype(jnp.int32)


def assemble_kernel(place_ref, *refs):
    pieces, whole_ref = refs[:10], refs[10]
    half = whole_ref.shape[-1] // 2
    blk, row, core = place_ref[0], place_ref[1], place_ref[2]
    for i in range(2):
        at_core = core if i == 0 else 1 - core
        own, across, beside, one, two = pieces[5 * i : 5 * i + 5]
        whole_ref[0, blk, row, at_core] = own[0]
        whole_ref[0, 1 - blk, row, at_core] = across[0]
        whole_ref[0, blk, 1 - row, at_core] = beside[0]
        whole_ref[0, 1 - blk, 1 - row, at_core, :, :half] = one[0]
        whole_ref[0, 1 - blk, 1 - row, at_core, :, half:] = two[0]


def assemble(pieces):
    batch, own, columns = pieces[0].shape
    specs = [
        pl.BlockSpec((1, own, piece.shape[-1]), lambda i, at: (i, 0, 0))
        for piece in pieces
    ]
    whole = pl.pallas_call(
        assemble_kernel,
        grid_spec=pltpu.PrefetchScalarGridSpec(
            num_scalar_prefetch=1,
            grid=(batch,),
            in_specs=specs,
            out_specs=pl.BlockSpec((1, 2, 2, 2, own, columns), lambda i, at: (i, 0, 0, 0, 0, 0)),
        ),
        out_shape=jax.ShapeDtypeStruct((batch, 2, 2, 2, own, columns), BF16),
        compiler_params=KERNEL,
        cost_estimate=LIGHT,
    )(place(), *pieces)
    return whole.reshape(-1, columns)


def assemble_columns_kernel(place_ref, along_ref, across_ref, whole_ref, *extra_ref):
    blk = place_ref[0]
    columns = whole_ref.shape[-1]
    whole_ref[0, blk] = along_ref[0, :, :columns]
    whole_ref[0, 1 - blk] = across_ref[0, :, :columns]
    for extra in extra_ref:
        extra[0, blk] = along_ref[0, :, columns:]
        extra[0, 1 - blk] = across_ref[0, :, columns:]


def assemble_columns(along, across, columns):
    batch, own, both = along.shape
    rows = pl.BlockSpec((1, own, both), lambda i, at: (i, 0, 0))
    shapes = [(batch, 2, own, columns)]
    if both > columns:
        shapes.append((batch, 2, own, both - columns))
    parts = pl.pallas_call(
        assemble_columns_kernel,
        grid_spec=pltpu.PrefetchScalarGridSpec(
            num_scalar_prefetch=1,
            grid=(batch,),
            in_specs=[rows, rows],
            out_specs=[pl.BlockSpec((1,) + s[1:], lambda i, at: (i, 0, 0, 0)) for s in shapes],
        ),
        out_shape=[pltpu.HBM(s, BF16) for s in shapes],
        compiler_params=KERNEL,
        cost_estimate=LIGHT,
    )(place(), *in_hbm(along, across))
    return [part.reshape(-1, part.shape[-1]) for part in parts]


def assemble_wide_kernel(place_ref, along_ref, across_ref, whole_ref):
    blk = place_ref[0]
    own, columns = along_ref.shape[1], whole_ref.shape[-1]
    for i in range(along_ref.shape[-1] // columns):
        place, part = slice(i * own, (i + 1) * own), slice(i * columns, (i + 1) * columns)
        whole_ref[0, blk, place, :] = along_ref[0, :, part]
        whole_ref[0, 1 - blk, place, :] = across_ref[0, :, part]


def assemble_wide(along, across, columns):
    batch, own, wide = along.shape
    rows = own * (wide // columns)
    piece = pl.BlockSpec((1, own, wide), lambda i, at: (i, 0, 0))
    whole = pl.pallas_call(
        assemble_wide_kernel,
        grid_spec=pltpu.PrefetchScalarGridSpec(
            num_scalar_prefetch=1,
            grid=(batch,),
            in_specs=[piece, piece],
            out_specs=pl.BlockSpec((1, 2, rows, columns), lambda i, at: (i, 0, 0, 0)),
        ),
        out_shape=pltpu.HBM((batch, 2, rows, columns), BF16),
        compiler_params=KERNEL,
        cost_estimate=LIGHT,
    )(place(), *in_hbm(along, across))
    return whole.reshape(-1, columns)


def project_kernel(with_norm, place_ref, *refs):
    pieces, (gain_ref, weight_ref, normed_ref, projected_ref) = refs[:4], refs[4:]
    head = place_ref[1] * 2 + place_ref[2]
    rows = pieces[0].shape[0]
    for i, piece in enumerate(pieces):
        value = piece[...]
        if with_norm:
            stream = value.astype(F32)
            factor = lax.rsqrt(jnp.mean(stream * stream, axis=-1, keepdims=True) + EPSILON)
            value = (stream * factor * gain_ref[...]).astype(BF16)
        normed_ref[pl.ds(pl.multiple_of((head ^ i) * rows, rows), rows), :] = value
    projected = jnp.dot(normed_ref[...], weight_ref[...], preferred_element_type=F32)
    projected_ref[...] = projected.T


def project(pieces, gain, weight, with_norm, token_rows):
    tokens, width = pieces[0].shape
    length, columns = 4 * tokens, weight.shape[1]
    groups = tokens // token_rows
    piece = pl.BlockSpec((token_rows, width), lambda g, at: (g, 0))
    return pl.pallas_call(
        functools.partial(project_kernel, with_norm),
        grid_spec=pltpu.PrefetchScalarGridSpec(
            num_scalar_prefetch=1,
            grid=(groups,),
            in_specs=[piece] * 4
            + [
                pl.BlockSpec((1, width), lambda g, at: (0, 0)),
                pl.BlockSpec((width, columns), lambda g, at: (0, 0)),
            ],
            out_specs=[
                pl.BlockSpec((4 * token_rows, width), lambda g, at: (g, 0)),
                pl.BlockSpec((columns, 4 * token_rows), lambda g, at: (0, g)),
            ],
        ),
        out_shape=[
            pltpu.HBM((length, width), BF16),
            jax.ShapeDtypeStruct((columns, length), F32),
        ],
        compiler_params=KERNEL,
        cost_estimate=LIGHT,
    )(place(), *in_hbm(*pieces), gain.reshape(1, width), *in_hbm(weight))


def project_back_kernel(
    place_ref, bars_ref, weight_ref, normed_ref, own_ref, other_ref, grad_ref, bars_t
):
    @pl.when(pl.program_id(0) == 0)
    def _():
        bars_t[...] = bars_ref[...].astype(F32).T.astype(BF16)

    upper = lax.dot_general(bars_t[...], weight_ref[...], NT, preferred_element_type=F32)
    upper = upper.reshape(2, 2, 2, -1, upper.shape[-1])
    first_core = place_ref[2] == 0
    one, two = upper[:, :, 0], upper[:, :, 1]
    own_ref[...] = jnp.where(first_core, one, two)
    other_ref[...] = jnp.where(first_core, two, one).astype(BF16)
    grad = lax.dot_general(normed_ref[...], bars_t[...], TN, preferred_element_type=F32)
    grad_ref[...] = grad.astype(BF16)


def project_back(bars, weight, normed, token_rows):
    columns, length = bars.shape
    width = weight.shape[0]
    tile = width // 2
    quarter = pl.BlockSpec((2, 2, token_rows, tile), lambda i, at: (0, 0, 0, i))
    return pl.pallas_call(
        project_back_kernel,
        grid_spec=pltpu.PrefetchScalarGridSpec(
            num_scalar_prefetch=1,
            grid=(2,),
            in_specs=[
                pl.BlockSpec((columns, length), lambda i, at: (0, 0)),
                pl.BlockSpec((tile, columns), lambda i, at: (i, 0)),
                pl.BlockSpec((length, tile), lambda i, at: (0, i)),
            ],
            out_specs=[quarter, quarter, pl.BlockSpec((tile, columns), lambda i, at: (i, 0))],
            scratch_shapes=[pltpu.VMEM((length, columns), BF16)],
        ),
        out_shape=[
            pltpu.HBM((2, 2, token_rows, width), F32),
            pltpu.HBM((2, 2, token_rows, width), BF16),
            pltpu.HBM((width, columns), BF16),
        ],
        compiler_params=KERNEL,
        cost_estimate=LIGHT,
    )(place(), *in_hbm(bars, weight, normed))


def rows_back_kernel(place_ref, bars_ref, weight_ref, own_ref, other_ref, bars_t):
    @pl.when(pl.program_id(0) == 0)
    def _():
        bars_t[...] = bars_ref[...].astype(F32).T.astype(BF16)

    upper = lax.dot_general(bars_t[...], weight_ref[...], NT, preferred_element_type=F32)
    upper = upper.reshape(2, 2, 2, -1, upper.shape[-1])
    first_core = place_ref[2] == 0
    one, two = upper[:, :, 0], upper[:, :, 1]
    own_ref[...] = jnp.where(first_core, one, two)
    other_ref[...] = jnp.where(first_core, two, one).astype(BF16)


def rows_back(bars, weight, token_rows):
    columns, length = bars.shape
    width = weight.shape[0]
    tile = width // 2
    quarter = pl.BlockSpec((2, 2, token_rows, tile), lambda i, at: (0, 0, 0, i))
    return pl.pallas_call(
        rows_back_kernel,
        grid_spec=pltpu.PrefetchScalarGridSpec(
            num_scalar_prefetch=1,
            grid=(2,),
            in_specs=[
                pl.BlockSpec((columns, length), lambda i, at: (0, 0)),
                pl.BlockSpec((tile, columns), lambda i, at: (i, 0)),
            ],
            out_specs=[quarter, quarter],
            scratch_shapes=[pltpu.VMEM((length, columns), BF16)],
        ),
        out_shape=[
            pltpu.HBM((2, 2, token_rows, width), F32),
            pltpu.HBM((2, 2, token_rows, width), BF16),
        ],
        compiler_params=KERNEL,
        cost_estimate=LIGHT,
    )(place(), *in_hbm(bars, weight))


def weight_back_kernel(bars_ref, normed_ref, grad_ref):
    grad = jnp.dot(bars_ref[...], normed_ref[...], preferred_element_type=F32)
    grad_ref[...] = grad.T.astype(BF16)


def weight_back(bars, normed):
    columns, length = bars.shape
    width = normed.shape[1]
    tile = width // 5
    return pl.pallas_call(
        weight_back_kernel,
        grid=(5,),
        in_specs=[
            pl.BlockSpec((columns, length), lambda i: (0, 0)),
            pl.BlockSpec((length, tile), lambda i: (0, i)),
        ],
        out_specs=pl.BlockSpec((tile, columns), lambda i: (i, 0)),
        out_shape=pltpu.HBM((width, columns), BF16),
        compiler_params=KERNEL,
        cost_estimate=LIGHT,
    )(*in_hbm(bars, normed))


def tied(*arrays):
    return lax.optimization_barrier(arrays)


def swapped(array, axis, mask):
    size = lax.axis_size(axis)
    return lax.ppermute(array, axis, [(i, i ^ mask) for i in range(size)])


def pick(array, index, axis=0):
    return lax.dynamic_index_in_dim(array, index, axis, keepdims=False)


def swap_halves(array):
    me = lax.axis_index("blk")
    got = swapped(pick(array, 1 - me), "blk", 1)
    kept = pick(array, me)
    return jnp.stack([jnp.where(me == 0, kept, got), jnp.where(me == 0, got, kept)])


def scatter_row(halves):
    row = lax.axis_index("head") // 2
    got = swapped(pick(halves, 1 - row, 1).astype(BF16), "head", 2).astype(F32)
    return (pick(halves, row, 1) + got).reshape(-1, halves.shape[-1])


def over_head(parts):
    return lax.all_to_all(parts, "head", split_axis=0, concat_axis=0, tiled=True)


def qkv_columns(rows, extra):
    own, width = rows.shape
    part = width // 3 // 4
    sent = rows.reshape(own, 3, 4, part).transpose(2, 0, 1, 3).reshape(4, own, 3 * part)
    if extra is not None:
        sent = jnp.concatenate([sent, jnp.broadcast_to(extra[None], (4,) + extra.shape)], axis=2)
    return over_head(sent)


def along_batch(piece):
    return lax.all_gather(piece, "batch", axis=0, tiled=False)


def other_core(array):
    return swapped(array, "head", 1)


def to_beside(across):
    return swapped(across[..., : across.shape[-1] // 2], "head", 2)


def to_across(beside):
    return swapped(beside[..., beside.shape[-1] // 2 :], "blk", 1)


def over_batch(parts):
    return lax.psum_scatter(parts.astype(BF16), "batch", scatter_dimension=0, tiled=False)


def across_sum(halves):
    blk = lax.axis_index("blk")
    got = swapped(pick(halves, 1 - blk), "blk", 1).astype(F32)
    return (pick(halves, blk).astype(F32) + got).astype(BF16)


def columns_to_rows(moved):
    rows = moved.shape[1]
    return moved.reshape(4, rows, 3, -1).transpose(1, 2, 0, 3).reshape(rows, -1).astype(F32)


def quarter(parts, blk, row):
    one, two = (pick(pick(part, blk), row).astype(F32) for part in parts)
    return one + two


def diagonal_rows(parts):
    blk, row = place()[:2]
    rows = quarter(parts, 1 - blk, 1 - row).astype(BF16)
    half = rows.shape[-1] // 2
    return rows[..., :half], rows[..., half:]


def neighbour_rows(parts, one, two):
    blk, row = place()[:2]
    half = one.shape[-1]
    across, beside = quarter(parts, 1 - blk, row), quarter(parts, blk, 1 - row)
    across = jnp.concatenate([across[..., :half], across[..., half:] + two.astype(F32)], axis=-1)
    beside = jnp.concatenate([beside[..., :half] + one.astype(F32), beside[..., half:]], axis=-1)
    return across.astype(BF16), beside.astype(BF16)


def sent_beside_and_across(across, beside):
    return swapped(across, "blk", 1), swapped(beside, "head", 2)


def heads_grad(weight, out_bar):
    return dot_cols(weight, out_bar).astype(BF16).reshape(4, -1, out_bar.shape[0])


def own_quarter(parts):
    blk, row = place()[:2]
    return quarter(parts, blk, row)


def own_sum(own, *more):
    return sum((part.astype(F32) for part in more), own).astype(BF16)


def sum_over(array, *hops):
    for axis, mask in hops:
        array = array + swapped(array, axis, mask)
    return array


def gain_back(weight, weight_grad, gain):
    return jnp.sum(weight.astype(F32) * weight_grad, axis=-1) / gain.astype(F32)


def lower_of(upper, stream, factor, gain):
    return norm_back(upper, stream, factor, gain)[0]


def spread_device(
    tokens,
    segments,
    qkv_weight,
    out_weight,
    up_weight,
    down_weight,
    attn_gain,
    mlp_gain,
    scale_param,
    cotangent,
):
    layers, head_dim = scale_param.shape
    _, token_rows, width = tokens.shape
    scale_vecs = SCALE_BASE / math.sqrt(head_dim) * jax.nn.softplus(scale_param)
    segments = pick(segments, lax.axis_index("blk"))
    own_gains = jnp.concatenate([attn_gain, mlp_gain], axis=0)

    part3 = 3 * width // 4
    dense_own = [
        jnp.concatenate([out_weight[i], up_weight[i], down_weight[i]], axis=1) for i in (0, 1)
    ]

    columns = qkv_columns(qkv_weight[0], own_gains.T)
    columns, tokens, cotangent = tied(columns.reshape(-1, columns.shape[-1]), tokens, cotangent)
    along = along_batch(columns)
    first = swap_halves(tokens).reshape(-1, width)
    stream = first.astype(F32)
    upper = swap_halves(cotangent)
    along, first, dense_near, upper = tied(along, first, dense_own[0], upper)
    far, near = swapped(first, "head", 2), other_core(first)
    both = other_core(far)
    dense_near = along_batch(dense_near)
    qkv_across = swapped(along, "blk", 1)
    next_columns = jnp.concatenate(list(qkv_columns(qkv_weight[1], None)), axis=1)
    qkv_across, dense_near, next_columns, near, far, both = tied(
        qkv_across, dense_near, next_columns, near, far, both
    )
    token_pieces = (first, near, far, both)
    across, beside = swapped(dense_near, "blk", 1), swapped(dense_near, "head", 2)
    next_both = along_batch(jnp.stack([next_columns, dense_own[1]]))
    weight, gains = assemble_columns(along, qkv_across, part3)
    qkvs = [weight]
    gains = gains.T.astype(F32)

    kept, denses = [], []
    for layer in range(layers):
        normed, factor_one = normalize(stream, gains[layer])
        if layer == 1:
            normed = normed.astype(BF16)
            far, near = swapped(normed, "head", 2), other_core(normed)
            far, next_across, dense_next = tied(far, next_across, dense_next)
            across, beside = swapped(dense_next, "blk", 1), swapped(dense_next, "head", 2)
            token_pieces = (normed, near, far, other_core(far))
            qkvs.append(assemble_wide(next_along, next_across, part3))
        normed_all, projected = project(
            token_pieces, gains[layer], qkvs[layer], layer == 0, token_rows
        )
        attended, log_total = attend_rows(
            projected, scale_vecs[layer], segments, 4, token_rows
        )
        attended, across, beside = tied(attended, across, beside)
        one, two = to_beside(across), to_across(beside)
        if layer == 0:
            two, next_both = tied(two, next_both)
            next_along, dense_next = next_both[:, 0], next_both[:, 1]
            next_across = swapped(next_along, "blk", 1)
            attended_t, one, two = tied(over_head(attended), one, two)
        else:
            dense_near = dense_next
            attended_t, one, two = tied(over_head(attended), one, two)
        pieces = (dense_near, across, beside, one, two)
        pieces += tuple(other_core(piece) for piece in pieces)
        attended_t = attended_t.reshape(width, -1)
        denses.append(assemble(pieces))
        dense = denses[layer]
        out_w, up_w, down_w = dense[:, :width], dense[:, width:-width], dense[:, -width:]
        middle = stream + dot_rows(attended_t, out_w)
        normed_two, factor_two = normalize(middle, gains[layers + layer])
        normed_two = normed_two.astype(BF16)
        hidden = dot(normed_two, up_w)
        active = (hidden * jax.nn.sigmoid(hidden)).astype(BF16)
        kept.append(
            (
                stream, factor_one, normed_all, projected, log_total, attended_t, middle,
                factor_two, normed_two, hidden, active,
            )
        )
        stream = middle + dot(active, down_w)
    layer_out = swap_halves(stream.astype(BF16).reshape(tokens.shape))
    upper = upper.reshape(-1, width).astype(F32)

    scale_grads = [None] * layers
    for layer in reversed(range(layers)):
        (
            stream, factor_one, normed_all, projected, log_total, attended_t, middle,
            factor_two, normed_two, hidden, active,
        ) = kept[layer]
        qkv, dense = qkvs[layer], denses[layer]
        out_w, up_w, down_w = dense[:, :width], dense[:, width:-width], dense[:, -width:]
        down_bar = upper.astype(BF16)
        gate = jax.nn.sigmoid(hidden)
        up_bar = (
            dot_cols(down_bar, down_w) * gate * (1.0 + hidden * (1.0 - gate))
        ).astype(BF16)
        middle_grad = upper + lower_of(
            dot_cols(up_bar, up_w), middle, factor_two, gains[layers + layer]
        )
        out_bar = middle_grad.astype(BF16)
        if layer == 0:
            attended_grad = over_head(heads_grad(out_w, out_bar))
            grads, others = dense_grads(attended_t, normed_two, active, out_bar, up_bar, down_bar)
            others, across = tied(others, across)
            others, own = tied(others, own_quarter(cored) + across.astype(F32))
            attended_grad, others, z_sum, beside = tied(attended_grad, others, z_sum, beside)
            others = other_core(others)
            attended_grad, summed = tied(attended_grad, own_sum(own, beside))
            summed = over_batch(summed)
            earlier = across_sum(z_sum)
        else:
            attended_grad = over_head(heads_grad(out_w, out_bar))
            grads, others = dense_grads(attended_t, normed_two, active, out_bar, up_bar, down_bar)
            attended_grad, others, layer_out = tied(attended_grad, others, layer_out)
            others = other_core(others)
        bars, scale_grads[layer] = attend_back_rows(
            projected, attended_grad, log_total, scale_vecs[layer], segments, token_rows
        )
        if layer == 0:
            bars, earlier = tied(bars, earlier)
            qkv_grad = weight_back(bars, normed_all)
            bars, qkv_grad, others = tied(bars, qkv_grad, others)
            z_sum = over_batch(qkv_grad.reshape(4, 2, -1, qkv_grad.shape[-1]))
            cored = (grads, others)
            bars, rows = tied(bars, diagonal_rows(cored))
            diagonal = sent_beside_and_across(*rows)
            halves, to_core = rows_back(bars, qkv, token_rows)
            scale_sum = sum_over(jnp.stack(scale_grads), ("head", 1))
            halves, to_core, diagonal, summed, scale_sum = tied(
                halves, to_core, diagonal, summed, scale_sum
            )
            scale_sum = sum_over(scale_sum, ("head", 2))
            halves, to_core, rows, scale_sum = tied(
                halves, to_core, neighbour_rows(cored, *diagonal), scale_sum
            )
            sent = sent_beside_and_across(*rows)
            halves = halves + other_core(to_core).astype(F32)
            scale_sum = sum_over(scale_sum, ("batch", 1), ("batch", 2), ("blk", 1))
            own = own_quarter(cored)
            halves, sent, z_sum, scale_sum, own = tied(halves, sent, z_sum, scale_sum, own)
            halves, own, earlier = tied(halves, own_sum(own, *sent), earlier)
            moved = over_head(earlier.reshape(4, -1, earlier.shape[-1]))
            dense_first = over_batch(own)
            normed_grad = scatter_row(halves)
            z_across, dense_first = tied(across_sum(z_sum), dense_first)
            z_across = over_head(z_across.reshape(4, -1, z_across.shape[-1]))
            dense_grad = [dense_first, summed]
            qkv_grads = [columns_to_rows(z_across), columns_to_rows(moved)]
        else:
            bars, others = tied(bars, others)
            cored = (grads, others)
            bars, rows = tied(bars, diagonal_rows(cored))
            diagonal = sent_beside_and_across(*rows)
            halves, to_core, qkv_grad = project_back(bars, qkv, normed_all, token_rows)
            z_sum = over_batch(qkv_grad.reshape(4, 2, -1, qkv_grad.shape[-1]))
            to_core, halves, diagonal = tied(to_core, halves, diagonal)
            to_core, rows = tied(to_core, neighbour_rows(cored, *diagonal))
            across = swapped(rows[0], "blk", 1)
            halves = halves + other_core(to_core).astype(F32)
            normed_grad = scatter_row(halves)
            normed_grad, beside = tied(normed_grad, rows[1])
            beside = swapped(beside, "head", 2)
        upper = middle_grad + lower_of(normed_grad, stream, factor_one, gains[layer])
    input_grad = swap_halves(upper.astype(BF16).reshape(tokens.shape)).astype(F32)
    scale_grad = scale_sum * (SCALE_BASE / math.sqrt(head_dim)) * jax.nn.sigmoid(scale_param)
    dense_all = jnp.stack([part.astype(F32) for part in dense_grad])
    qkv_all = jnp.stack(qkv_grads)
    up_all = dense_all[:, :, width:-width]
    return (
        layer_out,
        input_grad,
        qkv_all,
        dense_all[:, :, :width],
        up_all,
        dense_all[:, :, -width:],
        gain_back(qkv_weight, qkv_all, attn_gain),
        gain_back(up_weight, up_all, mlp_gain),
        scale_grad,
    )


def per_device(*args):
    tokens, segments = args[0], args[1]
    sizes = tuple(lax.axis_size(axis) for axis in ALL)
    heads = tokens.shape[2] // args[8].shape[1]
    spread = (
        sizes == (4, 2, 4)
        and tokens.shape[0] == 2
        and args[2].shape[0] == 2
        and tokens.shape[1] % 128 == 0
        and Q_ROWS % tokens.shape[1] == 0
        and segments.shape[1] <= WINDOW
        and segments.shape[1] % FORWARD_ROWS == 0
        and heads % 4 == 0
        and tokens.shape[2] % 256 == 0
    )
    return spread_device(*args) if spread else general_device(*args)


def solution(mesh):
    rows = P(None, ALL, None)
    by_token = P("batch", ("blk", "head"), None)
    return jax.shard_map(
        per_device,
        mesh=mesh,
        in_specs=(
            by_token, P("batch", None), rows, rows, rows, rows, P(None, ALL), P(None, ALL), P(),
            by_token,
        ),
        out_specs=(
            by_token, by_token, rows, rows, rows, rows, P(None, ALL), P(None, ALL), P(),
        ),
        check_vma=False,
    )
```
